32 devices in a mesh: tile: 16 (over z, y, x), scene: 2 (over core).
Axes of the slice: x: 2, y: 2, z: 4, core: 2. Of those that a mesh axis runs over, the one named last changes fastest.
Arguments:
- points: bfloat16 [2, 2, 9, 32, 2048], P(None, 'scene', None, None, 'tile'), may hold values from -6 to 6
- point_counts: int32 [2, 2, 2048], P(None, 'scene', 'tile'), may hold values from 1 to 32, as said below
- pillar_tile: int32 [2, 2, 2048], P(None, 'scene', 'tile'), may hold values from 0 to 15, as said below
- pillar_cell: int32 [2, 2, 2048], P(None, 'scene', 'tile'), may hold values from 0 to 2047
- pillar_weight: bfloat16 [64, 9], P('scene'), may hold values from -2 to 2
- pillar_gain: bfloat16 [64], P('scene'), may hold values from 0.25 to 1.75
- pillar_shift: bfloat16 [64], P('scene'), may hold values from -2.5 to 2.5
- first_weight: bfloat16 [64, 576], P('scene'), may hold values from -0.25 to 0.25
- first_gain: bfloat16 [64], P('scene'), may hold values from 0.25 to 1.75
- first_shift: bfloat16 [64], P('scene'), may hold values from -2.5 to 2.5
- second_weight: bfloat16 [64, 576], P('scene'), may hold values from -0.25 to 0.25
- second_gain: bfloat16 [64], P('scene'), may hold values from 0.25 to 1.75
- second_shift: bfloat16 [64], P('scene'), may hold values from -2.5 to 2.5
- up_weight: bfloat16 [128, 64], P('scene'), may hold values from -0.75 to 0.75
- up_gain: bfloat16 [128], P('scene'), may hold values from 0.25 to 1.75
- up_shift: bfloat16 [128], P('scene'), may hold values from -2.5 to 2.5
- cotangent: bfloat16 [2, 2, 128, 64, 512], P(None, 'scene', None, 'tile'), may hold values from -6 to 6
Outputs:
- features: bfloat16 [2, 2, 128, 64, 512], P(None, 'scene', None, 'tile')
- points_grad: float32 [2, 2, 9, 32, 2048], P(None, 'scene', None, None, 'tile')
- pillar_weight_grad: float32 [64, 9], P('scene')
- pillar_gain_grad: float32 [64], P('scene')
- pillar_shift_grad: float32 [64], P('scene')
- first_weight_grad: float32 [64, 576], P('scene')
- first_gain_grad: float32 [64], P('scene')
- first_shift_grad: float32 [64], P('scene')
- second_weight_grad: float32 [64, 576], P('scene')
- second_gain_grad: float32 [64], P('scene')
- second_shift_grad: float32 [64], P('scene')
- up_weight_grad: float32 [128, 64], P('scene')
- up_gain_grad: float32 [128], P('scene')
- up_shift_grad: float32 [128], P('scene')
The draws below stay inside these ranges and needn't reach their ends.
Inputs may be any that keep to these rules, and one draw needn't show every extreme that they name: `point_counts`: point slots at or beyond a pillar's count are padding. Each aligned block of 128 pillars holds a pillar of 32 points. `pillar_tile`: each aligned block of 128 pillars names every tile at most 16 times; in each micro-batch and scene one tile is named exactly 16 times by every block.
All inputs are finite; a program needn't handle non-finite values.
Results may differ from the reference program's by a relative error of at most 0.012.
The reference program's roundings to bfloat16 on the way count: a program that leaves them out, or rounds other values in their place, can miss the bound.
Values may be sent and summed in bfloat16 or wider, within the bound.
No kernel may reach another device: no remote copies, remote signals or barrier semaphores. Data moves between devices by JAX's collectives and lax.ppermute only.
A program may use at most 128 MiB of HBM per device.

```python
import jax
import jax.numpy as jnp
from jax import lax

FEAT = 64
UP = 128
INPUTS = 9
PMAX = 32
PIL_DEV = 128
ROWS_DEV = 4
WIDTH = 512
MICRO = 2
SCENES = 2
PILLARS = 2048
ROWS = 64
CAP = 16


def draw_point_counts(key, part):
    key = jax.random.fold_in(key, 7)
    first_key, second_key, third_key, spot_key = jax.random.split(key, 4)
    tile_count = PILLARS // PIL_DEV
    block_count = tile_count * MICRO * SCENES
    shape = (block_count, PIL_DEV)
    first_vals = jax.random.randint(first_key, shape, 0, PMAX)
    second_vals = jax.random.randint(second_key, shape, 0, PMAX)
    third_vals = jax.random.randint(third_key, shape, 0, PMAX)
    spots = jax.random.randint(spot_key, (block_count, 1), 0, PIL_DEV)
    product = first_vals * second_vals * third_vals // ((PMAX - 1) * (PMAX - 1))
    micro_ids = lax.broadcasted_iota(jnp.int32, shape, 0) // (tile_count * SCENES)
    counts = jnp.where(micro_ids % 2 == 0, 1 + product, PMAX - product)
    counts = jnp.where(lax.broadcasted_iota(jnp.int32, shape, 1) == spots, PMAX, counts)
    return counts.reshape(MICRO, SCENES, PILLARS).astype(jnp.int32)


def draw_pillar_tile(key, part):
    key = jax.random.fold_in(key, 11)
    tile_count = PILLARS // PIL_DEV
    block_count = MICRO * SCENES * tile_count
    slot_count = tile_count * CAP
    hot_key, order_key, shuffle_key = jax.random.split(key, 3)
    hot_tiles = jax.random.randint(hot_key, (MICRO * SCENES, 1), 0, tile_count)
    hot_tiles = jnp.repeat(hot_tiles, tile_count, axis=0)
    ranks = jax.vmap(lambda k: jax.random.permutation(k, slot_count))(jax.random.split(order_key, block_count)).astype(jnp.int32)
    slot_tiles = lax.broadcasted_iota(jnp.int32, (block_count, slot_count), 1) // CAP
    scores = jnp.where(slot_tiles == hot_tiles, ranks - slot_count, ranks)
    chosen = jnp.argsort(scores, axis=1, stable=True)[:, :PIL_DEV].astype(jnp.int32) // CAP
    shuffled = jax.vmap(lambda k, row: jax.random.permutation(k, row))(jax.random.split(shuffle_key, block_count), chosen)
    return shuffled.reshape(MICRO, SCENES, PILLARS).astype(jnp.int32)


def plant(values, own_key, least, largest):
    longest = values.shape.index(max(values.shape))
    spots = []
    for shift in (0, 1):
        where = [jax.random.randint(jax.random.fold_in(own_key, axis), (), 0, length) for axis, length in enumerate(values.shape)]
        where[longest] = (where[longest] + shift) % values.shape[longest]
        spots.append(tuple(where))
    return values.at[spots[0]].set(least).at[spots[1]].set(largest)


def block_levels(rng, dims, shards, smallest, top_value):
    def one(dim, shards_of):
        steps = jax.random.uniform(jax.random.fold_in(jax.random.fold_in(rng, 6), dim), (shards_of,), jnp.float32, smallest / len(shards), top_value / len(shards))
        return jnp.repeat(jnp.exp(steps), dims[dim] // shards_of).reshape((-1,) + (1,) * (len(dims) - dim - 1))

    level = one(*shards[0])
    for cut in shards[1:]:
        level = level * one(*cut)
    return level


def bell_draw(stream_key, shape, width, limit, cuts=(), held_as=jnp.bfloat16):
    values = jax.random.normal(stream_key, shape, jnp.float32) * width
    if len(cuts) > 0:
        values = block_levels(stream_key, shape, cuts, -0.22, 0.18) * values
    return jnp.clip(values, min=-limit, max=limit).astype(held_as)


def setup_inputs(seed: int = 0) -> dict:
    key_list = jax.random.split(jax.random.key(seed), 18)
    return {
        "points": bell_draw(key_list[0], (MICRO, SCENES, INPUTS, PMAX, PILLARS), 1.0, 6.0, ((1, 2), (4, 16))),
        "point_counts": draw_point_counts(jax.random.fold_in(key_list[17], 71), 0),
        "pillar_tile": draw_pillar_tile(jax.random.fold_in(key_list[17], 71), 0),
        "pillar_cell": plant(jax.random.randint(key_list[3], (MICRO, SCENES, PILLARS), 0, ROWS_DEV * WIDTH), jax.random.fold_in(key_list[3], 1), 0, (ROWS_DEV * WIDTH) - 1).astype(jnp.int32),
        "pillar_weight": bell_draw(key_list[4], (FEAT, INPUTS), INPUTS ** -0.5, 2.0, ((0, 2),)),
        "pillar_gain": jnp.clip(1.0 + 0.15 * jax.random.normal(key_list[5], (FEAT,), jnp.float32), 0.25, 1.75).astype(jnp.bfloat16),
        "pillar_shift": bell_draw(key_list[6], (FEAT,), 0.5, 2.5, ((0, 2),)),
        "first_weight": bell_draw(key_list[7], (FEAT, 9 * FEAT), (9 * FEAT) ** -0.5, 0.25, ((0, 2),)),
        "first_gain": jnp.clip(1.0 + 0.15 * jax.random.normal(key_list[8], (FEAT,), jnp.float32), 0.25, 1.75).astype(jnp.bfloat16),
        "first_shift": bell_draw(key_list[9], (FEAT,), 0.5, 2.5, ((0, 2),)),
        "second_weight": bell_draw(key_list[10], (FEAT, 9 * FEAT), (9 * FEAT) ** -0.5, 0.25, ((0, 2),)),
        "second_gain": jnp.clip(1.0 + 0.15 * jax.random.normal(key_list[11], (FEAT,), jnp.float32), 0.25, 1.75).astype(jnp.bfloat16),
        "second_shift": bell_draw(key_list[12], (FEAT,), 0.5, 2.5, ((0, 2),)),
        "up_weight": bell_draw(key_list[13], (UP, FEAT), FEAT ** -0.5, 0.75, ((0, 2),)),
        "up_gain": jnp.clip(1.0 + 0.15 * jax.random.normal(key_list[14], (UP,), jnp.float32), 0.25, 1.75).astype(jnp.bfloat16),
        "up_shift": bell_draw(key_list[15], (UP,), 0.5, 2.5, ((0, 2),)),
        "cotangent": bell_draw(key_list[16], (MICRO, SCENES, UP, ROWS, WIDTH), 1.0, 6.0, ((1, 2), (3, 16))),
    }


@jax.custom_vjp
def low(v):
    return lax.optimization_barrier(v.astype(jnp.bfloat16)).astype(jnp.float32)

@jax.custom_vjp
def low_back(v):
    return v

def low_keep(v):
    return (low(v), None)

def low_pass(kept, grad):
    return (grad,)

def back_keep(v):
    return (v, None)

def back_low(kept, grad):
    return (low(grad),)
low.defvjp(low_keep, low_pass)
low_back.defvjp(back_keep, back_low)
norm_eps = 0.001

def channel(vector):
    return vector[None, :, None, None]

def canvas_norm(values, gain, shift):
    centre = lax.optimization_barrier(jnp.mean(values, axis=(0, 2, 3), keepdims=True))
    spread = lax.optimization_barrier(jnp.mean(jnp.square(values - centre), axis=(0, 2, 3), keepdims=True))
    return (values - centre) * lax.rsqrt(spread + norm_eps) * channel(gain) + channel(shift)

def conv_layer(grid, weight):
    kernel = weight.reshape(FEAT, 3, 3, FEAT).transpose(0, 3, 1, 2)
    return lax.conv_general_dilated(grid, kernel, (1, 1), ((1, 1), (1, 1)), dimension_numbers=('NCHW', 'OIHW', 'NCHW'), precision=lax.Precision.HIGHEST)

def place_pillars(values, index):
    return jnp.zeros((FEAT, ROWS * WIDTH), values.dtype).at[:, index].add(values)

def micro_step(params, points, counts, tiles, cells):
    pillar_weight, pillar_gain, pillar_shift, first_weight, first_gain, first_shift, second_weight, second_gain, second_shift, up_weight, up_gain, up_shift = params
    lifted = low_back(jnp.einsum('ck,sknp->scnp', pillar_weight, points, precision=lax.Precision.HIGHEST))
    valid = lax.broadcasted_iota(jnp.int32, (PMAX, PILLARS), 0)[None] < counts[:, None, :]
    valid = valid[:, None]
    weights_mask = valid.astype(lifted.dtype)
    count_total = jnp.sum(weights_mask) * FEAT
    centre = lax.optimization_barrier(jnp.sum(lifted * weights_mask, axis=(0, 2, 3), keepdims=True)) / (count_total / FEAT)
    spread = lax.optimization_barrier(jnp.sum(weights_mask * jnp.square(lifted - centre), axis=(0, 2, 3), keepdims=True)) / (count_total / FEAT)
    normed = (lifted - centre) * lax.rsqrt(spread + norm_eps) * channel(pillar_gain) + channel(pillar_shift)
    pooled = jax.nn.logsumexp(jax.nn.silu(normed), axis=2, where=valid)
    sent = low(low_back(pooled))
    index = (tiles * (ROWS_DEV * WIDTH) + cells).astype(jnp.int32)
    canvas = low(jax.vmap(place_pillars)(sent, index)).reshape(SCENES, FEAT, ROWS, WIDTH)
    first_act = low(jax.nn.silu(canvas_norm(low_back(conv_layer(canvas, first_weight)), first_gain, first_shift)))
    second_act = low(jax.nn.silu(canvas_norm(low_back(conv_layer(first_act, second_weight)), second_gain, second_shift)))
    up_out = low_back(jnp.einsum('uc,schw->suhw', up_weight, second_act, precision=lax.Precision.HIGHEST))
    return jax.nn.silu(canvas_norm(up_out, up_gain, up_shift))

def reference(points, point_counts, pillar_tile, pillar_cell, pillar_weight, pillar_gain, pillar_shift, first_weight, first_gain, first_shift, second_weight, second_gain, second_shift, up_weight, up_gain, up_shift, cotangent):
    floats = [a.astype(jnp.float32) for a in (points, pillar_weight, pillar_gain, pillar_shift, first_weight, first_gain, first_shift, second_weight, second_gain, second_shift, up_weight, up_gain, up_shift)]

    def forward(points_all, *params):
        stepper = jax.checkpoint(lambda pts, cnt, til, cel: micro_step(params, pts, cnt, til, cel))

        def scan_body(carry, items):
            return (carry, stepper(*items))
        return lax.scan(scan_body, None, (points_all, point_counts, pillar_tile, pillar_cell))[1]
    result, pullback = jax.vjp(forward, *floats)
    grads = pullback(cotangent.astype(jnp.float32))
    return (result.astype(jnp.bfloat16), grads[0], grads[1], grads[2], grads[3], grads[4], grads[5], grads[6], grads[7], grads[8], grads[9], grads[10], grads[11], grads[12])
```

```python
import jax
import jax.numpy as jnp
from jax import lax
from jax.sharding import PartitionSpec as P

norm_eps = 0.001


def extended(value, sides, width):
    for axis, dim in sides:
        size, length = (lax.axis_size(axis), value.shape[dim])
        up = [(i, (i + 1) % size) for i in range(size - 1)]
        down = [(j, i) for i, j in up]
        last = lax.slice_in_dim(value, length - width, length, axis=dim)
        leading = lax.slice_in_dim(value, 0, width, axis=dim)
        before = lax.ppermute(last, axis, up)
        after = lax.ppermute(leading, axis, down)
        value = jnp.concatenate([before, value, after], axis=dim)
    return value


def silu_grad(values):
    sigmoid_vals = jax.nn.sigmoid(values)
    return sigmoid_vals * (1.0 + values * (1.0 - sigmoid_vals))


def masked_sum(values, weights_mask):
    return jnp.sum(values * weights_mask[None, :], axis=1)


BOTH = ("tile", "scene")


def everyone(block, how):
    if how == "gather":
        return lax.all_gather(block, BOTH)
    if how == "exchange":
        copies = jnp.broadcast_to(block[None], (lax.axis_size(BOTH),) + block.shape)
        return lax.all_to_all(copies, BOTH, split_axis=0, concat_axis=0)
    if how == "steps":
        pair = lax.all_gather(block, "scene")
        copies = jnp.broadcast_to(pair[None], (lax.axis_size("tile"),) + pair.shape)
        found = lax.all_to_all(copies, "tile", split_axis=0, concat_axis=0)
        return found.reshape((-1,) + block.shape)
    if how == "sums":
        pair = lax.psum(block, "scene")
        copies = jnp.broadcast_to(pair[None], (lax.axis_size("tile"),) + pair.shape)
        return lax.all_to_all(copies, "tile", split_axis=0, concat_axis=0)
    pair = lax.psum(block, "scene")
    return lax.all_gather(pair, "tile")


def normalize(pairs, how):
    rows = []
    for values, weights_mask, _, _ in pairs:
        count = jnp.sum(weights_mask)
        centre = masked_sum(values, weights_mask) / count
        centred = values - centre[:, None]
        spread = masked_sum(centred * centred, weights_mask)
        rows += [centre, spread, jnp.full(centre.shape, count)]
    found = everyone(jnp.stack(rows), how)
    result = []
    for index, (values, weights_mask, gain_vals, shift_vals) in enumerate(pairs):
        centres, spreads, counts = found[:, 3 * index], found[:, 3 * index + 1], found[:, 3 * index + 2]
        count_all = jnp.sum(counts, axis=0)
        centre = jnp.sum(counts * centres, axis=0) / count_all
        away = centres - centre[None]
        spread = jnp.sum(spreads + counts * away * away, axis=0) / count_all
        inverse_std = lax.rsqrt(spread + norm_eps)
        unit_vals = (values - centre[:, None]) * inverse_std[:, None]
        result.append(
            (unit_vals * gain_vals[:, None] + shift_vals[:, None], unit_vals, inverse_std, count_all)
        )
    return result


def norm_back(pairs, how):
    rows = []
    for grad_out, unit_vals, _, _, weights_mask, _ in pairs:
        rows += [masked_sum(grad_out * unit_vals, weights_mask), masked_sum(grad_out, weights_mask)]
    found = jnp.sum(everyone(jnp.stack(rows), how), axis=0)
    result = []
    for index, (grad_out, unit_vals, inverse_std, count_all, weights_mask, gain_vals) in enumerate(pairs):
        gain_part, shift_part = found[2 * index], found[2 * index + 1]
        grad_in = (gain_vals * inverse_std)[:, None] * (
            grad_out - (shift_part / count_all)[:, None] - unit_vals * (gain_part / count_all)[:, None]
        )
        result.append((grad_in * weights_mask[None, :], gain_part, shift_part))
    return result


def unfold(padded, rows, width):
    widened = jnp.pad(padded, ((0, 0), (0, 0), (1, 1)))
    pieces = [
        widened[:, lag_row : lag_row + rows, lag_col : lag_col + width]
        for lag_row in range(3)
        for lag_col in range(3)
    ]
    return jnp.concatenate(pieces, axis=0).reshape(9 * padded.shape[0], rows * width)


def conv_apply(padded, weight, rows, width):
    columns = unfold(padded, rows, width)
    return (jnp.dot(weight, columns, preferred_element_type=jnp.float32), columns)


def conv_forward(grid, weight, rows, width):
    padded = extended(grid.reshape(grid.shape[0], rows, width), (("tile", 1),), 1)
    return conv_apply(padded, weight, rows, width)


def conv_back(grad_out, weight, columns, rows, width):
    weight_grad = lax.dot_general(
        grad_out, columns, (((1,), (1,)), ((), ())), preferred_element_type=jnp.float32
    )
    padded = extended(grad_out.reshape(grad_out.shape[0], rows, width), (("tile", 1),), 1)
    out_count = weight.shape[0]
    in_count = weight.shape[1] // 9
    flipped = (
        weight.reshape(out_count, 9, in_count)[:, ::-1, :]
        .transpose(2, 1, 0)
        .reshape(in_count, 9 * out_count)
    )
    return (
        jnp.dot(flipped, unfold(padded, rows, width), preferred_element_type=jnp.float32),
        weight_grad,
    )


def contract_rows(left_mat, right_mat):
    return lax.dot_general(
        left_mat, right_mat, (((1,), (1,)), ((), ())), preferred_element_type=jnp.float32
    )


def contract_lead(left_mat, right_mat):
    return lax.dot_general(
        left_mat, right_mat, (((0,), (0,)), ((), ())), preferred_element_type=jnp.float32
    )


def shards(
    points,
    point_counts,
    pillar_tile,
    pillar_cell,
    pillar_weight,
    pillar_gain,
    pillar_shift,
    first_weight,
    first_gain,
    first_shift,
    second_weight,
    second_gain,
    second_shift,
    up_weight,
    up_gain,
    up_shift,
    cotangent,
):
    micro_count, _, inputs, depth, pillars = points.shape
    channels = up_weight.shape[1]
    rows = cotangent.shape[3]
    width = cotangent.shape[4]
    cells = rows * width
    tile_count = lax.axis_size("tile")
    scene_count = lax.axis_size("scene")
    capacity = 2 * pillars // tile_count
    slot_count = tile_count * capacity
    canvas_mask = jnp.ones((cells,), jnp.float32)
    upper = cotangent.shape[2]
    weights = [pillar_weight, first_weight, second_weight, up_weight]
    vectors = [
        pillar_gain, pillar_shift, first_gain, first_shift, second_gain, second_shift, up_gain, up_shift,
    ]
    flat = jnp.concatenate([part.reshape(-1) for part in weights + vectors])
    both = lax.all_gather(flat, "scene")
    whole = []
    start = 0
    for part in weights + vectors:
        stop = start + part.size
        whole.append(both[:, start:stop].reshape((-1,) + part.shape[1:]))
        start = stop
    w_pillar, w_first, w_second, w_up = whole[:4]
    g_pillar, s_pillar, g_first, s_first, g_second, s_second, g_up, s_up = [
        part.astype(jnp.float32) for part in whole[4:]
    ]
    micros = range(micro_count)
    flat_points = [points[m, 0].reshape(inputs, depth * pillars) for m in micros]
    lifted = [jnp.dot(w_pillar, flat_points[m], preferred_element_type=jnp.float32) for m in micros]
    valid = [
        lax.broadcasted_iota(jnp.int32, (depth, pillars), 0) < point_counts[m, 0][None, :] for m in micros
    ]
    point_mask = [valid[m].astype(jnp.float32).reshape(depth * pillars) for m in micros]
    pillar_norm = normalize([(lifted[m], point_mask[m], g_pillar, s_pillar) for m in micros], "gather")
    activated = [jax.nn.silu(pillar_norm[m][0]).reshape(channels, depth, pillars) for m in micros]
    pooled = [jax.nn.logsumexp(activated[m], axis=1, where=valid[m][None, :, :]) for m in micros]
    placing = []
    packed = []
    cell_slots = []
    for m in micros:
        tile_ids = pillar_tile[m, 0]
        row_index = lax.broadcasted_iota(jnp.int32, (pillars, pillars), 0)
        col_index = lax.broadcasted_iota(jnp.int32, (pillars, pillars), 1)
        earlier = (tile_ids[:, None] == tile_ids[None, :]) & (col_index < row_index)
        rank_ids = jnp.sum(earlier.astype(jnp.int32), axis=1)
        slot_ids = tile_ids * capacity + rank_ids
        placed_now = slot_ids[:, None] == lax.broadcasted_iota(jnp.int32, (pillars, slot_count), 1)
        placing.append(placed_now.astype(jnp.bfloat16))
        packed.append(
            jnp.dot(pooled[m].astype(jnp.bfloat16), placing[m], preferred_element_type=jnp.float32).astype(jnp.bfloat16)
        )
        cell_slots.append(jnp.sum(jnp.where(placed_now, pillar_cell[m, 0][:, None], 0), axis=0))

    def spread_out(stacked):
        micro, lead, _ = stacked.shape
        blocks = stacked.reshape(micro, lead, tile_count, capacity).transpose(2, 0, 1, 3)
        found = lax.all_to_all(blocks, "tile", split_axis=0, concat_axis=0)
        return found.transpose(1, 2, 0, 3).reshape(micro, lead, slot_count)

    arrived = spread_out(jnp.stack(packed))
    arrived_cells = spread_out(jnp.stack(cell_slots)[:, None])[:, 0]
    spreading = [
        (arrived_cells[m][:, None] == lax.broadcasted_iota(jnp.int32, (slot_count, cells), 1)).astype(jnp.bfloat16)
        for m in micros
    ]
    canvas = [
        jnp.dot(arrived[m], spreading[m], preferred_element_type=jnp.float32).astype(jnp.bfloat16) for m in micros
    ]
    first = [conv_forward(canvas[m], w_first, rows, width) for m in micros]
    first_norm = normalize([(first[m][0], canvas_mask, g_first, s_first) for m in micros], "exchange")
    first_act = [jax.nn.silu(first_norm[m][0]).astype(jnp.bfloat16) for m in micros]
    second = [conv_forward(first_act[m], w_second, rows, width) for m in micros]
    second_norm = normalize([(second[m][0], canvas_mask, g_second, s_second) for m in micros], "steps")
    second_act = [jax.nn.silu(second_norm[m][0]).astype(jnp.bfloat16) for m in micros]
    up_out = [jnp.dot(w_up, second_act[m], preferred_element_type=jnp.float32) for m in micros]
    up_norm = normalize([(up_out[m], canvas_mask, g_up, s_up) for m in micros], "exchange")
    features = jnp.stack(
        [jax.nn.silu(up_norm[m][0]).astype(jnp.bfloat16).reshape(upper, rows, width) for m in micros]
    )[:, None]
    up_back = norm_back(
        [
            (cotangent[m, 0].astype(jnp.float32).reshape(upper, cells) * silu_grad(up_norm[m][0]),)
            + up_norm[m][1:] + (canvas_mask, g_up)
            for m in micros
        ],
        "exchange",
    )
    grad_up = [up_back[m][0].astype(jnp.bfloat16) for m in micros]
    grad_up_weight = sum(contract_rows(grad_up[m], second_act[m]) for m in micros)
    second_back = norm_back(
        [
            (contract_lead(w_up, grad_up[m]) * silu_grad(second_norm[m][0]),)
            + second_norm[m][1:] + (canvas_mask, g_second)
            for m in micros
        ],
        "sums",
    )
    second_conv = [
        conv_back(second_back[m][0].astype(jnp.bfloat16), w_second, second[m][1], rows, width) for m in micros
    ]
    first_back = norm_back(
        [
            (second_conv[m][0] * silu_grad(first_norm[m][0]),) + first_norm[m][1:] + (canvas_mask, g_first)
            for m in micros
        ],
        "summed",
    )
    first_conv = [
        conv_back(first_back[m][0].astype(jnp.bfloat16), w_first, first[m][1], rows, width) for m in micros
    ]
    canvas_back = jnp.stack(
        [contract_rows(first_conv[m][0].astype(jnp.bfloat16), spreading[m]).astype(jnp.bfloat16) for m in micros]
    )
    returned = spread_out(canvas_back)
    grad_pillar = []
    for m in micros:
        grad_pooled = contract_rows(returned[m], placing[m])
        softmax_part = jnp.where(valid[m][None, :, :], jnp.exp(activated[m] - pooled[m][:, None, :]), 0.0)
        grad_act = (grad_pooled[:, None, :] * softmax_part).reshape(channels, depth * pillars)
        grad_pillar.append(
            (grad_act * silu_grad(pillar_norm[m][0]),) + pillar_norm[m][1:] + (point_mask[m], g_pillar)
        )
    pillar_back = norm_back(grad_pillar, "exchange")
    grad_lift = [pillar_back[m][0].astype(jnp.bfloat16) for m in micros]
    points_grad = jnp.stack(
        [contract_lead(w_pillar, grad_lift[m]).reshape(inputs, depth, pillars) for m in micros]
    )[:, None]
    weight_grads = [
        sum(contract_rows(grad_lift[m], flat_points[m]) for m in micros),
        sum(first_conv[m][1] for m in micros),
        sum(second_conv[m][1] for m in micros),
        grad_up_weight,
    ]
    halves = jnp.concatenate([part.reshape(scene_count, -1) for part in weight_grads], axis=1)
    length = halves.shape[1]
    unit = tile_count * 8 * 128
    padded = -(-length // unit) * unit
    halves = jnp.pad(halves, ((0, 0), (0, padded - length)))
    blocks = halves.reshape(scene_count, tile_count, -1, 128).transpose(1, 0, 2, 3).reshape(
        scene_count * tile_count, -1, 128
    )
    mine = jnp.sum(lax.all_to_all(blocks, BOTH, split_axis=0, concat_axis=0), axis=0)
    own = lax.all_gather(mine, "tile").reshape(-1)
    own_grads = []
    start = 0
    for part in weights:
        stop = start + part.size
        own_grads.append(own[start:stop].reshape(part.shape))
        start = stop
    scene_index = lax.axis_index("scene")

    def own_part(full):
        part_len = full.shape[0] // scene_count
        return lax.dynamic_slice_in_dim(full, scene_index * part_len, part_len)

    parts = []
    for back in (pillar_back, first_back, second_back, up_back):
        parts += [own_part(sum(back[m][1] for m in micros)), own_part(sum(back[m][2] for m in micros))]
    return (
        features,
        points_grad,
        own_grads[0],
        parts[0],
        parts[1],
        own_grads[1],
        parts[2],
        parts[3],
        own_grads[2],
        parts[4],
        parts[5],
        own_grads[3],
        parts[6],
        parts[7],
    )


def solution(mesh):
    placed = (
        P(None, "scene", None, None, "tile"),
        P(None, "scene", "tile"),
        P(None, "scene", "tile"),
        P(None, "scene", "tile"),
        P("scene", None),
        P("scene"),
        P("scene"),
        P("scene", None),
        P("scene"),
        P("scene"),
        P("scene", None),
        P("scene"),
        P("scene"),
        P("scene", None),
        P("scene"),
        P("scene"),
        P(None, "scene", None, "tile", None),
    )
    return jax.shard_map(
        shards,
        mesh=mesh,
        in_specs=placed,
        out_specs=(
            P(None, "scene", None, "tile", None),
            P(None, "scene", None, None, "tile"),
            P("scene", None),
            P("scene"),
            P("scene"),
            P("scene", None),
            P("scene"),
            P("scene"),
            P("scene", None),
            P("scene"),
            P("scene"),
            P("scene", None),
            P("scene"),
            P("scene"),
        ),
        check_vma=False,
    )
```

```python
import functools

import jax
import jax.numpy as jnp
from jax import lax
from jax.experimental import pallas as pl
from jax.experimental.pallas import tpu as pltpu
from jax.sharding import PartitionSpec as P

norm_eps = 0.001
BOTH = ("tile", "scene")
F32 = jnp.float32
BF16 = jnp.bfloat16
VMEM_LIMIT = 24 * 1024 * 1024
LANES = 128


def run(kernel, outs, *args, smem=(), scratch=(), cost=None):
    specs = [
        pl.BlockSpec(memory_space=pltpu.SMEM if index in smem else pltpu.VMEM)
        for index in range(len(args))
    ]
    return pl.pallas_call(
        kernel,
        out_shape=[jax.ShapeDtypeStruct(shape, dtype) for shape, dtype in outs],
        in_specs=specs,
        out_specs=[pl.BlockSpec(memory_space=pltpu.VMEM) for _ in outs],
        scratch_shapes=list(scratch),
        compiler_params=pltpu.CompilerParams(vmem_limit_bytes=VMEM_LIMIT),
        cost_estimate=cost,
    )(*args)


def dot(left, right, precision=None):
    return jnp.dot(left, right, preferred_element_type=F32, precision=precision)


def dot_lanes(left, right, precision=None):
    return lax.dot_general(
        left, right, (((1,), (1,)), ((), ())), preferred_element_type=F32, precision=precision
    )


def sigmoid(values):
    return 0.5 + 0.5 * jnp.tanh(0.5 * values)


def fold(values):
    total = values[:, :LANES]
    for start in range(LANES, values.shape[1], LANES):
        total = total + values[:, start : start + LANES]
    return total


def row_of(left, right=None):
    both = left if right is None else jnp.concatenate([left, right], axis=0)
    return jnp.sum(jnp.transpose(both), axis=0, keepdims=True)


def columns_of(rows):
    rows = rows + [jnp.zeros((8 - len(rows), LANES), F32)] if len(rows) < 8 else rows
    return jnp.transpose(jnp.concatenate(rows, axis=0))


def inside(tile, row, height):
    tiles, rows = height
    place = tile * rows + row
    return jnp.where((place >= 0) & (place < tiles * rows), 1.0, 0.0).astype(F32)


def send_all(ref, rows):
    for index, row in enumerate(rows):
        ref[:, index : index + 1, :] = jnp.broadcast_to(row[None], (ref.shape[0], 1, LANES))


def pooled_stats(means, squares, count):
    peers = means.shape[0]
    mean = jnp.sum(means, axis=0, keepdims=True) * (1.0 / peers)
    away = means - mean
    spread = jnp.sum(squares + count * away * away, axis=0, keepdims=True) * (1.0 / (peers * count))
    return mean, lax.rsqrt(spread + norm_eps)


def side_sum(stacked, channels):
    width = stacked.shape[1]
    lane = lax.broadcasted_iota(jnp.int32, (channels, width), 1)
    left = pltpu.roll(stacked[:channels], 1, 1)
    right = pltpu.roll(stacked[2 * channels :], width - 1, 1)
    return (
        stacked[channels : 2 * channels]
        + jnp.where(lane > 0, left, 0.0)
        + jnp.where(lane < width - 1, right, 0.0)
    )


def pack_kernel(first, second, up, pillar, *rest):
    vectors, out = rest[:8], rest[8]
    out[...] = jnp.zeros(out.shape, out.dtype)
    half = first.shape[0]
    taps = first.shape[1]
    out[0:half, 0:taps] = first[...]
    out[half : 2 * half, 0:taps] = second[...]
    out[0 : 2 * half, taps : taps + up.shape[1]] = up[...]
    out[2 * half : 3 * half, 0 : pillar.shape[1]] = pillar[...]
    rows = []
    for vector in vectors:
        row = vector[...].astype(F32).reshape(1, -1)
        rows.append(jnp.concatenate([row, jnp.zeros((1, LANES - row.shape[1]), F32)], axis=1))
    rows.append(jnp.zeros((8, LANES), F32))
    out[3 * half : 3 * half + 16, 0:LANES] = jnp.concatenate(rows, axis=0).astype(BF16)


def unpack_kernel(both, w_pillar, cols, l_first, l_second, b_first, b_second, w_up, w_up_t):
    half = w_pillar.shape[0] // 2
    channels = 2 * half
    taps = 9 * channels
    inputs = w_pillar.shape[1]
    first = jnp.concatenate([both[s, 0:half, 0:taps] for s in range(2)], axis=0).astype(F32)
    second = jnp.concatenate([both[s, half:channels, 0:taps] for s in range(2)], axis=0).astype(F32)
    up = jnp.concatenate([both[s, 0:channels, taps : taps + channels] for s in range(2)], axis=0)
    w_up[...] = up
    w_up_t[...] = jnp.transpose(up.astype(F32)).astype(BF16)
    w_pillar[...] = jnp.concatenate(
        [both[s, channels : channels + half, 0:inputs] for s in range(2)], axis=0
    )
    vectors = [both[s, channels + half : channels + half + 16, 0:LANES].astype(F32) for s in range(2)]
    rows = []
    for index in range(8):
        size = half if index < 6 else channels
        row = jnp.concatenate([vectors[s][index : index + 1, 0:size] for s in range(2)], axis=1)
        rows.append(jnp.concatenate([row] * (LANES // (2 * size)), axis=1))
    cols[...] = columns_of(rows)
    zero = jnp.zeros((channels, channels), F32)
    for weight, ahead, back in ((first, l_first, b_first), (second, l_second, b_second)):
        pieces = [
            [weight[:, (3 * a + b) * channels : (3 * a + b + 1) * channels] for b in range(3)]
            for a in range(3)
        ]
        flipped = [[jnp.transpose(pieces[a][b]) for b in range(3)] for a in range(3)]
        for j in range(2):
            for b in range(3):
                start = (3 * j + b) * channels
                ahead[start : start + channels, :] = jnp.concatenate(
                    [pieces[r - j][b] if 0 <= r - j <= 2 else zero for r in range(4)], axis=1
                ).astype(BF16)
                back[start : start + channels, :] = jnp.concatenate(
                    [flipped[j + 2 - r][2 - b] if 0 <= j + 2 - r <= 2 else zero for r in range(4)],
                    axis=1,
                ).astype(BF16)


def point_rows(points, micro, wide):
    inputs, depth, pillars = points.shape[2:]
    wide[...] = points[micro, 0].astype(F32).reshape(inputs * depth, pillars)
    return jnp.concatenate([wide[pl.ds(n, inputs, stride=depth), :] for n in range(depth)], axis=1)


def point_mask(counts, micro, depth):
    count = counts[micro]
    return jnp.concatenate([jnp.where(count > n, 1.0, 0.0) for n in range(depth)], axis=1)


def moments_kernel(points, counts, out, wide):
    micros, _, inputs, depth, pillars = points.shape
    blocks = []
    for micro in range(micros):
        rows = point_rows(points, micro, wide)
        mask = point_mask(counts, micro, depth)
        total = jnp.sum(mask, axis=1, keepdims=True)
        mean = jnp.sum(rows * mask, axis=1, keepdims=True) / total
        centred = (rows - mean) * mask
        products = dot_lanes(centred, centred, lax.Precision.HIGHEST)
        lane = lax.broadcasted_iota(jnp.int32, (inputs, inputs), 1)
        diagonal = lax.broadcasted_iota(jnp.int32, (inputs, inputs), 0) == lane
        mean_row = jnp.sum(jnp.where(diagonal, mean, 0.0), axis=0, keepdims=True)
        extra = jnp.concatenate(
            [products[8:9], mean_row, jnp.broadcast_to(total, (1, inputs)), jnp.zeros((5, inputs), F32)],
            axis=0,
        )
        blocks += [products[0:8], extra, jnp.zeros((8, 64 - 2 * inputs), F32)]
    block = jnp.concatenate(blocks, axis=1)
    out[...] = jnp.broadcast_to(block[None], out.shape)


def pillar_kernel(
    found, points, counts, tiles, cells, w_pillar, cols, send, pooled, stats, slots, wide, lifted, acts,
    *, capacity, width
):
    micros, _, inputs, depth, pillars = points.shape
    channels = w_pillar.shape[0]
    weight = w_pillar[...]
    wide_weight = weight.astype(F32)
    rows_out = send.shape[0]
    stacked = []
    slot_rows = []
    info = []
    for micro in range(micros):
        base = micro * 64
        lifted[...] = dot(weight, point_rows(points, micro, wide).astype(BF16))
        means = found[:, 1, base + inputs : base + 2 * inputs]
        totals = found[:, 2, base + inputs : base + 2 * inputs]
        count = jnp.sum(totals, axis=0, keepdims=True)
        mean = jnp.sum(means * totals, axis=0, keepdims=True) / count
        away = means - mean
        products = lax.dot_general(
            away * totals, away, (((0,), (0,)), ((), ())),
            preferred_element_type=F32, precision=lax.Precision.HIGHEST,
        )
        summed = jnp.sum(found[...], axis=0)
        products = products + jnp.concatenate(
            [summed[:, base : base + inputs], summed[0:1, base + inputs : base + 2 * inputs]], axis=0
        )
        cov = products / count
        spun = wide_weight[:, 0:1] * cov[0:1]
        for k in range(1, inputs):
            spun = spun + wide_weight[:, k : k + 1] * cov[k : k + 1]
        spread = jnp.sum(spun * wide_weight, axis=1, keepdims=True)
        centre = jnp.sum(wide_weight * mean, axis=1, keepdims=True)
        rstd = lax.rsqrt(spread + norm_eps)
        inverse = jnp.broadcast_to(1.0 / count[:, 0:1], (channels, 1))
        stats[micro] = jnp.concatenate(
            [
                centre, rstd, inverse, jnp.zeros((channels, 13), F32),
                spun, jnp.zeros((channels, 16 - inputs), F32),
                jnp.broadcast_to(mean, (channels, inputs)), jnp.zeros((channels, LANES - 32 - inputs), F32),
            ],
            axis=1,
        )
        scale = rstd * cols[0:channels, 0:1]
        shift = cols[0:channels, 1:2]
        limit = counts[micro]
        top = jnp.full((channels, pillars), -jnp.inf, F32)
        for n in range(depth):
            piece = slice(n * pillars, (n + 1) * pillars)
            normed = (lifted[:, piece] - centre) * scale + shift
            act = normed * sigmoid(normed)
            acts[:, piece] = act
            top = jnp.maximum(top, jnp.where(limit > n, act, -jnp.inf))
        total = jnp.zeros((channels, pillars), F32)
        for n in range(depth):
            piece = slice(n * pillars, (n + 1) * pillars)
            total = total + jnp.where(limit > n, jnp.exp(acts[:, piece] - top), 0.0)
        result = top + jnp.log(total)
        pooled[micro] = result
        zero = jnp.zeros((channels, pillars), F32)
        kept = result.astype(BF16).astype(F32)
        parts = [zero] * micros
        parts[micro] = kept
        stacked.append(jnp.transpose(jnp.concatenate(parts, axis=0)))
        tile = tiles[micro].astype(F32)
        across = jnp.broadcast_to(tile, (pillars, pillars))
        down = jnp.transpose(across)
        row = lax.broadcasted_iota(jnp.int32, (pillars, pillars), 0)
        col = lax.broadcasted_iota(jnp.int32, (pillars, pillars), 1)
        rank = jnp.sum(jnp.where((across == down) & (row < col), 1.0, 0.0), axis=0, keepdims=True)
        slot_rows.append(tile * capacity + rank)
        cell = cells[micro]
        row_of_cell = cell // width
        column = cell - row_of_cell * width
        high = column // 16
        lines = [
            (row_of_cell + 1).astype(F32), high.astype(F32), (column - high * 16).astype(F32),
            jnp.zeros((1, pillars), F32),
        ]
        pad = jnp.zeros((4, pillars), F32)
        pieces = [pad] * micros
        pieces[micro] = jnp.concatenate(lines, axis=0)
        pieces.append(jnp.zeros((LANES - 4 * micros, pillars), F32))
        info.append(jnp.transpose(jnp.concatenate(pieces, axis=0)))
    slots[...] = jnp.concatenate(slot_rows + [jnp.zeros((8 - micros, pillars), F32)], axis=0)
    values = jnp.concatenate(stacked, axis=0).astype(BF16)
    details = jnp.concatenate(info, axis=0)
    noted = jnp.zeros((rows_out, LANES), F32)
    for group in range(3):
        place = lax.broadcasted_iota(jnp.int32, (rows_out, pillars), 0) + (group - 1) * capacity
        chosen = jnp.concatenate(
            [jnp.where(place.astype(F32) == row, 1.0, 0.0) for row in slot_rows], axis=1
        ).astype(BF16)
        send[:, group * LANES : (group + 1) * LANES] = dot(chosen, values).astype(BF16)
        moved = details if group == 0 else pltpu.roll(details, 8 * group, 1)
        noted = noted + dot(chosen, moved.astype(BF16))
    send[:, 3 * LANES : 4 * LANES] = noted.astype(BF16)


def own_stats(ref, first_row, rows, send, micros):
    width = ref.shape[3]
    sums, squares = [], []
    for micro in range(micros):
        total = fold(ref[micro, first_row])
        for row in range(first_row + 1, first_row + rows):
            total = total + fold(ref[micro, row])
        total = total * (1.0 / (rows * width))
        mean = jnp.sum(total, axis=1, keepdims=True)
        spread = jnp.zeros(total.shape, F32)
        for row in range(first_row, first_row + rows):
            away = ref[micro, row] - mean
            spread = spread + fold(away * away)
        sums.append(total)
        squares.append(spread)
    if sums[0].shape[0] == LANES:
        send_all(send, [row_of(part) for part in sums + squares])
    else:
        send_all(send, [row_of(*sums), row_of(*squares)])


def canvas_kernel(found, l_first, out, kept, send, canvas, *, rows):
    micros = out.shape[0]
    channels, width = out.shape[2:]
    slots = found.shape[0]
    info = found[:, 3 * LANES : 4 * LANES].astype(F32)
    info_t = jnp.transpose(info)
    lane = lax.broadcasted_iota(jnp.int32, (slots, width), 1).astype(F32)
    for group in range(3):
        values = jnp.transpose(found[:, group * LANES : (group + 1) * LANES].astype(F32))
        for micro in range(micros):
            at = group * 8 + micro * 4
            column = info[:, at + 1 : at + 2] * 16.0 + info[:, at + 2 : at + 3]
            where = info_t[at : at + 1]
            mine = values[micro * channels : (micro + 1) * channels]
            placed = jnp.concatenate(
                [jnp.where(where == r + 1.0, mine, 0.0) for r in range(rows)], axis=0
            ).astype(BF16)
            chosen = jnp.where(lane == column, 1.0, 0.0).astype(BF16)
            grid = dot(placed, chosen).astype(BF16)
            canvas[micro, group * rows : (group + 1) * rows] = grid.reshape(rows, channels, width)
    pairs = out.shape[1] // 2

    def step(index, _):
        micro, at = index // pairs, 2 * (index % pairs)
        window = canvas[micro, pl.ds(at, 4)].reshape(4 * channels, width)
        parts = dot(l_first[...], window)
        out[micro, at] = side_sum(parts[: 3 * channels], channels)
        out[micro, at + 1] = side_sum(parts[3 * channels :], channels)
        return 0

    lax.fori_loop(0, micros * pairs, step, 0)
    for micro in range(micros):
        kept[micro] = canvas[micro, rows - 1 : 2 * rows + 1]
    own_stats(out, rows - 1, rows, send, micros)


def second_kernel(place, found, cols, first_out, l_second, out, kept, stats, send, acts, *, rows, tiles):
    micros, high, channels, width = first_out.shape
    tile = place[0]
    mean, rstd = pooled_stats(found[:, 0, :], found[:, 1, :], float(rows * width))
    turned = columns_of([mean, rstd])
    stats[...] = turned
    for micro in range(micros):
        part = slice(micro * channels, (micro + 1) * channels)
        centre = turned[part, 0:1]
        scale = turned[part, 1:2] * cols[0:channels, 2:3]
        shift = cols[0:channels, 3:4]

        def act_row(row, _, micro=micro, centre=centre, scale=scale, shift=shift):
            normed = (first_out[micro, row] - centre) * scale + shift
            on_grid = inside(tile, row - (rows - 1), (tiles, rows))
            acts[micro, row] = (normed * sigmoid(normed) * on_grid).astype(BF16)
            return 0

        lax.fori_loop(0, high, act_row, 0)
        kept[micro] = acts[micro, rows - 2 : 2 * rows]
    pairs = out.shape[1] // 2

    def step(index, _):
        micro, at = index // pairs, 2 * (index % pairs)
        window = acts[micro, pl.ds(at, 4)].reshape(4 * channels, width)
        parts = dot(l_second[...], window)
        out[micro, at] = side_sum(parts[: 3 * channels], channels)
        out[micro, at + 1] = side_sum(parts[3 * channels :], channels)
        return 0

    lax.fori_loop(0, micros * pairs, step, 0)
    own_stats(out, rows - 2, rows, send, micros)


def up_kernel(found, cols, second_out, w_up, out, stats, send, upper, *, rows):
    micros, high, channels, width = second_out.shape
    mean, rstd = pooled_stats(found[:, 0, :], found[:, 1, :], float(rows * width))
    turned = columns_of([mean, rstd])
    stats[...] = turned
    for micro in range(micros):
        part = slice(micro * channels, (micro + 1) * channels)
        centre = turned[part, 0:1]
        scale = turned[part, 1:2] * cols[0:channels, 4:5]
        shift = cols[0:channels, 5:6]

        def act_row(row, _, micro=micro, centre=centre, scale=scale, shift=shift):
            normed = (second_out[micro, row] - centre) * scale + shift
            out[micro, row] = (normed * sigmoid(normed)).astype(BF16)
            return 0

        lax.fori_loop(0, high, act_row, 0)

        def up_row(row, _, micro=micro):
            upper[micro, row] = dot(w_up[...], out[micro, row + (rows - 2)])
            return 0

        lax.fori_loop(0, rows, up_row, 0)
    own_stats(upper, 0, rows, send, micros)


def top_kernel(found, cols, second_act, w_up, before, own, after, features, grads, units, stats, send, *, rows):
    micros, high, channels, width = second_act.shape
    wide = w_up.shape[0]
    lines = []
    for micro in range(micros):
        lines += list(pooled_stats(found[:, micro, :], found[:, micros + micro, :], float(rows * width)))
    turned = columns_of(lines)
    stats[...] = turned
    halo = (high - rows) // 2
    gain_rows, shift_rows = [], []
    gain, shift = cols[:, 6:7], cols[:, 7:8]
    for micro in range(micros):
        centre, rstd = turned[:, 2 * micro : 2 * micro + 1], turned[:, 2 * micro + 1 : 2 * micro + 2]

        def both(row, cot, micro=micro, centre=centre, rstd=rstd):
            unit = (dot(w_up[...], second_act[micro, row]) - centre) * rstd
            normed = unit * gain + shift
            gate = sigmoid(normed)
            act = normed * gate
            grad = cot.astype(F32) * (gate + act * (1.0 - gate))
            grads[micro, row] = grad
            units[micro, row] = unit
            return act, grad, unit

        def edge(row, _, micro=micro, both=both):
            both(row, before[micro, row])
            both(row + halo + rows, after[micro, row])
            return 0

        lax.fori_loop(0, halo, edge, 0)

        def middle(row, carry, micro=micro, both=both):
            act, grad, unit = both(row + halo, own[micro, row])
            features[micro, row] = act.astype(BF16)
            return carry[0] + fold(grad * unit), carry[1] + fold(grad)

        zero = jnp.zeros((wide, LANES), F32)
        gain_sum, shift_sum = lax.fori_loop(0, rows, middle, (zero, zero))
        gain_rows.append(row_of(gain_sum))
        shift_rows.append(row_of(shift_sum))
    send_all(send, gain_rows + shift_rows)


def own_half(row, scene, out):
    size = out.shape[0]
    out[...] = jnp.where(scene == 0, row[:, 0:size], row[:, size : 2 * size]).reshape(size)


def norm_sums(found, lines):
    return [jnp.sum(found[:, index, :], axis=0, keepdims=True) for index in range(lines)]


def second_back_kernel(
    place, found, cols, grads, units, top_stats, second_out, second_stats, w_up_t,
    out, kept, gain_grad, shift_grad, send, *, rows, tiles
):
    scene = place[1]
    micros, high, wide, width = grads.shape
    channels = second_out.shape[2]
    sums = norm_sums(found, 2 * micros)
    own_half(sum(sums[:micros]), scene, gain_grad)
    own_half(sum(sums[micros:]), scene, shift_grad)
    count = found.shape[0] * rows * width
    turned = columns_of(sums) * (1.0 / count)
    halo = (high - rows) // 2
    gain_sums, shift_sums = [], []
    for micro in range(micros):
        factor = cols[:, 6:7] * top_stats[:, 2 * micro + 1 : 2 * micro + 2]
        gain_part = turned[:, micro : micro + 1]
        shift_part = turned[:, micros + micro : micros + micro + 1]
        part = slice(micro * channels, (micro + 1) * channels)
        centre, rstd = second_stats[part, 0:1], second_stats[part, 1:2]
        gain, shift = cols[0:channels, 4:5], cols[0:channels, 5:6]

        def both(row, micro=micro, factor=factor, gain_part=gain_part, shift_part=shift_part,
                 centre=centre, rstd=rstd, gain=gain, shift=shift):
            low = factor * (grads[micro, row] - shift_part - units[micro, row] * gain_part)
            low = low.astype(BF16)
            unit = (second_out[micro, row] - centre) * rstd
            normed = unit * gain + shift
            gate = sigmoid(normed)
            grad = dot(w_up_t[...], low) * (gate + normed * gate * (1.0 - gate))
            out[micro, row] = grad
            return low, grad, unit

        def edge(row, _, both=both):
            both(row)
            both(row + halo + rows)
            return 0

        lax.fori_loop(0, halo, edge, 0)

        def middle(row, carry, micro=micro, both=both):
            low, grad, unit = both(row + halo)
            kept[micro, row] = low
            return carry[0] + fold(grad * unit), carry[1] + fold(grad)

        zero = jnp.zeros((channels, LANES), F32)
        gain_sum, shift_sum = lax.fori_loop(0, rows, middle, (zero, zero))
        gain_sums.append(gain_sum)
        shift_sums.append(shift_sum)
    send_all(send, [row_of(*gain_sums), row_of(*shift_sums)])


def low_rows(sums, grads, values, value_stats, gain, low, tile, halo, value_halo, rows, tiles, count):
    micros, high, channels, width = grads.shape
    turned = columns_of(sums) * (1.0 / count)
    for micro in range(micros):
        part = slice(micro * channels, (micro + 1) * channels)
        centre, rstd = value_stats[part, 0:1], value_stats[part, 1:2]
        gain_part, shift_part = turned[part, 0:1], turned[part, 1:2]
        factor = gain * rstd

        def one(row, _, micro=micro, centre=centre, rstd=rstd, gain_part=gain_part, shift_part=shift_part,
                factor=factor):
            unit = (values[micro, row + (value_halo - halo)] - centre) * rstd
            grad = factor * (grads[micro, row] - shift_part - unit * gain_part)
            low[micro, row] = (grad * inside(tile, row - halo, (tiles, rows))).astype(BF16)
            return 0

        lax.fori_loop(0, high, one, 0)


def first_back_kernel(
    place, found, cols, grads, second_out, second_stats, first_out, first_stats, b_second,
    out, kept, gain_grad, shift_grad, send, low, *, rows, tiles
):
    tile, scene = place[0], place[1]
    micros, high, channels, width = grads.shape
    sums = norm_sums(found, 2)
    own_half(sums[0][:, :channels] + sums[0][:, channels:], scene, gain_grad)
    own_half(sums[1][:, :channels] + sums[1][:, channels:], scene, shift_grad)
    count = found.shape[0] * rows * width
    halo = (high - rows) // 2
    low_rows(sums, grads, second_out, second_stats, cols[0:channels, 4:5], low, tile, halo, halo, rows,
             tiles, count)
    for micro in range(micros):
        kept[micro] = low[micro, halo : halo + rows]
    pairs = out.shape[1] // 2
    gain, shift = cols[0:channels, 2:3], cols[0:channels, 3:4]
    gain_sums, shift_sums = [], []
    for micro in range(micros):
        part = slice(micro * channels, (micro + 1) * channels)
        centre, rstd = first_stats[part, 0:1], first_stats[part, 1:2]

        def step(index, carry, micro=micro, centre=centre, rstd=rstd):
            at = 2 * index
            window = low[micro, pl.ds(at, 4)].reshape(4 * channels, width)
            parts = dot(b_second[...], window)
            gain_sum, shift_sum = carry
            for j in range(2):
                grad_act = side_sum(parts[3 * channels * j : 3 * channels * (j + 1)], channels)
                unit = (first_out[micro, at + j + 2] - centre) * rstd
                normed = unit * gain + shift
                gate = sigmoid(normed)
                grad = grad_act * (gate + normed * gate * (1.0 - gate))
                out[micro, at + j] = grad
                own = jnp.where((at + j >= 1) & (at + j <= rows), 1.0, 0.0)
                gain_sum = gain_sum + own * fold(grad * unit)
                shift_sum = shift_sum + own * fold(grad)
            return gain_sum, shift_sum

        zero = jnp.zeros((channels, LANES), F32)
        gain_sum, shift_sum = lax.fori_loop(0, pairs, step, (zero, zero))
        gain_sums.append(gain_sum)
        shift_sums.append(shift_sum)
    send_all(send, [row_of(*gain_sums), row_of(*shift_sums)])


def pick_kernel(
    place, found, cols, grads, first_out, first_stats, b_first, arrived,
    send, kept, gain_grad, shift_grad, low, grid, *, rows, tiles
):
    tile, scene = place[0], place[1]
    micros, high, channels, width = grads.shape
    sums = norm_sums(found, 2)
    own_half(sums[0][:, :channels] + sums[0][:, channels:], scene, gain_grad)
    own_half(sums[1][:, :channels] + sums[1][:, channels:], scene, shift_grad)
    count = found.shape[0] * rows * width
    low_rows(sums, grads, first_out, first_stats, cols[0:channels, 2:3], low, tile, 1, 3, rows, tiles, count)
    for micro in range(micros):
        kept[micro] = low[micro, 1 : 1 + rows]

    def step(index, _):
        micro, at = index // (rows // 2), 2 * (index % (rows // 2))
        window = low[micro, pl.ds(at, 4)].reshape(4 * channels, width)
        parts = dot(b_first[...], window)
        grid[micro, at] = side_sum(parts[: 3 * channels], channels).astype(BF16)
        grid[micro, at + 1] = side_sum(parts[3 * channels :], channels).astype(BF16)
        return 0

    lax.fori_loop(0, micros * (rows // 2), step, 0)
    slots = arrived.shape[0]
    info = arrived[:, 3 * LANES : 4 * LANES].astype(F32)
    info_t = jnp.transpose(info)
    lane = lax.broadcasted_iota(jnp.int32, (slots, width), 1).astype(F32)
    picked = []
    for micro in range(micros):
        at = 8 + micro * 4
        column = info[:, at + 1 : at + 2] * 16.0 + info[:, at + 2 : at + 3]
        where = info_t[at : at + 1]
        chosen = jnp.where(lane == column, 1.0, 0.0).astype(BF16)
        found_here = dot_lanes(grid[micro].reshape(rows * channels, width), chosen)
        total = jnp.zeros((channels, slots), F32)
        for r in range(rows):
            total = total + jnp.where(where == r + 1.0, found_here[r * channels : (r + 1) * channels], 0.0)
        picked.append(total)
    send[...] = jnp.transpose(jnp.concatenate(picked, axis=0)).astype(BF16)


def grads_kernel(up_low, second_act, second_low, first_act, first_low, canvas, send, total, *, rows, tiles):
    micros, _, channels, width = canvas.shape
    lane = lax.broadcasted_iota(jnp.int32, (channels, width), 1)
    each = send.shape[2]
    halves = [[], []]
    for low, values in ((first_low, canvas), (second_low, first_act)):

        def step(index, carry, low=low, values=values):
            micro, row = index // rows, index % rows
            grad = low[micro, row].astype(F32)
            left = jnp.where(lane < width - 1, pltpu.roll(grad, width - 1, 1), 0.0)
            right = jnp.where(lane > 0, pltpu.roll(grad, 1, 1), 0.0)
            stacked = jnp.concatenate([left, grad, right], axis=0).astype(BF16)
            window = values[micro, pl.ds(row, 3)].reshape(3 * channels, width)
            total[...] = total[...] + dot_lanes(stacked, window)
            return carry

        total[...] = jnp.zeros(total.shape, F32)
        lax.fori_loop(0, micros * rows, step, 0)
        half = channels // 2
        for s in range(2):
            mine = jnp.concatenate(
                [total[b * channels + s * half : b * channels + (s + 1) * half, :] for b in range(3)], axis=0
            )
            wing = mine[:, LANES:]
            cut = wing.shape[0] // 2
            halves[s] += [mine[:, :LANES], jnp.concatenate([wing[:cut], wing[cut:]], axis=1)]
    up = jnp.zeros((up_low.shape[2], channels), F32)
    skip = (second_act.shape[1] - rows) // 2
    for micro in range(micros):
        for row in range(rows):
            up = up + dot_lanes(up_low[micro, row], second_act[micro, row + skip])
    for s in range(2):
        mine = up[s * channels : (s + 1) * channels]
        halves[s].append(jnp.concatenate([mine[: channels // 2], mine[channels // 2 :]], axis=1))
        whole = jnp.concatenate(halves[s], axis=0)
        for t in range(tiles):
            first, last = t * each, min((t + 1) * each, whole.shape[0])
            if last <= first:
                send[t, s] = jnp.zeros((each, LANES), F32)
            elif last - first < each:
                send[t, s, 0 : last - first] = whole[first:last]
                send[t, s, last - first :] = jnp.zeros((each - (last - first), LANES), F32)
            else:
                send[t, s] = whole[first:last]


def gate_parts(normed):
    gate = sigmoid(normed)
    act = normed * gate
    return act, gate + act * (1.0 - gate)


def pillar_back_kernel(
    found, points, counts, w_pillar, cols, pooled, stats, slots, send, grads, lifted, wide
):
    micros, _, inputs, depth, pillars = points.shape
    channels = w_pillar.shape[0]
    turned = jnp.transpose(found[...].astype(F32))
    slot_count = found.shape[0]
    place = lax.broadcasted_iota(jnp.int32, (slot_count, pillars), 0).astype(F32)
    gain_sums, shift_sums = [], []
    outer = jnp.zeros((inputs, channels), F32)
    for micro in range(micros):
        rows = point_rows(points, micro, wide).astype(BF16)
        lifted[micro] = dot(w_pillar[...], rows)
        chosen = jnp.where(place == slots[micro : micro + 1], 1.0, 0.0).astype(BF16)
        back = dot(turned[micro * channels : (micro + 1) * channels].astype(BF16), chosen)
        centre, rstd = stats[micro, :, 0:1], stats[micro, :, 1:2]
        gain, shift = cols[0:channels, 0:1], cols[0:channels, 1:2]
        limit = counts[micro]
        pool = pooled[micro]
        gain_sum = jnp.zeros((channels, pillars), F32)
        shift_sum = jnp.zeros((channels, pillars), F32)
        for n in range(depth):
            piece = slice(n * pillars, (n + 1) * pillars)
            unit = (lifted[micro, :, piece] - centre) * rstd
            act, slope = gate_parts(unit * gain + shift)
            grad = jnp.where(limit > n, back * jnp.exp(act - pool) * slope, 0.0)
            grads[micro, :, piece] = grad
            gain_sum = gain_sum + grad * unit
            shift_sum = shift_sum + grad
        gain_sums.append(gain_sum)
        shift_sums.append(shift_sum)
        scale = jnp.broadcast_to(rstd * gain, (channels, LANES))
        scale_row = jnp.transpose(scale)[0:1]
        outer = outer + dot_lanes(rows, grads[micro].astype(BF16)) * scale_row
    side = jnp.concatenate([outer[6:inputs], jnp.zeros((9 - inputs + 3, channels), F32)], axis=0)
    block = jnp.concatenate(
        [row_of(*gain_sums), row_of(*shift_sums), jnp.concatenate([outer[0:6], side], axis=1)], axis=0
    )
    send[...] = jnp.broadcast_to(block[None], send.shape)


def sum_kernel(found, out):
    total = jnp.sum(found[...], axis=0)
    out[...] = jnp.broadcast_to(total[None], out.shape)


def last_kernel(
    place, found, halves, counts, w_pillar, cols, stats, grads, lifted,
    points_grad, pillar_grad, gain_grad, shift_grad, first_grad, second_grad, up_grad
):
    scene = place[1]
    micros, channels, _ = grads.shape
    _, _, inputs, depth, pillars = points_grad.shape
    half = channels // 2
    total = jnp.sum(found[...], axis=0)
    own_half(total[0:1, :channels] + total[0:1, channels:], scene, gain_grad)
    own_half(total[1:2, :channels] + total[1:2, channels:], scene, shift_grad)
    turned = columns_of([total[0:1], total[1:2]])
    outer = jnp.concatenate([total[2:8, :channels], total[2 : 2 + inputs - 6, channels:]], axis=0)
    outer = jnp.concatenate([outer, jnp.zeros((16 - inputs, channels), F32)], axis=0)
    weight_grad = jnp.transpose(outer)[:, 0:inputs]
    weight = jnp.transpose(w_pillar[...].astype(F32)).astype(BF16)
    for micro in range(micros):
        part = slice(micro * channels, (micro + 1) * channels)
        centre, rstd, inverse = stats[micro, :, 0:1], stats[micro, :, 1:2], stats[micro, :, 2:3]
        factor = cols[0:channels, 0:1] * rstd
        gain_part, shift_part = turned[part, 0:1], turned[part, 1:2]
        spun, mean = stats[micro, :, 16 : 16 + inputs], stats[micro, :, 32 : 32 + inputs]
        weight_grad = weight_grad - factor * (shift_part * mean + gain_part * rstd * spun)
        limit = counts[micro]
        gain_part, shift_part = gain_part * inverse, shift_part * inverse
        for n in range(depth):
            piece = slice(n * pillars, (n + 1) * pillars)
            unit = (lifted[micro, :, piece] - centre) * rstd
            low = factor * (grads[micro, :, piece] - shift_part - unit * gain_part)
            low = jnp.where(limit > n, low, 0.0).astype(BF16)
            points_grad[micro, 0, :, n, :] = dot(weight, low)
    pillar_grad[...] = jnp.where(scene == 0, weight_grad[:half], weight_grad[half:])
    whole = halves[...].reshape(-1, LANES)
    for index, out in enumerate((first_grad, second_grad)):
        base = index * 9 * half * channels // LANES
        lead = 3 * half
        mine = whole[base : base + lead]
        wing = whole[base + lead : base + lead + lead // 2]
        wing = jnp.concatenate([wing[:, :channels], wing[:, channels:]], axis=0)
        both = jnp.concatenate([mine, wing], axis=1)
        for a in range(3):
            for b in range(3):
                at = (3 * a + b) * channels
                out[:, at : at + channels] = both[b * half : (b + 1) * half, a * channels : (a + 1) * channels]
    base = 2 * 9 * half * channels // LANES
    top = whole[base : base + half]
    up_grad[...] = jnp.concatenate([top[:, :channels], top[:, channels:]], axis=0)


def swap(blocks, axes):
    return lax.all_to_all(blocks, axes, split_axis=0, concat_axis=0)


def shards(
    points, point_counts, pillar_tile, pillar_cell,
    pillar_weight, pillar_gain, pillar_shift,
    first_weight, first_gain, first_shift,
    second_weight, second_gain, second_shift,
    up_weight, up_gain, up_shift, cotangent,
):
    micros, _, inputs, depth, pillars = points.shape
    channels = up_weight.shape[1]
    upper = cotangent.shape[2]
    rows, width = cotangent.shape[3:]
    tiles = lax.axis_size("tile")
    scenes = lax.axis_size("scene")
    peers = tiles * scenes
    capacity = 2 * pillars // tiles
    slot_count = tiles * capacity
    tile = lax.axis_index("tile")
    scene = lax.axis_index("scene")
    place = jnp.stack([tile, scene]).astype(jnp.int32)
    half = channels // 2
    high = 3 * rows

    (moments,) = run(
        moments_kernel, [((peers, 8, LANES), F32)], points, point_counts,
        scratch=[pltpu.VMEM((inputs * depth, pillars), F32)],
    )
    moments = swap(moments, BOTH)
    (packed,) = run(
        pack_kernel, [((3 * half + 16, 10 * channels), BF16)],
        first_weight, second_weight, up_weight, pillar_weight,
        pillar_gain, pillar_shift, first_gain, first_shift, second_gain, second_shift, up_gain, up_shift,
    )
    both = lax.all_gather(packed, "scene")
    taps = ((6 * channels, 4 * channels), BF16)
    w_pillar, cols, l_first, l_second, b_first, b_second, w_up, w_up_t = run(
        unpack_kernel,
        [
            ((channels, inputs), BF16), ((LANES, 8), F32), taps, taps, taps, taps,
            ((upper, channels), BF16), ((channels, upper), BF16),
        ],
        both,
    )
    top = cotangent[:, 0].transpose(0, 2, 1, 3)
    reach = rows // 2
    up_pairs = [(i, i + 1) for i in range(tiles - 1)]
    before = lax.ppermute(top[:, rows - reach :], "tile", up_pairs)
    after = lax.ppermute(top[:, :reach], "tile", [(j, i) for i, j in up_pairs])

    send, pooled, pillar_stats, slots = run(
        functools.partial(pillar_kernel, capacity=capacity, width=width),
        [
            ((slot_count, 4 * LANES), BF16), ((micros, channels, pillars), F32),
            ((micros, channels, LANES), F32), ((8, pillars), F32),
        ],
        moments, points, point_counts, pillar_tile, pillar_cell, w_pillar, cols,
        scratch=[
            pltpu.VMEM((inputs * depth, pillars), F32),
            pltpu.VMEM((channels, depth * pillars), F32),
            pltpu.VMEM((channels, depth * pillars), F32),
        ],
    )
    arrived = swap(send.reshape(tiles, capacity, 4 * LANES), "tile").reshape(slot_count, 4 * LANES)

    first_out, canvas, send = run(
        functools.partial(canvas_kernel, rows=rows),
        [
            ((micros, high - 2, channels, width), F32), ((micros, rows + 2, channels, width), BF16),
            ((peers, 2, LANES), F32),
        ],
        arrived, l_first,
        scratch=[pltpu.VMEM((micros, high, channels, width), BF16)],
    )
    second_out, first_act, first_stats, send = run(
        functools.partial(second_kernel, rows=rows, tiles=tiles),
        [
            ((micros, high - 4, channels, width), F32), ((micros, rows + 2, channels, width), BF16),
            ((LANES, 8), F32), ((peers, 2, LANES), F32),
        ],
        place, swap(send, BOTH), cols, first_out, l_second,
        smem=(0,),
        scratch=[pltpu.VMEM((micros, high - 2, channels, width), BF16)],
    )
    second_act, second_stats, send = run(
        functools.partial(up_kernel, rows=rows),
        [((micros, high - 4, channels, width), BF16), ((LANES, 8), F32), ((peers, 4, LANES), F32)],
        swap(send, BOTH), cols, second_out, w_up,
        scratch=[pltpu.VMEM((micros, rows, upper, width), F32)],
    )
    features, grads, units, top_stats, send = run(
        functools.partial(top_kernel, rows=rows),
        [
            ((micros, rows, upper, width), BF16), ((micros, high - 4, upper, width), F32),
            ((micros, high - 4, upper, width), F32), ((LANES, 8), F32), ((peers, 4, LANES), F32),
        ],
        swap(send, BOTH), cols, second_act, w_up, before, top, after,
    )
    features = features.transpose(0, 2, 1, 3)[:, None]
    vector = ((half,), F32)
    second_dz, up_low, up_gain_grad, up_shift_grad, send = run(
        functools.partial(second_back_kernel, rows=rows, tiles=tiles),
        [
            ((micros, high - 4, channels, width), F32), ((micros, rows, upper, width), BF16),
            ((upper // 2,), F32), ((upper // 2,), F32), ((peers, 2, LANES), F32),
        ],
        place, swap(send, BOTH), cols, grads, units, top_stats, second_out, second_stats, w_up_t,
        smem=(0,),
    )
    first_dz, second_low, second_gain_grad, second_shift_grad, send = run(
        functools.partial(first_back_kernel, rows=rows, tiles=tiles),
        [
            ((micros, high - 6, channels, width), F32), ((micros, rows, channels, width), BF16),
            vector, vector, ((peers, 2, LANES), F32),
        ],
        place, swap(send, BOTH), cols, second_dz, second_out, second_stats, first_out, first_stats, b_second,
        smem=(0,),
        scratch=[pltpu.VMEM((micros, high - 4, channels, width), BF16)],
    )
    send, first_low, first_gain_grad, first_shift_grad = run(
        functools.partial(pick_kernel, rows=rows, tiles=tiles),
        [((slot_count, LANES), BF16), ((micros, rows, channels, width), BF16), vector, vector],
        place, swap(send, BOTH), cols, first_dz, first_out, first_stats, b_first, arrived,
        smem=(0,),
        scratch=[
            pltpu.VMEM((micros, high - 6, channels, width), BF16),
            pltpu.VMEM((micros, rows, channels, width), BF16),
        ],
    )
    returned = swap(send.reshape(tiles, capacity, LANES), "tile").reshape(slot_count, LANES)
    length = (2 * 9 * half * channels + upper * channels // 2) // LANES
    each = -(-length // (8 * tiles)) * 8
    (send,) = run(
        functools.partial(grads_kernel, rows=rows, tiles=tiles),
        [((tiles, scenes, each, LANES), F32)],
        up_low, second_act, second_low, first_act, first_low, canvas,
        scratch=[pltpu.VMEM((3 * channels, 3 * channels), F32)],
        cost=pl.CostEstimate(flops=10**9, bytes_accessed=10**7, transcendentals=0),
    )
    own = swap(send.reshape(peers, each, LANES), BOTH)
    send, pillar_dz, lifted = run(
        pillar_back_kernel,
        [
            ((peers, 8, LANES), F32), ((micros, channels, depth * pillars), F32),
            ((micros, channels, depth * pillars), F32),
        ],
        returned, points, point_counts, w_pillar, cols, pooled, pillar_stats, slots,
        scratch=[pltpu.VMEM((inputs * depth, pillars), F32)],
    )
    (summed,) = run(sum_kernel, [((tiles, each, LANES), F32)], own)
    halves = swap(summed, "tile")
    points_grad, pillar_grad, pillar_gain_grad, pillar_shift_grad, first_grad, second_grad, up_grad = run(
        last_kernel,
        [
            ((micros, 1, inputs, depth, pillars), F32), ((half, inputs), F32), vector, vector,
            ((half, 9 * channels), F32), ((half, 9 * channels), F32), ((upper // 2, channels), F32),
        ],
        place, swap(send, BOTH), halves, point_counts, w_pillar, cols, pillar_stats, pillar_dz, lifted,
        smem=(0,),
    )
    return (
        features, points_grad,
        pillar_grad, pillar_gain_grad, pillar_shift_grad,
        first_grad, first_gain_grad, first_shift_grad,
        second_grad, second_gain_grad, second_shift_grad,
        up_grad, up_gain_grad, up_shift_grad,
    )


def solution(mesh):
    matrix, vector = P("scene", None), P("scene")
    grid = P(None, "scene", None, "tile", None)
    cloud = P(None, "scene", None, None, "tile")
    pillar = P(None, "scene", "tile")
    weights = (matrix, vector, vector) * 4
    return jax.shard_map(
        shards,
        mesh=mesh,
        in_specs=(cloud, pillar, pillar, pillar) + weights + (grid,),
        out_specs=(grid, cloud) + weights,
        check_vma=False,
    )
```

```python
import functools

import jax
import jax.numpy as jnp
from jax import lax
from jax.experimental import pallas as pl
from jax.experimental.pallas import tpu as pltpu
from jax.sharding import PartitionSpec as P

norm_eps = 0.001
BOTH = ("tile", "scene")
F32 = jnp.float32
BF16 = jnp.bfloat16
VMEM_LIMIT = 24 * 1024 * 1024
LANES = 128


def run(kernel, outs, *args, hbm=(), scratch=(), copies=0, cost=None):
    specs = [
        pl.BlockSpec(memory_space=pltpu.HBM if index in hbm else pltpu.VMEM) for index in range(len(args))
    ]
    scratch = list(scratch)
    if copies:
        scratch.append(pltpu.SemaphoreType.DMA((copies,)))
    return pl.pallas_call(
        kernel,
        out_shape=[jax.ShapeDtypeStruct(out[0], out[1]) for out in outs],
        in_specs=specs,
        out_specs=[
            pl.BlockSpec(memory_space=pltpu.HBM if len(out) > 2 else pltpu.VMEM) for out in outs
        ],
        scratch_shapes=scratch,
        compiler_params=pltpu.CompilerParams(vmem_limit_bytes=VMEM_LIMIT),
        cost_estimate=cost,
    )(*args)


def move(source, target, sems, index):
    copy = pltpu.make_async_copy(source, target, sems.at[index])
    copy.start()
    return copy


def dot(left, right, precision=None):
    return jnp.dot(left, right, preferred_element_type=F32, precision=precision)


def dot_lanes(left, right, precision=None):
    return lax.dot_general(
        left, right, (((1,), (1,)), ((), ())), preferred_element_type=F32, precision=precision
    )


def sigmoid(values):
    return 0.5 + 0.5 * jnp.tanh(0.5 * values)


def fold(values):
    total = values[:, :LANES]
    for start in range(LANES, values.shape[1], LANES):
        total = total + values[:, start : start + LANES]
    return total


def row_of(left, right=None):
    both = left if right is None else jnp.concatenate([left, right], axis=0)
    return jnp.sum(jnp.transpose(both), axis=0, keepdims=True)


def columns_of(rows):
    rows = rows + [jnp.zeros((8 - len(rows), LANES), F32)] if len(rows) < 8 else rows
    return jnp.transpose(jnp.concatenate(rows, axis=0))


def inside(tile, row, height):
    tiles, rows = height
    place = tile * rows + row
    return jnp.where((place >= 0) & (place < tiles * rows), 1.0, 0.0).astype(F32)


def send_all(ref, rows):
    for index, row in enumerate(rows):
        ref[:, index : index + 1, :] = jnp.broadcast_to(row[None], (ref.shape[0], 1, LANES))


def pooled_stats(means, squares, count):
    peers = means.shape[0]
    mean = jnp.sum(means, axis=0, keepdims=True) * (1.0 / peers)
    away = means - mean
    spread = jnp.sum(squares + count * away * away, axis=0, keepdims=True) * (1.0 / (peers * count))
    return mean, lax.rsqrt(spread + norm_eps)


def half_stats(found, count):
    both = found[:, 0, :]
    mean, rstd = pooled_stats(both, pltpu.roll(both, LANES // 2, 1), count)
    return columns_of([mean, rstd])


def half_sums(found):
    row = jnp.sum(found[:, 0, :], axis=0, keepdims=True)
    return row, columns_of([row])


def side_sum(stacked, channels):
    width = stacked.shape[1]
    lane = lax.broadcasted_iota(jnp.int32, (channels, width), 1)
    left = pltpu.roll(stacked[:channels], 1, 1)
    right = pltpu.roll(stacked[2 * channels :], width - 1, 1)
    return (
        stacked[channels : 2 * channels]
        + jnp.where(lane > 0, left, 0.0)
        + jnp.where(lane < width - 1, right, 0.0)
    )


def layout(half, channels, inputs, depth):
    first = 0
    second = first + half * -(-9 * channels // LANES)
    up = second + half * -(-9 * channels // LANES)
    pillar = up + channels
    vectors = pillar + half
    points = vectors + 16
    return first, second, up, pillar, vectors, points


def widen(value):
    missing = LANES - value.shape[1]
    if missing == 0:
        return value
    return jnp.concatenate([value, jnp.zeros((value.shape[0], missing), value.dtype)], axis=1)


def pack_kernel(*refs):
    count = 15
    sources, out, held, sems = refs[:count], refs[count], refs[count + 1 : 2 * count + 1], refs[-1]
    copies = [move(sources[i], held[i], sems, i) for i in range(count)]
    for copy in copies:
        copy.wait()
    first, second, up, pillar, points, counts, tiles = held[:7]
    micros, _, inputs, depth, pillars = points.shape
    half, channels = first.shape[0], up.shape[1]
    starts = layout(half, channels, inputs, depth)
    for ref, start in ((first, starts[0]), (second, starts[1])):
        for j in range(-(-9 * channels // LANES)):
            out[start + j * half : start + (j + 1) * half, :] = widen(
                ref[:, j * LANES : min((j + 1) * LANES, 9 * channels)]
            )
    out[starts[2] : starts[2] + channels, :] = widen(up[...])
    out[starts[3] : starts[3] + half, :] = widen(pillar[...].astype(F32)).astype(BF16)
    rows = [widen(vector[...].astype(F32).reshape(1, -1)) for vector in held[7:]]
    for micro in range(micros):
        rows += [widen(counts[micro].astype(F32)), widen(tiles[micro].astype(F32))]
    rows.append(jnp.zeros((16 - len(rows), LANES), F32))
    out[starts[4] : starts[4] + 16, :] = jnp.concatenate(rows, axis=0).astype(BF16)
    size = inputs * depth
    for micro in range(micros):
        out[starts[5] + micro * size : starts[5] + (micro + 1) * size, :] = points[micro, 0].reshape(
            size, pillars
        )


def unpack_kernel(
    both, w_pillar, cols, l_first, l_second, b_first, b_second, w_up, w_up_t,
    h_second, h_first_back, h_second_back, sems, *, inputs, depth
):
    half = w_pillar.shape[0] // 2
    channels = 2 * half
    starts = layout(half, channels, inputs, depth)
    tiles = -(-9 * channels // LANES)

    def wide(start):
        return jnp.concatenate(
            [
                jnp.concatenate(
                    [both[s, start + j * half : start + (j + 1) * half, :] for j in range(tiles)], axis=1
                )
                for s in range(2)
            ],
            axis=0,
        ).astype(F32)

    up = jnp.concatenate(
        [both[s, starts[2] : starts[2] + channels, 0:channels] for s in range(2)], axis=0
    )
    w_up[...] = up
    w_up_t[...] = jnp.transpose(up.astype(F32)).astype(BF16)
    w_pillar[...] = jnp.concatenate(
        [both[s, starts[3] : starts[3] + half, 0:inputs] for s in range(2)], axis=0
    )
    vectors = [both[s, starts[4] : starts[4] + 16, :].astype(F32) for s in range(2)]
    rows = []
    for index in range(8):
        size = half if index < 6 else channels
        row = jnp.concatenate([vectors[s][index : index + 1, 0:size] for s in range(2)], axis=1)
        rows.append(jnp.concatenate([row] * (LANES // (2 * size)), axis=1))
    cols[...] = columns_of(rows)
    zero = jnp.zeros((channels, channels), F32)
    copies = []
    for weight, ahead, back in (
        (wide(starts[0]), l_first, h_first_back), (wide(starts[1]), h_second, h_second_back)
    ):
        pieces = [
            [weight[:, (3 * a + b) * channels : (3 * a + b + 1) * channels] for b in range(3)]
            for a in range(3)
        ]
        flipped = [[jnp.transpose(pieces[a][b]) for b in range(3)] for a in range(3)]
        for j in range(2):
            for b in range(3):
                start = (3 * j + b) * channels
                ahead[start : start + channels, :] = jnp.concatenate(
                    [pieces[r - j][b] if 0 <= r - j <= 2 else zero for r in range(4)], axis=1
                ).astype(BF16)
                back[start : start + channels, :] = jnp.concatenate(
                    [flipped[j + 2 - r][2 - b] if 0 <= j + 2 - r <= 2 else zero for r in range(4)],
                    axis=1,
                ).astype(BF16)
    copies.append(move(h_second, l_second, sems, 0))
    copies.append(move(h_first_back, b_first, sems, 1))
    copies.append(move(h_second_back, b_second, sems, 2))
    for copy in copies:
        copy.wait()


def slot_line(wide, depth, inputs):
    return jnp.concatenate([wide[pl.ds(n, inputs, stride=depth), :] for n in range(depth)], axis=1)


def slot_mask(count, depth):
    return jnp.concatenate([jnp.where(count > n, 1.0, 0.0) for n in range(depth)], axis=1)


def ranks(tile):
    pillars = tile.shape[1]
    across = jnp.broadcast_to(tile, (pillars, pillars))
    down = jnp.transpose(across)
    row = lax.broadcasted_iota(jnp.int32, (pillars, pillars), 0)
    col = lax.broadcasted_iota(jnp.int32, (pillars, pillars), 1)
    return jnp.sum(jnp.where((across == down) & (row < col), 1.0, 0.0), axis=0, keepdims=True)


def moments_kernel(points_in, counts_in, tiles_in, cells_in, out, points, counts, tiles, cells, wide, sems,
                   *, capacity):
    copies = [
        move(source, target, sems, index)
        for index, (source, target) in enumerate(
            ((tiles_in, tiles), (cells_in, cells), (counts_in, counts), (points_in, points))
        )
    ]
    micros, _, inputs, depth, pillars = points.shape
    peers = out.shape[0]
    copies[0].wait()
    copies[1].wait()
    for micro in range(micros):
        tile = tiles[micro].astype(F32)
        cell = (cells[micro] + 1).astype(F32)
        high = jnp.floor(cell * (1.0 / 16.0))
        low = cell - high * 16.0
        rank = ranks(tile)
        spot = lax.broadcasted_iota(jnp.int32, (capacity, pillars), 0).astype(F32)
        placed = jnp.where(spot == rank, 1.0, 0.0).astype(BF16)
        peer = lax.broadcasted_iota(jnp.int32, (peers, pillars), 0).astype(F32)
        lines = []
        for group in range(3):
            named = tile == peer + (group - 1.0)
            lines.append(
                16.0 * dot_lanes(jnp.where(named, high, 0.0).astype(BF16), placed)
                + dot_lanes(jnp.where(named, low, 0.0).astype(BF16), placed)
            )
        line = jnp.concatenate(lines + [jnp.zeros((peers, LANES - 3 * capacity), F32)], axis=1)
        out[:, micro, 1:2, :] = line.reshape(peers, 1, LANES)
    copies[2].wait()
    copies[3].wait()
    for micro in range(micros):
        wide[...] = points[micro, 0].astype(F32).reshape(inputs * depth, pillars)
        rows = slot_line(wide, depth, inputs)
        mask = slot_mask(counts[micro], depth)
        total = jnp.sum(mask, axis=1, keepdims=True)
        mean = jnp.sum(rows * mask, axis=1, keepdims=True) / total
        centred = (rows - mean) * mask
        products = dot_lanes(centred, centred, lax.Precision.HIGHEST)
        lane = lax.broadcasted_iota(jnp.int32, (inputs, inputs), 1)
        diagonal = lax.broadcasted_iota(jnp.int32, (inputs, inputs), 0) == lane
        mean_row = jnp.sum(jnp.where(diagonal, mean, 0.0), axis=0, keepdims=True)
        row = jnp.concatenate(
            [products[k : k + 1] for k in range(inputs)]
            + [mean_row, total, jnp.zeros((1, LANES - inputs * inputs - inputs - 1), F32)],
            axis=1,
        )
        out[:, micro, 0:1, :] = jnp.broadcast_to(row[None], (peers, 1, LANES))


def cells_kernel(found, columns, rows, *, capacity):
    slots = columns.shape[0]
    peers = found.shape[0]
    values = found[:, 1, :]
    slot = lax.broadcasted_iota(jnp.int32, (slots, peers), 0)
    peer = lax.broadcasted_iota(jnp.int32, (slots, peers), 1)
    lane = lax.broadcasted_iota(jnp.int32, (slots, LANES), 1)
    row = lax.broadcasted_iota(jnp.int32, (slots, LANES), 0)
    result = jnp.zeros((slots, LANES), F32)
    for scene in range(2):
        chosen = jnp.where(peer == 2 * (slot // capacity) + scene, 1.0, 0.0)
        spread = dot(chosen, values, lax.Precision.HIGHEST)
        for group in range(3):
            mine = jnp.where(lane == group * capacity + row % capacity, spread, 0.0)
            column = jnp.sum(mine, axis=1, keepdims=True)
            result = jnp.where(lane == 2 * group + scene, column, result)
    columns[...] = result
    rows[...] = jnp.transpose(result)[0:8]


def pillar_kernel(
    found, both, w_pillar, cols, send, pooled, stats, slots, kept, wide, lifted, acts, lines, sems,
    *, capacity, inputs, depth
):
    core = lax.axis_index("scene")
    peers = found.shape[0]
    channels, pillars = pooled.shape[1:]
    starts = layout(channels // 2, channels, inputs, depth)
    weight = w_pillar[...]
    wide_weight = weight.astype(F32)
    rows_out = send.shape[0]
    size = inputs * depth
    square = inputs * inputs

    moments = found[:, 0, :]
    counts = moments[:, square + inputs : square + inputs + 1]
    means = moments[:, square : square + inputs]
    count = jnp.sum(counts, axis=0, keepdims=True)
    mean = jnp.sum(means * counts, axis=0, keepdims=True) / count
    away = means - mean
    products = lax.dot_general(
        away * counts, away, (((0,), (0,)), ((), ())),
        preferred_element_type=F32, precision=lax.Precision.HIGHEST,
    )
    summed = jnp.sum(moments, axis=0, keepdims=True)
    products = products + jnp.concatenate(
        [summed[:, k * inputs : (k + 1) * inputs] for k in range(inputs)], axis=0
    )
    cov = products / count
    spun = wide_weight[:, 0:1] * cov[0:1]
    for k in range(1, inputs):
        spun = spun + wide_weight[:, k : k + 1] * cov[k : k + 1]
    spread = jnp.sum(spun * wide_weight, axis=1, keepdims=True)
    centre = jnp.sum(wide_weight * mean, axis=1, keepdims=True)
    rstd = lax.rsqrt(spread + norm_eps)
    inverse = jnp.broadcast_to(1.0 / count, (channels, 1))
    stats[...] = jnp.concatenate(
        [
            centre, rstd, inverse, jnp.zeros((channels, 13), F32),
            spun, jnp.zeros((channels, 16 - inputs), F32),
            jnp.broadcast_to(mean, (channels, inputs)), jnp.zeros((channels, LANES - 32 - inputs), F32),
        ],
        axis=1,
    )
    scale = rstd * cols[0:channels, 0:1]
    shift = cols[0:channels, 1:2]
    stacked, slot_rows, limits, copies = [], [], [], []
    for scene in range(2):
        start = pl.multiple_of(starts[5] + core * size, 16)
        wide[...] = both[scene, pl.ds(start, size), :].astype(F32)
        rows = slot_line(wide, depth, inputs)
        low = jnp.concatenate([rows, jnp.zeros((16 - inputs, rows.shape[1]), F32)], axis=0).astype(BF16)
        lines[scene] = low
        copies.append(move(lines.at[scene], kept.at[scene], sems, scene))
        lifted[...] = dot(weight, low[0:inputs])
        notes = both[scene, starts[4] : starts[4] + 16, :].astype(F32)
        limit = jnp.where(core == 0, notes[8:9], notes[10:11])
        tile = jnp.where(core == 0, notes[9:10], notes[11:12])
        limits.append(limit)
        top = jnp.full((channels, pillars), -jnp.inf, F32)
        for n in range(depth):
            piece = slice(n * pillars, (n + 1) * pillars)
            normed = (lifted[:, piece] - centre) * scale + shift
            act = normed * sigmoid(normed)
            acts[:, piece] = act
            top = jnp.maximum(top, jnp.where(limit > n, act, -jnp.inf))
        total = jnp.zeros((channels, pillars), F32)
        for n in range(depth):
            piece = slice(n * pillars, (n + 1) * pillars)
            total = total + jnp.where(limit > n, jnp.exp(acts[:, piece] - top), 0.0)
        result = top + jnp.log(total)
        pooled[scene] = result
        zero = jnp.zeros((channels, pillars), F32)
        parts = [zero, zero]
        parts[scene] = result.astype(BF16).astype(F32)
        stacked.append(jnp.transpose(jnp.concatenate(parts, axis=0)))
        slot_rows.append(tile * capacity + ranks(tile))
    slots[...] = jnp.concatenate(slot_rows + limits + [jnp.zeros((4, pillars), F32)], axis=0)
    values = jnp.concatenate(stacked, axis=0).astype(BF16)
    for group in range(3):
        place = lax.broadcasted_iota(jnp.int32, (rows_out, pillars), 0) + (group - 1) * capacity
        chosen = jnp.concatenate(
            [jnp.where(place.astype(F32) == row, 1.0, 0.0) for row in slot_rows], axis=1
        ).astype(BF16)
        send[:, group * LANES : (group + 1) * LANES] = dot(chosen, values).astype(BF16)
    for copy in copies:
        copy.wait()


def own_stats(ref, first_row, rows, send):
    scenes, _, channels, width = ref.shape
    spots = [(s, row) for s in range(scenes) for row in range(first_row, first_row + rows)]
    total = fold(ref[spots[0]])
    for spot in spots[1:]:
        total = total + fold(ref[spot])
    total = total * (1.0 / (len(spots) * width))
    mean = jnp.sum(total, axis=1, keepdims=True)
    squares = jnp.zeros(total.shape, F32)
    for spot in spots:
        away = ref[spot] - mean
        squares = squares + fold(away * away)
    if channels == LANES:
        send_all(send, [row_of(total), row_of(squares)])
    else:
        send_all(send, [row_of(total, squares)])


def conv_rows(source, weight, out, shape):
    scenes, high, channels, width = shape
    pairs = high // 2

    def step(index, _):
        scene, at = index // pairs, 2 * (index % pairs)
        window = source[scene, pl.ds(at, 4)].reshape(4 * channels, width)
        parts = dot(weight[...], window)
        out[scene, at] = side_sum(parts[: 3 * channels], channels).astype(out.dtype)
        out[scene, at + 1] = side_sum(parts[3 * channels :], channels).astype(out.dtype)
        return 0

    lax.fori_loop(0, scenes * pairs, step, 0)


def canvas_kernel(found, columns, where_rows, l_first, out, kept, first_kept, send, canvas, sems, *, rows):
    scenes, high, channels, width = out.shape
    slots = found.shape[0]
    lane = lax.broadcasted_iota(jnp.int32, (slots, width), 1).astype(F32)
    reach = rows - 1
    for group in range(3):
        values = jnp.transpose(found[:, group * LANES : (group + 1) * LANES].astype(F32))
        wanted = ((1, rows), (0, rows), (0, reach))[group]
        for scene in range(scenes):
            at = 2 * group + scene
            column = columns[:, at : at + 1] - 1.0
            column = column - jnp.floor(column * (1.0 / width)) * width
            row = jnp.floor((where_rows[at : at + 1] - 1.0) * (1.0 / width))
            mine = values[scene * channels : (scene + 1) * channels]
            placed = jnp.concatenate(
                [jnp.where(row == r * 1.0, mine, 0.0) for r in range(*wanted)], axis=0
            ).astype(BF16)
            chosen = jnp.where(lane == column, 1.0, 0.0).astype(BF16)
            grid = dot(placed, chosen).astype(BF16)
            count = wanted[1] - wanted[0]
            start = (0, reach, reach + rows)[group]
            canvas[scene, start : start + count] = grid.reshape(count, channels, width)
    copies = [
        move(canvas.at[scene, reach - 1 : reach + rows + 1], kept.at[scene], sems, scene)
        for scene in range(scenes)
    ]
    conv_rows(canvas, l_first, out, out.shape)
    copies += [
        move(out.at[scene, reach - 2 : reach + rows], first_kept.at[scene], sems, scenes + scene)
        for scene in range(scenes)
    ]
    own_stats(out, reach - 1, rows, send)
    for copy in copies:
        copy.wait()


def second_kernel(found, cols, first_out, l_second_in, out, kept, stats, send, acts, l_second, sems,
                  *, rows, tiles):
    weight_copy = move(l_second_in, l_second, sems, 0)
    scenes, high, channels, width = first_out.shape
    tile = lax.axis_index("tile")
    turned = half_stats(found, float(scenes * rows * width))
    stats[...] = turned
    centre = turned[0:channels, 0:1]
    scale = turned[0:channels, 1:2] * cols[0:channels, 2:3]
    shift = cols[0:channels, 3:4]

    def act_row(index, _):
        scene, row = index // high, index % high
        normed = (first_out[scene, row] - centre) * scale + shift
        on_grid = inside(tile, row - 2, (tiles, rows))
        acts[scene, row] = (normed * sigmoid(normed) * on_grid).astype(BF16)
        return 0

    lax.fori_loop(0, scenes * high, act_row, 0)
    copies = [
        move(acts.at[scene, 1 : rows + 3], kept.at[scene], sems, 1 + scene) for scene in range(scenes)
    ]
    weight_copy.wait()
    conv_rows(acts, l_second, out, out.shape)
    own_stats(out, 1, rows, send)
    for copy in copies:
        copy.wait()


def up_kernel(found, cols, second_out, w_up, kept, upper, stats, send, acts, sems, *, rows):
    scenes, _, channels, width = second_out.shape
    turned = half_stats(found, float(scenes * rows * width))
    stats[...] = turned
    centre = turned[0:channels, 0:1]
    scale = turned[0:channels, 1:2] * cols[0:channels, 4:5]
    shift = cols[0:channels, 5:6]

    def one(index, _):
        scene, row = index // rows, index % rows
        normed = (second_out[scene, row + 1] - centre) * scale + shift
        act = (normed * sigmoid(normed)).astype(BF16)
        acts[scene, row] = act
        upper[scene, row] = dot(w_up[...], act)
        return 0

    lax.fori_loop(0, scenes * rows, one, 0)
    copy = move(acts, kept, sems, 0)
    own_stats(upper, 0, rows, send)
    copy.wait()


def top_kernel(found, cols, upper, cot_in, features, grads, stats, send, cot, acts, sems, *, rows):
    fetched = move(cot_in, cot, sems, 0)
    scenes, _, wide, width = upper.shape
    mean, rstd = pooled_stats(found[:, 0, :], found[:, 1, :], float(scenes * rows * width))
    turned = columns_of([mean, rstd])
    stats[...] = turned
    gain, shift = cols[:, 6:7], cols[:, 7:8]
    centre, rstd = turned[:, 0:1], turned[:, 1:2]
    fetched.wait()

    def one(index, carry):
        scene, row = index // rows, index % rows
        unit = (upper[scene, row] - centre) * rstd
        normed = unit * gain + shift
        gate = sigmoid(normed)
        act = normed * gate
        grad = cot[scene, row].astype(F32) * (gate + act * (1.0 - gate))
        acts[scene, row] = act.astype(BF16)
        grads[scene, row] = grad
        return carry[0] + fold(grad * unit), carry[1] + fold(grad)

    zero = jnp.zeros((wide, LANES), F32)
    gain_sum, shift_sum = lax.fori_loop(0, scenes * rows, one, (zero, zero))
    copy = move(acts, features, sems, 1)
    send_all(send, [row_of(gain_sum), row_of(shift_sum)])
    copy.wait()


def second_back_kernel(
    found, cols, grads, upper, top_stats, second_out, second_stats, w_up_t,
    out, kept, down_edge, up_edge, notes, send, lows, sems, *, rows
):
    scenes, _, wide, width = grads.shape
    channels = second_out.shape[2]
    sums = [jnp.sum(found[:, index, :], axis=0, keepdims=True) for index in range(2)]
    notes[...] = jnp.concatenate(sums, axis=0)
    turned = columns_of(sums) * (1.0 / (found.shape[0] * scenes * rows * width))
    gain_part, shift_part = turned[:, 0:1], turned[:, 1:2]
    factor = cols[:, 6:7] * top_stats[:, 1:2]
    top_centre, top_rstd = top_stats[:, 0:1], top_stats[:, 1:2]
    centre, rstd = second_stats[0:channels, 0:1], second_stats[0:channels, 1:2]
    gain, shift = cols[0:channels, 4:5], cols[0:channels, 5:6]
    slope_part = top_rstd * gain_part

    def one(index, carry):
        scene, row = index // rows, index % rows
        low = factor * (
            grads[scene, row] - shift_part - (upper[scene, row] - top_centre) * slope_part
        )
        low = low.astype(BF16)
        lows[scene, row] = low
        unit = (second_out[scene, row + 1] - centre) * rstd
        normed = unit * gain + shift
        gate = sigmoid(normed)
        grad = dot(w_up_t[...], low) * (gate + normed * gate * (1.0 - gate))
        out[scene, row] = grad
        return carry[0] + fold(grad * unit), carry[1] + fold(grad)

    zero = jnp.zeros((channels, LANES), F32)
    gain_sum, shift_sum = lax.fori_loop(0, scenes * rows, one, (zero, zero))
    copy = move(lows, kept, sems, 0)
    for scene in range(scenes):
        down_edge[scene] = out[scene, 0].astype(BF16)
        up_edge[scene] = out[scene, rows - 1].astype(BF16)
    send_all(send, [row_of(gain_sum, shift_sum)])
    copy.wait()


def low_rows(turned, grads, before, after, values, centre, rstd, factor, low, rows, tiles):
    scenes, _, channels, width = grads.shape
    tile = lax.axis_index("tile")
    gain_part, shift_part = turned[0:channels, 0:1], turned[channels : 2 * channels, 0:1]
    slope_part = rstd * gain_part

    def one(grad, scene, row):
        return factor * (grad - shift_part - (values[scene, row] - centre) * slope_part)

    def own(index, _):
        scene, row = index // rows, index % rows
        low[scene, row + 1] = one(grads[scene, row], scene, row + 1).astype(BF16)
        return 0

    lax.fori_loop(0, scenes * rows, own, 0)
    for scene in range(scenes):
        for ref, row in ((before, 0), (after, rows + 1)):
            edge = one(ref[scene].astype(F32), scene, row) * inside(tile, row - 1, (tiles, rows))
            low[scene, row] = edge.astype(BF16)


def first_back_kernel(
    found, cols, grads, before, after, second_out, second_stats, first_in, first_stats, b_second_in,
    out, kept, down_edge, up_edge, notes, send, low, first_out, b_second, sems, *, rows, tiles
):
    weight_copy = move(b_second_in, b_second, sems, 0)
    first_copy = move(first_in, first_out, sems, 1)
    scenes, _, channels, width = grads.shape
    row, turned = half_sums(found)
    notes[...] = row
    turned = turned * (1.0 / (found.shape[0] * scenes * rows * width))
    centre, rstd = second_stats[0:channels, 0:1], second_stats[0:channels, 1:2]
    low_rows(turned, grads, before, after, second_out, centre, rstd, cols[0:channels, 4:5] * rstd, low,
             rows, tiles)
    copies = [move(low.at[scene, 1 : 1 + rows], kept.at[scene], sems, 2 + scene) for scene in range(scenes)]
    gain, shift = cols[0:channels, 2:3], cols[0:channels, 3:4]
    centre, rstd = first_stats[0:channels, 0:1], first_stats[0:channels, 1:2]
    weight_copy.wait()
    first_copy.wait()

    def step(index, carry):
        scene, at = index // (rows // 2), 2 * (index % (rows // 2))
        window = low[scene, pl.ds(at, 4)].reshape(4 * channels, width)
        parts = dot(b_second[...], window)
        gain_sum, shift_sum = carry
        for j in range(2):
            grad_act = side_sum(parts[3 * channels * j : 3 * channels * (j + 1)], channels)
            unit = (first_out[scene, at + j + 1] - centre) * rstd
            normed = unit * gain + shift
            gate = sigmoid(normed)
            grad = grad_act * (gate + normed * gate * (1.0 - gate))
            out[scene, at + j] = grad
            gain_sum = gain_sum + fold(grad * unit)
            shift_sum = shift_sum + fold(grad)
        return gain_sum, shift_sum

    zero = jnp.zeros((channels, LANES), F32)
    gain_sum, shift_sum = lax.fori_loop(0, scenes * (rows // 2), step, (zero, zero))
    for scene in range(scenes):
        down_edge[scene] = out[scene, 0].astype(BF16)
        up_edge[scene] = out[scene, rows - 1].astype(BF16)
    send_all(send, [row_of(gain_sum, shift_sum)])
    for copy in copies:
        copy.wait()


def pick_kernel(
    found, cols, grads, before, after, first_in, first_stats, b_first_in, columns, where_rows,
    send, kept, notes, low, grid, first_out, b_first, sems, *, rows, tiles
):
    weight_copy = move(b_first_in, b_first, sems, 0)
    first_copy = move(first_in, first_out, sems, 1)
    scenes, _, channels, width = grads.shape
    row, turned = half_sums(found)
    notes[...] = row
    turned = turned * (1.0 / (found.shape[0] * scenes * rows * width))
    centre, rstd = first_stats[0:channels, 0:1], first_stats[0:channels, 1:2]
    first_copy.wait()
    low_rows(turned, grads, before, after, first_out, centre, rstd, cols[0:channels, 2:3] * rstd, low,
             rows, tiles)
    copies = [move(low.at[scene, 1 : 1 + rows], kept.at[scene], sems, 2 + scene) for scene in range(scenes)]
    weight_copy.wait()
    conv_rows(low, b_first, grid, grid.shape)
    slots = send.shape[0]
    lane = lax.broadcasted_iota(jnp.int32, (slots, width), 1).astype(F32)
    picked = []
    for scene in range(scenes):
        at = 2 + scene
        column = columns[:, at : at + 1] - 1.0
        column = column - jnp.floor(column * (1.0 / width)) * width
        place = jnp.floor((where_rows[at : at + 1] - 1.0) * (1.0 / width))
        chosen = jnp.where(lane == column, 1.0, 0.0).astype(BF16)
        here = dot_lanes(grid[scene].reshape(rows * channels, width), chosen)
        total = jnp.zeros((channels, slots), F32)
        for r in range(rows):
            total = total + jnp.where(place == r * 1.0, here[r * channels : (r + 1) * channels], 0.0)
        picked.append(total)
    send[...] = jnp.transpose(jnp.concatenate(picked, axis=0)).astype(BF16)
    for copy in copies:
        copy.wait()


def grads_kernel(*refs, rows):
    sources, send, held, total, sems = refs[:6], refs[6], refs[7:13], refs[13], refs[14]
    copies = [move(sources[i], held[i], sems, i) for i in range(6)]
    up_low, second_act, second_low, first_act, first_low, canvas = held
    scenes, _, channels, width = canvas.shape
    lane = lax.broadcasted_iota(jnp.int32, (channels, width), 1)
    for copy in copies:
        copy.wait()
    half = channels // 2
    base = 0
    for low, values in ((first_low, canvas), (second_low, first_act)):

        def step(index, carry, low=low, values=values):
            scene, row = index // rows, index % rows
            grad = low[scene, row].astype(F32)
            left = jnp.where(lane < width - 1, pltpu.roll(grad, width - 1, 1), 0.0)
            right = jnp.where(lane > 0, pltpu.roll(grad, 1, 1), 0.0)
            stacked = jnp.concatenate([left, grad, right], axis=0).astype(BF16)
            window = values[scene, pl.ds(row, 3)].reshape(3 * channels, width)
            total[...] = total[...] + dot_lanes(stacked, window)
            return carry

        total[...] = jnp.zeros(total.shape, F32)
        lax.fori_loop(0, scenes * rows, step, 0)
        for s in range(2):
            mine = jnp.concatenate(
                [total[b * channels + s * half : b * channels + (s + 1) * half, :] for b in range(3)], axis=0
            )
            wing = mine[:, LANES:]
            cut = wing.shape[0] // 2
            lead = mine.shape[0]
            send[s, base : base + lead] = mine[:, :LANES].astype(BF16)
            send[s, base + lead : base + lead + cut] = jnp.concatenate(
                [wing[:cut], wing[cut:]], axis=1
            ).astype(BF16)
        base += 9 * half * channels // LANES
    up = jnp.zeros((up_low.shape[2], channels), F32)
    for scene in range(scenes):
        for row in range(rows):
            up = up + dot_lanes(up_low[scene, row], second_act[scene, row])
    for s in range(2):
        mine = up[s * channels : (s + 1) * channels]
        send[s, base : base + half] = jnp.concatenate([mine[:half], mine[half:]], axis=1).astype(BF16)
        rest = send.shape[1] - base - half
        if rest > 0:
            send[s, base + half :] = jnp.zeros((rest, LANES), BF16)


def pair_kernel(found, out):
    total = found[0].astype(F32) + found[1].astype(F32)
    out[...] = total.reshape(out.shape).astype(BF16)


def sum_kernel(found, out):
    total = jnp.sum(found[...].astype(F32), axis=0)
    out[...] = jnp.broadcast_to(total[None], out.shape).astype(BF16)


def pillar_back_kernel(found, rows_in, w_pillar, cols, pooled, stats, slots, send, grads, lifted, rows, sems):
    fetched = move(rows_in, rows, sems, 0)
    scenes, channels, pillars = pooled.shape
    inputs = w_pillar.shape[1]
    depth = rows.shape[2] // pillars
    slot_count = found.shape[0]
    turned = jnp.transpose(found[...].astype(F32))
    place = lax.broadcasted_iota(jnp.int32, (slot_count, pillars), 0).astype(F32)
    centre, rstd = stats[:, 0:1], stats[:, 1:2]
    gain, shift = cols[0:channels, 0:1], cols[0:channels, 1:2]
    gain_sum = jnp.zeros((channels, pillars), F32)
    shift_sum = jnp.zeros((channels, pillars), F32)
    outer = jnp.zeros((16, channels), F32)
    fetched.wait()
    for scene in range(scenes):
        lifted[...] = dot(w_pillar[...], rows[scene, 0:inputs])
        chosen = jnp.where(place == slots[scene : scene + 1], 1.0, 0.0).astype(BF16)
        back = dot(turned[scene * channels : (scene + 1) * channels].astype(BF16), chosen)
        limit = slots[scenes + scene : scenes + scene + 1]
        pool = pooled[scene]
        for n in range(depth):
            piece = slice(n * pillars, (n + 1) * pillars)
            unit = (lifted[:, piece] - centre) * rstd
            normed = unit * gain + shift
            gate = sigmoid(normed)
            act = normed * gate
            slope = gate + act * (1.0 - gate)
            grad = jnp.where(limit > n, back * jnp.exp(act - pool) * slope, 0.0)
            grads[scene, :, piece] = grad
            gain_sum = gain_sum + grad * unit
            shift_sum = shift_sum + grad
        outer = outer + dot_lanes(rows[scene], grads[scene].astype(BF16))
    scale = jnp.transpose(jnp.broadcast_to(rstd * gain, (channels, LANES)))[0:1]
    outer = outer * scale
    lines = [row_of(gain_sum, shift_sum)]
    for k in range(0, 14, 2):
        lines.append(jnp.concatenate([outer[k : k + 1], outer[k + 1 : k + 2]], axis=1))
    send[...] = jnp.broadcast_to(jnp.concatenate(lines, axis=0)[None], send.shape)


def points_kernel(
    found, rows_in, grads, w_pillar, cols, stats, slots, top_notes, second_notes, first_notes,
    out, rows, lifted, sems, *, inputs
):
    fetched = move(rows_in, rows, sems, 0)
    scenes, channels, wide = grads.shape
    pillars = slots.shape[1]
    depth = wide // pillars
    total = jnp.sum(found[...], axis=0)
    turned = jnp.transpose(total)
    gain_part, shift_part = turned[0:channels, 0:1], turned[channels : 2 * channels, 0:1]
    centre, rstd, inverse = stats[:, 0:1], stats[:, 1:2], stats[:, 2:3]
    factor = cols[0:channels, 0:1] * rstd
    spun, mean = stats[:, 16 : 16 + inputs], stats[:, 32 : 32 + inputs]
    outer = jnp.concatenate(
        [turned[(k % 2) * channels : (k % 2 + 1) * channels, 1 + k // 2 : 2 + k // 2] for k in range(inputs)],
        axis=1,
    )
    weight_grad = outer - factor * (shift_part * mean + gain_part * rstd * spun)
    weight_grad = jnp.concatenate(
        [weight_grad, jnp.zeros((channels, LANES - inputs), F32)], axis=1
    )
    notes = jnp.concatenate(
        [top_notes[...], second_notes[...], first_notes[...], total[0:1], jnp.zeros((3, LANES), F32)], axis=0
    )
    size = inputs * depth
    half = channels // 2
    for core in range(2):
        out[core, size : size + 8] = notes
        out[core, size + 8 : size + 8 + half] = weight_grad[core * half : (core + 1) * half]
    weight = jnp.transpose(w_pillar[...].astype(F32)).astype(BF16)
    gain_part, shift_part = gain_part * inverse * rstd, shift_part * inverse
    fetched.wait()
    for scene in range(scenes):
        lifted[...] = dot(w_pillar[...], rows[scene, 0:inputs])
        limit = slots[scenes + scene : scenes + scene + 1]
        for n in range(depth):
            piece = slice(n * pillars, (n + 1) * pillars)
            low = factor * (grads[scene, :, piece] - shift_part - (lifted[:, piece] - centre) * gain_part)
            low = jnp.where(limit > n, low, 0.0).astype(BF16)
            out[scene, pl.ds(n, inputs, stride=depth), :] = dot(weight, low)


def last_kernel(
    found, halves, points_grad, pillar_grad, pillar_gain, pillar_shift,
    first_grad, first_gain, first_shift, second_grad, second_gain, second_shift,
    up_grad, up_gain, up_shift
):
    core = lax.axis_index("scene")
    half, inputs = pillar_grad.shape
    channels = 2 * half
    _, _, _, depth, pillars = points_grad.shape
    size = inputs * depth
    for micro in range(2):
        points_grad[micro, 0] = found[micro, 0:size].reshape(inputs, depth, pillars)
    notes = found[0, size : size + 8] + found[1, size : size + 8]
    pillar_grad[...] = (found[0, size + 8 : size + 8 + half] + found[1, size + 8 : size + 8 + half])[:, :inputs]

    def own(row, start, out):
        length = out.shape[0]
        line = notes[row : row + 1]
        out[...] = jnp.where(
            core == 0, line[:, start : start + length], line[:, start + length : start + 2 * length]
        ).reshape(length)

    own(0, 0, up_gain)
    own(1, 0, up_shift)
    for row, gain, shift in ((2, second_gain, second_shift), (3, first_gain, first_shift),
                             (4, pillar_gain, pillar_shift)):
        own(row, 0, gain)
        own(row, channels, shift)
    whole = halves[...].astype(F32).reshape(-1, LANES)
    for index, out in enumerate((first_grad, second_grad)):
        base = index * 9 * half * channels // LANES
        lead = 3 * half
        mine = whole[base : base + lead]
        wing = whole[base + lead : base + lead + lead // 2]
        wing = jnp.concatenate([wing[:, :channels], wing[:, channels:]], axis=0)
        both = jnp.concatenate([mine, wing], axis=1)
        for a in range(3):
            for b in range(3):
                at = (3 * a + b) * channels
                out[:, at : at + channels] = both[b * half : (b + 1) * half, a * channels : (a + 1) * channels]
    base = 2 * 9 * half * channels // LANES
    top = whole[base : base + half]
    up_grad[...] = jnp.concatenate([top[:, :channels], top[:, channels:]], axis=0)


def swap(blocks, axes):
    return lax.all_to_all(blocks, axes, split_axis=0, concat_axis=0)


def shards(
    points, point_counts, pillar_tile, pillar_cell,
    pillar_weight, pillar_gain, pillar_shift,
    first_weight, first_gain, first_shift,
    second_weight, second_gain, second_shift,
    up_weight, up_gain, up_shift, cotangent,
):
    micros, _, inputs, depth, pillars = points.shape
    channels = up_weight.shape[1]
    upper = cotangent.shape[2]
    rows, width = cotangent.shape[3:]
    tiles = lax.axis_size("tile")
    scenes = lax.axis_size("scene")
    capacity = 2 * pillars // tiles
    slot_count = tiles * capacity
    half = channels // 2

    def vmem(shape, dtype):
        return pltpu.VMEM(shape, dtype)

    def grid(high, dtype=F32, lead=channels):
        return ((scenes, high, lead, width), dtype)

    cloud = (points.shape, BF16)
    note = (point_counts.shape, jnp.int32)
    (moments,) = run(
        functools.partial(moments_kernel, capacity=capacity),
        [((tiles, micros, 2, LANES), F32)],
        points, point_counts, pillar_tile, pillar_cell,
        hbm=range(4), copies=4,
        scratch=[vmem(*cloud), vmem(*note), vmem(*note), vmem(*note), vmem((inputs * depth, pillars), F32)],
    )
    moments = swap(moments.reshape(tiles * micros, 2, LANES), BOTH)
    sources = (
        first_weight, second_weight, up_weight, pillar_weight, points, point_counts, pillar_tile,
        pillar_gain, pillar_shift, first_gain, first_shift, second_gain, second_shift, up_gain, up_shift,
    )
    lines = layout(half, channels, inputs, depth)[-1] + micros * inputs * depth
    (packed,) = run(
        pack_kernel, [((lines, LANES), BF16)], *sources,
        hbm=range(len(sources)), copies=len(sources),
        scratch=[vmem(source.shape, source.dtype) for source in sources],
    )
    both = lax.all_gather(packed, "scene")
    taps = ((6 * channels, 4 * channels), BF16)
    w_pillar, cols, l_first, l_second, b_first, b_second, w_up, w_up_t = run(
        functools.partial(unpack_kernel, inputs=inputs, depth=depth),
        [
            ((channels, inputs), BF16), ((LANES, 8), F32), taps, taps + (1,), taps + (1,), taps + (1,),
            ((upper, channels), BF16), ((channels, upper), BF16),
        ],
        both,
        scratch=[vmem(*taps), vmem(*taps), vmem(*taps)], copies=3,
    )
    cot = swap(cotangent[:, 0], "scene").transpose(0, 2, 1, 3)

    send, pooled, pillar_stats, slots, point_rows = run(
        functools.partial(pillar_kernel, capacity=capacity, inputs=inputs, depth=depth),
        [
            ((slot_count, 3 * LANES), BF16), ((scenes, channels, pillars), F32),
            ((channels, LANES), F32), ((8, pillars), F32), ((scenes, 16, depth * pillars), BF16, 1),
        ],
        moments, both, w_pillar, cols,
        scratch=[
            vmem((inputs * depth, pillars), F32), vmem((channels, depth * pillars), F32),
            vmem((channels, depth * pillars), F32), vmem((scenes, 16, depth * pillars), BF16),
        ],
        copies=2,
    )
    arrived = swap(send.reshape(tiles, capacity, 3 * LANES), "tile").reshape(slot_count, 3 * LANES)
    cell_columns, cell_rows = run(
        functools.partial(cells_kernel, capacity=capacity),
        [((slot_count, LANES), F32), ((8, slot_count), F32)],
        moments,
        cost=pl.CostEstimate(flops=10**7, bytes_accessed=10**6, transcendentals=0),
    )
    arrived, cot = lax.optimization_barrier((arrived, cot))

    first_out, canvas, first_kept, send = run(
        functools.partial(canvas_kernel, rows=rows),
        [
            grid(rows + 4), grid(rows + 2, BF16) + (1,), grid(rows + 2) + (1,), ((tiles, 1, LANES), F32),
        ],
        arrived, cell_columns, cell_rows, l_first,
        scratch=[vmem(*grid(rows + 6, BF16))], copies=4,
    )
    second_out, first_act, first_stats, send = run(
        functools.partial(second_kernel, rows=rows, tiles=tiles),
        [
            grid(rows + 2), grid(rows + 2, BF16) + (1,), ((LANES, 8), F32), ((tiles, 1, LANES), F32),
        ],
        swap(send, "tile"), cols, first_out, l_second,
        hbm=(3,), scratch=[vmem(*grid(rows + 4, BF16)), vmem(*taps)], copies=3,
    )
    second_act, up_out, second_stats, send = run(
        functools.partial(up_kernel, rows=rows),
        [grid(rows, BF16) + (1,), grid(rows, F32, upper), ((LANES, 8), F32), ((tiles, 2, LANES), F32)],
        swap(send, "tile"), cols, second_out, w_up,
        scratch=[vmem(*grid(rows, BF16))], copies=1,
    )
    features, grads, top_stats, send = run(
        functools.partial(top_kernel, rows=rows),
        [
            grid(rows, BF16, upper) + (1,), grid(rows, F32, upper), ((LANES, 8), F32),
            ((tiles, 2, LANES), F32),
        ],
        swap(send, "tile"), cols, up_out, cot,
        hbm=(3,), scratch=[vmem(*grid(rows, BF16, upper)), vmem(*grid(rows, BF16, upper))], copies=2,
    )
    edge = ((scenes, channels, width), BF16)
    second_dz, up_low, down_edge, up_edge, top_notes, send = run(
        functools.partial(second_back_kernel, rows=rows),
        [
            grid(rows), grid(rows, BF16, upper) + (1,), edge, edge, ((2, LANES), F32),
            ((tiles, 1, LANES), F32),
        ],
        swap(send, "tile"), cols, grads, up_out, top_stats, second_out, second_stats, w_up_t,
        scratch=[vmem(*grid(rows, BF16, upper))], copies=1,
    )
    rising = [(i, i + 1) for i in range(tiles - 1)]
    falling = [(j, i) for i, j in rising]
    first_dz, second_low, down_next, up_next, second_notes, send_next = run(
        functools.partial(first_back_kernel, rows=rows, tiles=tiles),
        [
            grid(rows), grid(rows, BF16) + (1,), edge, edge, ((1, LANES), F32), ((tiles, 1, LANES), F32),
        ],
        swap(send, "tile"), cols, second_dz,
        lax.ppermute(up_edge, "tile", rising), lax.ppermute(down_edge, "tile", falling),
        second_out, second_stats, first_kept, first_stats, b_second,
        hbm=(7, 9),
        scratch=[vmem(*grid(rows + 2, BF16)), vmem(*grid(rows + 2)), vmem(*taps)], copies=4,
    )
    send, first_low, first_notes = run(
        functools.partial(pick_kernel, rows=rows, tiles=tiles),
        [((slot_count, LANES), BF16), grid(rows, BF16) + (1,), ((1, LANES), F32)],
        swap(send_next, "tile"), cols, first_dz,
        lax.ppermute(up_next, "tile", rising), lax.ppermute(down_next, "tile", falling),
        first_kept, first_stats, b_first, cell_columns, cell_rows,
        hbm=(5, 7),
        scratch=[
            vmem(*grid(rows + 2, BF16)), vmem(*grid(rows, BF16)), vmem(*grid(rows + 2)), vmem(*taps),
        ],
        copies=4,
    )
    send, features = lax.optimization_barrier((send, features))
    returned = swap(send.reshape(tiles, capacity, LANES), "tile").reshape(slot_count, LANES)
    features = swap(features.transpose(0, 2, 1, 3), "scene")[:, None]
    length = (2 * 9 * half * channels + upper * half) // LANES
    each = -(-length // (8 * tiles)) * 8
    factors = (up_low, second_act, second_low, first_act, first_low, canvas)
    (halves,) = run(
        functools.partial(grads_kernel, rows=rows),
        [((scenes, tiles * each, LANES), BF16)],
        *factors,
        hbm=range(6), copies=6,
        scratch=[vmem(factor.shape, factor.dtype) for factor in factors]
        + [vmem((3 * channels, 3 * channels), F32)],
        cost=pl.CostEstimate(flops=10**9, bytes_accessed=10**7, transcendentals=0),
    )
    (halves,) = run(pair_kernel, [((tiles, each, LANES), BF16)], swap(halves, "scene"))
    halves = swap(halves, "tile")
    send, pillar_dz = run(
        pillar_back_kernel,
        [((tiles, 8, LANES), F32), ((scenes, channels, depth * pillars), F32)],
        returned, point_rows, w_pillar, cols, pooled, pillar_stats, slots,
        hbm=(1,),
        scratch=[vmem((channels, depth * pillars), F32), vmem((scenes, 16, depth * pillars), BF16)],
        copies=1,
    )
    (halves,) = run(sum_kernel, [((tiles, each, LANES), BF16)], halves)
    halves = swap(halves, "tile")
    (mixed,) = run(
        functools.partial(points_kernel, inputs=inputs),
        [((scenes, inputs * depth + 8 + half, LANES), F32)],
        swap(send, "tile"), point_rows, pillar_dz, w_pillar, cols, pillar_stats, slots,
        top_notes, second_notes, first_notes,
        hbm=(1,),
        scratch=[vmem((scenes, 16, depth * pillars), BF16), vmem((channels, depth * pillars), F32)],
        copies=1,
    )
    vector, matrix = ((half,), F32), ((half, 9 * channels), F32)
    results = run(
        last_kernel,
        [
            ((micros, 1, inputs, depth, pillars), F32), ((half, inputs), F32), vector, vector,
            matrix, vector, vector, matrix, vector, vector,
            ((upper // 2, channels), F32), ((upper // 2,), F32), ((upper // 2,), F32),
        ],
        swap(mixed, "scene"), halves,
    )
    return (features,) + tuple(results)


def solution(mesh):
    matrix, vector = P("scene", None), P("scene")
    grid = P(None, "scene", None, "tile", None)
    cloud = P(None, "scene", None, None, "tile")
    pillar = P(None, "scene", "tile")
    weights = (matrix, vector, vector) * 4
    return jax.shard_map(
        shards,
        mesh=mesh,
        in_specs=(cloud, pillar, pillar, pillar) + weights + (grid,),
        out_specs=(grid, cloud) + weights,
        check_vma=False,
    )
```

```python
import functools

import jax
import jax.numpy as jnp
from jax import lax
from jax.experimental import pallas as pl
from jax.experimental.pallas import tpu as pltpu
from jax.sharding import PartitionSpec as P

norm_eps = 0.001
BOTH = ("tile", "scene")
F32 = jnp.float32
BF16 = jnp.bfloat16
VMEM_LIMIT = 24 * 1024 * 1024
WIDE_LIMIT = 60 * 1024 * 1024
LANES = 128


def run(kernel, outs, *args, hbm=(), scratch=(), copies=0, cost=None, limit=VMEM_LIMIT):
    specs = [
        pl.BlockSpec(memory_space=pltpu.HBM if index in hbm else pltpu.VMEM) for index in range(len(args))
    ]
    scratch = list(scratch)
    if copies:
        scratch.append(pltpu.SemaphoreType.DMA((copies,)))
    return pl.pallas_call(
        kernel,
        out_shape=[jax.ShapeDtypeStruct(out[0], out[1]) for out in outs],
        in_specs=specs,
        out_specs=[
            pl.BlockSpec(memory_space=pltpu.HBM if len(out) > 2 else pltpu.VMEM) for out in outs
        ],
        scratch_shapes=scratch,
        compiler_params=pltpu.CompilerParams(vmem_limit_bytes=limit),
        cost_estimate=cost,
    )(*args)


def move(source, target, sems, index):
    copy = pltpu.make_async_copy(source, target, sems.at[index])
    copy.start()
    return copy


def dot(left, right, precision=None):
    return jnp.dot(left, right, preferred_element_type=F32, precision=precision)


def dot_lanes(left, right, precision=None):
    return lax.dot_general(
        left, right, (((1,), (1,)), ((), ())), preferred_element_type=F32, precision=precision
    )


def sigmoid(values):
    return 0.5 + 0.5 * jnp.tanh(0.5 * values)


def fold(values):
    total = values[:, :LANES]
    for start in range(LANES, values.shape[1], LANES):
        total = total + values[:, start : start + LANES]
    return total


def row_of(left, right=None):
    both = left if right is None else jnp.concatenate([left, right], axis=0)
    return jnp.sum(jnp.transpose(both), axis=0, keepdims=True)


def columns_of(rows):
    rows = rows + [jnp.zeros((8 - len(rows), LANES), F32)] if len(rows) < 8 else rows
    return jnp.transpose(jnp.concatenate(rows, axis=0))


def inside(tile, row, height):
    tiles, rows = height
    place = tile * rows + row
    return jnp.where((place >= 0) & (place < tiles * rows), 1.0, 0.0).astype(F32)


def send_all(ref, rows):
    for index, row in enumerate(rows):
        ref[:, index : index + 1, :] = jnp.broadcast_to(row[None], (ref.shape[0], 1, LANES))


def pooled_stats(means, squares, count):
    peers = means.shape[0]
    mean = jnp.sum(means, axis=0, keepdims=True) * (1.0 / peers)
    away = means - mean
    spread = jnp.sum(squares + count * away * away, axis=0, keepdims=True) * (1.0 / (peers * count))
    return mean, lax.rsqrt(spread + norm_eps)


def stat_columns(found, count):
    return columns_of(list(pooled_stats(found[:, 0, :], found[:, 1, :], count)))


def sum_rows(found, lines):
    return [jnp.sum(found[:, index, :], axis=0, keepdims=True) for index in range(lines)]


def own_half(row, scene, out):
    size = out.shape[0]
    out[...] = jnp.where(scene == 0, row[:, 0:size], row[:, size : 2 * size]).reshape(size)


def side_sum(stacked, channels):
    width = stacked.shape[1]
    lane = lax.broadcasted_iota(jnp.int32, (channels, width), 1)
    left = pltpu.roll(stacked[:channels], 1, 1)
    right = pltpu.roll(stacked[2 * channels :], width - 1, 1)
    return (
        stacked[channels : 2 * channels]
        + jnp.where(lane > 0, left, 0.0)
        + jnp.where(lane < width - 1, right, 0.0)
    )


def layout(half, channels):
    first = 0
    second = first + half * -(-9 * channels // LANES)
    up = second + half * -(-9 * channels // LANES)
    pillar = up + channels
    vectors = pillar + half
    return first, second, up, pillar, vectors


def widen(value):
    missing = LANES - value.shape[1]
    if missing == 0:
        return value
    return jnp.concatenate([value, jnp.zeros((value.shape[0], missing), value.dtype)], axis=1)


def pack_kernel(*refs):
    count = 12
    sources, out, held, sems = refs[:count], refs[count], refs[count + 1 : 2 * count + 1], refs[-1]
    copies = [move(sources[i], held[i], sems, i) for i in range(count)]
    for copy in copies:
        copy.wait()
    first, second, up, pillar = held[:4]
    half, channels = first.shape[0], up.shape[1]
    starts = layout(half, channels)
    for ref, start in ((first, starts[0]), (second, starts[1])):
        for j in range(-(-9 * channels // LANES)):
            out[start + j * half : start + (j + 1) * half, :] = widen(
                ref[:, j * LANES : min((j + 1) * LANES, 9 * channels)]
            )
    out[starts[2] : starts[2] + channels, :] = widen(up[...])
    out[starts[3] : starts[3] + half, :] = widen(pillar[...].astype(F32)).astype(BF16)
    rows = [widen(vector[...].astype(F32).reshape(1, -1)) for vector in held[4:]]
    rows.append(jnp.zeros((16 - len(rows), LANES), F32))
    out[starts[4] : starts[4] + 16, :] = jnp.concatenate(rows, axis=0).astype(BF16)


def unpack_kernel(
    both, w_pillar, cols, l_first, l_second, b_first, b_second, w_up, w_up_t,
    h_second, h_first_back, h_second_back, sems, *, inputs
):
    half = w_pillar.shape[0] // 2
    channels = 2 * half
    starts = layout(half, channels)
    tiles = -(-9 * channels // LANES)

    def wide(start):
        return jnp.concatenate(
            [
                jnp.concatenate(
                    [both[s, start + j * half : start + (j + 1) * half, :] for j in range(tiles)], axis=1
                )
                for s in range(2)
            ],
            axis=0,
        ).astype(F32)

    up = jnp.concatenate(
        [both[s, starts[2] : starts[2] + channels, 0:channels] for s in range(2)], axis=0
    )
    w_up[...] = up
    w_up_t[...] = jnp.transpose(up.astype(F32)).astype(BF16)
    w_pillar[...] = jnp.concatenate(
        [both[s, starts[3] : starts[3] + half, 0:inputs] for s in range(2)], axis=0
    )
    vectors = [both[s, starts[4] : starts[4] + 16, :].astype(F32) for s in range(2)]
    rows = []
    for index in range(8):
        size = half if index < 6 else channels
        row = jnp.concatenate([vectors[s][index : index + 1, 0:size] for s in range(2)], axis=1)
        rows.append(jnp.concatenate([row] * (LANES // (2 * size)), axis=1))
    cols[...] = columns_of(rows)
    zero = jnp.zeros((channels, channels), F32)
    copies = []
    for weight, ahead, back in (
        (wide(starts[0]), l_first, h_first_back), (wide(starts[1]), h_second, h_second_back)
    ):
        pieces = [
            [weight[:, (3 * a + b) * channels : (3 * a + b + 1) * channels] for b in range(3)]
            for a in range(3)
        ]
        flipped = [[jnp.transpose(pieces[a][b]) for b in range(3)] for a in range(3)]
        for j in range(2):
            for b in range(3):
                start = (3 * j + b) * channels
                ahead[start : start + channels, :] = jnp.concatenate(
                    [pieces[r - j][b] if 0 <= r - j <= 2 else zero for r in range(4)], axis=1
                ).astype(BF16)
                back[start : start + channels, :] = jnp.concatenate(
                    [flipped[j + 2 - r][2 - b] if 0 <= j + 2 - r <= 2 else zero for r in range(4)],
                    axis=1,
                ).astype(BF16)
    copies.append(move(h_second, l_second, sems, 0))
    copies.append(move(h_first_back, b_first, sems, 1))
    copies.append(move(h_second_back, b_second, sems, 2))
    for copy in copies:
        copy.wait()


def slot_line(wide, depth, inputs):
    return jnp.concatenate([wide[pl.ds(n, inputs, stride=depth), :] for n in range(depth)], axis=1)


def slot_mask(count, depth):
    return jnp.concatenate([jnp.where(count > n, 1.0, 0.0) for n in range(depth)], axis=1)


def ranks(tile):
    pillars = tile.shape[1]
    across = jnp.broadcast_to(tile, (pillars, pillars))
    down = jnp.transpose(across)
    row = lax.broadcasted_iota(jnp.int32, (pillars, pillars), 0)
    col = lax.broadcasted_iota(jnp.int32, (pillars, pillars), 1)
    return jnp.sum(jnp.where((across == down) & (row < col), 1.0, 0.0), axis=0, keepdims=True)


def moments_kernel(points_in, counts_in, tiles_in, cells_in, out, points, counts, tiles, cells, wide, sems,
                   *, capacity):
    copies = [
        move(source, target, sems, index)
        for index, (source, target) in enumerate(
            ((tiles_in, tiles), (cells_in, cells), (counts_in, counts), (points_in, points))
        )
    ]
    micros, _, inputs, depth, pillars = points.shape
    peers, scenes = out.shape[:2]
    copies[0].wait()
    copies[1].wait()
    lines = []
    for micro in range(micros):
        tile = tiles[micro].astype(F32)
        cell = (cells[micro] + 1).astype(F32)
        high = jnp.floor(cell * (1.0 / 16.0))
        low = cell - high * 16.0
        rank = ranks(tile)
        spot = lax.broadcasted_iota(jnp.int32, (capacity, pillars), 0).astype(F32)
        placed = jnp.where(spot == rank, 1.0, 0.0).astype(BF16)
        peer = lax.broadcasted_iota(jnp.int32, (peers, pillars), 0).astype(F32)
        for group in range(3):
            named = tile == peer + (group - 1.0)
            lines.append(
                16.0 * dot_lanes(jnp.where(named, high, 0.0).astype(BF16), placed)
                + dot_lanes(jnp.where(named, low, 0.0).astype(BF16), placed)
            )
    used = 3 * micros * capacity
    line = jnp.concatenate(lines + [jnp.zeros((peers, LANES - used), F32)], axis=1).reshape(peers, 1, LANES)
    for scene in range(scenes):
        out[:, scene, micros : micros + 1, :] = line
    copies[2].wait()
    copies[3].wait()
    for micro in range(micros):
        wide[...] = points[micro, 0].astype(F32).reshape(inputs * depth, pillars)
        rows = slot_line(wide, depth, inputs)
        mask = slot_mask(counts[micro], depth)
        total = jnp.sum(mask, axis=1, keepdims=True)
        mean = jnp.sum(rows * mask, axis=1, keepdims=True) / total
        centred = (rows - mean) * mask
        products = dot_lanes(centred, centred, lax.Precision.HIGHEST)
        lane = lax.broadcasted_iota(jnp.int32, (inputs, inputs), 1)
        diagonal = lax.broadcasted_iota(jnp.int32, (inputs, inputs), 0) == lane
        mean_row = jnp.sum(jnp.where(diagonal, mean, 0.0), axis=0, keepdims=True)
        row = jnp.concatenate(
            [products[k : k + 1] for k in range(inputs)]
            + [mean_row, total, jnp.zeros((1, LANES - inputs * inputs - inputs - 1), F32)],
            axis=1,
        )
        for scene in range(scenes):
            out[:, scene, micro : micro + 1, :] = jnp.broadcast_to(row[None], (peers, 1, LANES))


def cells_kernel(found, columns, rows, *, capacity):
    scene = lax.axis_index("scene")
    slots = columns.shape[0]
    peers = found.shape[0]
    values = found[:, 2, :]
    slot = lax.broadcasted_iota(jnp.int32, (slots, peers), 0)
    peer = lax.broadcasted_iota(jnp.int32, (slots, peers), 1)
    lane = lax.broadcasted_iota(jnp.int32, (slots, LANES), 1)
    row = lax.broadcasted_iota(jnp.int32, (slots, LANES), 0)
    result = jnp.zeros((slots, LANES), F32)
    chosen = jnp.where(peer == 2 * (slot // capacity) + scene, 1.0, 0.0)
    spread = dot(chosen, values, lax.Precision.HIGHEST)
    for micro in range(2):
        for group in range(3):
            mine = jnp.where(lane == (3 * micro + group) * capacity + row % capacity, spread, 0.0)
            column = jnp.sum(mine, axis=1, keepdims=True)
            result = jnp.where(lane == 2 * group + micro, column, result)
    columns[...] = result
    rows[...] = jnp.transpose(result)[0:8]


def pillar_kernel(
    found, points, counts, tiles, w_pillar, cols, send, pooled, stats, slots, kept, wide, lifted, acts,
    *, capacity
):
    micros, _, inputs, depth, pillars = points.shape
    channels = w_pillar.shape[0]
    weight = w_pillar[...]
    wide_weight = weight.astype(F32)
    rows_out = send.shape[0]
    square = inputs * inputs
    stacked, slot_rows, limits = [], [], []
    for micro in range(micros):
        wide[...] = points[micro, 0].astype(F32).reshape(inputs * depth, pillars)
        rows = slot_line(wide, depth, inputs)
        low = jnp.concatenate([rows, jnp.zeros((16 - inputs, rows.shape[1]), F32)], axis=0).astype(BF16)
        kept[micro] = low
        lifted[...] = dot(weight, low[0:inputs])
        moments = found[:, micro, :]
        sizes = moments[:, square + inputs : square + inputs + 1]
        means = moments[:, square : square + inputs]
        count = jnp.sum(sizes, axis=0, keepdims=True)
        mean = jnp.sum(means * sizes, axis=0, keepdims=True) / count
        away = means - mean
        products = lax.dot_general(
            away * sizes, away, (((0,), (0,)), ((), ())),
            preferred_element_type=F32, precision=lax.Precision.HIGHEST,
        )
        summed = jnp.sum(moments, axis=0, keepdims=True)
        products = products + jnp.concatenate(
            [summed[:, k * inputs : (k + 1) * inputs] for k in range(inputs)], axis=0
        )
        cov = products / count
        spun = wide_weight[:, 0:1] * cov[0:1]
        for k in range(1, inputs):
            spun = spun + wide_weight[:, k : k + 1] * cov[k : k + 1]
        spread = jnp.sum(spun * wide_weight, axis=1, keepdims=True)
        centre = jnp.sum(wide_weight * mean, axis=1, keepdims=True)
        rstd = lax.rsqrt(spread + norm_eps)
        inverse = jnp.broadcast_to(1.0 / count, (channels, 1))
        stats[micro] = jnp.concatenate(
            [
                centre, rstd, inverse, jnp.zeros((channels, 13), F32),
                spun, jnp.zeros((channels, 16 - inputs), F32),
                jnp.broadcast_to(mean, (channels, inputs)), jnp.zeros((channels, LANES - 32 - inputs), F32),
            ],
            axis=1,
        )
        scale = rstd * cols[0:channels, 0:1]
        shift = cols[0:channels, 1:2]
        limit = counts[micro].astype(F32)
        limits.append(limit)
        top = jnp.full((channels, pillars), -jnp.inf, F32)
        for n in range(depth):
            piece = slice(n * pillars, (n + 1) * pillars)
            normed = (lifted[:, piece] - centre) * scale + shift
            act = normed * sigmoid(normed)
            acts[:, piece] = act
            top = jnp.maximum(top, jnp.where(limit > n, act, -jnp.inf))
        total = jnp.zeros((channels, pillars), F32)
        for n in range(depth):
            piece = slice(n * pillars, (n + 1) * pillars)
            total = total + jnp.where(limit > n, jnp.exp(acts[:, piece] - top), 0.0)
        result = top + jnp.log(total)
        pooled[micro] = result
        parts = [jnp.zeros((channels, pillars), F32)] * micros
        parts[micro] = result.astype(BF16).astype(F32)
        stacked.append(jnp.transpose(jnp.concatenate(parts, axis=0)))
        tile = tiles[micro].astype(F32)
        slot_rows.append(tile * capacity + ranks(tile))
    slots[...] = jnp.concatenate(slot_rows + limits + [jnp.zeros((4, pillars), F32)], axis=0)
    values = jnp.concatenate(stacked, axis=0).astype(BF16)
    for group in range(3):
        place = lax.broadcasted_iota(jnp.int32, (rows_out, pillars), 0) + (group - 1) * capacity
        chosen = jnp.concatenate(
            [jnp.where(place.astype(F32) == row, 1.0, 0.0) for row in slot_rows], axis=1
        ).astype(BF16)
        send[:, group * LANES : (group + 1) * LANES] = dot(chosen, values).astype(BF16)


def own_stats(ref, first_row, rows, send):
    micros, _, channels, width = ref.shape
    sums, squares = [], []
    for micro in range(micros):
        total = fold(ref[micro, first_row])
        for row in range(first_row + 1, first_row + rows):
            total = total + fold(ref[micro, row])
        total = total * (1.0 / (rows * width))
        mean = jnp.sum(total, axis=1, keepdims=True)
        spread = jnp.zeros(total.shape, F32)
        for row in range(first_row, first_row + rows):
            away = ref[micro, row] - mean
            spread = spread + fold(away * away)
        sums.append(total)
        squares.append(spread)
    if channels == LANES:
        send_all(send, [row_of(part) for part in sums + squares])
    else:
        send_all(send, [row_of(*sums), row_of(*squares)])


def conv_rows(source, weight, out, shape):
    scenes, high, channels, width = shape
    pairs = high // 2

    def step(index, _):
        scene, at = index // pairs, 2 * (index % pairs)
        window = source[scene, pl.ds(at, 4)].reshape(4 * channels, width)
        parts = dot(weight[...], window)
        out[scene, at] = side_sum(parts[: 3 * channels], channels).astype(out.dtype)
        out[scene, at + 1] = side_sum(parts[3 * channels :], channels).astype(out.dtype)
        return 0

    lax.fori_loop(0, scenes * pairs, step, 0)


def canvas_kernel(found, columns, where_rows, l_first, out, kept, first_kept, send, canvas, sems, *, rows):
    scenes, high, channels, width = out.shape
    slots = found.shape[0]
    lane = lax.broadcasted_iota(jnp.int32, (slots, width), 1).astype(F32)
    reach = rows - 1
    for group in range(3):
        values = jnp.transpose(found[:, group * LANES : (group + 1) * LANES].astype(F32))
        wanted = ((1, rows), (0, rows), (0, reach))[group]
        for scene in range(scenes):
            at = 2 * group + scene
            column = columns[:, at : at + 1] - 1.0
            column = column - jnp.floor(column * (1.0 / width)) * width
            row = jnp.floor((where_rows[at : at + 1] - 1.0) * (1.0 / width))
            mine = values[scene * channels : (scene + 1) * channels]
            placed = jnp.concatenate(
                [jnp.where(row == r * 1.0, mine, 0.0) for r in range(*wanted)], axis=0
            ).astype(BF16)
            chosen = jnp.where(lane == column, 1.0, 0.0).astype(BF16)
            grid = dot(placed, chosen).astype(BF16)
            count = wanted[1] - wanted[0]
            start = (0, reach, reach + rows)[group]
            canvas[scene, start : start + count] = grid.reshape(count, channels, width)
    copies = [
        move(canvas.at[scene, reach - 1 : reach + rows + 1], kept.at[scene], sems, scene)
        for scene in range(scenes)
    ]
    conv_rows(canvas, l_first, out, out.shape)
    copies += [
        move(out.at[scene, reach - 2 : reach + rows], first_kept.at[scene], sems, scenes + scene)
        for scene in range(scenes)
    ]
    own_stats(out, reach - 1, rows, send)
    for copy in copies:
        copy.wait()


def second_kernel(found, cols, first_out, l_second_in, out, kept, stats, send, acts, l_second, sems,
                  *, rows, tiles):
    weight_copy = move(l_second_in, l_second, sems, 0)
    micros, high, channels, width = first_out.shape
    tile = lax.axis_index("tile")
    turned = stat_columns(found, float(rows * width))
    stats[...] = turned
    copies = []
    for micro in range(micros):
        part = slice(micro * channels, (micro + 1) * channels)
        centre = turned[part, 0:1]
        scale = turned[part, 1:2] * cols[0:channels, 2:3]
        shift = cols[0:channels, 3:4]

        def act_row(row, _, micro=micro, centre=centre, scale=scale, shift=shift):
            normed = (first_out[micro, row] - centre) * scale + shift
            on_grid = inside(tile, row - 2, (tiles, rows))
            acts[micro, row] = (normed * sigmoid(normed) * on_grid).astype(BF16)
            return 0

        lax.fori_loop(0, high, act_row, 0)
        copies.append(move(acts.at[micro, 1 : rows + 3], kept.at[micro], sems, 1 + micro))
    weight_copy.wait()
    conv_rows(acts, l_second, out, out.shape)
    own_stats(out, 1, rows, send)
    for copy in copies:
        copy.wait()


def up_kernel(found, cols, second_out, w_up, kept, upper, stats, send, acts, sems, *, rows):
    micros, _, channels, width = second_out.shape
    turned = stat_columns(found, float(rows * width))
    stats[...] = turned
    for micro in range(micros):
        part = slice(micro * channels, (micro + 1) * channels)
        centre = turned[part, 0:1]
        scale = turned[part, 1:2] * cols[0:channels, 4:5]
        shift = cols[0:channels, 5:6]

        def one(row, _, micro=micro, centre=centre, scale=scale, shift=shift):
            normed = (second_out[micro, row + 1] - centre) * scale + shift
            act = (normed * sigmoid(normed)).astype(BF16)
            acts[micro, row] = act
            upper[micro, row] = dot(w_up[...], act)
            return 0

        lax.fori_loop(0, rows, one, 0)
    copy = move(acts, kept, sems, 0)
    own_stats(upper, 0, rows, send)
    copy.wait()


def top_kernel(found, cols, upper, cot_in, features, grads, stats, send, cot, acts, sems, *, rows):
    fetched = move(cot_in, cot, sems, 0)
    micros, _, wide, width = upper.shape
    lines = []
    for micro in range(micros):
        lines += list(pooled_stats(found[:, micro, :], found[:, micros + micro, :], float(rows * width)))
    turned = columns_of(lines)
    stats[...] = turned
    gain, shift = cols[:, 6:7], cols[:, 7:8]
    fetched.wait()
    gain_rows, shift_rows, copies = [], [], []
    for micro in range(micros):
        centre, rstd = turned[:, 2 * micro : 2 * micro + 1], turned[:, 2 * micro + 1 : 2 * micro + 2]

        def one(row, carry, micro=micro, centre=centre, rstd=rstd):
            unit = (upper[micro, row] - centre) * rstd
            normed = unit * gain + shift
            gate = sigmoid(normed)
            act = normed * gate
            grad = cot[micro, row].astype(F32) * (gate + act * (1.0 - gate))
            acts[micro, row] = act.astype(BF16)
            grads[micro, row] = grad
            return carry[0] + fold(grad * unit), carry[1] + fold(grad)

        zero = jnp.zeros((wide, LANES), F32)
        gain_sum, shift_sum = lax.fori_loop(0, rows, one, (zero, zero))
        copies.append(move(acts.at[micro], features.at[micro], sems, 1 + micro))
        gain_rows.append(row_of(gain_sum))
        shift_rows.append(row_of(shift_sum))
    send_all(send, gain_rows + shift_rows)
    for copy in copies:
        copy.wait()


def second_back_kernel(
    found, cols, grads, upper, top_stats, second_out, second_stats, w_up_t,
    out, kept, down_edge, up_edge, gain_grad, shift_grad, send, lows, sems, *, rows
):
    scene = lax.axis_index("scene")
    micros, _, wide, width = grads.shape
    channels = second_out.shape[2]
    sums = sum_rows(found, 2 * micros)
    own_half(sum(sums[:micros]), scene, gain_grad)
    own_half(sum(sums[micros:]), scene, shift_grad)
    turned = columns_of(sums) * (1.0 / (found.shape[0] * rows * width))
    gain, shift = cols[0:channels, 4:5], cols[0:channels, 5:6]
    gain_sums, shift_sums, copies = [], [], []
    for micro in range(micros):
        part = slice(micro * channels, (micro + 1) * channels)
        centre, rstd = second_stats[part, 0:1], second_stats[part, 1:2]
        top_centre = top_stats[:, 2 * micro : 2 * micro + 1]
        top_rstd = top_stats[:, 2 * micro + 1 : 2 * micro + 2]
        factor = cols[:, 6:7] * top_rstd
        slope_part = top_rstd * turned[:, micro : micro + 1]
        shift_part = turned[:, micros + micro : micros + micro + 1]

        def one(row, carry, micro=micro, centre=centre, rstd=rstd, top_centre=top_centre, factor=factor,
                slope_part=slope_part, shift_part=shift_part):
            low = factor * (grads[micro, row] - shift_part - (upper[micro, row] - top_centre) * slope_part)
            low = low.astype(BF16)
            lows[micro, row] = low
            unit = (second_out[micro, row + 1] - centre) * rstd
            normed = unit * gain + shift
            gate = sigmoid(normed)
            grad = dot(w_up_t[...], low) * (gate + normed * gate * (1.0 - gate))
            out[micro, row] = grad
            return carry[0] + fold(grad * unit), carry[1] + fold(grad)

        zero = jnp.zeros((channels, LANES), F32)
        gain_sum, shift_sum = lax.fori_loop(0, rows, one, (zero, zero))
        copies.append(move(lows.at[micro], kept.at[micro], sems, micro))
        down_edge[micro] = out[micro, 0].astype(BF16)
        up_edge[micro] = out[micro, rows - 1].astype(BF16)
        gain_sums.append(gain_sum)
        shift_sums.append(shift_sum)
    send_all(send, [row_of(*gain_sums), row_of(*shift_sums)])
    for copy in copies:
        copy.wait()


def low_rows(turned, grads, before, after, values, stats, gain, low, rows, tiles):
    micros, _, channels, width = grads.shape
    tile = lax.axis_index("tile")
    for micro in range(micros):
        part = slice(micro * channels, (micro + 1) * channels)
        centre, rstd = stats[part, 0:1], stats[part, 1:2]
        factor = gain * rstd
        slope_part, shift_part = rstd * turned[part, 0:1], turned[part, 1:2]

        def one(grad, row, micro=micro, centre=centre, factor=factor, slope_part=slope_part,
                shift_part=shift_part):
            return factor * (grad - shift_part - (values[micro, row] - centre) * slope_part)

        def own(row, _, micro=micro, one=one):
            low[micro, row + 1] = one(grads[micro, row], row + 1).astype(BF16)
            return 0

        lax.fori_loop(0, rows, own, 0)
        for ref, row in ((before, 0), (after, rows + 1)):
            edge = one(ref[micro].astype(F32), row) * inside(tile, row - 1, (tiles, rows))
            low[micro, row] = edge.astype(BF16)


def first_back_kernel(
    found, cols, grads, before, after, second_out, second_stats, first_in, first_stats, b_second_in,
    out, kept, down_edge, up_edge, gain_grad, shift_grad, send, low, first_out, b_second, sems, *, rows, tiles
):
    weight_copy = move(b_second_in, b_second, sems, 0)
    first_copy = move(first_in, first_out, sems, 1)
    scene = lax.axis_index("scene")
    micros, _, channels, width = grads.shape
    sums = sum_rows(found, 2)
    own_half(sums[0][:, :channels] + sums[0][:, channels:], scene, gain_grad)
    own_half(sums[1][:, :channels] + sums[1][:, channels:], scene, shift_grad)
    turned = columns_of(sums) * (1.0 / (found.shape[0] * rows * width))
    low_rows(turned, grads, before, after, second_out, second_stats, cols[0:channels, 4:5], low, rows, tiles)
    copies = [move(low.at[micro, 1 : 1 + rows], kept.at[micro], sems, 2 + micro) for micro in range(micros)]
    gain, shift = cols[0:channels, 2:3], cols[0:channels, 3:4]
    weight_copy.wait()
    first_copy.wait()
    gain_sums, shift_sums = [], []
    for micro in range(micros):
        part = slice(micro * channels, (micro + 1) * channels)
        centre, rstd = first_stats[part, 0:1], first_stats[part, 1:2]

        def step(index, carry, micro=micro, centre=centre, rstd=rstd):
            at = 2 * index
            window = low[micro, pl.ds(at, 4)].reshape(4 * channels, width)
            parts = dot(b_second[...], window)
            gain_sum, shift_sum = carry
            for j in range(2):
                grad_act = side_sum(parts[3 * channels * j : 3 * channels * (j + 1)], channels)
                unit = (first_out[micro, at + j + 1] - centre) * rstd
                normed = unit * gain + shift
                gate = sigmoid(normed)
                grad = grad_act * (gate + normed * gate * (1.0 - gate))
                out[micro, at + j] = grad
                gain_sum = gain_sum + fold(grad * unit)
                shift_sum = shift_sum + fold(grad)
            return gain_sum, shift_sum

        zero = jnp.zeros((channels, LANES), F32)
        gain_sum, shift_sum = lax.fori_loop(0, rows // 2, step, (zero, zero))
        down_edge[micro] = out[micro, 0].astype(BF16)
        up_edge[micro] = out[micro, rows - 1].astype(BF16)
        gain_sums.append(gain_sum)
        shift_sums.append(shift_sum)
    send_all(send, [row_of(*gain_sums), row_of(*shift_sums)])
    for copy in copies:
        copy.wait()


def pick_kernel(
    found, cols, grads, before, after, first_in, first_stats, b_first_in, columns, where_rows,
    send, kept, gain_grad, shift_grad, low, grid, first_out, b_first, sems, *, rows, tiles
):
    weight_copy = move(b_first_in, b_first, sems, 0)
    first_copy = move(first_in, first_out, sems, 1)
    scene = lax.axis_index("scene")
    micros, _, channels, width = grads.shape
    sums = sum_rows(found, 2)
    own_half(sums[0][:, :channels] + sums[0][:, channels:], scene, gain_grad)
    own_half(sums[1][:, :channels] + sums[1][:, channels:], scene, shift_grad)
    turned = columns_of(sums) * (1.0 / (found.shape[0] * rows * width))
    first_copy.wait()
    low_rows(turned, grads, before, after, first_out, first_stats, cols[0:channels, 2:3], low, rows, tiles)
    copies = [move(low.at[micro, 1 : 1 + rows], kept.at[micro], sems, 2 + micro) for micro in range(micros)]
    weight_copy.wait()
    conv_rows(low, b_first, grid, grid.shape)
    slots = send.shape[0]
    lane = lax.broadcasted_iota(jnp.int32, (slots, width), 1).astype(F32)
    picked = []
    for micro in range(micros):
        at = 2 + micro
        column = columns[:, at : at + 1] - 1.0
        column = column - jnp.floor(column * (1.0 / width)) * width
        place = jnp.floor((where_rows[at : at + 1] - 1.0) * (1.0 / width))
        chosen = jnp.where(lane == column, 1.0, 0.0).astype(BF16)
        here = dot_lanes(grid[micro].reshape(rows * channels, width), chosen)
        total = jnp.zeros((channels, slots), F32)
        for r in range(rows):
            total = total + jnp.where(place == r * 1.0, here[r * channels : (r + 1) * channels], 0.0)
        picked.append(total)
    send[...] = jnp.transpose(jnp.concatenate(picked, axis=0)).astype(BF16)
    for copy in copies:
        copy.wait()


def grads_kernel(*refs, rows):
    sources, send, held, total, whole, sems = refs[:6], refs[6], refs[7:13], refs[13], refs[14], refs[15]
    copies = [move(sources[i], held[i], sems, i) for i in range(6)]
    up_low, second_act, second_low, first_act, first_low, canvas = held
    micros, _, channels, width = canvas.shape
    lane = lax.broadcasted_iota(jnp.int32, (channels, width), 1)
    for copy in copies:
        copy.wait()
    half = channels // 2
    base = 0
    for low, values in ((first_low, canvas), (second_low, first_act)):

        def step(index, carry, low=low, values=values):
            micro, row = index // rows, index % rows
            grad = low[micro, row].astype(F32)
            left = jnp.where(lane < width - 1, pltpu.roll(grad, width - 1, 1), 0.0)
            right = jnp.where(lane > 0, pltpu.roll(grad, 1, 1), 0.0)
            stacked = jnp.concatenate([left, grad, right], axis=0).astype(BF16)
            window = values[micro, pl.ds(row, 3)].reshape(3 * channels, width)
            total[...] = total[...] + dot_lanes(stacked, window)
            return carry

        total[...] = jnp.zeros(total.shape, F32)
        lax.fori_loop(0, micros * rows, step, 0)
        for s in range(2):
            mine = jnp.concatenate(
                [total[b * channels + s * half : b * channels + (s + 1) * half, :] for b in range(3)], axis=0
            )
            wing = mine[:, LANES:]
            cut = wing.shape[0] // 2
            lead = mine.shape[0]
            whole[s, base : base + lead] = mine[:, :LANES]
            whole[s, base + lead : base + lead + cut] = jnp.concatenate([wing[:cut], wing[cut:]], axis=1)
        base += 9 * half * channels // LANES
    up = jnp.zeros((up_low.shape[2], channels), F32)
    for micro in range(micros):
        for row in range(rows):
            up = up + dot_lanes(up_low[micro, row], second_act[micro, row])
    tiles, _, each, _ = send.shape
    for s in range(2):
        mine = up[s * channels : (s + 1) * channels]
        whole[s, base : base + half] = jnp.concatenate([mine[:half], mine[half:]], axis=1)
        rest = whole.shape[1] - base - half
        if rest > 0:
            whole[s, base + half :] = jnp.zeros((rest, LANES), F32)
        for t in range(tiles):
            send[t, s] = whole[s, t * each : (t + 1) * each].astype(BF16)


def sum_kernel(found, out):
    total = jnp.sum(found[...].astype(F32), axis=0)
    out[...] = jnp.broadcast_to(total[None], out.shape).astype(BF16)


def pillar_back_kernel(found, rows_in, w_pillar, cols, pooled, stats, slots, send, grads, lifted, rows, sems):
    fetched = move(rows_in, rows, sems, 0)
    micros, channels, pillars = pooled.shape
    inputs = w_pillar.shape[1]
    depth = rows.shape[2] // pillars
    slot_count = found.shape[0]
    turned = jnp.transpose(found[...].astype(F32))
    place = lax.broadcasted_iota(jnp.int32, (slot_count, pillars), 0).astype(F32)
    gain, shift = cols[0:channels, 0:1], cols[0:channels, 1:2]
    gain_sums, shift_sums = [], []
    outer = jnp.zeros((16, channels), F32)
    fetched.wait()
    for micro in range(micros):
        lifted[...] = dot(w_pillar[...], rows[micro, 0:inputs])
        chosen = jnp.where(place == slots[micro : micro + 1], 1.0, 0.0).astype(BF16)
        back = dot(turned[micro * channels : (micro + 1) * channels].astype(BF16), chosen)
        limit = slots[micros + micro : micros + micro + 1]
        centre, rstd = stats[micro, :, 0:1], stats[micro, :, 1:2]
        pool = pooled[micro]
        gain_sum = jnp.zeros((channels, pillars), F32)
        shift_sum = jnp.zeros((channels, pillars), F32)
        for n in range(depth):
            piece = slice(n * pillars, (n + 1) * pillars)
            unit = (lifted[:, piece] - centre) * rstd
            normed = unit * gain + shift
            gate = sigmoid(normed)
            act = normed * gate
            slope = gate + act * (1.0 - gate)
            grad = jnp.where(limit > n, back * jnp.exp(act - pool) * slope, 0.0)
            grads[micro, :, piece] = grad
            gain_sum = gain_sum + grad * unit
            shift_sum = shift_sum + grad
        gain_sums.append(gain_sum)
        shift_sums.append(shift_sum)
        scale = jnp.transpose(jnp.broadcast_to(rstd * gain, (channels, LANES)))[0:1]
        outer = outer + dot_lanes(rows[micro], grads[micro].astype(BF16)) * scale
    lines = [row_of(*gain_sums), row_of(*shift_sums)]
    for k in range(0, 12, 2):
        lines.append(jnp.concatenate([outer[k : k + 1], outer[k + 1 : k + 2]], axis=1))
    send[...] = jnp.broadcast_to(jnp.concatenate(lines, axis=0)[None], send.shape)


def points_kernel(
    found, rows_in, grads, w_pillar, cols, stats, slots,
    points_grad, pillar_grad, gain_grad, shift_grad, rows, lifted, sems
):
    fetched = move(rows_in, rows, sems, 0)
    scene = lax.axis_index("scene")
    micros, channels, _ = grads.shape
    _, _, inputs, depth, pillars = points_grad.shape
    half = channels // 2
    total = jnp.sum(found[...], axis=0)
    own_half(total[0:1, :channels] + total[0:1, channels:], scene, gain_grad)
    own_half(total[1:2, :channels] + total[1:2, channels:], scene, shift_grad)
    turned = jnp.transpose(total)
    weight_grad = jnp.concatenate(
        [turned[(k % 2) * channels : (k % 2 + 1) * channels, 2 + k // 2 : 3 + k // 2] for k in range(inputs)],
        axis=1,
    )
    weight = jnp.transpose(w_pillar[...].astype(F32)).astype(BF16)
    fetched.wait()
    for micro in range(micros):
        lifted[...] = dot(w_pillar[...], rows[micro, 0:inputs])
        part = slice(micro * channels, (micro + 1) * channels)
        centre, rstd, inverse = stats[micro, :, 0:1], stats[micro, :, 1:2], stats[micro, :, 2:3]
        factor = cols[0:channels, 0:1] * rstd
        gain_part, shift_part = turned[part, 0:1], turned[part, 1:2]
        spun, mean = stats[micro, :, 16 : 16 + inputs], stats[micro, :, 32 : 32 + inputs]
        weight_grad = weight_grad - factor * (shift_part * mean + gain_part * rstd * spun)
        gain_part, shift_part = gain_part * inverse * rstd, shift_part * inverse
        limit = slots[micros + micro : micros + micro + 1]
        for n in range(depth):
            piece = slice(n * pillars, (n + 1) * pillars)
            low = factor * (grads[micro, :, piece] - shift_part - (lifted[:, piece] - centre) * gain_part)
            low = jnp.where(limit > n, low, 0.0).astype(BF16)
            points_grad[micro, 0, :, n, :] = dot(weight, low)
    pillar_grad[...] = jnp.where(scene == 0, weight_grad[:half], weight_grad[half:])


def unfold_kernel(halves, first_grad, second_grad, up_grad):
    half = first_grad.shape[0]
    channels = 2 * half
    whole = halves[...].astype(F32).reshape(-1, LANES)
    for index, out in enumerate((first_grad, second_grad)):
        base = index * 9 * half * channels // LANES
        lead = 3 * half
        mine = whole[base : base + lead]
        wing = whole[base + lead : base + lead + lead // 2]
        wing = jnp.concatenate([wing[:, :channels], wing[:, channels:]], axis=0)
        both = jnp.concatenate([mine, wing], axis=1)
        for a in range(3):
            for b in range(3):
                at = (3 * a + b) * channels
                out[:, at : at + channels] = both[b * half : (b + 1) * half, a * channels : (a + 1) * channels]
    base = 2 * 9 * half * channels // LANES
    top = whole[base : base + half]
    up_grad[...] = jnp.concatenate([top[:, :channels], top[:, channels:]], axis=0)


def swap(blocks, axes):
    return lax.all_to_all(blocks, axes, split_axis=0, concat_axis=0)


def shards(
    points, point_counts, pillar_tile, pillar_cell,
    pillar_weight, pillar_gain, pillar_shift,
    first_weight, first_gain, first_shift,
    second_weight, second_gain, second_shift,
    up_weight, up_gain, up_shift, cotangent,
):
    micros, _, inputs, depth, pillars = points.shape
    channels = up_weight.shape[1]
    upper = cotangent.shape[2]
    rows, width = cotangent.shape[3:]
    tiles = lax.axis_size("tile")
    scenes = lax.axis_size("scene")
    peers = tiles * scenes
    capacity = 2 * pillars // tiles
    slot_count = tiles * capacity
    half = channels // 2

    def vmem(shape, dtype):
        return pltpu.VMEM(shape, dtype)

    def grid(high, dtype=F32, lead=channels):
        return ((micros, high, lead, width), dtype)

    cloud = (points.shape, BF16)
    note = (point_counts.shape, jnp.int32)
    sums = ((peers, 2, LANES), F32)
    (moments,) = run(
        functools.partial(moments_kernel, capacity=capacity),
        [((tiles, scenes, 4, LANES), F32)],
        points, point_counts, pillar_tile, pillar_cell,
        hbm=range(4), copies=4, limit=WIDE_LIMIT,
        scratch=[vmem(*cloud), vmem(*note), vmem(*note), vmem(*note), vmem((inputs * depth, pillars), F32)],
    )
    moments = swap(moments.reshape(peers, 4, LANES), BOTH)
    sources = (
        first_weight, second_weight, up_weight, pillar_weight,
        pillar_gain, pillar_shift, first_gain, first_shift, second_gain, second_shift, up_gain, up_shift,
    )
    (packed,) = run(
        pack_kernel, [((layout(half, channels)[-1] + 16, LANES), BF16)], *sources,
        hbm=range(len(sources)), copies=len(sources), limit=WIDE_LIMIT,
        scratch=[vmem(source.shape, source.dtype) for source in sources],
    )
    both = lax.all_gather(packed, "scene")
    taps = ((6 * channels, 4 * channels), BF16)
    w_pillar, cols, l_first, l_second, b_first, b_second, w_up, w_up_t = run(
        functools.partial(unpack_kernel, inputs=inputs),
        [
            ((channels, inputs), BF16), ((LANES, 8), F32), taps, taps + (1,), taps + (1,), taps + (1,),
            ((upper, channels), BF16), ((channels, upper), BF16),
        ],
        both,
        scratch=[vmem(*taps), vmem(*taps), vmem(*taps)], copies=3,
    )
    cot = cotangent[:, 0].transpose(0, 2, 1, 3)

    send, pooled, pillar_stats, slots, point_rows = run(
        functools.partial(pillar_kernel, capacity=capacity),
        [
            ((slot_count, 3 * LANES), BF16), ((micros, channels, pillars), F32),
            ((micros, channels, LANES), F32), ((8, pillars), F32), ((micros, 16, depth * pillars), BF16),
        ],
        moments, points, point_counts, pillar_tile, w_pillar, cols,
        scratch=[
            vmem((inputs * depth, pillars), F32), vmem((channels, depth * pillars), F32),
            vmem((channels, depth * pillars), F32),
        ],
    )
    arrived = swap(send.reshape(tiles, capacity, 3 * LANES), "tile").reshape(slot_count, 3 * LANES)
    cell_columns, cell_rows = run(
        functools.partial(cells_kernel, capacity=capacity),
        [((slot_count, LANES), F32), ((8, slot_count), F32)],
        moments,
        cost=pl.CostEstimate(flops=10**7, bytes_accessed=10**6, transcendentals=0),
    )
    arrived, cot = lax.optimization_barrier((arrived, cot))

    first_out, canvas, first_kept, send = run(
        functools.partial(canvas_kernel, rows=rows),
        [grid(rows + 4), grid(rows + 2, BF16) + (1,), grid(rows + 2) + (1,), sums],
        arrived, cell_columns, cell_rows, l_first,
        scratch=[vmem(*grid(rows + 6, BF16))], copies=4,
    )
    second_out, first_act, first_stats, send = run(
        functools.partial(second_kernel, rows=rows, tiles=tiles),
        [grid(rows + 2), grid(rows + 2, BF16) + (1,), ((LANES, 8), F32), sums],
        swap(send, BOTH), cols, first_out, l_second,
        hbm=(3,), scratch=[vmem(*grid(rows + 4, BF16)), vmem(*taps)], copies=3,
    )
    second_act, up_out, second_stats, send = run(
        functools.partial(up_kernel, rows=rows),
        [grid(rows, BF16) + (1,), grid(rows, F32, upper), ((LANES, 8), F32), ((peers, 4, LANES), F32)],
        swap(send, BOTH), cols, second_out, w_up,
        scratch=[vmem(*grid(rows, BF16))], copies=1,
    )
    features, grads, top_stats, send = run(
        functools.partial(top_kernel, rows=rows),
        [
            grid(rows, BF16, upper) + (1,), grid(rows, F32, upper), ((LANES, 8), F32),
            ((peers, 4, LANES), F32),
        ],
        swap(send, BOTH), cols, up_out, cot,
        hbm=(3,), scratch=[vmem(*grid(rows, BF16, upper)), vmem(*grid(rows, BF16, upper))], copies=3,
    )
    edge = ((micros, channels, width), BF16)
    vector, top_vector, matrix = ((half,), F32), ((upper // 2,), F32), ((half, 9 * channels), F32)
    second_dz, up_low, down_edge, up_edge, up_gain_grad, up_shift_grad, send = run(
        functools.partial(second_back_kernel, rows=rows),
        [grid(rows), grid(rows, BF16, upper) + (1,), edge, edge, top_vector, top_vector, sums],
        swap(send, BOTH), cols, grads, up_out, top_stats, second_out, second_stats, w_up_t,
        scratch=[vmem(*grid(rows, BF16, upper))], copies=2,
    )
    rising = [(i, i + 1) for i in range(tiles - 1)]
    falling = [(j, i) for i, j in rising]
    first_dz, second_low, down_next, up_next, second_gain_grad, second_shift_grad, send = run(
        functools.partial(first_back_kernel, rows=rows, tiles=tiles),
        [grid(rows), grid(rows, BF16) + (1,), edge, edge, vector, vector, sums],
        swap(send, BOTH), cols, second_dz,
        lax.ppermute(up_edge, "tile", rising), lax.ppermute(down_edge, "tile", falling),
        second_out, second_stats, first_kept, first_stats, b_second,
        hbm=(7, 9),
        scratch=[vmem(*grid(rows + 2, BF16)), vmem(*grid(rows + 2)), vmem(*taps)], copies=4,
    )
    send, first_low, first_gain_grad, first_shift_grad = run(
        functools.partial(pick_kernel, rows=rows, tiles=tiles),
        [((slot_count, LANES), BF16), grid(rows, BF16) + (1,), vector, vector],
        swap(send, BOTH), cols, first_dz,
        lax.ppermute(up_next, "tile", rising), lax.ppermute(down_next, "tile", falling),
        first_kept, first_stats, b_first, cell_columns, cell_rows,
        hbm=(5, 7),
        scratch=[
            vmem(*grid(rows + 2, BF16)), vmem(*grid(rows, BF16)), vmem(*grid(rows + 2)), vmem(*taps),
        ],
        copies=4,
    )
    send, features = lax.optimization_barrier((send, features))
    returned = swap(send.reshape(tiles, capacity, LANES), "tile").reshape(slot_count, LANES)
    features = features.transpose(0, 2, 1, 3)[:, None]
    length = (2 * 9 * half * channels + upper * half) // LANES
    each = -(-length // (8 * tiles)) * 8
    factors = (up_low, second_act, second_low, first_act, first_low, canvas)
    (halves,) = run(
        functools.partial(grads_kernel, rows=rows),
        [((tiles, scenes, each, LANES), BF16)],
        *factors,
        hbm=range(6), copies=6,
        scratch=[vmem(factor.shape, factor.dtype) for factor in factors]
        + [vmem((3 * channels, 3 * channels), F32), vmem((scenes, tiles * each, LANES), F32)],
        cost=pl.CostEstimate(flops=10**9, bytes_accessed=10**7, transcendentals=0),
    )
    halves = swap(halves.reshape(peers, each, LANES), BOTH)
    send, pillar_dz = run(
        pillar_back_kernel,
        [((peers, 8, LANES), F32), ((micros, channels, depth * pillars), F32)],
        returned, point_rows, w_pillar, cols, pooled, pillar_stats, slots,
        hbm=(1,),
        scratch=[vmem((channels, depth * pillars), F32), vmem((micros, 16, depth * pillars), BF16)],
        copies=1,
    )
    (halves,) = run(sum_kernel, [((tiles, each, LANES), BF16)], halves)
    halves = swap(halves, "tile")
    points_grad, pillar_grad, pillar_gain_grad, pillar_shift_grad = run(
        points_kernel,
        [((micros, 1, inputs, depth, pillars), F32), ((half, inputs), F32), vector, vector],
        swap(send, BOTH), point_rows, pillar_dz, w_pillar, cols, pillar_stats, slots,
        hbm=(1,),
        scratch=[vmem((micros, 16, depth * pillars), BF16), vmem((channels, depth * pillars), F32)],
        copies=1,
    )
    first_grad, second_grad, up_grad = run(
        unfold_kernel, [matrix, matrix, ((upper // 2, channels), F32)], halves
    )
    return (
        features, points_grad,
        pillar_grad, pillar_gain_grad, pillar_shift_grad,
        first_grad, first_gain_grad, first_shift_grad,
        second_grad, second_gain_grad, second_shift_grad,
        up_grad, up_gain_grad, up_shift_grad,
    )


def solution(mesh):
    matrix, vector = P("scene", None), P("scene")
    grid = P(None, "scene", None, "tile", None)
    cloud = P(None, "scene", None, None, "tile")
    pillar = P(None, "scene", "tile")
    weights = (matrix, vector, vector) * 4
    return jax.shard_map(
        shards,
        mesh=mesh,
        in_specs=(cloud, pillar, pillar, pillar) + weights + (grid,),
        out_specs=(grid, cloud) + weights,
        check_vma=False,
    )
```

```python
import functools

import jax
import jax.numpy as jnp
from jax import lax
from jax.experimental import pallas as pl
from jax.experimental.pallas import tpu as pltpu
from jax.sharding import PartitionSpec as P

norm_eps = 0.001
BOTH = ("tile", "scene")
F32 = jnp.float32
BF16 = jnp.bfloat16
VMEM_LIMIT = 24 * 1024 * 1024
WIDE_LIMIT = 60 * 1024 * 1024
LANES = 128


def run(kernel, outs, *args, hbm=(), scratch=(), copies=0, cost=None, limit=VMEM_LIMIT):
    specs = [
        pl.BlockSpec(memory_space=pltpu.HBM if index in hbm else pltpu.VMEM) for index in range(len(args))
    ]
    scratch = list(scratch)
    if copies:
        scratch.append(pltpu.SemaphoreType.DMA((copies,)))
    return pl.pallas_call(
        kernel,
        out_shape=[jax.ShapeDtypeStruct(out[0], out[1]) for out in outs],
        in_specs=specs,
        out_specs=[
            pl.BlockSpec(memory_space=pltpu.HBM if len(out) > 2 else pltpu.VMEM) for out in outs
        ],
        scratch_shapes=scratch,
        compiler_params=pltpu.CompilerParams(vmem_limit_bytes=limit),
        cost_estimate=cost,
    )(*args)


def move(source, target, sems, index):
    copy = pltpu.make_async_copy(source, target, sems.at[index])
    copy.start()
    return copy


def dot(left, right, precision=None):
    return jnp.dot(left, right, preferred_element_type=F32, precision=precision)


def dot_lanes(left, right, precision=None):
    return lax.dot_general(
        left, right, (((1,), (1,)), ((), ())), preferred_element_type=F32, precision=precision
    )


def sigmoid(values):
    return 0.5 + 0.5 * jnp.tanh(0.5 * values)


def fold(values):
    total = values[:, :LANES]
    for start in range(LANES, values.shape[1], LANES):
        total = total + values[:, start : start + LANES]
    return total


def row_of(left, right=None):
    both = left if right is None else jnp.concatenate([left, right], axis=0)
    return jnp.sum(jnp.transpose(both), axis=0, keepdims=True)


def columns_of(rows):
    rows = rows + [jnp.zeros((8 - len(rows), LANES), F32)] if len(rows) < 8 else rows
    return jnp.transpose(jnp.concatenate(rows, axis=0))


def inside(tile, row, height):
    tiles, rows = height
    place = tile * rows + row
    return jnp.where((place >= 0) & (place < tiles * rows), 1.0, 0.0).astype(F32)


def send_all(ref, rows):
    for index, row in enumerate(rows):
        ref[:, index : index + 1, :] = jnp.broadcast_to(row[None], (ref.shape[0], 1, LANES))


def pooled_stats(means, squares, count):
    peers = means.shape[0]
    mean = jnp.sum(means, axis=0, keepdims=True) * (1.0 / peers)
    away = means - mean
    spread = jnp.sum(squares + count * away * away, axis=0, keepdims=True) * (1.0 / (peers * count))
    return mean, lax.rsqrt(spread + norm_eps)


def stat_columns(found, count):
    return columns_of(list(pooled_stats(found[:, 0, :], found[:, 1, :], count)))


def sum_rows(found, lines):
    return [jnp.sum(found[:, index, :], axis=0, keepdims=True) for index in range(lines)]


def own_half(row, scene, out):
    size = out.shape[0]
    out[...] = jnp.where(scene == 0, row[:, 0:size], row[:, size : 2 * size]).reshape(size)


def side_sum(stacked, channels):
    width = stacked.shape[1]
    lane = lax.broadcasted_iota(jnp.int32, (channels, width), 1)
    left = pltpu.roll(stacked[:channels], 1, 1)
    right = pltpu.roll(stacked[2 * channels :], width - 1, 1)
    return (
        stacked[channels : 2 * channels]
        + jnp.where(lane > 0, left, 0.0)
        + jnp.where(lane < width - 1, right, 0.0)
    )


def layout(half, channels):
    first = 0
    second = first + half * -(-9 * channels // LANES)
    up = second + half * -(-9 * channels // LANES)
    vectors = up + channels
    return first, second, up, vectors, vectors + 16


def widen(value):
    missing = LANES - value.shape[1]
    if missing == 0:
        return value
    return jnp.concatenate([value, jnp.zeros((value.shape[0], missing), value.dtype)], axis=1)


def pack(held, out):
    first, second, up, pillar = held[:4]
    half, channels = first.shape[0], up.shape[1]
    starts = layout(half, channels)
    for ref, start in ((first, starts[0]), (second, starts[1])):
        for j in range(-(-9 * channels // LANES)):
            out[start + j * half : start + (j + 1) * half, :] = widen(
                ref[:, j * LANES : min((j + 1) * LANES, 9 * channels)]
            )
    out[starts[2] : starts[2] + channels, :] = widen(up[...])
    rows = [vector[...].astype(F32).reshape(1, -1) for vector in held[4:]]
    rows = [widen(row) for row in rows] + [jnp.zeros((16 - len(rows), LANES), F32)]
    turned = widen(pillar[...].astype(F32))
    rows += [turned, jnp.zeros((16 - turned.shape[0], LANES), F32)]
    out[starts[3] :, :] = jnp.concatenate(rows, axis=0).astype(BF16)


def unpack_kernel(
    both, w_pillar, cols, l_first, l_second, b_first, b_second, w_up, w_up_t,
    h_second, h_first_back, h_second_back, sems, *, inputs
):
    half = w_pillar.shape[0] // 2
    channels = 2 * half
    starts = layout(half, channels)
    tiles = -(-9 * channels // LANES)

    def wide(start):
        return jnp.concatenate(
            [
                jnp.concatenate(
                    [both[s, start + j * half : start + (j + 1) * half, :] for j in range(tiles)], axis=1
                )
                for s in range(2)
            ],
            axis=0,
        ).astype(F32)

    up = jnp.concatenate(
        [both[s, starts[2] : starts[2] + channels, 0:channels] for s in range(2)], axis=0
    )
    w_up[...] = up
    w_up_t[...] = jnp.transpose(up.astype(F32)).astype(BF16)
    turned = jnp.concatenate(
        [both[s, starts[4] : starts[4] + 16, 0:half].astype(F32) for s in range(2)], axis=1
    )
    w_pillar[...] = jnp.transpose(widen(turned))[0:channels, 0:inputs].astype(BF16)
    vectors = [both[s, starts[3] : starts[3] + 16, :].astype(F32) for s in range(2)]
    rows = []
    for index in range(8):
        size = half if index < 6 else channels
        row = jnp.concatenate([vectors[s][index : index + 1, 0:size] for s in range(2)], axis=1)
        rows.append(jnp.concatenate([row] * (LANES // (2 * size)), axis=1))
    cols[...] = columns_of(rows)
    zero = jnp.zeros((channels, channels), F32)
    copies = []
    for weight, ahead, back in (
        (wide(starts[0]), l_first, h_first_back), (wide(starts[1]), h_second, h_second_back)
    ):
        pieces = [
            [weight[:, (3 * a + b) * channels : (3 * a + b + 1) * channels] for b in range(3)]
            for a in range(3)
        ]
        flipped = [[jnp.transpose(pieces[a][b]) for b in range(3)] for a in range(3)]
        for j in range(2):
            for b in range(3):
                start = (3 * j + b) * channels
                ahead[start : start + channels, :] = jnp.concatenate(
                    [pieces[r - j][b] if 0 <= r - j <= 2 else zero for r in range(4)], axis=1
                ).astype(BF16)
                back[start : start + channels, :] = jnp.concatenate(
                    [flipped[j + 2 - r][2 - b] if 0 <= j + 2 - r <= 2 else zero for r in range(4)],
                    axis=1,
                ).astype(BF16)
    copies.append(move(h_second, l_second, sems, 0))
    copies.append(move(h_first_back, b_first, sems, 1))
    copies.append(move(h_second_back, b_second, sems, 2))
    for copy in copies:
        copy.wait()


def slot_line(wide, depth, inputs):
    return jnp.concatenate([wide[pl.ds(n, inputs, stride=depth), :] for n in range(depth)], axis=1)


def slot_mask(count, depth):
    return jnp.concatenate([jnp.where(count > n, 1.0, 0.0) for n in range(depth)], axis=1)


def ranks(tile):
    pillars = tile.shape[1]
    across = jnp.broadcast_to(tile, (pillars, pillars))
    down = jnp.transpose(across)
    row = lax.broadcasted_iota(jnp.int32, (pillars, pillars), 0)
    col = lax.broadcasted_iota(jnp.int32, (pillars, pillars), 1)
    return jnp.sum(jnp.where((across == down) & (row < col), 1.0, 0.0), axis=0, keepdims=True)


def moments_kernel(*refs, capacity):
    number = 16
    sources, out, packed = refs[:number], refs[number], refs[number + 1]
    held, wide, sems = refs[number + 2 : 2 * number + 2], refs[-2], refs[-1]
    copies = [move(sources[i], held[i], sems, i) for i in range(number)]
    tiles, cells, counts, points = held[:4]
    micros, _, inputs, depth, pillars = points.shape
    peers, scenes = out.shape[:2]
    copies[0].wait()
    copies[1].wait()
    lines = []
    for micro in range(micros):
        tile = tiles[micro].astype(F32)
        cell = (cells[micro] + 1).astype(F32)
        high = jnp.floor(cell * (1.0 / 16.0))
        low = cell - high * 16.0
        rank = ranks(tile)
        spot = lax.broadcasted_iota(jnp.int32, (capacity, pillars), 0).astype(F32)
        placed = jnp.where(spot == rank, 1.0, 0.0).astype(BF16)
        peer = lax.broadcasted_iota(jnp.int32, (peers, pillars), 0).astype(F32)
        for group in range(3):
            named = tile == peer + (group - 1.0)
            lines.append(
                16.0 * dot_lanes(jnp.where(named, high, 0.0).astype(BF16), placed)
                + dot_lanes(jnp.where(named, low, 0.0).astype(BF16), placed)
            )
    used = 3 * micros * capacity
    line = jnp.concatenate(lines + [jnp.zeros((peers, LANES - used), F32)], axis=1).reshape(peers, 1, LANES)
    for scene in range(scenes):
        out[:, scene, micros : micros + 1, :] = line
    copies[2].wait()
    copies[3].wait()
    for micro in range(micros):
        wide[...] = points[micro, 0].astype(F32).reshape(inputs * depth, pillars)
        rows = slot_line(wide, depth, inputs)
        mask = slot_mask(counts[micro], depth)
        total = jnp.sum(mask, axis=1, keepdims=True)
        mean = jnp.sum(rows * mask, axis=1, keepdims=True) / total
        centred = (rows - mean) * mask
        products = dot_lanes(centred, centred, lax.Precision.HIGHEST)
        lane = lax.broadcasted_iota(jnp.int32, (inputs, inputs), 1)
        diagonal = lax.broadcasted_iota(jnp.int32, (inputs, inputs), 0) == lane
        mean_row = jnp.sum(jnp.where(diagonal, mean, 0.0), axis=0, keepdims=True)
        row = jnp.concatenate(
            [products[k : k + 1] for k in range(inputs)]
            + [mean_row, total, jnp.zeros((1, LANES - inputs * inputs - inputs - 1), F32)],
            axis=1,
        )
        for scene in range(scenes):
            out[:, scene, micro : micro + 1, :] = jnp.broadcast_to(row[None], (peers, 1, LANES))
    for copy in copies[4:]:
        copy.wait()
    pack(held[4:], packed)


def cells_kernel(found, columns, rows, *, capacity):
    scene = lax.axis_index("scene")
    slots = columns.shape[0]
    peers = found.shape[0]
    values = found[:, 2, :]
    slot = lax.broadcasted_iota(jnp.int32, (slots, peers), 0)
    peer = lax.broadcasted_iota(jnp.int32, (slots, peers), 1)
    lane = lax.broadcasted_iota(jnp.int32, (slots, LANES), 1)
    row = lax.broadcasted_iota(jnp.int32, (slots, LANES), 0)
    result = jnp.zeros((slots, LANES), F32)
    chosen = jnp.where(peer == 2 * (slot // capacity) + scene, 1.0, 0.0)
    spread = dot(chosen, values, lax.Precision.HIGHEST)
    for micro in range(2):
        for group in range(3):
            mine = jnp.where(lane == (3 * micro + group) * capacity + row % capacity, spread, 0.0)
            column = jnp.sum(mine, axis=1, keepdims=True)
            result = jnp.where(lane == 2 * group + micro, column, result)
    columns[...] = result
    rows[...] = jnp.transpose(result)[0:8]


def pillar_kernel(
    found, points, counts, tiles, w_pillar, cols, send, pooled, stats, slots, kept, wide, lifted, acts,
    *, capacity
):
    micros, _, inputs, depth, pillars = points.shape
    channels = w_pillar.shape[0]
    weight = w_pillar[...]
    wide_weight = weight.astype(F32)
    rows_out = send.shape[0]
    square = inputs * inputs
    stacked, slot_rows, limits = [], [], []
    for micro in range(micros):
        wide[...] = points[micro, 0].astype(F32).reshape(inputs * depth, pillars)
        rows = slot_line(wide, depth, inputs)
        low = jnp.concatenate([rows, jnp.zeros((16 - inputs, rows.shape[1]), F32)], axis=0).astype(BF16)
        kept[micro] = low
        lifted[...] = dot(weight, low[0:inputs])
        moments = found[:, micro, :]
        sizes = moments[:, square + inputs : square + inputs + 1]
        means = moments[:, square : square + inputs]
        count = jnp.sum(sizes, axis=0, keepdims=True)
        mean = jnp.sum(means * sizes, axis=0, keepdims=True) / count
        away = means - mean
        products = lax.dot_general(
            away * sizes, away, (((0,), (0,)), ((), ())),
            preferred_element_type=F32, precision=lax.Precision.HIGHEST,
        )
        summed = jnp.sum(moments, axis=0, keepdims=True)
        products = products + jnp.concatenate(
            [summed[:, k * inputs : (k + 1) * inputs] for k in range(inputs)], axis=0
        )
        cov = products / count
        spun = wide_weight[:, 0:1] * cov[0:1]
        for k in range(1, inputs):
            spun = spun + wide_weight[:, k : k + 1] * cov[k : k + 1]
        spread = jnp.sum(spun * wide_weight, axis=1, keepdims=True)
        centre = jnp.sum(wide_weight * mean, axis=1, keepdims=True)
        rstd = lax.rsqrt(spread + norm_eps)
        inverse = jnp.broadcast_to(1.0 / count, (channels, 1))
        stats[micro] = jnp.concatenate(
            [
                centre, rstd, inverse, jnp.zeros((channels, 13), F32),
                spun, jnp.zeros((channels, 16 - inputs), F32),
                jnp.broadcast_to(mean, (channels, inputs)), jnp.zeros((channels, LANES - 32 - inputs), F32),
            ],
            axis=1,
        )
        scale = rstd * cols[0:channels, 0:1]
        shift = cols[0:channels, 1:2]
        limit = counts[micro].astype(F32)
        limits.append(limit)
        top = jnp.full((channels, pillars), -jnp.inf, F32)
        for n in range(depth):
            piece = slice(n * pillars, (n + 1) * pillars)
            normed = (lifted[:, piece] - centre) * scale + shift
            act = normed * sigmoid(normed)
            acts[:, piece] = act
            top = jnp.maximum(top, jnp.where(limit > n, act, -jnp.inf))
        total = jnp.zeros((channels, pillars), F32)
        for n in range(depth):
            piece = slice(n * pillars, (n + 1) * pillars)
            total = total + jnp.where(limit > n, jnp.exp(acts[:, piece] - top), 0.0)
        result = top + jnp.log(total)
        pooled[micro] = result
        parts = [jnp.zeros((channels, pillars), F32)] * micros
        parts[micro] = result.astype(BF16).astype(F32)
        stacked.append(jnp.transpose(jnp.concatenate(parts, axis=0)))
        tile = tiles[micro].astype(F32)
        slot_rows.append(tile * capacity + ranks(tile))
    slots[...] = jnp.concatenate(slot_rows + limits + [jnp.zeros((4, pillars), F32)], axis=0)
    values = jnp.concatenate(stacked, axis=0).astype(BF16)
    for group in range(3):
        place = lax.broadcasted_iota(jnp.int32, (rows_out, pillars), 0) + (group - 1) * capacity
        chosen = jnp.concatenate(
            [jnp.where(place.astype(F32) == row, 1.0, 0.0) for row in slot_rows], axis=1
        ).astype(BF16)
        send[:, group * LANES : (group + 1) * LANES] = dot(chosen, values).astype(BF16)


def own_stats(ref, first_row, rows, send):
    micros, _, channels, width = ref.shape
    sums, squares = [], []
    for micro in range(micros):
        total = fold(ref[micro, first_row])
        for row in range(first_row + 1, first_row + rows):
            total = total + fold(ref[micro, row])
        total = total * (1.0 / (rows * width))
        mean = jnp.sum(total, axis=1, keepdims=True)
        spread = jnp.zeros(total.shape, F32)
        for row in range(first_row, first_row + rows):
            away = ref[micro, row] - mean
            spread = spread + fold(away * away)
        sums.append(total)
        squares.append(spread)
    if channels == LANES:
        send_all(send, [row_of(part) for part in sums + squares])
    else:
        send_all(send, [row_of(*sums), row_of(*squares)])


def conv_rows(source, weight, out, shape):
    scenes, high, channels, width = shape
    pairs = high // 2

    def step(index, _):
        scene, at = index // pairs, 2 * (index % pairs)
        window = source[scene, pl.ds(at, 4)].reshape(4 * channels, width)
        parts = dot(weight[...], window)
        out[scene, at] = side_sum(parts[: 3 * channels], channels).astype(out.dtype)
        out[scene, at + 1] = side_sum(parts[3 * channels :], channels).astype(out.dtype)
        return 0

    lax.fori_loop(0, scenes * pairs, step, 0)


def canvas_kernel(found, columns, where_rows, l_first, out, kept, first_kept, send, canvas, sems, *, rows):
    scenes, high, channels, width = out.shape
    slots = found.shape[0]
    lane = lax.broadcasted_iota(jnp.int32, (slots, width), 1).astype(F32)
    reach = rows - 1
    for group in range(3):
        values = jnp.transpose(found[:, group * LANES : (group + 1) * LANES].astype(F32))
        wanted = ((1, rows), (0, rows), (0, reach))[group]
        for scene in range(scenes):
            at = 2 * group + scene
            column = columns[:, at : at + 1] - 1.0
            column = column - jnp.floor(column * (1.0 / width)) * width
            row = jnp.floor((where_rows[at : at + 1] - 1.0) * (1.0 / width))
            mine = values[scene * channels : (scene + 1) * channels]
            placed = jnp.concatenate(
                [jnp.where(row == r * 1.0, mine, 0.0) for r in range(*wanted)], axis=0
            ).astype(BF16)
            chosen = jnp.where(lane == column, 1.0, 0.0).astype(BF16)
            grid = dot(placed, chosen).astype(BF16)
            count = wanted[1] - wanted[0]
            start = (0, reach, reach + rows)[group]
            canvas[scene, start : start + count] = grid.reshape(count, channels, width)
    copies = [
        move(canvas.at[scene, reach - 1 : reach + rows + 1], kept.at[scene], sems, scene)
        for scene in range(scenes)
    ]
    conv_rows(canvas, l_first, out, out.shape)
    copies += [
        move(out.at[scene, reach - 2 : reach + rows], first_kept.at[scene], sems, scenes + scene)
        for scene in range(scenes)
    ]
    own_stats(out, reach - 1, rows, send)
    for copy in copies:
        copy.wait()


def second_kernel(found, cols, first_out, l_second_in, out, kept, stats, send, acts, l_second, sems,
                  *, rows, tiles):
    weight_copy = move(l_second_in, l_second, sems, 0)
    micros, high, channels, width = first_out.shape
    tile = lax.axis_index("tile")
    turned = stat_columns(found, float(rows * width))
    stats[...] = turned
    copies = []
    for micro in range(micros):
        part = slice(micro * channels, (micro + 1) * channels)
        centre = turned[part, 0:1]
        scale = turned[part, 1:2] * cols[0:channels, 2:3]
        shift = cols[0:channels, 3:4]

        def act_row(row, _, micro=micro, centre=centre, scale=scale, shift=shift):
            normed = (first_out[micro, row] - centre) * scale + shift
            on_grid = inside(tile, row - 2, (tiles, rows))
            acts[micro, row] = (normed * sigmoid(normed) * on_grid).astype(BF16)
            return 0

        lax.fori_loop(0, high, act_row, 0)
        copies.append(move(acts.at[micro, 1 : rows + 3], kept.at[micro], sems, 1 + micro))
    weight_copy.wait()
    conv_rows(acts, l_second, out, out.shape)
    own_stats(out, 1, rows, send)
    for copy in copies:
        copy.wait()


def up_kernel(found, cols, second_out, w_up, kept, upper, stats, send, acts, sems, *, rows):
    micros, _, channels, width = second_out.shape
    turned = stat_columns(found, float(rows * width))
    stats[...] = turned
    for micro in range(micros):
        part = slice(micro * channels, (micro + 1) * channels)
        centre = turned[part, 0:1]
        scale = turned[part, 1:2] * cols[0:channels, 4:5]
        shift = cols[0:channels, 5:6]

        def one(row, _, micro=micro, centre=centre, scale=scale, shift=shift):
            normed = (second_out[micro, row + 1] - centre) * scale + shift
            act = (normed * sigmoid(normed)).astype(BF16)
            acts[micro, row] = act
            upper[micro, row] = dot(w_up[...], act)
            return 0

        lax.fori_loop(0, rows, one, 0)
    copy = move(acts, kept, sems, 0)
    own_stats(upper, 0, rows, send)
    copy.wait()


def top_kernel(found, cols, upper, cot_in, features, grads, stats, send, cot, acts, sems, *, rows):
    fetched = move(cot_in, cot, sems, 0)
    micros, _, wide, width = upper.shape
    lines = []
    for micro in range(micros):
        lines += list(pooled_stats(found[:, micro, :], found[:, micros + micro, :], float(rows * width)))
    turned = columns_of(lines)
    stats[...] = turned
    gain, shift = cols[:, 6:7], cols[:, 7:8]
    fetched.wait()
    gain_rows, shift_rows, copies = [], [], []
    for micro in range(micros):
        centre, rstd = turned[:, 2 * micro : 2 * micro + 1], turned[:, 2 * micro + 1 : 2 * micro + 2]

        def one(row, carry, micro=micro, centre=centre, rstd=rstd):
            unit = (upper[micro, row] - centre) * rstd
            normed = unit * gain + shift
            gate = sigmoid(normed)
            act = normed * gate
            grad = cot[micro, row].astype(F32) * (gate + act * (1.0 - gate))
            acts[micro, row] = act.astype(BF16)
            grads[micro, row] = grad
            return carry[0] + fold(grad * unit), carry[1] + fold(grad)

        zero = jnp.zeros((wide, LANES), F32)
        gain_sum, shift_sum = lax.fori_loop(0, rows, one, (zero, zero))
        copies.append(move(acts.at[micro], features.at[micro], sems, 1 + micro))
        gain_rows.append(row_of(gain_sum))
        shift_rows.append(row_of(shift_sum))
    send_all(send, gain_rows + shift_rows)
    for copy in copies:
        copy.wait()


def second_back_kernel(
    found, cols, grads, upper, top_stats, second_out, second_stats, w_up_t, second_act,
    out, weight_grad, down_edge, up_edge, gain_grad, shift_grad, send, *, rows
):
    scene = lax.axis_index("scene")
    micros, _, wide, width = grads.shape
    channels = second_out.shape[2]
    sums = sum_rows(found, 2 * micros)
    own_half(sum(sums[:micros]), scene, gain_grad)
    own_half(sum(sums[micros:]), scene, shift_grad)
    turned = columns_of(sums) * (1.0 / (found.shape[0] * rows * width))
    gain, shift = cols[0:channels, 4:5], cols[0:channels, 5:6]
    gain_sums, shift_sums = [], []
    weight_grad[...] = jnp.zeros(weight_grad.shape, F32)
    for micro in range(micros):
        part = slice(micro * channels, (micro + 1) * channels)
        centre, rstd = second_stats[part, 0:1], second_stats[part, 1:2]
        top_centre = top_stats[:, 2 * micro : 2 * micro + 1]
        top_rstd = top_stats[:, 2 * micro + 1 : 2 * micro + 2]
        factor = cols[:, 6:7] * top_rstd
        slope_part = top_rstd * turned[:, micro : micro + 1]
        shift_part = turned[:, micros + micro : micros + micro + 1]

        def one(row, carry, micro=micro, centre=centre, rstd=rstd, top_centre=top_centre, factor=factor,
                slope_part=slope_part, shift_part=shift_part):
            low = factor * (grads[micro, row] - shift_part - (upper[micro, row] - top_centre) * slope_part)
            low = low.astype(BF16)
            weight_grad[...] = weight_grad[...] + dot_lanes(low, second_act[micro, row])
            unit = (second_out[micro, row + 1] - centre) * rstd
            normed = unit * gain + shift
            gate = sigmoid(normed)
            grad = dot(w_up_t[...], low) * (gate + normed * gate * (1.0 - gate))
            out[micro, row] = grad
            return carry[0] + fold(grad * unit), carry[1] + fold(grad)

        zero = jnp.zeros((channels, LANES), F32)
        gain_sum, shift_sum = lax.fori_loop(0, rows, one, (zero, zero))
        down_edge[micro] = out[micro, 0].astype(BF16)
        up_edge[micro] = out[micro, rows - 1].astype(BF16)
        gain_sums.append(gain_sum)
        shift_sums.append(shift_sum)
    send_all(send, [row_of(*gain_sums), row_of(*shift_sums)])


def low_rows(turned, grads, before, after, values, stats, gain, low, rows, tiles):
    micros, _, channels, width = grads.shape
    tile = lax.axis_index("tile")
    for micro in range(micros):
        part = slice(micro * channels, (micro + 1) * channels)
        centre, rstd = stats[part, 0:1], stats[part, 1:2]
        factor = gain * rstd
        slope_part, shift_part = rstd * turned[part, 0:1], turned[part, 1:2]

        def one(grad, row, micro=micro, centre=centre, factor=factor, slope_part=slope_part,
                shift_part=shift_part):
            return factor * (grad - shift_part - (values[micro, row] - centre) * slope_part)

        def own(row, _, micro=micro, one=one):
            low[micro, row + 1] = one(grads[micro, row], row + 1).astype(BF16)
            return 0

        lax.fori_loop(0, rows, own, 0)
        for ref, row in ((before, 0), (after, rows + 1)):
            edge = one(ref[micro].astype(F32), row) * inside(tile, row - 1, (tiles, rows))
            low[micro, row] = edge.astype(BF16)


def first_back_kernel(
    found, cols, grads, before, after, second_out, second_stats, first_in, first_stats, b_second_in, act_in,
    out, weight_grad, down_edge, up_edge, gain_grad, shift_grad, send, low, first_out, b_second, acts, sems,
    *, rows, tiles
):
    weight_copy = move(b_second_in, b_second, sems, 0)
    first_copy = move(first_in, first_out, sems, 1)
    act_copy = move(act_in, acts, sems, 2)
    scene = lax.axis_index("scene")
    micros, _, channels, width = grads.shape
    sums = sum_rows(found, 2)
    own_half(sums[0][:, :channels] + sums[0][:, channels:], scene, gain_grad)
    own_half(sums[1][:, :channels] + sums[1][:, channels:], scene, shift_grad)
    turned = columns_of(sums) * (1.0 / (found.shape[0] * rows * width))
    low_rows(turned, grads, before, after, second_out, second_stats, cols[0:channels, 4:5], low, rows, tiles)
    gain, shift = cols[0:channels, 2:3], cols[0:channels, 3:4]
    act_copy.wait()
    conv_grad(low, acts, weight_grad, rows)
    weight_copy.wait()
    first_copy.wait()
    gain_sums, shift_sums = [], []
    for micro in range(micros):
        part = slice(micro * channels, (micro + 1) * channels)
        centre, rstd = first_stats[part, 0:1], first_stats[part, 1:2]

        def step(index, carry, micro=micro, centre=centre, rstd=rstd):
            at = 2 * index
            window = low[micro, pl.ds(at, 4)].reshape(4 * channels, width)
            parts = dot(b_second[...], window)
            gain_sum, shift_sum = carry
            for j in range(2):
                grad_act = side_sum(parts[3 * channels * j : 3 * channels * (j + 1)], channels)
                unit = (first_out[micro, at + j + 1] - centre) * rstd
                normed = unit * gain + shift
                gate = sigmoid(normed)
                grad = grad_act * (gate + normed * gate * (1.0 - gate))
                out[micro, at + j] = grad
                gain_sum = gain_sum + fold(grad * unit)
                shift_sum = shift_sum + fold(grad)
            return gain_sum, shift_sum

        zero = jnp.zeros((channels, LANES), F32)
        gain_sum, shift_sum = lax.fori_loop(0, rows // 2, step, (zero, zero))
        down_edge[micro] = out[micro, 0].astype(BF16)
        up_edge[micro] = out[micro, rows - 1].astype(BF16)
        gain_sums.append(gain_sum)
        shift_sums.append(shift_sum)
    send_all(send, [row_of(*gain_sums), row_of(*shift_sums)])


def conv_grad(low, values, total, rows):
    micros, _, channels, width = low.shape
    lane = lax.broadcasted_iota(jnp.int32, (channels, width), 1)

    def step(index, carry):
        micro, row = index // rows, index % rows
        grad = low[micro, row + 1].astype(F32)
        left = jnp.where(lane < width - 1, pltpu.roll(grad, width - 1, 1), 0.0)
        right = jnp.where(lane > 0, pltpu.roll(grad, 1, 1), 0.0)
        stacked = jnp.concatenate([left, grad, right], axis=0).astype(BF16)
        window = values[micro, pl.ds(row, 3)].reshape(3 * channels, width)
        total[...] = total[...] + dot_lanes(stacked, window)
        return carry

    total[...] = jnp.zeros(total.shape, F32)
    lax.fori_loop(0, micros * rows, step, 0)


def half_rows(total, half, scene):
    channels = 2 * half
    start = scene * half
    mine = jnp.concatenate(
        [total[b * channels + start : b * channels + start + half, :] for b in range(3)], axis=0
    )
    wing = mine[:, LANES:]
    cut = wing.shape[0] // 2
    return [mine[:, :LANES], jnp.concatenate([wing[:cut], wing[cut:]], axis=1)]


def pick_kernel(
    found, cols, grads, before, after, first_in, first_stats, b_first_in, columns, where_rows,
    canvas_in, second_grad, top_grad,
    send, gain_grad, shift_grad, low, grid, first_out, b_first, canvas, first_grad, whole, sems,
    *, rows, tiles, each
):
    weight_copy = move(b_first_in, b_first, sems, 0)
    first_copy = move(first_in, first_out, sems, 1)
    canvas_copy = move(canvas_in, canvas, sems, 2)
    scene = lax.axis_index("scene")
    micros, _, channels, width = grads.shape
    sums = sum_rows(found, 2)
    own_half(sums[0][:, :channels] + sums[0][:, channels:], scene, gain_grad)
    own_half(sums[1][:, :channels] + sums[1][:, channels:], scene, shift_grad)
    turned = columns_of(sums) * (1.0 / (found.shape[0] * rows * width))
    first_copy.wait()
    low_rows(turned, grads, before, after, first_out, first_stats, cols[0:channels, 2:3], low, rows, tiles)
    weight_copy.wait()
    conv_rows(low, b_first, grid, grid.shape)
    canvas_copy.wait()
    conv_grad(low, canvas, first_grad, rows)
    half = channels // 2
    peers, block = send.shape[:2]
    for s in range(2):
        parts = half_rows(first_grad, half, s) + half_rows(second_grad, half, s)
        mine = top_grad[s * channels : (s + 1) * channels, :]
        parts.append(jnp.concatenate([mine[:half], mine[half:]], axis=1))
        parts = jnp.concatenate(parts, axis=0)
        whole[s, 0 : parts.shape[0]] = parts
        if whole.shape[1] > parts.shape[0]:
            whole[s, parts.shape[0] :] = jnp.zeros((whole.shape[1] - parts.shape[0], LANES), F32)
    slots = columns.shape[0]
    lane = lax.broadcasted_iota(jnp.int32, (slots, width), 1).astype(F32)
    picked = []
    for micro in range(micros):
        at = 2 + micro
        column = columns[:, at : at + 1] - 1.0
        column = column - jnp.floor(column * (1.0 / width)) * width
        place = jnp.floor((where_rows[at : at + 1] - 1.0) * (1.0 / width))
        chosen = jnp.where(lane == column, 1.0, 0.0).astype(BF16)
        here = dot_lanes(grid[micro].reshape(rows * channels, width), chosen)
        total = jnp.zeros((channels, slots), F32)
        for r in range(rows):
            total = total + jnp.where(place == r * 1.0, here[r * channels : (r + 1) * channels], 0.0)
        picked.append(total)
    picked = jnp.transpose(jnp.concatenate(picked, axis=0))
    capacity = slots // tiles
    rest = block - capacity - 2 * each
    for peer in range(peers):
        spot = peer // 2
        parts = [picked[spot * capacity : (spot + 1) * capacity]]
        parts += [whole[s, peer * each : (peer + 1) * each] for s in range(2)]
        parts.append(jnp.zeros((rest, LANES), F32))
        send[peer] = jnp.concatenate(parts, axis=0).astype(BF16)


def pillar_back_kernel(found, rows_in, w_pillar, cols, pooled, stats, slots, send, grads, lifted, rows, sems,
                       *, capacity, each):
    fetched = move(rows_in, rows, sems, 0)
    micros, channels, pillars = pooled.shape
    inputs = w_pillar.shape[1]
    depth = rows.shape[2] // pillars
    scene = lax.axis_index("scene")
    peers = found.shape[0]
    slot_count = peers // 2 * capacity
    returned = jnp.concatenate(
        [found[2 * t + scene].astype(F32)[0:capacity] for t in range(peers // 2)], axis=0
    )
    turned = jnp.transpose(returned)
    place = lax.broadcasted_iota(jnp.int32, (slot_count, pillars), 0).astype(F32)
    gain, shift = cols[0:channels, 0:1], cols[0:channels, 1:2]
    gain_sums, shift_sums = [], []
    outer = jnp.zeros((16, channels), F32)
    fetched.wait()
    for micro in range(micros):
        lifted[...] = dot(w_pillar[...], rows[micro, 0:inputs])
        chosen = jnp.where(place == slots[micro : micro + 1], 1.0, 0.0).astype(BF16)
        back = dot(turned[micro * channels : (micro + 1) * channels].astype(BF16), chosen)
        limit = slots[micros + micro : micros + micro + 1]
        centre, rstd = stats[micro, :, 0:1], stats[micro, :, 1:2]
        pool = pooled[micro]
        gain_sum = jnp.zeros((channels, pillars), F32)
        shift_sum = jnp.zeros((channels, pillars), F32)
        for n in range(depth):
            piece = slice(n * pillars, (n + 1) * pillars)
            unit = (lifted[:, piece] - centre) * rstd
            normed = unit * gain + shift
            gate = sigmoid(normed)
            act = normed * gate
            slope = gate + act * (1.0 - gate)
            grad = jnp.where(limit > n, back * jnp.exp(act - pool) * slope, 0.0)
            grads[micro, :, piece] = grad
            gain_sum = gain_sum + grad * unit
            shift_sum = shift_sum + grad
        gain_sums.append(gain_sum)
        shift_sums.append(shift_sum)
        scale = jnp.transpose(jnp.broadcast_to(rstd * gain, (channels, LANES)))[0:1]
        outer = outer + dot_lanes(rows[micro], grads[micro].astype(BF16)) * scale
    lines = [row_of(*gain_sums), row_of(*shift_sums)]
    for k in range(0, 12, 2):
        lines.append(jnp.concatenate([outer[k : k + 1], outer[k + 1 : k + 2]], axis=1))
    exact = jnp.concatenate(lines, axis=0)
    high = exact.astype(BF16).astype(F32)
    weights = jnp.sum(found[...].astype(F32), axis=0)
    rest = send.shape[2] - 16 - each
    for s in range(2):
        mine = weights[capacity + s * each : capacity + (s + 1) * each]
        block = jnp.concatenate([high, exact - high, mine, jnp.zeros((rest, LANES), F32)], axis=0).astype(BF16)
        send[:, s] = jnp.broadcast_to(block[None], (send.shape[0],) + block.shape)


def points_kernel(
    found, rows_in, grads, w_pillar, cols, stats, slots,
    points_grad, pillar_grad, gain_grad, shift_grad, first_grad, second_grad, up_grad, rows, lifted, sems,
    *, each
):
    fetched = move(rows_in, rows, sems, 0)
    scene = lax.axis_index("scene")
    micros, channels, _ = grads.shape
    _, _, inputs, depth, pillars = points_grad.shape
    half = channels // 2
    total = jnp.sum(found[:, 0:16, :].astype(F32), axis=0)
    total = total[0:8] + total[8:16]
    own_half(total[0:1, :channels] + total[0:1, channels:], scene, gain_grad)
    own_half(total[1:2, :channels] + total[1:2, channels:], scene, shift_grad)
    turned = jnp.transpose(total)
    weight_grad = jnp.concatenate(
        [turned[(k % 2) * channels : (k % 2 + 1) * channels, 2 + k // 2 : 3 + k // 2] for k in range(inputs)],
        axis=1,
    )
    weight = jnp.transpose(w_pillar[...].astype(F32)).astype(BF16)
    fetched.wait()
    for micro in range(micros):
        lifted[...] = dot(w_pillar[...], rows[micro, 0:inputs])
        part = slice(micro * channels, (micro + 1) * channels)
        centre, rstd, inverse = stats[micro, :, 0:1], stats[micro, :, 1:2], stats[micro, :, 2:3]
        factor = cols[0:channels, 0:1] * rstd
        gain_part, shift_part = turned[part, 0:1], turned[part, 1:2]
        spun, mean = stats[micro, :, 16 : 16 + inputs], stats[micro, :, 32 : 32 + inputs]
        weight_grad = weight_grad - factor * (shift_part * mean + gain_part * rstd * spun)
        gain_part, shift_part = gain_part * inverse * rstd, shift_part * inverse
        limit = slots[micros + micro : micros + micro + 1]
        for n in range(depth):
            piece = slice(n * pillars, (n + 1) * pillars)
            low = factor * (grads[micro, :, piece] - shift_part - (lifted[:, piece] - centre) * gain_part)
            low = jnp.where(limit > n, low, 0.0).astype(BF16)
            points_grad[micro, 0, :, n, :] = dot(weight, low)
    weight_grad = jnp.concatenate([weight_grad, jnp.zeros((channels, LANES - inputs), F32)], axis=1)
    weight_grad = jnp.transpose(weight_grad)[0:inputs]
    pillar_grad[...] = jnp.where(scene == 0, weight_grad[:, :half], weight_grad[:, half:])
    whole = jnp.concatenate(
        [found[peer].astype(F32)[16 : 16 + each] for peer in range(found.shape[0])], axis=0
    )
    for index, out in enumerate((first_grad, second_grad)):
        base = index * 9 * half * channels // LANES
        lead = 3 * half
        mine = whole[base : base + lead]
        wing = whole[base + lead : base + lead + lead // 2]
        wing = jnp.concatenate([wing[:, :channels], wing[:, channels:]], axis=0)
        both = jnp.concatenate([mine, wing], axis=1)
        for a in range(3):
            for b in range(3):
                at = (3 * a + b) * channels
                out[:, at : at + channels] = both[b * half : (b + 1) * half, a * channels : (a + 1) * channels]
    base = 2 * 9 * half * channels // LANES
    top = whole[base : base + half]
    up_grad[...] = jnp.concatenate([top[:, :channels], top[:, channels:]], axis=0)


def gathered(block, tiles):
    near = [[4 * i + j for j in range(4)] for i in range(tiles // 4)]
    far = [[4 * i + j for i in range(tiles // 4)] for j in range(4)]
    block = lax.all_gather(block, "scene", axis=0, tiled=True)
    block = lax.all_gather(block, "tile", axis=0, tiled=True, axis_index_groups=near)
    return lax.all_gather(block, "tile", axis=0, tiled=True, axis_index_groups=far)


def swap(blocks, axes):
    return lax.all_to_all(blocks, axes, split_axis=0, concat_axis=0)


def shards(
    points, point_counts, pillar_tile, pillar_cell,
    pillar_weight, pillar_gain, pillar_shift,
    first_weight, first_gain, first_shift,
    second_weight, second_gain, second_shift,
    up_weight, up_gain, up_shift, cotangent,
):
    micros, _, inputs, depth, pillars = points.shape
    channels = up_weight.shape[1]
    upper = cotangent.shape[2]
    rows, width = cotangent.shape[3:]
    tiles = lax.axis_size("tile")
    scenes = lax.axis_size("scene")
    peers = tiles * scenes
    capacity = 2 * pillars // tiles
    slot_count = tiles * capacity
    half = channels // 2

    def vmem(shape, dtype):
        return pltpu.VMEM(shape, dtype)

    def grid(high, dtype=F32, lead=channels):
        return ((micros, high, lead, width), dtype)

    sums = ((peers, 2, LANES), F32)
    sources = (
        pillar_tile, pillar_cell, point_counts, points,
        first_weight, second_weight, up_weight, pillar_weight.T,
        pillar_gain, pillar_shift, first_gain, first_shift, second_gain, second_shift, up_gain, up_shift,
    )
    moments, packed = run(
        functools.partial(moments_kernel, capacity=capacity),
        [((tiles, scenes, 4, LANES), F32), ((layout(half, channels)[-1] + 16, LANES), BF16)],
        *sources,
        hbm=range(len(sources)), copies=len(sources), limit=WIDE_LIMIT,
        scratch=[vmem(source.shape, source.dtype) for source in sources]
        + [vmem((inputs * depth, pillars), F32)],
    )
    moments = swap(moments.reshape(peers, 4, LANES), BOTH)
    both = lax.all_gather(packed, "scene")
    taps = ((6 * channels, 4 * channels), BF16)
    w_pillar, cols, l_first, l_second, b_first, b_second, w_up, w_up_t = run(
        functools.partial(unpack_kernel, inputs=inputs),
        [
            ((channels, inputs), BF16), ((LANES, 8), F32), taps, taps + (1,), taps + (1,), taps + (1,),
            ((upper, channels), BF16), ((channels, upper), BF16),
        ],
        both,
        scratch=[vmem(*taps), vmem(*taps), vmem(*taps)], copies=3,
    )
    cot = cotangent[:, 0].transpose(0, 2, 1, 3)

    send, pooled, pillar_stats, slots, point_rows = run(
        functools.partial(pillar_kernel, capacity=capacity),
        [
            ((slot_count, 3 * LANES), BF16), ((micros, channels, pillars), F32),
            ((micros, channels, LANES), F32), ((8, pillars), F32), ((micros, 16, depth * pillars), BF16),
        ],
        moments, points, point_counts, pillar_tile, w_pillar, cols,
        scratch=[
            vmem((inputs * depth, pillars), F32), vmem((channels, depth * pillars), F32),
            vmem((channels, depth * pillars), F32),
        ],
    )
    arrived = swap(send.reshape(tiles, capacity, 3 * LANES), "tile").reshape(slot_count, 3 * LANES)
    cell_columns, cell_rows = run(
        functools.partial(cells_kernel, capacity=capacity),
        [((slot_count, LANES), F32), ((8, slot_count), F32)],
        moments,
        cost=pl.CostEstimate(flops=10**7, bytes_accessed=10**6, transcendentals=0),
    )
    arrived, cot = lax.optimization_barrier((arrived, cot))

    first_out, canvas, first_kept, send = run(
        functools.partial(canvas_kernel, rows=rows),
        [grid(rows + 4), grid(rows + 2, BF16) + (1,), grid(rows + 2) + (1,), ((1, 2, LANES), F32)],
        arrived, cell_columns, cell_rows, l_first,
        scratch=[vmem(*grid(rows + 6, BF16))], copies=4,
    )
    second_out, first_act, first_stats, send = run(
        functools.partial(second_kernel, rows=rows, tiles=tiles),
        [grid(rows + 2), grid(rows + 2, BF16) + (1,), ((LANES, 8), F32), sums],
        gathered(send, tiles), cols, first_out, l_second,
        hbm=(3,), scratch=[vmem(*grid(rows + 4, BF16)), vmem(*taps)], copies=3,
    )
    second_act, up_out, second_stats, send = run(
        functools.partial(up_kernel, rows=rows),
        [grid(rows, BF16) + (1,), grid(rows, F32, upper), ((LANES, 8), F32), ((peers, 4, LANES), F32)],
        swap(send, BOTH), cols, second_out, w_up,
        scratch=[vmem(*grid(rows, BF16))], copies=1,
    )
    features, grads, top_stats, send = run(
        functools.partial(top_kernel, rows=rows),
        [
            grid(rows, BF16, upper) + (1,), grid(rows, F32, upper), ((LANES, 8), F32),
            ((peers, 4, LANES), F32),
        ],
        swap(send, BOTH), cols, up_out, cot,
        hbm=(3,), scratch=[vmem(*grid(rows, BF16, upper)), vmem(*grid(rows, BF16, upper))], copies=3,
    )
    edge = ((micros, channels, width), BF16)
    vector, top_vector, matrix = ((half,), F32), ((upper // 2,), F32), ((half, 9 * channels), F32)
    second_dz, top_grad, down_edge, up_edge, up_gain_grad, up_shift_grad, send = run(
        functools.partial(second_back_kernel, rows=rows),
        [grid(rows), ((upper, channels), F32), edge, edge, top_vector, top_vector, sums],
        swap(send, BOTH), cols, grads, up_out, top_stats, second_out, second_stats, w_up_t, second_act,
    )
    rising = [(i, i + 1) for i in range(tiles - 1)]
    falling = [(j, i) for i, j in rising]
    cross = ((3 * channels, 3 * channels), F32)
    first_dz, second_cross, down_next, up_next, second_gain_grad, second_shift_grad, send = run(
        functools.partial(first_back_kernel, rows=rows, tiles=tiles),
        [grid(rows), cross, edge, edge, vector, vector, sums],
        swap(send, BOTH), cols, second_dz,
        lax.ppermute(up_edge, "tile", rising), lax.ppermute(down_edge, "tile", falling),
        second_out, second_stats, first_kept, first_stats, b_second, first_act,
        hbm=(7, 9, 10),
        scratch=[
            vmem(*grid(rows + 2, BF16)), vmem(*grid(rows + 2)), vmem(*taps), vmem(*grid(rows + 2, BF16)),
        ],
        copies=3,
    )
    length = (2 * 9 * half * channels + upper * half) // LANES
    each = -(-length // peers)
    block = -(-(capacity + 2 * each) // 8) * 8
    send, first_gain_grad, first_shift_grad = run(
        functools.partial(pick_kernel, rows=rows, tiles=tiles, each=each),
        [((peers, block, LANES), BF16), vector, vector],
        swap(send, BOTH), cols, first_dz,
        lax.ppermute(up_next, "tile", rising), lax.ppermute(down_next, "tile", falling),
        first_kept, first_stats, b_first, cell_columns, cell_rows, canvas, second_cross, top_grad,
        hbm=(5, 7, 10),
        scratch=[
            vmem(*grid(rows + 2, BF16)), vmem(*grid(rows, BF16)), vmem(*grid(rows + 2)), vmem(*taps),
            vmem(*grid(rows + 2, BF16)), vmem(*cross), vmem((scenes, peers * each, LANES), F32),
        ],
        copies=3,
    )
    block = 16 + -(-each // 16) * 16
    send, pillar_dz = run(
        functools.partial(pillar_back_kernel, capacity=capacity, each=each),
        [((tiles, scenes, block, LANES), BF16), ((micros, channels, depth * pillars), F32)],
        swap(send, BOTH), point_rows, w_pillar, cols, pooled, pillar_stats, slots,
        hbm=(1,),
        scratch=[vmem((channels, depth * pillars), F32), vmem((micros, 16, depth * pillars), BF16)],
        copies=1,
    )
    send, features = lax.optimization_barrier((send, features))
    features = features.transpose(0, 2, 1, 3)[:, None]
    points_grad, pillar_grad, pillar_gain_grad, pillar_shift_grad, first_grad, second_grad, up_grad = run(
        functools.partial(points_kernel, each=each),
        [
            ((micros, 1, inputs, depth, pillars), F32), ((inputs, half), F32), vector, vector,
            matrix, matrix, ((upper // 2, channels), F32),
        ],
        swap(send.reshape(peers, block, LANES), BOTH), point_rows, pillar_dz, w_pillar, cols, pillar_stats, slots,
        hbm=(1,),
        scratch=[vmem((micros, 16, depth * pillars), BF16), vmem((channels, depth * pillars), F32)],
        copies=1,
    )
    return (
        features, points_grad,
        pillar_grad.T, pillar_gain_grad, pillar_shift_grad,
        first_grad, first_gain_grad, first_shift_grad,
        second_grad, second_gain_grad, second_shift_grad,
        up_grad, up_gain_grad, up_shift_grad,
    )


def solution(mesh):
    matrix, vector = P("scene", None), P("scene")
    grid = P(None, "scene", None, "tile", None)
    cloud = P(None, "scene", None, None, "tile")
    pillar = P(None, "scene", "tile")
    weights = (matrix, vector, vector) * 4
    return jax.shard_map(
        shards,
        mesh=mesh,
        in_specs=(cloud, pillar, pillar, pillar) + weights + (grid,),
        out_specs=(grid, cloud) + weights,
        check_vma=False,
    )
```

```python
import functools

import jax
import jax.numpy as jnp
from jax import lax
from jax.experimental import pallas as pl
from jax.experimental.pallas import tpu as pltpu
from jax.sharding import PartitionSpec as P

norm_eps = 0.001
BOTH = ("tile", "scene")
F32 = jnp.float32
BF16 = jnp.bfloat16
VMEM_LIMIT = 24 * 1024 * 1024
WIDE_LIMIT = 60 * 1024 * 1024
LANES = 128


def run(kernel, outs, *args, hbm=(), scratch=(), copies=0, cost=None, limit=VMEM_LIMIT):
    specs = [
        pl.BlockSpec(memory_space=pltpu.HBM if index in hbm else pltpu.VMEM) for index in range(len(args))
    ]
    scratch = list(scratch)
    if copies:
        scratch.append(pltpu.SemaphoreType.DMA((copies,)))
    return pl.pallas_call(
        kernel,
        out_shape=[jax.ShapeDtypeStruct(out[0], out[1]) for out in outs],
        in_specs=specs,
        out_specs=[
            pl.BlockSpec(memory_space=pltpu.HBM if len(out) > 2 else pltpu.VMEM) for out in outs
        ],
        scratch_shapes=scratch,
        compiler_params=pltpu.CompilerParams(vmem_limit_bytes=limit),
        cost_estimate=cost,
    )(*args)


def move(source, target, sems, index):
    copy = pltpu.make_async_copy(source, target, sems.at[index])
    copy.start()
    return copy


def dot(left, right, precision=None):
    return jnp.dot(left, right, preferred_element_type=F32, precision=precision)


def dot_lanes(left, right, precision=None):
    return lax.dot_general(
        left, right, (((1,), (1,)), ((), ())), preferred_element_type=F32, precision=precision
    )


def sigmoid(values):
    return 0.5 + 0.5 * jnp.tanh(0.5 * values)


def fold(values):
    total = values[:, :LANES]
    for start in range(LANES, values.shape[1], LANES):
        total = total + values[:, start : start + LANES]
    return total


def row_of(left, right=None):
    both = left if right is None else jnp.concatenate([left, right], axis=0)
    return jnp.sum(jnp.transpose(both), axis=0, keepdims=True)


def columns_of(rows):
    rows = rows + [jnp.zeros((8 - len(rows), LANES), F32)] if len(rows) < 8 else rows
    return jnp.transpose(jnp.concatenate(rows, axis=0))


def inside(tile, row, height):
    tiles, rows = height
    place = tile * rows + row
    return jnp.where((place >= 0) & (place < tiles * rows), 1.0, 0.0).astype(F32)


def send_all(ref, rows):
    for index, row in enumerate(rows):
        ref[:, index : index + 1, :] = jnp.broadcast_to(row[None], (ref.shape[0], 1, LANES))


def pooled_stats(means, squares, count):
    peers = means.shape[0]
    mean = jnp.sum(means, axis=0, keepdims=True) * (1.0 / peers)
    away = means - mean
    spread = jnp.sum(squares + count * away * away, axis=0, keepdims=True) * (1.0 / (peers * count))
    return mean, lax.rsqrt(spread + norm_eps)


def stat_columns(found, count):
    return columns_of(list(pooled_stats(found[:, 0, :], found[:, 1, :], count)))


def sum_rows(found, lines):
    return [jnp.sum(found[:, index, :], axis=0, keepdims=True) for index in range(lines)]


def own_half(row, scene, out):
    size = out.shape[0]
    out[...] = jnp.where(scene == 0, row[:, 0:size], row[:, size : 2 * size]).reshape(size)


def edges(channels, width):
    lane = lax.broadcasted_iota(jnp.int32, (channels, width), 1)
    return lane > 0, lane < width - 1


def spread(row, masks):
    zero = jnp.zeros_like(row)
    left = jnp.where(masks[0], pltpu.roll(row, 1, 1), zero)
    right = jnp.where(masks[1], pltpu.roll(row, row.shape[1] - 1, 1), zero)
    return jnp.concatenate([left, row, right], axis=0)


def layout(half, channels):
    first = 0
    second = first + half * -(-9 * channels // LANES)
    up = second + half * -(-9 * channels // LANES)
    vectors = up + channels
    return first, second, up, vectors, vectors + 16


def widen(value):
    missing = LANES - value.shape[1]
    if missing == 0:
        return value
    return jnp.concatenate([value, jnp.zeros((value.shape[0], missing), value.dtype)], axis=1)


def pack(held, out):
    first, second, up, pillar = held[:4]
    half, channels = first.shape[0], up.shape[1]
    starts = layout(half, channels)
    for ref, start in ((first, starts[0]), (second, starts[1])):
        for j in range(-(-9 * channels // LANES)):
            out[start + j * half : start + (j + 1) * half, :] = widen(
                ref[:, j * LANES : min((j + 1) * LANES, 9 * channels)]
            )
    out[starts[2] : starts[2] + channels, :] = widen(up[...])
    rows = [vector[...].astype(F32).reshape(1, -1) for vector in held[4:]]
    rows = [widen(row) for row in rows] + [jnp.zeros((16 - len(rows), LANES), F32)]
    turned = widen(pillar[...].astype(F32))
    rows += [turned, jnp.zeros((16 - turned.shape[0], LANES), F32)]
    out[starts[3] :, :] = jnp.concatenate(rows, axis=0).astype(BF16)


def unpack_kernel(
    both, w_pillar, cols, l_first, l_second, b_first, b_second, w_up, w_up_t,
    h_second, h_first_back, h_second_back, sems, *, inputs
):
    half = w_pillar.shape[0] // 2
    channels = 2 * half
    starts = layout(half, channels)
    tiles = -(-9 * channels // LANES)

    def wide(start):
        return jnp.concatenate(
            [
                jnp.concatenate(
                    [both[s, start + j * half : start + (j + 1) * half, :] for j in range(tiles)], axis=1
                )
                for s in range(2)
            ],
            axis=0,
        ).astype(F32)

    up = jnp.concatenate(
        [both[s, starts[2] : starts[2] + channels, 0:channels] for s in range(2)], axis=0
    )
    w_up[...] = up
    w_up_t[...] = jnp.transpose(up.astype(F32)).astype(BF16)
    turned = jnp.concatenate(
        [both[s, starts[4] : starts[4] + 16, 0:half].astype(F32) for s in range(2)], axis=1
    )
    w_pillar[...] = jnp.transpose(widen(turned))[0:channels, 0:inputs].astype(BF16)
    vectors = [both[s, starts[3] : starts[3] + 16, :].astype(F32) for s in range(2)]
    rows = []
    for index in range(8):
        size = half if index < 6 else channels
        row = jnp.concatenate([vectors[s][index : index + 1, 0:size] for s in range(2)], axis=1)
        rows.append(jnp.concatenate([row] * (LANES // (2 * size)), axis=1))
    cols[...] = columns_of(rows)
    zero = jnp.zeros((channels, 3 * channels), F32)
    copies = []
    for weight, ahead, back in (
        (wide(starts[0]), l_first, h_first_back), (wide(starts[1]), h_second, h_second_back)
    ):
        weight = weight[:, : 9 * channels]
        turned = jnp.transpose(weight)
        flipped = jnp.concatenate(
            [turned[tap * channels : (tap + 1) * channels] for tap in range(8, -1, -1)], axis=1
        )
        for ref, taps in ((ahead, weight), (back, flipped)):
            ref[0:channels, :] = jnp.concatenate([taps, zero], axis=1).astype(BF16)
            ref[channels : 2 * channels, :] = jnp.concatenate([zero, taps], axis=1).astype(BF16)
    copies.append(move(h_second, l_second, sems, 0))
    copies.append(move(h_first_back, b_first, sems, 1))
    copies.append(move(h_second_back, b_second, sems, 2))
    for copy in copies:
        copy.wait()


def slot_line(wide, depth, inputs):
    return jnp.concatenate([wide[pl.ds(n, inputs, stride=depth), :] for n in range(depth)], axis=1)


def slot_mask(count, depth):
    return jnp.concatenate([jnp.where(count > n, 1.0, 0.0) for n in range(depth)], axis=1)


def ranks(tile):
    pillars = tile.shape[1]
    across = jnp.broadcast_to(tile, (pillars, pillars))
    down = jnp.transpose(across)
    row = lax.broadcasted_iota(jnp.int32, (pillars, pillars), 0)
    col = lax.broadcasted_iota(jnp.int32, (pillars, pillars), 1)
    return jnp.sum(jnp.where((across == down) & (row < col), 1.0, 0.0), axis=0, keepdims=True)


def moments_kernel(*refs, capacity):
    number = 16
    sources, out, packed, lines_out, slots = refs[:number], *refs[number : number + 4]
    held, wide, sems = refs[number + 4 : 2 * number + 4], refs[-2], refs[-1]
    copies = [move(sources[i], held[i], sems, i) for i in range(number)]
    tiles, cells, counts, points = held[:4]
    micros, _, inputs, depth, pillars = points.shape
    peers, scenes = out.shape[:2]
    copies[0].wait()
    copies[1].wait()
    lines, slot_rows = [], []
    for micro in range(micros):
        tile = tiles[micro].astype(F32)
        cell = (cells[micro] + 1).astype(F32)
        high = jnp.floor(cell * (1.0 / 16.0))
        low = cell - high * 16.0
        rank = ranks(tile)
        slot_rows.append(tile * capacity + rank)
        spot = lax.broadcasted_iota(jnp.int32, (capacity, pillars), 0).astype(F32)
        placed = jnp.where(spot == rank, 1.0, 0.0).astype(BF16)
        peer = lax.broadcasted_iota(jnp.int32, (peers, pillars), 0).astype(F32)
        for group in range(3):
            named = tile == peer + (group - 1.0)
            lines.append(
                16.0 * dot_lanes(jnp.where(named, high, 0.0).astype(BF16), placed)
                + dot_lanes(jnp.where(named, low, 0.0).astype(BF16), placed)
            )
    used = 3 * micros * capacity
    line = jnp.concatenate(lines + [jnp.zeros((peers, LANES - used), F32)], axis=1).reshape(peers, 1, LANES)
    for scene in range(scenes):
        out[:, scene, micros : micros + 1, :] = line
    copies[2].wait()
    copies[3].wait()
    limits = [counts[micro].astype(F32) for micro in range(micros)]
    slots[...] = jnp.concatenate(
        slot_rows + limits + [jnp.zeros((8 - 2 * micros, pillars), F32)], axis=0
    )
    for micro in range(micros):
        wide[...] = points[micro, 0].astype(F32).reshape(inputs * depth, pillars)
        rows = slot_line(wide, depth, inputs)
        lines_out[micro] = jnp.concatenate(
            [rows, jnp.zeros((16 - inputs, rows.shape[1]), F32)], axis=0
        ).astype(BF16)
        mask = slot_mask(counts[micro], depth)
        total = jnp.sum(mask, axis=1, keepdims=True)
        mean = jnp.sum(rows * mask, axis=1, keepdims=True) / total
        centred = (rows - mean) * mask
        products = dot_lanes(centred, centred, lax.Precision.HIGHEST)
        lane = lax.broadcasted_iota(jnp.int32, (inputs, inputs), 1)
        diagonal = lax.broadcasted_iota(jnp.int32, (inputs, inputs), 0) == lane
        mean_row = jnp.sum(jnp.where(diagonal, mean, 0.0), axis=0, keepdims=True)
        row = jnp.concatenate(
            [products[k : k + 1] for k in range(inputs)]
            + [mean_row, total, jnp.zeros((1, LANES - inputs * inputs - inputs - 1), F32)],
            axis=1,
        )
        for scene in range(scenes):
            out[:, scene, micro : micro + 1, :] = jnp.broadcast_to(row[None], (peers, 1, LANES))
    for copy in copies[4:]:
        copy.wait()
    pack(held[4:], packed)


def cells_kernel(found, columns, rows, *, capacity):
    scene = lax.axis_index("scene")
    slots = columns.shape[0]
    peers = found.shape[0]
    values = found[:, 2, :]
    slot = lax.broadcasted_iota(jnp.int32, (slots, peers), 0)
    peer = lax.broadcasted_iota(jnp.int32, (slots, peers), 1)
    lane = lax.broadcasted_iota(jnp.int32, (slots, LANES), 1)
    row = lax.broadcasted_iota(jnp.int32, (slots, LANES), 0)
    result = jnp.zeros((slots, LANES), F32)
    chosen = jnp.where(peer == 2 * (slot // capacity) + scene, 1.0, 0.0)
    spread = dot(chosen, values, lax.Precision.HIGHEST)
    for micro in range(2):
        for group in range(3):
            mine = jnp.where(lane == (3 * micro + group) * capacity + row % capacity, spread, 0.0)
            column = jnp.sum(mine, axis=1, keepdims=True)
            result = jnp.where(lane == 2 * group + micro, column, result)
    columns[...] = result
    rows[...] = jnp.transpose(result)[0:8]


def pillar_kernel(
    found, point_rows, slots, w_pillar, cols, send, pooled, lifted, acts, *, capacity
):
    micros = point_rows.shape[0]
    channels, inputs = w_pillar.shape
    pillars = slots.shape[1]
    depth = point_rows.shape[2] // pillars
    weight = w_pillar[...]
    wide_weight = weight.astype(F32)
    rows_out = send.shape[0]
    square = inputs * inputs
    stacked = []
    for micro in range(micros):
        lifted[...] = dot(weight, point_rows[micro, 0:inputs])
        moments = found[:, micro, :]
        sizes = moments[:, square + inputs : square + inputs + 1]
        means = moments[:, square : square + inputs]
        count = jnp.sum(sizes, axis=0, keepdims=True)
        mean = jnp.sum(means * sizes, axis=0, keepdims=True) / count
        away = means - mean
        products = lax.dot_general(
            away * sizes, away, (((0,), (0,)), ((), ())),
            preferred_element_type=F32, precision=lax.Precision.HIGHEST,
        )
        summed = jnp.sum(moments, axis=0, keepdims=True)
        products = products + jnp.concatenate(
            [summed[:, k * inputs : (k + 1) * inputs] for k in range(inputs)], axis=0
        )
        cov = products / count
        spun = wide_weight[:, 0:1] * cov[0:1]
        for k in range(1, inputs):
            spun = spun + wide_weight[:, k : k + 1] * cov[k : k + 1]
        spread = jnp.sum(spun * wide_weight, axis=1, keepdims=True)
        centre = jnp.sum(wide_weight * mean, axis=1, keepdims=True)
        rstd = lax.rsqrt(spread + norm_eps)
        inverse = jnp.broadcast_to(1.0 / count, (channels, 1))
        pooled[micros + micro] = jnp.concatenate(
            [
                centre, rstd, inverse, jnp.zeros((channels, 13), F32),
                spun, jnp.zeros((channels, 16 - inputs), F32),
                jnp.broadcast_to(mean, (channels, inputs)), jnp.zeros((channels, LANES - 32 - inputs), F32),
            ],
            axis=1,
        )
        scale = rstd * cols[0:channels, 0:1]
        shift = cols[0:channels, 1:2]
        limit = slots[micros + micro : micros + micro + 1]
        top = jnp.full((channels, pillars), -jnp.inf, F32)
        for n in range(depth):
            piece = slice(n * pillars, (n + 1) * pillars)
            normed = (lifted[:, piece] - centre) * scale + shift
            act = normed * sigmoid(normed)
            acts[:, piece] = act
            top = jnp.maximum(top, jnp.where(limit > n, act, -jnp.inf))
        total = jnp.zeros((channels, pillars), F32)
        for n in range(depth):
            piece = slice(n * pillars, (n + 1) * pillars)
            total = total + jnp.where(limit > n, jnp.exp(acts[:, piece] - top), 0.0)
        result = top + jnp.log(total)
        pooled[micro] = result
        parts = [jnp.zeros((channels, pillars), F32)] * micros
        parts[micro] = result.astype(BF16).astype(F32)
        stacked.append(jnp.transpose(jnp.concatenate(parts, axis=0)))
    pooled[2 * micros, 0:8] = slots[...]
    slot_rows = [slots[micro : micro + 1] for micro in range(micros)]
    values = jnp.concatenate(stacked, axis=0).astype(BF16)
    for group in range(3):
        place = lax.broadcasted_iota(jnp.int32, (rows_out, pillars), 0) + (group - 1) * capacity
        chosen = jnp.concatenate(
            [jnp.where(place.astype(F32) == row, 1.0, 0.0) for row in slot_rows], axis=1
        ).astype(BF16)
        send[:, group * LANES : (group + 1) * LANES] = dot(chosen, values).astype(BF16)


def own_stats(ref, first_row, rows, send):
    micros, _, channels, width = ref.shape
    sums, squares = [], []
    for micro in range(micros):
        total = fold(ref[micro, first_row])
        for row in range(first_row + 1, first_row + rows):
            total = total + fold(ref[micro, row])
        total = total * (1.0 / (rows * width))
        mean = jnp.sum(total, axis=1, keepdims=True)
        spread = jnp.zeros(total.shape, F32)
        for row in range(first_row, first_row + rows):
            away = ref[micro, row] - mean
            spread = spread + fold(away * away)
        sums.append(total)
        squares.append(spread)
    if channels == LANES:
        send_all(send, [row_of(part) for part in sums + squares])
    else:
        send_all(send, [row_of(*sums), row_of(*squares)])


def conv_pair(source, weight, micro, at, channels):
    window = source[micro, pl.ds(at, 4)].reshape(12 * channels, source.shape[3])
    return dot(weight[...], window)


def conv_rows(source, weight, out, shape):
    micros, high, channels, width = shape
    pairs = high // 2

    def step(index, _):
        micro, at = index // pairs, 2 * (index % pairs)
        both = conv_pair(source, weight, micro, at, channels)
        out[micro, at] = both[:channels].astype(out.dtype)
        out[micro, at + 1] = both[channels:].astype(out.dtype)
        return 0

    lax.fori_loop(0, micros * pairs, step, 0, unroll=2)


def canvas_kernel(found, columns, where_rows, l_first, out, kept, send, canvas, *, rows):
    scenes, high, channels, width = out.shape
    masks = edges(channels, width)
    slots = found.shape[0]
    lane = lax.broadcasted_iota(jnp.int32, (slots, width), 1).astype(F32)
    reach = rows - 1
    for group in range(3):
        values = jnp.transpose(found[:, group * LANES : (group + 1) * LANES].astype(F32))
        wanted = ((1, rows), (0, rows), (0, reach))[group]
        for scene in range(scenes):
            at = 2 * group + scene
            column = columns[:, at : at + 1] - 1.0
            column = column - jnp.floor(column * (1.0 / width)) * width
            row = jnp.floor((where_rows[at : at + 1] - 1.0) * (1.0 / width))
            mine = values[scene * channels : (scene + 1) * channels]
            placed = jnp.concatenate(
                [jnp.where(row == r * 1.0, mine, 0.0) for r in range(*wanted)], axis=0
            ).astype(BF16)
            chosen = jnp.where(lane == column, 1.0, 0.0).astype(BF16)
            grid = dot(placed, chosen).astype(BF16)
            count = wanted[1] - wanted[0]
            start = (0, reach, reach + rows)[group]
            for r in range(count):
                row = grid[r * channels : (r + 1) * channels]
                canvas[scene, start + r] = spread(row, masks)
                if reach - 1 <= start + r <= reach + rows:
                    kept[scene, start + r - (reach - 1)] = row
    conv_rows(canvas, l_first, out, out.shape)
    own_stats(out, reach - 1, rows, send)


def second_kernel(found, cols, first_out, l_second_in, out, kept, stats, send, acts, l_second, sems,
                  *, rows, tiles):
    weight_copy = move(l_second_in, l_second, sems, 0)
    micros, high, channels, width = first_out.shape
    tile = lax.axis_index("tile")
    turned = stat_columns(found, float(rows * width))
    stats[...] = turned
    masks = edges(channels, width)
    for micro in range(micros):
        part = slice(micro * channels, (micro + 1) * channels)
        centre = turned[part, 0:1]
        scale = turned[part, 1:2] * cols[0:channels, 2:3]
        shift = cols[0:channels, 3:4]

        def act_row(row, _, micro=micro, centre=centre, scale=scale, shift=shift):
            normed = (first_out[micro, row] - centre) * scale + shift
            on_grid = inside(tile, row - 2, (tiles, rows))
            act = (normed * sigmoid(normed) * on_grid).astype(BF16)
            acts[micro, row] = spread(act, masks)
            kept[micro, row] = act
            return 0

        lax.fori_loop(0, high, act_row, 0, unroll=2)
    weight_copy.wait()
    conv_rows(acts, l_second, out, out.shape)
    own_stats(out, 1, rows, send)


def up_kernel(found, cols, second_out, w_up, acts, upper, stats, send, *, rows):
    micros, _, channels, width = second_out.shape
    turned = stat_columns(found, float(rows * width))
    stats[...] = turned
    for micro in range(micros):
        part = slice(micro * channels, (micro + 1) * channels)
        centre = turned[part, 0:1]
        scale = turned[part, 1:2] * cols[0:channels, 4:5]
        shift = cols[0:channels, 5:6]

        def one(row, _, micro=micro, centre=centre, scale=scale, shift=shift):
            normed = (second_out[micro, row + 1] - centre) * scale + shift
            act = (normed * sigmoid(normed)).astype(BF16)
            acts[micro, row] = act
            upper[micro, row] = dot(w_up[...], act)
            return 0

        lax.fori_loop(0, rows, one, 0)
    own_stats(upper, 0, rows, send)


def top_kernel(found, cols, upper, cot, features, grads, stats, send, *, rows):
    micros, _, wide, width = upper.shape
    lines = []
    for micro in range(micros):
        lines += list(pooled_stats(found[:, micro, :], found[:, micros + micro, :], float(rows * width)))
    turned = columns_of(lines)
    stats[...] = turned
    gain, shift = cols[:, 6:7], cols[:, 7:8]
    gain_rows, shift_rows = [], []
    for micro in range(micros):
        centre, rstd = turned[:, 2 * micro : 2 * micro + 1], turned[:, 2 * micro + 1 : 2 * micro + 2]

        def one(row, carry, micro=micro, centre=centre, rstd=rstd):
            unit = (upper[micro, row] - centre) * rstd
            normed = unit * gain + shift
            gate = sigmoid(normed)
            act = normed * gate
            grad = cot[micro, row].astype(F32) * (gate + act * (1.0 - gate))
            features[micro, row] = act.astype(BF16)
            grads[micro, row] = grad
            return carry[0] + fold(grad * unit), carry[1] + fold(grad)

        zero = jnp.zeros((wide, LANES), F32)
        gain_sum, shift_sum = lax.fori_loop(0, rows, one, (zero, zero))
        gain_rows.append(row_of(gain_sum))
        shift_rows.append(row_of(shift_sum))
    send_all(send, gain_rows + shift_rows)


def second_back_kernel(
    found, cols, grads, upper, top_stats, second_out, second_stats, w_up_t, second_act,
    out, weight_grad, down_edge, up_edge, gain_grad, shift_grad, send, *, rows
):
    scene = lax.axis_index("scene")
    micros, _, wide, width = grads.shape
    channels = second_out.shape[2]
    sums = sum_rows(found, 2 * micros)
    own_half(sum(sums[:micros]), scene, gain_grad)
    own_half(sum(sums[micros:]), scene, shift_grad)
    turned = columns_of(sums) * (1.0 / (found.shape[0] * rows * width))
    gain, shift = cols[0:channels, 4:5], cols[0:channels, 5:6]
    gain_sums, shift_sums = [], []
    weight_grad[...] = jnp.zeros(weight_grad.shape, F32)
    for micro in range(micros):
        part = slice(micro * channels, (micro + 1) * channels)
        centre, rstd = second_stats[part, 0:1], second_stats[part, 1:2]
        top_centre = top_stats[:, 2 * micro : 2 * micro + 1]
        top_rstd = top_stats[:, 2 * micro + 1 : 2 * micro + 2]
        factor = cols[:, 6:7] * top_rstd
        slope_part = top_rstd * turned[:, micro : micro + 1]
        shift_part = turned[:, micros + micro : micros + micro + 1]

        def one(row, carry, micro=micro, centre=centre, rstd=rstd, top_centre=top_centre, factor=factor,
                slope_part=slope_part, shift_part=shift_part):
            low = factor * (grads[micro, row] - shift_part - (upper[micro, row] - top_centre) * slope_part)
            low = low.astype(BF16)
            weight_grad[...] = weight_grad[...] + dot_lanes(low, second_act[micro, row])
            unit = (second_out[micro, row + 1] - centre) * rstd
            normed = unit * gain + shift
            gate = sigmoid(normed)
            grad = dot(w_up_t[...], low) * (gate + normed * gate * (1.0 - gate))
            out[micro, row] = grad
            return carry[0] + fold(grad * unit), carry[1] + fold(grad)

        zero = jnp.zeros((channels, LANES), F32)
        gain_sum, shift_sum = lax.fori_loop(0, rows, one, (zero, zero))
        down_edge[micro] = out[micro, 0].astype(BF16)
        up_edge[micro] = out[micro, rows - 1].astype(BF16)
        gain_sums.append(gain_sum)
        shift_sums.append(shift_sum)
    send_all(send, [row_of(*gain_sums), row_of(*shift_sums)])


def low_rows(turned, grads, before, after, values, stats, gain, low, rows, tiles):
    micros, _, channels, width = grads.shape
    tile = lax.axis_index("tile")
    masks = edges(channels, width)
    skip = (values.shape[1] - rows) // 2 - 1
    for micro in range(micros):
        part = slice(micro * channels, (micro + 1) * channels)
        centre, rstd = stats[part, 0:1], stats[part, 1:2]
        factor = gain * rstd
        slope_part, shift_part = rstd * turned[part, 0:1], turned[part, 1:2]

        def one(grad, row, micro=micro, centre=centre, factor=factor, slope_part=slope_part,
                shift_part=shift_part):
            return factor * (grad - shift_part - (values[micro, row + skip] - centre) * slope_part)

        def own(row, _, micro=micro, one=one):
            low[micro, row + 1] = spread(one(grads[micro, row], row + 1).astype(BF16), masks)
            return 0

        lax.fori_loop(0, rows, own, 0, unroll=2)
        for ref, row in ((before, 0), (after, rows + 1)):
            edge = one(ref[micro].astype(F32), row) * inside(tile, row - 1, (tiles, rows))
            low[micro, row] = spread(edge.astype(BF16), masks)


def first_back_kernel(
    found, cols, grads, before, after, second_out, second_stats, first_out, first_stats, b_second_in, acts,
    out, weight_grad, down_edge, up_edge, gain_grad, shift_grad, send, low, b_second, sems, *, rows, tiles
):
    weight_copy = move(b_second_in, b_second, sems, 0)
    scene = lax.axis_index("scene")
    micros, _, channels, width = grads.shape
    sums = sum_rows(found, 2)
    own_half(sums[0][:, :channels] + sums[0][:, channels:], scene, gain_grad)
    own_half(sums[1][:, :channels] + sums[1][:, channels:], scene, shift_grad)
    turned = columns_of(sums) * (1.0 / (found.shape[0] * rows * width))
    low_rows(turned, grads, before, after, second_out, second_stats, cols[0:channels, 4:5], low, rows, tiles)
    gain, shift = cols[0:channels, 2:3], cols[0:channels, 3:4]
    conv_grad(low, acts, weight_grad, rows)
    weight_copy.wait()
    gain_sums, shift_sums = [], []
    for micro in range(micros):
        part = slice(micro * channels, (micro + 1) * channels)
        centre, rstd = first_stats[part, 0:1], first_stats[part, 1:2]

        def step(index, carry, micro=micro, centre=centre, rstd=rstd):
            at = 2 * index
            parts = conv_pair(low, b_second, micro, at, channels)
            gain_sum, shift_sum = carry
            for j in range(2):
                grad_act = parts[channels * j : channels * (j + 1)]
                unit = (first_out[micro, at + j + 2] - centre) * rstd
                normed = unit * gain + shift
                gate = sigmoid(normed)
                grad = grad_act * (gate + normed * gate * (1.0 - gate))
                out[micro, at + j] = grad
                gain_sum = gain_sum + fold(grad * unit)
                shift_sum = shift_sum + fold(grad)
            return gain_sum, shift_sum

        zero = jnp.zeros((channels, LANES), F32)
        gain_sum, shift_sum = lax.fori_loop(0, rows // 2, step, (zero, zero), unroll=2)
        down_edge[micro] = out[micro, 0].astype(BF16)
        up_edge[micro] = out[micro, rows - 1].astype(BF16)
        gain_sums.append(gain_sum)
        shift_sums.append(shift_sum)
    send_all(send, [row_of(*gain_sums), row_of(*shift_sums)])


def conv_grad(low, values, total, rows):
    micros, high, channels, width = values.shape
    skip = (high - rows) // 2 - 1
    for micro in range(micros):
        grads = jnp.concatenate([low[micro, row + 1] for row in range(rows)], axis=1)
        windows = jnp.concatenate(
            [values[micro, row + skip : row + skip + 3].reshape(3 * channels, width) for row in range(rows)],
            axis=1,
        )
        product = dot_lanes(grads, windows)
        total[...] = product if micro == 0 else total[...] + product


def half_rows(total, half, scene):
    channels = 2 * half
    start = scene * half
    mine = jnp.concatenate(
        [total[b * channels + start : b * channels + start + half, :] for b in range(2, -1, -1)], axis=0
    )
    wing = mine[:, LANES:]
    cut = wing.shape[0] // 2
    return [mine[:, :LANES], jnp.concatenate([wing[:cut], wing[cut:]], axis=1)]


def pick_kernel(
    found, cols, grads, before, after, first_out, first_stats, b_first_in, columns, where_rows,
    canvas, second_grad, top_grad,
    send, gain_grad, shift_grad, low, grid, b_first, first_grad, whole, sems, *, rows, tiles, each
):
    weight_copy = move(b_first_in, b_first, sems, 0)
    scene = lax.axis_index("scene")
    micros, _, channels, width = grads.shape
    sums = sum_rows(found, 2)
    own_half(sums[0][:, :channels] + sums[0][:, channels:], scene, gain_grad)
    own_half(sums[1][:, :channels] + sums[1][:, channels:], scene, shift_grad)
    turned = columns_of(sums) * (1.0 / (found.shape[0] * rows * width))
    low_rows(turned, grads, before, after, first_out, first_stats, cols[0:channels, 2:3], low, rows, tiles)
    weight_copy.wait()
    conv_rows(low, b_first, grid, grid.shape)
    conv_grad(low, canvas, first_grad, rows)
    half = channels // 2
    peers, block = send.shape[:2]
    for s in range(2):
        parts = half_rows(first_grad, half, s) + half_rows(second_grad, half, s)
        mine = top_grad[s * channels : (s + 1) * channels, :]
        parts.append(jnp.concatenate([mine[:half], mine[half:]], axis=1))
        parts = jnp.concatenate(parts, axis=0)
        whole[s, 0 : parts.shape[0]] = parts
        if whole.shape[1] > parts.shape[0]:
            whole[s, parts.shape[0] :] = jnp.zeros((whole.shape[1] - parts.shape[0], LANES), F32)
    slots = columns.shape[0]
    lane = lax.broadcasted_iota(jnp.int32, (slots, width), 1).astype(F32)
    picked = []
    for micro in range(micros):
        at = 2 + micro
        column = columns[:, at : at + 1] - 1.0
        column = column - jnp.floor(column * (1.0 / width)) * width
        place = jnp.floor((where_rows[at : at + 1] - 1.0) * (1.0 / width))
        chosen = jnp.where(lane == column, 1.0, 0.0).astype(BF16)
        here = dot_lanes(grid[micro].reshape(rows * channels, width), chosen)
        total = jnp.zeros((channels, slots), F32)
        for r in range(rows):
            total = total + jnp.where(place == r * 1.0, here[r * channels : (r + 1) * channels], 0.0)
        picked.append(total)
    picked = jnp.transpose(jnp.concatenate(picked, axis=0))
    capacity = slots // tiles
    rest = block - capacity - 2 * each
    for peer in range(peers):
        spot = peer // 2
        parts = [picked[spot * capacity : (spot + 1) * capacity]]
        parts += [whole[s, peer * each : (peer + 1) * each] for s in range(2)]
        parts.append(jnp.zeros((rest, LANES), F32))
        send[peer] = jnp.concatenate(parts, axis=0).astype(BF16)


def pillar_back_kernel(found, rows_in, w_pillar, cols, pooled, send, grads, lifted, rows, sems,
                       *, capacity, each):
    fetched = move(rows_in, rows, sems, 0)
    micros = rows.shape[0]
    _, channels, pillars = pooled.shape
    stats, slots = pooled.at[micros : 2 * micros], pooled.at[2 * micros]
    inputs = w_pillar.shape[1]
    depth = rows.shape[2] // pillars
    scene = lax.axis_index("scene")
    peers = found.shape[0]
    slot_count = peers // 2 * capacity
    returned = jnp.concatenate(
        [found[2 * t + scene].astype(F32)[0:capacity] for t in range(peers // 2)], axis=0
    )
    turned = jnp.transpose(returned)
    place = lax.broadcasted_iota(jnp.int32, (slot_count, pillars), 0).astype(F32)
    gain, shift = cols[0:channels, 0:1], cols[0:channels, 1:2]
    gain_sums, shift_sums = [], []
    outer = jnp.zeros((16, channels), F32)
    fetched.wait()
    for micro in range(micros):
        lifted[...] = dot(w_pillar[...], rows[micro, 0:inputs])
        chosen = jnp.where(place == slots[micro : micro + 1], 1.0, 0.0).astype(BF16)
        back = dot(turned[micro * channels : (micro + 1) * channels].astype(BF16), chosen)
        limit = slots[micros + micro : micros + micro + 1]
        centre, rstd = stats[micro, :, 0:1], stats[micro, :, 1:2]
        pool = pooled[micro]
        gain_sum = jnp.zeros((channels, pillars), F32)
        shift_sum = jnp.zeros((channels, pillars), F32)
        for n in range(depth):
            piece = slice(n * pillars, (n + 1) * pillars)
            unit = (lifted[:, piece] - centre) * rstd
            normed = unit * gain + shift
            gate = sigmoid(normed)
            act = normed * gate
            slope = gate + act * (1.0 - gate)
            grad = jnp.where(limit > n, back * jnp.exp(act - pool) * slope, 0.0)
            grads[micro, :, piece] = grad
            gain_sum = gain_sum + grad * unit
            shift_sum = shift_sum + grad
        gain_sums.append(gain_sum)
        shift_sums.append(shift_sum)
        scale = jnp.transpose(jnp.broadcast_to(rstd * gain, (channels, LANES)))[0:1]
        outer = outer + dot_lanes(rows[micro], grads[micro].astype(BF16)) * scale
    lines = [row_of(*gain_sums), row_of(*shift_sums)]
    for k in range(0, 12, 2):
        lines.append(jnp.concatenate([outer[k : k + 1], outer[k + 1 : k + 2]], axis=1))
    exact = jnp.concatenate(lines, axis=0)
    high = exact.astype(BF16).astype(F32)
    weights = jnp.sum(found[...].astype(F32), axis=0)
    rest = send.shape[2] - 16 - each
    for s in range(2):
        mine = weights[capacity + s * each : capacity + (s + 1) * each]
        block = jnp.concatenate([high, exact - high, mine, jnp.zeros((rest, LANES), F32)], axis=0).astype(BF16)
        send[:, s] = jnp.broadcast_to(block[None], (send.shape[0],) + block.shape)


def points_kernel(
    found, rows_in, grads, w_pillar, cols, pooled,
    points_grad, pillar_grad, gain_grad, shift_grad, first_grad, second_grad, up_grad, rows, lifted, sems,
    *, each
):
    fetched = move(rows_in, rows, sems, 0)
    scene = lax.axis_index("scene")
    micros, channels, _ = grads.shape
    stats, slots = pooled.at[micros : 2 * micros], pooled.at[2 * micros]
    _, _, inputs, depth, pillars = points_grad.shape
    half = channels // 2
    total = jnp.sum(found[:, 0:16, :].astype(F32), axis=0)
    total = total[0:8] + total[8:16]
    own_half(total[0:1, :channels] + total[0:1, channels:], scene, gain_grad)
    own_half(total[1:2, :channels] + total[1:2, channels:], scene, shift_grad)
    turned = jnp.transpose(total)
    weight_grad = jnp.concatenate(
        [turned[(k % 2) * channels : (k % 2 + 1) * channels, 2 + k // 2 : 3 + k // 2] for k in range(inputs)],
        axis=1,
    )
    weight = jnp.transpose(w_pillar[...].astype(F32)).astype(BF16)
    fetched.wait()
    for micro in range(micros):
        lifted[...] = dot(w_pillar[...], rows[micro, 0:inputs])
        part = slice(micro * channels, (micro + 1) * channels)
        centre, rstd, inverse = stats[micro, :, 0:1], stats[micro, :, 1:2], stats[micro, :, 2:3]
        factor = cols[0:channels, 0:1] * rstd
        gain_part, shift_part = turned[part, 0:1], turned[part, 1:2]
        spun, mean = stats[micro, :, 16 : 16 + inputs], stats[micro, :, 32 : 32 + inputs]
        weight_grad = weight_grad - factor * (shift_part * mean + gain_part * rstd * spun)
        gain_part, shift_part = gain_part * inverse * rstd, shift_part * inverse
        limit = slots[micros + micro : micros + micro + 1]
        for n in range(depth):
            piece = slice(n * pillars, (n + 1) * pillars)
            low = factor * (grads[micro, :, piece] - shift_part - (lifted[:, piece] - centre) * gain_part)
            low = jnp.where(limit > n, low, 0.0).astype(BF16)
            points_grad[micro, 0, :, n, :] = dot(weight, low)
    weight_grad = jnp.concatenate([weight_grad, jnp.zeros((channels, LANES - inputs), F32)], axis=1)
    weight_grad = jnp.transpose(weight_grad)[0:inputs]
    pillar_grad[...] = jnp.where(scene == 0, weight_grad[:, :half], weight_grad[:, half:])
    whole = jnp.concatenate(
        [found[peer].astype(F32)[16 : 16 + each] for peer in range(found.shape[0])], axis=0
    )
    for index, out in enumerate((first_grad, second_grad)):
        base = index * 9 * half * channels // LANES
        lead = 3 * half
        mine = whole[base : base + lead]
        wing = whole[base + lead : base + lead + lead // 2]
        wing = jnp.concatenate([wing[:, :channels], wing[:, channels:]], axis=0)
        both = jnp.concatenate([mine, wing], axis=1)
        for a in range(3):
            for b in range(3):
                at = (3 * a + b) * channels
                out[:, at : at + channels] = both[b * half : (b + 1) * half, a * channels : (a + 1) * channels]
    base = 2 * 9 * half * channels // LANES
    top = whole[base : base + half]
    up_grad[...] = jnp.concatenate([top[:, :channels], top[:, channels:]], axis=0)


def swap(blocks, axes):
    return lax.all_to_all(blocks, axes, split_axis=0, concat_axis=0)


def shards(
    points, point_counts, pillar_tile, pillar_cell,
    pillar_weight, pillar_gain, pillar_shift,
    first_weight, first_gain, first_shift,
    second_weight, second_gain, second_shift,
    up_weight, up_gain, up_shift, cotangent,
):
    micros, _, inputs, depth, pillars = points.shape
    channels = up_weight.shape[1]
    upper = cotangent.shape[2]
    rows, width = cotangent.shape[3:]
    tiles = lax.axis_size("tile")
    scenes = lax.axis_size("scene")
    peers = tiles * scenes
    capacity = 2 * pillars // tiles
    slot_count = tiles * capacity
    half = channels // 2

    def vmem(shape, dtype):
        return pltpu.VMEM(shape, dtype)

    def grid(high, dtype=F32, lead=channels):
        return ((micros, high, lead, width), dtype)

    sums = ((peers, 2, LANES), F32)
    sources = (
        pillar_tile, pillar_cell, point_counts, points,
        first_weight, second_weight, up_weight, pillar_weight.T,
        pillar_gain, pillar_shift, first_gain, first_shift, second_gain, second_shift, up_gain, up_shift,
    )
    moments, packed, point_rows, slots = run(
        functools.partial(moments_kernel, capacity=capacity),
        [
            ((tiles, scenes, 4, LANES), F32), ((layout(half, channels)[-1] + 16, LANES), BF16),
            ((micros, 16, depth * pillars), BF16), ((8, pillars), F32),
        ],
        *sources,
        hbm=range(len(sources)), copies=len(sources), limit=WIDE_LIMIT,
        scratch=[vmem(source.shape, source.dtype) for source in sources]
        + [vmem((inputs * depth, pillars), F32)],
    )
    moments = swap(moments.reshape(peers, 4, LANES), BOTH)
    both = lax.all_gather(packed, "scene")
    taps = ((2 * channels, 12 * channels), BF16)
    w_pillar, cols, l_first, l_second, b_first, b_second, w_up, w_up_t = run(
        functools.partial(unpack_kernel, inputs=inputs),
        [
            ((channels, inputs), BF16), ((LANES, 8), F32), taps, taps + (1,), taps + (1,), taps + (1,),
            ((upper, channels), BF16), ((channels, upper), BF16),
        ],
        both,
        scratch=[vmem(*taps), vmem(*taps), vmem(*taps)], copies=3,
    )
    cot = cotangent[:, 0].transpose(0, 2, 1, 3)

    send, pooled = run(
        functools.partial(pillar_kernel, capacity=capacity),
        [((slot_count, 3 * LANES), BF16), ((2 * micros + 1, channels, pillars), F32)],
        moments, point_rows, slots, w_pillar, cols,
        scratch=[vmem((channels, depth * pillars), F32), vmem((channels, depth * pillars), F32)],
    )
    arrived = swap(send.reshape(tiles, capacity, 3 * LANES), "tile").reshape(slot_count, 3 * LANES)
    cell_columns, cell_rows = run(
        functools.partial(cells_kernel, capacity=capacity),
        [((slot_count, LANES), F32), ((8, slot_count), F32)],
        moments,
        cost=pl.CostEstimate(flops=10**7, bytes_accessed=10**6, transcendentals=0),
    )
    arrived, cot = lax.optimization_barrier((arrived, cot))

    first_out, canvas, send = run(
        functools.partial(canvas_kernel, rows=rows),
        [grid(rows + 4), grid(rows + 2, BF16), sums],
        arrived, cell_columns, cell_rows, l_first,
        scratch=[vmem(*grid(rows + 6, BF16, 3 * channels))],
    )
    second_out, first_act, first_stats, send = run(
        functools.partial(second_kernel, rows=rows, tiles=tiles),
        [grid(rows + 2), grid(rows + 4, BF16), ((LANES, 8), F32), sums],
        swap(send, BOTH), cols, first_out, l_second,
        hbm=(3,), scratch=[vmem(*grid(rows + 4, BF16, 3 * channels)), vmem(*taps)], copies=1,
    )
    second_act, up_out, second_stats, send = run(
        functools.partial(up_kernel, rows=rows),
        [grid(rows, BF16), grid(rows, F32, upper), ((LANES, 8), F32), ((peers, 4, LANES), F32)],
        swap(send, BOTH), cols, second_out, w_up,
    )
    features, grads, top_stats, send = run(
        functools.partial(top_kernel, rows=rows),
        [grid(rows, BF16, upper), grid(rows, F32, upper), ((LANES, 8), F32), ((peers, 4, LANES), F32)],
        swap(send, BOTH), cols, up_out, cot,
    )
    edge = ((micros, channels, width), BF16)
    vector, top_vector, matrix = ((half,), F32), ((upper // 2,), F32), ((half, 9 * channels), F32)
    second_dz, top_grad, down_edge, up_edge, up_gain_grad, up_shift_grad, send = run(
        functools.partial(second_back_kernel, rows=rows),
        [grid(rows), ((upper, channels), F32), edge, edge, top_vector, top_vector, sums],
        swap(send, BOTH), cols, grads, up_out, top_stats, second_out, second_stats, w_up_t, second_act,
    )
    rising = [(i, i + 1) for i in range(tiles - 1)]
    falling = [(j, i) for i, j in rising]
    cross = ((3 * channels, 3 * channels), F32)
    first_dz, second_cross, down_next, up_next, second_gain_grad, second_shift_grad, send = run(
        functools.partial(first_back_kernel, rows=rows, tiles=tiles),
        [grid(rows), cross, edge, edge, vector, vector, sums],
        swap(send, BOTH), cols, second_dz,
        lax.ppermute(up_edge, "tile", rising), lax.ppermute(down_edge, "tile", falling),
        second_out, second_stats, first_out, first_stats, b_second, first_act,
        hbm=(9,), scratch=[vmem(*grid(rows + 2, BF16, 3 * channels)), vmem(*taps)], copies=1,
    )
    length = (2 * 9 * half * channels + upper * half) // LANES
    each = -(-length // peers)
    block = -(-(capacity + 2 * each) // 8) * 8
    send, first_gain_grad, first_shift_grad = run(
        functools.partial(pick_kernel, rows=rows, tiles=tiles, each=each),
        [((peers, block, LANES), BF16), vector, vector],
        swap(send, BOTH), cols, first_dz,
        lax.ppermute(up_next, "tile", rising), lax.ppermute(down_next, "tile", falling),
        first_out, first_stats, b_first, cell_columns, cell_rows, canvas, second_cross, top_grad,
        hbm=(7,),
        scratch=[
            vmem(*grid(rows + 2, BF16, 3 * channels)), vmem(*grid(rows, BF16)), vmem(*taps), vmem(*cross),
            vmem((scenes, peers * each, LANES), F32),
        ],
        copies=1,
    )
    block = 16 + -(-each // 16) * 16
    send, pillar_dz = run(
        functools.partial(pillar_back_kernel, capacity=capacity, each=each),
        [((tiles, scenes, block, LANES), BF16), ((micros, channels, depth * pillars), F32)],
        swap(send, BOTH), point_rows, w_pillar, cols, pooled,
        hbm=(1,),
        scratch=[vmem((channels, depth * pillars), F32), vmem((micros, 16, depth * pillars), BF16)],
        copies=1,
    )
    send, features = lax.optimization_barrier((send, features))
    features = features.transpose(0, 2, 1, 3)[:, None]
    points_grad, pillar_grad, pillar_gain_grad, pillar_shift_grad, first_grad, second_grad, up_grad = run(
        functools.partial(points_kernel, each=each),
        [
            ((micros, 1, inputs, depth, pillars), F32), ((inputs, half), F32), vector, vector,
            matrix, matrix, ((upper // 2, channels), F32),
        ],
        swap(send.reshape(peers, block, LANES), BOTH), point_rows, pillar_dz, w_pillar, cols, pooled,
        hbm=(1,),
        scratch=[vmem((micros, 16, depth * pillars), BF16), vmem((channels, depth * pillars), F32)],
        copies=1,
    )
    return (
        features, points_grad,
        pillar_grad.T, pillar_gain_grad, pillar_shift_grad,
        first_grad, first_gain_grad, first_shift_grad,
        second_grad, second_gain_grad, second_shift_grad,
        up_grad, up_gain_grad, up_shift_grad,
    )


def solution(mesh):
    matrix, vector = P("scene", None), P("scene")
    grid = P(None, "scene", None, "tile", None)
    cloud = P(None, "scene", None, None, "tile")
    pillar = P(None, "scene", "tile")
    weights = (matrix, vector, vector) * 4
    return jax.shard_map(
        shards,
        mesh=mesh,
        in_specs=(cloud, pillar, pillar, pillar) + weights + (grid,),
        out_specs=(grid, cloud) + weights,
        check_vma=False,
    )
```

```python
import functools

import jax
import jax.numpy as jnp
from jax import lax
from jax.experimental import pallas as pl
from jax.experimental.pallas import tpu as pltpu
from jax.sharding import PartitionSpec as P

norm_eps = 0.001
BOTH = ("tile", "scene")
F32 = jnp.float32
BF16 = jnp.bfloat16
VMEM_LIMIT = 24 * 1024 * 1024
WIDE_LIMIT = 60 * 1024 * 1024
LANES = 128


def run(kernel, outs, *args, hbm=(), scratch=(), copies=0, cost=None, limit=VMEM_LIMIT):
    specs = [
        pl.BlockSpec(memory_space=pltpu.HBM if index in hbm else pltpu.VMEM) for index in range(len(args))
    ]
    scratch = list(scratch)
    if copies:
        scratch.append(pltpu.SemaphoreType.DMA((copies,)))
    return pl.pallas_call(
        kernel,
        out_shape=[jax.ShapeDtypeStruct(out[0], out[1]) for out in outs],
        in_specs=specs,
        out_specs=[
            pl.BlockSpec(memory_space=pltpu.HBM if len(out) > 2 else pltpu.VMEM) for out in outs
        ],
        scratch_shapes=scratch,
        compiler_params=pltpu.CompilerParams(vmem_limit_bytes=limit),
        cost_estimate=cost,
    )(*args)


def move(source, target, sems, index):
    copy = pltpu.make_async_copy(source, target, sems.at[index])
    copy.start()
    return copy


def dot(left, right, precision=None):
    return jnp.dot(left, right, preferred_element_type=F32, precision=precision)


def dot_lanes(left, right, precision=None):
    return lax.dot_general(
        left, right, (((1,), (1,)), ((), ())), preferred_element_type=F32, precision=precision
    )


def sigmoid(values):
    return 0.5 + 0.5 * jnp.tanh(0.5 * values)


def fold(values):
    total = values[:, :LANES]
    for start in range(LANES, values.shape[1], LANES):
        total = total + values[:, start : start + LANES]
    return total


def row_of(left, right=None):
    both = left if right is None else jnp.concatenate([left, right], axis=0)
    return jnp.sum(jnp.transpose(both), axis=0, keepdims=True)


def columns_of(rows):
    rows = rows + [jnp.zeros((8 - len(rows), LANES), F32)] if len(rows) < 8 else rows
    return jnp.transpose(jnp.concatenate(rows, axis=0))


def inside(tile, row, height):
    tiles, rows = height
    place = tile * rows + row
    return jnp.where((place >= 0) & (place < tiles * rows), 1.0, 0.0).astype(F32)


def send_all(ref, rows):
    for index, row in enumerate(rows):
        ref[:, index : index + 1, :] = jnp.broadcast_to(row[None], (ref.shape[0], 1, LANES))


def pooled_stats(means, squares, count):
    peers = means.shape[0]
    mean = jnp.sum(means, axis=0, keepdims=True) * (1.0 / peers)
    away = means - mean
    spread = jnp.sum(squares + count * away * away, axis=0, keepdims=True) * (1.0 / (peers * count))
    return mean, lax.rsqrt(spread + norm_eps)


def stat_columns(found, count):
    return columns_of(list(pooled_stats(found[:, 0, :], found[:, 1, :], count)))


def sum_rows(found, lines):
    return [jnp.sum(found[:, index, :], axis=0, keepdims=True) for index in range(lines)]


def own_half(row, scene, out):
    size = out.shape[0]
    out[...] = jnp.where(scene == 0, row[:, 0:size], row[:, size : 2 * size]).reshape(size)


def edges(channels, width):
    lane = lax.broadcasted_iota(jnp.int32, (channels, width), 1)
    return lane > 0, lane < width - 1


def spread(row, masks):
    zero = jnp.zeros_like(row)
    left = jnp.where(masks[0], pltpu.roll(row, 1, 1), zero)
    right = jnp.where(masks[1], pltpu.roll(row, row.shape[1] - 1, 1), zero)
    return jnp.concatenate([left, row, right], axis=0)


def layout(half, channels):
    first = 0
    second = first + half * -(-9 * channels // LANES)
    up = second + half * -(-9 * channels // LANES)
    vectors = up + channels
    return first, second, up, vectors, vectors + 16


def widen(value):
    missing = LANES - value.shape[1]
    if missing == 0:
        return value
    return jnp.concatenate([value, jnp.zeros((value.shape[0], missing), value.dtype)], axis=1)


def pack(held, out):
    first, second, up, pillar = held[:4]
    half, channels = first.shape[0], up.shape[1]
    starts = layout(half, channels)
    for ref, start in ((first, starts[0]), (second, starts[1])):
        for j in range(-(-9 * channels // LANES)):
            out[start + j * half : start + (j + 1) * half, :] = widen(
                ref[:, j * LANES : min((j + 1) * LANES, 9 * channels)]
            )
    out[starts[2] : starts[2] + channels, :] = widen(up[...])
    rows = [vector[...].astype(F32).reshape(1, -1) for vector in held[4:]]
    rows = [widen(row) for row in rows] + [jnp.zeros((16 - len(rows), LANES), F32)]
    turned = widen(pillar[...].astype(F32))
    rows += [turned, jnp.zeros((16 - turned.shape[0], LANES), F32)]
    out[starts[3] :, :] = jnp.concatenate(rows, axis=0).astype(BF16)


def unpack_kernel(
    both, w_pillar, cols, l_first, l_second, b_first, b_second, w_up, w_up_t,
    h_second, h_first_back, h_second_back, sems, *, inputs
):
    half = w_pillar.shape[0] // 2
    channels = 2 * half
    starts = layout(half, channels)
    tiles = -(-9 * channels // LANES)

    def wide(start):
        return jnp.concatenate(
            [
                jnp.concatenate(
                    [both[s, start + j * half : start + (j + 1) * half, :] for j in range(tiles)], axis=1
                )
                for s in range(2)
            ],
            axis=0,
        ).astype(F32)

    up = jnp.concatenate(
        [both[s, starts[2] : starts[2] + channels, 0:channels] for s in range(2)], axis=0
    )
    w_up[...] = up
    w_up_t[...] = jnp.transpose(up.astype(F32)).astype(BF16)
    turned = jnp.concatenate(
        [both[s, starts[4] : starts[4] + 16, 0:half].astype(F32) for s in range(2)], axis=1
    )
    w_pillar[...] = jnp.transpose(widen(turned))[0:channels, 0:inputs].astype(BF16)
    vectors = [both[s, starts[3] : starts[3] + 16, :].astype(F32) for s in range(2)]
    rows = []
    for index in range(8):
        size = half if index < 6 else channels
        row = jnp.concatenate([vectors[s][index : index + 1, 0:size] for s in range(2)], axis=1)
        rows.append(jnp.concatenate([row] * (LANES // (2 * size)), axis=1))
    cols[...] = columns_of(rows)
    zero = jnp.zeros((channels, 3 * channels), F32)
    copies = []
    for weight, ahead, back in (
        (wide(starts[0]), l_first, h_first_back), (wide(starts[1]), h_second, h_second_back)
    ):
        weight = weight[:, : 9 * channels]
        turned = jnp.transpose(weight)
        flipped = jnp.concatenate(
            [turned[tap * channels : (tap + 1) * channels] for tap in range(8, -1, -1)], axis=1
        )
        for ref, taps in ((ahead, weight), (back, flipped)):
            ref[0:channels, :] = jnp.concatenate([taps, zero], axis=1).astype(BF16)
            ref[channels : 2 * channels, :] = jnp.concatenate([zero, taps], axis=1).astype(BF16)
    copies.append(move(h_second, l_second, sems, 0))
    copies.append(move(h_first_back, b_first, sems, 1))
    copies.append(move(h_second_back, b_second, sems, 2))
    for copy in copies:
        copy.wait()


def slot_line(wide, depth, inputs):
    return jnp.concatenate([wide[pl.ds(n, inputs, stride=depth), :] for n in range(depth)], axis=1)


def slot_mask(count, depth):
    return jnp.concatenate([jnp.where(count > n, 1.0, 0.0) for n in range(depth)], axis=1)


def ranks(tile):
    pillars = tile.shape[1]
    across = jnp.broadcast_to(tile, (pillars, pillars))
    down = jnp.transpose(across)
    row = lax.broadcasted_iota(jnp.int32, (pillars, pillars), 0)
    col = lax.broadcasted_iota(jnp.int32, (pillars, pillars), 1)
    return jnp.sum(jnp.where((across == down) & (row < col), 1.0, 0.0), axis=0, keepdims=True)


def moments_kernel(*refs, capacity):
    number = 16
    sources, out, packed, lines_out, slots = refs[:number], *refs[number : number + 4]
    held, wide, sems = refs[number + 4 : 2 * number + 4], refs[-2], refs[-1]
    copies = [move(sources[i], held[i], sems, i) for i in range(number)]
    tiles, cells, counts, points = held[:4]
    micros, _, inputs, depth, pillars = points.shape
    peers, scenes = out.shape[:2]
    copies[0].wait()
    copies[1].wait()
    lines, slot_rows = [], []
    for micro in range(micros):
        tile = tiles[micro].astype(F32)
        cell = (cells[micro] + 1).astype(F32)
        high = jnp.floor(cell * (1.0 / 16.0))
        low = cell - high * 16.0
        rank = ranks(tile)
        slot_rows.append(tile * capacity + rank)
        spot = lax.broadcasted_iota(jnp.int32, (capacity, pillars), 0).astype(F32)
        placed = jnp.where(spot == rank, 1.0, 0.0).astype(BF16)
        peer = lax.broadcasted_iota(jnp.int32, (peers, pillars), 0).astype(F32)
        for group in range(3):
            named = tile == peer + (group - 1.0)
            lines.append(
                16.0 * dot_lanes(jnp.where(named, high, 0.0).astype(BF16), placed)
                + dot_lanes(jnp.where(named, low, 0.0).astype(BF16), placed)
            )
    used = 3 * micros * capacity
    line = jnp.concatenate(lines + [jnp.zeros((peers, LANES - used), F32)], axis=1).reshape(peers, 1, LANES)
    for scene in range(scenes):
        out[:, scene, micros : micros + 1, :] = line
    copies[2].wait()
    copies[3].wait()
    limits = [counts[micro].astype(F32) for micro in range(micros)]
    slots[...] = jnp.concatenate(
        slot_rows + limits + [jnp.zeros((8 - 2 * micros, pillars), F32)], axis=0
    )
    for micro in range(micros):
        wide[...] = points[micro, 0].astype(F32).reshape(inputs * depth, pillars)
        rows = slot_line(wide, depth, inputs)
        lines_out[micro] = jnp.concatenate(
            [rows, jnp.zeros((16 - inputs, rows.shape[1]), F32)], axis=0
        ).astype(BF16)
        mask = slot_mask(counts[micro], depth)
        total = jnp.sum(mask, axis=1, keepdims=True)
        mean = jnp.sum(rows * mask, axis=1, keepdims=True) / total
        centred = (rows - mean) * mask
        products = dot_lanes(centred, centred, lax.Precision.HIGHEST)
        lane = lax.broadcasted_iota(jnp.int32, (inputs, inputs), 1)
        diagonal = lax.broadcasted_iota(jnp.int32, (inputs, inputs), 0) == lane
        mean_row = jnp.sum(jnp.where(diagonal, mean, 0.0), axis=0, keepdims=True)
        row = jnp.concatenate(
            [products[k : k + 1] for k in range(inputs)]
            + [mean_row, total, jnp.zeros((1, LANES - inputs * inputs - inputs - 1), F32)],
            axis=1,
        )
        for scene in range(scenes):
            out[:, scene, micro : micro + 1, :] = jnp.broadcast_to(row[None], (peers, 1, LANES))
    for copy in copies[4:]:
        copy.wait()
    pack(held[4:], packed)


def cells_kernel(found, columns, rows, *, capacity):
    scene = lax.axis_index("scene")
    slots = columns.shape[0]
    peers = found.shape[0]
    values = found[:, 2, :]
    slot = lax.broadcasted_iota(jnp.int32, (slots, peers), 0)
    peer = lax.broadcasted_iota(jnp.int32, (slots, peers), 1)
    lane = lax.broadcasted_iota(jnp.int32, (slots, LANES), 1)
    row = lax.broadcasted_iota(jnp.int32, (slots, LANES), 0)
    result = jnp.zeros((slots, LANES), F32)
    chosen = jnp.where(peer == 2 * (slot // capacity) + scene, 1.0, 0.0)
    spread = dot(chosen, values, lax.Precision.HIGHEST)
    for micro in range(2):
        for group in range(3):
            mine = jnp.where(lane == (3 * micro + group) * capacity + row % capacity, spread, 0.0)
            column = jnp.sum(mine, axis=1, keepdims=True)
            result = jnp.where(lane == 2 * group + micro, column, result)
    columns[...] = result
    rows[...] = jnp.transpose(result)[0:8]


def pillar_kernel(
    found, rows_in, slots_in, w_pillar, cols, send, pooled, lifted, acts, point_rows, slots, sems, *, capacity
):
    copies = [move(rows_in, point_rows, sems, 0), move(slots_in, slots, sems, 1)]
    micros = point_rows.shape[0]
    channels, inputs = w_pillar.shape
    pillars = slots.shape[1]
    depth = point_rows.shape[2] // pillars
    weight = w_pillar[...]
    wide_weight = weight.astype(F32)
    rows_out = send.shape[0]
    square = inputs * inputs
    stacked = []
    for copy in copies:
        copy.wait()
    for micro in range(micros):
        lifted[...] = dot(weight, point_rows[micro, 0:inputs])
        moments = found[:, micro, :]
        sizes = moments[:, square + inputs : square + inputs + 1]
        means = moments[:, square : square + inputs]
        count = jnp.sum(sizes, axis=0, keepdims=True)
        mean = jnp.sum(means * sizes, axis=0, keepdims=True) / count
        away = means - mean
        products = lax.dot_general(
            away * sizes, away, (((0,), (0,)), ((), ())),
            preferred_element_type=F32, precision=lax.Precision.HIGHEST,
        )
        summed = jnp.sum(moments, axis=0, keepdims=True)
        products = products + jnp.concatenate(
            [summed[:, k * inputs : (k + 1) * inputs] for k in range(inputs)], axis=0
        )
        cov = products / count
        spun = wide_weight[:, 0:1] * cov[0:1]
        for k in range(1, inputs):
            spun = spun + wide_weight[:, k : k + 1] * cov[k : k + 1]
        spread = jnp.sum(spun * wide_weight, axis=1, keepdims=True)
        centre = jnp.sum(wide_weight * mean, axis=1, keepdims=True)
        rstd = lax.rsqrt(spread + norm_eps)
        inverse = jnp.broadcast_to(1.0 / count, (channels, 1))
        pooled[micros + micro] = jnp.concatenate(
            [
                centre, rstd, inverse, jnp.zeros((channels, 13), F32),
                spun, jnp.zeros((channels, 16 - inputs), F32),
                jnp.broadcast_to(mean, (channels, inputs)), jnp.zeros((channels, LANES - 32 - inputs), F32),
            ],
            axis=1,
        )
        scale = rstd * cols[0:channels, 0:1]
        shift = cols[0:channels, 1:2]
        limit = slots[micros + micro : micros + micro + 1]
        top = jnp.full((channels, pillars), -jnp.inf, F32)
        for n in range(depth):
            piece = slice(n * pillars, (n + 1) * pillars)
            normed = (lifted[:, piece] - centre) * scale + shift
            act = normed * sigmoid(normed)
            acts[:, piece] = act
            top = jnp.maximum(top, jnp.where(limit > n, act, -jnp.inf))
        total = jnp.zeros((channels, pillars), F32)
        for n in range(depth):
            piece = slice(n * pillars, (n + 1) * pillars)
            total = total + jnp.where(limit > n, jnp.exp(acts[:, piece] - top), 0.0)
        result = top + jnp.log(total)
        pooled[micro] = result
        parts = [jnp.zeros((channels, pillars), F32)] * micros
        parts[micro] = result.astype(BF16).astype(F32)
        stacked.append(jnp.transpose(jnp.concatenate(parts, axis=0)))
    pooled[2 * micros, 0:8] = slots[...]
    slot_rows = [slots[micro : micro + 1] for micro in range(micros)]
    values = jnp.concatenate(stacked, axis=0).astype(BF16)
    for group in range(3):
        place = lax.broadcasted_iota(jnp.int32, (rows_out, pillars), 0) + (group - 1) * capacity
        chosen = jnp.concatenate(
            [jnp.where(place.astype(F32) == row, 1.0, 0.0) for row in slot_rows], axis=1
        ).astype(BF16)
        send[:, group * LANES : (group + 1) * LANES] = dot(chosen, values).astype(BF16)


def own_stats(ref, first_row, rows, send):
    micros, _, channels, width = ref.shape
    sums, squares = [], []
    for micro in range(micros):
        total = fold(ref[micro, first_row])
        for row in range(first_row + 1, first_row + rows):
            total = total + fold(ref[micro, row])
        total = total * (1.0 / (rows * width))
        mean = jnp.sum(total, axis=1, keepdims=True)
        spread = jnp.zeros(total.shape, F32)
        for row in range(first_row, first_row + rows):
            away = ref[micro, row] - mean
            spread = spread + fold(away * away)
        sums.append(total)
        squares.append(spread)
    if channels == LANES:
        send_all(send, [row_of(part) for part in sums + squares])
    else:
        send_all(send, [row_of(*sums), row_of(*squares)])


def conv_pair(source, weight, micro, at, channels):
    window = source[micro, pl.ds(at, 4)].reshape(12 * channels, source.shape[3])
    return dot(weight[...], window)


def conv_rows(source, weight, out, shape):
    micros, high, channels, width = shape
    pairs = high // 2

    def step(index, _):
        micro, at = index // pairs, 2 * (index % pairs)
        both = conv_pair(source, weight, micro, at, channels)
        out[micro, at] = both[:channels].astype(out.dtype)
        out[micro, at + 1] = both[channels:].astype(out.dtype)
        return 0

    lax.fori_loop(0, micros * pairs, step, 0, unroll=2)


def canvas_kernel(found, columns, where_rows, l_first, out, kept, send, canvas, *, rows):
    scenes, high, channels, width = out.shape
    masks = edges(channels, width)
    slots = found.shape[0]
    lane = lax.broadcasted_iota(jnp.int32, (slots, width), 1).astype(F32)
    for group in range(3):
        values = jnp.transpose(found[:, group * LANES : (group + 1) * LANES].astype(F32))
        count = (rows, rows, rows // 2)[group]
        for scene in range(scenes):
            at = 2 * group + scene
            column = columns[:, at : at + 1] - 1.0
            column = column - jnp.floor(column * (1.0 / width)) * width
            row = jnp.floor((where_rows[at : at + 1] - 1.0) * (1.0 / width))
            mine = values[scene * channels : (scene + 1) * channels]
            placed = jnp.concatenate(
                [jnp.where(row == r * 1.0, mine, 0.0) for r in range(count)], axis=0
            ).astype(BF16)
            chosen = jnp.where(lane == column, 1.0, 0.0).astype(BF16)
            grid = dot(placed, chosen).astype(BF16)
            start = group * rows
            for r in range(count):
                row = grid[r * channels : (r + 1) * channels]
                canvas[scene, start + r] = spread(row, masks)
                if rows - 1 <= start + r <= 2 * rows:
                    kept[scene, start + r - (rows - 1)] = row
    conv_rows(canvas, l_first, out, out.shape)
    own_stats(out, rows - 1, rows, send)


def second_kernel(found, cols, first_out, l_second_in, out, kept, stats, send, acts, l_second, sems,
                  *, rows, tiles):
    weight_copy = move(l_second_in, l_second, sems, 0)
    micros, high, channels, width = first_out.shape
    tile = lax.axis_index("tile")
    turned = stat_columns(found, float(rows * width))
    stats[...] = turned
    masks = edges(channels, width)
    for micro in range(micros):
        part = slice(micro * channels, (micro + 1) * channels)
        centre = turned[part, 0:1]
        scale = turned[part, 1:2] * cols[0:channels, 2:3]
        shift = cols[0:channels, 3:4]

        def act_row(row, _, micro=micro, centre=centre, scale=scale, shift=shift):
            normed = (first_out[micro, row] - centre) * scale + shift
            on_grid = inside(tile, row - 3, (tiles, rows))
            act = (normed * sigmoid(normed) * on_grid).astype(BF16)
            acts[micro, row] = spread(act, masks)
            kept[micro, row] = act
            return 0

        lax.fori_loop(0, high, act_row, 0, unroll=2)
    weight_copy.wait()
    conv_rows(acts, l_second, out, out.shape)
    own_stats(out, 2, rows, send)


def up_kernel(found, cols, second_out, w_up, acts, upper, stats, send, *, rows):
    micros, _, channels, width = second_out.shape
    turned = stat_columns(found, float(rows * width))
    stats[...] = turned
    for micro in range(micros):
        part = slice(micro * channels, (micro + 1) * channels)
        centre = turned[part, 0:1]
        scale = turned[part, 1:2] * cols[0:channels, 4:5]
        shift = cols[0:channels, 5:6]

        def one(row, _, micro=micro, centre=centre, scale=scale, shift=shift):
            normed = (second_out[micro, row + 2] - centre) * scale + shift
            act = (normed * sigmoid(normed)).astype(BF16)
            acts[micro, row] = act
            upper[micro, row] = dot(w_up[...], act)
            return 0

        lax.fori_loop(0, rows, one, 0)
    own_stats(upper, 0, rows, send)


def top_kernel(found, cols, upper, cot, features, grads, stats, send, *, rows):
    micros, _, wide, width = upper.shape
    lines = []
    for micro in range(micros):
        lines += list(pooled_stats(found[:, micro, :], found[:, micros + micro, :], float(rows * width)))
    turned = columns_of(lines)
    stats[...] = turned
    gain, shift = cols[:, 6:7], cols[:, 7:8]
    gain_rows, shift_rows = [], []
    for micro in range(micros):
        centre, rstd = turned[:, 2 * micro : 2 * micro + 1], turned[:, 2 * micro + 1 : 2 * micro + 2]

        def one(row, carry, micro=micro, centre=centre, rstd=rstd):
            unit = (upper[micro, row] - centre) * rstd
            normed = unit * gain + shift
            gate = sigmoid(normed)
            act = normed * gate
            grad = cot[micro, row].astype(F32) * (gate + act * (1.0 - gate))
            features[micro, row] = act.astype(BF16)
            grads[micro, row] = grad
            return carry[0] + fold(grad * unit), carry[1] + fold(grad)

        zero = jnp.zeros((wide, LANES), F32)
        gain_sum, shift_sum = lax.fori_loop(0, rows, one, (zero, zero))
        gain_rows.append(row_of(gain_sum))
        shift_rows.append(row_of(shift_sum))
    send_all(send, gain_rows + shift_rows)


def second_back_kernel(
    found, cols, grads, upper, top_stats, second_out, second_stats, w_up_t, second_act,
    out, weight_grad, edge, gain_grad, shift_grad, send, *, rows
):
    scene = lax.axis_index("scene")
    micros, _, wide, width = grads.shape
    channels = second_out.shape[2]
    sums = sum_rows(found, 2 * micros)
    own_half(sum(sums[:micros]), scene, gain_grad)
    own_half(sum(sums[micros:]), scene, shift_grad)
    turned = columns_of(sums) * (1.0 / (found.shape[0] * rows * width))
    gain, shift = cols[0:channels, 4:5], cols[0:channels, 5:6]
    gain_sums, shift_sums = [], []
    weight_grad[...] = jnp.zeros(weight_grad.shape, F32)
    for micro in range(micros):
        part = slice(micro * channels, (micro + 1) * channels)
        centre, rstd = second_stats[part, 0:1], second_stats[part, 1:2]
        top_centre = top_stats[:, 2 * micro : 2 * micro + 1]
        top_rstd = top_stats[:, 2 * micro + 1 : 2 * micro + 2]
        factor = cols[:, 6:7] * top_rstd
        slope_part = top_rstd * turned[:, micro : micro + 1]
        shift_part = turned[:, micros + micro : micros + micro + 1]

        def one(row, carry, micro=micro, centre=centre, rstd=rstd, top_centre=top_centre, factor=factor,
                slope_part=slope_part, shift_part=shift_part):
            low = factor * (grads[micro, row] - shift_part - (upper[micro, row] - top_centre) * slope_part)
            low = low.astype(BF16)
            weight_grad[...] = weight_grad[...] + dot_lanes(low, second_act[micro, row])
            unit = (second_out[micro, row + 2] - centre) * rstd
            normed = unit * gain + shift
            gate = sigmoid(normed)
            grad = dot(w_up_t[...], low) * (gate + normed * gate * (1.0 - gate))
            out[micro, row] = grad
            return carry[0] + fold(grad * unit), carry[1] + fold(grad)

        zero = jnp.zeros((channels, LANES), F32)
        gain_sum, shift_sum = lax.fori_loop(0, rows, one, (zero, zero))
        edge[micro] = out[micro, rows - 2 : rows].astype(BF16)
        gain_sums.append(gain_sum)
        shift_sums.append(shift_sum)
    send_all(send, [row_of(*gain_sums), row_of(*shift_sums)])


def low_rows(turned, value_of, values, stats, gain, low, high, first, rows, tiles):
    micros, _, channels, width = values.shape
    tile = lax.axis_index("tile")
    masks = edges(channels, width)
    for micro in range(micros):
        part = slice(micro * channels, (micro + 1) * channels)
        centre, rstd = stats[part, 0:1], stats[part, 1:2]
        factor = gain * rstd
        slope_part, shift_part = rstd * turned[part, 0:1], turned[part, 1:2]
        for index in range(high):
            grad, value = value_of(micro, index)
            grad = factor * (grad - shift_part - (value - centre) * slope_part)
            if index + first < 0 or index + first >= rows:
                grad = grad * inside(tile, index + first, (tiles, rows))
            low[micro, index] = spread(grad.astype(BF16), masks)


def first_back_kernel(
    found, cols, grads, before, second_out, second_stats, first_out, first_stats, b_second_in, acts,
    out, weight_grad, edge, gain_grad, shift_grad, send, low, b_second, sems, *, rows, tiles
):
    weight_copy = move(b_second_in, b_second, sems, 0)
    scene = lax.axis_index("scene")
    tile = lax.axis_index("tile")
    micros, _, channels, width = grads.shape
    sums = sum_rows(found, 2)
    own_half(sums[0][:, :channels] + sums[0][:, channels:], scene, gain_grad)
    own_half(sums[1][:, :channels] + sums[1][:, channels:], scene, shift_grad)
    turned = columns_of(sums) * (1.0 / (found.shape[0] * rows * width))

    def value_of(micro, index):
        grad = before[micro, index].astype(F32) if index < 2 else grads[micro, index - 2]
        return grad, second_out[micro, index]

    low_rows(turned, value_of, second_out, second_stats, cols[0:channels, 4:5], low, rows + 2, -2, rows, tiles)
    conv_grad(low, 2, acts, 2, weight_grad, rows)
    weight_copy.wait()
    gain, shift = cols[0:channels, 2:3], cols[0:channels, 3:4]
    last = jnp.where(tile == tiles - 1, 1.0, 0.0)
    gain_sums, shift_sums = [], []
    for micro in range(micros):
        part = slice(micro * channels, (micro + 1) * channels)
        centre, rstd = first_stats[part, 0:1], first_stats[part, 1:2]
        low[micro, rows + 2] = jnp.zeros(low.shape[2:], BF16)
        gain_sum = jnp.zeros((channels, LANES), F32)
        shift_sum = jnp.zeros((channels, LANES), F32)
        for at in range(0, rows + 1, 2):
            if at < rows:
                parts = conv_pair(low, b_second, micro, at, channels)
            else:
                window = low[micro, at : at + 3].reshape(9 * channels, width)
                parts = dot(b_second[0:channels, 0 : 9 * channels], window)
            for j in range(parts.shape[0] // channels):
                grad_act = parts[channels * j : channels * (j + 1)]
                if at + j == 0:
                    grad_act = grad_act * inside(tile, -1, (tiles, rows))
                if at + j == rows:
                    grad_act = grad_act * last
                unit = (first_out[micro, at + j + 2] - centre) * rstd
                normed = unit * gain + shift
                gate = sigmoid(normed)
                grad = grad_act * (gate + normed * gate * (1.0 - gate))
                out[micro, at + j] = grad
                gain_sum = gain_sum + fold(grad * unit)
                shift_sum = shift_sum + fold(grad)
        edge[micro] = out[micro, 0:2].astype(BF16)
        gain_sums.append(gain_sum)
        shift_sums.append(shift_sum)
    send_all(send, [row_of(*gain_sums), row_of(*shift_sums)])


def conv_grad(low, low_first, values, value_first, total, rows):
    micros, _, channels, width = values.shape
    for micro in range(micros):
        grads = jnp.concatenate([low[micro, row + low_first] for row in range(rows)], axis=1)
        windows = jnp.concatenate(
            [
                values[micro, row + value_first : row + value_first + 3].reshape(3 * channels, width)
                for row in range(rows)
            ],
            axis=1,
        )
        product = dot_lanes(grads, windows)
        total[...] = product if micro == 0 else total[...] + product


def half_rows(total, half, scene):
    channels = 2 * half
    start = scene * half
    mine = jnp.concatenate(
        [total[b * channels + start : b * channels + start + half, :] for b in range(2, -1, -1)], axis=0
    )
    wing = mine[:, LANES:]
    cut = wing.shape[0] // 2
    return [mine[:, :LANES], jnp.concatenate([wing[:cut], wing[cut:]], axis=1)]


def pick_kernel(
    found, cols, grads, after, first_out, first_stats, b_first_in, columns, where_rows,
    canvas, second_grad, top_grad,
    send, gain_grad, shift_grad, low, grid, b_first, first_grad, whole, sems, *, rows, tiles, each
):
    weight_copy = move(b_first_in, b_first, sems, 0)
    scene = lax.axis_index("scene")
    micros, _, channels, width = grads.shape
    sums = sum_rows(found, 2)
    own_half(sums[0][:, :channels] + sums[0][:, channels:], scene, gain_grad)
    own_half(sums[1][:, :channels] + sums[1][:, channels:], scene, shift_grad)
    turned = columns_of(sums) * (1.0 / (found.shape[0] * rows * width))

    def value_of(micro, index):
        if index < rows:
            grad = grads[micro, index]
        elif index == rows:
            grad = grads[micro, index] + after[micro, 0].astype(F32)
        else:
            grad = after[micro, 1].astype(F32)
        return grad, first_out[micro, index + 2]

    low_rows(turned, value_of, first_out, first_stats, cols[0:channels, 2:3], low, rows + 2, -1, rows, tiles)
    weight_copy.wait()
    conv_rows(low, b_first, grid, grid.shape)
    conv_grad(low, 1, canvas, 0, first_grad, rows)
    half = channels // 2
    peers, block = send.shape[:2]
    for s in range(2):
        parts = half_rows(first_grad, half, s) + half_rows(second_grad, half, s)
        mine = top_grad[s * channels : (s + 1) * channels, :]
        parts.append(jnp.concatenate([mine[:half], mine[half:]], axis=1))
        parts = jnp.concatenate(parts, axis=0)
        whole[s, 0 : parts.shape[0]] = parts
        if whole.shape[1] > parts.shape[0]:
            whole[s, parts.shape[0] :] = jnp.zeros((whole.shape[1] - parts.shape[0], LANES), F32)
    slots = columns.shape[0]
    lane = lax.broadcasted_iota(jnp.int32, (slots, width), 1).astype(F32)
    picked = []
    for micro in range(micros):
        at = 2 + micro
        column = columns[:, at : at + 1] - 1.0
        column = column - jnp.floor(column * (1.0 / width)) * width
        place = jnp.floor((where_rows[at : at + 1] - 1.0) * (1.0 / width))
        chosen = jnp.where(lane == column, 1.0, 0.0).astype(BF16)
        here = dot_lanes(grid[micro].reshape(rows * channels, width), chosen)
        total = jnp.zeros((channels, slots), F32)
        for r in range(rows):
            total = total + jnp.where(place == r * 1.0, here[r * channels : (r + 1) * channels], 0.0)
        picked.append(total)
    picked = jnp.transpose(jnp.concatenate(picked, axis=0))
    capacity = slots // tiles
    rest = block - capacity - 2 * each
    for peer in range(peers):
        spot = peer // 2
        parts = [picked[spot * capacity : (spot + 1) * capacity]]
        parts += [whole[s, peer * each : (peer + 1) * each] for s in range(2)]
        parts.append(jnp.zeros((rest, LANES), F32))
        send[peer] = jnp.concatenate(parts, axis=0).astype(BF16)


def pillar_back_kernel(found, rows_in, w_pillar, cols, pooled, send, grads, lifted, rows, sems,
                       *, capacity, each):
    fetched = move(rows_in, rows, sems, 0)
    micros = rows.shape[0]
    _, channels, pillars = pooled.shape
    stats, slots = pooled.at[micros : 2 * micros], pooled.at[2 * micros]
    inputs = w_pillar.shape[1]
    depth = rows.shape[2] // pillars
    scene = lax.axis_index("scene")
    peers = found.shape[0]
    slot_count = peers // 2 * capacity
    returned = jnp.concatenate(
        [found[2 * t + scene].astype(F32)[0:capacity] for t in range(peers // 2)], axis=0
    )
    turned = jnp.transpose(returned)
    place = lax.broadcasted_iota(jnp.int32, (slot_count, pillars), 0).astype(F32)
    gain, shift = cols[0:channels, 0:1], cols[0:channels, 1:2]
    gain_sums, shift_sums = [], []
    outer = jnp.zeros((16, channels), F32)
    fetched.wait()
    for micro in range(micros):
        lifted[...] = dot(w_pillar[...], rows[micro, 0:inputs])
        chosen = jnp.where(place == slots[micro : micro + 1], 1.0, 0.0).astype(BF16)
        back = dot(turned[micro * channels : (micro + 1) * channels].astype(BF16), chosen)
        limit = slots[micros + micro : micros + micro + 1]
        centre, rstd = stats[micro, :, 0:1], stats[micro, :, 1:2]
        pool = pooled[micro]
        gain_sum = jnp.zeros((channels, pillars), F32)
        shift_sum = jnp.zeros((channels, pillars), F32)
        for n in range(depth):
            piece = slice(n * pillars, (n + 1) * pillars)
            unit = (lifted[:, piece] - centre) * rstd
            normed = unit * gain + shift
            gate = sigmoid(normed)
            act = normed * gate
            slope = gate + act * (1.0 - gate)
            grad = jnp.where(limit > n, back * jnp.exp(act - pool) * slope, 0.0)
            grads[micro, :, piece] = grad
            gain_sum = gain_sum + grad * unit
            shift_sum = shift_sum + grad
        gain_sums.append(gain_sum)
        shift_sums.append(shift_sum)
        scale = jnp.transpose(jnp.broadcast_to(rstd * gain, (channels, LANES)))[0:1]
        outer = outer + dot_lanes(rows[micro], grads[micro].astype(BF16)) * scale
    lines = [row_of(*gain_sums), row_of(*shift_sums)]
    for k in range(0, 12, 2):
        lines.append(jnp.concatenate([outer[k : k + 1], outer[k + 1 : k + 2]], axis=1))
    exact = jnp.concatenate(lines, axis=0)
    high = exact.astype(BF16).astype(F32)
    weights = jnp.sum(found[...].astype(F32), axis=0)
    rest = send.shape[2] - 16 - each
    for s in range(2):
        mine = weights[capacity + s * each : capacity + (s + 1) * each]
        block = jnp.concatenate([high, exact - high, mine, jnp.zeros((rest, LANES), F32)], axis=0).astype(BF16)
        send[:, s] = jnp.broadcast_to(block[None], (send.shape[0],) + block.shape)


def points_kernel(
    found, rows_in, grads, w_pillar, cols, pooled,
    points_grad, pillar_grad, gain_grad, shift_grad, first_grad, second_grad, up_grad, rows, lifted, sems,
    *, each
):
    fetched = move(rows_in, rows, sems, 0)
    scene = lax.axis_index("scene")
    micros, channels, _ = grads.shape
    stats, slots = pooled.at[micros : 2 * micros], pooled.at[2 * micros]
    _, _, inputs, depth, pillars = points_grad.shape
    half = channels // 2
    total = jnp.sum(found[:, 0:16, :].astype(F32), axis=0)
    total = total[0:8] + total[8:16]
    own_half(total[0:1, :channels] + total[0:1, channels:], scene, gain_grad)
    own_half(total[1:2, :channels] + total[1:2, channels:], scene, shift_grad)
    turned = jnp.transpose(total)
    weight_grad = jnp.concatenate(
        [turned[(k % 2) * channels : (k % 2 + 1) * channels, 2 + k // 2 : 3 + k // 2] for k in range(inputs)],
        axis=1,
    )
    weight = jnp.transpose(w_pillar[...].astype(F32)).astype(BF16)
    fetched.wait()
    for micro in range(micros):
        lifted[...] = dot(w_pillar[...], rows[micro, 0:inputs])
        part = slice(micro * channels, (micro + 1) * channels)
        centre, rstd, inverse = stats[micro, :, 0:1], stats[micro, :, 1:2], stats[micro, :, 2:3]
        factor = cols[0:channels, 0:1] * rstd
        gain_part, shift_part = turned[part, 0:1], turned[part, 1:2]
        spun, mean = stats[micro, :, 16 : 16 + inputs], stats[micro, :, 32 : 32 + inputs]
        weight_grad = weight_grad - factor * (shift_part * mean + gain_part * rstd * spun)
        gain_part, shift_part = gain_part * inverse * rstd, shift_part * inverse
        limit = slots[micros + micro : micros + micro + 1]
        for n in range(depth):
            piece = slice(n * pillars, (n + 1) * pillars)
            low = factor * (grads[micro, :, piece] - shift_part - (lifted[:, piece] - centre) * gain_part)
            low = jnp.where(limit > n, low, 0.0).astype(BF16)
            points_grad[micro, 0, :, n, :] = dot(weight, low)
    weight_grad = jnp.concatenate([weight_grad, jnp.zeros((channels, LANES - inputs), F32)], axis=1)
    weight_grad = jnp.transpose(weight_grad)[0:inputs]
    pillar_grad[...] = jnp.where(scene == 0, weight_grad[:, :half], weight_grad[:, half:])
    whole = jnp.concatenate(
        [found[peer].astype(F32)[16 : 16 + each] for peer in range(found.shape[0])], axis=0
    )
    for index, out in enumerate((first_grad, second_grad)):
        base = index * 9 * half * channels // LANES
        lead = 3 * half
        mine = whole[base : base + lead]
        wing = whole[base + lead : base + lead + lead // 2]
        wing = jnp.concatenate([wing[:, :channels], wing[:, channels:]], axis=0)
        both = jnp.concatenate([mine, wing], axis=1)
        for a in range(3):
            for b in range(3):
                at = (3 * a + b) * channels
                out[:, at : at + channels] = both[b * half : (b + 1) * half, a * channels : (a + 1) * channels]
    base = 2 * 9 * half * channels // LANES
    top = whole[base : base + half]
    up_grad[...] = jnp.concatenate([top[:, :channels], top[:, channels:]], axis=0)


def swap(blocks, axes):
    return lax.all_to_all(blocks, axes, split_axis=0, concat_axis=0)


def shards(
    points, point_counts, pillar_tile, pillar_cell,
    pillar_weight, pillar_gain, pillar_shift,
    first_weight, first_gain, first_shift,
    second_weight, second_gain, second_shift,
    up_weight, up_gain, up_shift, cotangent,
):
    micros, _, inputs, depth, pillars = points.shape
    channels = up_weight.shape[1]
    upper = cotangent.shape[2]
    rows, width = cotangent.shape[3:]
    tiles = lax.axis_size("tile")
    scenes = lax.axis_size("scene")
    peers = tiles * scenes
    capacity = 2 * pillars // tiles
    slot_count = tiles * capacity
    half = channels // 2

    def vmem(shape, dtype):
        return pltpu.VMEM(shape, dtype)

    def grid(high, dtype=F32, lead=channels):
        return ((micros, high, lead, width), dtype)

    sums = ((peers, 2, LANES), F32)
    sources = (
        pillar_tile, pillar_cell, point_counts, points,
        first_weight, second_weight, up_weight, pillar_weight.T,
        pillar_gain, pillar_shift, first_gain, first_shift, second_gain, second_shift, up_gain, up_shift,
    )
    moments, packed, point_rows, slots = run(
        functools.partial(moments_kernel, capacity=capacity),
        [
            ((tiles, scenes, 4, LANES), F32), ((layout(half, channels)[-1] + 16, LANES), BF16),
            ((micros, 16, depth * pillars), BF16), ((8, pillars), F32),
        ],
        *sources,
        hbm=range(len(sources)), copies=len(sources), limit=WIDE_LIMIT,
        scratch=[vmem(source.shape, source.dtype) for source in sources]
        + [vmem((inputs * depth, pillars), F32)],
    )
    moments = swap(moments.reshape(peers, 4, LANES), BOTH)
    both = lax.all_gather(packed, "scene")
    taps = ((2 * channels, 12 * channels), BF16)
    w_pillar, cols, l_first, l_second, b_first, b_second, w_up, w_up_t = run(
        functools.partial(unpack_kernel, inputs=inputs),
        [
            ((channels, inputs), BF16), ((LANES, 8), F32), taps, taps + (1,), taps + (1,), taps + (1,),
            ((upper, channels), BF16), ((channels, upper), BF16),
        ],
        both,
        scratch=[vmem(*taps), vmem(*taps), vmem(*taps)], copies=3,
    )
    cot = cotangent[:, 0].transpose(0, 2, 1, 3)

    send, pooled = run(
        functools.partial(pillar_kernel, capacity=capacity),
        [((slot_count, 3 * LANES), BF16), ((2 * micros + 1, channels, pillars), F32)],
        moments, point_rows, slots, w_pillar, cols,
        hbm=(1, 2), copies=2, limit=WIDE_LIMIT,
        scratch=[
            vmem((channels, depth * pillars), F32), vmem((channels, depth * pillars), F32),
            vmem((micros, 16, depth * pillars), BF16), vmem((8, pillars), F32),
        ],
    )
    arrived = swap(send.reshape(tiles, capacity, 3 * LANES), "tile").reshape(slot_count, 3 * LANES)
    cell_columns, cell_rows = run(
        functools.partial(cells_kernel, capacity=capacity),
        [((slot_count, LANES), F32), ((8, slot_count), F32)],
        moments,
        cost=pl.CostEstimate(flops=10**7, bytes_accessed=10**6, transcendentals=0),
    )
    arrived, cot = lax.optimization_barrier((arrived, cot))

    first_out, canvas, send = run(
        functools.partial(canvas_kernel, rows=rows),
        [grid(rows + 4), grid(rows + 2, BF16), sums],
        arrived, cell_columns, cell_rows, l_first,
        scratch=[vmem(*grid(rows + 6, BF16, 3 * channels))],
    )
    second_out, first_act, first_stats, send = run(
        functools.partial(second_kernel, rows=rows, tiles=tiles),
        [grid(rows + 2), grid(rows + 4, BF16), ((LANES, 8), F32), sums],
        swap(send, BOTH), cols, first_out, l_second,
        hbm=(3,), scratch=[vmem(*grid(rows + 4, BF16, 3 * channels)), vmem(*taps)], copies=1,
    )
    second_act, up_out, second_stats, send = run(
        functools.partial(up_kernel, rows=rows),
        [grid(rows, BF16), grid(rows, F32, upper), ((LANES, 8), F32), ((peers, 4, LANES), F32)],
        swap(send, BOTH), cols, second_out, w_up,
    )
    features, grads, top_stats, send = run(
        functools.partial(top_kernel, rows=rows),
        [grid(rows, BF16, upper), grid(rows, F32, upper), ((LANES, 8), F32), ((peers, 4, LANES), F32)],
        swap(send, BOTH), cols, up_out, cot,
    )
    edge = ((micros, 2, channels, width), BF16)
    vector, top_vector, matrix = ((half,), F32), ((upper // 2,), F32), ((half, 9 * channels), F32)
    second_dz, top_grad, rising_edge, up_gain_grad, up_shift_grad, send = run(
        functools.partial(second_back_kernel, rows=rows),
        [grid(rows), ((upper, channels), F32), edge, top_vector, top_vector, sums],
        swap(send, BOTH), cols, grads, up_out, top_stats, second_out, second_stats, w_up_t, second_act,
    )
    rising = [(i, i + 1) for i in range(tiles - 1)]
    falling = [(j, i) for i, j in rising]
    cross = ((3 * channels, 3 * channels), F32)
    first_dz, second_cross, falling_edge, second_gain_grad, second_shift_grad, send = run(
        functools.partial(first_back_kernel, rows=rows, tiles=tiles),
        [grid(rows + 1), cross, edge, vector, vector, sums],
        swap(send, BOTH), cols, second_dz,
        lax.ppermute(rising_edge, "tile", rising), second_out, second_stats, first_out, first_stats, b_second, first_act,
        hbm=(8,), scratch=[vmem(*grid(rows + 3, BF16, 3 * channels)), vmem(*taps)], copies=1,
    )
    length = (2 * 9 * half * channels + upper * half) // LANES
    each = -(-length // peers)
    block = -(-(capacity + 2 * each) // 8) * 8
    send, first_gain_grad, first_shift_grad = run(
        functools.partial(pick_kernel, rows=rows, tiles=tiles, each=each),
        [((peers, block, LANES), BF16), vector, vector],
        swap(send, BOTH), cols, first_dz,
        lax.ppermute(falling_edge, "tile", falling), first_out, first_stats, b_first, cell_columns, cell_rows, canvas, second_cross, top_grad,
        hbm=(6,),
        scratch=[
            vmem(*grid(rows + 2, BF16, 3 * channels)), vmem(*grid(rows, BF16)), vmem(*taps), vmem(*cross),
            vmem((scenes, peers * each, LANES), F32),
        ],
        copies=1,
    )
    block = 16 + -(-each // 16) * 16
    send, pillar_dz = run(
        functools.partial(pillar_back_kernel, capacity=capacity, each=each),
        [((tiles, scenes, block, LANES), BF16), ((micros, channels, depth * pillars), F32)],
        swap(send, BOTH), point_rows, w_pillar, cols, pooled,
        hbm=(1,),
        scratch=[vmem((channels, depth * pillars), F32), vmem((micros, 16, depth * pillars), BF16)],
        copies=1,
    )
    send, features = lax.optimization_barrier((send, features))
    features = features.transpose(0, 2, 1, 3)[:, None]
    points_grad, pillar_grad, pillar_gain_grad, pillar_shift_grad, first_grad, second_grad, up_grad = run(
        functools.partial(points_kernel, each=each),
        [
            ((micros, 1, inputs, depth, pillars), F32), ((inputs, half), F32), vector, vector,
            matrix, matrix, ((upper // 2, channels), F32),
        ],
        swap(send.reshape(peers, block, LANES), BOTH), point_rows, pillar_dz, w_pillar, cols, pooled,
        hbm=(1,),
        scratch=[vmem((micros, 16, depth * pillars), BF16), vmem((channels, depth * pillars), F32)],
        copies=1,
    )
    return (
        features, points_grad,
        pillar_grad.T, pillar_gain_grad, pillar_shift_grad,
        first_grad, first_gain_grad, first_shift_grad,
        second_grad, second_gain_grad, second_shift_grad,
        up_grad, up_gain_grad, up_shift_grad,
    )


def solution(mesh):
    matrix, vector = P("scene", None), P("scene")
    grid = P(None, "scene", None, "tile", None)
    cloud = P(None, "scene", None, None, "tile")
    pillar = P(None, "scene", "tile")
    weights = (matrix, vector, vector) * 4
    return jax.shard_map(
        shards,
        mesh=mesh,
        in_specs=(cloud, pillar, pillar, pillar) + weights + (grid,),
        out_specs=(grid, cloud) + weights,
        check_vma=False,
    )
```

```python
import functools

import jax
import jax.numpy as jnp
from jax import lax
from jax.experimental import pallas as pl
from jax.experimental.pallas import tpu as pltpu
from jax.sharding import PartitionSpec as P

norm_eps = 0.001
BOTH = ("tile", "scene")
F32 = jnp.float32
BF16 = jnp.bfloat16
VMEM_LIMIT = 24 * 1024 * 1024
WIDE_LIMIT = 60 * 1024 * 1024
LANES = 128


def run(kernel, outs, *args, hbm=(), scratch=(), copies=0, cost=None, limit=VMEM_LIMIT):
    specs = [
        pl.BlockSpec(memory_space=pltpu.HBM if index in hbm else pltpu.VMEM) for index in range(len(args))
    ]
    scratch = list(scratch)
    if copies:
        scratch.append(pltpu.SemaphoreType.DMA((copies,)))
    return pl.pallas_call(
        kernel,
        out_shape=[jax.ShapeDtypeStruct(out[0], out[1]) for out in outs],
        in_specs=specs,
        out_specs=[
            pl.BlockSpec(memory_space=pltpu.HBM if len(out) > 2 else pltpu.VMEM) for out in outs
        ],
        scratch_shapes=scratch,
        compiler_params=pltpu.CompilerParams(vmem_limit_bytes=limit),
        cost_estimate=cost,
    )(*args)


def move(source, target, sems, index):
    copy = pltpu.make_async_copy(source, target, sems.at[index])
    copy.start()
    return copy


def dot(left, right, precision=None):
    return jnp.dot(left, right, preferred_element_type=F32, precision=precision)


def dot_lanes(left, right, precision=None):
    return lax.dot_general(
        left, right, (((1,), (1,)), ((), ())), preferred_element_type=F32, precision=precision
    )


def sigmoid(values):
    return 0.5 + 0.5 * jnp.tanh(0.5 * values)


def fold(values):
    total = values[:, :LANES]
    for start in range(LANES, values.shape[1], LANES):
        total = total + values[:, start : start + LANES]
    return total


def row_of(left, right=None):
    both = left if right is None else jnp.concatenate([left, right], axis=0)
    return jnp.sum(jnp.transpose(both), axis=0, keepdims=True)


def columns_of(rows):
    rows = rows + [jnp.zeros((8 - len(rows), LANES), F32)] if len(rows) < 8 else rows
    return jnp.transpose(jnp.concatenate(rows, axis=0))


def inside(tile, row, height):
    tiles, rows = height
    place = tile * rows + row
    return jnp.where((place >= 0) & (place < tiles * rows), 1.0, 0.0).astype(F32)


def send_all(ref, rows):
    for index, row in enumerate(rows):
        ref[:, index : index + 1, :] = jnp.broadcast_to(row[None], (ref.shape[0], 1, LANES))


def pooled_stats(means, squares, count):
    peers = means.shape[0]
    mean = jnp.sum(means, axis=0, keepdims=True) * (1.0 / peers)
    away = means - mean
    spread = jnp.sum(squares + count * away * away, axis=0, keepdims=True) * (1.0 / (peers * count))
    return mean, lax.rsqrt(spread + norm_eps)


def stat_columns(found, count):
    return columns_of(list(pooled_stats(found[:, 0, :], found[:, 1, :], count)))


def sum_rows(found, lines):
    return [jnp.sum(found[:, index, :], axis=0, keepdims=True) for index in range(lines)]


def own_half(row, scene, out):
    size = out.shape[0]
    out[...] = jnp.where(scene == 0, row[:, 0:size], row[:, size : 2 * size]).reshape(size)


def edges(channels, width):
    lane = lax.broadcasted_iota(jnp.int32, (channels, width), 1)
    return lane > 0, lane < width - 1


def spread(row, masks):
    zero = jnp.zeros_like(row)
    left = jnp.where(masks[0], pltpu.roll(row, 1, 1), zero)
    right = jnp.where(masks[1], pltpu.roll(row, row.shape[1] - 1, 1), zero)
    return jnp.concatenate([left, row, right], axis=0)


def layout(half, channels):
    first = 0
    second = first + half * -(-9 * channels // LANES)
    up = second + half * -(-9 * channels // LANES)
    vectors = up + channels
    return first, second, up, vectors, vectors + 16


def widen(value):
    missing = LANES - value.shape[1]
    if missing == 0:
        return value
    return jnp.concatenate([value, jnp.zeros((value.shape[0], missing), value.dtype)], axis=1)


def pack(held, out):
    first, second, up, pillar = held[:4]
    half, channels = first.shape[0], up.shape[1]
    starts = layout(half, channels)
    for ref, start in ((first, starts[0]), (second, starts[1])):
        for j in range(-(-9 * channels // LANES)):
            out[start + j * half : start + (j + 1) * half, :] = widen(
                ref[:, j * LANES : min((j + 1) * LANES, 9 * channels)]
            )
    out[starts[2] : starts[2] + channels, :] = widen(up[...])
    rows = [vector[...].astype(F32).reshape(1, -1) for vector in held[4:]]
    rows = [widen(row) for row in rows] + [jnp.zeros((16 - len(rows), LANES), F32)]
    turned = widen(pillar[...].astype(F32))
    rows += [turned, jnp.zeros((16 - turned.shape[0], LANES), F32)]
    out[starts[3] :, :] = jnp.concatenate(rows, axis=0).astype(BF16)


def unpack_kernel(
    both, w_pillar, cols, l_first, l_second, b_first, b_second, w_up, w_up_t,
    h_second, h_first_back, h_second_back, sems, *, inputs
):
    half = w_pillar.shape[0] // 2
    channels = 2 * half
    starts = layout(half, channels)
    tiles = -(-9 * channels // LANES)

    def wide(start):
        return jnp.concatenate(
            [
                jnp.concatenate(
                    [both[s, start + j * half : start + (j + 1) * half, :] for j in range(tiles)], axis=1
                )
                for s in range(2)
            ],
            axis=0,
        ).astype(F32)

    up = jnp.concatenate(
        [both[s, starts[2] : starts[2] + channels, 0:channels] for s in range(2)], axis=0
    )
    w_up[...] = up
    w_up_t[...] = jnp.transpose(up.astype(F32)).astype(BF16)
    turned = jnp.concatenate(
        [both[s, starts[4] : starts[4] + 16, 0:half].astype(F32) for s in range(2)], axis=1
    )
    w_pillar[...] = jnp.transpose(widen(turned))[0:channels, 0:inputs].astype(BF16)
    vectors = [both[s, starts[3] : starts[3] + 16, :].astype(F32) for s in range(2)]
    rows = []
    for index in range(8):
        size = half if index < 6 else channels
        row = jnp.concatenate([vectors[s][index : index + 1, 0:size] for s in range(2)], axis=1)
        rows.append(jnp.concatenate([row] * (LANES // (2 * size)), axis=1))
    cols[...] = columns_of(rows)
    zero = jnp.zeros((channels, 3 * channels), F32)
    copies = []
    for weight, ahead, back in (
        (wide(starts[0]), l_first, h_first_back), (wide(starts[1]), h_second, h_second_back)
    ):
        weight = weight[:, : 9 * channels]
        turned = jnp.transpose(weight)
        flipped = jnp.concatenate(
            [turned[tap * channels : (tap + 1) * channels] for tap in range(8, -1, -1)], axis=1
        )
        for ref, taps in ((ahead, weight), (back, flipped)):
            ref[0:channels, :] = jnp.concatenate([taps, zero], axis=1).astype(BF16)
            ref[channels : 2 * channels, :] = jnp.concatenate([zero, taps], axis=1).astype(BF16)
    copies.append(move(h_second, l_second, sems, 0))
    copies.append(move(h_first_back, b_first, sems, 1))
    copies.append(move(h_second_back, b_second, sems, 2))
    for copy in copies:
        copy.wait()


def slot_line(wide, depth, inputs):
    return jnp.concatenate([wide[pl.ds(n, inputs, stride=depth), :] for n in range(depth)], axis=1)


def slot_mask(count, depth):
    return jnp.concatenate([jnp.where(count > n, 1.0, 0.0) for n in range(depth)], axis=1)


def ranks(tile):
    pillars = tile.shape[1]
    across = jnp.broadcast_to(tile, (pillars, pillars))
    down = jnp.transpose(across)
    row = lax.broadcasted_iota(jnp.int32, (pillars, pillars), 0)
    col = lax.broadcasted_iota(jnp.int32, (pillars, pillars), 1)
    return jnp.sum(jnp.where((across == down) & (row < col), 1.0, 0.0), axis=0, keepdims=True)


def moments_kernel(*refs, capacity):
    number = 16
    sources, out, packed, lines_out = refs[:number], *refs[number : number + 3]
    held, wide, sems = refs[number + 3 : 2 * number + 3], refs[-2], refs[-1]
    copies = [move(sources[i], held[i], sems, i) for i in range(number)]
    tiles, cells, counts, points = held[:4]
    micros, _, inputs, depth, pillars = points.shape
    peers, scenes = out.shape[:2]
    copies[0].wait()
    copies[1].wait()
    lines, slot_rows = [], []
    for micro in range(micros):
        tile = tiles[micro].astype(F32)
        cell = (cells[micro] + 1).astype(F32)
        high = jnp.floor(cell * (1.0 / 16.0))
        low = cell - high * 16.0
        rank = ranks(tile)
        slot_rows.append(tile * capacity + rank)
        spot = lax.broadcasted_iota(jnp.int32, (capacity, pillars), 0).astype(F32)
        placed = jnp.where(spot == rank, 1.0, 0.0).astype(BF16)
        peer = lax.broadcasted_iota(jnp.int32, (peers, pillars), 0).astype(F32)
        for group in range(3):
            named = tile == peer + (group - 1.0)
            lines.append(
                16.0 * dot_lanes(jnp.where(named, high, 0.0).astype(BF16), placed)
                + dot_lanes(jnp.where(named, low, 0.0).astype(BF16), placed)
            )
    used = 3 * micros * capacity
    line = jnp.concatenate(lines + [jnp.zeros((peers, LANES - used), F32)], axis=1).reshape(peers, 1, LANES)
    for scene in range(scenes):
        out[:, scene, micros : micros + 1, :] = line
    copies[2].wait()
    copies[3].wait()
    for micro in range(micros):
        wide[...] = points[micro, 0].astype(F32).reshape(inputs * depth, pillars)
        rows = slot_line(wide, depth, inputs)
        notes = jnp.concatenate([slot_rows[micro], counts[micro].astype(F32)], axis=0)
        notes = jnp.concatenate([notes, jnp.zeros((2, rows.shape[1] - pillars), F32)], axis=1)
        lines_out[micro] = jnp.concatenate(
            [rows, notes, jnp.zeros((14 - inputs, rows.shape[1]), F32)], axis=0
        ).astype(BF16)
        mask = slot_mask(counts[micro], depth)
        total = jnp.sum(mask, axis=1, keepdims=True)
        mean = jnp.sum(rows * mask, axis=1, keepdims=True) / total
        centred = (rows - mean) * mask
        products = dot_lanes(centred, centred, lax.Precision.HIGHEST)
        lane = lax.broadcasted_iota(jnp.int32, (inputs, inputs), 1)
        diagonal = lax.broadcasted_iota(jnp.int32, (inputs, inputs), 0) == lane
        mean_row = jnp.sum(jnp.where(diagonal, mean, 0.0), axis=0, keepdims=True)
        row = jnp.concatenate(
            [products[k : k + 1] for k in range(inputs)]
            + [mean_row, total, jnp.zeros((1, LANES - inputs * inputs - inputs - 1), F32)],
            axis=1,
        )
        for scene in range(scenes):
            out[:, scene, micro : micro + 1, :] = jnp.broadcast_to(row[None], (peers, 1, LANES))
    for copy in copies[4:]:
        copy.wait()
    pack(held[4:], packed)


def cells_kernel(found, columns, rows, *, capacity):
    scene = lax.axis_index("scene")
    slots = columns.shape[0]
    peers = found.shape[0]
    values = found[:, 2, :]
    slot = lax.broadcasted_iota(jnp.int32, (slots, peers), 0)
    peer = lax.broadcasted_iota(jnp.int32, (slots, peers), 1)
    lane = lax.broadcasted_iota(jnp.int32, (slots, LANES), 1)
    row = lax.broadcasted_iota(jnp.int32, (slots, LANES), 0)
    result = jnp.zeros((slots, LANES), F32)
    chosen = jnp.where(peer == 2 * (slot // capacity) + scene, 1.0, 0.0)
    spread = dot(chosen, values, lax.Precision.HIGHEST)
    for micro in range(2):
        for group in range(3):
            mine = jnp.where(lane == (3 * micro + group) * capacity + row % capacity, spread, 0.0)
            column = jnp.sum(mine, axis=1, keepdims=True)
            result = jnp.where(lane == 2 * group + micro, column, result)
    columns[...] = result
    rows[...] = jnp.transpose(result)[0:8]


def pillar_notes(rows, micro, inputs, pillars):
    notes = rows[micro, :, 0:pillars].astype(F32)
    return notes[inputs : inputs + 1], notes[inputs + 1 : inputs + 2]


def pillar_kernel(
    found, point_rows, w_pillar, cols, send, pooled, lifted, acts, *, capacity
):
    micros = point_rows.shape[0]
    channels, inputs = w_pillar.shape
    pillars = pooled.shape[2]
    depth = point_rows.shape[2] // pillars
    weight = w_pillar[...]
    wide_weight = weight.astype(F32)
    rows_out = send.shape[0]
    square = inputs * inputs
    stacked, slot_rows = [], []
    for micro in range(micros):
        lifted[...] = dot(weight, point_rows[micro, 0:inputs])
        moments = found[:, micro, :]
        sizes = moments[:, square + inputs : square + inputs + 1]
        means = moments[:, square : square + inputs]
        count = jnp.sum(sizes, axis=0, keepdims=True)
        mean = jnp.sum(means * sizes, axis=0, keepdims=True) / count
        away = means - mean
        products = lax.dot_general(
            away * sizes, away, (((0,), (0,)), ((), ())),
            preferred_element_type=F32, precision=lax.Precision.HIGHEST,
        )
        summed = jnp.sum(moments, axis=0, keepdims=True)
        products = products + jnp.concatenate(
            [summed[:, k * inputs : (k + 1) * inputs] for k in range(inputs)], axis=0
        )
        cov = products / count
        spun = wide_weight[:, 0:1] * cov[0:1]
        for k in range(1, inputs):
            spun = spun + wide_weight[:, k : k + 1] * cov[k : k + 1]
        spread = jnp.sum(spun * wide_weight, axis=1, keepdims=True)
        centre = jnp.sum(wide_weight * mean, axis=1, keepdims=True)
        rstd = lax.rsqrt(spread + norm_eps)
        inverse = jnp.broadcast_to(1.0 / count, (channels, 1))
        pooled[micros + micro] = jnp.concatenate(
            [
                centre, rstd, inverse, jnp.zeros((channels, 13), F32),
                spun, jnp.zeros((channels, 16 - inputs), F32),
                jnp.broadcast_to(mean, (channels, inputs)), jnp.zeros((channels, LANES - 32 - inputs), F32),
            ],
            axis=1,
        )
        scale = rstd * cols[0:channels, 0:1]
        shift = cols[0:channels, 1:2]
        slot, limit = pillar_notes(point_rows, micro, inputs, pillars)
        slot_rows.append(slot)
        top = jnp.full((channels, pillars), -jnp.inf, F32)
        for n in range(depth):
            piece = slice(n * pillars, (n + 1) * pillars)
            normed = (lifted[:, piece] - centre) * scale + shift
            act = normed * sigmoid(normed)
            acts[:, piece] = act
            top = jnp.maximum(top, jnp.where(limit > n, act, -jnp.inf))
        total = jnp.zeros((channels, pillars), F32)
        for n in range(depth):
            piece = slice(n * pillars, (n + 1) * pillars)
            total = total + jnp.where(limit > n, jnp.exp(acts[:, piece] - top), 0.0)
        result = top + jnp.log(total)
        pooled[micro] = result
        parts = [jnp.zeros((channels, pillars), F32)] * micros
        parts[micro] = result.astype(BF16).astype(F32)
        stacked.append(jnp.transpose(jnp.concatenate(parts, axis=0)))
    values = jnp.concatenate(stacked, axis=0).astype(BF16)
    for group in range(3):
        place = lax.broadcasted_iota(jnp.int32, (rows_out, pillars), 0) + (group - 1) * capacity
        chosen = jnp.concatenate(
            [jnp.where(place.astype(F32) == row, 1.0, 0.0) for row in slot_rows], axis=1
        ).astype(BF16)
        send[:, group * LANES : (group + 1) * LANES] = dot(chosen, values).astype(BF16)


def own_stats(ref, first_row, rows, send):
    micros, _, channels, width = ref.shape
    sums, squares = [], []
    for micro in range(micros):
        total = fold(ref[micro, first_row])
        for row in range(first_row + 1, first_row + rows):
            total = total + fold(ref[micro, row])
        total = total * (1.0 / (rows * width))
        mean = jnp.sum(total, axis=1, keepdims=True)
        spread = jnp.zeros(total.shape, F32)
        for row in range(first_row, first_row + rows):
            away = ref[micro, row] - mean
            spread = spread + fold(away * away)
        sums.append(total)
        squares.append(spread)
    if channels == LANES:
        send_all(send, [row_of(part) for part in sums + squares])
    else:
        send_all(send, [row_of(*sums), row_of(*squares)])


def conv_pair(source, weight, micro, at, channels):
    window = source[micro, pl.ds(at, 4)].reshape(12 * channels, source.shape[3])
    return dot(weight[...], window)


def conv_rows(source, weight, out, shape):
    micros, high, channels, width = shape
    pairs = high // 2

    def step(index, _):
        micro, at = index // pairs, 2 * (index % pairs)
        both = conv_pair(source, weight, micro, at, channels)
        out[micro, at] = both[:channels].astype(out.dtype)
        out[micro, at + 1] = both[channels:].astype(out.dtype)
        return 0

    lax.fori_loop(0, micros * pairs, step, 0, unroll=2)


def canvas_kernel(found, columns, where_rows, l_first, out, kept, send, canvas, *, rows):
    scenes, high, channels, width = out.shape
    masks = edges(channels, width)
    slots = found.shape[0]
    lane = lax.broadcasted_iota(jnp.int32, (slots, width), 1).astype(F32)
    for group in range(3):
        values = jnp.transpose(found[:, group * LANES : (group + 1) * LANES].astype(F32))
        first, count = ((rows - 2, 2), (0, rows), (0, 2))[group]
        for scene in range(scenes):
            at = 2 * group + scene
            column = columns[:, at : at + 1] - 1.0
            column = column - jnp.floor(column * (1.0 / width)) * width
            row = jnp.floor((where_rows[at : at + 1] - 1.0) * (1.0 / width))
            mine = values[scene * channels : (scene + 1) * channels]
            placed = jnp.concatenate(
                [jnp.where(row == r * 1.0, mine, 0.0) for r in range(first, first + count)], axis=0
            ).astype(BF16)
            chosen = jnp.where(lane == column, 1.0, 0.0).astype(BF16)
            grid = dot(placed, chosen).astype(BF16)
            start = (0, 2, rows + 2)[group]
            for r in range(count):
                row = grid[r * channels : (r + 1) * channels]
                canvas[scene, start + r] = spread(row, masks)
                if 1 <= start + r <= rows + 2:
                    kept[scene, start + r - 1] = row
    conv_rows(canvas, l_first, out, out.shape)
    own_stats(out, 1, rows, send)


def second_kernel(found, cols, first_out, l_second_in, out, kept, stats, send, acts, l_second, sems,
                  *, rows, tiles):
    weight_copy = move(l_second_in, l_second, sems, 0)
    micros, high, channels, width = first_out.shape
    tile = lax.axis_index("tile")
    turned = stat_columns(found, float(rows * width))
    stats[...] = turned
    masks = edges(channels, width)
    for micro in range(micros):
        part = slice(micro * channels, (micro + 1) * channels)
        centre = turned[part, 0:1]
        scale = turned[part, 1:2] * cols[0:channels, 2:3]
        shift = cols[0:channels, 3:4]

        def act_row(row, _, micro=micro, centre=centre, scale=scale, shift=shift):
            normed = (first_out[micro, row] - centre) * scale + shift
            on_grid = inside(tile, row - 1, (tiles, rows))
            act = (normed * sigmoid(normed) * on_grid).astype(BF16)
            acts[micro, row] = spread(act, masks)
            kept[micro, row] = act
            return 0

        lax.fori_loop(0, high, act_row, 0, unroll=2)
    weight_copy.wait()
    conv_rows(acts, l_second, out, out.shape)
    own_stats(out, 0, rows, send)


def up_kernel(found, cols, second_out, w_up, acts, upper, stats, send, *, rows):
    micros, _, channels, width = second_out.shape
    turned = stat_columns(found, float(rows * width))
    stats[...] = turned
    for micro in range(micros):
        part = slice(micro * channels, (micro + 1) * channels)
        centre = turned[part, 0:1]
        scale = turned[part, 1:2] * cols[0:channels, 4:5]
        shift = cols[0:channels, 5:6]

        def one(row, _, micro=micro, centre=centre, scale=scale, shift=shift):
            normed = (second_out[micro, row] - centre) * scale + shift
            act = (normed * sigmoid(normed)).astype(BF16)
            acts[micro, row] = act
            upper[micro, row] = dot(w_up[...], act)
            return 0

        lax.fori_loop(0, rows, one, 0)
    own_stats(upper, 0, rows, send)


def top_kernel(found, cols, upper, cot, features, grads, stats, send, *, rows):
    micros, _, wide, width = upper.shape
    lines = []
    for micro in range(micros):
        lines += list(pooled_stats(found[:, micro, :], found[:, micros + micro, :], float(rows * width)))
    turned = columns_of(lines)
    stats[...] = turned
    gain, shift = cols[:, 6:7], cols[:, 7:8]
    gain_rows, shift_rows = [], []
    for micro in range(micros):
        centre, rstd = turned[:, 2 * micro : 2 * micro + 1], turned[:, 2 * micro + 1 : 2 * micro + 2]

        def one(row, carry, micro=micro, centre=centre, rstd=rstd):
            unit = (upper[micro, row] - centre) * rstd
            normed = unit * gain + shift
            gate = sigmoid(normed)
            act = normed * gate
            grad = cot[micro, row].astype(F32) * (gate + act * (1.0 - gate))
            features[micro, row] = act.astype(BF16)
            grads[micro, row] = grad
            return carry[0] + fold(grad * unit), carry[1] + fold(grad)

        zero = jnp.zeros((wide, LANES), F32)
        gain_sum, shift_sum = lax.fori_loop(0, rows, one, (zero, zero))
        gain_rows.append(row_of(gain_sum))
        shift_rows.append(row_of(shift_sum))
    send_all(send, gain_rows + shift_rows)


def second_back_kernel(
    found, cols, grads, upper, top_stats, second_out, second_stats, w_up_t, second_act,
    out, weight_grad, gain_grad, shift_grad, send, *, rows
):
    scene = lax.axis_index("scene")
    micros, _, wide, width = grads.shape
    channels = second_out.shape[2]
    sums = sum_rows(found, 2 * micros)
    own_half(sum(sums[:micros]), scene, gain_grad)
    own_half(sum(sums[micros:]), scene, shift_grad)
    turned = columns_of(sums) * (1.0 / (found.shape[0] * rows * width))
    gain, shift = cols[0:channels, 4:5], cols[0:channels, 5:6]
    gain_sums, shift_sums = [], []
    weight_grad[...] = jnp.zeros(weight_grad.shape, F32)
    for micro in range(micros):
        part = slice(micro * channels, (micro + 1) * channels)
        centre, rstd = second_stats[part, 0:1], second_stats[part, 1:2]
        top_centre = top_stats[:, 2 * micro : 2 * micro + 1]
        top_rstd = top_stats[:, 2 * micro + 1 : 2 * micro + 2]
        factor = cols[:, 6:7] * top_rstd
        slope_part = top_rstd * turned[:, micro : micro + 1]
        shift_part = turned[:, micros + micro : micros + micro + 1]

        def one(row, carry, micro=micro, centre=centre, rstd=rstd, top_centre=top_centre, factor=factor,
                slope_part=slope_part, shift_part=shift_part):
            low = factor * (grads[micro, row] - shift_part - (upper[micro, row] - top_centre) * slope_part)
            low = low.astype(BF16)
            weight_grad[...] = weight_grad[...] + dot_lanes(low, second_act[micro, row])
            unit = (second_out[micro, row] - centre) * rstd
            normed = unit * gain + shift
            gate = sigmoid(normed)
            grad = dot(w_up_t[...], low) * (gate + normed * gate * (1.0 - gate))
            out[micro, row] = grad
            return carry[0] + fold(grad * unit), carry[1] + fold(grad)

        zero = jnp.zeros((channels, LANES), F32)
        gain_sum, shift_sum = lax.fori_loop(0, rows, one, (zero, zero))
        gain_sums.append(gain_sum)
        shift_sums.append(shift_sum)
    send_all(send, [row_of(*gain_sums), row_of(*shift_sums)])


def low_rows(turned, value_of, values, stats, gain, low, high, first, rows, tiles):
    micros, _, channels, width = values.shape
    tile = lax.axis_index("tile")
    masks = edges(channels, width)
    for micro in range(micros):
        part = slice(micro * channels, (micro + 1) * channels)
        centre, rstd = stats[part, 0:1], stats[part, 1:2]
        factor = gain * rstd
        slope_part, shift_part = rstd * turned[part, 0:1], turned[part, 1:2]
        for index in range(high):
            grad, value = value_of(micro, index)
            grad = factor * (grad - shift_part - (value - centre) * slope_part)
            if index + first < 0 or index + first >= rows:
                grad = grad * inside(tile, index + first, (tiles, rows))
            low[micro, index] = spread(grad.astype(BF16), masks)


def first_slopes(first_out, stats, cols, micro, channels):
    part = slice(micro * channels, (micro + 1) * channels)
    centre, rstd = stats[part, 0:1], stats[part, 1:2]
    gain, shift = cols[0:channels, 2:3], cols[0:channels, 3:4]

    def at(row):
        unit = (first_out[micro, row] - centre) * rstd
        normed = unit * gain + shift
        gate = sigmoid(normed)
        return gate + normed * gate * (1.0 - gate), unit

    return at


def first_back_kernel(
    found, cols, grads, second_out, second_stats, first_out, first_stats, b_second_in, acts,
    out, weight_grad, rising, falling, gain_grad, shift_grad, send, low, b_second, sems, *, rows, tiles
):
    weight_copy = move(b_second_in, b_second, sems, 0)
    scene = lax.axis_index("scene")
    tile = lax.axis_index("tile")
    micros, _, channels, width = grads.shape
    sums = sum_rows(found, 2)
    own_half(sums[0][:, :channels] + sums[0][:, channels:], scene, gain_grad)
    own_half(sums[1][:, :channels] + sums[1][:, channels:], scene, shift_grad)
    turned = columns_of(sums) * (1.0 / (found.shape[0] * rows * width))
    low_rows(
        turned, lambda micro, row: (grads[micro, row], second_out[micro, row]), second_out, second_stats,
        cols[0:channels, 4:5], low, rows, 0, rows, tiles,
    )
    for micro in range(micros):
        for row in range(2):
            falling[micro, row] = low[micro, row, channels : 2 * channels]
            rising[micro, row] = low[micro, rows - 2 + row, channels : 2 * channels]
    conv_grad(low, 0, acts, 0, weight_grad, rows)
    weight_copy.wait()
    half = 6 * channels
    gain_sums, shift_sums = [], []
    for micro in range(micros):
        slopes = first_slopes(first_out, first_stats, cols, micro, channels)
        gain_sum = jnp.zeros((channels, LANES), F32)
        shift_sum = jnp.zeros((channels, LANES), F32)
        for at in range(0, rows + 2, 2):
            if at == 0:
                parts = dot(b_second[:, half:], low[micro, 0:2].reshape(half, width))
            elif at == rows:
                parts = dot(b_second[:, :half], low[micro, rows - 2 : rows].reshape(half, width))
            else:
                parts = conv_pair(low, b_second, micro, at - 2, channels)
            for j in range(2):
                slope, unit = slopes(at + j)
                grad = parts[channels * j : channels * (j + 1)] * slope
                if at + j == 0 or at + j == rows + 1:
                    grad = grad * inside(tile, at + j - 1, (tiles, rows))
                out[micro, at + j] = grad
                gain_sum = gain_sum + fold(grad * unit)
                shift_sum = shift_sum + fold(grad)
        gain_sums.append(gain_sum)
        shift_sums.append(shift_sum)
    send_all(send, [row_of(*gain_sums), row_of(*shift_sums)])


def conv_grad(low, low_first, values, value_first, total, rows):
    micros, _, channels, width = values.shape
    for micro in range(micros):
        grads = jnp.concatenate([low[micro, row + low_first] for row in range(rows)], axis=1)
        windows = jnp.concatenate(
            [
                values[micro, row + value_first : row + value_first + 3].reshape(3 * channels, width)
                for row in range(rows)
            ],
            axis=1,
        )
        product = dot_lanes(grads, windows)
        total[...] = product if micro == 0 else total[...] + product


def half_rows(total, half, scene):
    channels = 2 * half
    start = scene * half
    mine = jnp.concatenate(
        [total[b * channels + start : b * channels + start + half, :] for b in range(2, -1, -1)], axis=0
    )
    wing = mine[:, LANES:]
    cut = wing.shape[0] // 2
    return [mine[:, :LANES], jnp.concatenate([wing[:cut], wing[cut:]], axis=1)]


def pick_kernel(
    found, cols, grads, before, after, first_out, first_stats, b_first_in, b_second_in, columns, where_rows,
    canvas, second_grad, top_grad,
    send, gain_grad, shift_grad, low, grid, b_first, b_second, halo, first_grad, whole, sems,
    *, rows, tiles, each
):
    second_copy = move(b_second_in, b_second, sems, 1)
    weight_copy = move(b_first_in, b_first, sems, 0)
    scene = lax.axis_index("scene")
    micros, _, channels, width = grads.shape
    sums = sum_rows(found, 2)
    own_half(sums[0][:, :channels] + sums[0][:, channels:], scene, gain_grad)
    own_half(sums[1][:, :channels] + sums[1][:, channels:], scene, shift_grad)
    turned = columns_of(sums) * (1.0 / (found.shape[0] * rows * width))
    masks = edges(channels, width)
    half = 6 * channels
    second_copy.wait()
    for micro in range(micros):
        slopes = first_slopes(first_out, first_stats, cols, micro, channels)
        for at, ref, columns_used in ((0, before, slice(0, half)), (rows, after, slice(half, 2 * half))):
            window = jnp.concatenate([spread(ref[micro, row], masks) for row in range(2)], axis=0)
            parts = dot(b_second[:, columns_used], window)
            for j in range(2):
                slope, _ = slopes(at + j)
                halo[micro, at + j] = parts[channels * j : channels * (j + 1)] * slope

    def value_of(micro, index):
        grad = grads[micro, index]
        if index < 2 or index >= rows:
            grad = grad + halo[micro, index]
        return grad, first_out[micro, index]

    low_rows(turned, value_of, first_out, first_stats, cols[0:channels, 2:3], low, rows + 2, -1, rows, tiles)
    weight_copy.wait()
    conv_rows(low, b_first, grid, grid.shape)
    conv_grad(low, 1, canvas, 0, first_grad, rows)
    half = channels // 2
    peers, block = send.shape[:2]
    for s in range(2):
        parts = half_rows(first_grad, half, s) + half_rows(second_grad, half, s)
        mine = top_grad[s * channels : (s + 1) * channels, :]
        parts.append(jnp.concatenate([mine[:half], mine[half:]], axis=1))
        parts = jnp.concatenate(parts, axis=0)
        whole[s, 0 : parts.shape[0]] = parts
        if whole.shape[1] > parts.shape[0]:
            whole[s, parts.shape[0] :] = jnp.zeros((whole.shape[1] - parts.shape[0], LANES), F32)
    slots = columns.shape[0]
    lane = lax.broadcasted_iota(jnp.int32, (slots, width), 1).astype(F32)
    picked = []
    for micro in range(micros):
        at = 2 + micro
        column = columns[:, at : at + 1] - 1.0
        column = column - jnp.floor(column * (1.0 / width)) * width
        place = jnp.floor((where_rows[at : at + 1] - 1.0) * (1.0 / width))
        chosen = jnp.where(lane == column, 1.0, 0.0).astype(BF16)
        here = dot_lanes(grid[micro].reshape(rows * channels, width), chosen)
        total = jnp.zeros((channels, slots), F32)
        for r in range(rows):
            total = total + jnp.where(place == r * 1.0, here[r * channels : (r + 1) * channels], 0.0)
        picked.append(total)
    picked = jnp.transpose(jnp.concatenate(picked, axis=0))
    capacity = slots // tiles
    rest = block - capacity - 2 * each
    for peer in range(peers):
        spot = peer // 2
        parts = [picked[spot * capacity : (spot + 1) * capacity]]
        parts += [whole[s, peer * each : (peer + 1) * each] for s in range(2)]
        parts.append(jnp.zeros((rest, LANES), F32))
        send[peer] = jnp.concatenate(parts, axis=0).astype(BF16)


def pillar_back_kernel(found, rows_in, w_pillar, cols, pooled, send, grads, lifted, rows, sems,
                       *, capacity, each):
    fetched = move(rows_in, rows, sems, 0)
    micros = rows.shape[0]
    _, channels, pillars = pooled.shape
    stats = pooled.at[micros : 2 * micros]
    inputs = w_pillar.shape[1]
    depth = rows.shape[2] // pillars
    scene = lax.axis_index("scene")
    peers = found.shape[0]
    slot_count = peers // 2 * capacity
    returned = jnp.concatenate(
        [found[2 * t + scene].astype(F32)[0:capacity] for t in range(peers // 2)], axis=0
    )
    turned = jnp.transpose(returned)
    place = lax.broadcasted_iota(jnp.int32, (slot_count, pillars), 0).astype(F32)
    gain, shift = cols[0:channels, 0:1], cols[0:channels, 1:2]
    gain_sums, shift_sums = [], []
    outer = jnp.zeros((16, channels), F32)
    fetched.wait()
    for micro in range(micros):
        lifted[...] = dot(w_pillar[...], rows[micro, 0:inputs])
        slot, limit = pillar_notes(rows, micro, inputs, pillars)
        chosen = jnp.where(place == slot, 1.0, 0.0).astype(BF16)
        back = dot(turned[micro * channels : (micro + 1) * channels].astype(BF16), chosen)
        centre, rstd = stats[micro, :, 0:1], stats[micro, :, 1:2]
        pool = pooled[micro]
        gain_sum = jnp.zeros((channels, pillars), F32)
        shift_sum = jnp.zeros((channels, pillars), F32)
        for n in range(depth):
            piece = slice(n * pillars, (n + 1) * pillars)
            unit = (lifted[:, piece] - centre) * rstd
            normed = unit * gain + shift
            gate = sigmoid(normed)
            act = normed * gate
            slope = gate + act * (1.0 - gate)
            grad = jnp.where(limit > n, back * jnp.exp(act - pool) * slope, 0.0)
            grads[micro, :, piece] = grad
            gain_sum = gain_sum + grad * unit
            shift_sum = shift_sum + grad
        gain_sums.append(gain_sum)
        shift_sums.append(shift_sum)
        scale = jnp.transpose(jnp.broadcast_to(rstd * gain, (channels, LANES)))[0:1]
        outer = outer + dot_lanes(rows[micro], grads[micro].astype(BF16)) * scale
    lines = [row_of(*gain_sums), row_of(*shift_sums)]
    for k in range(0, 12, 2):
        lines.append(jnp.concatenate([outer[k : k + 1], outer[k + 1 : k + 2]], axis=1))
    exact = jnp.concatenate(lines, axis=0)
    high = exact.astype(BF16).astype(F32)
    weights = jnp.sum(found[...].astype(F32), axis=0)
    rest = send.shape[2] - 16 - each
    for s in range(2):
        mine = weights[capacity + s * each : capacity + (s + 1) * each]
        block = jnp.concatenate([high, exact - high, mine, jnp.zeros((rest, LANES), F32)], axis=0).astype(BF16)
        send[:, s] = jnp.broadcast_to(block[None], (send.shape[0],) + block.shape)


def points_kernel(
    found, rows_in, grads, w_pillar, cols, pooled,
    points_grad, pillar_grad, gain_grad, shift_grad, first_grad, second_grad, up_grad, rows, lifted, sems,
    *, each
):
    fetched = move(rows_in, rows, sems, 0)
    scene = lax.axis_index("scene")
    micros, channels, _ = grads.shape
    stats = pooled.at[micros : 2 * micros]
    _, _, inputs, depth, pillars = points_grad.shape
    half = channels // 2
    total = jnp.sum(found[:, 0:16, :].astype(F32), axis=0)
    total = total[0:8] + total[8:16]
    own_half(total[0:1, :channels] + total[0:1, channels:], scene, gain_grad)
    own_half(total[1:2, :channels] + total[1:2, channels:], scene, shift_grad)
    turned = jnp.transpose(total)
    weight_grad = jnp.concatenate(
        [turned[(k % 2) * channels : (k % 2 + 1) * channels, 2 + k // 2 : 3 + k // 2] for k in range(inputs)],
        axis=1,
    )
    weight = jnp.transpose(w_pillar[...].astype(F32)).astype(BF16)
    fetched.wait()
    for micro in range(micros):
        lifted[...] = dot(w_pillar[...], rows[micro, 0:inputs])
        part = slice(micro * channels, (micro + 1) * channels)
        centre, rstd, inverse = stats[micro, :, 0:1], stats[micro, :, 1:2], stats[micro, :, 2:3]
        factor = cols[0:channels, 0:1] * rstd
        gain_part, shift_part = turned[part, 0:1], turned[part, 1:2]
        spun, mean = stats[micro, :, 16 : 16 + inputs], stats[micro, :, 32 : 32 + inputs]
        weight_grad = weight_grad - factor * (shift_part * mean + gain_part * rstd * spun)
        gain_part, shift_part = gain_part * inverse * rstd, shift_part * inverse
        _, limit = pillar_notes(rows, micro, inputs, pillars)
        for n in range(depth):
            piece = slice(n * pillars, (n + 1) * pillars)
            low = factor * (grads[micro, :, piece] - shift_part - (lifted[:, piece] - centre) * gain_part)
            low = jnp.where(limit > n, low, 0.0).astype(BF16)
            points_grad[micro, 0, :, n, :] = dot(weight, low)
    weight_grad = jnp.concatenate([weight_grad, jnp.zeros((channels, LANES - inputs), F32)], axis=1)
    weight_grad = jnp.transpose(weight_grad)[0:inputs]
    pillar_grad[...] = jnp.where(scene == 0, weight_grad[:, :half], weight_grad[:, half:])
    whole = jnp.concatenate(
        [found[peer].astype(F32)[16 : 16 + each] for peer in range(found.shape[0])], axis=0
    )
    for index, out in enumerate((first_grad, second_grad)):
        base = index * 9 * half * channels // LANES
        lead = 3 * half
        mine = whole[base : base + lead]
        wing = whole[base + lead : base + lead + lead // 2]
        wing = jnp.concatenate([wing[:, :channels], wing[:, channels:]], axis=0)
        both = jnp.concatenate([mine, wing], axis=1)
        for a in range(3):
            for b in range(3):
                at = (3 * a + b) * channels
                out[:, at : at + channels] = both[b * half : (b + 1) * half, a * channels : (a + 1) * channels]
    base = 2 * 9 * half * channels // LANES
    top = whole[base : base + half]
    up_grad[...] = jnp.concatenate([top[:, :channels], top[:, channels:]], axis=0)


def swap(blocks, axes):
    return lax.all_to_all(blocks, axes, split_axis=0, concat_axis=0)


def shards(
    points, point_counts, pillar_tile, pillar_cell,
    pillar_weight, pillar_gain, pillar_shift,
    first_weight, first_gain, first_shift,
    second_weight, second_gain, second_shift,
    up_weight, up_gain, up_shift, cotangent,
):
    micros, _, inputs, depth, pillars = points.shape
    channels = up_weight.shape[1]
    upper = cotangent.shape[2]
    rows, width = cotangent.shape[3:]
    tiles = lax.axis_size("tile")
    scenes = lax.axis_size("scene")
    peers = tiles * scenes
    capacity = 2 * pillars // tiles
    slot_count = tiles * capacity
    half = channels // 2

    def vmem(shape, dtype):
        return pltpu.VMEM(shape, dtype)

    def grid(high, dtype=F32, lead=channels):
        return ((micros, high, lead, width), dtype)

    sums = ((peers, 2, LANES), F32)
    sources = (
        pillar_tile, pillar_cell, point_counts, points,
        first_weight, second_weight, up_weight, pillar_weight.T,
        pillar_gain, pillar_shift, first_gain, first_shift, second_gain, second_shift, up_gain, up_shift,
    )
    moments, packed, point_rows = run(
        functools.partial(moments_kernel, capacity=capacity),
        [
            ((tiles, scenes, 4, LANES), F32), ((layout(half, channels)[-1] + 16, LANES), BF16),
            ((micros, 16, depth * pillars), BF16),
        ],
        *sources,
        hbm=range(len(sources)), copies=len(sources), limit=WIDE_LIMIT,
        scratch=[vmem(source.shape, source.dtype) for source in sources]
        + [vmem((inputs * depth, pillars), F32)],
    )
    moments = swap(moments.reshape(peers, 4, LANES), BOTH)
    both = lax.all_gather(packed, "scene")
    taps = ((2 * channels, 12 * channels), BF16)
    w_pillar, cols, l_first, l_second, b_first, b_second, w_up, w_up_t = run(
        functools.partial(unpack_kernel, inputs=inputs),
        [
            ((channels, inputs), BF16), ((LANES, 8), F32), taps, taps + (1,), taps + (1,), taps + (1,),
            ((upper, channels), BF16), ((channels, upper), BF16),
        ],
        both,
        scratch=[vmem(*taps), vmem(*taps), vmem(*taps)], copies=3,
    )
    cot = cotangent[:, 0].transpose(0, 2, 1, 3)

    send, pooled = run(
        functools.partial(pillar_kernel, capacity=capacity),
        [((slot_count, 3 * LANES), BF16), ((2 * micros, channels, pillars), F32)],
        moments, point_rows, w_pillar, cols,
        scratch=[vmem((channels, depth * pillars), F32), vmem((channels, depth * pillars), F32)],
    )
    arrived = swap(send.reshape(tiles, capacity, 3 * LANES), "tile").reshape(slot_count, 3 * LANES)
    cell_columns, cell_rows = run(
        functools.partial(cells_kernel, capacity=capacity),
        [((slot_count, LANES), F32), ((8, slot_count), F32)],
        moments,
        cost=pl.CostEstimate(flops=10**7, bytes_accessed=10**6, transcendentals=0),
    )
    arrived, cot = lax.optimization_barrier((arrived, cot))

    first_out, canvas, send = run(
        functools.partial(canvas_kernel, rows=rows),
        [grid(rows + 2), grid(rows + 2, BF16), sums],
        arrived, cell_columns, cell_rows, l_first,
        scratch=[vmem(*grid(rows + 4, BF16, 3 * channels))],
    )
    second_out, first_act, first_stats, send = run(
        functools.partial(second_kernel, rows=rows, tiles=tiles),
        [grid(rows), grid(rows + 2, BF16), ((LANES, 8), F32), sums],
        swap(send, BOTH), cols, first_out, l_second,
        hbm=(3,), scratch=[vmem(*grid(rows + 2, BF16, 3 * channels)), vmem(*taps)], copies=1,
    )
    second_act, up_out, second_stats, send = run(
        functools.partial(up_kernel, rows=rows),
        [grid(rows, BF16), grid(rows, F32, upper), ((LANES, 8), F32), ((peers, 4, LANES), F32)],
        swap(send, BOTH), cols, second_out, w_up,
    )
    features, grads, top_stats, send = run(
        functools.partial(top_kernel, rows=rows),
        [grid(rows, BF16, upper), grid(rows, F32, upper), ((LANES, 8), F32), ((peers, 4, LANES), F32)],
        swap(send, BOTH), cols, up_out, cot,
    )
    edge = ((micros, 2, channels, width), BF16)
    vector, top_vector, matrix = ((half,), F32), ((upper // 2,), F32), ((half, 9 * channels), F32)
    second_dz, top_grad, up_gain_grad, up_shift_grad, send = run(
        functools.partial(second_back_kernel, rows=rows),
        [grid(rows), ((upper, channels), F32), top_vector, top_vector, sums],
        swap(send, BOTH), cols, grads, up_out, top_stats, second_out, second_stats, w_up_t, second_act,
    )
    rising = [(i, i + 1) for i in range(tiles - 1)]
    falling = [(j, i) for i, j in rising]
    cross = ((3 * channels, 3 * channels), F32)
    first_dz, second_cross, rising_edge, falling_edge, second_gain_grad, second_shift_grad, send = run(
        functools.partial(first_back_kernel, rows=rows, tiles=tiles),
        [grid(rows + 2), cross, edge, edge, vector, vector, sums],
        swap(send, BOTH), cols, second_dz,
        second_out, second_stats, first_out, first_stats, b_second, first_act,
        hbm=(7,), scratch=[vmem(*grid(rows, BF16, 3 * channels)), vmem(*taps)], copies=1,
    )
    length = (2 * 9 * half * channels + upper * half) // LANES
    each = -(-length // peers)
    block = -(-(capacity + 2 * each) // 8) * 8
    send, first_gain_grad, first_shift_grad = run(
        functools.partial(pick_kernel, rows=rows, tiles=tiles, each=each),
        [((peers, block, LANES), BF16), vector, vector],
        swap(send, BOTH), cols, first_dz,
        lax.ppermute(rising_edge, "tile", rising), lax.ppermute(falling_edge, "tile", falling),
        first_out, first_stats, b_first, b_second, cell_columns, cell_rows, canvas, second_cross, top_grad,
        hbm=(7, 8),
        scratch=[
            vmem(*grid(rows + 2, BF16, 3 * channels)), vmem(*grid(rows, BF16)), vmem(*taps), vmem(*taps),
            vmem(*grid(rows + 2)), vmem(*cross), vmem((scenes, peers * each, LANES), F32),
        ],
        copies=2,
    )
    block = 16 + -(-each // 16) * 16
    send, pillar_dz = run(
        functools.partial(pillar_back_kernel, capacity=capacity, each=each),
        [((tiles, scenes, block, LANES), BF16), ((micros, channels, depth * pillars), F32)],
        swap(send, BOTH), point_rows, w_pillar, cols, pooled,
        hbm=(1,),
        scratch=[vmem((channels, depth * pillars), F32), vmem((micros, 16, depth * pillars), BF16)],
        copies=1,
    )
    send, features = lax.optimization_barrier((send, features))
    features = features.transpose(0, 2, 1, 3)[:, None]
    points_grad, pillar_grad, pillar_gain_grad, pillar_shift_grad, first_grad, second_grad, up_grad = run(
        functools.partial(points_kernel, each=each),
        [
            ((micros, 1, inputs, depth, pillars), F32), ((inputs, half), F32), vector, vector,
            matrix, matrix, ((upper // 2, channels), F32),
        ],
        swap(send.reshape(peers, block, LANES), BOTH), point_rows, pillar_dz, w_pillar, cols, pooled,
        hbm=(1,),
        scratch=[vmem((micros, 16, depth * pillars), BF16), vmem((channels, depth * pillars), F32)],
        copies=1,
    )
    return (
        features, points_grad,
        pillar_grad.T, pillar_gain_grad, pillar_shift_grad,
        first_grad, first_gain_grad, first_shift_grad,
        second_grad, second_gain_grad, second_shift_grad,
        up_grad, up_gain_grad, up_shift_grad,
    )


def solution(mesh):
    matrix, vector = P("scene", None), P("scene")
    grid = P(None, "scene", None, "tile", None)
    cloud = P(None, "scene", None, None, "tile")
    pillar = P(None, "scene", "tile")
    weights = (matrix, vector, vector) * 4
    return jax.shard_map(
        shards,
        mesh=mesh,
        in_specs=(cloud, pillar, pillar, pillar) + weights + (grid,),
        out_specs=(grid, cloud) + weights,
        check_vma=False,
    )
```

```python
import functools

import jax
import jax.numpy as jnp
from jax import lax
from jax.experimental import pallas as pl
from jax.experimental.pallas import tpu as pltpu
from jax.sharding import PartitionSpec as P

norm_eps = 0.001
BOTH = ("tile", "scene")
F32 = jnp.float32
BF16 = jnp.bfloat16
VMEM_LIMIT = 24 * 1024 * 1024
WIDE_LIMIT = 60 * 1024 * 1024
LANES = 128


def run(kernel, outs, *args, hbm=(), scratch=(), copies=0, cost=None, limit=VMEM_LIMIT):
    specs = [
        pl.BlockSpec(memory_space=pltpu.HBM if index in hbm else pltpu.VMEM) for index in range(len(args))
    ]
    scratch = list(scratch)
    if copies:
        scratch.append(pltpu.SemaphoreType.DMA((copies,)))
    return pl.pallas_call(
        kernel,
        out_shape=[jax.ShapeDtypeStruct(out[0], out[1]) for out in outs],
        in_specs=specs,
        out_specs=[
            pl.BlockSpec(memory_space=pltpu.HBM if len(out) > 2 else pltpu.VMEM) for out in outs
        ],
        scratch_shapes=scratch,
        compiler_params=pltpu.CompilerParams(vmem_limit_bytes=limit),
        cost_estimate=cost,
    )(*args)


def move(source, target, sems, index):
    copy = pltpu.make_async_copy(source, target, sems.at[index])
    copy.start()
    return copy


def dot(left, right, precision=None):
    return jnp.dot(left, right, preferred_element_type=F32, precision=precision)


def dot_lanes(left, right, precision=None):
    return lax.dot_general(
        left, right, (((1,), (1,)), ((), ())), preferred_element_type=F32, precision=precision
    )


def sigmoid(values):
    return 0.5 + 0.5 * jnp.tanh(0.5 * values)


def fold(values):
    total = values[:, :LANES]
    for start in range(LANES, values.shape[1], LANES):
        total = total + values[:, start : start + LANES]
    return total


def row_of(left, right=None):
    both = left if right is None else jnp.concatenate([left, right], axis=0)
    return jnp.sum(jnp.transpose(both), axis=0, keepdims=True)


def columns_of(rows):
    rows = rows + [jnp.zeros((8 - len(rows), LANES), F32)] if len(rows) < 8 else rows
    return jnp.transpose(jnp.concatenate(rows, axis=0))


def inside(tile, row, height):
    tiles, rows = height
    place = tile * rows + row
    return jnp.where((place >= 0) & (place < tiles * rows), 1.0, 0.0).astype(F32)


def send_all(ref, rows):
    for index, row in enumerate(rows):
        ref[:, index : index + 1, :] = jnp.broadcast_to(row[None], (ref.shape[0], 1, LANES))


def pooled_stats(means, squares, count):
    peers = means.shape[0]
    mean = jnp.sum(means, axis=0, keepdims=True) * (1.0 / peers)
    away = means - mean
    spread = jnp.sum(squares + count * away * away, axis=0, keepdims=True) * (1.0 / (peers * count))
    return mean, lax.rsqrt(spread + norm_eps)


def stat_columns(found, count):
    return columns_of(list(pooled_stats(found[:, 0, :], found[:, 1, :], count)))


def sum_rows(found, lines):
    return [jnp.sum(found[:, index, :], axis=0, keepdims=True) for index in range(lines)]


def own_half(row, scene, out):
    size = out.shape[0]
    out[...] = jnp.where(scene == 0, row[:, 0:size], row[:, size : 2 * size]).reshape(size)


def edges(channels, width):
    lane = lax.broadcasted_iota(jnp.int32, (channels, width), 1)
    return lane > 0, lane < width - 1


def spread(row, masks):
    zero = jnp.zeros_like(row)
    left = jnp.where(masks[0], pltpu.roll(row, 1, 1), zero)
    right = jnp.where(masks[1], pltpu.roll(row, row.shape[1] - 1, 1), zero)
    return jnp.concatenate([left, row, right], axis=0)


def layout(half, channels):
    first = 0
    second = first + half * -(-9 * channels // LANES)
    up = second + half * -(-9 * channels // LANES)
    vectors = up + channels
    return first, second, up, vectors, vectors + 16


def widen(value):
    missing = LANES - value.shape[1]
    if missing == 0:
        return value
    return jnp.concatenate([value, jnp.zeros((value.shape[0], missing), value.dtype)], axis=1)


def pack(held, out):
    first, second, up, pillar = held[:4]
    half, channels = first.shape[0], up.shape[1]
    starts = layout(half, channels)
    for ref, start in ((first, starts[0]), (second, starts[1])):
        for j in range(-(-9 * channels // LANES)):
            out[start + j * half : start + (j + 1) * half, :] = widen(
                ref[:, j * LANES : min((j + 1) * LANES, 9 * channels)]
            )
    out[starts[2] : starts[2] + channels, :] = widen(up[...])
    rows = [vector[...].astype(F32).reshape(1, -1) for vector in held[4:]]
    rows = [widen(row) for row in rows] + [jnp.zeros((16 - len(rows), LANES), F32)]
    turned = widen(pillar[...].astype(F32))
    rows += [turned, jnp.zeros((16 - turned.shape[0], LANES), F32)]
    out[starts[3] :, :] = jnp.concatenate(rows, axis=0).astype(BF16)


def unpack_kernel(
    both, w_pillar, cols, l_first, l_second, b_first, b_second, w_up, w_up_t,
    h_second, h_first_back, h_second_back, sems, *, inputs
):
    half = w_pillar.shape[0] // 2
    channels = 2 * half
    starts = layout(half, channels)
    tiles = -(-9 * channels // LANES)

    def wide(start):
        return jnp.concatenate(
            [
                jnp.concatenate(
                    [both[s, start + j * half : start + (j + 1) * half, :] for j in range(tiles)], axis=1
                )
                for s in range(2)
            ],
            axis=0,
        ).astype(F32)

    up = jnp.concatenate(
        [both[s, starts[2] : starts[2] + channels, 0:channels] for s in range(2)], axis=0
    )
    w_up[...] = up
    w_up_t[...] = jnp.transpose(up.astype(F32)).astype(BF16)
    turned = jnp.concatenate(
        [both[s, starts[4] : starts[4] + 16, 0:half].astype(F32) for s in range(2)], axis=1
    )
    w_pillar[...] = jnp.transpose(widen(turned))[0:channels, 0:inputs].astype(BF16)
    vectors = [both[s, starts[3] : starts[3] + 16, :].astype(F32) for s in range(2)]
    rows = []
    for index in range(8):
        size = half if index < 6 else channels
        row = jnp.concatenate([vectors[s][index : index + 1, 0:size] for s in range(2)], axis=1)
        rows.append(jnp.concatenate([row] * (LANES // (2 * size)), axis=1))
    cols[...] = columns_of(rows)
    zero = jnp.zeros((channels, 3 * channels), F32)
    copies = []
    for weight, ahead, back in (
        (wide(starts[0]), l_first, h_first_back), (wide(starts[1]), h_second, h_second_back)
    ):
        weight = weight[:, : 9 * channels]
        turned = jnp.transpose(weight)
        flipped = jnp.concatenate(
            [turned[tap * channels : (tap + 1) * channels] for tap in range(8, -1, -1)], axis=1
        )
        for ref, taps in ((ahead, weight), (back, flipped)):
            ref[0:channels, :] = jnp.concatenate([taps, zero], axis=1).astype(BF16)
            ref[channels : 2 * channels, :] = jnp.concatenate([zero, taps], axis=1).astype(BF16)
    copies.append(move(h_second, l_second, sems, 0))
    copies.append(move(h_first_back, b_first, sems, 1))
    copies.append(move(h_second_back, b_second, sems, 2))
    for copy in copies:
        copy.wait()


def slot_line(wide, depth, inputs):
    return jnp.concatenate([wide[pl.ds(n, inputs, stride=depth), :] for n in range(depth)], axis=1)


def slot_mask(count, depth):
    return jnp.concatenate([jnp.where(count > n, 1.0, 0.0) for n in range(depth)], axis=1)


def ranks(tile):
    pillars = tile.shape[1]
    across = jnp.broadcast_to(tile, (pillars, pillars))
    down = jnp.transpose(across)
    row = lax.broadcasted_iota(jnp.int32, (pillars, pillars), 0)
    col = lax.broadcasted_iota(jnp.int32, (pillars, pillars), 1)
    return jnp.sum(jnp.where((across == down) & (row < col), 1.0, 0.0), axis=0, keepdims=True)


def moments_kernel(*refs, capacity):
    number = 16
    sources, out, packed, lines_out = refs[:number], *refs[number : number + 3]
    held, wide, sems = refs[number + 3 : 2 * number + 3], refs[-2], refs[-1]
    copies = [move(sources[i], held[i], sems, i) for i in range(number)]
    tiles, cells, counts, points = held[:4]
    micros, _, inputs, depth, pillars = points.shape
    peers, scenes = out.shape[:2]
    copies[0].wait()
    copies[1].wait()
    lines, slot_rows = [], []
    for micro in range(micros):
        tile = tiles[micro].astype(F32)
        cell = (cells[micro] + 1).astype(F32)
        high = jnp.floor(cell * (1.0 / 16.0))
        low = cell - high * 16.0
        rank = ranks(tile)
        slot_rows.append(tile * capacity + rank)
        spot = lax.broadcasted_iota(jnp.int32, (capacity, pillars), 0).astype(F32)
        placed = jnp.where(spot == rank, 1.0, 0.0).astype(BF16)
        peer = lax.broadcasted_iota(jnp.int32, (peers, pillars), 0).astype(F32)
        for group in range(3):
            named = tile == peer + (group - 1.0)
            lines.append(
                16.0 * dot_lanes(jnp.where(named, high, 0.0).astype(BF16), placed)
                + dot_lanes(jnp.where(named, low, 0.0).astype(BF16), placed)
            )
    used = 3 * micros * capacity
    line = jnp.concatenate(lines + [jnp.zeros((peers, LANES - used), F32)], axis=1).reshape(peers, 1, LANES)
    for scene in range(scenes):
        out[:, scene, micros : micros + 1, :] = line
    copies[2].wait()
    copies[3].wait()
    for micro in range(micros):
        wide[...] = points[micro, 0].astype(F32).reshape(inputs * depth, pillars)
        rows = slot_line(wide, depth, inputs)
        notes = jnp.concatenate([slot_rows[micro], counts[micro].astype(F32)], axis=0)
        notes = jnp.concatenate([notes, jnp.zeros((2, rows.shape[1] - pillars), F32)], axis=1)
        lines_out[micro] = jnp.concatenate(
            [rows, notes, jnp.zeros((14 - inputs, rows.shape[1]), F32)], axis=0
        ).astype(BF16)
        mask = slot_mask(counts[micro], depth)
        total = jnp.sum(mask, axis=1, keepdims=True)
        mean = jnp.sum(rows * mask, axis=1, keepdims=True) / total
        centred = (rows - mean) * mask
        products = dot_lanes(centred, centred, lax.Precision.HIGHEST)
        lane = lax.broadcasted_iota(jnp.int32, (inputs, inputs), 1)
        diagonal = lax.broadcasted_iota(jnp.int32, (inputs, inputs), 0) == lane
        mean_row = jnp.sum(jnp.where(diagonal, mean, 0.0), axis=0, keepdims=True)
        row = jnp.concatenate(
            [products[k : k + 1] for k in range(inputs)]
            + [mean_row, total, jnp.zeros((1, LANES - inputs * inputs - inputs - 1), F32)],
            axis=1,
        )
        for scene in range(scenes):
            out[:, scene, micro : micro + 1, :] = jnp.broadcast_to(row[None], (peers, 1, LANES))
    for copy in copies[4:]:
        copy.wait()
    pack(held[4:], packed)


def cells_kernel(found, columns, rows, *, capacity):
    scene = lax.axis_index("scene")
    slots = columns.shape[0]
    peers = found.shape[0]
    values = found[:, 2, :]
    slot = lax.broadcasted_iota(jnp.int32, (slots, peers), 0)
    peer = lax.broadcasted_iota(jnp.int32, (slots, peers), 1)
    lane = lax.broadcasted_iota(jnp.int32, (slots, LANES), 1)
    row = lax.broadcasted_iota(jnp.int32, (slots, LANES), 0)
    result = jnp.zeros((slots, LANES), F32)
    chosen = jnp.where(peer == 2 * (slot // capacity) + scene, 1.0, 0.0)
    spread = dot(chosen, values, lax.Precision.HIGHEST)
    for micro in range(2):
        for group in range(3):
            mine = jnp.where(lane == (3 * micro + group) * capacity + row % capacity, spread, 0.0)
            column = jnp.sum(mine, axis=1, keepdims=True)
            result = jnp.where(lane == 2 * group + micro, column, result)
    columns[...] = result
    rows[...] = jnp.transpose(result)[0:8]


def pillar_notes(rows, micro, inputs, pillars):
    notes = rows[micro, :, 0:pillars].astype(F32)
    return notes[inputs : inputs + 1], notes[inputs + 1 : inputs + 2]


def pillar_kernel(
    found, point_rows, w_pillar, cols, send, pooled, lifted, acts, *, capacity
):
    micros = point_rows.shape[0]
    channels, inputs = w_pillar.shape
    pillars = pooled.shape[2]
    depth = point_rows.shape[2] // pillars
    weight = w_pillar[...]
    wide_weight = weight.astype(F32)
    rows_out = send.shape[0]
    square = inputs * inputs
    stacked, slot_rows = [], []
    for micro in range(micros):
        lifted[...] = dot(weight, point_rows[micro, 0:inputs])
        moments = found[:, micro, :]
        sizes = moments[:, square + inputs : square + inputs + 1]
        means = moments[:, square : square + inputs]
        count = jnp.sum(sizes, axis=0, keepdims=True)
        mean = jnp.sum(means * sizes, axis=0, keepdims=True) / count
        away = means - mean
        products = lax.dot_general(
            away * sizes, away, (((0,), (0,)), ((), ())),
            preferred_element_type=F32, precision=lax.Precision.HIGHEST,
        )
        summed = jnp.sum(moments, axis=0, keepdims=True)
        products = products + jnp.concatenate(
            [summed[:, k * inputs : (k + 1) * inputs] for k in range(inputs)], axis=0
        )
        cov = products / count
        spun = wide_weight[:, 0:1] * cov[0:1]
        for k in range(1, inputs):
            spun = spun + wide_weight[:, k : k + 1] * cov[k : k + 1]
        spread = jnp.sum(spun * wide_weight, axis=1, keepdims=True)
        centre = jnp.sum(wide_weight * mean, axis=1, keepdims=True)
        rstd = lax.rsqrt(spread + norm_eps)
        inverse = jnp.broadcast_to(1.0 / count, (channels, 1))
        pooled[micros + micro] = jnp.concatenate(
            [
                centre, rstd, inverse, jnp.zeros((channels, 13), F32),
                spun, jnp.zeros((channels, 16 - inputs), F32),
                jnp.broadcast_to(mean, (channels, inputs)), jnp.zeros((channels, LANES - 32 - inputs), F32),
            ],
            axis=1,
        )
        scale = rstd * cols[0:channels, 0:1]
        shift = cols[0:channels, 1:2]
        slot, limit = pillar_notes(point_rows, micro, inputs, pillars)
        slot_rows.append(slot)
        top = jnp.full((channels, pillars), -jnp.inf, F32)
        for n in range(depth):
            piece = slice(n * pillars, (n + 1) * pillars)
            normed = (lifted[:, piece] - centre) * scale + shift
            act = normed * sigmoid(normed)
            acts[:, piece] = act
            top = jnp.maximum(top, jnp.where(limit > n, act, -jnp.inf))
        total = jnp.zeros((channels, pillars), F32)
        for n in range(depth):
            piece = slice(n * pillars, (n + 1) * pillars)
            total = total + jnp.where(limit > n, jnp.exp(acts[:, piece] - top), 0.0)
        result = top + jnp.log(total)
        pooled[micro] = result
        parts = [jnp.zeros((channels, pillars), F32)] * micros
        parts[micro] = result.astype(BF16).astype(F32)
        stacked.append(jnp.transpose(jnp.concatenate(parts, axis=0)))
    values = jnp.concatenate(stacked, axis=0).astype(BF16)
    for group in range(3):
        place = lax.broadcasted_iota(jnp.int32, (rows_out, pillars), 0) + (group - 1) * capacity
        chosen = jnp.concatenate(
            [jnp.where(place.astype(F32) == row, 1.0, 0.0) for row in slot_rows], axis=1
        ).astype(BF16)
        send[:, group * LANES : (group + 1) * LANES] = dot(chosen, values).astype(BF16)


def own_stats(ref, first_row, rows, send):
    micros, _, channels, width = ref.shape
    sums, squares = [], []
    for micro in range(micros):
        total = fold(ref[micro, first_row])
        for row in range(first_row + 1, first_row + rows):
            total = total + fold(ref[micro, row])
        total = total * (1.0 / (rows * width))
        mean = jnp.sum(total, axis=1, keepdims=True)
        spread = jnp.zeros(total.shape, F32)
        for row in range(first_row, first_row + rows):
            away = ref[micro, row] - mean
            spread = spread + fold(away * away)
        sums.append(total)
        squares.append(spread)
    if channels == LANES:
        send_all(send, [row_of(part) for part in sums + squares])
    else:
        send_all(send, [row_of(*sums), row_of(*squares)])


def conv_pair(source, weight, micro, at, channels):
    window = source[micro, pl.ds(at, 4)].reshape(12 * channels, source.shape[3])
    return dot(weight[...], window)


def conv_rows(source, weight, out, shape):
    micros, high, channels, width = shape
    pairs = high // 2

    def step(index, _):
        micro, at = index // pairs, 2 * (index % pairs)
        both = conv_pair(source, weight, micro, at, channels)
        out[micro, at] = both[:channels].astype(out.dtype)
        out[micro, at + 1] = both[channels:].astype(out.dtype)
        return 0

    lax.fori_loop(0, micros * pairs, step, 0, unroll=2)


def canvas_kernel(found, columns, where_rows, l_first, out, kept, send, canvas, *, rows):
    scenes, high, channels, width = out.shape
    masks = edges(channels, width)
    slots = found.shape[0]
    lane = lax.broadcasted_iota(jnp.int32, (slots, width), 1).astype(F32)
    for group in range(3):
        values = jnp.transpose(found[:, group * LANES : (group + 1) * LANES].astype(F32))
        first, count = ((rows - 2, 2), (0, rows), (0, 2))[group]
        for scene in range(scenes):
            at = 2 * group + scene
            column = columns[:, at : at + 1] - 1.0
            column = column - jnp.floor(column * (1.0 / width)) * width
            row = jnp.floor((where_rows[at : at + 1] - 1.0) * (1.0 / width))
            mine = values[scene * channels : (scene + 1) * channels]
            placed = jnp.concatenate(
                [jnp.where(row == r * 1.0, mine, 0.0) for r in range(first, first + count)], axis=0
            ).astype(BF16)
            chosen = jnp.where(lane == column, 1.0, 0.0).astype(BF16)
            grid = dot(placed, chosen).astype(BF16)
            start = (0, 2, rows + 2)[group]
            for r in range(count):
                row = grid[r * channels : (r + 1) * channels]
                canvas[scene, start + r] = spread(row, masks)
                if 1 <= start + r <= rows + 2:
                    kept[scene, start + r - 1] = row
    conv_rows(canvas, l_first, out, out.shape)
    own_stats(out, 1, rows, send)


def second_kernel(found, cols, first_out, l_second_in, out, kept, stats, send, acts, l_second, sems,
                  *, rows, tiles):
    weight_copy = move(l_second_in, l_second, sems, 0)
    micros, high, channels, width = first_out.shape
    tile = lax.axis_index("tile")
    turned = stat_columns(found, float(rows * width))
    stats[...] = turned
    masks = edges(channels, width)
    for micro in range(micros):
        part = slice(micro * channels, (micro + 1) * channels)
        centre = turned[part, 0:1]
        scale = turned[part, 1:2] * cols[0:channels, 2:3]
        shift = cols[0:channels, 3:4]

        def act_row(row, _, micro=micro, centre=centre, scale=scale, shift=shift):
            normed = (first_out[micro, row] - centre) * scale + shift
            on_grid = inside(tile, row - 1, (tiles, rows))
            act = (normed * sigmoid(normed) * on_grid).astype(BF16)
            acts[micro, row] = spread(act, masks)
            kept[micro, row] = act
            return 0

        lax.fori_loop(0, high, act_row, 0, unroll=2)
    weight_copy.wait()
    conv_rows(acts, l_second, out, out.shape)
    own_stats(out, 0, rows, send)


def up_kernel(found, cols, second_out, w_up, acts, upper, slopes, plain, crossed, stats, send, *, rows):
    micros, _, channels, width = second_out.shape
    peers = send.shape[0]
    each = crossed.shape[0] // peers
    turned = stat_columns(found, float(rows * width))
    stats[...] = turned
    gain, shift = cols[0:channels, 4:5], cols[0:channels, 5:6]
    lines = []
    for micro in range(micros):
        part = slice(micro * channels, (micro + 1) * channels)
        centre, rstd = turned[part, 0:1], turned[part, 1:2]
        slope_sum = jnp.zeros((channels, LANES), F32)
        unit_sum = jnp.zeros((channels, LANES), F32)
        for row in range(rows):
            unit = (second_out[micro, row] - centre) * rstd
            normed = unit * gain + shift
            gate = sigmoid(normed)
            act = normed * gate
            slope = gate + act * (1.0 - gate)
            sloped = slope * unit
            slope_sum = slope_sum + fold(slope)
            unit_sum = unit_sum + fold(sloped)
            slopes[micro, row] = jnp.concatenate([slope, sloped], axis=0).astype(BF16)
            act = act.astype(BF16)
            acts[micro, row] = act
            upper[micro, row] = dot(w_up[...], act)
        lines.append(row_of(slope_sum, unit_sum))
        crossed[micro * channels : (micro + 1) * channels] = dot_lanes(
            jnp.concatenate([acts[micro, row] for row in range(rows)], axis=1),
            jnp.concatenate([slopes[micro, row] for row in range(rows)], axis=1),
        )
    plain[...] = jnp.concatenate(lines, axis=0)
    used = micros * channels
    if crossed.shape[0] > used:
        crossed[used:] = jnp.zeros((crossed.shape[0] - used, LANES), F32)
    if 2 * micros + each < send.shape[1]:
        send[...] = jnp.zeros(send.shape, F32)
    for peer in range(peers):
        send[peer, 2 * micros : 2 * micros + each] = crossed[peer * each : (peer + 1) * each]
    own_stats(upper, 0, rows, send)


def exact_rows(rows):
    high = rows.astype(BF16).astype(F32)
    return [high, rows - high]


def top_kernel(found, cols, upper, cot, slopes, plain, w_up_t, features, grads, mixed, stats, send, *, rows, each):
    micros, _, wide, width = upper.shape
    channels = w_up_t.shape[0]
    lines = []
    for micro in range(micros):
        lines += list(pooled_stats(found[:, micro, :], found[:, micros + micro, :], float(rows * width)))
    turned = columns_of(lines)
    stats[...] = turned
    gain, shift = cols[:, 6:7], cols[:, 7:8]
    gain_rows, shift_rows, mixed_rows = [], [], []
    for micro in range(micros):
        centre, rstd = turned[:, 2 * micro : 2 * micro + 1], turned[:, 2 * micro + 1 : 2 * micro + 2]
        factor = gain * rstd
        gain_sum = jnp.zeros((wide, LANES), F32)
        shift_sum = jnp.zeros((wide, LANES), F32)
        mixed_sum = jnp.zeros((2 * channels, LANES), F32)
        for row in range(rows):
            unit = (upper[micro, row] - centre) * rstd
            normed = unit * gain + shift
            gate = sigmoid(normed)
            act = normed * gate
            grad = cot[micro, row].astype(F32) * (gate + act * (1.0 - gate))
            features[micro, row] = act.astype(BF16)
            grads[micro, row] = grad
            gain_sum = gain_sum + fold(grad * unit)
            shift_sum = shift_sum + fold(grad)
            below = dot(w_up_t[...], (grad * factor).astype(BF16))
            mixed_sum = mixed_sum + fold(
                slopes[micro, row].astype(F32) * jnp.concatenate([below, below], axis=0)
            )
        gain_rows.append(row_of(gain_sum))
        shift_rows.append(row_of(shift_sum))
        mixed_rows.append(row_of(mixed_sum))
    mixed[...] = jnp.concatenate(mixed_rows, axis=0)
    rows_out = jnp.concatenate(gain_rows + shift_rows + mixed_rows + [plain[...]], axis=0)
    crossed = jnp.sum(found[:, 2 * micros : 2 * micros + each, :], axis=0)
    rest = send.shape[1] - 2 * rows_out.shape[0] - each
    block = jnp.concatenate(exact_rows(rows_out) + [crossed, jnp.zeros((rest, LANES), F32)], axis=0)
    send[...] = jnp.broadcast_to(block.astype(BF16)[None], send.shape)


def low_rows(turned, value_of, values, stats, gain, low, high, first, rows, tiles):
    micros, _, channels, width = values.shape
    tile = lax.axis_index("tile")
    masks = edges(channels, width)
    for micro in range(micros):
        part = slice(micro * channels, (micro + 1) * channels)
        centre, rstd = stats[part, 0:1], stats[part, 1:2]
        factor = gain * rstd
        slope_part, shift_part = rstd * turned[part, 0:1], turned[part, 1:2]
        for index in range(high):
            grad, value = value_of(micro, index)
            grad = factor * (grad - shift_part - (value - centre) * slope_part)
            if index + first < 0 or index + first >= rows:
                grad = grad * inside(tile, index + first, (tiles, rows))
            low[micro, index] = spread(grad.astype(BF16), masks)


def first_slopes(first_out, stats, cols, micro, channels):
    part = slice(micro * channels, (micro + 1) * channels)
    centre, rstd = stats[part, 0:1], stats[part, 1:2]
    gain, shift = cols[0:channels, 2:3], cols[0:channels, 3:4]

    def at(row):
        unit = (first_out[micro, row] - centre) * rstd
        normed = unit * gain + shift
        gate = sigmoid(normed)
        return gate + normed * gate * (1.0 - gate), unit

    return at


def second_sums(total, weight, factors, stats, micro, micros, count):
    channels = weight.shape[1]
    factor, centre = factors[micro], stats[:, 2 * micro : 2 * micro + 1]
    columns = jnp.transpose(total)
    beta = factor * stats[:, 2 * micro + 1 : 2 * micro + 2] * columns[:, micro : micro + 1] * (1.0 / count)
    alpha = factor * columns[:, micros + micro : micros + micro + 1] * (1.0 / count)
    square = lax.dot_general(
        weight * beta, weight, (((0,), (0,)), ((), ())),
        preferred_element_type=F32, precision=lax.Precision.HIGHEST,
    )
    square = jnp.concatenate([square, square], axis=1)
    line = jnp.sum(weight * (alpha - beta * centre), axis=0, keepdims=True)
    line = jnp.concatenate([line, line], axis=1)

    def give(mixed, plain, crossed):
        mine = crossed[micro * channels : (micro + 1) * channels]
        return mixed - plain * line - jnp.sum(square * mine, axis=0, keepdims=True)

    return give


def middle_back_kernel(
    found, cols, grads, upper, top_stats, second_out, second_stats, w_up, w_up_t, second_act,
    first_out, first_stats, b_second_in, acts, own_mixed, own_plain, own_crossed,
    out, top_grad, weight_grad, rising, falling,
    top_gain_grad, top_shift_grad, expected, send, low, top_low, second_dz, b_second, sems, *, rows, tiles, each
):
    weight_copy = move(b_second_in, b_second, sems, 0)
    scene = lax.axis_index("scene")
    tile = lax.axis_index("tile")
    micros, _, wide, width = grads.shape
    channels = second_out.shape[2]
    peers = found.shape[0]
    count = float(peers * rows * width)
    kept = 4 * micros
    total = jnp.sum(found[:, 0 : 2 * kept, :].astype(F32), axis=0)
    total = total[0:kept] + total[kept : 2 * kept]
    crossed = jnp.concatenate(
        [
            found[peer].astype(F32)[2 * kept : 2 * kept + each]
            for peer in range(-(-micros * channels // each))
        ],
        axis=0,
    )
    own_half(total[0:1] + total[1:2], scene, top_gain_grad)
    own_half(total[2:3] + total[3:4], scene, top_shift_grad)
    factors = [cols[:, 6:7] * top_stats[:, 2 * micro + 1 : 2 * micro + 2] for micro in range(micros)]
    wide_weight = w_up[...].astype(F32)
    mixed, plain = total[2 * micros : 3 * micros], total[3 * micros : 4 * micros]
    turned = columns_of([total[index : index + 1] for index in range(2 * micros)]) * (1.0 / count)
    gain, shift = cols[0:channels, 4:5], cols[0:channels, 5:6]
    masks = edges(channels, width)
    extra_rows = []
    for micro in range(micros):
        top_centre = top_stats[:, 2 * micro : 2 * micro + 1]
        top_slope = top_stats[:, 2 * micro + 1 : 2 * micro + 2] * turned[:, micro : micro + 1]
        top_shift = turned[:, micros + micro : micros + micro + 1]
        part = slice(micro * channels, (micro + 1) * channels)
        centre, rstd = second_stats[part, 0:1], second_stats[part, 1:2]
        gain_sum = jnp.zeros((channels, LANES), F32)
        shift_sum = jnp.zeros((channels, LANES), F32)
        for row in range(rows):
            grad = factors[micro] * (
                grads[micro, row] - top_shift - (upper[micro, row] - top_centre) * top_slope
            )
            grad = grad.astype(BF16)
            top_low[micro, row] = grad
            unit = (second_out[micro, row] - centre) * rstd
            normed = unit * gain + shift
            gate = sigmoid(normed)
            grad = dot(w_up_t[...], grad) * (gate + normed * gate * (1.0 - gate))
            second_dz[micro, row] = grad
            shift_sum = shift_sum + fold(grad)
            gain_sum = gain_sum + fold(grad * unit)
        give = second_sums(total, wide_weight, factors, top_stats, micro, micros, count)
        whole = give(mixed[micro : micro + 1], plain[micro : micro + 1], crossed)
        extra = row_of(shift_sum, gain_sum) - give(
            own_mixed[micro : micro + 1], own_plain[micro : micro + 1], own_crossed[...]
        )
        expected[micro : micro + 1] = whole
        extra_rows.append(extra)
        part = columns_of([whole * (1.0 / count) + extra * (1.0 / (rows * width))])
        shift_part, gain_part = part[0:channels, 0:1], part[channels : 2 * channels, 0:1]
        for row in range(rows):
            unit = (second_out[micro, row] - centre) * rstd
            grad = (gain * rstd) * (second_dz[micro, row] - shift_part - unit * gain_part)
            low[micro, row] = spread(grad.astype(BF16), masks)
        product = dot_lanes(
            jnp.concatenate([top_low[micro, row] for row in range(rows)], axis=1),
            jnp.concatenate([second_act[micro, row] for row in range(rows)], axis=1),
        )
        top_grad[...] = product if micro == 0 else top_grad[...] + product
    for micro in range(micros):
        for row in range(2):
            falling[micro, row] = low[micro, row, channels : 2 * channels]
            rising[micro, row] = low[micro, rows - 2 + row, channels : 2 * channels]
    conv_grad(low, 0, acts, 0, weight_grad, rows)
    weight_copy.wait()
    half = 6 * channels
    gain_sums, shift_sums = [], []
    for micro in range(micros):
        slopes = first_slopes(first_out, first_stats, cols, micro, channels)
        gain_sum = jnp.zeros((channels, LANES), F32)
        shift_sum = jnp.zeros((channels, LANES), F32)
        for at in range(0, rows + 2, 2):
            if at == 0:
                parts = dot(b_second[:, half:], low[micro, 0:2].reshape(half, width))
            elif at == rows:
                parts = dot(b_second[:, :half], low[micro, rows - 2 : rows].reshape(half, width))
            else:
                parts = conv_pair(low, b_second, micro, at - 2, channels)
            for j in range(2):
                slope, unit = slopes(at + j)
                grad = parts[channels * j : channels * (j + 1)] * slope
                if at + j == 0 or at + j == rows + 1:
                    grad = grad * inside(tile, at + j - 1, (tiles, rows))
                out[micro, at + j] = grad
                gain_sum = gain_sum + fold(grad * unit)
                shift_sum = shift_sum + fold(grad)
        gain_sums.append(gain_sum)
        shift_sums.append(shift_sum)
    send_all(send, [row_of(*gain_sums), row_of(*shift_sums)] + extra_rows)


def conv_grad(low, low_first, values, value_first, total, rows):
    micros, _, channels, width = values.shape
    for micro in range(micros):
        grads = jnp.concatenate([low[micro, row + low_first] for row in range(rows)], axis=1)
        windows = jnp.concatenate(
            [
                values[micro, row + value_first : row + value_first + 3].reshape(3 * channels, width)
                for row in range(rows)
            ],
            axis=1,
        )
        product = dot_lanes(grads, windows)
        total[...] = product if micro == 0 else total[...] + product


def half_rows(total, half, scene):
    channels = 2 * half
    start = scene * half
    mine = jnp.concatenate(
        [total[b * channels + start : b * channels + start + half, :] for b in range(2, -1, -1)], axis=0
    )
    wing = mine[:, LANES:]
    cut = wing.shape[0] // 2
    return [mine[:, :LANES], jnp.concatenate([wing[:cut], wing[cut:]], axis=1)]


def pick_kernel(
    found, cols, grads, before, after, first_out, first_stats, b_first_in, b_second_in, columns, where_rows,
    canvas, second_grad, top_grad, expected,
    send, gain_grad, shift_grad, second_gain_grad, second_shift_grad, low, grid, b_first, b_second, halo, first_grad, whole, sems,
    *, rows, tiles, each
):
    second_copy = move(b_second_in, b_second, sems, 1)
    weight_copy = move(b_first_in, b_first, sems, 0)
    scene = lax.axis_index("scene")
    micros, _, channels, width = grads.shape
    sums = sum_rows(found, 2 + micros)
    second = sum(sums[2:]) + jnp.sum(expected[...], axis=0, keepdims=True)
    own_half(second[:, :channels], scene, second_shift_grad)
    own_half(second[:, channels:], scene, second_gain_grad)
    sums = sums[:2]
    own_half(sums[0][:, :channels] + sums[0][:, channels:], scene, gain_grad)
    own_half(sums[1][:, :channels] + sums[1][:, channels:], scene, shift_grad)
    turned = columns_of(sums) * (1.0 / (found.shape[0] * rows * width))
    masks = edges(channels, width)
    half = 6 * channels
    second_copy.wait()
    for micro in range(micros):
        slopes = first_slopes(first_out, first_stats, cols, micro, channels)
        for at, ref, columns_used in ((0, before, slice(0, half)), (rows, after, slice(half, 2 * half))):
            window = jnp.concatenate([spread(ref[micro, row], masks) for row in range(2)], axis=0)
            parts = dot(b_second[:, columns_used], window)
            for j in range(2):
                slope, _ = slopes(at + j)
                halo[micro, at + j] = parts[channels * j : channels * (j + 1)] * slope

    def value_of(micro, index):
        grad = grads[micro, index]
        if index < 2 or index >= rows:
            grad = grad + halo[micro, index]
        return grad, first_out[micro, index]

    low_rows(turned, value_of, first_out, first_stats, cols[0:channels, 2:3], low, rows + 2, -1, rows, tiles)
    weight_copy.wait()
    conv_rows(low, b_first, grid, grid.shape)
    conv_grad(low, 1, canvas, 0, first_grad, rows)
    half = channels // 2
    peers, block = send.shape[:2]
    for s in range(2):
        parts = half_rows(first_grad, half, s) + half_rows(second_grad, half, s)
        mine = top_grad[s * channels : (s + 1) * channels, :]
        parts.append(jnp.concatenate([mine[:half], mine[half:]], axis=1))
        parts = jnp.concatenate(parts, axis=0)
        whole[s, 0 : parts.shape[0]] = parts
        if whole.shape[1] > parts.shape[0]:
            whole[s, parts.shape[0] :] = jnp.zeros((whole.shape[1] - parts.shape[0], LANES), F32)
    slots = columns.shape[0]
    lane = lax.broadcasted_iota(jnp.int32, (slots, width), 1).astype(F32)
    picked = []
    for micro in range(micros):
        at = 2 + micro
        column = columns[:, at : at + 1] - 1.0
        column = column - jnp.floor(column * (1.0 / width)) * width
        place = jnp.floor((where_rows[at : at + 1] - 1.0) * (1.0 / width))
        chosen = jnp.where(lane == column, 1.0, 0.0).astype(BF16)
        here = dot_lanes(grid[micro].reshape(rows * channels, width), chosen)
        total = jnp.zeros((channels, slots), F32)
        for r in range(rows):
            total = total + jnp.where(place == r * 1.0, here[r * channels : (r + 1) * channels], 0.0)
        picked.append(total)
    picked = jnp.transpose(jnp.concatenate(picked, axis=0))
    capacity = slots // tiles
    rest = block - capacity - 2 * each
    for peer in range(peers):
        spot = peer // 2
        parts = [picked[spot * capacity : (spot + 1) * capacity]]
        parts += [whole[s, peer * each : (peer + 1) * each] for s in range(2)]
        parts.append(jnp.zeros((rest, LANES), F32))
        send[peer] = jnp.concatenate(parts, axis=0).astype(BF16)


def pillar_back_kernel(found, rows_in, w_pillar, cols, pooled, send, grads, lifted, rows, sems,
                       *, capacity, each):
    fetched = move(rows_in, rows, sems, 0)
    micros = rows.shape[0]
    _, channels, pillars = pooled.shape
    stats = pooled.at[micros : 2 * micros]
    inputs = w_pillar.shape[1]
    depth = rows.shape[2] // pillars
    scene = lax.axis_index("scene")
    peers = found.shape[0]
    slot_count = peers // 2 * capacity
    returned = jnp.concatenate(
        [found[2 * t + scene].astype(F32)[0:capacity] for t in range(peers // 2)], axis=0
    )
    turned = jnp.transpose(returned)
    place = lax.broadcasted_iota(jnp.int32, (slot_count, pillars), 0).astype(F32)
    gain, shift = cols[0:channels, 0:1], cols[0:channels, 1:2]
    gain_sums, shift_sums = [], []
    outer = jnp.zeros((16, channels), F32)
    fetched.wait()
    for micro in range(micros):
        lifted[...] = dot(w_pillar[...], rows[micro, 0:inputs])
        slot, limit = pillar_notes(rows, micro, inputs, pillars)
        chosen = jnp.where(place == slot, 1.0, 0.0).astype(BF16)
        back = dot(turned[micro * channels : (micro + 1) * channels].astype(BF16), chosen)
        centre, rstd = stats[micro, :, 0:1], stats[micro, :, 1:2]
        pool = pooled[micro]
        gain_sum = jnp.zeros((channels, pillars), F32)
        shift_sum = jnp.zeros((channels, pillars), F32)
        for n in range(depth):
            piece = slice(n * pillars, (n + 1) * pillars)
            unit = (lifted[:, piece] - centre) * rstd
            normed = unit * gain + shift
            gate = sigmoid(normed)
            act = normed * gate
            slope = gate + act * (1.0 - gate)
            grad = jnp.where(limit > n, back * jnp.exp(act - pool) * slope, 0.0)
            grads[micro, :, piece] = grad
            gain_sum = gain_sum + grad * unit
            shift_sum = shift_sum + grad
        gain_sums.append(gain_sum)
        shift_sums.append(shift_sum)
        scale = jnp.transpose(jnp.broadcast_to(rstd * gain, (channels, LANES)))[0:1]
        outer = outer + dot_lanes(rows[micro], grads[micro].astype(BF16)) * scale
    lines = [row_of(*gain_sums), row_of(*shift_sums)]
    for k in range(0, 10, 2):
        lines.append(jnp.concatenate([outer[k : k + 1], outer[k + 1 : k + 2]], axis=1))
    exact = jnp.concatenate(lines, axis=0)
    kept = 2 * exact.shape[0]
    weights = jnp.sum(found[...].astype(F32), axis=0)
    rest = send.shape[2] - kept - each
    for s in range(2):
        mine = weights[capacity + s * each : capacity + (s + 1) * each]
        block = exact_rows(exact) + [mine] + ([jnp.zeros((rest, LANES), F32)] if rest > 0 else [])
        block = jnp.concatenate(block, axis=0).astype(BF16)
        send[:, s] = jnp.broadcast_to(block[None], (send.shape[0],) + block.shape)


def points_kernel(
    found, rows_in, grads, w_pillar, cols, pooled,
    points_grad, pillar_grad, gain_grad, shift_grad, first_grad, second_grad, up_grad, rows, lifted, sems,
    *, each
):
    fetched = move(rows_in, rows, sems, 0)
    scene = lax.axis_index("scene")
    micros, channels, _ = grads.shape
    stats = pooled.at[micros : 2 * micros]
    _, _, inputs, depth, pillars = points_grad.shape
    half = channels // 2
    kept = 7
    total = jnp.sum(found[...].astype(F32), axis=0)
    total = total[0:kept] + total[kept : 2 * kept]
    own_half(total[0:1, :channels] + total[0:1, channels:], scene, gain_grad)
    own_half(total[1:2, :channels] + total[1:2, channels:], scene, shift_grad)
    turned = jnp.transpose(jnp.concatenate([total, jnp.zeros((1, LANES), F32)], axis=0))
    weight_grad = jnp.concatenate(
        [turned[(k % 2) * channels : (k % 2 + 1) * channels, 2 + k // 2 : 3 + k // 2] for k in range(inputs)],
        axis=1,
    )
    weight = jnp.transpose(w_pillar[...].astype(F32)).astype(BF16)
    fetched.wait()
    for micro in range(micros):
        lifted[...] = dot(w_pillar[...], rows[micro, 0:inputs])
        part = slice(micro * channels, (micro + 1) * channels)
        centre, rstd, inverse = stats[micro, :, 0:1], stats[micro, :, 1:2], stats[micro, :, 2:3]
        factor = cols[0:channels, 0:1] * rstd
        gain_part, shift_part = turned[part, 0:1], turned[part, 1:2]
        spun, mean = stats[micro, :, 16 : 16 + inputs], stats[micro, :, 32 : 32 + inputs]
        weight_grad = weight_grad - factor * (shift_part * mean + gain_part * rstd * spun)
        gain_part, shift_part = gain_part * inverse * rstd, shift_part * inverse
        _, limit = pillar_notes(rows, micro, inputs, pillars)
        for n in range(depth):
            piece = slice(n * pillars, (n + 1) * pillars)
            low = factor * (grads[micro, :, piece] - shift_part - (lifted[:, piece] - centre) * gain_part)
            low = jnp.where(limit > n, low, 0.0).astype(BF16)
            points_grad[micro, 0, :, n, :] = dot(weight, low)
    weight_grad = jnp.concatenate([weight_grad, jnp.zeros((channels, LANES - inputs), F32)], axis=1)
    weight_grad = jnp.transpose(weight_grad)[0:inputs]
    pillar_grad[...] = jnp.where(scene == 0, weight_grad[:, :half], weight_grad[:, half:])
    whole = jnp.concatenate(
        [found[peer].astype(F32)[2 * kept : 2 * kept + each] for peer in range(found.shape[0])], axis=0
    )
    for index, out in enumerate((first_grad, second_grad)):
        base = index * 9 * half * channels // LANES
        lead = 3 * half
        mine = whole[base : base + lead]
        wing = whole[base + lead : base + lead + lead // 2]
        wing = jnp.concatenate([wing[:, :channels], wing[:, channels:]], axis=0)
        both = jnp.concatenate([mine, wing], axis=1)
        for a in range(3):
            for b in range(3):
                at = (3 * a + b) * channels
                out[:, at : at + channels] = both[b * half : (b + 1) * half, a * channels : (a + 1) * channels]
    base = 2 * 9 * half * channels // LANES
    top = whole[base : base + half]
    up_grad[...] = jnp.concatenate([top[:, :channels], top[:, channels:]], axis=0)


def swap(blocks, axes):
    return lax.all_to_all(blocks, axes, split_axis=0, concat_axis=0)


def shards(
    points, point_counts, pillar_tile, pillar_cell,
    pillar_weight, pillar_gain, pillar_shift,
    first_weight, first_gain, first_shift,
    second_weight, second_gain, second_shift,
    up_weight, up_gain, up_shift, cotangent,
):
    micros, _, inputs, depth, pillars = points.shape
    channels = up_weight.shape[1]
    upper = cotangent.shape[2]
    rows, width = cotangent.shape[3:]
    tiles = lax.axis_size("tile")
    scenes = lax.axis_size("scene")
    peers = tiles * scenes
    capacity = 2 * pillars // tiles
    slot_count = tiles * capacity
    half = channels // 2

    def vmem(shape, dtype):
        return pltpu.VMEM(shape, dtype)

    def grid(high, dtype=F32, lead=channels):
        return ((micros, high, lead, width), dtype)

    sums = ((peers, 2, LANES), F32)
    sources = (
        pillar_tile, pillar_cell, point_counts, points,
        first_weight, second_weight, up_weight, pillar_weight.T,
        pillar_gain, pillar_shift, first_gain, first_shift, second_gain, second_shift, up_gain, up_shift,
    )
    moments, packed, point_rows = run(
        functools.partial(moments_kernel, capacity=capacity),
        [
            ((tiles, scenes, 4, LANES), F32), ((layout(half, channels)[-1] + 16, LANES), BF16),
            ((micros, 16, depth * pillars), BF16),
        ],
        *sources,
        hbm=range(len(sources)), copies=len(sources), limit=WIDE_LIMIT,
        scratch=[vmem(source.shape, source.dtype) for source in sources]
        + [vmem((inputs * depth, pillars), F32)],
    )
    moments = swap(moments.reshape(peers, 4, LANES), BOTH)
    both = lax.all_gather(packed, "scene")
    taps = ((2 * channels, 12 * channels), BF16)
    w_pillar, cols, l_first, l_second, b_first, b_second, w_up, w_up_t = run(
        functools.partial(unpack_kernel, inputs=inputs),
        [
            ((channels, inputs), BF16), ((LANES, 8), F32), taps, taps + (1,), taps + (1,), taps + (1,),
            ((upper, channels), BF16), ((channels, upper), BF16),
        ],
        both,
        scratch=[vmem(*taps), vmem(*taps), vmem(*taps)], copies=3,
    )
    cot = cotangent[:, 0].transpose(0, 2, 1, 3)

    send, pooled = run(
        functools.partial(pillar_kernel, capacity=capacity),
        [((slot_count, 3 * LANES), BF16), ((2 * micros, channels, pillars), F32)],
        moments, point_rows, w_pillar, cols,
        scratch=[vmem((channels, depth * pillars), F32), vmem((channels, depth * pillars), F32)],
    )
    arrived = swap(send.reshape(tiles, capacity, 3 * LANES), "tile").reshape(slot_count, 3 * LANES)
    cell_columns, cell_rows = run(
        functools.partial(cells_kernel, capacity=capacity),
        [((slot_count, LANES), F32), ((8, slot_count), F32)],
        moments,
        cost=pl.CostEstimate(flops=10**7, bytes_accessed=10**6, transcendentals=0),
    )
    arrived, cot = lax.optimization_barrier((arrived, cot))

    first_out, canvas, send = run(
        functools.partial(canvas_kernel, rows=rows),
        [grid(rows + 2), grid(rows + 2, BF16), sums],
        arrived, cell_columns, cell_rows, l_first,
        scratch=[vmem(*grid(rows + 4, BF16, 3 * channels))],
    )
    second_out, first_act, first_stats, send = run(
        functools.partial(second_kernel, rows=rows, tiles=tiles),
        [grid(rows), grid(rows + 2, BF16), ((LANES, 8), F32), sums],
        swap(send, BOTH), cols, first_out, l_second,
        hbm=(3,), scratch=[vmem(*grid(rows + 2, BF16, 3 * channels)), vmem(*taps)], copies=1,
    )
    part = -(-micros * channels // peers)
    second_act, up_out, slopes, plain, crossed, second_stats, send = run(
        functools.partial(up_kernel, rows=rows),
        [
            grid(rows, BF16), grid(rows, F32, upper), grid(rows, BF16, 2 * channels), ((micros, LANES), F32),
            ((peers * part, LANES), F32), ((LANES, 8), F32), ((peers, -(-(2 * micros + part) // 8) * 8, LANES), F32),
        ],
        swap(send, BOTH), cols, second_out, w_up,
    )
    features, grads, mixed, top_stats, send = run(
        functools.partial(top_kernel, rows=rows, each=part),
        [
            grid(rows, BF16, upper), grid(rows, F32, upper), ((micros, LANES), F32), ((LANES, 8), F32),
            ((peers, -(-(8 * micros + part) // 8) * 8, LANES), BF16),
        ],
        swap(send, BOTH), cols, up_out, cot, slopes, plain, w_up_t,
    )
    features, send = lax.optimization_barrier((features.transpose(0, 2, 1, 3)[:, None], send))
    edge = ((micros, 2, channels, width), BF16)
    vector, top_vector, matrix = ((half,), F32), ((upper // 2,), F32), ((half, 9 * channels), F32)
    rising = [(i, i + 1) for i in range(tiles - 1)]
    falling = [(j, i) for i, j in rising]
    cross = ((3 * channels, 3 * channels), F32)
    (
        first_dz, top_grad, second_cross, rising_edge, falling_edge,
        up_gain_grad, up_shift_grad, expected, send,
    ) = run(
        functools.partial(middle_back_kernel, rows=rows, tiles=tiles, each=part),
        [
            grid(rows + 2), ((upper, channels), F32), cross, edge, edge,
            top_vector, top_vector, ((micros, LANES), F32), ((peers, 2 + micros, LANES), F32),
        ],
        swap(send, BOTH), cols, grads, up_out, top_stats, second_out, second_stats, w_up, w_up_t, second_act,
        first_out, first_stats, b_second, first_act, mixed, plain, crossed,
        hbm=(12,),
        scratch=[
            vmem(*grid(rows, BF16, 3 * channels)), vmem(*grid(rows, BF16, upper)), vmem(*grid(rows)), vmem(*taps),
        ],
        copies=1,
    )
    length = (2 * 9 * half * channels + upper * half) // LANES
    each = -(-length // peers)
    block = -(-(capacity + 2 * each) // 8) * 8
    send, first_gain_grad, first_shift_grad, second_gain_grad, second_shift_grad = run(
        functools.partial(pick_kernel, rows=rows, tiles=tiles, each=each),
        [((peers, block, LANES), BF16), vector, vector, vector, vector],
        swap(send, BOTH), cols, first_dz,
        lax.ppermute(rising_edge, "tile", rising), lax.ppermute(falling_edge, "tile", falling),
        first_out, first_stats, b_first, b_second, cell_columns, cell_rows, canvas, second_cross, top_grad, expected,
        hbm=(7, 8),
        scratch=[
            vmem(*grid(rows + 2, BF16, 3 * channels)), vmem(*grid(rows, BF16)), vmem(*taps), vmem(*taps),
            vmem(*grid(rows + 2)), vmem(*cross), vmem((scenes, peers * each, LANES), F32),
        ],
        copies=2,
    )
    block = -(-(14 + each) // 8) * 8
    send, pillar_dz = run(
        functools.partial(pillar_back_kernel, capacity=capacity, each=each),
        [((tiles, scenes, block, LANES), BF16), ((micros, channels, depth * pillars), F32)],
        swap(send, BOTH), point_rows, w_pillar, cols, pooled,
        hbm=(1,),
        scratch=[vmem((channels, depth * pillars), F32), vmem((micros, 16, depth * pillars), BF16)],
        copies=1,
    )
    points_grad, pillar_grad, pillar_gain_grad, pillar_shift_grad, first_grad, second_grad, up_grad = run(
        functools.partial(points_kernel, each=each),
        [
            ((micros, 1, inputs, depth, pillars), F32), ((inputs, half), F32), vector, vector,
            matrix, matrix, ((upper // 2, channels), F32),
        ],
        swap(send.reshape(peers, block, LANES), BOTH), point_rows, pillar_dz, w_pillar, cols, pooled,
        hbm=(1,),
        scratch=[vmem((micros, 16, depth * pillars), BF16), vmem((channels, depth * pillars), F32)],
        copies=1,
    )
    return (
        features, points_grad,
        pillar_grad.T, pillar_gain_grad, pillar_shift_grad,
        first_grad, first_gain_grad, first_shift_grad,
        second_grad, second_gain_grad, second_shift_grad,
        up_grad, up_gain_grad, up_shift_grad,
    )


def solution(mesh):
    matrix, vector = P("scene", None), P("scene")
    grid = P(None, "scene", None, "tile", None)
    cloud = P(None, "scene", None, None, "tile")
    pillar = P(None, "scene", "tile")
    weights = (matrix, vector, vector) * 4
    return jax.shard_map(
        shards,
        mesh=mesh,
        in_specs=(cloud, pillar, pillar, pillar) + weights + (grid,),
        out_specs=(grid, cloud) + weights,
        check_vma=False,
    )
```

```python
import functools

import jax
import jax.numpy as jnp
from jax import lax
from jax.experimental import pallas as pl
from jax.experimental.layout import Layout, with_layout_constraint
from jax.experimental.pallas import tpu as pltpu
from jax.sharding import PartitionSpec as P

norm_eps = 0.001
BOTH = ("tile", "scene")
F32 = jnp.float32
BF16 = jnp.bfloat16
VMEM_LIMIT = 24 * 1024 * 1024
WIDE_LIMIT = 60 * 1024 * 1024
LANES = 128


def run(kernel, outs, *args, hbm=(), scratch=(), copies=0, cost=None, limit=VMEM_LIMIT):
    specs = [
        pl.BlockSpec(memory_space=pltpu.HBM if index in hbm else pltpu.VMEM) for index in range(len(args))
    ]
    scratch = list(scratch)
    if copies:
        scratch.append(pltpu.SemaphoreType.DMA((copies,)))
    return pl.pallas_call(
        kernel,
        out_shape=[jax.ShapeDtypeStruct(out[0], out[1]) for out in outs],
        in_specs=specs,
        out_specs=[
            pl.BlockSpec(memory_space=pltpu.HBM if len(out) > 2 else pltpu.VMEM) for out in outs
        ],
        scratch_shapes=scratch,
        compiler_params=pltpu.CompilerParams(vmem_limit_bytes=limit),
        cost_estimate=cost,
    )(*args)


def move(source, target, sems, index):
    copy = pltpu.make_async_copy(source, target, sems.at[index])
    copy.start()
    return copy


def dot(left, right, precision=None):
    return jnp.dot(left, right, preferred_element_type=F32, precision=precision)


def dot_lanes(left, right, precision=None):
    return lax.dot_general(
        left, right, (((1,), (1,)), ((), ())), preferred_element_type=F32, precision=precision
    )


def sigmoid(values):
    return 0.5 + 0.5 * jnp.tanh(0.5 * values)


def fold(values):
    total = values[:, :LANES]
    for start in range(LANES, values.shape[1], LANES):
        total = total + values[:, start : start + LANES]
    return total


def row_of(left, right=None):
    both = left if right is None else jnp.concatenate([left, right], axis=0)
    return jnp.sum(jnp.transpose(both), axis=0, keepdims=True)


def columns_of(rows):
    rows = rows + [jnp.zeros((8 - len(rows), LANES), F32)] if len(rows) < 8 else rows
    return jnp.transpose(jnp.concatenate(rows, axis=0))


def inside(tile, row, height):
    tiles, rows = height
    place = tile * rows + row
    return jnp.where((place >= 0) & (place < tiles * rows), 1.0, 0.0).astype(F32)


def send_all(ref, rows):
    for index, row in enumerate(rows):
        ref[:, index : index + 1, :] = jnp.broadcast_to(row[None], (ref.shape[0], 1, LANES))


def pooled_stats(means, squares, count):
    peers = means.shape[0]
    mean = jnp.sum(means, axis=0, keepdims=True) * (1.0 / peers)
    away = means - mean
    spread = jnp.sum(squares + count * away * away, axis=0, keepdims=True) * (1.0 / (peers * count))
    return mean, lax.rsqrt(spread + norm_eps)


def stat_columns(found, count):
    return columns_of(list(pooled_stats(found[:, 0, :], found[:, 1, :], count)))


def sum_rows(found, lines):
    return [jnp.sum(found[:, index, :], axis=0, keepdims=True) for index in range(lines)]


def own_half(row, scene, out):
    size = out.shape[0]
    out[...] = jnp.where(scene == 0, row[:, 0:size], row[:, size : 2 * size]).reshape(size)


def edges(channels, width):
    lane = lax.broadcasted_iota(jnp.int32, (channels, width), 1)
    return lane > 0, lane < width - 1


def spread(row, masks):
    zero = jnp.zeros_like(row)
    left = jnp.where(masks[0], pltpu.roll(row, 1, 1), zero)
    right = jnp.where(masks[1], pltpu.roll(row, row.shape[1] - 1, 1), zero)
    return jnp.concatenate([left, row, right], axis=0)


def layout(half, channels):
    first = 0
    second = first + half * -(-9 * channels // LANES)
    up = second + half * -(-9 * channels // LANES)
    vectors = up + channels
    return first, second, up, vectors, vectors + 16


def widen(value):
    missing = LANES - value.shape[1]
    if missing == 0:
        return value
    return jnp.concatenate([value, jnp.zeros((value.shape[0], missing), value.dtype)], axis=1)


def pack(held, out):
    first, second, up, pillar = held[:4]
    half, channels = first.shape[0], up.shape[1]
    starts = layout(half, channels)
    for ref, start in ((first, starts[0]), (second, starts[1])):
        for j in range(-(-9 * channels // LANES)):
            out[start + j * half : start + (j + 1) * half, :] = widen(
                ref[:, j * LANES : min((j + 1) * LANES, 9 * channels)]
            )
    out[starts[2] : starts[2] + channels, :] = widen(up[...])
    rows = [vector[...].astype(F32).reshape(1, -1) for vector in held[4:]]
    rows = [widen(row) for row in rows] + [jnp.zeros((16 - len(rows), LANES), F32)]
    turned = widen(pillar[...].astype(F32))
    rows += [turned, jnp.zeros((16 - turned.shape[0], LANES), F32)]
    out[starts[3] :, :] = jnp.concatenate(rows, axis=0).astype(BF16)


def unpack_kernel(
    both, w_pillar, cols, l_first, l_second, b_first, b_second, w_up, w_up_t,
    h_second, h_first_back, h_second_back, sems, *, inputs
):
    half = w_pillar.shape[0] // 2
    channels = 2 * half
    starts = layout(half, channels)
    tiles = -(-9 * channels // LANES)

    def wide(start):
        return jnp.concatenate(
            [
                jnp.concatenate(
                    [both[s, start + j * half : start + (j + 1) * half, :] for j in range(tiles)], axis=1
                )
                for s in range(2)
            ],
            axis=0,
        ).astype(F32)

    up = jnp.concatenate(
        [both[s, starts[2] : starts[2] + channels, 0:channels] for s in range(2)], axis=0
    )
    w_up[...] = up
    w_up_t[...] = jnp.transpose(up.astype(F32)).astype(BF16)
    turned = jnp.concatenate(
        [both[s, starts[4] : starts[4] + 16, 0:half].astype(F32) for s in range(2)], axis=1
    )
    w_pillar[...] = jnp.transpose(widen(turned))[0:channels, 0:inputs].astype(BF16)
    vectors = [both[s, starts[3] : starts[3] + 16, :].astype(F32) for s in range(2)]
    rows = []
    for index in range(8):
        size = half if index < 6 else channels
        row = jnp.concatenate([vectors[s][index : index + 1, 0:size] for s in range(2)], axis=1)
        rows.append(jnp.concatenate([row] * (LANES // (2 * size)), axis=1))
    cols[...] = columns_of(rows)
    zero = jnp.zeros((channels, 3 * channels), F32)
    copies = []
    for weight, ahead, back in (
        (wide(starts[0]), l_first, h_first_back), (wide(starts[1]), h_second, h_second_back)
    ):
        weight = weight[:, : 9 * channels]
        turned = jnp.transpose(weight)
        flipped = jnp.concatenate(
            [turned[tap * channels : (tap + 1) * channels] for tap in range(8, -1, -1)], axis=1
        )
        for ref, taps in ((ahead, weight), (back, flipped)):
            ref[0:channels, :] = jnp.concatenate([taps, zero], axis=1).astype(BF16)
            ref[channels : 2 * channels, :] = jnp.concatenate([zero, taps], axis=1).astype(BF16)
    copies.append(move(h_second, l_second, sems, 0))
    copies.append(move(h_first_back, b_first, sems, 1))
    copies.append(move(h_second_back, b_second, sems, 2))
    for copy in copies:
        copy.wait()


def slot_line(wide, depth, inputs):
    return jnp.concatenate([wide[pl.ds(n, inputs, stride=depth), :] for n in range(depth)], axis=1)


def slot_mask(count, depth):
    return jnp.concatenate([jnp.where(count > n, 1.0, 0.0) for n in range(depth)], axis=1)


def ranks(tile):
    pillars = tile.shape[1]
    across = jnp.broadcast_to(tile, (pillars, pillars))
    down = jnp.transpose(across)
    row = lax.broadcasted_iota(jnp.int32, (pillars, pillars), 0)
    col = lax.broadcasted_iota(jnp.int32, (pillars, pillars), 1)
    return jnp.sum(jnp.where((across == down) & (row < col), 1.0, 0.0), axis=0, keepdims=True)


def moments_kernel(*refs, capacity):
    number = 16
    sources, out, packed, lines_out = refs[:number], *refs[number : number + 3]
    held, wide, sems = refs[number + 3 : 2 * number + 3], refs[-2], refs[-1]
    copies = [move(sources[i], held[i], sems, i) for i in range(number)]
    tiles, cells, counts, points = held[:4]
    micros, _, inputs, depth, pillars = points.shape
    peers, scenes = out.shape[:2]
    copies[0].wait()
    copies[1].wait()
    lines, slot_rows = [], []
    for micro in range(micros):
        tile = tiles[micro].astype(F32)
        cell = (cells[micro] + 1).astype(F32)
        high = jnp.floor(cell * (1.0 / 16.0))
        low = cell - high * 16.0
        rank = ranks(tile)
        slot_rows.append(tile * capacity + rank)
        spot = lax.broadcasted_iota(jnp.int32, (capacity, pillars), 0).astype(F32)
        placed = jnp.where(spot == rank, 1.0, 0.0).astype(BF16)
        peer = lax.broadcasted_iota(jnp.int32, (peers, pillars), 0).astype(F32)
        for group in range(3):
            named = tile == peer + (group - 1.0)
            lines.append(
                16.0 * dot_lanes(jnp.where(named, high, 0.0).astype(BF16), placed)
                + dot_lanes(jnp.where(named, low, 0.0).astype(BF16), placed)
            )
    used = 3 * micros * capacity
    line = jnp.concatenate(lines + [jnp.zeros((peers, LANES - used), F32)], axis=1).reshape(peers, 1, LANES)
    for scene in range(scenes):
        out[:, scene, micros : micros + 1, :] = line
    copies[2].wait()
    copies[3].wait()
    for micro in range(micros):
        wide[...] = points[micro, 0].astype(F32).reshape(inputs * depth, pillars)
        rows = slot_line(wide, depth, inputs)
        notes = jnp.concatenate([slot_rows[micro], counts[micro].astype(F32)], axis=0)
        notes = jnp.concatenate([notes, jnp.zeros((2, rows.shape[1] - pillars), F32)], axis=1)
        lines_out[micro] = jnp.concatenate(
            [rows, notes, jnp.zeros((14 - inputs, rows.shape[1]), F32)], axis=0
        ).astype(BF16)
        mask = slot_mask(counts[micro], depth)
        total = jnp.sum(mask, axis=1, keepdims=True)
        mean = jnp.sum(rows * mask, axis=1, keepdims=True) / total
        centred = (rows - mean) * mask
        products = dot_lanes(centred, centred, lax.Precision.HIGHEST)
        lane = lax.broadcasted_iota(jnp.int32, (inputs, inputs), 1)
        diagonal = lax.broadcasted_iota(jnp.int32, (inputs, inputs), 0) == lane
        mean_row = jnp.sum(jnp.where(diagonal, mean, 0.0), axis=0, keepdims=True)
        row = jnp.concatenate(
            [products[k : k + 1] for k in range(inputs)]
            + [mean_row, total, jnp.zeros((1, LANES - inputs * inputs - inputs - 1), F32)],
            axis=1,
        )
        for scene in range(scenes):
            out[:, scene, micro : micro + 1, :] = jnp.broadcast_to(row[None], (peers, 1, LANES))
    for copy in copies[4:]:
        copy.wait()
    pack(held[4:], packed)


def cells_kernel(found, columns, rows, *, capacity):
    scene = lax.axis_index("scene")
    slots = columns.shape[0]
    peers = found.shape[0]
    values = found[:, 2, :]
    slot = lax.broadcasted_iota(jnp.int32, (slots, peers), 0)
    peer = lax.broadcasted_iota(jnp.int32, (slots, peers), 1)
    lane = lax.broadcasted_iota(jnp.int32, (slots, LANES), 1)
    row = lax.broadcasted_iota(jnp.int32, (slots, LANES), 0)
    result = jnp.zeros((slots, LANES), F32)
    chosen = jnp.where(peer == 2 * (slot // capacity) + scene, 1.0, 0.0)
    spread = dot(chosen, values, lax.Precision.HIGHEST)
    for micro in range(2):
        for group in range(3):
            mine = jnp.where(lane == (3 * micro + group) * capacity + row % capacity, spread, 0.0)
            column = jnp.sum(mine, axis=1, keepdims=True)
            result = jnp.where(lane == 2 * group + micro, column, result)
    columns[...] = result
    rows[...] = jnp.transpose(result)[0:8]


def pillar_notes(rows, micro, inputs, pillars):
    notes = rows[micro, :, 0:pillars].astype(F32)
    return notes[inputs : inputs + 1], notes[inputs + 1 : inputs + 2]


def pillar_kernel(
    found, point_rows, w_pillar, cols, send, pooled, lifted, acts, *, capacity
):
    micros = point_rows.shape[0]
    channels, inputs = w_pillar.shape
    pillars = pooled.shape[2]
    depth = point_rows.shape[2] // pillars
    weight = w_pillar[...]
    wide_weight = weight.astype(F32)
    rows_out = send.shape[0]
    square = inputs * inputs
    stacked, slot_rows = [], []
    for micro in range(micros):
        lifted[...] = dot(weight, point_rows[micro, 0:inputs])
        moments = found[:, micro, :]
        sizes = moments[:, square + inputs : square + inputs + 1]
        means = moments[:, square : square + inputs]
        count = jnp.sum(sizes, axis=0, keepdims=True)
        mean = jnp.sum(means * sizes, axis=0, keepdims=True) / count
        away = means - mean
        products = lax.dot_general(
            away * sizes, away, (((0,), (0,)), ((), ())),
            preferred_element_type=F32, precision=lax.Precision.HIGHEST,
        )
        summed = jnp.sum(moments, axis=0, keepdims=True)
        products = products + jnp.concatenate(
            [summed[:, k * inputs : (k + 1) * inputs] for k in range(inputs)], axis=0
        )
        cov = products / count
        spun = wide_weight[:, 0:1] * cov[0:1]
        for k in range(1, inputs):
            spun = spun + wide_weight[:, k : k + 1] * cov[k : k + 1]
        spread = jnp.sum(spun * wide_weight, axis=1, keepdims=True)
        centre = jnp.sum(wide_weight * mean, axis=1, keepdims=True)
        rstd = lax.rsqrt(spread + norm_eps)
        inverse = jnp.broadcast_to(1.0 / count, (channels, 1))
        pooled[micros + micro] = jnp.concatenate(
            [
                centre, rstd, inverse, jnp.zeros((channels, 13), F32),
                spun, jnp.zeros((channels, 16 - inputs), F32),
                jnp.broadcast_to(mean, (channels, inputs)), jnp.zeros((channels, LANES - 32 - inputs), F32),
            ],
            axis=1,
        )
        scale = rstd * cols[0:channels, 0:1]
        shift = cols[0:channels, 1:2]
        slot, limit = pillar_notes(point_rows, micro, inputs, pillars)
        slot_rows.append(slot)
        top = jnp.full((channels, pillars), -jnp.inf, F32)
        for n in range(depth):
            piece = slice(n * pillars, (n + 1) * pillars)
            normed = (lifted[:, piece] - centre) * scale + shift
            act = normed * sigmoid(normed)
            acts[:, piece] = act
            top = jnp.maximum(top, jnp.where(limit > n, act, -jnp.inf))
        total = jnp.zeros((channels, pillars), F32)
        for n in range(depth):
            piece = slice(n * pillars, (n + 1) * pillars)
            total = total + jnp.where(limit > n, jnp.exp(acts[:, piece] - top), 0.0)
        result = top + jnp.log(total)
        pooled[micro] = result
        parts = [jnp.zeros((channels, pillars), F32)] * micros
        parts[micro] = result.astype(BF16).astype(F32)
        stacked.append(jnp.transpose(jnp.concatenate(parts, axis=0)))
    values = jnp.concatenate(stacked, axis=0).astype(BF16)
    for group in range(3):
        place = lax.broadcasted_iota(jnp.int32, (rows_out, pillars), 0) + (group - 1) * capacity
        chosen = jnp.concatenate(
            [jnp.where(place.astype(F32) == row, 1.0, 0.0) for row in slot_rows], axis=1
        ).astype(BF16)
        send[:, group * LANES : (group + 1) * LANES] = dot(chosen, values).astype(BF16)


def own_stats(ref, first_row, rows, send):
    micros, _, channels, width = ref.shape
    sums, squares = [], []
    for micro in range(micros):
        total = fold(ref[micro, first_row])
        for row in range(first_row + 1, first_row + rows):
            total = total + fold(ref[micro, row])
        total = total * (1.0 / (rows * width))
        mean = jnp.sum(total, axis=1, keepdims=True)
        spread = jnp.zeros(total.shape, F32)
        for row in range(first_row, first_row + rows):
            away = ref[micro, row] - mean
            spread = spread + fold(away * away)
        sums.append(total)
        squares.append(spread)
    if channels == LANES:
        send_all(send, [row_of(part) for part in sums + squares])
    else:
        send_all(send, [row_of(*sums), row_of(*squares)])


def conv_pair(source, weight, micro, at, channels):
    window = source[micro, at : at + 4].reshape(12 * channels, source.shape[3])
    return dot(weight[...], window)


def conv_rows(source, weight, out, shape):
    micros, high, channels, width = shape
    for micro in range(micros):
        for at in range(0, high, 2):
            both = conv_pair(source, weight, micro, at, channels)
            out[micro, at] = both[:channels].astype(out.dtype)
            out[micro, at + 1] = both[channels:].astype(out.dtype)


def canvas_kernel(found, columns, where_rows, l_first, out, kept, send, canvas, *, rows):
    scenes, high, channels, width = out.shape
    masks = edges(channels, width)
    slots = found.shape[0]
    lane = lax.broadcasted_iota(jnp.int32, (slots, width), 1).astype(F32)
    for group in range(3):
        values = jnp.transpose(found[:, group * LANES : (group + 1) * LANES].astype(F32))
        first, count = ((rows - 2, 2), (0, rows), (0, 2))[group]
        for scene in range(scenes):
            at = 2 * group + scene
            column = columns[:, at : at + 1] - 1.0
            column = column - jnp.floor(column * (1.0 / width)) * width
            row = jnp.floor((where_rows[at : at + 1] - 1.0) * (1.0 / width))
            mine = values[scene * channels : (scene + 1) * channels]
            placed = jnp.concatenate(
                [jnp.where(row == r * 1.0, mine, 0.0) for r in range(first, first + count)], axis=0
            ).astype(BF16)
            chosen = jnp.where(lane == column, 1.0, 0.0).astype(BF16)
            grid = dot(placed, chosen).astype(BF16)
            start = (0, 2, rows + 2)[group]
            for r in range(count):
                row = grid[r * channels : (r + 1) * channels]
                canvas[scene, start + r] = spread(row, masks)
                if 1 <= start + r <= rows + 2:
                    kept[scene, start + r - 1] = row
    conv_rows(canvas, l_first, out, out.shape)
    own_stats(out, 1, rows, send)


def second_kernel(found, cols, first_out, l_second_in, out, kept, stats, send, acts, l_second, sems,
                  *, rows, tiles):
    weight_copy = move(l_second_in, l_second, sems, 0)
    micros, high, channels, width = first_out.shape
    tile = lax.axis_index("tile")
    turned = stat_columns(found, float(rows * width))
    stats[...] = turned
    masks = edges(channels, width)
    for micro in range(micros):
        part = slice(micro * channels, (micro + 1) * channels)
        centre = turned[part, 0:1]
        scale = turned[part, 1:2] * cols[0:channels, 2:3]
        shift = cols[0:channels, 3:4]

        for row in range(high):
            normed = (first_out[micro, row] - centre) * scale + shift
            act = normed * sigmoid(normed)
            if row == 0 or row == high - 1:
                act = act * inside(tile, row - 1, (tiles, rows))
            act = act.astype(BF16)
            acts[micro, row] = spread(act, masks)
            kept[micro, row] = act
    weight_copy.wait()
    conv_rows(acts, l_second, out, out.shape)
    own_stats(out, 0, rows, send)


def up_kernel(found, cols, second_out, w_up, acts, upper, slopes, plain, crossed, stats, send, *, rows):
    micros, _, channels, width = second_out.shape
    peers = send.shape[0]
    each = crossed.shape[0] // peers
    turned = stat_columns(found, float(rows * width))
    stats[...] = turned
    gain, shift = cols[0:channels, 4:5], cols[0:channels, 5:6]
    lines = []
    for micro in range(micros):
        part = slice(micro * channels, (micro + 1) * channels)
        centre, rstd = turned[part, 0:1], turned[part, 1:2]
        slope_sum = jnp.zeros((channels, LANES), F32)
        unit_sum = jnp.zeros((channels, LANES), F32)
        for row in range(rows):
            unit = (second_out[micro, row] - centre) * rstd
            normed = unit * gain + shift
            gate = sigmoid(normed)
            act = normed * gate
            slope = gate + act * (1.0 - gate)
            sloped = slope * unit
            slope_sum = slope_sum + fold(slope)
            unit_sum = unit_sum + fold(sloped)
            slopes[micro, row] = jnp.concatenate([slope, sloped], axis=0).astype(BF16)
            act = act.astype(BF16)
            acts[micro, row] = act
            upper[micro, row] = dot(w_up[...], act)
        lines.append(row_of(slope_sum, unit_sum).astype(BF16).astype(F32))
        crossed[micro * channels : (micro + 1) * channels] = dot_lanes(
            jnp.concatenate([acts[micro, row] for row in range(rows)], axis=1),
            jnp.concatenate([slopes[micro, row] for row in range(rows)], axis=1),
        )
    plain[...] = jnp.concatenate(lines, axis=0)
    used = micros * channels
    if crossed.shape[0] > used:
        crossed[used:] = jnp.zeros((crossed.shape[0] - used, LANES), F32)
    if 2 * micros + each < send.shape[1]:
        send[...] = jnp.zeros(send.shape, F32)
    for peer in range(peers):
        send[peer, 2 * micros : 2 * micros + each] = crossed[peer * each : (peer + 1) * each]
    own_stats(upper, 0, rows, send)


def exact_rows(rows):
    high = rows.astype(BF16).astype(F32)
    return [high, rows - high]


def top_kernel(found, cols, upper, cot, slopes, plain, w_up_t, features, grads, mixed, stats, send, *, rows, each):
    micros, _, wide, width = upper.shape
    channels = w_up_t.shape[0]
    lines = []
    for micro in range(micros):
        lines += list(pooled_stats(found[:, micro, :], found[:, micros + micro, :], float(rows * width)))
    turned = columns_of(lines)
    stats[...] = turned
    gain, shift = cols[:, 6:7], cols[:, 7:8]
    gain_rows, shift_rows, mixed_rows = [], [], []
    for micro in range(micros):
        centre, rstd = turned[:, 2 * micro : 2 * micro + 1], turned[:, 2 * micro + 1 : 2 * micro + 2]
        factor = gain * rstd
        gain_sum = jnp.zeros((wide, LANES), F32)
        shift_sum = jnp.zeros((wide, LANES), F32)
        mixed_sum = jnp.zeros((2 * channels, LANES), F32)
        for row in range(rows):
            unit = (upper[micro, row] - centre) * rstd
            normed = unit * gain + shift
            gate = sigmoid(normed)
            act = normed * gate
            grad = cot[micro, row].astype(F32) * (gate + act * (1.0 - gate))
            features[micro, row] = act.astype(BF16)
            grads[micro, row] = grad
            gain_sum = gain_sum + fold(grad * unit)
            shift_sum = shift_sum + fold(grad)
            below = dot(w_up_t[...], (grad * factor).astype(BF16))
            mixed_sum = mixed_sum + fold(
                slopes[micro, row].astype(F32) * jnp.concatenate([below, below], axis=0)
            )
        gain_rows.append(row_of(gain_sum))
        shift_rows.append(row_of(shift_sum))
        mixed_rows.append(row_of(mixed_sum).astype(BF16).astype(F32))
    mixed[...] = jnp.concatenate(mixed_rows, axis=0)
    rows_out = jnp.concatenate(gain_rows + shift_rows, axis=0)
    crossed = jnp.sum(found[:, 2 * micros : 2 * micros + each, :], axis=0)
    rest = send.shape[1] - 6 * micros - each
    block = exact_rows(rows_out) + mixed_rows + [plain[...], crossed]
    if rest > 0:
        block.append(jnp.zeros((rest, LANES), F32))
    block = jnp.concatenate(block, axis=0)
    send[...] = jnp.broadcast_to(block.astype(BF16)[None], send.shape)


def low_rows(turned, value_of, values, stats, gain, low, high, first, rows, tiles):
    micros, _, channels, width = values.shape
    tile = lax.axis_index("tile")
    masks = edges(channels, width)
    for micro in range(micros):
        part = slice(micro * channels, (micro + 1) * channels)
        centre, rstd = stats[part, 0:1], stats[part, 1:2]
        factor = gain * rstd
        slope_part, shift_part = rstd * turned[part, 0:1], turned[part, 1:2]
        for index in range(high):
            grad, value = value_of(micro, index)
            grad = factor * (grad - shift_part - (value - centre) * slope_part)
            if index + first < 0 or index + first >= rows:
                grad = grad * inside(tile, index + first, (tiles, rows))
            low[micro, index] = spread(grad.astype(BF16), masks)


def first_slopes(first_out, stats, cols, micro, channels):
    part = slice(micro * channels, (micro + 1) * channels)
    centre, rstd = stats[part, 0:1], stats[part, 1:2]
    gain, shift = cols[0:channels, 2:3], cols[0:channels, 3:4]

    def at(row):
        unit = (first_out[micro, row] - centre) * rstd
        normed = unit * gain + shift
        gate = sigmoid(normed)
        return gate + normed * gate * (1.0 - gate), unit

    return at


def second_sums(total, weight, factors, stats, micro, micros, count):
    channels = weight.shape[1]
    factor, centre = factors[micro], stats[:, 2 * micro : 2 * micro + 1]
    columns = jnp.transpose(jnp.concatenate([total, jnp.zeros((8 - total.shape[0], LANES), F32)], axis=0))
    beta = factor * stats[:, 2 * micro + 1 : 2 * micro + 2] * columns[:, micro : micro + 1] * (1.0 / count)
    alpha = factor * columns[:, micros + micro : micros + micro + 1] * (1.0 / count)
    square = lax.dot_general(
        weight * beta, weight, (((0,), (0,)), ((), ())),
        preferred_element_type=F32, precision=lax.Precision.HIGHEST,
    )
    square = jnp.concatenate([square, square], axis=1)
    line = jnp.sum(weight * (alpha - beta * centre), axis=0, keepdims=True)
    line = jnp.concatenate([line, line], axis=1)

    def give(mixed, plain, crossed):
        mine = crossed[micro * channels : (micro + 1) * channels]
        return mixed - plain * line - jnp.sum(square * mine, axis=0, keepdims=True)

    return give


def middle_back_kernel(
    found, cols, grads, upper, top_stats, second_out, second_stats, w_up, w_up_t, second_act,
    first_out, first_stats, b_second_in, acts, own_mixed, own_plain, own_crossed,
    out, top_grad, weight_grad, rising, falling,
    top_gain_grad, top_shift_grad, expected, send, low, top_low, second_dz, b_second, sems, *, rows, tiles, each
):
    weight_copy = move(b_second_in, b_second, sems, 0)
    scene = lax.axis_index("scene")
    tile = lax.axis_index("tile")
    micros, _, wide, width = grads.shape
    channels = second_out.shape[2]
    peers = found.shape[0]
    count = float(peers * rows * width)
    kept = 2 * micros
    total = jnp.sum(found[...].astype(F32), axis=0)
    mixed, plain = total[2 * kept : 2 * kept + micros], total[2 * kept + micros : 3 * kept]
    total = total[0:kept] + total[kept : 2 * kept]
    crossed = jnp.concatenate(
        [
            found[peer].astype(F32)[3 * kept : 3 * kept + each]
            for peer in range(-(-micros * channels // each))
        ],
        axis=0,
    )
    own_half(total[0:1] + total[1:2], scene, top_gain_grad)
    own_half(total[2:3] + total[3:4], scene, top_shift_grad)
    factors = [cols[:, 6:7] * top_stats[:, 2 * micro + 1 : 2 * micro + 2] for micro in range(micros)]
    wide_weight = w_up[...].astype(F32)
    turned = columns_of([total[index : index + 1] for index in range(2 * micros)]) * (1.0 / count)
    gain, shift = cols[0:channels, 4:5], cols[0:channels, 5:6]
    masks = edges(channels, width)
    extra_rows = []
    for micro in range(micros):
        top_centre = top_stats[:, 2 * micro : 2 * micro + 1]
        top_slope = top_stats[:, 2 * micro + 1 : 2 * micro + 2] * turned[:, micro : micro + 1]
        top_shift = turned[:, micros + micro : micros + micro + 1]
        part = slice(micro * channels, (micro + 1) * channels)
        centre, rstd = second_stats[part, 0:1], second_stats[part, 1:2]
        gain_sum = jnp.zeros((channels, LANES), F32)
        shift_sum = jnp.zeros((channels, LANES), F32)
        for row in range(rows):
            grad = factors[micro] * (
                grads[micro, row] - top_shift - (upper[micro, row] - top_centre) * top_slope
            )
            grad = grad.astype(BF16)
            top_low[micro, row] = grad
            unit = (second_out[micro, row] - centre) * rstd
            normed = unit * gain + shift
            gate = sigmoid(normed)
            grad = dot(w_up_t[...], grad) * (gate + normed * gate * (1.0 - gate))
            second_dz[micro, row] = grad
            shift_sum = shift_sum + fold(grad)
            gain_sum = gain_sum + fold(grad * unit)
        give = second_sums(total, wide_weight, factors, top_stats, micro, micros, count)
        whole = give(mixed[micro : micro + 1], plain[micro : micro + 1], crossed)
        extra = row_of(shift_sum, gain_sum) - give(
            own_mixed[micro : micro + 1], own_plain[micro : micro + 1], own_crossed[...]
        )
        expected[micro : micro + 1] = whole
        extra_rows.append(extra)
        part = columns_of([whole * (1.0 / count) + extra * (1.0 / (rows * width))])
        shift_part, gain_part = part[0:channels, 0:1], part[channels : 2 * channels, 0:1]
        for row in range(rows):
            unit = (second_out[micro, row] - centre) * rstd
            grad = (gain * rstd) * (second_dz[micro, row] - shift_part - unit * gain_part)
            low[micro, row] = spread(grad.astype(BF16), masks)
        product = dot_lanes(
            jnp.concatenate([top_low[micro, row] for row in range(rows)], axis=1),
            jnp.concatenate([second_act[micro, row] for row in range(rows)], axis=1),
        )
        top_grad[...] = product if micro == 0 else top_grad[...] + product
    for micro in range(micros):
        for row in range(2):
            falling[micro, row] = low[micro, row, channels : 2 * channels]
            rising[micro, row] = low[micro, rows - 2 + row, channels : 2 * channels]
    conv_grad(low, 0, acts, 0, weight_grad, rows)
    weight_copy.wait()
    half = 6 * channels
    gain_sums, shift_sums = [], []
    for micro in range(micros):
        slopes = first_slopes(first_out, first_stats, cols, micro, channels)
        gain_sum = jnp.zeros((channels, LANES), F32)
        shift_sum = jnp.zeros((channels, LANES), F32)
        for at in range(0, rows + 2, 2):
            if at == 0:
                parts = dot(b_second[:, half:], low[micro, 0:2].reshape(half, width))
            elif at == rows:
                parts = dot(b_second[:, :half], low[micro, rows - 2 : rows].reshape(half, width))
            else:
                parts = conv_pair(low, b_second, micro, at - 2, channels)
            for j in range(2):
                slope, unit = slopes(at + j)
                grad = parts[channels * j : channels * (j + 1)] * slope
                if at + j == 0 or at + j == rows + 1:
                    grad = grad * inside(tile, at + j - 1, (tiles, rows))
                out[micro, at + j] = grad
                gain_sum = gain_sum + fold(grad * unit)
                shift_sum = shift_sum + fold(grad)
        gain_sums.append(gain_sum)
        shift_sums.append(shift_sum)
    send_all(send, [row_of(*gain_sums), row_of(*shift_sums)] + extra_rows)


def conv_grad(low, low_first, values, value_first, total, rows):
    micros, _, channels, width = values.shape
    for micro in range(micros):
        grads = jnp.concatenate([low[micro, row + low_first] for row in range(rows)], axis=1)
        windows = jnp.concatenate(
            [
                values[micro, row + value_first : row + value_first + 3].reshape(3 * channels, width)
                for row in range(rows)
            ],
            axis=1,
        )
        product = dot_lanes(grads, windows)
        total[...] = product if micro == 0 else total[...] + product


def half_rows(total, half, scene):
    channels = 2 * half
    start = scene * half
    mine = jnp.concatenate(
        [total[b * channels + start : b * channels + start + half, :] for b in range(2, -1, -1)], axis=0
    )
    wing = mine[:, LANES:]
    cut = wing.shape[0] // 2
    return [mine[:, :LANES], jnp.concatenate([wing[:cut], wing[cut:]], axis=1)]


def pick_kernel(
    found, cols, grads, before, after, first_out, first_stats, b_first_in, b_second_in, columns, where_rows,
    canvas, second_grad, top_grad, expected,
    send, gain_grad, shift_grad, second_gain_grad, second_shift_grad, low, grid, b_first, b_second, halo, first_grad, whole, sems,
    *, rows, tiles, each
):
    second_copy = move(b_second_in, b_second, sems, 1)
    weight_copy = move(b_first_in, b_first, sems, 0)
    scene = lax.axis_index("scene")
    micros, _, channels, width = grads.shape
    sums = sum_rows(found, 2 + micros)
    second = sum(sums[2:]) + jnp.sum(expected[...], axis=0, keepdims=True)
    own_half(second[:, :channels], scene, second_shift_grad)
    own_half(second[:, channels:], scene, second_gain_grad)
    sums = sums[:2]
    own_half(sums[0][:, :channels] + sums[0][:, channels:], scene, gain_grad)
    own_half(sums[1][:, :channels] + sums[1][:, channels:], scene, shift_grad)
    turned = columns_of(sums) * (1.0 / (found.shape[0] * rows * width))
    masks = edges(channels, width)
    half = 6 * channels
    second_copy.wait()
    for micro in range(micros):
        slopes = first_slopes(first_out, first_stats, cols, micro, channels)
        for at, ref, columns_used in ((0, before, slice(0, half)), (rows, after, slice(half, 2 * half))):
            window = jnp.concatenate([spread(ref[micro, row], masks) for row in range(2)], axis=0)
            parts = dot(b_second[:, columns_used], window)
            for j in range(2):
                slope, _ = slopes(at + j)
                halo[micro, at + j] = parts[channels * j : channels * (j + 1)] * slope

    def value_of(micro, index):
        grad = grads[micro, index]
        if index < 2 or index >= rows:
            grad = grad + halo[micro, index]
        return grad, first_out[micro, index]

    low_rows(turned, value_of, first_out, first_stats, cols[0:channels, 2:3], low, rows + 2, -1, rows, tiles)
    weight_copy.wait()
    conv_rows(low, b_first, grid, grid.shape)
    conv_grad(low, 1, canvas, 0, first_grad, rows)
    half = channels // 2
    peers, block = send.shape[:2]
    for s in range(2):
        parts = half_rows(first_grad, half, s) + half_rows(second_grad, half, s)
        mine = top_grad[s * channels : (s + 1) * channels, :]
        parts.append(jnp.concatenate([mine[:half], mine[half:]], axis=1))
        parts = jnp.concatenate(parts, axis=0)
        whole[s, 0 : parts.shape[0]] = parts
        if whole.shape[1] > parts.shape[0]:
            whole[s, parts.shape[0] :] = jnp.zeros((whole.shape[1] - parts.shape[0], LANES), F32)
    slots = columns.shape[0]
    lane = lax.broadcasted_iota(jnp.int32, (slots, width), 1).astype(F32)
    picked = []
    for micro in range(micros):
        at = 2 + micro
        column = columns[:, at : at + 1] - 1.0
        column = column - jnp.floor(column * (1.0 / width)) * width
        place = jnp.floor((where_rows[at : at + 1] - 1.0) * (1.0 / width))
        chosen = jnp.where(lane == column, 1.0, 0.0).astype(BF16)
        here = dot_lanes(grid[micro].reshape(rows * channels, width), chosen)
        total = jnp.zeros((channels, slots), F32)
        for r in range(rows):
            total = total + jnp.where(place == r * 1.0, here[r * channels : (r + 1) * channels], 0.0)
        picked.append(total)
    picked = jnp.transpose(jnp.concatenate(picked, axis=0))
    capacity = slots // tiles
    rest = block - capacity - 2 * each
    for peer in range(peers):
        spot = peer // 2
        parts = [picked[spot * capacity : (spot + 1) * capacity]]
        parts += [whole[s, peer * each : (peer + 1) * each] for s in range(2)]
        parts.append(jnp.zeros((rest, LANES), F32))
        send[peer] = jnp.concatenate(parts, axis=0).astype(BF16)


def pillar_back_kernel(found, rows_in, w_pillar, cols, pooled, send, grads, lifted, rows, sems,
                       *, capacity, each):
    fetched = move(rows_in, rows, sems, 0)
    micros = rows.shape[0]
    _, channels, pillars = pooled.shape
    stats = pooled.at[micros : 2 * micros]
    inputs = w_pillar.shape[1]
    depth = rows.shape[2] // pillars
    scene = lax.axis_index("scene")
    peers = found.shape[0]
    slot_count = peers // 2 * capacity
    returned = jnp.concatenate(
        [found[2 * t + scene].astype(F32)[0:capacity] for t in range(peers // 2)], axis=0
    )
    turned = jnp.transpose(returned)
    place = lax.broadcasted_iota(jnp.int32, (slot_count, pillars), 0).astype(F32)
    gain, shift = cols[0:channels, 0:1], cols[0:channels, 1:2]
    gain_sums, shift_sums = [], []
    outer = jnp.zeros((16, channels), F32)
    fetched.wait()
    for micro in range(micros):
        lifted[...] = dot(w_pillar[...], rows[micro, 0:inputs])
        slot, limit = pillar_notes(rows, micro, inputs, pillars)
        chosen = jnp.where(place == slot, 1.0, 0.0).astype(BF16)
        back = dot(turned[micro * channels : (micro + 1) * channels].astype(BF16), chosen)
        centre, rstd = stats[micro, :, 0:1], stats[micro, :, 1:2]
        pool = pooled[micro]
        gain_sum = jnp.zeros((channels, pillars), F32)
        shift_sum = jnp.zeros((channels, pillars), F32)
        for n in range(depth):
            piece = slice(n * pillars, (n + 1) * pillars)
            unit = (lifted[:, piece] - centre) * rstd
            normed = unit * gain + shift
            gate = sigmoid(normed)
            act = normed * gate
            slope = gate + act * (1.0 - gate)
            grad = jnp.where(limit > n, back * jnp.exp(act - pool) * slope, 0.0)
            grads[micro, :, piece] = grad
            gain_sum = gain_sum + grad * unit
            shift_sum = shift_sum + grad
        gain_sums.append(gain_sum)
        shift_sums.append(shift_sum)
        scale = jnp.transpose(jnp.broadcast_to(rstd * gain, (channels, LANES)))[0:1]
        outer = outer + dot_lanes(rows[micro], grads[micro].astype(BF16)) * scale
    lines = [row_of(*gain_sums), row_of(*shift_sums)]
    for k in range(0, 10, 2):
        lines.append(jnp.concatenate([outer[k : k + 1], outer[k + 1 : k + 2]], axis=1))
    exact = jnp.concatenate(lines, axis=0)
    kept = 2 * exact.shape[0]
    weights = jnp.sum(found[...].astype(F32), axis=0)
    rest = send.shape[2] - kept - each
    for s in range(2):
        mine = weights[capacity + s * each : capacity + (s + 1) * each]
        block = exact_rows(exact) + [mine] + ([jnp.zeros((rest, LANES), F32)] if rest > 0 else [])
        block = jnp.concatenate(block, axis=0).astype(BF16)
        send[:, s] = jnp.broadcast_to(block[None], (send.shape[0],) + block.shape)


def points_kernel(
    found, rows_in, grads, w_pillar, cols, pooled,
    points_grad, pillar_grad, gain_grad, shift_grad, first_grad, second_grad, up_grad, rows, lifted, sems,
    *, each
):
    fetched = move(rows_in, rows, sems, 0)
    scene = lax.axis_index("scene")
    micros, channels, _ = grads.shape
    stats = pooled.at[micros : 2 * micros]
    _, _, inputs, depth, pillars = points_grad.shape
    half = channels // 2
    kept = 7
    total = jnp.sum(found[...].astype(F32), axis=0)
    total = total[0:kept] + total[kept : 2 * kept]
    own_half(total[0:1, :channels] + total[0:1, channels:], scene, gain_grad)
    own_half(total[1:2, :channels] + total[1:2, channels:], scene, shift_grad)
    turned = jnp.transpose(jnp.concatenate([total, jnp.zeros((1, LANES), F32)], axis=0))
    weight_grad = jnp.concatenate(
        [turned[(k % 2) * channels : (k % 2 + 1) * channels, 2 + k // 2 : 3 + k // 2] for k in range(inputs)],
        axis=1,
    )
    weight = jnp.transpose(w_pillar[...].astype(F32)).astype(BF16)
    fetched.wait()
    for micro in range(micros):
        lifted[...] = dot(w_pillar[...], rows[micro, 0:inputs])
        part = slice(micro * channels, (micro + 1) * channels)
        centre, rstd, inverse = stats[micro, :, 0:1], stats[micro, :, 1:2], stats[micro, :, 2:3]
        factor = cols[0:channels, 0:1] * rstd
        gain_part, shift_part = turned[part, 0:1], turned[part, 1:2]
        spun, mean = stats[micro, :, 16 : 16 + inputs], stats[micro, :, 32 : 32 + inputs]
        weight_grad = weight_grad - factor * (shift_part * mean + gain_part * rstd * spun)
        gain_part, shift_part = gain_part * inverse * rstd, shift_part * inverse
        _, limit = pillar_notes(rows, micro, inputs, pillars)
        for n in range(depth):
            piece = slice(n * pillars, (n + 1) * pillars)
            low = factor * (grads[micro, :, piece] - shift_part - (lifted[:, piece] - centre) * gain_part)
            low = jnp.where(limit > n, low, 0.0).astype(BF16)
            points_grad[micro, 0, :, n, :] = dot(weight, low)
    weight_grad = jnp.concatenate([weight_grad, jnp.zeros((channels, LANES - inputs), F32)], axis=1)
    weight_grad = jnp.transpose(weight_grad)[0:inputs]
    pillar_grad[...] = jnp.where(scene == 0, weight_grad[:, :half], weight_grad[:, half:])
    whole = jnp.concatenate(
        [found[peer].astype(F32)[2 * kept : 2 * kept + each] for peer in range(found.shape[0])], axis=0
    )
    for index, out in enumerate((first_grad, second_grad)):
        base = index * 9 * half * channels // LANES
        lead = 3 * half
        mine = whole[base : base + lead]
        wing = whole[base + lead : base + lead + lead // 2]
        wing = jnp.concatenate([wing[:, :channels], wing[:, channels:]], axis=0)
        both = jnp.concatenate([mine, wing], axis=1)
        for a in range(3):
            for b in range(3):
                at = (3 * a + b) * channels
                out[:, at : at + channels] = both[b * half : (b + 1) * half, a * channels : (a + 1) * channels]
    base = 2 * 9 * half * channels // LANES
    top = whole[base : base + half]
    up_grad[...] = jnp.concatenate([top[:, :channels], top[:, channels:]], axis=0)


def swap(blocks, axes):
    return lax.all_to_all(blocks, axes, split_axis=0, concat_axis=0)


def shards(
    points, point_counts, pillar_tile, pillar_cell,
    pillar_weight, pillar_gain, pillar_shift,
    first_weight, first_gain, first_shift,
    second_weight, second_gain, second_shift,
    up_weight, up_gain, up_shift, cotangent,
):
    micros, _, inputs, depth, pillars = points.shape
    channels = up_weight.shape[1]
    upper = cotangent.shape[2]
    rows, width = cotangent.shape[3:]
    tiles = lax.axis_size("tile")
    scenes = lax.axis_size("scene")
    peers = tiles * scenes
    capacity = 2 * pillars // tiles
    slot_count = tiles * capacity
    half = channels // 2

    def vmem(shape, dtype):
        return pltpu.VMEM(shape, dtype)

    def grid(high, dtype=F32, lead=channels):
        return ((micros, high, lead, width), dtype)

    sums = ((peers, 2, LANES), F32)
    sources = (
        pillar_tile, pillar_cell, point_counts, points,
        first_weight, second_weight, up_weight, pillar_weight.T,
        pillar_gain, pillar_shift, first_gain, first_shift, second_gain, second_shift, up_gain, up_shift,
    )
    moments, packed, point_rows = run(
        functools.partial(moments_kernel, capacity=capacity),
        [
            ((tiles, scenes, 4, LANES), F32), ((layout(half, channels)[-1] + 16, LANES), BF16),
            ((micros, 16, depth * pillars), BF16),
        ],
        *sources,
        hbm=range(len(sources)), copies=len(sources), limit=WIDE_LIMIT,
        scratch=[vmem(source.shape, source.dtype) for source in sources]
        + [vmem((inputs * depth, pillars), F32)],
    )
    moments = swap(moments.reshape(peers, 4, LANES), BOTH)
    both = lax.all_gather(packed, "scene")
    taps = ((2 * channels, 12 * channels), BF16)
    w_pillar, cols, l_first, l_second, b_first, b_second, w_up, w_up_t = run(
        functools.partial(unpack_kernel, inputs=inputs),
        [
            ((channels, inputs), BF16), ((LANES, 8), F32), taps, taps + (1,), taps + (1,), taps + (1,),
            ((upper, channels), BF16), ((channels, upper), BF16),
        ],
        both,
        scratch=[vmem(*taps), vmem(*taps), vmem(*taps)], copies=3,
    )
    cot = cotangent[:, 0].transpose(0, 2, 1, 3)

    send, pooled = run(
        functools.partial(pillar_kernel, capacity=capacity),
        [((slot_count, 3 * LANES), BF16), ((2 * micros, channels, pillars), F32)],
        moments, point_rows, w_pillar, cols,
        scratch=[vmem((channels, depth * pillars), F32), vmem((channels, depth * pillars), F32)],
    )
    arrived = swap(send.reshape(tiles, capacity, 3 * LANES), "tile").reshape(slot_count, 3 * LANES)
    cell_columns, cell_rows = run(
        functools.partial(cells_kernel, capacity=capacity),
        [((slot_count, LANES), F32), ((8, slot_count), F32)],
        moments,
        cost=pl.CostEstimate(flops=10**7, bytes_accessed=10**6, transcendentals=0),
    )
    arrived, cot = lax.optimization_barrier((arrived, cot))

    first_out, canvas, send = run(
        functools.partial(canvas_kernel, rows=rows),
        [grid(rows + 2), grid(rows + 2, BF16), sums],
        arrived, cell_columns, cell_rows, l_first,
        scratch=[vmem(*grid(rows + 4, BF16, 3 * channels))],
    )
    second_out, first_act, first_stats, send = run(
        functools.partial(second_kernel, rows=rows, tiles=tiles),
        [grid(rows), grid(rows + 2, BF16), ((LANES, 8), F32), sums],
        swap(send, BOTH), cols, first_out, l_second,
        hbm=(3,), scratch=[vmem(*grid(rows + 2, BF16, 3 * channels)), vmem(*taps)], copies=1,
    )
    part = -(-micros * channels // peers)
    second_act, up_out, slopes, plain, crossed, second_stats, send = run(
        functools.partial(up_kernel, rows=rows),
        [
            grid(rows, BF16), grid(rows, F32, upper), grid(rows, BF16, 2 * channels), ((micros, LANES), F32),
            ((peers * part, LANES), F32), ((LANES, 8), F32), ((peers, -(-(2 * micros + part) // 8) * 8, LANES), F32),
        ],
        swap(send, BOTH), cols, second_out, w_up,
    )
    features, grads, mixed, top_stats, send = run(
        functools.partial(top_kernel, rows=rows, each=part),
        [
            grid(rows, BF16, upper), grid(rows, F32, upper), ((micros, LANES), F32), ((LANES, 8), F32),
            ((peers, -(-(6 * micros + part) // 8) * 8, LANES), BF16),
        ],
        swap(send, BOTH), cols, up_out, cot, slopes, plain, w_up_t,
    )
    features = with_layout_constraint(features.transpose(0, 2, 1, 3)[:, None], Layout((0, 1, 2, 3, 4)))
    features, send = lax.optimization_barrier((features, send))
    edge = ((micros, 2, channels, width), BF16)
    vector, top_vector, matrix = ((half,), F32), ((upper // 2,), F32), ((half, 9 * channels), F32)
    rising = [(i, i + 1) for i in range(tiles - 1)]
    falling = [(j, i) for i, j in rising]
    cross = ((3 * channels, 3 * channels), F32)
    (
        first_dz, top_grad, second_cross, rising_edge, falling_edge,
        up_gain_grad, up_shift_grad, expected, send,
    ) = run(
        functools.partial(middle_back_kernel, rows=rows, tiles=tiles, each=part),
        [
            grid(rows + 2), ((upper, channels), F32), cross, edge, edge,
            top_vector, top_vector, ((micros, LANES), F32), ((peers, 2 + micros, LANES), F32),
        ],
        swap(send, BOTH), cols, grads, up_out, top_stats, second_out, second_stats, w_up, w_up_t, second_act,
        first_out, first_stats, b_second, first_act, mixed, plain, crossed,
        hbm=(12,),
        scratch=[
            vmem(*grid(rows, BF16, 3 * channels)), vmem(*grid(rows, BF16, upper)), vmem(*grid(rows)), vmem(*taps),
        ],
        copies=1,
    )
    length = (2 * 9 * half * channels + upper * half) // LANES
    each = -(-length // peers)
    block = -(-(capacity + 2 * each) // 8) * 8
    send, first_gain_grad, first_shift_grad, second_gain_grad, second_shift_grad = run(
        functools.partial(pick_kernel, rows=rows, tiles=tiles, each=each),
        [((peers, block, LANES), BF16), vector, vector, vector, vector],
        swap(send, BOTH), cols, first_dz,
        lax.ppermute(rising_edge, "tile", rising), lax.ppermute(falling_edge, "tile", falling),
        first_out, first_stats, b_first, b_second, cell_columns, cell_rows, canvas, second_cross, top_grad, expected,
        hbm=(7, 8),
        scratch=[
            vmem(*grid(rows + 2, BF16, 3 * channels)), vmem(*grid(rows, BF16)), vmem(*taps), vmem(*taps),
            vmem(*grid(rows + 2)), vmem(*cross), vmem((scenes, peers * each, LANES), F32),
        ],
        copies=2,
    )
    block = -(-(14 + each) // 8) * 8
    send, pillar_dz = run(
        functools.partial(pillar_back_kernel, capacity=capacity, each=each),
        [((tiles, scenes, block, LANES), BF16), ((micros, channels, depth * pillars), F32)],
        swap(send, BOTH), point_rows, w_pillar, cols, pooled,
        hbm=(1,),
        scratch=[vmem((channels, depth * pillars), F32), vmem((micros, 16, depth * pillars), BF16)],
        copies=1,
    )
    points_grad, pillar_grad, pillar_gain_grad, pillar_shift_grad, first_grad, second_grad, up_grad = run(
        functools.partial(points_kernel, each=each),
        [
            ((micros, 1, inputs, depth, pillars), F32), ((inputs, half), F32), vector, vector,
            matrix, matrix, ((upper // 2, channels), F32),
        ],
        swap(send.reshape(peers, block, LANES), BOTH), point_rows, pillar_dz, w_pillar, cols, pooled,
        hbm=(1,),
        scratch=[vmem((micros, 16, depth * pillars), BF16), vmem((channels, depth * pillars), F32)],
        copies=1,
    )
    return (
        features, points_grad,
        pillar_grad.T, pillar_gain_grad, pillar_shift_grad,
        first_grad, first_gain_grad, first_shift_grad,
        second_grad, second_gain_grad, second_shift_grad,
        up_grad, up_gain_grad, up_shift_grad,
    )


def solution(mesh):
    matrix, vector = P("scene", None), P("scene")
    grid = P(None, "scene", None, "tile", None)
    cloud = P(None, "scene", None, None, "tile")
    pillar = P(None, "scene", "tile")
    weights = (matrix, vector, vector) * 4
    return jax.shard_map(
        shards,
        mesh=mesh,
        in_specs=(cloud, pillar, pillar, pillar) + weights + (grid,),
        out_specs=(grid, cloud) + weights,
        check_vma=False,
    )
```

```python
import functools

import jax
import jax.numpy as jnp
from jax import lax
from jax.experimental import pallas as pl
from jax.experimental.layout import Layout, with_layout_constraint
from jax.experimental.pallas import tpu as pltpu
from jax.sharding import PartitionSpec as P

norm_eps = 0.001
BOTH = ("tile", "scene")
F32 = jnp.float32
BF16 = jnp.bfloat16
VMEM_LIMIT = 24 * 1024 * 1024
WIDE_LIMIT = 60 * 1024 * 1024
LANES = 128


def run(kernel, outs, *args, hbm=(), scratch=(), copies=0, cost=None, limit=VMEM_LIMIT):
    specs = [
        pl.BlockSpec(memory_space=pltpu.HBM if index in hbm else pltpu.VMEM) for index in range(len(args))
    ]
    scratch = list(scratch)
    if copies:
        scratch.append(pltpu.SemaphoreType.DMA((copies,)))
    return pl.pallas_call(
        kernel,
        out_shape=[jax.ShapeDtypeStruct(out[0], out[1]) for out in outs],
        in_specs=specs,
        out_specs=[
            pl.BlockSpec(memory_space=pltpu.HBM if len(out) > 2 else pltpu.VMEM) for out in outs
        ],
        scratch_shapes=scratch,
        compiler_params=pltpu.CompilerParams(vmem_limit_bytes=limit),
        cost_estimate=cost,
    )(*args)


def move(source, target, sems, index):
    copy = pltpu.make_async_copy(source, target, sems.at[index])
    copy.start()
    return copy


def dot(left, right, precision=None):
    return jnp.dot(left, right, preferred_element_type=F32, precision=precision)


def dot_lanes(left, right, precision=None):
    return lax.dot_general(
        left, right, (((1,), (1,)), ((), ())), preferred_element_type=F32, precision=precision
    )


def sigmoid(values):
    return 0.5 + 0.5 * jnp.tanh(0.5 * values)


def fold(values):
    total = values[:, :LANES]
    for start in range(LANES, values.shape[1], LANES):
        total = total + values[:, start : start + LANES]
    return total


def row_of(left, right=None):
    both = left if right is None else jnp.concatenate([left, right], axis=0)
    return jnp.sum(jnp.transpose(both), axis=0, keepdims=True)


def columns_of(rows):
    rows = rows + [jnp.zeros((8 - len(rows), LANES), F32)] if len(rows) < 8 else rows
    return jnp.transpose(jnp.concatenate(rows, axis=0))


def inside(tile, row, height):
    tiles, rows = height
    place = tile * rows + row
    return jnp.where((place >= 0) & (place < tiles * rows), 1.0, 0.0).astype(F32)


def send_all(ref, rows):
    for index, row in enumerate(rows):
        ref[:, index : index + 1, :] = jnp.broadcast_to(row[None], (ref.shape[0], 1, LANES))


def pooled_stats(means, squares, count):
    peers = means.shape[0]
    mean = jnp.sum(means, axis=0, keepdims=True) * (1.0 / peers)
    away = means - mean
    spread = jnp.sum(squares + count * away * away, axis=0, keepdims=True) * (1.0 / (peers * count))
    return mean, lax.rsqrt(spread + norm_eps)


def stat_columns(found, count):
    return columns_of(list(pooled_stats(found[:, 0, :], found[:, 1, :], count)))


def sum_rows(found, lines):
    return [jnp.sum(found[:, index, :], axis=0, keepdims=True) for index in range(lines)]


def own_half(row, scene, out):
    size = out.shape[0]
    out[...] = jnp.where(scene == 0, row[:, 0:size], row[:, size : 2 * size]).reshape(size)


def edges(channels, width):
    lane = lax.broadcasted_iota(jnp.int32, (channels, width), 1)
    return lane > 0, lane < width - 1


def spread(row, masks):
    zero = jnp.zeros_like(row)
    left = jnp.where(masks[0], pltpu.roll(row, 1, 1), zero)
    right = jnp.where(masks[1], pltpu.roll(row, row.shape[1] - 1, 1), zero)
    return jnp.concatenate([left, row, right], axis=0)


def layout(half, channels):
    first = 0
    second = first + half * -(-9 * channels // LANES)
    up = second + half * -(-9 * channels // LANES)
    vectors = up + channels
    return first, second, up, vectors, vectors + 16


def widen(value):
    missing = LANES - value.shape[1]
    if missing == 0:
        return value
    return jnp.concatenate([value, jnp.zeros((value.shape[0], missing), value.dtype)], axis=1)


def pack(held, out):
    first, second, up, pillar = held[:4]
    half, channels = first.shape[0], up.shape[1]
    starts = layout(half, channels)
    for ref, start in ((first, starts[0]), (second, starts[1])):
        for j in range(-(-9 * channels // LANES)):
            out[start + j * half : start + (j + 1) * half, :] = widen(
                ref[:, j * LANES : min((j + 1) * LANES, 9 * channels)]
            )
    out[starts[2] : starts[2] + channels, :] = widen(up[...])
    rows = [vector[...].astype(F32).reshape(1, -1) for vector in held[4:]]
    rows = [widen(row) for row in rows] + [jnp.zeros((16 - len(rows), LANES), F32)]
    turned = widen(pillar[...].astype(F32))
    rows += [turned, jnp.zeros((16 - turned.shape[0], LANES), F32)]
    out[starts[3] :, :] = jnp.concatenate(rows, axis=0).astype(BF16)


def unpack_kernel(
    both, w_pillar, cols, l_first, l_second, b_first, b_second, w_up, w_up_t,
    h_second, h_first_back, h_second_back, sems, *, inputs
):
    half = w_pillar.shape[0] // 2
    channels = 2 * half
    starts = layout(half, channels)
    tiles = -(-9 * channels // LANES)

    def wide(start):
        return jnp.concatenate(
            [
                jnp.concatenate(
                    [both[s, start + j * half : start + (j + 1) * half, :] for j in range(tiles)], axis=1
                )
                for s in range(2)
            ],
            axis=0,
        ).astype(F32)

    up = jnp.concatenate(
        [both[s, starts[2] : starts[2] + channels, 0:channels] for s in range(2)], axis=0
    )
    w_up[...] = up
    w_up_t[...] = jnp.transpose(up.astype(F32)).astype(BF16)
    turned = jnp.concatenate(
        [both[s, starts[4] : starts[4] + 16, 0:half].astype(F32) for s in range(2)], axis=1
    )
    w_pillar[...] = jnp.transpose(widen(turned))[0:channels, 0:inputs].astype(BF16)
    vectors = [both[s, starts[3] : starts[3] + 16, :].astype(F32) for s in range(2)]
    rows = []
    for index in range(8):
        size = half if index < 6 else channels
        row = jnp.concatenate([vectors[s][index : index + 1, 0:size] for s in range(2)], axis=1)
        rows.append(jnp.concatenate([row] * (LANES // (2 * size)), axis=1))
    cols[...] = columns_of(rows)
    zero = jnp.zeros((channels, 3 * channels), F32)
    copies = []
    for weight, ahead, back in (
        (wide(starts[0]), l_first, h_first_back), (wide(starts[1]), h_second, h_second_back)
    ):
        weight = weight[:, : 9 * channels]
        turned = jnp.transpose(weight)
        flipped = jnp.concatenate(
            [turned[tap * channels : (tap + 1) * channels] for tap in range(8, -1, -1)], axis=1
        )
        for ref, taps in ((ahead, weight), (back, flipped)):
            ref[0:channels, :] = jnp.concatenate([taps, zero], axis=1).astype(BF16)
            ref[channels : 2 * channels, :] = jnp.concatenate([zero, taps], axis=1).astype(BF16)
    copies.append(move(h_second, l_second, sems, 0))
    copies.append(move(h_first_back, b_first, sems, 1))
    copies.append(move(h_second_back, b_second, sems, 2))
    for copy in copies:
        copy.wait()


def slot_line(wide, depth, inputs):
    return jnp.concatenate([wide[pl.ds(n, inputs, stride=depth), :] for n in range(depth)], axis=1)


def slot_mask(count, depth):
    return jnp.concatenate([jnp.where(count > n, 1.0, 0.0) for n in range(depth)], axis=1)


def ranks(tile):
    pillars = tile.shape[1]
    across = jnp.broadcast_to(tile, (pillars, pillars))
    down = jnp.transpose(across)
    row = lax.broadcasted_iota(jnp.int32, (pillars, pillars), 0)
    col = lax.broadcasted_iota(jnp.int32, (pillars, pillars), 1)
    return jnp.sum(jnp.where((across == down) & (row < col), 1.0, 0.0), axis=0, keepdims=True)


def moments_kernel(*refs, capacity):
    number = 16
    sources, out, packed, lines_out = refs[:number], *refs[number : number + 3]
    held, wide, sems = refs[number + 3 : 2 * number + 3], refs[-2], refs[-1]
    copies = [move(sources[i], held[i], sems, i) for i in range(number)]
    tiles, cells, counts, points = held[:4]
    micros, _, inputs, depth, pillars = points.shape
    peers, scenes = out.shape[:2]
    copies[0].wait()
    copies[1].wait()
    lines, slot_rows = [], []
    for micro in range(micros):
        tile = tiles[micro].astype(F32)
        cell = (cells[micro] + 1).astype(F32)
        high = jnp.floor(cell * (1.0 / 16.0))
        low = cell - high * 16.0
        rank = ranks(tile)
        slot_rows.append(tile * capacity + rank)
        spot = lax.broadcasted_iota(jnp.int32, (capacity, pillars), 0).astype(F32)
        placed = jnp.where(spot == rank, 1.0, 0.0).astype(BF16)
        peer = lax.broadcasted_iota(jnp.int32, (peers, pillars), 0).astype(F32)
        for group in range(3):
            named = tile == peer + (group - 1.0)
            lines.append(
                16.0 * dot_lanes(jnp.where(named, high, 0.0).astype(BF16), placed)
                + dot_lanes(jnp.where(named, low, 0.0).astype(BF16), placed)
            )
    used = 3 * micros * capacity
    line = jnp.concatenate(lines + [jnp.zeros((peers, LANES - used), F32)], axis=1).reshape(peers, 1, LANES)
    for scene in range(scenes):
        out[:, scene, micros : micros + 1, :] = line
    copies[2].wait()
    copies[3].wait()
    parts, mean_rows, totals = [], [], []
    for micro in range(micros):
        wide[...] = points[micro, 0].astype(F32).reshape(inputs * depth, pillars)
        rows = slot_line(wide, depth, inputs)
        notes = jnp.concatenate([slot_rows[micro], counts[micro].astype(F32)], axis=0)
        notes = jnp.concatenate([notes, jnp.zeros((2, rows.shape[1] - pillars), F32)], axis=1)
        lines_out[micro] = jnp.concatenate(
            [rows, notes, jnp.zeros((14 - inputs, rows.shape[1]), F32)], axis=0
        ).astype(BF16)
        mask = slot_mask(counts[micro], depth)
        total = jnp.sum(mask, axis=1, keepdims=True)
        mean = jnp.sum(rows * mask, axis=1, keepdims=True) / total
        centred = jnp.concatenate(
            [(rows - mean) * mask, jnp.zeros((16 - inputs, rows.shape[1]), F32)], axis=0
        )
        high = centred.astype(BF16)
        parts += [high, (centred - high.astype(F32)).astype(BF16)]
        lane = lax.broadcasted_iota(jnp.int32, (inputs, inputs), 1)
        diagonal = lax.broadcasted_iota(jnp.int32, (inputs, inputs), 0) == lane
        mean_rows.append(jnp.sum(jnp.where(diagonal, mean, 0.0), axis=0, keepdims=True))
        totals.append(total)
    parts = jnp.concatenate(parts, axis=0)
    every = dot_lanes(parts, parts)
    for micro in range(micros):
        at = 32 * micro
        square = every[at : at + 32, at : at + 32]
        products = (
            square[0:inputs, 0:inputs] + square[16 : 16 + inputs, 0:inputs]
            + square[0:inputs, 16 : 16 + inputs] + square[16 : 16 + inputs, 16 : 16 + inputs]
        )
        row = jnp.concatenate(
            [products[k : k + 1] for k in range(inputs)]
            + [mean_rows[micro], totals[micro], jnp.zeros((1, LANES - inputs * inputs - inputs - 1), F32)],
            axis=1,
        )
        for scene in range(scenes):
            out[:, scene, micro : micro + 1, :] = jnp.broadcast_to(row[None], (peers, 1, LANES))
    for copy in copies[4:]:
        copy.wait()
    pack(held[4:], packed)


def cells_kernel(found, columns, rows, *, capacity):
    scene = lax.axis_index("scene")
    slots = columns.shape[0]
    peers = found.shape[0]
    values = found[:, 2, :]
    slot = lax.broadcasted_iota(jnp.int32, (slots, peers), 0)
    peer = lax.broadcasted_iota(jnp.int32, (slots, peers), 1)
    lane = lax.broadcasted_iota(jnp.int32, (slots, LANES), 1)
    row = lax.broadcasted_iota(jnp.int32, (slots, LANES), 0)
    result = jnp.zeros((slots, LANES), F32)
    chosen = jnp.where(peer == 2 * (slot // capacity) + scene, 1.0, 0.0)
    spread = dot(chosen, values, lax.Precision.HIGHEST)
    for micro in range(2):
        for group in range(3):
            mine = jnp.where(lane == (3 * micro + group) * capacity + row % capacity, spread, 0.0)
            column = jnp.sum(mine, axis=1, keepdims=True)
            result = jnp.where(lane == 2 * group + micro, column, result)
    columns[...] = result
    rows[...] = jnp.transpose(result)[0:8]


def pillar_notes(rows, micro, inputs, pillars):
    notes = rows[micro, :, 0:pillars].astype(F32)
    return notes[inputs : inputs + 1], notes[inputs + 1 : inputs + 2]


def pillar_kernel(
    found, point_rows, w_pillar, cols, send, pooled, lifted, acts, *, capacity
):
    micros = point_rows.shape[0]
    channels, inputs = w_pillar.shape
    pillars = pooled.shape[2]
    depth = point_rows.shape[2] // pillars
    weight = w_pillar[...]
    wide_weight = weight.astype(F32)
    rows_out = send.shape[0]
    square = inputs * inputs
    stacked, slot_rows = [], []
    for micro in range(micros):
        lifted[...] = dot(weight, point_rows[micro, 0:inputs])
        moments = found[:, micro, :]
        sizes = moments[:, square + inputs : square + inputs + 1]
        means = moments[:, square : square + inputs]
        count = jnp.sum(sizes, axis=0, keepdims=True)
        mean = jnp.sum(means * sizes, axis=0, keepdims=True) / count
        away = means - mean
        products = lax.dot_general(
            away * sizes, away, (((0,), (0,)), ((), ())),
            preferred_element_type=F32, precision=lax.Precision.HIGHEST,
        )
        summed = jnp.sum(moments, axis=0, keepdims=True)
        products = products + jnp.concatenate(
            [summed[:, k * inputs : (k + 1) * inputs] for k in range(inputs)], axis=0
        )
        cov = products / count
        spun = wide_weight[:, 0:1] * cov[0:1]
        for k in range(1, inputs):
            spun = spun + wide_weight[:, k : k + 1] * cov[k : k + 1]
        spread = jnp.sum(spun * wide_weight, axis=1, keepdims=True)
        centre = jnp.sum(wide_weight * mean, axis=1, keepdims=True)
        rstd = lax.rsqrt(spread + norm_eps)
        inverse = jnp.broadcast_to(1.0 / count, (channels, 1))
        pooled[micros + micro] = jnp.concatenate(
            [
                centre, rstd, inverse, jnp.zeros((channels, 13), F32),
                spun, jnp.zeros((channels, 16 - inputs), F32),
                jnp.broadcast_to(mean, (channels, inputs)), jnp.zeros((channels, LANES - 32 - inputs), F32),
            ],
            axis=1,
        )
        scale = rstd * cols[0:channels, 0:1]
        shift = cols[0:channels, 1:2]
        slot, limit = pillar_notes(point_rows, micro, inputs, pillars)
        slot_rows.append(slot)
        top = jnp.full((channels, pillars), -jnp.inf, F32)
        for n in range(depth):
            piece = slice(n * pillars, (n + 1) * pillars)
            normed = (lifted[:, piece] - centre) * scale + shift
            act = normed * sigmoid(normed)
            acts[:, piece] = act
            top = jnp.maximum(top, jnp.where(limit > n, act, -jnp.inf))
        total = jnp.zeros((channels, pillars), F32)
        for n in range(depth):
            piece = slice(n * pillars, (n + 1) * pillars)
            total = total + jnp.where(limit > n, jnp.exp(acts[:, piece] - top), 0.0)
        result = top + jnp.log(total)
        pooled[micro] = result
        parts = [jnp.zeros((channels, pillars), F32)] * micros
        parts[micro] = result.astype(BF16).astype(F32)
        stacked.append(jnp.transpose(jnp.concatenate(parts, axis=0)))
    values = jnp.concatenate(stacked, axis=0).astype(BF16)
    for group in range(3):
        place = lax.broadcasted_iota(jnp.int32, (rows_out, pillars), 0) + (group - 1) * capacity
        chosen = jnp.concatenate(
            [jnp.where(place.astype(F32) == row, 1.0, 0.0) for row in slot_rows], axis=1
        ).astype(BF16)
        send[:, group * LANES : (group + 1) * LANES] = dot(chosen, values).astype(BF16)


def own_stats(ref, first_row, rows, send):
    micros, _, channels, width = ref.shape
    sums, squares = [], []
    for micro in range(micros):
        total = fold(ref[micro, first_row])
        for row in range(first_row + 1, first_row + rows):
            total = total + fold(ref[micro, row])
        total = total * (1.0 / (rows * width))
        mean = jnp.sum(total, axis=1, keepdims=True)
        spread = jnp.zeros(total.shape, F32)
        for row in range(first_row, first_row + rows):
            away = ref[micro, row] - mean
            spread = spread + fold(away * away)
        sums.append(total)
        squares.append(spread)
    if channels == LANES:
        send_all(send, [row_of(part) for part in sums + squares])
    else:
        send_all(send, [row_of(*sums), row_of(*squares)])


def conv_pair(source, weight, micro, at, channels):
    window = source[micro, at : at + 4].reshape(12 * channels, source.shape[3])
    return dot(weight[...], window)


def conv_rows(source, weight, out, shape):
    micros, high, channels, width = shape
    for micro in range(micros):
        for at in range(0, high, 2):
            both = conv_pair(source, weight, micro, at, channels)
            out[micro, at] = both[:channels].astype(out.dtype)
            out[micro, at + 1] = both[channels:].astype(out.dtype)


def canvas_kernel(found, columns, where_rows, l_first, out, kept, send, canvas, *, rows):
    scenes, high, channels, width = out.shape
    masks = edges(channels, width)
    slots = found.shape[0]
    lane = lax.broadcasted_iota(jnp.int32, (slots, width), 1).astype(F32)
    for group in range(3):
        values = jnp.transpose(found[:, group * LANES : (group + 1) * LANES].astype(F32))
        first, count = ((rows - 2, 2), (0, rows), (0, 2))[group]
        for scene in range(scenes):
            at = 2 * group + scene
            column = columns[:, at : at + 1] - 1.0
            column = column - jnp.floor(column * (1.0 / width)) * width
            row = jnp.floor((where_rows[at : at + 1] - 1.0) * (1.0 / width))
            mine = values[scene * channels : (scene + 1) * channels]
            placed = jnp.concatenate(
                [jnp.where(row == r * 1.0, mine, 0.0) for r in range(first, first + count)], axis=0
            ).astype(BF16)
            chosen = jnp.where(lane == column, 1.0, 0.0).astype(BF16)
            grid = dot(placed, chosen).astype(BF16)
            start = (0, 2, rows + 2)[group]
            for r in range(count):
                row = grid[r * channels : (r + 1) * channels]
                canvas[scene, start + r] = spread(row, masks)
                if 1 <= start + r <= rows + 2:
                    kept[scene, start + r - 1] = row
    conv_rows(canvas, l_first, out, out.shape)
    own_stats(out, 1, rows, send)


def second_kernel(found, cols, first_out, l_second_in, out, kept, slopes, stats, send, acts, l_second, sems,
                  *, rows, tiles):
    weight_copy = move(l_second_in, l_second, sems, 0)
    micros, high, channels, width = first_out.shape
    tile = lax.axis_index("tile")
    turned = stat_columns(found, float(rows * width))
    stats[...] = turned
    masks = edges(channels, width)
    for micro in range(micros):
        part = slice(micro * channels, (micro + 1) * channels)
        centre = turned[part, 0:1]
        scale = turned[part, 1:2] * cols[0:channels, 2:3]
        shift = cols[0:channels, 3:4]

        for row in range(high):
            normed = (first_out[micro, row] - centre) * scale + shift
            gate = sigmoid(normed)
            act = normed * gate
            slopes[micro, row] = gate + act * (1.0 - gate)
            if row == 0 or row == high - 1:
                act = act * inside(tile, row - 1, (tiles, rows))
            act = act.astype(BF16)
            acts[micro, row] = spread(act, masks)
            kept[micro, row] = act
    weight_copy.wait()
    conv_rows(acts, l_second, out, out.shape)
    own_stats(out, 0, rows, send)


def up_kernel(found, cols, second_out, w_up, acts, upper, slopes, plain, crossed, stats, send, *, rows):
    micros, _, channels, width = second_out.shape
    peers = send.shape[0]
    each = crossed.shape[0] // peers
    turned = stat_columns(found, float(rows * width))
    stats[...] = turned
    gain, shift = cols[0:channels, 4:5], cols[0:channels, 5:6]
    lines = []
    for micro in range(micros):
        part = slice(micro * channels, (micro + 1) * channels)
        centre, rstd = turned[part, 0:1], turned[part, 1:2]
        slope_sum = jnp.zeros((channels, LANES), F32)
        unit_sum = jnp.zeros((channels, LANES), F32)
        for row in range(rows):
            unit = (second_out[micro, row] - centre) * rstd
            normed = unit * gain + shift
            gate = sigmoid(normed)
            act = normed * gate
            slope = gate + act * (1.0 - gate)
            sloped = slope * unit
            slope_sum = slope_sum + fold(slope)
            unit_sum = unit_sum + fold(sloped)
            slopes[micro, row] = jnp.concatenate([slope, sloped], axis=0)
            act = act.astype(BF16)
            acts[micro, row] = act
            upper[micro, row] = dot(w_up[...], act)
        lines.append(row_of(slope_sum, unit_sum).astype(BF16).astype(F32))
        crossed[micro * channels : (micro + 1) * channels] = dot_lanes(
            jnp.concatenate([acts[micro, row] for row in range(rows)], axis=1),
            jnp.concatenate([slopes[micro, row].astype(BF16) for row in range(rows)], axis=1),
        )
    plain[...] = jnp.concatenate(lines, axis=0)
    used = micros * channels
    if crossed.shape[0] > used:
        crossed[used:] = jnp.zeros((crossed.shape[0] - used, LANES), F32)
    if 2 * micros + each < send.shape[1]:
        send[...] = jnp.zeros(send.shape, F32)
    for peer in range(peers):
        send[peer, 2 * micros : 2 * micros + each] = crossed[peer * each : (peer + 1) * each]
    own_stats(upper, 0, rows, send)


def exact_rows(rows):
    high = rows.astype(BF16).astype(F32)
    return [high, rows - high]


def top_kernel(found, cols, upper, cot, slopes, plain, w_up_t, features, grads, mixed, stats, send, *, rows, each):
    micros, _, wide, width = upper.shape
    channels = w_up_t.shape[0]
    lines = []
    for micro in range(micros):
        lines += list(pooled_stats(found[:, micro, :], found[:, micros + micro, :], float(rows * width)))
    turned = columns_of(lines)
    stats[...] = turned
    gain, shift = cols[:, 6:7], cols[:, 7:8]
    gain_rows, shift_rows, mixed_rows = [], [], []
    for micro in range(micros):
        centre, rstd = turned[:, 2 * micro : 2 * micro + 1], turned[:, 2 * micro + 1 : 2 * micro + 2]
        factor = gain * rstd
        gain_sum = jnp.zeros((wide, LANES), F32)
        shift_sum = jnp.zeros((wide, LANES), F32)
        mixed_sum = jnp.zeros((2 * channels, LANES), F32)
        for row in range(rows):
            unit = (upper[micro, row] - centre) * rstd
            normed = unit * gain + shift
            gate = sigmoid(normed)
            act = normed * gate
            grad = cot[micro, row].astype(F32) * (gate + act * (1.0 - gate))
            features[micro, row] = act.astype(BF16)
            grads[micro, row] = grad
            gain_sum = gain_sum + fold(grad * unit)
            shift_sum = shift_sum + fold(grad)
            below = dot(w_up_t[...], (grad * factor).astype(BF16))
            mixed_sum = mixed_sum + fold(
                slopes[micro, row] * jnp.concatenate([below, below], axis=0)
            )
        gain_rows.append(row_of(gain_sum))
        shift_rows.append(row_of(shift_sum))
        mixed_rows.append(row_of(mixed_sum).astype(BF16).astype(F32))
    mixed[...] = jnp.concatenate(mixed_rows, axis=0)
    rows_out = jnp.concatenate(gain_rows + shift_rows, axis=0)
    crossed = jnp.sum(found[:, 2 * micros : 2 * micros + each, :], axis=0)
    rest = send.shape[1] - 6 * micros - each
    block = exact_rows(rows_out) + mixed_rows + [plain[...], crossed]
    if rest > 0:
        block.append(jnp.zeros((rest, LANES), F32))
    block = jnp.concatenate(block, axis=0)
    send[...] = jnp.broadcast_to(block.astype(BF16)[None], send.shape)


def low_rows(turned, value_of, values, stats, gain, low, high, first, rows, tiles):
    micros, _, channels, width = values.shape
    tile = lax.axis_index("tile")
    masks = edges(channels, width)
    for micro in range(micros):
        part = slice(micro * channels, (micro + 1) * channels)
        centre, rstd = stats[part, 0:1], stats[part, 1:2]
        factor = gain * rstd
        slope_part, shift_part = rstd * turned[part, 0:1], turned[part, 1:2]
        for index in range(high):
            grad, value = value_of(micro, index)
            grad = factor * (grad - shift_part - (value - centre) * slope_part)
            if index + first < 0 or index + first >= rows:
                grad = grad * inside(tile, index + first, (tiles, rows))
            low[micro, index] = spread(grad.astype(BF16), masks)


def first_units(first_out, stats, micro, channels):
    part = slice(micro * channels, (micro + 1) * channels)
    centre, rstd = stats[part, 0:1], stats[part, 1:2]
    return lambda row: (first_out[micro, row] - centre) * rstd


def second_sums(total, weight, factors, stats, micro, micros, count):
    channels = weight.shape[1]
    factor, centre = factors[micro], stats[:, 2 * micro : 2 * micro + 1]
    columns = jnp.transpose(jnp.concatenate([total, jnp.zeros((8 - total.shape[0], LANES), F32)], axis=0))
    beta = factor * stats[:, 2 * micro + 1 : 2 * micro + 2] * columns[:, micro : micro + 1] * (1.0 / count)
    alpha = factor * columns[:, micros + micro : micros + micro + 1] * (1.0 / count)
    square = lax.dot_general(
        weight * beta, weight, (((0,), (0,)), ((), ())),
        preferred_element_type=F32, precision=lax.Precision.HIGHEST,
    )
    square = jnp.concatenate([square, square], axis=1)
    line = jnp.sum(weight * (alpha - beta * centre), axis=0, keepdims=True)
    line = jnp.concatenate([line, line], axis=1)

    def give(mixed, plain, crossed):
        mine = crossed[micro * channels : (micro + 1) * channels]
        return mixed - plain * line - jnp.sum(square * mine, axis=0, keepdims=True)

    return give


def middle_back_kernel(
    found, cols, grads, upper, top_stats, second_out, second_stats, slopes, w_up, w_up_t,
    own_mixed, own_plain, own_crossed,
    low, top_low, rising, falling, top_gain_grad, top_shift_grad, expected, extras, second_dz, *, rows, each
):
    scene = lax.axis_index("scene")
    micros, _, wide, width = grads.shape
    channels = second_out.shape[2]
    peers = found.shape[0]
    count = float(peers * rows * width)
    kept = 2 * micros
    total = jnp.sum(found[...].astype(F32), axis=0)
    mixed, plain = total[2 * kept : 2 * kept + micros], total[2 * kept + micros : 3 * kept]
    total = total[0:kept] + total[kept : 2 * kept]
    crossed = jnp.concatenate(
        [
            found[peer].astype(F32)[3 * kept : 3 * kept + each]
            for peer in range(-(-micros * channels // each))
        ],
        axis=0,
    )
    own_half(total[0:1] + total[1:2], scene, top_gain_grad)
    own_half(total[2:3] + total[3:4], scene, top_shift_grad)
    factors = [cols[:, 6:7] * top_stats[:, 2 * micro + 1 : 2 * micro + 2] for micro in range(micros)]
    wide_weight = w_up[...].astype(F32)
    turned = columns_of([total[index : index + 1] for index in range(2 * micros)]) * (1.0 / count)
    gain = cols[0:channels, 4:5]
    masks = edges(channels, width)
    for micro in range(micros):
        top_centre = top_stats[:, 2 * micro : 2 * micro + 1]
        top_slope = top_stats[:, 2 * micro + 1 : 2 * micro + 2] * turned[:, micro : micro + 1]
        top_shift = turned[:, micros + micro : micros + micro + 1]
        part = slice(micro * channels, (micro + 1) * channels)
        centre, rstd = second_stats[part, 0:1], second_stats[part, 1:2]
        gain_sum = jnp.zeros((channels, LANES), F32)
        shift_sum = jnp.zeros((channels, LANES), F32)
        for row in range(rows):
            grad = factors[micro] * (
                grads[micro, row] - top_shift - (upper[micro, row] - top_centre) * top_slope
            )
            grad = grad.astype(BF16)
            top_low[micro, row] = grad
            unit = (second_out[micro, row] - centre) * rstd
            grad = dot(w_up_t[...], grad) * slopes[micro, row, 0:channels]
            second_dz[micro, row] = grad
            shift_sum = shift_sum + fold(grad)
            gain_sum = gain_sum + fold(grad * unit)
        give = second_sums(total, wide_weight, factors, top_stats, micro, micros, count)
        whole = give(mixed[micro : micro + 1], plain[micro : micro + 1], crossed)
        extra = row_of(shift_sum, gain_sum) - give(
            own_mixed[micro : micro + 1], own_plain[micro : micro + 1], own_crossed[...]
        )
        expected[micro : micro + 1] = whole
        extras[micro : micro + 1] = extra
        part = columns_of([whole * (1.0 / count) + extra * (1.0 / (rows * width))])
        shift_part, gain_part = part[0:channels, 0:1], part[channels : 2 * channels, 0:1]
        for row in range(rows):
            unit = (second_out[micro, row] - centre) * rstd
            grad = (gain * rstd) * (second_dz[micro, row] - shift_part - unit * gain_part)
            low[micro, row] = spread(grad.astype(BF16), masks)
    for micro in range(micros):
        for row in range(2):
            falling[micro, row] = low[micro, row, channels : 2 * channels]
            rising[micro, row] = low[micro, rows - 2 + row, channels : 2 * channels]


def first_back_kernel(
    low, top_low, second_act, acts, first_out, first_stats, slopes, b_second_in, extras,
    out, top_grad, weight_grad, send, b_second, sems, *, rows, tiles
):
    weight_copy = move(b_second_in, b_second, sems, 0)
    tile = lax.axis_index("tile")
    micros, _, channels, width = first_out.shape
    weight_copy.wait()
    half = 6 * channels
    gain_sums, shift_sums = [], []
    for micro in range(micros):
        units = first_units(first_out, first_stats, micro, channels)
        gain_sum = jnp.zeros((channels, LANES), F32)
        shift_sum = jnp.zeros((channels, LANES), F32)
        for at in range(0, rows + 2, 2):
            if at == 0:
                parts = dot(b_second[:, half:], low[micro, 0:2].reshape(half, width))
            elif at == rows:
                parts = dot(b_second[:, :half], low[micro, rows - 2 : rows].reshape(half, width))
            else:
                parts = conv_pair(low, b_second, micro, at - 2, channels)
            for j in range(2):
                grad = parts[channels * j : channels * (j + 1)] * slopes[micro, at + j]
                if at + j == 0 or at + j == rows + 1:
                    grad = grad * inside(tile, at + j - 1, (tiles, rows))
                out[micro, at + j] = grad
                gain_sum = gain_sum + fold(grad * units(at + j))
                shift_sum = shift_sum + fold(grad)
        gain_sums.append(gain_sum)
        shift_sums.append(shift_sum)
        product = dot_lanes(
            jnp.concatenate([top_low[micro, row] for row in range(rows)], axis=1),
            jnp.concatenate([second_act[micro, row] for row in range(rows)], axis=1),
        )
        top_grad[...] = product if micro == 0 else top_grad[...] + product
    conv_grad(low, 0, acts, 0, weight_grad, rows)
    send_all(send, [row_of(*gain_sums), row_of(*shift_sums)] + [extras[m : m + 1] for m in range(micros)])


def conv_grad(low, low_first, values, value_first, total, rows):
    micros, _, channels, width = values.shape
    for micro in range(micros):
        grads = jnp.concatenate([low[micro, row + low_first] for row in range(rows)], axis=1)
        windows = jnp.concatenate(
            [
                values[micro, row + value_first : row + value_first + 3].reshape(3 * channels, width)
                for row in range(rows)
            ],
            axis=1,
        )
        product = dot_lanes(grads, windows)
        total[...] = product if micro == 0 else total[...] + product


def half_rows(total, half, scene):
    channels = 2 * half
    start = scene * half
    mine = jnp.concatenate(
        [total[b * channels + start : b * channels + start + half, :] for b in range(2, -1, -1)], axis=0
    )
    wing = mine[:, LANES:]
    cut = wing.shape[0] // 2
    return [mine[:, :LANES], jnp.concatenate([wing[:cut], wing[cut:]], axis=1)]


def pick_kernel(
    found, cols, grads, before, after, first_out, first_stats, slopes, b_first_in, b_second_in, columns, where_rows,
    canvas, second_grad, top_grad, expected,
    send, gain_grad, shift_grad, second_gain_grad, second_shift_grad, low, grid, b_first, b_second, halo, first_grad, whole, sems,
    *, rows, tiles, each
):
    second_copy = move(b_second_in, b_second, sems, 1)
    weight_copy = move(b_first_in, b_first, sems, 0)
    scene = lax.axis_index("scene")
    micros, _, channels, width = grads.shape
    sums = sum_rows(found, 2 + micros)
    second = sum(sums[2:]) + jnp.sum(expected[...], axis=0, keepdims=True)
    own_half(second[:, :channels], scene, second_shift_grad)
    own_half(second[:, channels:], scene, second_gain_grad)
    sums = sums[:2]
    own_half(sums[0][:, :channels] + sums[0][:, channels:], scene, gain_grad)
    own_half(sums[1][:, :channels] + sums[1][:, channels:], scene, shift_grad)
    turned = columns_of(sums) * (1.0 / (found.shape[0] * rows * width))
    masks = edges(channels, width)
    half = 6 * channels
    second_copy.wait()
    for micro in range(micros):
        for at, ref, columns_used in ((0, before, slice(0, half)), (rows, after, slice(half, 2 * half))):
            window = jnp.concatenate([spread(ref[micro, row], masks) for row in range(2)], axis=0)
            parts = dot(b_second[:, columns_used], window)
            for j in range(2):
                halo[micro, at + j] = parts[channels * j : channels * (j + 1)] * slopes[micro, at + j]

    def value_of(micro, index):
        grad = grads[micro, index]
        if index < 2 or index >= rows:
            grad = grad + halo[micro, index]
        return grad, first_out[micro, index]

    low_rows(turned, value_of, first_out, first_stats, cols[0:channels, 2:3], low, rows + 2, -1, rows, tiles)
    weight_copy.wait()
    conv_rows(low, b_first, grid, grid.shape)
    conv_grad(low, 1, canvas, 0, first_grad, rows)
    half = channels // 2
    peers, block = send.shape[:2]
    for s in range(2):
        parts = half_rows(first_grad, half, s) + half_rows(second_grad, half, s)
        mine = top_grad[s * channels : (s + 1) * channels, :]
        parts.append(jnp.concatenate([mine[:half], mine[half:]], axis=1))
        parts = jnp.concatenate(parts, axis=0)
        whole[s, 0 : parts.shape[0]] = parts
        if whole.shape[1] > parts.shape[0]:
            whole[s, parts.shape[0] :] = jnp.zeros((whole.shape[1] - parts.shape[0], LANES), F32)
    slots = columns.shape[0]
    lane = lax.broadcasted_iota(jnp.int32, (slots, width), 1).astype(F32)
    picked = []
    for micro in range(micros):
        at = 2 + micro
        column = columns[:, at : at + 1] - 1.0
        column = column - jnp.floor(column * (1.0 / width)) * width
        place = jnp.floor((where_rows[at : at + 1] - 1.0) * (1.0 / width))
        chosen = jnp.where(lane == column, 1.0, 0.0).astype(BF16)
        here = dot_lanes(grid[micro].reshape(rows * channels, width), chosen)
        total = jnp.zeros((channels, slots), F32)
        for r in range(rows):
            total = total + jnp.where(place == r * 1.0, here[r * channels : (r + 1) * channels], 0.0)
        picked.append(total)
    picked = jnp.transpose(jnp.concatenate(picked, axis=0))
    capacity = slots // tiles
    rest = block - capacity - 2 * each
    for peer in range(peers):
        spot = peer // 2
        parts = [picked[spot * capacity : (spot + 1) * capacity]]
        parts += [whole[s, peer * each : (peer + 1) * each] for s in range(2)]
        parts.append(jnp.zeros((rest, LANES), F32))
        send[peer] = jnp.concatenate(parts, axis=0).astype(BF16)


def pillar_back_kernel(found, rows_in, w_pillar, cols, pooled, send, grads, lifted, rows, sems,
                       *, capacity, each):
    fetched = move(rows_in, rows, sems, 0)
    micros = rows.shape[0]
    _, channels, pillars = pooled.shape
    stats = pooled.at[micros : 2 * micros]
    inputs = w_pillar.shape[1]
    depth = rows.shape[2] // pillars
    scene = lax.axis_index("scene")
    peers = found.shape[0]
    slot_count = peers // 2 * capacity
    returned = jnp.concatenate(
        [found[2 * t + scene].astype(F32)[0:capacity] for t in range(peers // 2)], axis=0
    )
    turned = jnp.transpose(returned)
    place = lax.broadcasted_iota(jnp.int32, (slot_count, pillars), 0).astype(F32)
    gain, shift = cols[0:channels, 0:1], cols[0:channels, 1:2]
    gain_sums, shift_sums = [], []
    outer = jnp.zeros((16, channels), F32)
    fetched.wait()
    for micro in range(micros):
        lifted[...] = dot(w_pillar[...], rows[micro, 0:inputs])
        slot, limit = pillar_notes(rows, micro, inputs, pillars)
        chosen = jnp.where(place == slot, 1.0, 0.0).astype(BF16)
        back = dot(turned[micro * channels : (micro + 1) * channels].astype(BF16), chosen)
        centre, rstd = stats[micro, :, 0:1], stats[micro, :, 1:2]
        pool = pooled[micro]
        gain_sum = jnp.zeros((channels, pillars), F32)
        shift_sum = jnp.zeros((channels, pillars), F32)
        for n in range(depth):
            piece = slice(n * pillars, (n + 1) * pillars)
            unit = (lifted[:, piece] - centre) * rstd
            normed = unit * gain + shift
            gate = sigmoid(normed)
            act = normed * gate
            slope = gate + act * (1.0 - gate)
            grad = jnp.where(limit > n, back * jnp.exp(act - pool) * slope, 0.0)
            grads[micro, :, piece] = grad
            gain_sum = gain_sum + grad * unit
            shift_sum = shift_sum + grad
        gain_sums.append(gain_sum)
        shift_sums.append(shift_sum)
        scale = jnp.transpose(jnp.broadcast_to(rstd * gain, (channels, LANES)))[0:1]
        outer = outer + dot_lanes(rows[micro], grads[micro].astype(BF16)) * scale
    lines = [row_of(*gain_sums), row_of(*shift_sums)]
    for k in range(0, 10, 2):
        lines.append(jnp.concatenate([outer[k : k + 1], outer[k + 1 : k + 2]], axis=1))
    exact = jnp.concatenate(lines, axis=0)
    kept = 2 * exact.shape[0]
    weights = jnp.sum(found[...].astype(F32), axis=0)
    rest = send.shape[2] - kept - each
    for s in range(2):
        mine = weights[capacity + s * each : capacity + (s + 1) * each]
        block = exact_rows(exact) + [mine] + ([jnp.zeros((rest, LANES), F32)] if rest > 0 else [])
        block = jnp.concatenate(block, axis=0).astype(BF16)
        send[:, s] = jnp.broadcast_to(block[None], (send.shape[0],) + block.shape)


def points_kernel(
    found, rows_in, grads, w_pillar, cols, pooled,
    points_grad, pillar_grad, gain_grad, shift_grad, first_grad, second_grad, up_grad, rows, lifted, sems,
    *, each
):
    fetched = move(rows_in, rows, sems, 0)
    scene = lax.axis_index("scene")
    micros, channels, _ = grads.shape
    stats = pooled.at[micros : 2 * micros]
    _, _, inputs, depth, pillars = points_grad.shape
    half = channels // 2
    kept = 7
    total = jnp.sum(found[...].astype(F32), axis=0)
    total = total[0:kept] + total[kept : 2 * kept]
    own_half(total[0:1, :channels] + total[0:1, channels:], scene, gain_grad)
    own_half(total[1:2, :channels] + total[1:2, channels:], scene, shift_grad)
    turned = jnp.transpose(jnp.concatenate([total, jnp.zeros((1, LANES), F32)], axis=0))
    weight_grad = jnp.concatenate(
        [turned[(k % 2) * channels : (k % 2 + 1) * channels, 2 + k // 2 : 3 + k // 2] for k in range(inputs)],
        axis=1,
    )
    weight = jnp.transpose(w_pillar[...].astype(F32)).astype(BF16)
    fetched.wait()
    for micro in range(micros):
        lifted[...] = dot(w_pillar[...], rows[micro, 0:inputs])
        part = slice(micro * channels, (micro + 1) * channels)
        centre, rstd, inverse = stats[micro, :, 0:1], stats[micro, :, 1:2], stats[micro, :, 2:3]
        factor = cols[0:channels, 0:1] * rstd
        gain_part, shift_part = turned[part, 0:1], turned[part, 1:2]
        spun, mean = stats[micro, :, 16 : 16 + inputs], stats[micro, :, 32 : 32 + inputs]
        weight_grad = weight_grad - factor * (shift_part * mean + gain_part * rstd * spun)
        gain_part, shift_part = gain_part * inverse * rstd, shift_part * inverse
        _, limit = pillar_notes(rows, micro, inputs, pillars)
        for n in range(depth):
            piece = slice(n * pillars, (n + 1) * pillars)
            low = factor * (grads[micro, :, piece] - shift_part - (lifted[:, piece] - centre) * gain_part)
            low = jnp.where(limit > n, low, 0.0).astype(BF16)
            points_grad[micro, 0, :, n, :] = dot(weight, low)
    weight_grad = jnp.concatenate([weight_grad, jnp.zeros((channels, LANES - inputs), F32)], axis=1)
    weight_grad = jnp.transpose(weight_grad)[0:inputs]
    pillar_grad[...] = jnp.where(scene == 0, weight_grad[:, :half], weight_grad[:, half:])
    whole = jnp.concatenate(
        [found[peer].astype(F32)[2 * kept : 2 * kept + each] for peer in range(found.shape[0])], axis=0
    )
    for index, out in enumerate((first_grad, second_grad)):
        base = index * 9 * half * channels // LANES
        lead = 3 * half
        mine = whole[base : base + lead]
        wing = whole[base + lead : base + lead + lead // 2]
        wing = jnp.concatenate([wing[:, :channels], wing[:, channels:]], axis=0)
        both = jnp.concatenate([mine, wing], axis=1)
        for a in range(3):
            for b in range(3):
                at = (3 * a + b) * channels
                out[:, at : at + channels] = both[b * half : (b + 1) * half, a * channels : (a + 1) * channels]
    base = 2 * 9 * half * channels // LANES
    top = whole[base : base + half]
    up_grad[...] = jnp.concatenate([top[:, :channels], top[:, channels:]], axis=0)


def swap(blocks, axes):
    return lax.all_to_all(blocks, axes, split_axis=0, concat_axis=0)


def shards(
    points, point_counts, pillar_tile, pillar_cell,
    pillar_weight, pillar_gain, pillar_shift,
    first_weight, first_gain, first_shift,
    second_weight, second_gain, second_shift,
    up_weight, up_gain, up_shift, cotangent,
):
    micros, _, inputs, depth, pillars = points.shape
    channels = up_weight.shape[1]
    upper = cotangent.shape[2]
    rows, width = cotangent.shape[3:]
    tiles = lax.axis_size("tile")
    scenes = lax.axis_size("scene")
    peers = tiles * scenes
    capacity = 2 * pillars // tiles
    slot_count = tiles * capacity
    half = channels // 2

    def vmem(shape, dtype):
        return pltpu.VMEM(shape, dtype)

    def grid(high, dtype=F32, lead=channels):
        return ((micros, high, lead, width), dtype)

    sums = ((peers, 2, LANES), F32)
    sources = (
        pillar_tile, pillar_cell, point_counts, points,
        first_weight, second_weight, up_weight, pillar_weight.T,
        pillar_gain, pillar_shift, first_gain, first_shift, second_gain, second_shift, up_gain, up_shift,
    )
    moments, packed, point_rows = run(
        functools.partial(moments_kernel, capacity=capacity),
        [
            ((tiles, scenes, 4, LANES), F32), ((layout(half, channels)[-1] + 16, LANES), BF16),
            ((micros, 16, depth * pillars), BF16),
        ],
        *sources,
        hbm=range(len(sources)), copies=len(sources), limit=WIDE_LIMIT,
        scratch=[vmem(source.shape, source.dtype) for source in sources]
        + [vmem((inputs * depth, pillars), F32)],
    )
    moments = swap(moments.reshape(peers, 4, LANES), BOTH)
    both = lax.all_gather(packed, "scene")
    taps = ((2 * channels, 12 * channels), BF16)
    w_pillar, cols, l_first, l_second, b_first, b_second, w_up, w_up_t = run(
        functools.partial(unpack_kernel, inputs=inputs),
        [
            ((channels, inputs), BF16), ((LANES, 8), F32), taps, taps + (1,), taps + (1,), taps + (1,),
            ((upper, channels), BF16), ((channels, upper), BF16),
        ],
        both,
        scratch=[vmem(*taps), vmem(*taps), vmem(*taps)], copies=3,
    )
    cot = cotangent[:, 0].transpose(0, 2, 1, 3)

    send, pooled = run(
        functools.partial(pillar_kernel, capacity=capacity),
        [((slot_count, 3 * LANES), BF16), ((2 * micros, channels, pillars), F32)],
        moments, point_rows, w_pillar, cols,
        scratch=[vmem((channels, depth * pillars), F32), vmem((channels, depth * pillars), F32)],
    )
    arrived = swap(send.reshape(tiles, capacity, 3 * LANES), "tile").reshape(slot_count, 3 * LANES)
    cell_columns, cell_rows = run(
        functools.partial(cells_kernel, capacity=capacity),
        [((slot_count, LANES), F32), ((8, slot_count), F32)],
        moments,
        cost=pl.CostEstimate(flops=10**7, bytes_accessed=10**6, transcendentals=0),
    )
    arrived, cot = lax.optimization_barrier((arrived, cot))

    first_out, canvas, send = run(
        functools.partial(canvas_kernel, rows=rows),
        [grid(rows + 2), grid(rows + 2, BF16), sums],
        arrived, cell_columns, cell_rows, l_first,
        scratch=[vmem(*grid(rows + 4, BF16, 3 * channels))],
    )
    second_out, first_act, first_slopes, first_stats, send = run(
        functools.partial(second_kernel, rows=rows, tiles=tiles),
        [grid(rows), grid(rows + 2, BF16), grid(rows + 2), ((LANES, 8), F32), sums],
        swap(send, BOTH), cols, first_out, l_second,
        hbm=(3,), scratch=[vmem(*grid(rows + 2, BF16, 3 * channels)), vmem(*taps)], copies=1,
    )
    part = -(-micros * channels // peers)
    second_act, up_out, slopes, plain, crossed, second_stats, send = run(
        functools.partial(up_kernel, rows=rows),
        [
            grid(rows, BF16), grid(rows, F32, upper), grid(rows, F32, 2 * channels), ((micros, LANES), F32),
            ((peers * part, LANES), F32), ((LANES, 8), F32), ((peers, -(-(2 * micros + part) // 8) * 8, LANES), F32),
        ],
        swap(send, BOTH), cols, second_out, w_up,
    )
    features, grads, mixed, top_stats, send = run(
        functools.partial(top_kernel, rows=rows, each=part),
        [
            grid(rows, BF16, upper), grid(rows, F32, upper), ((micros, LANES), F32), ((LANES, 8), F32),
            ((peers, -(-(6 * micros + part) // 8) * 8, LANES), BF16),
        ],
        swap(send, BOTH), cols, up_out, cot, slopes, plain, w_up_t,
    )
    features = with_layout_constraint(features.transpose(0, 2, 1, 3)[:, None], Layout((0, 1, 2, 3, 4)))
    features, send = lax.optimization_barrier((features, send))
    edge = ((micros, 2, channels, width), BF16)
    vector, top_vector, matrix = ((half,), F32), ((upper // 2,), F32), ((half, 9 * channels), F32)
    rising = [(i, i + 1) for i in range(tiles - 1)]
    falling = [(j, i) for i, j in rising]
    cross = ((3 * channels, 3 * channels), F32)
    low, top_low, rising_edge, falling_edge, up_gain_grad, up_shift_grad, expected, extras = run(
        functools.partial(middle_back_kernel, rows=rows, each=part),
        [
            grid(rows, BF16, 3 * channels), grid(rows, BF16, upper), edge, edge, top_vector, top_vector,
            ((micros, LANES), F32), ((micros, LANES), F32),
        ],
        swap(send, BOTH), cols, grads, up_out, top_stats, second_out, second_stats, slopes, w_up, w_up_t,
        mixed, plain, crossed,
        scratch=[vmem(*grid(rows))],
    )
    before = lax.ppermute(rising_edge, "tile", rising)
    after = lax.ppermute(falling_edge, "tile", falling)
    first_dz, top_grad, second_cross, send = run(
        functools.partial(first_back_kernel, rows=rows, tiles=tiles),
        [grid(rows + 2), ((upper, channels), F32), cross, ((peers, 2 + micros, LANES), F32)],
        low, top_low, second_act, first_act, first_out, first_stats, first_slopes, b_second, extras,
        hbm=(7,), scratch=[vmem(*taps)], copies=1,
        cost=pl.CostEstimate(flops=2 * 10**9, bytes_accessed=10**7, transcendentals=0),
    )
    length = (2 * 9 * half * channels + upper * half) // LANES
    each = -(-length // peers)
    block = -(-(capacity + 2 * each) // 8) * 8
    send, first_gain_grad, first_shift_grad, second_gain_grad, second_shift_grad = run(
        functools.partial(pick_kernel, rows=rows, tiles=tiles, each=each),
        [((peers, block, LANES), BF16), vector, vector, vector, vector],
        swap(send, BOTH), cols, first_dz,
        before, after, first_out, first_stats, first_slopes, b_first, b_second, cell_columns, cell_rows, canvas, second_cross, top_grad, expected,
        hbm=(8, 9),
        scratch=[
            vmem(*grid(rows + 2, BF16, 3 * channels)), vmem(*grid(rows, BF16)), vmem(*taps), vmem(*taps),
            vmem(*grid(rows + 2)), vmem(*cross), vmem((scenes, peers * each, LANES), F32),
        ],
        copies=2,
    )
    block = -(-(14 + each) // 8) * 8
    send, pillar_dz = run(
        functools.partial(pillar_back_kernel, capacity=capacity, each=each),
        [((tiles, scenes, block, LANES), BF16), ((micros, channels, depth * pillars), F32)],
        swap(send, BOTH), point_rows, w_pillar, cols, pooled,
        hbm=(1,),
        scratch=[vmem((channels, depth * pillars), F32), vmem((micros, 16, depth * pillars), BF16)],
        copies=1,
    )
    points_grad, pillar_grad, pillar_gain_grad, pillar_shift_grad, first_grad, second_grad, up_grad = run(
        functools.partial(points_kernel, each=each),
        [
            ((micros, 1, inputs, depth, pillars), F32), ((inputs, half), F32), vector, vector,
            matrix, matrix, ((upper // 2, channels), F32),
        ],
        swap(send.reshape(peers, block, LANES), BOTH), point_rows, pillar_dz, w_pillar, cols, pooled,
        hbm=(1,),
        scratch=[vmem((micros, 16, depth * pillars), BF16), vmem((channels, depth * pillars), F32)],
        copies=1,
    )
    return (
        features, points_grad,
        pillar_grad.T, pillar_gain_grad, pillar_shift_grad,
        first_grad, first_gain_grad, first_shift_grad,
        second_grad, second_gain_grad, second_shift_grad,
        up_grad, up_gain_grad, up_shift_grad,
    )


def solution(mesh):
    matrix, vector = P("scene", None), P("scene")
    grid = P(None, "scene", None, "tile", None)
    cloud = P(None, "scene", None, None, "tile")
    pillar = P(None, "scene", "tile")
    weights = (matrix, vector, vector) * 4
    return jax.shard_map(
        shards,
        mesh=mesh,
        in_specs=(cloud, pillar, pillar, pillar) + weights + (grid,),
        out_specs=(grid, cloud) + weights,
        check_vma=False,
    )
```

```python
import functools

import jax
import jax.numpy as jnp
from jax import lax
from jax.experimental import pallas as pl
from jax.experimental.layout import Layout, with_layout_constraint
from jax.experimental.pallas import tpu as pltpu
from jax.sharding import PartitionSpec as P

norm_eps = 0.001
BOTH = ("tile", "scene")
F32 = jnp.float32
BF16 = jnp.bfloat16
VMEM_LIMIT = 24 * 1024 * 1024
WIDE_LIMIT = 60 * 1024 * 1024
LANES = 128


def run(kernel, outs, *args, hbm=(), scratch=(), copies=0, cost=None, limit=VMEM_LIMIT):
    specs = [
        pl.BlockSpec(memory_space=pltpu.HBM if index in hbm else pltpu.VMEM) for index in range(len(args))
    ]
    scratch = list(scratch)
    if copies:
        scratch.append(pltpu.SemaphoreType.DMA((copies,)))
    return pl.pallas_call(
        kernel,
        out_shape=[jax.ShapeDtypeStruct(out[0], out[1]) for out in outs],
        in_specs=specs,
        out_specs=[
            pl.BlockSpec(memory_space=pltpu.HBM if len(out) > 2 else pltpu.VMEM) for out in outs
        ],
        scratch_shapes=scratch,
        compiler_params=pltpu.CompilerParams(vmem_limit_bytes=limit),
        cost_estimate=cost,
    )(*args)


def move(source, target, sems, index):
    copy = pltpu.make_async_copy(source, target, sems.at[index])
    copy.start()
    return copy


def dot(left, right, precision=None):
    return jnp.dot(left, right, preferred_element_type=F32, precision=precision)


def dot_lanes(left, right, precision=None):
    return lax.dot_general(
        left, right, (((1,), (1,)), ((), ())), preferred_element_type=F32, precision=precision
    )


def sigmoid(values):
    return 0.5 + 0.5 * jnp.tanh(0.5 * values)


def fold(values):
    total = values[:, :LANES]
    for start in range(LANES, values.shape[1], LANES):
        total = total + values[:, start : start + LANES]
    return total


def row_of(left, right=None):
    both = left if right is None else jnp.concatenate([left, right], axis=0)
    return jnp.sum(jnp.transpose(both), axis=0, keepdims=True)


def columns_of(rows):
    rows = rows + [jnp.zeros((8 - len(rows), LANES), F32)] if len(rows) < 8 else rows
    return jnp.transpose(jnp.concatenate(rows, axis=0))


def inside(tile, row, height):
    tiles, rows = height
    place = tile * rows + row
    return jnp.where((place >= 0) & (place < tiles * rows), 1.0, 0.0).astype(F32)


def send_all(ref, rows):
    for index, row in enumerate(rows):
        ref[:, index : index + 1, :] = jnp.broadcast_to(row[None], (ref.shape[0], 1, LANES))


def pooled_stats(means, squares, count):
    peers = means.shape[0]
    mean = jnp.sum(means, axis=0, keepdims=True) * (1.0 / peers)
    away = means - mean
    spread = jnp.sum(squares + count * away * away, axis=0, keepdims=True) * (1.0 / (peers * count))
    return mean, lax.rsqrt(spread + norm_eps)


def stat_columns(found, count):
    return columns_of(list(pooled_stats(found[:, 0, :], found[:, 1, :], count)))


def sum_rows(found, lines):
    return [jnp.sum(found[:, index, :], axis=0, keepdims=True) for index in range(lines)]


def own_half(row, scene, out):
    size = out.shape[0]
    out[...] = jnp.where(scene == 0, row[:, 0:size], row[:, size : 2 * size]).reshape(size)


def edges(channels, width):
    lane = lax.broadcasted_iota(jnp.int32, (channels, width), 1)
    return lane > 0, lane < width - 1


def spread(row, masks):
    zero = jnp.zeros_like(row)
    left = jnp.where(masks[0], pltpu.roll(row, 1, 1), zero)
    right = jnp.where(masks[1], pltpu.roll(row, row.shape[1] - 1, 1), zero)
    return jnp.concatenate([left, row, right], axis=0)


def layout(half, channels):
    first = 0
    second = first + half * -(-9 * channels // LANES)
    up = second + half * -(-9 * channels // LANES)
    vectors = up + channels
    return first, second, up, vectors, vectors + 16


def widen(value):
    missing = LANES - value.shape[1]
    if missing == 0:
        return value
    return jnp.concatenate([value, jnp.zeros((value.shape[0], missing), value.dtype)], axis=1)


def pack(held, out):
    first, second, up, pillar = held[:4]
    half, channels = first.shape[0], up.shape[1]
    starts = layout(half, channels)
    for ref, start in ((first, starts[0]), (second, starts[1])):
        for j in range(-(-9 * channels // LANES)):
            out[start + j * half : start + (j + 1) * half, :] = widen(
                ref[:, j * LANES : min((j + 1) * LANES, 9 * channels)]
            )
    out[starts[2] : starts[2] + channels, :] = widen(up[...])
    rows = [vector[...].astype(F32).reshape(1, -1) for vector in held[4:]]
    rows = [widen(row) for row in rows] + [jnp.zeros((16 - len(rows), LANES), F32)]
    turned = widen(pillar[...].astype(F32))
    rows += [turned, jnp.zeros((16 - turned.shape[0], LANES), F32)]
    out[starts[3] :, :] = jnp.concatenate(rows, axis=0).astype(BF16)


def unpack_kernel(
    both, w_pillar, cols, l_first, l_second, b_first, b_second, w_up, w_up_t,
    h_second, h_first_back, h_second_back, sems, *, inputs
):
    half = w_pillar.shape[0] // 2
    channels = 2 * half
    starts = layout(half, channels)
    tiles = -(-9 * channels // LANES)

    def wide(start):
        return jnp.concatenate(
            [
                jnp.concatenate(
                    [both[s, start + j * half : start + (j + 1) * half, :] for j in range(tiles)], axis=1
                )
                for s in range(2)
            ],
            axis=0,
        ).astype(F32)

    up = jnp.concatenate(
        [both[s, starts[2] : starts[2] + channels, 0:channels] for s in range(2)], axis=0
    )
    w_up[...] = up
    w_up_t[...] = jnp.transpose(up.astype(F32)).astype(BF16)
    turned = jnp.concatenate(
        [both[s, starts[4] : starts[4] + 16, 0:half].astype(F32) for s in range(2)], axis=1
    )
    w_pillar[...] = jnp.transpose(widen(turned))[0:channels, 0:inputs].astype(BF16)
    vectors = [both[s, starts[3] : starts[3] + 16, :].astype(F32) for s in range(2)]
    rows = []
    for index in range(8):
        size = half if index < 6 else channels
        row = jnp.concatenate([vectors[s][index : index + 1, 0:size] for s in range(2)], axis=1)
        rows.append(jnp.concatenate([row] * (LANES // (2 * size)), axis=1))
    cols[...] = columns_of(rows)
    zero = jnp.zeros((channels, 3 * channels), F32)
    copies = []
    for weight, ahead, back in (
        (wide(starts[0]), l_first, h_first_back), (wide(starts[1]), h_second, h_second_back)
    ):
        weight = weight[:, : 9 * channels]
        turned = jnp.transpose(weight)
        flipped = jnp.concatenate(
            [turned[tap * channels : (tap + 1) * channels] for tap in range(8, -1, -1)], axis=1
        )
        for ref, taps in ((ahead, weight), (back, flipped)):
            ref[0:channels, :] = jnp.concatenate([taps, zero], axis=1).astype(BF16)
            ref[channels : 2 * channels, :] = jnp.concatenate([zero, taps], axis=1).astype(BF16)
    copies.append(move(h_second, l_second, sems, 0))
    copies.append(move(h_first_back, b_first, sems, 1))
    copies.append(move(h_second_back, b_second, sems, 2))
    for copy in copies:
        copy.wait()


def slot_line(wide, depth, inputs):
    return jnp.concatenate([wide[pl.ds(n, inputs, stride=depth), :] for n in range(depth)], axis=1)


def slot_mask(count, depth):
    return jnp.concatenate([jnp.where(count > n, 1.0, 0.0) for n in range(depth)], axis=1)


def ranks(tile):
    pillars = tile.shape[1]
    across = jnp.broadcast_to(tile, (pillars, pillars))
    down = jnp.transpose(across)
    row = lax.broadcasted_iota(jnp.int32, (pillars, pillars), 0)
    col = lax.broadcasted_iota(jnp.int32, (pillars, pillars), 1)
    return jnp.sum(jnp.where((across == down) & (row < col), 1.0, 0.0), axis=0, keepdims=True)


def moments_kernel(*refs, capacity):
    number = 16
    sources, out, packed, lines_out = refs[:number], *refs[number : number + 3]
    held, wide, sems = refs[number + 3 : 2 * number + 3], refs[-2], refs[-1]
    copies = [move(sources[i], held[i], sems, i) for i in range(number)]
    tiles, cells, counts, points = held[:4]
    micros, _, inputs, depth, pillars = points.shape
    peers, scenes = out.shape[:2]
    copies[0].wait()
    copies[1].wait()
    lines, slot_rows = [], []
    for micro in range(micros):
        tile = tiles[micro].astype(F32)
        cell = (cells[micro] + 1).astype(F32)
        high = jnp.floor(cell * (1.0 / 16.0))
        low = cell - high * 16.0
        rank = ranks(tile)
        slot_rows.append(tile * capacity + rank)
        spot = lax.broadcasted_iota(jnp.int32, (capacity, pillars), 0).astype(F32)
        placed = jnp.where(spot == rank, 1.0, 0.0).astype(BF16)
        peer = lax.broadcasted_iota(jnp.int32, (peers, pillars), 0).astype(F32)
        for group in range(3):
            named = tile == peer + (group - 1.0)
            lines.append(
                16.0 * dot_lanes(jnp.where(named, high, 0.0).astype(BF16), placed)
                + dot_lanes(jnp.where(named, low, 0.0).astype(BF16), placed)
            )
    used = 3 * micros * capacity
    line = jnp.concatenate(lines + [jnp.zeros((peers, LANES - used), F32)], axis=1).reshape(peers, 1, LANES)
    for scene in range(scenes):
        out[:, scene, micros : micros + 1, :] = line
    copies[2].wait()
    copies[3].wait()
    parts, mean_rows, totals = [], [], []
    for micro in range(micros):
        wide[...] = points[micro, 0].astype(F32).reshape(inputs * depth, pillars)
        rows = slot_line(wide, depth, inputs)
        notes = jnp.concatenate([slot_rows[micro], counts[micro].astype(F32)], axis=0)
        notes = jnp.concatenate([notes, jnp.zeros((2, rows.shape[1] - pillars), F32)], axis=1)
        lines_out[micro] = jnp.concatenate(
            [rows, notes, jnp.zeros((14 - inputs, rows.shape[1]), F32)], axis=0
        ).astype(BF16)
        mask = slot_mask(counts[micro], depth)
        total = jnp.sum(mask, axis=1, keepdims=True)
        mean = jnp.sum(rows * mask, axis=1, keepdims=True) / total
        centred = jnp.concatenate(
            [(rows - mean) * mask, jnp.zeros((16 - inputs, rows.shape[1]), F32)], axis=0
        )
        high = centred.astype(BF16)
        parts += [high, (centred - high.astype(F32)).astype(BF16)]
        lane = lax.broadcasted_iota(jnp.int32, (inputs, inputs), 1)
        diagonal = lax.broadcasted_iota(jnp.int32, (inputs, inputs), 0) == lane
        mean_rows.append(jnp.sum(jnp.where(diagonal, mean, 0.0), axis=0, keepdims=True))
        totals.append(total)
    parts = jnp.concatenate(parts, axis=0)
    every = dot_lanes(parts, parts)
    for micro in range(micros):
        at = 32 * micro
        square = every[at : at + 32, at : at + 32]
        products = (
            square[0:inputs, 0:inputs] + square[16 : 16 + inputs, 0:inputs]
            + square[0:inputs, 16 : 16 + inputs] + square[16 : 16 + inputs, 16 : 16 + inputs]
        )
        row = jnp.concatenate(
            [products[k : k + 1] for k in range(inputs)]
            + [mean_rows[micro], totals[micro], jnp.zeros((1, LANES - inputs * inputs - inputs - 1), F32)],
            axis=1,
        )
        for scene in range(scenes):
            out[:, scene, micro : micro + 1, :] = jnp.broadcast_to(row[None], (peers, 1, LANES))
    for copy in copies[4:]:
        copy.wait()
    pack(held[4:], packed)


def cells_kernel(found, columns, rows, *, capacity):
    scene = lax.axis_index("scene")
    slots = columns.shape[0]
    peers = found.shape[0]
    values = found[:, 2, :]
    slot = lax.broadcasted_iota(jnp.int32, (slots, peers), 0)
    peer = lax.broadcasted_iota(jnp.int32, (slots, peers), 1)
    lane = lax.broadcasted_iota(jnp.int32, (slots, LANES), 1)
    row = lax.broadcasted_iota(jnp.int32, (slots, LANES), 0)
    result = jnp.zeros((slots, LANES), F32)
    chosen = jnp.where(peer == 2 * (slot // capacity) + scene, 1.0, 0.0)
    spread = dot(chosen, values, lax.Precision.HIGHEST)
    for micro in range(2):
        for group in range(3):
            mine = jnp.where(lane == (3 * micro + group) * capacity + row % capacity, spread, 0.0)
            column = jnp.sum(mine, axis=1, keepdims=True)
            result = jnp.where(lane == 2 * group + micro, column, result)
    columns[...] = result
    rows[...] = jnp.transpose(result)[0:8]


def pillar_notes(rows, micro, inputs, pillars):
    notes = rows[micro, :, 0:pillars].astype(F32)
    return notes[inputs : inputs + 1], notes[inputs + 1 : inputs + 2]


def pillar_kernel(
    found, point_rows, w_pillar, cols, send, pooled, lifted, acts, *, capacity
):
    micros = point_rows.shape[0]
    channels, inputs = w_pillar.shape
    pillars = pooled.shape[2]
    depth = point_rows.shape[2] // pillars
    weight = w_pillar[...]
    wide_weight = weight.astype(F32)
    rows_out = send.shape[0]
    square = inputs * inputs
    stacked, slot_rows = [], []
    for micro in range(micros):
        lifted[...] = dot(weight, point_rows[micro, 0:inputs])
        moments = found[:, micro, :]
        sizes = moments[:, square + inputs : square + inputs + 1]
        means = moments[:, square : square + inputs]
        count = jnp.sum(sizes, axis=0, keepdims=True)
        mean = jnp.sum(means * sizes, axis=0, keepdims=True) / count
        away = means - mean
        products = lax.dot_general(
            away * sizes, away, (((0,), (0,)), ((), ())),
            preferred_element_type=F32, precision=lax.Precision.HIGHEST,
        )
        summed = jnp.sum(moments, axis=0, keepdims=True)
        products = products + jnp.concatenate(
            [summed[:, k * inputs : (k + 1) * inputs] for k in range(inputs)], axis=0
        )
        cov = products / count
        spun = wide_weight[:, 0:1] * cov[0:1]
        for k in range(1, inputs):
            spun = spun + wide_weight[:, k : k + 1] * cov[k : k + 1]
        spread = jnp.sum(spun * wide_weight, axis=1, keepdims=True)
        centre = jnp.sum(wide_weight * mean, axis=1, keepdims=True)
        rstd = lax.rsqrt(spread + norm_eps)
        inverse = jnp.broadcast_to(1.0 / count, (channels, 1))
        pooled[micros + micro] = jnp.concatenate(
            [
                centre, rstd, inverse, jnp.zeros((channels, 13), F32),
                spun, jnp.zeros((channels, 16 - inputs), F32),
                jnp.broadcast_to(mean, (channels, inputs)), jnp.zeros((channels, LANES - 32 - inputs), F32),
            ],
            axis=1,
        )
        scale = rstd * cols[0:channels, 0:1]
        shift = cols[0:channels, 1:2]
        slot, limit = pillar_notes(point_rows, micro, inputs, pillars)
        slot_rows.append(slot)
        top = jnp.full((channels, pillars), -jnp.inf, F32)
        for n in range(depth):
            piece = slice(n * pillars, (n + 1) * pillars)
            normed = (lifted[:, piece] - centre) * scale + shift
            act = normed * sigmoid(normed)
            acts[:, piece] = act
            top = jnp.maximum(top, jnp.where(limit > n, act, -jnp.inf))
        total = jnp.zeros((channels, pillars), F32)
        for n in range(depth):
            piece = slice(n * pillars, (n + 1) * pillars)
            total = total + jnp.where(limit > n, jnp.exp(acts[:, piece] - top), 0.0)
        result = top + jnp.log(total)
        pooled[micro] = result
        parts = [jnp.zeros((channels, pillars), F32)] * micros
        parts[micro] = result.astype(BF16).astype(F32)
        stacked.append(jnp.transpose(jnp.concatenate(parts, axis=0)))
    values = jnp.concatenate(stacked, axis=0).astype(BF16)
    for group in range(3):
        place = lax.broadcasted_iota(jnp.int32, (rows_out, pillars), 0) + (group - 1) * capacity
        chosen = jnp.concatenate(
            [jnp.where(place.astype(F32) == row, 1.0, 0.0) for row in slot_rows], axis=1
        ).astype(BF16)
        send[:, group * LANES : (group + 1) * LANES] = dot(chosen, values).astype(BF16)


def own_stats(ref, first_row, rows, send):
    micros, _, channels, width = ref.shape
    sums, squares = [], []
    for micro in range(micros):
        total = fold(ref[micro, first_row])
        for row in range(first_row + 1, first_row + rows):
            total = total + fold(ref[micro, row])
        sums.append(total * (1.0 / (rows * width)))
    means = [jnp.sum(total, axis=1, keepdims=True) for total in sums]
    for micro in range(micros):
        spread = jnp.zeros(sums[micro].shape, F32)
        for row in range(first_row, first_row + rows):
            away = ref[micro, row] - means[micro]
            spread = spread + fold(away * away)
        squares.append(spread)
    if channels == LANES:
        send_all(send, [row_of(part) for part in sums + squares])
    else:
        send_all(send, [row_of(*sums), row_of(*squares)])


def conv_pair(source, weight, micro, at, channels):
    window = source[micro, at : at + 4].reshape(12 * channels, source.shape[3])
    return dot(weight[...], window)


def conv_rows(source, weight, out, shape):
    micros, high, channels, width = shape
    for micro in range(micros):
        for at in range(0, high, 2):
            both = conv_pair(source, weight, micro, at, channels)
            out[micro, at] = both[:channels].astype(out.dtype)
            out[micro, at + 1] = both[channels:].astype(out.dtype)


def canvas_kernel(found, columns, where_rows, l_first, out, kept, send, canvas, *, rows):
    scenes, high, channels, width = out.shape
    masks = edges(channels, width)
    slots = found.shape[0]
    lane = lax.broadcasted_iota(jnp.int32, (slots, width), 1).astype(F32)
    for group in range(3):
        values = jnp.transpose(found[:, group * LANES : (group + 1) * LANES].astype(F32))
        first, count = ((rows - 2, 2), (0, rows), (0, 2))[group]
        for scene in range(scenes):
            at = 2 * group + scene
            column = columns[:, at : at + 1] - 1.0
            column = column - jnp.floor(column * (1.0 / width)) * width
            row = jnp.floor((where_rows[at : at + 1] - 1.0) * (1.0 / width))
            mine = values[scene * channels : (scene + 1) * channels]
            placed = jnp.concatenate(
                [jnp.where(row == r * 1.0, mine, 0.0) for r in range(first, first + count)], axis=0
            ).astype(BF16)
            chosen = jnp.where(lane == column, 1.0, 0.0).astype(BF16)
            grid = dot(placed, chosen).astype(BF16)
            start = (0, 2, rows + 2)[group]
            for r in range(count):
                row = grid[r * channels : (r + 1) * channels]
                canvas[scene, start + r] = spread(row, masks)
                if 1 <= start + r <= rows + 2:
                    kept[scene, start + r - 1] = row
    conv_rows(canvas, l_first, out, out.shape)
    own_stats(out, 1, rows, send)


def second_kernel(found, cols, first_out, l_second_in, out, kept, slopes, stats, send, acts, l_second, sems,
                  *, rows, tiles):
    weight_copy = move(l_second_in, l_second, sems, 0)
    micros, high, channels, width = first_out.shape
    tile = lax.axis_index("tile")
    turned = stat_columns(found, float(rows * width))
    stats[...] = turned
    masks = edges(channels, width)
    for micro in range(micros):
        part = slice(micro * channels, (micro + 1) * channels)
        centre = turned[part, 0:1]
        scale = turned[part, 1:2] * cols[0:channels, 2:3]
        shift = cols[0:channels, 3:4]

        for row in range(high):
            normed = (first_out[micro, row] - centre) * scale + shift
            gate = sigmoid(normed)
            act = normed * gate
            slopes[micro, row] = gate + act * (1.0 - gate)
            if row == 0 or row == high - 1:
                act = act * inside(tile, row - 1, (tiles, rows))
            act = act.astype(BF16)
            acts[micro, row] = spread(act, masks)
            kept[micro, row] = act
    weight_copy.wait()
    conv_rows(acts, l_second, out, out.shape)
    own_stats(out, 0, rows, send)


def up_kernel(found, cols, second_out, w_up, acts, upper, slopes, plain, crossed, stats, send, *, rows):
    micros, _, channels, width = second_out.shape
    peers = send.shape[0]
    each = crossed.shape[0] // peers
    turned = stat_columns(found, float(rows * width))
    stats[...] = turned
    gain, shift = cols[0:channels, 4:5], cols[0:channels, 5:6]
    lines = []
    for micro in range(micros):
        part = slice(micro * channels, (micro + 1) * channels)
        centre, rstd = turned[part, 0:1], turned[part, 1:2]
        slope_sum = jnp.zeros((channels, LANES), F32)
        unit_sum = jnp.zeros((channels, LANES), F32)
        for row in range(rows):
            unit = (second_out[micro, row] - centre) * rstd
            normed = unit * gain + shift
            gate = sigmoid(normed)
            act = normed * gate
            slope = gate + act * (1.0 - gate)
            sloped = slope * unit
            slope_sum = slope_sum + fold(slope)
            unit_sum = unit_sum + fold(sloped)
            slopes[micro, row] = jnp.concatenate([slope, sloped], axis=0)
            act = act.astype(BF16)
            acts[micro, row] = act
            upper[micro, row] = dot(w_up[...], act)
        lines.append(row_of(slope_sum, unit_sum).astype(BF16).astype(F32))
        crossed[micro * channels : (micro + 1) * channels] = dot_lanes(
            jnp.concatenate([acts[micro, row] for row in range(rows)], axis=1),
            jnp.concatenate([slopes[micro, row].astype(BF16) for row in range(rows)], axis=1),
        )
    plain[...] = jnp.concatenate(lines, axis=0)
    used = micros * channels
    if crossed.shape[0] > used:
        crossed[used:] = jnp.zeros((crossed.shape[0] - used, LANES), F32)
    if 2 * micros + each < send.shape[1]:
        send[...] = jnp.zeros(send.shape, F32)
    for peer in range(peers):
        send[peer, 2 * micros : 2 * micros + each] = crossed[peer * each : (peer + 1) * each]
    own_stats(upper, 0, rows, send)


def exact_rows(rows):
    high = rows.astype(BF16).astype(F32)
    return [high, rows - high]


def top_kernel(found, cols, upper, cot, slopes, plain, w_up_t, features, grads, mixed, stats, send, *, rows, each):
    micros, _, wide, width = upper.shape
    channels = w_up_t.shape[0]
    lines = []
    for micro in range(micros):
        lines += list(pooled_stats(found[:, micro, :], found[:, micros + micro, :], float(rows * width)))
    turned = columns_of(lines)
    stats[...] = turned
    gain, shift = cols[:, 6:7], cols[:, 7:8]
    gain_rows, shift_rows, mixed_rows = [], [], []
    for micro in range(micros):
        centre, rstd = turned[:, 2 * micro : 2 * micro + 1], turned[:, 2 * micro + 1 : 2 * micro + 2]
        factor = gain * rstd
        gain_sum = jnp.zeros((wide, LANES), F32)
        shift_sum = jnp.zeros((wide, LANES), F32)
        mixed_sum = jnp.zeros((2 * channels, LANES), F32)
        for row in range(rows):
            unit = (upper[micro, row] - centre) * rstd
            normed = unit * gain + shift
            gate = sigmoid(normed)
            act = normed * gate
            grad = cot[micro, row].astype(F32) * (gate + act * (1.0 - gate))
            features[micro, row] = act.astype(BF16)
            grads[micro, row] = grad
            gain_sum = gain_sum + fold(grad * unit)
            shift_sum = shift_sum + fold(grad)
            below = dot(w_up_t[...], (grad * factor).astype(BF16))
            mixed_sum = mixed_sum + fold(
                slopes[micro, row] * jnp.concatenate([below, below], axis=0)
            )
        gain_rows.append(row_of(gain_sum))
        shift_rows.append(row_of(shift_sum))
        mixed_rows.append(row_of(mixed_sum).astype(BF16).astype(F32))
    mixed[...] = jnp.concatenate(mixed_rows, axis=0)
    rows_out = jnp.concatenate(gain_rows + shift_rows, axis=0)
    crossed = jnp.sum(found[:, 2 * micros : 2 * micros + each, :], axis=0)
    rest = send.shape[1] - 6 * micros - each
    block = exact_rows(rows_out) + mixed_rows + [plain[...], crossed]
    if rest > 0:
        block.append(jnp.zeros((rest, LANES), F32))
    block = jnp.concatenate(block, axis=0)
    send[...] = jnp.broadcast_to(block.astype(BF16)[None], send.shape)


def low_rows(turned, value_of, values, stats, gain, low, high, first, rows, tiles):
    micros, _, channels, width = values.shape
    tile = lax.axis_index("tile")
    masks = edges(channels, width)
    for micro in range(micros):
        part = slice(micro * channels, (micro + 1) * channels)
        centre, rstd = stats[part, 0:1], stats[part, 1:2]
        factor = gain * rstd
        slope_part, shift_part = rstd * turned[part, 0:1], turned[part, 1:2]
        for index in range(high):
            grad, value = value_of(micro, index)
            grad = factor * (grad - shift_part - (value - centre) * slope_part)
            if index + first < 0 or index + first >= rows:
                grad = grad * inside(tile, index + first, (tiles, rows))
            low[micro, index] = spread(grad.astype(BF16), masks)


def first_units(first_out, stats, micro, channels):
    part = slice(micro * channels, (micro + 1) * channels)
    centre, rstd = stats[part, 0:1], stats[part, 1:2]
    return lambda row: (first_out[micro, row] - centre) * rstd


def second_sums(total, weight, factors, stats, micro, micros, count):
    channels = weight.shape[1]
    factor, centre = factors[micro], stats[:, 2 * micro : 2 * micro + 1]
    columns = jnp.transpose(jnp.concatenate([total, jnp.zeros((8 - total.shape[0], LANES), F32)], axis=0))
    beta = factor * stats[:, 2 * micro + 1 : 2 * micro + 2] * columns[:, micro : micro + 1] * (1.0 / count)
    alpha = factor * columns[:, micros + micro : micros + micro + 1] * (1.0 / count)
    square = lax.dot_general(
        weight * beta, weight, (((0,), (0,)), ((), ())),
        preferred_element_type=F32, precision=lax.Precision.HIGHEST,
    )
    square = jnp.concatenate([square, square], axis=1)
    line = jnp.sum(weight * (alpha - beta * centre), axis=0, keepdims=True)
    line = jnp.concatenate([line, line], axis=1)

    def give(mixed, plain, crossed):
        mine = crossed[micro * channels : (micro + 1) * channels]
        return mixed - plain * line - jnp.sum(square * mine, axis=0, keepdims=True)

    return give


def middle_back_kernel(
    found, cols, grads, upper, top_stats, second_out, second_stats, slopes, w_up, w_up_t,
    own_mixed, own_plain, own_crossed,
    low, top_low, rising, falling, top_gain_grad, top_shift_grad, expected, extras, second_dz, *, rows, each
):
    scene = lax.axis_index("scene")
    micros, _, wide, width = grads.shape
    channels = second_out.shape[2]
    peers = found.shape[0]
    count = float(peers * rows * width)
    kept = 2 * micros
    total = jnp.sum(found[...].astype(F32), axis=0)
    mixed, plain = total[2 * kept : 2 * kept + micros], total[2 * kept + micros : 3 * kept]
    total = total[0:kept] + total[kept : 2 * kept]
    crossed = jnp.concatenate(
        [
            found[peer].astype(F32)[3 * kept : 3 * kept + each]
            for peer in range(-(-micros * channels // each))
        ],
        axis=0,
    )
    own_half(total[0:1] + total[1:2], scene, top_gain_grad)
    own_half(total[2:3] + total[3:4], scene, top_shift_grad)
    factors = [cols[:, 6:7] * top_stats[:, 2 * micro + 1 : 2 * micro + 2] for micro in range(micros)]
    wide_weight = w_up[...].astype(F32)
    turned = columns_of([total[index : index + 1] for index in range(2 * micros)]) * (1.0 / count)
    gain = cols[0:channels, 4:5]
    masks = edges(channels, width)
    second_rows = []
    for micro in range(micros):
        top_centre = top_stats[:, 2 * micro : 2 * micro + 1]
        top_slope = top_stats[:, 2 * micro + 1 : 2 * micro + 2] * turned[:, micro : micro + 1]
        top_shift = turned[:, micros + micro : micros + micro + 1]
        part = slice(micro * channels, (micro + 1) * channels)
        centre, rstd = second_stats[part, 0:1], second_stats[part, 1:2]
        gain_sum = jnp.zeros((channels, LANES), F32)
        shift_sum = jnp.zeros((channels, LANES), F32)
        for row in range(rows):
            grad = factors[micro] * (
                grads[micro, row] - top_shift - (upper[micro, row] - top_centre) * top_slope
            )
            grad = grad.astype(BF16)
            top_low[micro, row] = grad
            unit = (second_out[micro, row] - centre) * rstd
            grad = dot(w_up_t[...], grad) * slopes[micro, row, 0:channels]
            second_dz[micro, row] = grad
            shift_sum = shift_sum + fold(grad)
            gain_sum = gain_sum + fold(grad * unit)
        second_rows.append((shift_sum, gain_sum))
    parts = []
    for micro in range(micros):
        give = second_sums(total, wide_weight, factors, top_stats, micro, micros, count)
        whole = give(mixed[micro : micro + 1], plain[micro : micro + 1], crossed)
        extra = row_of(*second_rows[micro]) - give(
            own_mixed[micro : micro + 1], own_plain[micro : micro + 1], own_crossed[...]
        )
        expected[micro : micro + 1] = whole
        extras[micro : micro + 1] = extra
        parts.append(whole * (1.0 / count) + extra * (1.0 / (rows * width)))
    parts = columns_of(parts)
    for micro in range(micros):
        part = slice(micro * channels, (micro + 1) * channels)
        centre, rstd = second_stats[part, 0:1], second_stats[part, 1:2]
        factor = gain * rstd
        shift_part = parts[0:channels, micro : micro + 1]
        slope_part = parts[channels : 2 * channels, micro : micro + 1] * rstd
        for row in range(rows):
            grad = factor * (
                second_dz[micro, row] - shift_part - (second_out[micro, row] - centre) * slope_part
            )
            low[micro, row] = spread(grad.astype(BF16), masks)
    for micro in range(micros):
        for row in range(2):
            falling[micro, row] = low[micro, row, channels : 2 * channels]
            rising[micro, row] = low[micro, rows - 2 + row, channels : 2 * channels]


def first_back_kernel(
    low, top_low, second_act, acts, first_out, first_stats, slopes, b_second_in, extras,
    out, top_grad, weight_grad, send, b_second, sems, *, rows, tiles
):
    weight_copy = move(b_second_in, b_second, sems, 0)
    tile = lax.axis_index("tile")
    micros, _, channels, width = first_out.shape
    weight_copy.wait()
    half = 6 * channels
    gain_sums, shift_sums = [], []
    for micro in range(micros):
        units = first_units(first_out, first_stats, micro, channels)
        gain_sum = jnp.zeros((channels, LANES), F32)
        shift_sum = jnp.zeros((channels, LANES), F32)
        for at in range(0, rows + 2, 2):
            if at == 0:
                parts = dot(b_second[:, half:], low[micro, 0:2].reshape(half, width))
            elif at == rows:
                parts = dot(b_second[:, :half], low[micro, rows - 2 : rows].reshape(half, width))
            else:
                parts = conv_pair(low, b_second, micro, at - 2, channels)
            for j in range(2):
                grad = parts[channels * j : channels * (j + 1)] * slopes[micro, at + j]
                if at + j == 0 or at + j == rows + 1:
                    grad = grad * inside(tile, at + j - 1, (tiles, rows))
                out[micro, at + j] = grad
                gain_sum = gain_sum + fold(grad * units(at + j))
                shift_sum = shift_sum + fold(grad)
        gain_sums.append(gain_sum)
        shift_sums.append(shift_sum)
        product = dot_lanes(
            jnp.concatenate([top_low[micro, row] for row in range(rows)], axis=1),
            jnp.concatenate([second_act[micro, row] for row in range(rows)], axis=1),
        )
        top_grad[...] = product if micro == 0 else top_grad[...] + product
    conv_grad(low, 0, acts, 0, weight_grad, rows)
    send_all(send, [row_of(*gain_sums), row_of(*shift_sums)] + [extras[m : m + 1] for m in range(micros)])


def conv_grad(low, low_first, values, value_first, total, rows):
    micros, _, channels, width = values.shape
    for micro in range(micros):
        grads = jnp.concatenate([low[micro, row + low_first] for row in range(rows)], axis=1)
        windows = jnp.concatenate(
            [
                values[micro, row + value_first : row + value_first + 3].reshape(3 * channels, width)
                for row in range(rows)
            ],
            axis=1,
        )
        product = dot_lanes(grads, windows)
        total[...] = product if micro == 0 else total[...] + product


def half_rows(total, half, scene):
    channels = 2 * half
    start = scene * half
    mine = jnp.concatenate(
        [total[b * channels + start : b * channels + start + half, :] for b in range(2, -1, -1)], axis=0
    )
    wing = mine[:, LANES:]
    cut = wing.shape[0] // 2
    return [mine[:, :LANES], jnp.concatenate([wing[:cut], wing[cut:]], axis=1)]


def pick_kernel(
    found, cols, grads, before, after, first_out, first_stats, slopes, b_first_in, b_second_in, columns, where_rows,
    canvas, second_grad, top_grad, expected,
    send, gain_grad, shift_grad, second_gain_grad, second_shift_grad, low, grid, b_first, b_second, halo, first_grad, whole, sems,
    *, rows, tiles, each
):
    second_copy = move(b_second_in, b_second, sems, 1)
    weight_copy = move(b_first_in, b_first, sems, 0)
    scene = lax.axis_index("scene")
    micros, _, channels, width = grads.shape
    sums = sum_rows(found, 2 + micros)
    second = sum(sums[2:]) + jnp.sum(expected[...], axis=0, keepdims=True)
    own_half(second[:, :channels], scene, second_shift_grad)
    own_half(second[:, channels:], scene, second_gain_grad)
    sums = sums[:2]
    own_half(sums[0][:, :channels] + sums[0][:, channels:], scene, gain_grad)
    own_half(sums[1][:, :channels] + sums[1][:, channels:], scene, shift_grad)
    turned = columns_of(sums) * (1.0 / (found.shape[0] * rows * width))
    masks = edges(channels, width)
    half = 6 * channels
    second_copy.wait()
    for micro in range(micros):
        for at, ref, columns_used in ((0, before, slice(0, half)), (rows, after, slice(half, 2 * half))):
            window = jnp.concatenate([spread(ref[micro, row], masks) for row in range(2)], axis=0)
            parts = dot(b_second[:, columns_used], window)
            for j in range(2):
                halo[micro, at + j] = parts[channels * j : channels * (j + 1)] * slopes[micro, at + j]

    def value_of(micro, index):
        grad = grads[micro, index]
        if index < 2 or index >= rows:
            grad = grad + halo[micro, index]
        return grad, first_out[micro, index]

    low_rows(turned, value_of, first_out, first_stats, cols[0:channels, 2:3], low, rows + 2, -1, rows, tiles)
    weight_copy.wait()
    conv_rows(low, b_first, grid, grid.shape)
    conv_grad(low, 1, canvas, 0, first_grad, rows)
    half = channels // 2
    peers, block = send.shape[:2]
    for s in range(2):
        parts = half_rows(first_grad, half, s) + half_rows(second_grad, half, s)
        mine = top_grad[s * channels : (s + 1) * channels, :]
        parts.append(jnp.concatenate([mine[:half], mine[half:]], axis=1))
        parts = jnp.concatenate(parts, axis=0)
        whole[s, 0 : parts.shape[0]] = parts
        if whole.shape[1] > parts.shape[0]:
            whole[s, parts.shape[0] :] = jnp.zeros((whole.shape[1] - parts.shape[0], LANES), F32)
    slots = columns.shape[0]
    lane = lax.broadcasted_iota(jnp.int32, (slots, width), 1).astype(F32)
    picked = []
    for micro in range(micros):
        at = 2 + micro
        column = columns[:, at : at + 1] - 1.0
        column = column - jnp.floor(column * (1.0 / width)) * width
        place = jnp.floor((where_rows[at : at + 1] - 1.0) * (1.0 / width))
        chosen = jnp.where(lane == column, 1.0, 0.0).astype(BF16)
        here = dot_lanes(grid[micro].reshape(rows * channels, width), chosen)
        total = jnp.zeros((channels, slots), F32)
        for r in range(rows):
            total = total + jnp.where(place == r * 1.0, here[r * channels : (r + 1) * channels], 0.0)
        picked.append(total)
    picked = jnp.transpose(jnp.concatenate(picked, axis=0))
    capacity = slots // tiles
    rest = block - capacity - 2 * each
    for peer in range(peers):
        spot = peer // 2
        parts = [picked[spot * capacity : (spot + 1) * capacity]]
        parts += [whole[s, peer * each : (peer + 1) * each] for s in range(2)]
        parts.append(jnp.zeros((rest, LANES), F32))
        send[peer] = jnp.concatenate(parts, axis=0).astype(BF16)


def pillar_weights_kernel(rows, w_pillar, cols, pooled, out, lifted):
    micros, channels, wide = out.shape
    pillars = pooled.shape[2]
    inputs = w_pillar.shape[1]
    gain, shift = cols[0:channels, 0:1], cols[0:channels, 1:2]
    for micro in range(micros):
        lifted[...] = dot(w_pillar[...], rows[micro, 0:inputs])
        _, limit = pillar_notes(rows, micro, inputs, pillars)
        centre, rstd = pooled[micros + micro, :, 0:1], pooled[micros + micro, :, 1:2]
        pool = pooled[micro]
        for n in range(wide // pillars):
            piece = slice(n * pillars, (n + 1) * pillars)
            normed = (lifted[:, piece] - centre) * rstd * gain + shift
            gate = sigmoid(normed)
            act = normed * gate
            slope = gate + act * (1.0 - gate)
            out[micro, :, piece] = jnp.where(limit > n, jnp.exp(act - pool) * slope, 0.0)


def pillar_back_kernel(found, rows_in, w_pillar, cols, pooled, factors, send, grads, lifted, rows, sems,
                       *, capacity, each):
    fetched = move(rows_in, rows, sems, 0)
    micros = rows.shape[0]
    _, channels, pillars = pooled.shape
    stats = pooled.at[micros : 2 * micros]
    inputs = w_pillar.shape[1]
    depth = rows.shape[2] // pillars
    scene = lax.axis_index("scene")
    peers = found.shape[0]
    slot_count = peers // 2 * capacity
    returned = jnp.concatenate(
        [found[2 * t + scene].astype(F32)[0:capacity] for t in range(peers // 2)], axis=0
    )
    turned = jnp.transpose(returned)
    place = lax.broadcasted_iota(jnp.int32, (slot_count, pillars), 0).astype(F32)
    gain = cols[0:channels, 0:1]
    gain_sums, shift_sums = [], []
    outer = jnp.zeros((16, channels), F32)
    fetched.wait()
    for micro in range(micros):
        lifted[...] = dot(w_pillar[...], rows[micro, 0:inputs])
        slot, _ = pillar_notes(rows, micro, inputs, pillars)
        chosen = jnp.where(place == slot, 1.0, 0.0).astype(BF16)
        back = dot(turned[micro * channels : (micro + 1) * channels].astype(BF16), chosen)
        centre, rstd = stats[micro, :, 0:1], stats[micro, :, 1:2]
        gain_sum = jnp.zeros((channels, pillars), F32)
        shift_sum = jnp.zeros((channels, pillars), F32)
        for n in range(depth):
            piece = slice(n * pillars, (n + 1) * pillars)
            grad = back * factors[micro, :, piece]
            grads[micro, :, piece] = grad
            gain_sum = gain_sum + grad * (lifted[:, piece] - centre)
            shift_sum = shift_sum + grad
        gain_sum = gain_sum * rstd
        gain_sums.append(gain_sum)
        shift_sums.append(shift_sum)
        scale = jnp.transpose(jnp.broadcast_to(rstd * gain, (channels, LANES)))[0:1]
        outer = outer + dot_lanes(rows[micro], grads[micro].astype(BF16)) * scale
    lines = [row_of(*gain_sums), row_of(*shift_sums)]
    for k in range(0, 10, 2):
        lines.append(jnp.concatenate([outer[k : k + 1], outer[k + 1 : k + 2]], axis=1))
    exact = jnp.concatenate(lines, axis=0)
    kept = 2 * exact.shape[0]
    weights = jnp.sum(found[...].astype(F32), axis=0)
    rest = send.shape[2] - kept - each
    for s in range(2):
        mine = weights[capacity + s * each : capacity + (s + 1) * each]
        block = exact_rows(exact) + [mine] + ([jnp.zeros((rest, LANES), F32)] if rest > 0 else [])
        block = jnp.concatenate(block, axis=0).astype(BF16)
        send[:, s] = jnp.broadcast_to(block[None], (send.shape[0],) + block.shape)


def points_kernel(
    found, rows_in, grads, w_pillar, cols, pooled,
    points_grad, pillar_grad, gain_grad, shift_grad, first_grad, second_grad, up_grad, rows, lifted, sems,
    *, each
):
    fetched = move(rows_in, rows, sems, 0)
    scene = lax.axis_index("scene")
    micros, channels, _ = grads.shape
    stats = pooled.at[micros : 2 * micros]
    _, _, inputs, depth, pillars = points_grad.shape
    half = channels // 2
    kept = 7
    total = jnp.sum(found[...].astype(F32), axis=0)
    total = total[0:kept] + total[kept : 2 * kept]
    own_half(total[0:1, :channels] + total[0:1, channels:], scene, gain_grad)
    own_half(total[1:2, :channels] + total[1:2, channels:], scene, shift_grad)
    turned = jnp.transpose(jnp.concatenate([total, jnp.zeros((1, LANES), F32)], axis=0))
    weight_grad = jnp.concatenate(
        [turned[(k % 2) * channels : (k % 2 + 1) * channels, 2 + k // 2 : 3 + k // 2] for k in range(inputs)],
        axis=1,
    )
    weight = jnp.transpose(w_pillar[...].astype(F32)).astype(BF16)
    fetched.wait()
    for micro in range(micros):
        lifted[...] = dot(w_pillar[...], rows[micro, 0:inputs])
        part = slice(micro * channels, (micro + 1) * channels)
        centre, rstd, inverse = stats[micro, :, 0:1], stats[micro, :, 1:2], stats[micro, :, 2:3]
        factor = cols[0:channels, 0:1] * rstd
        gain_part, shift_part = turned[part, 0:1], turned[part, 1:2]
        spun, mean = stats[micro, :, 16 : 16 + inputs], stats[micro, :, 32 : 32 + inputs]
        weight_grad = weight_grad - factor * (shift_part * mean + gain_part * rstd * spun)
        gain_part, shift_part = gain_part * inverse * rstd, shift_part * inverse
        _, limit = pillar_notes(rows, micro, inputs, pillars)
        for n in range(depth):
            piece = slice(n * pillars, (n + 1) * pillars)
            low = factor * (grads[micro, :, piece] - shift_part - (lifted[:, piece] - centre) * gain_part)
            low = jnp.where(limit > n, low, 0.0).astype(BF16)
            points_grad[micro, 0, :, n, :] = dot(weight, low)
    weight_grad = jnp.concatenate([weight_grad, jnp.zeros((channels, LANES - inputs), F32)], axis=1)
    weight_grad = jnp.transpose(weight_grad)[0:inputs]
    pillar_grad[...] = jnp.where(scene == 0, weight_grad[:, :half], weight_grad[:, half:])
    whole = jnp.concatenate(
        [found[peer].astype(F32)[2 * kept : 2 * kept + each] for peer in range(found.shape[0])], axis=0
    )
    for index, out in enumerate((first_grad, second_grad)):
        base = index * 9 * half * channels // LANES
        lead = 3 * half
        mine = whole[base : base + lead]
        wing = whole[base + lead : base + lead + lead // 2]
        wing = jnp.concatenate([wing[:, :channels], wing[:, channels:]], axis=0)
        both = jnp.concatenate([mine, wing], axis=1)
        for a in range(3):
            for b in range(3):
                at = (3 * a + b) * channels
                out[:, at : at + channels] = both[b * half : (b + 1) * half, a * channels : (a + 1) * channels]
    base = 2 * 9 * half * channels // LANES
    top = whole[base : base + half]
    up_grad[...] = jnp.concatenate([top[:, :channels], top[:, channels:]], axis=0)


def swap(blocks, axes):
    return lax.all_to_all(blocks, axes, split_axis=0, concat_axis=0)


def shards(
    points, point_counts, pillar_tile, pillar_cell,
    pillar_weight, pillar_gain, pillar_shift,
    first_weight, first_gain, first_shift,
    second_weight, second_gain, second_shift,
    up_weight, up_gain, up_shift, cotangent,
):
    micros, _, inputs, depth, pillars = points.shape
    channels = up_weight.shape[1]
    upper = cotangent.shape[2]
    rows, width = cotangent.shape[3:]
    tiles = lax.axis_size("tile")
    scenes = lax.axis_size("scene")
    peers = tiles * scenes
    capacity = 2 * pillars // tiles
    slot_count = tiles * capacity
    half = channels // 2

    def vmem(shape, dtype):
        return pltpu.VMEM(shape, dtype)

    def grid(high, dtype=F32, lead=channels):
        return ((micros, high, lead, width), dtype)

    sums = ((peers, 2, LANES), F32)
    sources = (
        pillar_tile, pillar_cell, point_counts, points,
        first_weight, second_weight, up_weight, pillar_weight.T,
        pillar_gain, pillar_shift, first_gain, first_shift, second_gain, second_shift, up_gain, up_shift,
    )
    moments, packed, point_rows = run(
        functools.partial(moments_kernel, capacity=capacity),
        [
            ((tiles, scenes, 4, LANES), F32), ((layout(half, channels)[-1] + 16, LANES), BF16),
            ((micros, 16, depth * pillars), BF16),
        ],
        *sources,
        hbm=range(len(sources)), copies=len(sources), limit=WIDE_LIMIT,
        scratch=[vmem(source.shape, source.dtype) for source in sources]
        + [vmem((inputs * depth, pillars), F32)],
    )
    moments = swap(moments.reshape(peers, 4, LANES), BOTH)
    both = lax.all_gather(packed, "scene")
    taps = ((2 * channels, 12 * channels), BF16)
    w_pillar, cols, l_first, l_second, b_first, b_second, w_up, w_up_t = run(
        functools.partial(unpack_kernel, inputs=inputs),
        [
            ((channels, inputs), BF16), ((LANES, 8), F32), taps, taps + (1,), taps + (1,), taps + (1,),
            ((upper, channels), BF16), ((channels, upper), BF16),
        ],
        both,
        scratch=[vmem(*taps), vmem(*taps), vmem(*taps)], copies=3,
    )
    cot = cotangent[:, 0].transpose(0, 2, 1, 3)

    send, pooled = run(
        functools.partial(pillar_kernel, capacity=capacity),
        [((slot_count, 3 * LANES), BF16), ((2 * micros, channels, pillars), F32)],
        moments, point_rows, w_pillar, cols,
        scratch=[vmem((channels, depth * pillars), F32), vmem((channels, depth * pillars), F32)],
    )
    arrived = swap(send.reshape(tiles, capacity, 3 * LANES), "tile").reshape(slot_count, 3 * LANES)
    cell_columns, cell_rows = run(
        functools.partial(cells_kernel, capacity=capacity),
        [((slot_count, LANES), F32), ((8, slot_count), F32)],
        moments,
        cost=pl.CostEstimate(flops=10**7, bytes_accessed=10**6, transcendentals=0),
    )
    (pillar_factors,) = run(
        pillar_weights_kernel,
        [((micros, channels, depth * pillars), F32)],
        point_rows, w_pillar, cols, pooled,
        scratch=[vmem((channels, depth * pillars), F32)],
        cost=pl.CostEstimate(flops=10**7, bytes_accessed=10**6, transcendentals=0),
    )
    arrived, cot, pillar_factors = lax.optimization_barrier((arrived, cot, pillar_factors))

    first_out, canvas, send = run(
        functools.partial(canvas_kernel, rows=rows),
        [grid(rows + 2), grid(rows + 2, BF16), sums],
        arrived, cell_columns, cell_rows, l_first,
        scratch=[vmem(*grid(rows + 4, BF16, 3 * channels))],
    )
    second_out, first_act, first_slopes, first_stats, send = run(
        functools.partial(second_kernel, rows=rows, tiles=tiles),
        [grid(rows), grid(rows + 2, BF16), grid(rows + 2), ((LANES, 8), F32), sums],
        swap(send, BOTH), cols, first_out, l_second,
        hbm=(3,), scratch=[vmem(*grid(rows + 2, BF16, 3 * channels)), vmem(*taps)], copies=1,
    )
    part = -(-micros * channels // peers)
    second_act, up_out, slopes, plain, crossed, second_stats, send = run(
        functools.partial(up_kernel, rows=rows),
        [
            grid(rows, BF16), grid(rows, F32, upper), grid(rows, F32, 2 * channels), ((micros, LANES), F32),
            ((peers * part, LANES), F32), ((LANES, 8), F32), ((peers, -(-(2 * micros + part) // 8) * 8, LANES), F32),
        ],
        swap(send, BOTH), cols, second_out, w_up,
    )
    features, grads, mixed, top_stats, send = run(
        functools.partial(top_kernel, rows=rows, each=part),
        [
            grid(rows, BF16, upper), grid(rows, F32, upper), ((micros, LANES), F32), ((LANES, 8), F32),
            ((peers, -(-(6 * micros + part) // 8) * 8, LANES), BF16),
        ],
        swap(send, BOTH), cols, up_out, cot, slopes, plain, w_up_t,
    )
    features = with_layout_constraint(features.transpose(0, 2, 1, 3)[:, None], Layout((0, 1, 2, 3, 4)))
    features, send = lax.optimization_barrier((features, send))
    edge = ((micros, 2, channels, width), BF16)
    vector, top_vector, matrix = ((half,), F32), ((upper // 2,), F32), ((half, 9 * channels), F32)
    rising = [(i, i + 1) for i in range(tiles - 1)]
    falling = [(j, i) for i, j in rising]
    cross = ((3 * channels, 3 * channels), F32)
    low, top_low, rising_edge, falling_edge, up_gain_grad, up_shift_grad, expected, extras = run(
        functools.partial(middle_back_kernel, rows=rows, each=part),
        [
            grid(rows, BF16, 3 * channels), grid(rows, BF16, upper), edge, edge, top_vector, top_vector,
            ((micros, LANES), F32), ((micros, LANES), F32),
        ],
        swap(send, BOTH), cols, grads, up_out, top_stats, second_out, second_stats, slopes, w_up, w_up_t,
        mixed, plain, crossed,
        scratch=[vmem(*grid(rows))],
    )
    before = lax.ppermute(rising_edge, "tile", rising)
    after = lax.ppermute(falling_edge, "tile", falling)
    first_dz, top_grad, second_cross, send = run(
        functools.partial(first_back_kernel, rows=rows, tiles=tiles),
        [grid(rows + 2), ((upper, channels), F32), cross, ((peers, 2 + micros, LANES), F32)],
        low, top_low, second_act, first_act, first_out, first_stats, first_slopes, b_second, extras,
        hbm=(7,), scratch=[vmem(*taps)], copies=1,
        cost=pl.CostEstimate(flops=2 * 10**9, bytes_accessed=10**7, transcendentals=0),
    )
    length = (2 * 9 * half * channels + upper * half) // LANES
    each = -(-length // peers)
    block = -(-(capacity + 2 * each) // 8) * 8
    send, first_gain_grad, first_shift_grad, second_gain_grad, second_shift_grad = run(
        functools.partial(pick_kernel, rows=rows, tiles=tiles, each=each),
        [((peers, block, LANES), BF16), vector, vector, vector, vector],
        swap(send, BOTH), cols, first_dz,
        before, after, first_out, first_stats, first_slopes, b_first, b_second, cell_columns, cell_rows, canvas, second_cross, top_grad, expected,
        hbm=(8, 9),
        scratch=[
            vmem(*grid(rows + 2, BF16, 3 * channels)), vmem(*grid(rows, BF16)), vmem(*taps), vmem(*taps),
            vmem(*grid(rows + 2)), vmem(*cross), vmem((scenes, peers * each, LANES), F32),
        ],
        copies=2,
    )
    block = -(-(14 + each) // 8) * 8
    send, pillar_dz = run(
        functools.partial(pillar_back_kernel, capacity=capacity, each=each),
        [((tiles, scenes, block, LANES), BF16), ((micros, channels, depth * pillars), F32)],
        swap(send, BOTH), point_rows, w_pillar, cols, pooled, pillar_factors,
        hbm=(1,),
        scratch=[vmem((channels, depth * pillars), F32), vmem((micros, 16, depth * pillars), BF16)],
        copies=1,
    )
    points_grad, pillar_grad, pillar_gain_grad, pillar_shift_grad, first_grad, second_grad, up_grad = run(
        functools.partial(points_kernel, each=each),
        [
            ((micros, 1, inputs, depth, pillars), F32), ((inputs, half), F32), vector, vector,
            matrix, matrix, ((upper // 2, channels), F32),
        ],
        swap(send.reshape(peers, block, LANES), BOTH), point_rows, pillar_dz, w_pillar, cols, pooled,
        hbm=(1,),
        scratch=[vmem((micros, 16, depth * pillars), BF16), vmem((channels, depth * pillars), F32)],
        copies=1,
    )
    return (
        features, points_grad,
        pillar_grad.T, pillar_gain_grad, pillar_shift_grad,
        first_grad, first_gain_grad, first_shift_grad,
        second_grad, second_gain_grad, second_shift_grad,
        up_grad, up_gain_grad, up_shift_grad,
    )


def solution(mesh):
    matrix, vector = P("scene", None), P("scene")
    grid = P(None, "scene", None, "tile", None)
    cloud = P(None, "scene", None, None, "tile")
    pillar = P(None, "scene", "tile")
    weights = (matrix, vector, vector) * 4
    return jax.shard_map(
        shards,
        mesh=mesh,
        in_specs=(cloud, pillar, pillar, pillar) + weights + (grid,),
        out_specs=(grid, cloud) + weights,
        check_vma=False,
    )
```

```python
import functools

import jax
import jax.numpy as jnp
from jax import lax
from jax.experimental import pallas as pl
from jax.experimental.layout import Layout, with_layout_constraint
from jax.experimental.pallas import tpu as pltpu
from jax.sharding import PartitionSpec as P

norm_eps = 0.001
BOTH = ("tile", "scene")
F32 = jnp.float32
BF16 = jnp.bfloat16
VMEM_LIMIT = 24 * 1024 * 1024
WIDE_LIMIT = 60 * 1024 * 1024
LANES = 128


def run(kernel, outs, *args, hbm=(), scratch=(), copies=0, cost=None, limit=VMEM_LIMIT):
    specs = [
        pl.BlockSpec(memory_space=pltpu.HBM if index in hbm else pltpu.VMEM) for index in range(len(args))
    ]
    scratch = list(scratch)
    if copies:
        scratch.append(pltpu.SemaphoreType.DMA((copies,)))
    return pl.pallas_call(
        kernel,
        out_shape=[jax.ShapeDtypeStruct(out[0], out[1]) for out in outs],
        in_specs=specs,
        out_specs=[
            pl.BlockSpec(memory_space=pltpu.HBM if len(out) > 2 else pltpu.VMEM) for out in outs
        ],
        scratch_shapes=scratch,
        compiler_params=pltpu.CompilerParams(vmem_limit_bytes=limit),
        cost_estimate=cost,
    )(*args)


def move(source, target, sems, index):
    copy = pltpu.make_async_copy(source, target, sems.at[index])
    copy.start()
    return copy


def dot(left, right, precision=None):
    return jnp.dot(left, right, preferred_element_type=F32, precision=precision)


def dot_lanes(left, right, precision=None):
    return lax.dot_general(
        left, right, (((1,), (1,)), ((), ())), preferred_element_type=F32, precision=precision
    )


def sigmoid(values):
    return 0.5 + 0.5 * jnp.tanh(0.5 * values)


def fold(values):
    total = values[:, :LANES]
    for start in range(LANES, values.shape[1], LANES):
        total = total + values[:, start : start + LANES]
    return total


def row_of(left, right=None):
    both = left if right is None else jnp.concatenate([left, right], axis=0)
    return jnp.sum(jnp.transpose(both), axis=0, keepdims=True)


def columns_of(rows):
    rows = rows + [jnp.zeros((8 - len(rows), LANES), F32)] if len(rows) < 8 else rows
    return jnp.transpose(jnp.concatenate(rows, axis=0))


def inside(tile, row, height):
    tiles, rows = height
    place = tile * rows + row
    return jnp.where((place >= 0) & (place < tiles * rows), 1.0, 0.0).astype(F32)


def send_all(ref, rows):
    for index, row in enumerate(rows):
        ref[:, index : index + 1, :] = jnp.broadcast_to(row[None], (ref.shape[0], 1, LANES))


def pooled_stats(means, squares, count):
    peers = means.shape[0]
    mean = jnp.sum(means, axis=0, keepdims=True) * (1.0 / peers)
    away = means - mean
    spread = jnp.sum(squares + count * away * away, axis=0, keepdims=True) * (1.0 / (peers * count))
    return mean, lax.rsqrt(spread + norm_eps)


def stat_columns(found, count):
    return columns_of(list(pooled_stats(found[:, 0, :], found[:, 1, :], count)))


def sum_rows(found, lines):
    return [jnp.sum(found[:, index, :], axis=0, keepdims=True) for index in range(lines)]


def own_half(row, scene, out):
    size = out.shape[0]
    out[...] = jnp.where(scene == 0, row[:, 0:size], row[:, size : 2 * size]).reshape(size)


def edges(channels, width):
    lane = lax.broadcasted_iota(jnp.int32, (channels, width), 1)
    return lane > 0, lane < width - 1


def spread(row, masks):
    zero = jnp.zeros_like(row)
    left = jnp.where(masks[0], pltpu.roll(row, 1, 1), zero)
    right = jnp.where(masks[1], pltpu.roll(row, row.shape[1] - 1, 1), zero)
    return jnp.concatenate([left, row, right], axis=0)


def layout(half, channels):
    first = 0
    second = first + half * -(-9 * channels // LANES)
    up = second + half * -(-9 * channels // LANES)
    vectors = up + channels
    return first, second, up, vectors, vectors + 16


def widen(value):
    missing = LANES - value.shape[1]
    if missing == 0:
        return value
    return jnp.concatenate([value, jnp.zeros((value.shape[0], missing), value.dtype)], axis=1)


def pack(held, out):
    first, second, up, pillar = held[:4]
    half, channels = first.shape[0], up.shape[1]
    starts = layout(half, channels)
    for ref, start in ((first, starts[0]), (second, starts[1])):
        for j in range(-(-9 * channels // LANES)):
            out[start + j * half : start + (j + 1) * half, :] = widen(
                ref[:, j * LANES : min((j + 1) * LANES, 9 * channels)]
            )
    out[starts[2] : starts[2] + channels, :] = widen(up[...])
    rows = [vector[...].astype(F32).reshape(1, -1) for vector in held[4:]]
    rows = [widen(row) for row in rows] + [jnp.zeros((16 - len(rows), LANES), F32)]
    turned = widen(pillar[...].astype(F32))
    rows += [turned, jnp.zeros((16 - turned.shape[0], LANES), F32)]
    out[starts[3] :, :] = jnp.concatenate(rows, axis=0).astype(BF16)


def unpack_kernel(
    both, w_pillar, cols, l_first, l_second, b_first, b_second, w_up, w_up_t,
    h_second, h_first_back, h_second_back, sems, *, inputs
):
    half = w_pillar.shape[0] // 2
    channels = 2 * half
    starts = layout(half, channels)
    tiles = -(-9 * channels // LANES)

    def wide(start):
        return jnp.concatenate(
            [
                jnp.concatenate(
                    [both[s, start + j * half : start + (j + 1) * half, :] for j in range(tiles)], axis=1
                )
                for s in range(2)
            ],
            axis=0,
        ).astype(F32)

    up = jnp.concatenate(
        [both[s, starts[2] : starts[2] + channels, 0:channels] for s in range(2)], axis=0
    )
    w_up[...] = up
    w_up_t[...] = jnp.transpose(up.astype(F32)).astype(BF16)
    turned = jnp.concatenate(
        [both[s, starts[4] : starts[4] + 16, 0:half].astype(F32) for s in range(2)], axis=1
    )
    w_pillar[...] = jnp.transpose(widen(turned))[0:channels, 0:inputs].astype(BF16)
    vectors = [both[s, starts[3] : starts[3] + 16, :].astype(F32) for s in range(2)]
    rows = []
    for index in range(8):
        size = half if index < 6 else channels
        row = jnp.concatenate([vectors[s][index : index + 1, 0:size] for s in range(2)], axis=1)
        rows.append(jnp.concatenate([row] * (LANES // (2 * size)), axis=1))
    cols[...] = columns_of(rows)
    zero = jnp.zeros((channels, 3 * channels), F32)
    copies = []
    for weight, ahead, back in (
        (wide(starts[0]), l_first, h_first_back), (wide(starts[1]), h_second, h_second_back)
    ):
        weight = weight[:, : 9 * channels]
        turned = jnp.transpose(weight)
        flipped = jnp.concatenate(
            [turned[tap * channels : (tap + 1) * channels] for tap in range(8, -1, -1)], axis=1
        )
        for ref, taps in ((ahead, weight), (back, flipped)):
            ref[0:channels, :] = jnp.concatenate([taps, zero], axis=1).astype(BF16)
            ref[channels : 2 * channels, :] = jnp.concatenate([zero, taps], axis=1).astype(BF16)
    copies.append(move(h_second, l_second, sems, 0))
    copies.append(move(h_first_back, b_first, sems, 1))
    copies.append(move(h_second_back, b_second, sems, 2))
    for copy in copies:
        copy.wait()


def slot_line(wide, depth, inputs):
    return jnp.concatenate([wide[pl.ds(n, inputs, stride=depth), :] for n in range(depth)], axis=1)


def slot_mask(count, depth):
    return jnp.concatenate([jnp.where(count > n, 1.0, 0.0) for n in range(depth)], axis=1)


def ranks(tile):
    pillars = tile.shape[1]
    across = jnp.broadcast_to(tile, (pillars, pillars))
    down = jnp.transpose(across)
    row = lax.broadcasted_iota(jnp.int32, (pillars, pillars), 0)
    col = lax.broadcasted_iota(jnp.int32, (pillars, pillars), 1)
    return jnp.sum(jnp.where((across == down) & (row < col), 1.0, 0.0), axis=0, keepdims=True)


def moments_kernel(*refs, capacity):
    number = 16
    sources, out, packed, lines_out = refs[:number], *refs[number : number + 3]
    held, wide, sems = refs[number + 3 : 2 * number + 3], refs[-2], refs[-1]
    copies = [move(sources[i], held[i], sems, i) for i in range(number)]
    tiles, cells, counts, points = held[:4]
    micros, _, inputs, depth, pillars = points.shape
    peers, scenes = out.shape[:2]
    copies[0].wait()
    copies[1].wait()
    lines, slot_rows = [], []
    for micro in range(micros):
        tile = tiles[micro].astype(F32)
        cell = (cells[micro] + 1).astype(F32)
        high = jnp.floor(cell * (1.0 / 16.0))
        low = cell - high * 16.0
        rank = ranks(tile)
        slot_rows.append(tile * capacity + rank)
        spot = lax.broadcasted_iota(jnp.int32, (capacity, pillars), 0).astype(F32)
        placed = jnp.where(spot == rank, 1.0, 0.0).astype(BF16)
        peer = lax.broadcasted_iota(jnp.int32, (peers, pillars), 0).astype(F32)
        for group in range(3):
            named = tile == peer + (group - 1.0)
            lines.append(
                16.0 * dot_lanes(jnp.where(named, high, 0.0).astype(BF16), placed)
                + dot_lanes(jnp.where(named, low, 0.0).astype(BF16), placed)
            )
    used = 3 * micros * capacity
    line = jnp.concatenate(lines + [jnp.zeros((peers, LANES - used), F32)], axis=1).reshape(peers, 1, LANES)
    for scene in range(scenes):
        out[:, scene, micros : micros + 1, :] = line
    copies[2].wait()
    copies[3].wait()
    parts, mean_rows, totals = [], [], []
    for micro in range(micros):
        wide[...] = points[micro, 0].astype(F32).reshape(inputs * depth, pillars)
        rows = slot_line(wide, depth, inputs)
        notes = jnp.concatenate([slot_rows[micro], counts[micro].astype(F32)], axis=0)
        notes = jnp.concatenate([notes, jnp.zeros((2, rows.shape[1] - pillars), F32)], axis=1)
        lines_out[micro] = jnp.concatenate(
            [rows, notes, jnp.zeros((14 - inputs, rows.shape[1]), F32)], axis=0
        ).astype(BF16)
        mask = slot_mask(counts[micro], depth)
        total = jnp.sum(mask, axis=1, keepdims=True)
        mean = jnp.sum(rows * mask, axis=1, keepdims=True) / total
        centred = jnp.concatenate(
            [(rows - mean) * mask, jnp.zeros((16 - inputs, rows.shape[1]), F32)], axis=0
        )
        high = centred.astype(BF16)
        parts += [high, (centred - high.astype(F32)).astype(BF16)]
        lane = lax.broadcasted_iota(jnp.int32, (inputs, inputs), 1)
        diagonal = lax.broadcasted_iota(jnp.int32, (inputs, inputs), 0) == lane
        mean_rows.append(jnp.sum(jnp.where(diagonal, mean, 0.0), axis=0, keepdims=True))
        totals.append(total)
    parts = jnp.concatenate(parts, axis=0)
    every = dot_lanes(parts, parts)
    for micro in range(micros):
        at = 32 * micro
        square = every[at : at + 32, at : at + 32]
        products = (
            square[0:inputs, 0:inputs] + square[16 : 16 + inputs, 0:inputs]
            + square[0:inputs, 16 : 16 + inputs] + square[16 : 16 + inputs, 16 : 16 + inputs]
        )
        row = jnp.concatenate(
            [products[k : k + 1] for k in range(inputs)]
            + [mean_rows[micro], totals[micro], jnp.zeros((1, LANES - inputs * inputs - inputs - 1), F32)],
            axis=1,
        )
        for scene in range(scenes):
            out[:, scene, micro : micro + 1, :] = jnp.broadcast_to(row[None], (peers, 1, LANES))
    for copy in copies[4:]:
        copy.wait()
    pack(held[4:], packed)
    lines = [held[7][k : k + 1].astype(F32) for k in range(inputs)]
    lines += [held[8][...].astype(F32).reshape(1, -1), held[9][...].astype(F32).reshape(1, -1)]
    fit = LANES // lines[0].shape[1]
    for row in range(-(-len(lines) // fit)):
        line = widen(jnp.concatenate(lines[row * fit : (row + 1) * fit], axis=1))
        for scene in range(scenes):
            at = micros + 1 + row
            out[:, scene, at : at + 1, :] = jnp.broadcast_to(line[None], (peers, 1, LANES))
    for scene in range(scenes):
        for at in range(micros + 1 - (-len(lines) // fit), out.shape[2]):
            out[:, scene, at : at + 1, :] = jnp.zeros((peers, 1, LANES), F32)


def cells_kernel(found, columns, rows, *, capacity):
    scene = lax.axis_index("scene")
    slots = columns.shape[0]
    peers = found.shape[0]
    values = found[:, 2, :]
    slot = lax.broadcasted_iota(jnp.int32, (slots, peers), 0)
    peer = lax.broadcasted_iota(jnp.int32, (slots, peers), 1)
    lane = lax.broadcasted_iota(jnp.int32, (slots, LANES), 1)
    row = lax.broadcasted_iota(jnp.int32, (slots, LANES), 0)
    result = jnp.zeros((slots, LANES), F32)
    chosen = jnp.where(peer == 2 * (slot // capacity) + scene, 1.0, 0.0)
    spread = dot(chosen, values, lax.Precision.HIGHEST)
    for micro in range(2):
        for group in range(3):
            mine = jnp.where(lane == (3 * micro + group) * capacity + row % capacity, spread, 0.0)
            column = jnp.sum(mine, axis=1, keepdims=True)
            result = jnp.where(lane == 2 * group + micro, column, result)
    columns[...] = result
    rows[...] = jnp.transpose(result)[0:8]


def pillar_notes(rows, micro, inputs, pillars):
    notes = rows[micro, :, 0:pillars].astype(F32)
    return notes[inputs : inputs + 1], notes[inputs + 1 : inputs + 2]


def pillar_kernel(
    found, point_rows, send, pooled, lifted, acts, *, capacity, inputs
):
    micros = point_rows.shape[0]
    channels, pillars = pooled.shape[1:]
    depth = point_rows.shape[2] // pillars
    half = channels // 2
    fit = LANES // half
    tile = lax.axis_index("tile")
    cores = [found[2 * tile + core] for core in range(2)]
    lines = [
        jnp.concatenate(
            [
                core[micros + 1 + k // fit : micros + 2 + k // fit, (k % fit) * half : (k % fit + 1) * half]
                for core in cores
            ],
            axis=1,
        )
        for k in range(inputs + 2)
    ]
    lines = jnp.concatenate(lines + [jnp.zeros((16 - len(lines), channels), F32)], axis=0)
    params = jnp.transpose(widen(lines))[0:channels]
    wide_weight = params[:, 0:inputs]
    weight = wide_weight.astype(BF16)
    rows_out = send.shape[0]
    square = inputs * inputs
    stacked, slot_rows = [], []
    for micro in range(micros):
        lifted[...] = dot(weight, point_rows[micro, 0:inputs])
        moments = found[:, micro, :]
        sizes = moments[:, square + inputs : square + inputs + 1]
        means = moments[:, square : square + inputs]
        count = jnp.sum(sizes, axis=0, keepdims=True)
        mean = jnp.sum(means * sizes, axis=0, keepdims=True) / count
        away = means - mean
        products = lax.dot_general(
            away * sizes, away, (((0,), (0,)), ((), ())),
            preferred_element_type=F32, precision=lax.Precision.HIGHEST,
        )
        summed = jnp.sum(moments, axis=0, keepdims=True)
        products = products + jnp.concatenate(
            [summed[:, k * inputs : (k + 1) * inputs] for k in range(inputs)], axis=0
        )
        cov = products / count
        spun = wide_weight[:, 0:1] * cov[0:1]
        for k in range(1, inputs):
            spun = spun + wide_weight[:, k : k + 1] * cov[k : k + 1]
        spread = jnp.sum(spun * wide_weight, axis=1, keepdims=True)
        centre = jnp.sum(wide_weight * mean, axis=1, keepdims=True)
        rstd = lax.rsqrt(spread + norm_eps)
        inverse = jnp.broadcast_to(1.0 / count, (channels, 1))
        pooled[micros + micro] = jnp.concatenate(
            [
                centre, rstd, inverse, jnp.zeros((channels, 13), F32),
                spun, jnp.zeros((channels, 16 - inputs), F32),
                jnp.broadcast_to(mean, (channels, inputs)), jnp.zeros((channels, LANES - 32 - inputs), F32),
            ],
            axis=1,
        )
        scale = rstd * params[:, inputs : inputs + 1]
        shift = params[:, inputs + 1 : inputs + 2]
        slot, limit = pillar_notes(point_rows, micro, inputs, pillars)
        slot_rows.append(slot)
        top = jnp.full((channels, pillars), -jnp.inf, F32)
        for n in range(depth):
            piece = slice(n * pillars, (n + 1) * pillars)
            normed = (lifted[:, piece] - centre) * scale + shift
            act = normed * sigmoid(normed)
            acts[:, piece] = act
            top = jnp.maximum(top, jnp.where(limit > n, act, -jnp.inf))
        total = jnp.zeros((channels, pillars), F32)
        for n in range(depth):
            piece = slice(n * pillars, (n + 1) * pillars)
            total = total + jnp.where(limit > n, jnp.exp(acts[:, piece] - top), 0.0)
        result = top + jnp.log(total)
        pooled[micro] = result
        parts = [jnp.zeros((channels, pillars), F32)] * micros
        parts[micro] = result.astype(BF16).astype(F32)
        stacked.append(jnp.transpose(jnp.concatenate(parts, axis=0)))
    values = jnp.concatenate(stacked, axis=0).astype(BF16)
    for group in range(3):
        place = lax.broadcasted_iota(jnp.int32, (rows_out, pillars), 0) + (group - 1) * capacity
        chosen = jnp.concatenate(
            [jnp.where(place.astype(F32) == row, 1.0, 0.0) for row in slot_rows], axis=1
        ).astype(BF16)
        send[:, group * LANES : (group + 1) * LANES] = dot(chosen, values).astype(BF16)


def own_stats(ref, first_row, rows, send):
    micros, _, channels, width = ref.shape
    sums, squares = [], []
    for micro in range(micros):
        total = fold(ref[micro, first_row])
        for row in range(first_row + 1, first_row + rows):
            total = total + fold(ref[micro, row])
        sums.append(total * (1.0 / (rows * width)))
    means = [jnp.sum(total, axis=1, keepdims=True) for total in sums]
    for micro in range(micros):
        spread = jnp.zeros(sums[micro].shape, F32)
        for row in range(first_row, first_row + rows):
            away = ref[micro, row] - means[micro]
            spread = spread + fold(away * away)
        squares.append(spread)
    if channels == LANES:
        send_all(send, [row_of(part) for part in sums + squares])
    else:
        send_all(send, [row_of(*sums), row_of(*squares)])


def conv_pair(source, weight, micro, at, channels):
    window = source[micro, at : at + 4].reshape(12 * channels, source.shape[3])
    return dot(weight[...], window)


def conv_rows(source, weight, out, shape):
    micros, high, channels, width = shape
    for micro in range(micros):
        for at in range(0, high, 2):
            both = conv_pair(source, weight, micro, at, channels)
            out[micro, at] = both[:channels].astype(out.dtype)
            out[micro, at + 1] = both[channels:].astype(out.dtype)


def canvas_kernel(found, columns, where_rows, l_first, out, kept, send, canvas, *, rows):
    scenes, high, channels, width = out.shape
    masks = edges(channels, width)
    slots = found.shape[0]
    lane = lax.broadcasted_iota(jnp.int32, (slots, width), 1).astype(F32)
    for group in range(3):
        values = jnp.transpose(found[:, group * LANES : (group + 1) * LANES].astype(F32))
        first, count = ((rows - 2, 2), (0, rows), (0, 2))[group]
        for scene in range(scenes):
            at = 2 * group + scene
            column = columns[:, at : at + 1] - 1.0
            column = column - jnp.floor(column * (1.0 / width)) * width
            row = jnp.floor((where_rows[at : at + 1] - 1.0) * (1.0 / width))
            mine = values[scene * channels : (scene + 1) * channels]
            placed = jnp.concatenate(
                [jnp.where(row == r * 1.0, mine, 0.0) for r in range(first, first + count)], axis=0
            ).astype(BF16)
            chosen = jnp.where(lane == column, 1.0, 0.0).astype(BF16)
            grid = dot(placed, chosen).astype(BF16)
            start = (0, 2, rows + 2)[group]
            for r in range(count):
                row = grid[r * channels : (r + 1) * channels]
                canvas[scene, start + r] = spread(row, masks)
                if 1 <= start + r <= rows + 2:
                    kept[scene, start + r - 1] = row
    conv_rows(canvas, l_first, out, out.shape)
    own_stats(out, 1, rows, send)


def second_kernel(found, cols, first_out, l_second_in, out, kept, slopes, stats, send, acts, l_second, sems,
                  *, rows, tiles):
    weight_copy = move(l_second_in, l_second, sems, 0)
    micros, high, channels, width = first_out.shape
    tile = lax.axis_index("tile")
    turned = stat_columns(found, float(rows * width))
    stats[...] = turned
    masks = edges(channels, width)
    for micro in range(micros):
        part = slice(micro * channels, (micro + 1) * channels)
        centre = turned[part, 0:1]
        scale = turned[part, 1:2] * cols[0:channels, 2:3]
        shift = cols[0:channels, 3:4]

        for row in range(high):
            normed = (first_out[micro, row] - centre) * scale + shift
            gate = sigmoid(normed)
            act = normed * gate
            slopes[micro, row] = gate + act * (1.0 - gate)
            if row == 0 or row == high - 1:
                act = act * inside(tile, row - 1, (tiles, rows))
            act = act.astype(BF16)
            acts[micro, row] = spread(act, masks)
            kept[micro, row] = act
    weight_copy.wait()
    conv_rows(acts, l_second, out, out.shape)
    own_stats(out, 0, rows, send)


def up_kernel(found, cols, second_out, w_up, acts, upper, slopes, plain, crossed, stats, send, *, rows):
    micros, _, channels, width = second_out.shape
    peers = send.shape[0]
    each = crossed.shape[0] // peers
    turned = stat_columns(found, float(rows * width))
    stats[...] = turned
    gain, shift = cols[0:channels, 4:5], cols[0:channels, 5:6]
    lines = []
    for micro in range(micros):
        part = slice(micro * channels, (micro + 1) * channels)
        centre, rstd = turned[part, 0:1], turned[part, 1:2]
        slope_sum = jnp.zeros((channels, LANES), F32)
        unit_sum = jnp.zeros((channels, LANES), F32)
        for row in range(rows):
            unit = (second_out[micro, row] - centre) * rstd
            normed = unit * gain + shift
            gate = sigmoid(normed)
            act = normed * gate
            slope = gate + act * (1.0 - gate)
            sloped = slope * unit
            slope_sum = slope_sum + fold(slope)
            unit_sum = unit_sum + fold(sloped)
            slopes[micro, row] = jnp.concatenate([slope, sloped], axis=0)
            act = act.astype(BF16)
            acts[micro, row] = act
            upper[micro, row] = dot(w_up[...], act)
        lines.append(row_of(slope_sum, unit_sum).astype(BF16).astype(F32))
        crossed[micro * channels : (micro + 1) * channels] = dot_lanes(
            jnp.concatenate([acts[micro, row] for row in range(rows)], axis=1),
            jnp.concatenate([slopes[micro, row].astype(BF16) for row in range(rows)], axis=1),
        )
    plain[...] = jnp.concatenate(lines, axis=0)
    used = micros * channels
    if crossed.shape[0] > used:
        crossed[used:] = jnp.zeros((crossed.shape[0] - used, LANES), F32)
    if 2 * micros + each < send.shape[1]:
        send[...] = jnp.zeros(send.shape, F32)
    for peer in range(peers):
        send[peer, 2 * micros : 2 * micros + each] = crossed[peer * each : (peer + 1) * each]
    own_stats(upper, 0, rows, send)


def exact_rows(rows):
    high = rows.astype(BF16).astype(F32)
    return [high, rows - high]


def top_kernel(found, cols, upper, cot, slopes, plain, w_up_t, features, grads, mixed, stats, send, *, rows, each):
    micros, _, wide, width = upper.shape
    channels = w_up_t.shape[0]
    lines = []
    for micro in range(micros):
        lines += list(pooled_stats(found[:, micro, :], found[:, micros + micro, :], float(rows * width)))
    turned = columns_of(lines)
    stats[...] = turned
    gain, shift = cols[:, 6:7], cols[:, 7:8]
    gain_rows, shift_rows, mixed_rows = [], [], []
    for micro in range(micros):
        centre, rstd = turned[:, 2 * micro : 2 * micro + 1], turned[:, 2 * micro + 1 : 2 * micro + 2]
        factor = gain * rstd
        gain_sum = jnp.zeros((wide, LANES), F32)
        shift_sum = jnp.zeros((wide, LANES), F32)
        mixed_sum = jnp.zeros((2 * channels, LANES), F32)
        for row in range(rows):
            unit = (upper[micro, row] - centre) * rstd
            normed = unit * gain + shift
            gate = sigmoid(normed)
            act = normed * gate
            grad = cot[micro, row].astype(F32) * (gate + act * (1.0 - gate))
            features[micro, row] = act.astype(BF16)
            grads[micro, row] = grad
            gain_sum = gain_sum + fold(grad * unit)
            shift_sum = shift_sum + fold(grad)
            below = dot(w_up_t[...], (grad * factor).astype(BF16))
            mixed_sum = mixed_sum + fold(
                slopes[micro, row] * jnp.concatenate([below, below], axis=0)
            )
        gain_rows.append(row_of(gain_sum))
        shift_rows.append(row_of(shift_sum))
        mixed_rows.append(row_of(mixed_sum).astype(BF16).astype(F32))
    mixed[...] = jnp.concatenate(mixed_rows, axis=0)
    rows_out = jnp.concatenate(gain_rows + shift_rows, axis=0)
    crossed = jnp.sum(found[:, 2 * micros : 2 * micros + each, :], axis=0)
    rest = send.shape[1] - 6 * micros - each
    block = exact_rows(rows_out) + mixed_rows + [plain[...], crossed]
    if rest > 0:
        block.append(jnp.zeros((rest, LANES), F32))
    block = jnp.concatenate(block, axis=0)
    send[...] = jnp.broadcast_to(block.astype(BF16)[None], send.shape)


def low_rows(turned, value_of, values, stats, gain, low, high, first, rows, tiles):
    micros, _, channels, width = values.shape
    tile = lax.axis_index("tile")
    masks = edges(channels, width)
    for micro in range(micros):
        part = slice(micro * channels, (micro + 1) * channels)
        centre, rstd = stats[part, 0:1], stats[part, 1:2]
        factor = gain * rstd
        slope_part, shift_part = rstd * turned[part, 0:1], turned[part, 1:2]
        for index in range(high):
            grad, value = value_of(micro, index)
            grad = factor * (grad - shift_part - (value - centre) * slope_part)
            if index + first < 0 or index + first >= rows:
                grad = grad * inside(tile, index + first, (tiles, rows))
            low[micro, index] = spread(grad.astype(BF16), masks)


def first_units(first_out, stats, micro, channels):
    part = slice(micro * channels, (micro + 1) * channels)
    centre, rstd = stats[part, 0:1], stats[part, 1:2]
    return lambda row: (first_out[micro, row] - centre) * rstd


def second_sums(total, weight, factors, stats, micro, micros, count):
    channels = weight.shape[1]
    factor, centre = factors[micro], stats[:, 2 * micro : 2 * micro + 1]
    columns = jnp.transpose(jnp.concatenate([total, jnp.zeros((8 - total.shape[0], LANES), F32)], axis=0))
    beta = factor * stats[:, 2 * micro + 1 : 2 * micro + 2] * columns[:, micro : micro + 1] * (1.0 / count)
    alpha = factor * columns[:, micros + micro : micros + micro + 1] * (1.0 / count)
    square = lax.dot_general(
        weight * beta, weight, (((0,), (0,)), ((), ())),
        preferred_element_type=F32, precision=lax.Precision.HIGHEST,
    )
    square = jnp.concatenate([square, square], axis=1)
    line = jnp.sum(weight * (alpha - beta * centre), axis=0, keepdims=True)
    line = jnp.concatenate([line, line], axis=1)

    def give(mixed, plain, crossed):
        mine = crossed[micro * channels : (micro + 1) * channels]
        return mixed - plain * line - jnp.sum(square * mine, axis=0, keepdims=True)

    return give


def middle_back_kernel(
    found, cols, grads, upper, top_stats, second_out, second_stats, slopes, w_up, w_up_t,
    own_mixed, own_plain, own_crossed,
    low, top_low, rising, falling, top_gain_grad, top_shift_grad, expected, extras, second_dz, *, rows, each
):
    scene = lax.axis_index("scene")
    micros, _, wide, width = grads.shape
    channels = second_out.shape[2]
    peers = found.shape[0]
    count = float(peers * rows * width)
    kept = 2 * micros
    total = jnp.sum(found[...].astype(F32), axis=0)
    mixed, plain = total[2 * kept : 2 * kept + micros], total[2 * kept + micros : 3 * kept]
    total = total[0:kept] + total[kept : 2 * kept]
    crossed = jnp.concatenate(
        [
            found[peer].astype(F32)[3 * kept : 3 * kept + each]
            for peer in range(-(-micros * channels // each))
        ],
        axis=0,
    )
    own_half(total[0:1] + total[1:2], scene, top_gain_grad)
    own_half(total[2:3] + total[3:4], scene, top_shift_grad)
    factors = [cols[:, 6:7] * top_stats[:, 2 * micro + 1 : 2 * micro + 2] for micro in range(micros)]
    wide_weight = w_up[...].astype(F32)
    turned = columns_of([total[index : index + 1] for index in range(2 * micros)]) * (1.0 / count)
    gain = cols[0:channels, 4:5]
    masks = edges(channels, width)
    second_rows = []
    for micro in range(micros):
        top_centre = top_stats[:, 2 * micro : 2 * micro + 1]
        top_slope = top_stats[:, 2 * micro + 1 : 2 * micro + 2] * turned[:, micro : micro + 1]
        top_shift = turned[:, micros + micro : micros + micro + 1]
        part = slice(micro * channels, (micro + 1) * channels)
        centre, rstd = second_stats[part, 0:1], second_stats[part, 1:2]
        gain_sum = jnp.zeros((channels, LANES), F32)
        shift_sum = jnp.zeros((channels, LANES), F32)
        for row in range(rows):
            grad = factors[micro] * (
                grads[micro, row] - top_shift - (upper[micro, row] - top_centre) * top_slope
            )
            grad = grad.astype(BF16)
            top_low[micro, row] = grad
            unit = (second_out[micro, row] - centre) * rstd
            grad = dot(w_up_t[...], grad) * slopes[micro, row, 0:channels]
            second_dz[micro, row] = grad
            shift_sum = shift_sum + fold(grad)
            gain_sum = gain_sum + fold(grad * unit)
        second_rows.append((shift_sum, gain_sum))
    parts = []
    for micro in range(micros):
        give = second_sums(total, wide_weight, factors, top_stats, micro, micros, count)
        whole = give(mixed[micro : micro + 1], plain[micro : micro + 1], crossed)
        extra = row_of(*second_rows[micro]) - give(
            own_mixed[micro : micro + 1], own_plain[micro : micro + 1], own_crossed[...]
        )
        expected[micro : micro + 1] = whole
        extras[micro : micro + 1] = extra
        parts.append(whole * (1.0 / count) + extra * (1.0 / (rows * width)))
    parts = columns_of(parts)
    for micro in range(micros):
        part = slice(micro * channels, (micro + 1) * channels)
        centre, rstd = second_stats[part, 0:1], second_stats[part, 1:2]
        factor = gain * rstd
        shift_part = parts[0:channels, micro : micro + 1]
        slope_part = parts[channels : 2 * channels, micro : micro + 1] * rstd
        for row in range(rows):
            grad = factor * (
                second_dz[micro, row] - shift_part - (second_out[micro, row] - centre) * slope_part
            )
            low[micro, row] = spread(grad.astype(BF16), masks)
    for micro in range(micros):
        for row in range(2):
            falling[micro, row] = low[micro, row, channels : 2 * channels]
            rising[micro, row] = low[micro, rows - 2 + row, channels : 2 * channels]


def first_back_kernel(
    low, top_low, second_act, acts, first_out, first_stats, slopes, b_second_in, extras,
    out, top_grad, weight_grad, send, b_second, sems, *, rows, tiles
):
    weight_copy = move(b_second_in, b_second, sems, 0)
    tile = lax.axis_index("tile")
    micros, _, channels, width = first_out.shape
    weight_copy.wait()
    half = 6 * channels
    gain_sums, shift_sums = [], []
    for micro in range(micros):
        units = first_units(first_out, first_stats, micro, channels)
        gain_sum = jnp.zeros((channels, LANES), F32)
        shift_sum = jnp.zeros((channels, LANES), F32)
        for at in range(0, rows + 2, 2):
            if at == 0:
                parts = dot(b_second[:, half:], low[micro, 0:2].reshape(half, width))
            elif at == rows:
                parts = dot(b_second[:, :half], low[micro, rows - 2 : rows].reshape(half, width))
            else:
                parts = conv_pair(low, b_second, micro, at - 2, channels)
            for j in range(2):
                grad = parts[channels * j : channels * (j + 1)] * slopes[micro, at + j]
                if at + j == 0 or at + j == rows + 1:
                    grad = grad * inside(tile, at + j - 1, (tiles, rows))
                out[micro, at + j] = grad
                gain_sum = gain_sum + fold(grad * units(at + j))
                shift_sum = shift_sum + fold(grad)
        gain_sums.append(gain_sum)
        shift_sums.append(shift_sum)
        product = dot_lanes(
            jnp.concatenate([top_low[micro, row] for row in range(rows)], axis=1),
            jnp.concatenate([second_act[micro, row] for row in range(rows)], axis=1),
        )
        top_grad[...] = product if micro == 0 else top_grad[...] + product
    conv_grad(low, 0, acts, 0, weight_grad, rows)
    send_all(send, [row_of(*gain_sums), row_of(*shift_sums)] + [extras[m : m + 1] for m in range(micros)])


def conv_grad(low, low_first, values, value_first, total, rows):
    micros, _, channels, width = values.shape
    for micro in range(micros):
        grads = jnp.concatenate([low[micro, row + low_first] for row in range(rows)], axis=1)
        windows = jnp.concatenate(
            [
                values[micro, row + value_first : row + value_first + 3].reshape(3 * channels, width)
                for row in range(rows)
            ],
            axis=1,
        )
        product = dot_lanes(grads, windows)
        total[...] = product if micro == 0 else total[...] + product


def half_rows(total, half, scene):
    channels = 2 * half
    start = scene * half
    mine = jnp.concatenate(
        [total[b * channels + start : b * channels + start + half, :] for b in range(2, -1, -1)], axis=0
    )
    wing = mine[:, LANES:]
    cut = wing.shape[0] // 2
    return [mine[:, :LANES], jnp.concatenate([wing[:cut], wing[cut:]], axis=1)]


def pick_kernel(
    found, cols, grads, before, after, first_out, first_stats, slopes, b_first_in, b_second_in, columns, where_rows,
    canvas, second_grad, top_grad, expected,
    send, gain_grad, shift_grad, second_gain_grad, second_shift_grad, low, grid, b_first, b_second, halo, first_grad, whole, sems,
    *, rows, tiles, each
):
    second_copy = move(b_second_in, b_second, sems, 1)
    weight_copy = move(b_first_in, b_first, sems, 0)
    scene = lax.axis_index("scene")
    micros, _, channels, width = grads.shape
    sums = sum_rows(found, 2 + micros)
    second = sum(sums[2:]) + jnp.sum(expected[...], axis=0, keepdims=True)
    own_half(second[:, :channels], scene, second_shift_grad)
    own_half(second[:, channels:], scene, second_gain_grad)
    sums = sums[:2]
    own_half(sums[0][:, :channels] + sums[0][:, channels:], scene, gain_grad)
    own_half(sums[1][:, :channels] + sums[1][:, channels:], scene, shift_grad)
    turned = columns_of(sums) * (1.0 / (found.shape[0] * rows * width))
    masks = edges(channels, width)
    half = 6 * channels
    second_copy.wait()
    for micro in range(micros):
        for at, ref, columns_used in ((0, before, slice(0, half)), (rows, after, slice(half, 2 * half))):
            window = jnp.concatenate([spread(ref[micro, row], masks) for row in range(2)], axis=0)
            parts = dot(b_second[:, columns_used], window)
            for j in range(2):
                halo[micro, at + j] = parts[channels * j : channels * (j + 1)] * slopes[micro, at + j]

    def value_of(micro, index):
        grad = grads[micro, index]
        if index < 2 or index >= rows:
            grad = grad + halo[micro, index]
        return grad, first_out[micro, index]

    low_rows(turned, value_of, first_out, first_stats, cols[0:channels, 2:3], low, rows + 2, -1, rows, tiles)
    weight_copy.wait()
    conv_rows(low, b_first, grid, grid.shape)
    conv_grad(low, 1, canvas, 0, first_grad, rows)
    half = channels // 2
    peers, block = send.shape[:2]
    for s in range(2):
        parts = half_rows(first_grad, half, s) + half_rows(second_grad, half, s)
        mine = top_grad[s * channels : (s + 1) * channels, :]
        parts.append(jnp.concatenate([mine[:half], mine[half:]], axis=1))
        parts = jnp.concatenate(parts, axis=0)
        whole[s, 0 : parts.shape[0]] = parts
        if whole.shape[1] > parts.shape[0]:
            whole[s, parts.shape[0] :] = jnp.zeros((whole.shape[1] - parts.shape[0], LANES), F32)
    slots = columns.shape[0]
    lane = lax.broadcasted_iota(jnp.int32, (slots, width), 1).astype(F32)
    picked = []
    for micro in range(micros):
        at = 2 + micro
        column = columns[:, at : at + 1] - 1.0
        column = column - jnp.floor(column * (1.0 / width)) * width
        place = jnp.floor((where_rows[at : at + 1] - 1.0) * (1.0 / width))
        chosen = jnp.where(lane == column, 1.0, 0.0).astype(BF16)
        here = dot_lanes(grid[micro].reshape(rows * channels, width), chosen)
        total = jnp.zeros((channels, slots), F32)
        for r in range(rows):
            total = total + jnp.where(place == r * 1.0, here[r * channels : (r + 1) * channels], 0.0)
        picked.append(total)
    picked = jnp.transpose(jnp.concatenate(picked, axis=0))
    capacity = slots // tiles
    rest = block - capacity - 2 * each
    for peer in range(peers):
        spot = peer // 2
        parts = [picked[spot * capacity : (spot + 1) * capacity]]
        parts += [whole[s, peer * each : (peer + 1) * each] for s in range(2)]
        parts.append(jnp.zeros((rest, LANES), F32))
        send[peer] = jnp.concatenate(parts, axis=0).astype(BF16)


def pillar_back_kernel(found, rows_in, w_pillar, cols, pooled, send, grads, lifted, rows, sems,
                       *, capacity, each):
    fetched = move(rows_in, rows, sems, 0)
    micros = rows.shape[0]
    _, channels, pillars = pooled.shape
    stats = pooled.at[micros : 2 * micros]
    inputs = w_pillar.shape[1]
    depth = rows.shape[2] // pillars
    scene = lax.axis_index("scene")
    peers = found.shape[0]
    slot_count = peers // 2 * capacity
    returned = jnp.concatenate(
        [found[2 * t + scene].astype(F32)[0:capacity] for t in range(peers // 2)], axis=0
    )
    turned = jnp.transpose(returned)
    place = lax.broadcasted_iota(jnp.int32, (slot_count, pillars), 0).astype(F32)
    gain, shift = cols[0:channels, 0:1], cols[0:channels, 1:2]
    gain_sums, shift_sums = [], []
    outer = jnp.zeros((16, channels), F32)
    fetched.wait()
    for micro in range(micros):
        lifted[...] = dot(w_pillar[...], rows[micro, 0:inputs])
        slot, limit = pillar_notes(rows, micro, inputs, pillars)
        chosen = jnp.where(place == slot, 1.0, 0.0).astype(BF16)
        back = dot(turned[micro * channels : (micro + 1) * channels].astype(BF16), chosen)
        centre, rstd = stats[micro, :, 0:1], stats[micro, :, 1:2]
        pool = pooled[micro]
        gain_sum = jnp.zeros((channels, pillars), F32)
        shift_sum = jnp.zeros((channels, pillars), F32)
        for n in range(depth):
            piece = slice(n * pillars, (n + 1) * pillars)
            unit = (lifted[:, piece] - centre) * rstd
            normed = unit * gain + shift
            gate = sigmoid(normed)
            act = normed * gate
            slope = gate + act * (1.0 - gate)
            grad = jnp.where(limit > n, back * jnp.exp(act - pool) * slope, 0.0)
            grads[micro, :, piece] = grad
            gain_sum = gain_sum + grad * unit
            shift_sum = shift_sum + grad
        gain_sums.append(gain_sum)
        shift_sums.append(shift_sum)
        scale = jnp.transpose(jnp.broadcast_to(rstd * gain, (channels, LANES)))[0:1]
        outer = outer + dot_lanes(rows[micro], grads[micro].astype(BF16)) * scale
    lines = [row_of(*gain_sums), row_of(*shift_sums)]
    for k in range(0, 10, 2):
        lines.append(jnp.concatenate([outer[k : k + 1], outer[k + 1 : k + 2]], axis=1))
    exact = jnp.concatenate(lines, axis=0)
    kept = 2 * exact.shape[0]
    weights = jnp.sum(found[...].astype(F32), axis=0)
    rest = send.shape[2] - kept - each
    for s in range(2):
        mine = weights[capacity + s * each : capacity + (s + 1) * each]
        block = exact_rows(exact) + [mine] + ([jnp.zeros((rest, LANES), F32)] if rest > 0 else [])
        block = jnp.concatenate(block, axis=0).astype(BF16)
        send[:, s] = jnp.broadcast_to(block[None], (send.shape[0],) + block.shape)


def points_kernel(
    found, rows_in, grads, w_pillar, cols, pooled,
    points_grad, pillar_grad, gain_grad, shift_grad, first_grad, second_grad, up_grad, rows, lifted, sems,
    *, each
):
    fetched = move(rows_in, rows, sems, 0)
    scene = lax.axis_index("scene")
    micros, channels, _ = grads.shape
    stats = pooled.at[micros : 2 * micros]
    _, _, inputs, depth, pillars = points_grad.shape
    half = channels // 2
    kept = 7
    total = jnp.sum(found[...].astype(F32), axis=0)
    total = total[0:kept] + total[kept : 2 * kept]
    own_half(total[0:1, :channels] + total[0:1, channels:], scene, gain_grad)
    own_half(total[1:2, :channels] + total[1:2, channels:], scene, shift_grad)
    turned = jnp.transpose(jnp.concatenate([total, jnp.zeros((1, LANES), F32)], axis=0))
    weight_grad = jnp.concatenate(
        [turned[(k % 2) * channels : (k % 2 + 1) * channels, 2 + k // 2 : 3 + k // 2] for k in range(inputs)],
        axis=1,
    )
    weight = jnp.transpose(w_pillar[...].astype(F32)).astype(BF16)
    fetched.wait()
    for micro in range(micros):
        lifted[...] = dot(w_pillar[...], rows[micro, 0:inputs])
        part = slice(micro * channels, (micro + 1) * channels)
        centre, rstd, inverse = stats[micro, :, 0:1], stats[micro, :, 1:2], stats[micro, :, 2:3]
        factor = cols[0:channels, 0:1] * rstd
        gain_part, shift_part = turned[part, 0:1], turned[part, 1:2]
        spun, mean = stats[micro, :, 16 : 16 + inputs], stats[micro, :, 32 : 32 + inputs]
        weight_grad = weight_grad - factor * (shift_part * mean + gain_part * rstd * spun)
        gain_part, shift_part = gain_part * inverse * rstd, shift_part * inverse
        _, limit = pillar_notes(rows, micro, inputs, pillars)
        for n in range(depth):
            piece = slice(n * pillars, (n + 1) * pillars)
            low = factor * (grads[micro, :, piece] - shift_part - (lifted[:, piece] - centre) * gain_part)
            low = jnp.where(limit > n, low, 0.0).astype(BF16)
            points_grad[micro, 0, :, n, :] = dot(weight, low)
    weight_grad = jnp.concatenate([weight_grad, jnp.zeros((channels, LANES - inputs), F32)], axis=1)
    weight_grad = jnp.transpose(weight_grad)[0:inputs]
    pillar_grad[...] = jnp.where(scene == 0, weight_grad[:, :half], weight_grad[:, half:])
    whole = jnp.concatenate(
        [found[peer].astype(F32)[2 * kept : 2 * kept + each] for peer in range(found.shape[0])], axis=0
    )
    for index, out in enumerate((first_grad, second_grad)):
        base = index * 9 * half * channels // LANES
        lead = 3 * half
        mine = whole[base : base + lead]
        wing = whole[base + lead : base + lead + lead // 2]
        wing = jnp.concatenate([wing[:, :channels], wing[:, channels:]], axis=0)
        both = jnp.concatenate([mine, wing], axis=1)
        for a in range(3):
            for b in range(3):
                at = (3 * a + b) * channels
                out[:, at : at + channels] = both[b * half : (b + 1) * half, a * channels : (a + 1) * channels]
    base = 2 * 9 * half * channels // LANES
    top = whole[base : base + half]
    up_grad[...] = jnp.concatenate([top[:, :channels], top[:, channels:]], axis=0)


def swap(blocks, axes):
    return lax.all_to_all(blocks, axes, split_axis=0, concat_axis=0)


def shards(
    points, point_counts, pillar_tile, pillar_cell,
    pillar_weight, pillar_gain, pillar_shift,
    first_weight, first_gain, first_shift,
    second_weight, second_gain, second_shift,
    up_weight, up_gain, up_shift, cotangent,
):
    micros, _, inputs, depth, pillars = points.shape
    channels = up_weight.shape[1]
    upper = cotangent.shape[2]
    rows, width = cotangent.shape[3:]
    tiles = lax.axis_size("tile")
    scenes = lax.axis_size("scene")
    peers = tiles * scenes
    capacity = 2 * pillars // tiles
    slot_count = tiles * capacity
    half = channels // 2

    def vmem(shape, dtype):
        return pltpu.VMEM(shape, dtype)

    def grid(high, dtype=F32, lead=channels):
        return ((micros, high, lead, width), dtype)

    sums = ((peers, 2, LANES), F32)
    sources = (
        pillar_tile, pillar_cell, point_counts, points,
        first_weight, second_weight, up_weight, pillar_weight.T,
        pillar_gain, pillar_shift, first_gain, first_shift, second_gain, second_shift, up_gain, up_shift,
    )
    moments, packed, point_rows = run(
        functools.partial(moments_kernel, capacity=capacity),
        [
            ((tiles, scenes, 8, LANES), F32), ((layout(half, channels)[-1] + 16, LANES), BF16),
            ((micros, 16, depth * pillars), BF16),
        ],
        *sources,
        hbm=range(len(sources)), copies=len(sources), limit=WIDE_LIMIT,
        scratch=[vmem(source.shape, source.dtype) for source in sources]
        + [vmem((inputs * depth, pillars), F32)],
    )
    moments = swap(moments.reshape(peers, 8, LANES), BOTH)

    send, pooled = run(
        functools.partial(pillar_kernel, capacity=capacity, inputs=inputs),
        [((slot_count, 3 * LANES), BF16), ((2 * micros, channels, pillars), F32)],
        moments, point_rows,
        scratch=[vmem((channels, depth * pillars), F32), vmem((channels, depth * pillars), F32)],
    )
    send, packed, cotangent = lax.optimization_barrier((send, packed, cotangent))
    cot = cotangent[:, 0].transpose(0, 2, 1, 3)
    both = lax.all_gather(packed, "scene")
    taps = ((2 * channels, 12 * channels), BF16)
    w_pillar, cols, l_first, l_second, b_first, b_second, w_up, w_up_t = run(
        functools.partial(unpack_kernel, inputs=inputs),
        [
            ((channels, inputs), BF16), ((LANES, 8), F32), taps, taps + (1,), taps + (1,), taps + (1,),
            ((upper, channels), BF16), ((channels, upper), BF16),
        ],
        both,
        scratch=[vmem(*taps), vmem(*taps), vmem(*taps)], copies=3,
    )
    arrived = swap(send.reshape(tiles, capacity, 3 * LANES), "tile").reshape(slot_count, 3 * LANES)
    cell_columns, cell_rows = run(
        functools.partial(cells_kernel, capacity=capacity),
        [((slot_count, LANES), F32), ((8, slot_count), F32)],
        moments,
        cost=pl.CostEstimate(flops=10**7, bytes_accessed=10**6, transcendentals=0),
    )
    arrived, cot, l_first = lax.optimization_barrier((arrived, cot, l_first))

    first_out, canvas, send = run(
        functools.partial(canvas_kernel, rows=rows),
        [grid(rows + 2), grid(rows + 2, BF16), sums],
        arrived, cell_columns, cell_rows, l_first,
        scratch=[vmem(*grid(rows + 4, BF16, 3 * channels))],
    )
    second_out, first_act, first_slopes, first_stats, send = run(
        functools.partial(second_kernel, rows=rows, tiles=tiles),
        [grid(rows), grid(rows + 2, BF16), grid(rows + 2), ((LANES, 8), F32), sums],
        swap(send, BOTH), cols, first_out, l_second,
        hbm=(3,), scratch=[vmem(*grid(rows + 2, BF16, 3 * channels)), vmem(*taps)], copies=1,
    )
    part = -(-micros * channels // peers)
    second_act, up_out, slopes, plain, crossed, second_stats, send = run(
        functools.partial(up_kernel, rows=rows),
        [
            grid(rows, BF16), grid(rows, F32, upper), grid(rows, F32, 2 * channels), ((micros, LANES), F32),
            ((peers * part, LANES), F32), ((LANES, 8), F32), ((peers, -(-(2 * micros + part) // 8) * 8, LANES), F32),
        ],
        swap(send, BOTH), cols, second_out, w_up,
    )
    features, grads, mixed, top_stats, send = run(
        functools.partial(top_kernel, rows=rows, each=part),
        [
            grid(rows, BF16, upper), grid(rows, F32, upper), ((micros, LANES), F32), ((LANES, 8), F32),
            ((peers, -(-(6 * micros + part) // 8) * 8, LANES), BF16),
        ],
        swap(send, BOTH), cols, up_out, cot, slopes, plain, w_up_t,
    )
    features = with_layout_constraint(features.transpose(0, 2, 1, 3)[:, None], Layout((0, 1, 2, 3, 4)))
    features, send = lax.optimization_barrier((features, send))
    edge = ((micros, 2, channels, width), BF16)
    vector, top_vector, matrix = ((half,), F32), ((upper // 2,), F32), ((half, 9 * channels), F32)
    rising = [(i, i + 1) for i in range(tiles - 1)]
    falling = [(j, i) for i, j in rising]
    cross = ((3 * channels, 3 * channels), F32)
    low, top_low, rising_edge, falling_edge, up_gain_grad, up_shift_grad, expected, extras = run(
        functools.partial(middle_back_kernel, rows=rows, each=part),
        [
            grid(rows, BF16, 3 * channels), grid(rows, BF16, upper), edge, edge, top_vector, top_vector,
            ((micros, LANES), F32), ((micros, LANES), F32),
        ],
        swap(send, BOTH), cols, grads, up_out, top_stats, second_out, second_stats, slopes, w_up, w_up_t,
        mixed, plain, crossed,
        scratch=[vmem(*grid(rows))],
    )
    before = lax.ppermute(rising_edge, "tile", rising)
    after = lax.ppermute(falling_edge, "tile", falling)
    first_dz, top_grad, second_cross, send = run(
        functools.partial(first_back_kernel, rows=rows, tiles=tiles),
        [grid(rows + 2), ((upper, channels), F32), cross, ((peers, 2 + micros, LANES), F32)],
        low, top_low, second_act, first_act, first_out, first_stats, first_slopes, b_second, extras,
        hbm=(7,), scratch=[vmem(*taps)], copies=1,
        cost=pl.CostEstimate(flops=2 * 10**9, bytes_accessed=10**7, transcendentals=0),
    )
    length = (2 * 9 * half * channels + upper * half) // LANES
    each = -(-length // peers)
    block = -(-(capacity + 2 * each) // 8) * 8
    send, first_gain_grad, first_shift_grad, second_gain_grad, second_shift_grad = run(
        functools.partial(pick_kernel, rows=rows, tiles=tiles, each=each),
        [((peers, block, LANES), BF16), vector, vector, vector, vector],
        swap(send, BOTH), cols, first_dz,
        before, after, first_out, first_stats, first_slopes, b_first, b_second, cell_columns, cell_rows, canvas, second_cross, top_grad, expected,
        hbm=(8, 9),
        scratch=[
            vmem(*grid(rows + 2, BF16, 3 * channels)), vmem(*grid(rows, BF16)), vmem(*taps), vmem(*taps),
            vmem(*grid(rows + 2)), vmem(*cross), vmem((scenes, peers * each, LANES), F32),
        ],
        copies=2,
    )
    block = -(-(14 + each) // 8) * 8
    send, pillar_dz = run(
        functools.partial(pillar_back_kernel, capacity=capacity, each=each),
        [((tiles, scenes, block, LANES), BF16), ((micros, channels, depth * pillars), F32)],
        swap(send, BOTH), point_rows, w_pillar, cols, pooled,
        hbm=(1,),
        scratch=[vmem((channels, depth * pillars), F32), vmem((micros, 16, depth * pillars), BF16)],
        copies=1,
    )
    points_grad, pillar_grad, pillar_gain_grad, pillar_shift_grad, first_grad, second_grad, up_grad = run(
        functools.partial(points_kernel, each=each),
        [
            ((micros, 1, inputs, depth, pillars), F32), ((inputs, half), F32), vector, vector,
            matrix, matrix, ((upper // 2, channels), F32),
        ],
        swap(send.reshape(peers, block, LANES), BOTH), point_rows, pillar_dz, w_pillar, cols, pooled,
        hbm=(1,),
        scratch=[vmem((micros, 16, depth * pillars), BF16), vmem((channels, depth * pillars), F32)],
        copies=1,
    )
    return (
        features, points_grad,
        pillar_grad.T, pillar_gain_grad, pillar_shift_grad,
        first_grad, first_gain_grad, first_shift_grad,
        second_grad, second_gain_grad, second_shift_grad,
        up_grad, up_gain_grad, up_shift_grad,
    )


def solution(mesh):
    matrix, vector = P("scene", None), P("scene")
    grid = P(None, "scene", None, "tile", None)
    cloud = P(None, "scene", None, None, "tile")
    pillar = P(None, "scene", "tile")
    weights = (matrix, vector, vector) * 4
    return jax.shard_map(
        shards,
        mesh=mesh,
        in_specs=(cloud, pillar, pillar, pillar) + weights + (grid,),
        out_specs=(grid, cloud) + weights,
        check_vma=False,
    )
```

```python
import functools

import jax
import jax.numpy as jnp
from jax import lax
from jax.experimental import pallas as pl
from jax.experimental.layout import Layout, with_layout_constraint
from jax.experimental.pallas import tpu as pltpu
from jax.sharding import PartitionSpec as P

norm_eps = 0.001
BOTH = ("tile", "scene")
F32 = jnp.float32
BF16 = jnp.bfloat16
VMEM_LIMIT = 24 * 1024 * 1024
WIDE_LIMIT = 60 * 1024 * 1024
LANES = 128


def run(kernel, outs, *args, hbm=(), scratch=(), copies=0, cost=None, limit=VMEM_LIMIT):
    specs = [
        pl.BlockSpec(memory_space=pltpu.HBM if index in hbm else pltpu.VMEM) for index in range(len(args))
    ]
    scratch = list(scratch)
    if copies:
        scratch.append(pltpu.SemaphoreType.DMA((copies,)))
    return pl.pallas_call(
        kernel,
        out_shape=[jax.ShapeDtypeStruct(out[0], out[1]) for out in outs],
        in_specs=specs,
        out_specs=[
            pl.BlockSpec(memory_space=pltpu.HBM if len(out) > 2 else pltpu.VMEM) for out in outs
        ],
        scratch_shapes=scratch,
        compiler_params=pltpu.CompilerParams(vmem_limit_bytes=limit),
        cost_estimate=cost,
    )(*args)


def move(source, target, sems, index):
    copy = pltpu.make_async_copy(source, target, sems.at[index])
    copy.start()
    return copy


def dot(left, right, precision=None):
    return jnp.dot(left, right, preferred_element_type=F32, precision=precision)


def dot_lanes(left, right, precision=None):
    return lax.dot_general(
        left, right, (((1,), (1,)), ((), ())), preferred_element_type=F32, precision=precision
    )


def sigmoid(values):
    return 0.5 + 0.5 * jnp.tanh(0.5 * values)


def fold(values):
    total = values[:, :LANES]
    for start in range(LANES, values.shape[1], LANES):
        total = total + values[:, start : start + LANES]
    return total


def row_of(left, right=None):
    both = left if right is None else jnp.concatenate([left, right], axis=0)
    return jnp.sum(jnp.transpose(both), axis=0, keepdims=True)


def columns_of(rows):
    rows = rows + [jnp.zeros((8 - len(rows), LANES), F32)] if len(rows) < 8 else rows
    return jnp.transpose(jnp.concatenate(rows, axis=0))


def inside(tile, row, height):
    tiles, rows = height
    place = tile * rows + row
    return jnp.where((place >= 0) & (place < tiles * rows), 1.0, 0.0).astype(F32)


def send_all(ref, rows):
    for index, row in enumerate(rows):
        ref[:, index : index + 1, :] = jnp.broadcast_to(row[None], (ref.shape[0], 1, LANES))


def pooled_stats(means, squares, count):
    peers = means.shape[0]
    mean = jnp.sum(means, axis=0, keepdims=True) * (1.0 / peers)
    away = means - mean
    spread = jnp.sum(squares + count * away * away, axis=0, keepdims=True) * (1.0 / (peers * count))
    return mean, lax.rsqrt(spread + norm_eps)


def stat_columns(found, count):
    return columns_of(list(pooled_stats(found[:, 0, :], found[:, 1, :], count)))


def sum_rows(found, lines):
    return [jnp.sum(found[:, index, :], axis=0, keepdims=True) for index in range(lines)]


def own_half(row, scene, out):
    size = out.shape[0]
    out[...] = jnp.where(scene == 0, row[:, 0:size], row[:, size : 2 * size]).reshape(size)


def edges(channels, width):
    lane = lax.broadcasted_iota(jnp.int32, (channels, width), 1)
    return lane > 0, lane < width - 1


def spread(row, masks):
    zero = jnp.zeros_like(row)
    left = jnp.where(masks[0], pltpu.roll(row, 1, 1), zero)
    right = jnp.where(masks[1], pltpu.roll(row, row.shape[1] - 1, 1), zero)
    return jnp.concatenate([left, row, right], axis=0)


def layout(half, channels):
    first = 0
    second = first + half * -(-9 * channels // LANES)
    up = second + half * -(-9 * channels // LANES)
    vectors = up + channels
    return first, second, up, vectors, vectors + 16


def widen(value):
    missing = LANES - value.shape[1]
    if missing == 0:
        return value
    return jnp.concatenate([value, jnp.zeros((value.shape[0], missing), value.dtype)], axis=1)


def pack(held, out):
    first, second, up, pillar = held[:4]
    half, channels = first.shape[0], up.shape[1]
    starts = layout(half, channels)
    for ref, start in ((first, starts[0]), (second, starts[1])):
        for j in range(-(-9 * channels // LANES)):
            out[start + j * half : start + (j + 1) * half, :] = widen(
                ref[:, j * LANES : min((j + 1) * LANES, 9 * channels)]
            )
    out[starts[2] : starts[2] + channels, :] = widen(up[...])
    rows = [vector[...].astype(F32).reshape(1, -1) for vector in held[4:]]
    rows = [widen(row) for row in rows] + [jnp.zeros((16 - len(rows), LANES), F32)]
    turned = widen(pillar[...].astype(F32))
    rows += [turned, jnp.zeros((16 - turned.shape[0], LANES), F32)]
    out[starts[3] :, :] = jnp.concatenate(rows, axis=0).astype(BF16)


def unpack_kernel(
    both, w_pillar, cols, l_first, l_second, b_first, b_second, w_up, w_up_t,
    h_second, h_first_back, h_second_back, sems, *, inputs
):
    half = w_pillar.shape[0] // 2
    channels = 2 * half
    starts = layout(half, channels)
    tiles = -(-9 * channels // LANES)

    def wide(start):
        return jnp.concatenate(
            [
                jnp.concatenate(
                    [both[s, start + j * half : start + (j + 1) * half, :] for j in range(tiles)], axis=1
                )
                for s in range(2)
            ],
            axis=0,
        ).astype(F32)

    up = jnp.concatenate(
        [both[s, starts[2] : starts[2] + channels, 0:channels] for s in range(2)], axis=0
    )
    w_up[...] = up
    w_up_t[...] = jnp.transpose(up.astype(F32)).astype(BF16)
    turned = jnp.concatenate(
        [both[s, starts[4] : starts[4] + 16, 0:half].astype(F32) for s in range(2)], axis=1
    )
    w_pillar[...] = jnp.transpose(widen(turned))[0:channels, 0:inputs].astype(BF16)
    vectors = [both[s, starts[3] : starts[3] + 16, :].astype(F32) for s in range(2)]
    rows = []
    for index in range(8):
        size = half if index < 6 else channels
        row = jnp.concatenate([vectors[s][index : index + 1, 0:size] for s in range(2)], axis=1)
        rows.append(jnp.concatenate([row] * (LANES // (2 * size)), axis=1))
    cols[...] = columns_of(rows)
    zero = jnp.zeros((channels, 3 * channels), F32)
    copies = []
    for weight, ahead, back in (
        (wide(starts[0]), l_first, h_first_back), (wide(starts[1]), h_second, h_second_back)
    ):
        weight = weight[:, : 9 * channels]
        turned = jnp.transpose(weight)
        flipped = jnp.concatenate(
            [turned[tap * channels : (tap + 1) * channels] for tap in range(8, -1, -1)], axis=1
        )
        for ref, taps in ((ahead, weight), (back, flipped)):
            ref[0:channels, :] = jnp.concatenate([taps, zero], axis=1).astype(BF16)
            ref[channels : 2 * channels, :] = jnp.concatenate([zero, taps], axis=1).astype(BF16)
    copies.append(move(h_second, l_second, sems, 0))
    copies.append(move(h_first_back, b_first, sems, 1))
    copies.append(move(h_second_back, b_second, sems, 2))
    for copy in copies:
        copy.wait()


def slot_line(wide, depth, inputs):
    return jnp.concatenate([wide[pl.ds(n, inputs, stride=depth), :] for n in range(depth)], axis=1)


def slot_mask(count, depth):
    return jnp.concatenate([jnp.where(count > n, 1.0, 0.0) for n in range(depth)], axis=1)


def ranks(tile):
    pillars = tile.shape[1]
    across = jnp.broadcast_to(tile, (pillars, pillars))
    down = jnp.transpose(across)
    row = lax.broadcasted_iota(jnp.int32, (pillars, pillars), 0)
    col = lax.broadcasted_iota(jnp.int32, (pillars, pillars), 1)
    return jnp.sum(jnp.where((across == down) & (row < col), 1.0, 0.0), axis=0, keepdims=True)


def moments_kernel(*refs, capacity):
    number = 16
    sources, out, packed, lines_out = refs[:number], *refs[number : number + 3]
    held, wide, sems = refs[number + 3 : 2 * number + 3], refs[-2], refs[-1]
    copies = [move(sources[i], held[i], sems, i) for i in range(number)]
    tiles, cells, counts, points = held[:4]
    micros, _, inputs, depth, pillars = points.shape
    peers, scenes = out.shape[:2]
    copies[0].wait()
    copies[1].wait()
    lines, slot_rows = [], []
    for micro in range(micros):
        tile = tiles[micro].astype(F32)
        cell = (cells[micro] + 1).astype(F32)
        high = jnp.floor(cell * (1.0 / 16.0))
        low = cell - high * 16.0
        rank = ranks(tile)
        slot_rows.append(tile * capacity + rank)
        spot = lax.broadcasted_iota(jnp.int32, (capacity, pillars), 0).astype(F32)
        placed = jnp.where(spot == rank, 1.0, 0.0).astype(BF16)
        peer = lax.broadcasted_iota(jnp.int32, (peers, pillars), 0).astype(F32)
        for group in range(3):
            named = tile == peer + (group - 1.0)
            lines.append(
                16.0 * dot_lanes(jnp.where(named, high, 0.0).astype(BF16), placed)
                + dot_lanes(jnp.where(named, low, 0.0).astype(BF16), placed)
            )
    used = 3 * micros * capacity
    line = jnp.concatenate(lines + [jnp.zeros((peers, LANES - used), F32)], axis=1).reshape(peers, 1, LANES)
    for scene in range(scenes):
        out[:, scene, micros : micros + 1, :] = line
    copies[2].wait()
    copies[3].wait()
    parts, mean_rows, totals = [], [], []
    for micro in range(micros):
        wide[...] = points[micro, 0].astype(F32).reshape(inputs * depth, pillars)
        rows = slot_line(wide, depth, inputs)
        notes = jnp.concatenate([slot_rows[micro], counts[micro].astype(F32)], axis=0)
        notes = jnp.concatenate([notes, jnp.zeros((2, rows.shape[1] - pillars), F32)], axis=1)
        lines_out[micro] = jnp.concatenate(
            [rows, notes, jnp.zeros((14 - inputs, rows.shape[1]), F32)], axis=0
        ).astype(BF16)
        mask = slot_mask(counts[micro], depth)
        total = jnp.sum(mask, axis=1, keepdims=True)
        mean = jnp.sum(rows * mask, axis=1, keepdims=True) / total
        centred = jnp.concatenate(
            [(rows - mean) * mask, jnp.zeros((16 - inputs, rows.shape[1]), F32)], axis=0
        )
        high = centred.astype(BF16)
        parts += [high, (centred - high.astype(F32)).astype(BF16)]
        lane = lax.broadcasted_iota(jnp.int32, (inputs, inputs), 1)
        diagonal = lax.broadcasted_iota(jnp.int32, (inputs, inputs), 0) == lane
        mean_rows.append(jnp.sum(jnp.where(diagonal, mean, 0.0), axis=0, keepdims=True))
        totals.append(total)
    parts = jnp.concatenate(parts, axis=0)
    every = dot_lanes(parts, parts)
    for micro in range(micros):
        at = 32 * micro
        square = every[at : at + 32, at : at + 32]
        products = (
            square[0:inputs, 0:inputs] + square[16 : 16 + inputs, 0:inputs]
            + square[0:inputs, 16 : 16 + inputs] + square[16 : 16 + inputs, 16 : 16 + inputs]
        )
        row = jnp.concatenate(
            [products[k : k + 1] for k in range(inputs)]
            + [mean_rows[micro], totals[micro], jnp.zeros((1, LANES - inputs * inputs - inputs - 1), F32)],
            axis=1,
        )
        for scene in range(scenes):
            out[:, scene, micro : micro + 1, :] = jnp.broadcast_to(row[None], (peers, 1, LANES))
    for copy in copies[4:]:
        copy.wait()
    pack(held[4:], packed)


def cells_kernel(found, columns, rows, *, capacity):
    scene = lax.axis_index("scene")
    slots = columns.shape[0]
    peers = found.shape[0]
    values = found[:, 2, :]
    slot = lax.broadcasted_iota(jnp.int32, (slots, peers), 0)
    peer = lax.broadcasted_iota(jnp.int32, (slots, peers), 1)
    lane = lax.broadcasted_iota(jnp.int32, (slots, LANES), 1)
    row = lax.broadcasted_iota(jnp.int32, (slots, LANES), 0)
    result = jnp.zeros((slots, LANES), F32)
    chosen = jnp.where(peer == 2 * (slot // capacity) + scene, 1.0, 0.0)
    spread = dot(chosen, values, lax.Precision.HIGHEST)
    for micro in range(2):
        for group in range(3):
            mine = jnp.where(lane == (3 * micro + group) * capacity + row % capacity, spread, 0.0)
            column = jnp.sum(mine, axis=1, keepdims=True)
            result = jnp.where(lane == 2 * group + micro, column, result)
    columns[...] = result
    rows[...] = jnp.transpose(result)[0:8]


def pillar_notes(rows, micro, inputs, pillars):
    notes = rows[micro, :, 0:pillars].astype(F32)
    return notes[inputs : inputs + 1], notes[inputs + 1 : inputs + 2]


def pillar_kernel(
    found, point_rows, w_pillar, cols, send, pooled, lifted, acts, *, capacity
):
    micros = point_rows.shape[0]
    channels, inputs = w_pillar.shape
    pillars = pooled.shape[2]
    depth = point_rows.shape[2] // pillars
    weight = w_pillar[...]
    wide_weight = weight.astype(F32)
    rows_out = send.shape[0]
    square = inputs * inputs
    stacked, slot_rows = [], []
    for micro in range(micros):
        lifted[...] = dot(weight, point_rows[micro, 0:inputs])
        moments = found[:, micro, :]
        sizes = moments[:, square + inputs : square + inputs + 1]
        means = moments[:, square : square + inputs]
        count = jnp.sum(sizes, axis=0, keepdims=True)
        mean = jnp.sum(means * sizes, axis=0, keepdims=True) / count
        away = means - mean
        products = lax.dot_general(
            away * sizes, away, (((0,), (0,)), ((), ())),
            preferred_element_type=F32, precision=lax.Precision.HIGHEST,
        )
        summed = jnp.sum(moments, axis=0, keepdims=True)
        products = products + jnp.concatenate(
            [summed[:, k * inputs : (k + 1) * inputs] for k in range(inputs)], axis=0
        )
        cov = products / count
        spun = wide_weight[:, 0:1] * cov[0:1]
        for k in range(1, inputs):
            spun = spun + wide_weight[:, k : k + 1] * cov[k : k + 1]
        spread = jnp.sum(spun * wide_weight, axis=1, keepdims=True)
        centre = jnp.sum(wide_weight * mean, axis=1, keepdims=True)
        rstd = lax.rsqrt(spread + norm_eps)
        inverse = jnp.broadcast_to(1.0 / count, (channels, 1))
        pooled[micros + micro] = jnp.concatenate(
            [
                centre, rstd, inverse, jnp.zeros((channels, 13), F32),
                spun, jnp.zeros((channels, 16 - inputs), F32),
                jnp.broadcast_to(mean, (channels, inputs)), jnp.zeros((channels, LANES - 32 - inputs), F32),
            ],
            axis=1,
        )
        scale = rstd * cols[0:channels, 0:1]
        shift = cols[0:channels, 1:2]
        slot, limit = pillar_notes(point_rows, micro, inputs, pillars)
        slot_rows.append(slot)
        top = jnp.full((channels, pillars), -jnp.inf, F32)
        for n in range(depth):
            piece = slice(n * pillars, (n + 1) * pillars)
            normed = (lifted[:, piece] - centre) * scale + shift
            act = normed * sigmoid(normed)
            acts[:, piece] = act
            top = jnp.maximum(top, jnp.where(limit > n, act, -jnp.inf))
        total = jnp.zeros((channels, pillars), F32)
        for n in range(depth):
            piece = slice(n * pillars, (n + 1) * pillars)
            total = total + jnp.where(limit > n, jnp.exp(acts[:, piece] - top), 0.0)
        result = top + jnp.log(total)
        pooled[micro] = result
        parts = [jnp.zeros((channels, pillars), F32)] * micros
        parts[micro] = result.astype(BF16).astype(F32)
        stacked.append(jnp.transpose(jnp.concatenate(parts, axis=0)))
    values = jnp.concatenate(stacked, axis=0).astype(BF16)
    for group in range(3):
        place = lax.broadcasted_iota(jnp.int32, (rows_out, pillars), 0) + (group - 1) * capacity
        chosen = jnp.concatenate(
            [jnp.where(place.astype(F32) == row, 1.0, 0.0) for row in slot_rows], axis=1
        ).astype(BF16)
        send[:, group * LANES : (group + 1) * LANES] = dot(chosen, values).astype(BF16)


def own_stats(ref, first_row, rows, send):
    micros, _, channels, width = ref.shape
    sums, squares = [], []
    for micro in range(micros):
        total = fold(ref[micro, first_row])
        for row in range(first_row + 1, first_row + rows):
            total = total + fold(ref[micro, row])
        sums.append(total * (1.0 / (rows * width)))
    means = [jnp.sum(total, axis=1, keepdims=True) for total in sums]
    for micro in range(micros):
        spread = jnp.zeros(sums[micro].shape, F32)
        for row in range(first_row, first_row + rows):
            away = ref[micro, row] - means[micro]
            spread = spread + fold(away * away)
        squares.append(spread)
    if channels == LANES:
        send_all(send, [row_of(part) for part in sums + squares])
    else:
        send_all(send, [row_of(*sums), row_of(*squares)])


def conv_pair(source, weight, micro, at, channels):
    window = source[micro, at : at + 4].reshape(12 * channels, source.shape[3])
    return dot(weight[...], window)


def conv_rows(source, weight, out, shape):
    micros, high, channels, width = shape
    for micro in range(micros):
        for at in range(0, high, 2):
            both = conv_pair(source, weight, micro, at, channels)
            out[micro, at] = both[:channels].astype(out.dtype)
            out[micro, at + 1] = both[channels:].astype(out.dtype)


def canvas_kernel(found, columns, where_rows, l_first, out, kept, send, canvas, *, rows):
    scenes, high, channels, width = out.shape
    masks = edges(channels, width)
    slots = found.shape[0]
    lane = lax.broadcasted_iota(jnp.int32, (slots, width), 1).astype(F32)
    for group in range(3):
        values = jnp.transpose(found[:, group * LANES : (group + 1) * LANES].astype(F32))
        first, count = ((rows - 2, 2), (0, rows), (0, 2))[group]
        for scene in range(scenes):
            at = 2 * group + scene
            column = columns[:, at : at + 1] - 1.0
            column = column - jnp.floor(column * (1.0 / width)) * width
            row = jnp.floor((where_rows[at : at + 1] - 1.0) * (1.0 / width))
            mine = values[scene * channels : (scene + 1) * channels]
            placed = jnp.concatenate(
                [jnp.where(row == r * 1.0, mine, 0.0) for r in range(first, first + count)], axis=0
            ).astype(BF16)
            chosen = jnp.where(lane == column, 1.0, 0.0).astype(BF16)
            grid = dot(placed, chosen).astype(BF16)
            start = (0, 2, rows + 2)[group]
            for r in range(count):
                row = grid[r * channels : (r + 1) * channels]
                canvas[scene, start + r] = spread(row, masks)
                kept[scene, start + r] = row
    conv_rows(canvas, l_first, out, out.shape)
    own_stats(out, 1, rows, send)


def second_kernel(found, cols, first_out, l_second_in, out, kept, slopes, stats, send, acts, l_second, sems,
                  *, rows, tiles):
    weight_copy = move(l_second_in, l_second, sems, 0)
    micros, high, channels, width = first_out.shape
    tile = lax.axis_index("tile")
    turned = stat_columns(found, float(rows * width))
    stats[...] = turned
    masks = edges(channels, width)
    for micro in range(micros):
        part = slice(micro * channels, (micro + 1) * channels)
        centre = turned[part, 0:1]
        scale = turned[part, 1:2] * cols[0:channels, 2:3]
        shift = cols[0:channels, 3:4]

        for row in range(high):
            normed = (first_out[micro, row] - centre) * scale + shift
            gate = sigmoid(normed)
            act = normed * gate
            slopes[micro, row] = gate + act * (1.0 - gate)
            if row == 0 or row == high - 1:
                act = act * inside(tile, row - 1, (tiles, rows))
            act = act.astype(BF16)
            acts[micro, row] = spread(act, masks)
            kept[micro, row] = act
    weight_copy.wait()
    conv_rows(acts, l_second, out, out.shape)
    own_stats(out, 0, rows, send)


def up_kernel(found, cols, second_out, w_up, acts, upper, slopes, plain, crossed, stats, send, *, rows):
    micros, _, channels, width = second_out.shape
    peers = send.shape[0]
    each = crossed.shape[0] // peers
    turned = stat_columns(found, float(rows * width))
    stats[...] = turned
    gain, shift = cols[0:channels, 4:5], cols[0:channels, 5:6]
    lines = []
    for micro in range(micros):
        part = slice(micro * channels, (micro + 1) * channels)
        centre, rstd = turned[part, 0:1], turned[part, 1:2]
        slope_sum = jnp.zeros((channels, LANES), F32)
        unit_sum = jnp.zeros((channels, LANES), F32)
        for row in range(rows):
            unit = (second_out[micro, row] - centre) * rstd
            normed = unit * gain + shift
            gate = sigmoid(normed)
            act = normed * gate
            slope = gate + act * (1.0 - gate)
            sloped = slope * unit
            slope_sum = slope_sum + fold(slope)
            unit_sum = unit_sum + fold(sloped)
            slopes[micro, row] = jnp.concatenate([slope, sloped], axis=0)
            act = act.astype(BF16)
            acts[micro, row] = act
            upper[micro, row] = dot(w_up[...], act)
        lines.append(row_of(slope_sum, unit_sum).astype(BF16).astype(F32))
        crossed[micro * channels : (micro + 1) * channels] = dot_lanes(
            jnp.concatenate([acts[micro, row] for row in range(rows)], axis=1),
            jnp.concatenate([slopes[micro, row].astype(BF16) for row in range(rows)], axis=1),
        )
    plain[...] = jnp.concatenate(lines, axis=0)
    used = micros * channels
    if crossed.shape[0] > used:
        crossed[used:] = jnp.zeros((crossed.shape[0] - used, LANES), F32)
    if 2 * micros + each < send.shape[1]:
        send[...] = jnp.zeros(send.shape, F32)
    for peer in range(peers):
        send[peer, 2 * micros : 2 * micros + each] = crossed[peer * each : (peer + 1) * each]
    own_stats(upper, 0, rows, send)


def exact_rows(rows):
    high = rows.astype(BF16).astype(F32)
    return [high, rows - high]


def top_kernel(found, cols, upper, cot, slopes, plain, w_up_t, features, grads, mixed, stats, send, *, rows, each):
    micros, _, wide, width = upper.shape
    channels = w_up_t.shape[0]
    lines = []
    for micro in range(micros):
        lines += list(pooled_stats(found[:, micro, :], found[:, micros + micro, :], float(rows * width)))
    turned = columns_of(lines)
    stats[...] = turned
    gain, shift = cols[:, 6:7], cols[:, 7:8]
    gain_rows, shift_rows, mixed_rows = [], [], []
    for micro in range(micros):
        centre, rstd = turned[:, 2 * micro : 2 * micro + 1], turned[:, 2 * micro + 1 : 2 * micro + 2]
        factor = gain * rstd
        gain_sum = jnp.zeros((wide, LANES), F32)
        shift_sum = jnp.zeros((wide, LANES), F32)
        mixed_sum = jnp.zeros((2 * channels, LANES), F32)
        for row in range(rows):
            unit = (upper[micro, row] - centre) * rstd
            normed = unit * gain + shift
            gate = sigmoid(normed)
            act = normed * gate
            grad = cot[micro, row].astype(F32) * (gate + act * (1.0 - gate))
            features[micro, row] = act.astype(BF16)
            grads[micro, row] = grad
            gain_sum = gain_sum + fold(grad * unit)
            shift_sum = shift_sum + fold(grad)
            below = dot(w_up_t[...], (grad * factor).astype(BF16))
            mixed_sum = mixed_sum + fold(
                slopes[micro, row] * jnp.concatenate([below, below], axis=0)
            )
        gain_rows.append(row_of(gain_sum))
        shift_rows.append(row_of(shift_sum))
        mixed_rows.append(row_of(mixed_sum).astype(BF16).astype(F32))
    mixed[...] = jnp.concatenate(mixed_rows, axis=0)
    rows_out = jnp.concatenate(gain_rows + shift_rows, axis=0)
    crossed = jnp.sum(found[:, 2 * micros : 2 * micros + each, :], axis=0)
    rest = send.shape[1] - 6 * micros - each
    block = exact_rows(rows_out) + mixed_rows + [plain[...], crossed]
    if rest > 0:
        block.append(jnp.zeros((rest, LANES), F32))
    block = jnp.concatenate(block, axis=0)
    send[...] = jnp.broadcast_to(block.astype(BF16)[None], send.shape)


def low_rows(turned, value_of, values, stats, gain, low, high, first, rows, tiles):
    micros, _, channels, width = values.shape
    tile = lax.axis_index("tile")
    masks = edges(channels, width)
    for micro in range(micros):
        part = slice(micro * channels, (micro + 1) * channels)
        centre, rstd = stats[part, 0:1], stats[part, 1:2]
        factor = gain * rstd
        slope_part, shift_part = rstd * turned[part, 0:1], turned[part, 1:2]
        for index in range(high):
            grad, value = value_of(micro, index)
            grad = factor * (grad - shift_part - (value - centre) * slope_part)
            if index + first < 0 or index + first >= rows:
                grad = grad * inside(tile, index + first, (tiles, rows))
            low[micro, index] = spread(grad.astype(BF16), masks)


def first_units(first_out, stats, micro, channels):
    part = slice(micro * channels, (micro + 1) * channels)
    centre, rstd = stats[part, 0:1], stats[part, 1:2]
    return lambda row: (first_out[micro, row] - centre) * rstd


def second_sums(total, weight, factors, stats, micro, micros, count):
    channels = weight.shape[1]
    factor, centre = factors[micro], stats[:, 2 * micro : 2 * micro + 1]
    columns = jnp.transpose(jnp.concatenate([total, jnp.zeros((8 - total.shape[0], LANES), F32)], axis=0))
    beta = factor * stats[:, 2 * micro + 1 : 2 * micro + 2] * columns[:, micro : micro + 1] * (1.0 / count)
    alpha = factor * columns[:, micros + micro : micros + micro + 1] * (1.0 / count)
    square = lax.dot_general(
        weight * beta, weight, (((0,), (0,)), ((), ())),
        preferred_element_type=F32, precision=lax.Precision.HIGHEST,
    )
    square = jnp.concatenate([square, square], axis=1)
    line = jnp.sum(weight * (alpha - beta * centre), axis=0, keepdims=True)
    line = jnp.concatenate([line, line], axis=1)

    def give(mixed, plain, crossed):
        mine = crossed[micro * channels : (micro + 1) * channels]
        return mixed - plain * line - jnp.sum(square * mine, axis=0, keepdims=True)

    return give


def middle_back_kernel(
    found, cols, grads, upper, top_stats, second_out, second_stats, slopes, w_up, w_up_t,
    own_mixed, own_plain, own_crossed, second_act, acts, first_out, first_stats, first_slopes, b_second_in,
    out, top_grad, weight_grad, top_gain_grad, top_shift_grad, expected, send,
    low, top_low, extras, second_dz, b_second, sems, *, rows, tiles, each
):
    weight_copy = move(b_second_in, b_second, sems, 0)
    scene = lax.axis_index("scene")
    micros, _, wide, width = grads.shape
    channels = second_out.shape[2]
    peers = found.shape[0]
    count = float(peers * rows * width)
    kept = 2 * micros
    total = jnp.sum(found[...].astype(F32), axis=0)
    mixed, plain = total[2 * kept : 2 * kept + micros], total[2 * kept + micros : 3 * kept]
    total = total[0:kept] + total[kept : 2 * kept]
    crossed = jnp.concatenate(
        [
            found[peer].astype(F32)[3 * kept : 3 * kept + each]
            for peer in range(-(-micros * channels // each))
        ],
        axis=0,
    )
    own_half(total[0:1] + total[1:2], scene, top_gain_grad)
    own_half(total[2:3] + total[3:4], scene, top_shift_grad)
    factors = [cols[:, 6:7] * top_stats[:, 2 * micro + 1 : 2 * micro + 2] for micro in range(micros)]
    wide_weight = w_up[...].astype(F32)
    turned = columns_of([total[index : index + 1] for index in range(2 * micros)]) * (1.0 / count)
    gain = cols[0:channels, 4:5]
    masks = edges(channels, width)
    second_rows = []
    for micro in range(micros):
        top_centre = top_stats[:, 2 * micro : 2 * micro + 1]
        top_slope = top_stats[:, 2 * micro + 1 : 2 * micro + 2] * turned[:, micro : micro + 1]
        top_shift = turned[:, micros + micro : micros + micro + 1]
        part = slice(micro * channels, (micro + 1) * channels)
        centre, rstd = second_stats[part, 0:1], second_stats[part, 1:2]
        gain_sum = jnp.zeros((channels, LANES), F32)
        shift_sum = jnp.zeros((channels, LANES), F32)
        for row in range(rows):
            grad = factors[micro] * (
                grads[micro, row] - top_shift - (upper[micro, row] - top_centre) * top_slope
            )
            grad = grad.astype(BF16)
            top_low[micro, row] = grad
            unit = (second_out[micro, row] - centre) * rstd
            grad = dot(w_up_t[...], grad) * slopes[micro, row, 0:channels]
            second_dz[micro, row] = grad
            shift_sum = shift_sum + fold(grad)
            gain_sum = gain_sum + fold(grad * unit)
        second_rows.append((shift_sum, gain_sum))
    parts = []
    for micro in range(micros):
        give = second_sums(total, wide_weight, factors, top_stats, micro, micros, count)
        whole = give(mixed[micro : micro + 1], plain[micro : micro + 1], crossed)
        extra = row_of(*second_rows[micro]) - give(
            own_mixed[micro : micro + 1], own_plain[micro : micro + 1], own_crossed[...]
        )
        expected[micro : micro + 1] = whole
        extras[micro : micro + 1] = extra
        parts.append(whole * (1.0 / count) + extra * (1.0 / (rows * width)))
    parts = columns_of(parts)
    for micro in range(micros):
        part = slice(micro * channels, (micro + 1) * channels)
        centre, rstd = second_stats[part, 0:1], second_stats[part, 1:2]
        factor = gain * rstd
        shift_part = parts[0:channels, micro : micro + 1]
        slope_part = parts[channels : 2 * channels, micro : micro + 1] * rstd
        for row in range(rows):
            grad = factor * (
                second_dz[micro, row] - shift_part - (second_out[micro, row] - centre) * slope_part
            )
            low[micro, row] = spread(grad.astype(BF16), masks)
    weight_copy.wait()
    first_back(
        low, top_low, second_act, acts, first_out, first_stats, first_slopes, b_second, extras,
        out, top_grad, weight_grad, send, rows, tiles,
    )


def first_back(
    low, top_low, second_act, acts, first_out, first_stats, slopes, b_second, extras,
    out, top_grad, weight_grad, send, rows, tiles
):
    tile = lax.axis_index("tile")
    micros, _, channels, width = first_out.shape
    half = 6 * channels
    gain_sums, shift_sums = [], []
    for micro in range(micros):
        units = first_units(first_out, first_stats, micro, channels)
        gain_sum = jnp.zeros((channels, LANES), F32)
        shift_sum = jnp.zeros((channels, LANES), F32)
        for at in range(0, rows + 2, 2):
            if at == 0:
                parts = dot(b_second[:, half:], low[micro, 0:2].reshape(half, width))
            elif at == rows:
                parts = dot(b_second[:, :half], low[micro, rows - 2 : rows].reshape(half, width))
            else:
                parts = conv_pair(low, b_second, micro, at - 2, channels)
            for j in range(2):
                grad = parts[channels * j : channels * (j + 1)] * slopes[micro, at + j]
                if at + j == 0 or at + j == rows + 1:
                    grad = grad * inside(tile, at + j - 1, (tiles, rows))
                out[micro, at + j] = grad
                gain_sum = gain_sum + fold(grad * units(at + j))
                shift_sum = shift_sum + fold(grad)
        gain_sums.append(gain_sum)
        shift_sums.append(shift_sum)
        product = dot_lanes(
            jnp.concatenate([top_low[micro, row] for row in range(rows)], axis=1),
            jnp.concatenate([second_act[micro, row] for row in range(rows)], axis=1),
        )
        top_grad[...] = product if micro == 0 else top_grad[...] + product
    conv_grad(low, 0, acts, 0, weight_grad, rows)
    send_all(send, [row_of(*gain_sums), row_of(*shift_sums)] + [extras[m : m + 1] for m in range(micros)])


def conv_grad(low, low_first, values, value_first, total, rows):
    micros, _, channels, width = values.shape
    for micro in range(micros):
        grads = jnp.concatenate([low[micro, row + low_first] for row in range(rows)], axis=1)
        windows = jnp.concatenate(
            [
                values[micro, row + value_first : row + value_first + 3].reshape(3 * channels, width)
                for row in range(rows)
            ],
            axis=1,
        )
        product = dot_lanes(grads, windows)
        total[...] = product if micro == 0 else total[...] + product


def half_rows(total, half, scene):
    channels = 2 * half
    start = scene * half
    mine = jnp.concatenate(
        [total[b * channels + start : b * channels + start + half, :] for b in range(2, -1, -1)], axis=0
    )
    wing = mine[:, LANES:]
    cut = wing.shape[0] // 2
    return [mine[:, :LANES], jnp.concatenate([wing[:cut], wing[cut:]], axis=1)]


def pick_kernel(
    found, cols, grads, first_out, first_stats, b_first_in, columns, where_rows,
    canvas, second_grad, top_grad, expected,
    send, gain_grad, shift_grad, second_gain_grad, second_shift_grad, low, grid, b_first, first_grad, whole, sems,
    *, rows, tiles, each
):
    weight_copy = move(b_first_in, b_first, sems, 0)
    scene = lax.axis_index("scene")
    micros, high, channels, width = grads.shape
    sums = sum_rows(found, 2 + micros)
    second = sum(sums[2:]) + jnp.sum(expected[...], axis=0, keepdims=True)
    own_half(second[:, :channels], scene, second_shift_grad)
    own_half(second[:, channels:], scene, second_gain_grad)
    sums = sums[:2]
    own_half(sums[0][:, :channels] + sums[0][:, channels:], scene, gain_grad)
    own_half(sums[1][:, :channels] + sums[1][:, channels:], scene, shift_grad)
    turned = columns_of(sums) * (1.0 / (found.shape[0] * rows * width))
    masks = edges(channels, width)
    for micro in range(micros):
        part = slice(micro * channels, (micro + 1) * channels)
        centre, rstd = first_stats[part, 0:1], first_stats[part, 1:2]
        factor = cols[0:channels, 2:3] * rstd
        slope_part, shift_part = rstd * turned[part, 0:1], turned[part, 1:2]
        for row in range(high):
            grad = grads[micro, row]
            if 1 <= row <= rows:
                grad = grad - shift_part - (first_out[micro, row] - centre) * slope_part
            low[micro, row] = spread((factor * grad).astype(BF16), masks)
    weight_copy.wait()
    half = 6 * channels
    for micro in range(micros):
        for at in range(0, rows + 4, 2):
            if at == 0:
                parts = dot(b_first[:, half:], low[micro, 0:2].reshape(half, width))
            elif at == rows + 2:
                parts = dot(b_first[:, :half], low[micro, rows : rows + 2].reshape(half, width))
            else:
                parts = conv_pair(low, b_first, micro, at - 2, channels)
            grid[micro, at] = parts[:channels].astype(BF16)
            grid[micro, at + 1] = parts[channels:].astype(BF16)
    conv_grad(low, 0, canvas, 0, first_grad, high)
    half = channels // 2
    for s in range(2):
        parts = half_rows(first_grad, half, s) + half_rows(second_grad, half, s)
        mine = top_grad[s * channels : (s + 1) * channels, :]
        parts.append(jnp.concatenate([mine[:half], mine[half:]], axis=1))
        parts = jnp.concatenate(parts, axis=0)
        whole[s, 0 : parts.shape[0]] = parts
        if whole.shape[1] > parts.shape[0]:
            whole[s, parts.shape[0] :] = jnp.zeros((whole.shape[1] - parts.shape[0], LANES), F32)
    slots = columns.shape[0]
    lane = lax.broadcasted_iota(jnp.int32, (slots, width), 1).astype(F32)
    groups = []
    for group in range(3):
        start, first, count = ((0, rows - 2, 2), (2, 0, rows), (rows + 2, 0, 2))[group]
        picked = []
        for micro in range(micros):
            at = 2 * group + micro
            column = columns[:, at : at + 1] - 1.0
            column = column - jnp.floor(column * (1.0 / width)) * width
            place = jnp.floor((where_rows[at : at + 1] - 1.0) * (1.0 / width))
            chosen = jnp.where(lane == column, 1.0, 0.0).astype(BF16)
            here = dot_lanes(grid[micro, start : start + count].reshape(count * channels, width), chosen)
            total = jnp.zeros((channels, slots), F32)
            for r in range(count):
                total = total + jnp.where(
                    place == (first + r) * 1.0, here[r * channels : (r + 1) * channels], 0.0
                )
            picked.append(total)
        groups.append(jnp.transpose(jnp.concatenate(picked, axis=0)))
    capacity = slots // tiles
    block = send.shape[1]

    def filled(parts):
        missing = block - sum(part.shape[0] for part in parts)
        if missing > 0:
            parts = parts + [jnp.zeros((missing, LANES), F32)]
        return jnp.concatenate(parts, axis=0).astype(BF16)

    for spot in range(tiles):
        mine = slice(spot * capacity, (spot + 1) * capacity)
        send[2 * spot + scene] = filled([picked[mine] for picked in groups])
        send[2 * spot + 1 - scene] = filled([whole[s, spot * each : (spot + 1) * each] for s in range(2)])


def pillar_back_kernel(found, rows_in, w_pillar, cols, pooled, send, grads, lifted, rows, sems,
                       *, capacity, each):
    fetched = move(rows_in, rows, sems, 0)
    micros = rows.shape[0]
    _, channels, pillars = pooled.shape
    stats = pooled.at[micros : 2 * micros]
    inputs = w_pillar.shape[1]
    depth = rows.shape[2] // pillars
    scene = lax.axis_index("scene")
    peers = found.shape[0]
    slot_count = peers // 2 * capacity
    blocks = [found[2 * t + scene].astype(F32) for t in range(peers // 2)]
    before, own, after = [
        jnp.concatenate([block[group * capacity : (group + 1) * capacity] for block in blocks], axis=0)
        for group in range(3)
    ]
    gap = jnp.zeros((capacity, LANES), F32)
    returned = (
        own
        + jnp.concatenate([before[capacity:], gap], axis=0)
        + jnp.concatenate([gap, after[: slot_count - capacity]], axis=0)
    )
    turned = jnp.transpose(returned)
    place = lax.broadcasted_iota(jnp.int32, (slot_count, pillars), 0).astype(F32)
    gain, shift = cols[0:channels, 0:1], cols[0:channels, 1:2]
    gain_sums, shift_sums = [], []
    outer = jnp.zeros((16, channels), F32)
    fetched.wait()
    for micro in range(micros):
        lifted[...] = dot(w_pillar[...], rows[micro, 0:inputs])
        slot, limit = pillar_notes(rows, micro, inputs, pillars)
        chosen = jnp.where(place == slot, 1.0, 0.0).astype(BF16)
        back = dot(turned[micro * channels : (micro + 1) * channels].astype(BF16), chosen)
        centre, rstd = stats[micro, :, 0:1], stats[micro, :, 1:2]
        pool = pooled[micro]
        gain_sum = jnp.zeros((channels, pillars), F32)
        shift_sum = jnp.zeros((channels, pillars), F32)
        for n in range(depth):
            piece = slice(n * pillars, (n + 1) * pillars)
            unit = (lifted[:, piece] - centre) * rstd
            normed = unit * gain + shift
            gate = sigmoid(normed)
            act = normed * gate
            slope = gate + act * (1.0 - gate)
            grad = jnp.where(limit > n, back * jnp.exp(act - pool) * slope, 0.0)
            grads[micro, :, piece] = grad
            gain_sum = gain_sum + grad * unit
            shift_sum = shift_sum + grad
        gain_sums.append(gain_sum)
        shift_sums.append(shift_sum)
        scale = jnp.transpose(jnp.broadcast_to(rstd * gain, (channels, LANES)))[0:1]
        outer = outer + dot_lanes(rows[micro], grads[micro].astype(BF16)) * scale
    exact = jnp.concatenate([row_of(*gain_sums), row_of(*shift_sums)], axis=0)
    lines = [jnp.concatenate([outer[k : k + 1], outer[k + 1 : k + 2]], axis=1) for k in range(0, 10, 2)]
    weights = found[1 - scene].astype(F32)
    for t in range(1, peers // 2):
        weights = weights + found[2 * t + 1 - scene].astype(F32)
    rest = send.shape[2] - 9 - each
    for s in range(2):
        block = exact_rows(exact) + lines + [weights[s * each : (s + 1) * each]]
        if rest > 0:
            block.append(jnp.zeros((rest, LANES), F32))
        block = jnp.concatenate(block, axis=0).astype(BF16)
        send[:, s] = jnp.broadcast_to(block[None], (send.shape[0],) + block.shape)


def points_kernel(
    found, rows_in, grads, w_pillar, cols, pooled,
    points_grad, pillar_grad, gain_grad, shift_grad, first_grad, second_grad, up_grad, rows, lifted, sems,
    *, each
):
    fetched = move(rows_in, rows, sems, 0)
    scene = lax.axis_index("scene")
    micros, channels, _ = grads.shape
    stats = pooled.at[micros : 2 * micros]
    _, _, inputs, depth, pillars = points_grad.shape
    half = channels // 2
    total = jnp.sum(found[...].astype(F32), axis=0)
    total = jnp.concatenate([total[0:2] + total[2:4], total[4:9]], axis=0)
    own_half(total[0:1, :channels] + total[0:1, channels:], scene, gain_grad)
    own_half(total[1:2, :channels] + total[1:2, channels:], scene, shift_grad)
    turned = jnp.transpose(jnp.concatenate([total, jnp.zeros((1, LANES), F32)], axis=0))
    weight_grad = jnp.concatenate(
        [turned[(k % 2) * channels : (k % 2 + 1) * channels, 2 + k // 2 : 3 + k // 2] for k in range(inputs)],
        axis=1,
    )
    weight = jnp.transpose(w_pillar[...].astype(F32)).astype(BF16)
    fetched.wait()
    for micro in range(micros):
        lifted[...] = dot(w_pillar[...], rows[micro, 0:inputs])
        part = slice(micro * channels, (micro + 1) * channels)
        centre, rstd, inverse = stats[micro, :, 0:1], stats[micro, :, 1:2], stats[micro, :, 2:3]
        factor = cols[0:channels, 0:1] * rstd
        gain_part, shift_part = turned[part, 0:1], turned[part, 1:2]
        spun, mean = stats[micro, :, 16 : 16 + inputs], stats[micro, :, 32 : 32 + inputs]
        weight_grad = weight_grad - factor * (shift_part * mean + gain_part * rstd * spun)
        gain_part, shift_part = gain_part * inverse * rstd, shift_part * inverse
        _, limit = pillar_notes(rows, micro, inputs, pillars)
        for n in range(depth):
            piece = slice(n * pillars, (n + 1) * pillars)
            low = factor * (grads[micro, :, piece] - shift_part - (lifted[:, piece] - centre) * gain_part)
            low = jnp.where(limit > n, low, 0.0).astype(BF16)
            points_grad[micro, 0, :, n, :] = dot(weight, low)
    weight_grad = jnp.concatenate([weight_grad, jnp.zeros((channels, LANES - inputs), F32)], axis=1)
    weight_grad = jnp.transpose(weight_grad)[0:inputs]
    pillar_grad[...] = jnp.where(scene == 0, weight_grad[:, :half], weight_grad[:, half:])
    whole = jnp.concatenate(
        [
            (found[2 * t].astype(F32) + found[2 * t + 1].astype(F32))[9 : 9 + each]
            for t in range(found.shape[0] // 2)
        ],
        axis=0,
    )
    for index, out in enumerate((first_grad, second_grad)):
        base = index * 9 * half * channels // LANES
        lead = 3 * half
        mine = whole[base : base + lead]
        wing = whole[base + lead : base + lead + lead // 2]
        wing = jnp.concatenate([wing[:, :channels], wing[:, channels:]], axis=0)
        both = jnp.concatenate([mine, wing], axis=1)
        for a in range(3):
            for b in range(3):
                at = (3 * a + b) * channels
                out[:, at : at + channels] = both[b * half : (b + 1) * half, a * channels : (a + 1) * channels]
    base = 2 * 9 * half * channels // LANES
    top = whole[base : base + half]
    up_grad[...] = jnp.concatenate([top[:, :channels], top[:, channels:]], axis=0)


def swap(blocks, axes):
    return lax.all_to_all(blocks, axes, split_axis=0, concat_axis=0)


def shards(
    points, point_counts, pillar_tile, pillar_cell,
    pillar_weight, pillar_gain, pillar_shift,
    first_weight, first_gain, first_shift,
    second_weight, second_gain, second_shift,
    up_weight, up_gain, up_shift, cotangent,
):
    micros, _, inputs, depth, pillars = points.shape
    channels = up_weight.shape[1]
    upper = cotangent.shape[2]
    rows, width = cotangent.shape[3:]
    tiles = lax.axis_size("tile")
    scenes = lax.axis_size("scene")
    peers = tiles * scenes
    capacity = 2 * pillars // tiles
    slot_count = tiles * capacity
    half = channels // 2

    def vmem(shape, dtype):
        return pltpu.VMEM(shape, dtype)

    def grid(high, dtype=F32, lead=channels):
        return ((micros, high, lead, width), dtype)

    sums = ((peers, 2, LANES), F32)
    sources = (
        pillar_tile, pillar_cell, point_counts, points,
        first_weight, second_weight, up_weight, pillar_weight.T,
        pillar_gain, pillar_shift, first_gain, first_shift, second_gain, second_shift, up_gain, up_shift,
    )
    moments, packed, point_rows = run(
        functools.partial(moments_kernel, capacity=capacity),
        [
            ((tiles, scenes, 4, LANES), F32), ((layout(half, channels)[-1] + 16, LANES), BF16),
            ((micros, 16, depth * pillars), BF16),
        ],
        *sources,
        hbm=range(len(sources)), copies=len(sources), limit=WIDE_LIMIT,
        scratch=[vmem(source.shape, source.dtype) for source in sources]
        + [vmem((inputs * depth, pillars), F32)],
    )
    moments = swap(moments.reshape(peers, 4, LANES), BOTH)
    both = lax.all_gather(packed, "scene")
    taps = ((2 * channels, 12 * channels), BF16)
    w_pillar, cols, l_first, l_second, b_first, b_second, w_up, w_up_t = run(
        functools.partial(unpack_kernel, inputs=inputs),
        [
            ((channels, inputs), BF16), ((LANES, 8), F32), taps, taps + (1,), taps + (1,), taps + (1,),
            ((upper, channels), BF16), ((channels, upper), BF16),
        ],
        both,
        scratch=[vmem(*taps), vmem(*taps), vmem(*taps)], copies=3,
    )
    cot = cotangent[:, 0].transpose(0, 2, 1, 3)

    send, pooled = run(
        functools.partial(pillar_kernel, capacity=capacity),
        [((slot_count, 3 * LANES), BF16), ((2 * micros, channels, pillars), F32)],
        moments, point_rows, w_pillar, cols,
        scratch=[vmem((channels, depth * pillars), F32), vmem((channels, depth * pillars), F32)],
    )
    arrived = swap(send.reshape(tiles, capacity, 3 * LANES), "tile").reshape(slot_count, 3 * LANES)
    cell_columns, cell_rows = run(
        functools.partial(cells_kernel, capacity=capacity),
        [((slot_count, LANES), F32), ((8, slot_count), F32)],
        moments,
        cost=pl.CostEstimate(flops=10**7, bytes_accessed=10**6, transcendentals=0),
    )
    arrived, cot = lax.optimization_barrier((arrived, cot))

    first_out, canvas, send = run(
        functools.partial(canvas_kernel, rows=rows),
        [grid(rows + 2), grid(rows + 4, BF16), sums],
        arrived, cell_columns, cell_rows, l_first,
        scratch=[vmem(*grid(rows + 4, BF16, 3 * channels))],
    )
    second_out, first_act, first_slopes, first_stats, send = run(
        functools.partial(second_kernel, rows=rows, tiles=tiles),
        [grid(rows), grid(rows + 2, BF16), grid(rows + 2), ((LANES, 8), F32), sums],
        swap(send, BOTH), cols, first_out, l_second,
        hbm=(3,), scratch=[vmem(*grid(rows + 2, BF16, 3 * channels)), vmem(*taps)], copies=1,
    )
    part = -(-micros * channels // peers)
    second_act, up_out, slopes, plain, crossed, second_stats, send = run(
        functools.partial(up_kernel, rows=rows),
        [
            grid(rows, BF16), grid(rows, F32, upper), grid(rows, F32, 2 * channels), ((micros, LANES), F32),
            ((peers * part, LANES), F32), ((LANES, 8), F32), ((peers, -(-(2 * micros + part) // 8) * 8, LANES), F32),
        ],
        swap(send, BOTH), cols, second_out, w_up,
    )
    features, grads, mixed, top_stats, send = run(
        functools.partial(top_kernel, rows=rows, each=part),
        [
            grid(rows, BF16, upper), grid(rows, F32, upper), ((micros, LANES), F32), ((LANES, 8), F32),
            ((peers, -(-(6 * micros + part) // 8) * 8, LANES), BF16),
        ],
        swap(send, BOTH), cols, up_out, cot, slopes, plain, w_up_t,
    )
    features = with_layout_constraint(features.transpose(0, 2, 1, 3)[:, None], Layout((0, 1, 2, 3, 4)))
    features, send = lax.optimization_barrier((features, send))
    vector, top_vector, matrix = ((half,), F32), ((upper // 2,), F32), ((half, 9 * channels), F32)
    cross = ((3 * channels, 3 * channels), F32)
    first_dz, top_grad, second_cross, up_gain_grad, up_shift_grad, expected, send = run(
        functools.partial(middle_back_kernel, rows=rows, tiles=tiles, each=part),
        [
            grid(rows + 2), ((upper, channels), F32), cross, top_vector, top_vector, ((micros, LANES), F32),
            ((peers, 2 + micros, LANES), F32),
        ],
        swap(send, BOTH), cols, grads, up_out, top_stats, second_out, second_stats, slopes, w_up, w_up_t,
        mixed, plain, crossed, second_act, first_act, first_out, first_stats, first_slopes, b_second,
        hbm=(18,),
        scratch=[
            vmem(*grid(rows, BF16, 3 * channels)), vmem(*grid(rows, BF16, upper)), vmem((micros, LANES), F32),
            vmem(*grid(rows)), vmem(*taps),
        ],
        copies=1,
    )
    length = (2 * 9 * half * channels + upper * half) // LANES
    each = -(-length // tiles)
    block = -(-max(3 * capacity, 2 * each) // 8) * 8
    send, first_gain_grad, first_shift_grad, second_gain_grad, second_shift_grad = run(
        functools.partial(pick_kernel, rows=rows, tiles=tiles, each=each),
        [((peers, block, LANES), BF16), vector, vector, vector, vector],
        swap(send, BOTH), cols, first_dz, first_out, first_stats, b_first, cell_columns, cell_rows,
        canvas, second_cross, top_grad, expected,
        hbm=(5,),
        scratch=[
            vmem(*grid(rows + 2, BF16, 3 * channels)), vmem(*grid(rows + 4, BF16)), vmem(*taps), vmem(*cross),
            vmem((scenes, tiles * each, LANES), F32),
        ],
        copies=1,
    )
    block = -(-(9 + each) // 8) * 8
    send, pillar_dz = run(
        functools.partial(pillar_back_kernel, capacity=capacity, each=each),
        [((tiles, scenes, block, LANES), BF16), ((micros, channels, depth * pillars), F32)],
        swap(send, BOTH), point_rows, w_pillar, cols, pooled,
        hbm=(1,),
        scratch=[vmem((channels, depth * pillars), F32), vmem((micros, 16, depth * pillars), BF16)],
        copies=1,
    )
    points_grad, pillar_grad, pillar_gain_grad, pillar_shift_grad, first_grad, second_grad, up_grad = run(
        functools.partial(points_kernel, each=each),
        [
            ((micros, 1, inputs, depth, pillars), F32), ((inputs, half), F32), vector, vector,
            matrix, matrix, ((upper // 2, channels), F32),
        ],
        swap(send.reshape(peers, block, LANES), BOTH), point_rows, pillar_dz, w_pillar, cols, pooled,
        hbm=(1,),
        scratch=[vmem((micros, 16, depth * pillars), BF16), vmem((channels, depth * pillars), F32)],
        copies=1,
    )
    return (
        features, points_grad,
        pillar_grad.T, pillar_gain_grad, pillar_shift_grad,
        first_grad, first_gain_grad, first_shift_grad,
        second_grad, second_gain_grad, second_shift_grad,
        up_grad, up_gain_grad, up_shift_grad,
    )


def solution(mesh):
    matrix, vector = P("scene", None), P("scene")
    grid = P(None, "scene", None, "tile", None)
    cloud = P(None, "scene", None, None, "tile")
    pillar = P(None, "scene", "tile")
    weights = (matrix, vector, vector) * 4
    return jax.shard_map(
        shards,
        mesh=mesh,
        in_specs=(cloud, pillar, pillar, pillar) + weights + (grid,),
        out_specs=(grid, cloud) + weights,
        check_vma=False,
    )
```

```python
import functools

import jax
import jax.numpy as jnp
from jax import lax
from jax.experimental import pallas as pl
from jax.experimental.layout import Layout, with_layout_constraint
from jax.experimental.pallas import tpu as pltpu
from jax.sharding import PartitionSpec as P

norm_eps = 0.001
BOTH = ("tile", "scene")
F32 = jnp.float32
BF16 = jnp.bfloat16
VMEM_LIMIT = 24 * 1024 * 1024
WIDE_LIMIT = 60 * 1024 * 1024
LANES = 128


def run(kernel, outs, *args, hbm=(), scratch=(), copies=0, cost=None, limit=VMEM_LIMIT):
    specs = [
        pl.BlockSpec(memory_space=pltpu.HBM if index in hbm else pltpu.VMEM) for index in range(len(args))
    ]
    scratch = list(scratch)
    if copies:
        scratch.append(pltpu.SemaphoreType.DMA((copies,)))
    return pl.pallas_call(
        kernel,
        out_shape=[jax.ShapeDtypeStruct(out[0], out[1]) for out in outs],
        in_specs=specs,
        out_specs=[
            pl.BlockSpec(memory_space=pltpu.HBM if len(out) > 2 else pltpu.VMEM) for out in outs
        ],
        scratch_shapes=scratch,
        compiler_params=pltpu.CompilerParams(vmem_limit_bytes=limit),
        cost_estimate=cost,
    )(*args)


def move(source, target, sems, index):
    copy = pltpu.make_async_copy(source, target, sems.at[index])
    copy.start()
    return copy


def dot(left, right, precision=None):
    return jnp.dot(left, right, preferred_element_type=F32, precision=precision)


def dot_lanes(left, right, precision=None):
    return lax.dot_general(
        left, right, (((1,), (1,)), ((), ())), preferred_element_type=F32, precision=precision
    )


def sigmoid(values):
    return 0.5 + 0.5 * jnp.tanh(0.5 * values)


def fold(values):
    total = values[:, :LANES]
    for start in range(LANES, values.shape[1], LANES):
        total = total + values[:, start : start + LANES]
    return total


def row_of(left, right=None):
    both = left if right is None else jnp.concatenate([left, right], axis=0)
    return jnp.sum(jnp.transpose(both), axis=0, keepdims=True)


def columns_of(rows):
    rows = rows + [jnp.zeros((8 - len(rows), LANES), F32)] if len(rows) < 8 else rows
    return jnp.transpose(jnp.concatenate(rows, axis=0))


def inside(tile, row, height):
    tiles, rows = height
    place = tile * rows + row
    return jnp.where((place >= 0) & (place < tiles * rows), 1.0, 0.0).astype(F32)


def send_all(ref, rows):
    for index, row in enumerate(rows):
        ref[:, index : index + 1, :] = jnp.broadcast_to(row[None], (ref.shape[0], 1, LANES))


def pooled_stats(means, squares, count):
    peers = means.shape[0]
    mean = jnp.sum(means, axis=0, keepdims=True) * (1.0 / peers)
    away = means - mean
    spread = jnp.sum(squares + count * away * away, axis=0, keepdims=True) * (1.0 / (peers * count))
    return mean, lax.rsqrt(spread + norm_eps)


def stat_columns(found, count):
    return columns_of(list(pooled_stats(found[:, 0, :], found[:, 1, :], count)))


def sum_rows(found, lines):
    return [jnp.sum(found[:, index, :], axis=0, keepdims=True) for index in range(lines)]


def own_half(row, scene, out):
    size = out.shape[0]
    out[...] = jnp.where(scene == 0, row[:, 0:size], row[:, size : 2 * size]).reshape(size)


def edges(channels, width):
    lane = lax.broadcasted_iota(jnp.int32, (channels, width), 1)
    return lane > 0, lane < width - 1


def spread(row, masks):
    zero = jnp.zeros_like(row)
    left = jnp.where(masks[0], pltpu.roll(row, 1, 1), zero)
    right = jnp.where(masks[1], pltpu.roll(row, row.shape[1] - 1, 1), zero)
    return jnp.concatenate([left, row, right], axis=0)


def layout(half, channels):
    first = 0
    second = first + half * -(-9 * channels // LANES)
    up = second + half * -(-9 * channels // LANES)
    vectors = up + channels
    return first, second, up, vectors, vectors + 16


def widen(value):
    missing = LANES - value.shape[1]
    if missing == 0:
        return value
    return jnp.concatenate([value, jnp.zeros((value.shape[0], missing), value.dtype)], axis=1)


def pack(held, out):
    first, second, up, pillar = held[:4]
    half, channels = first.shape[0], up.shape[1]
    starts = layout(half, channels)
    for ref, start in ((first, starts[0]), (second, starts[1])):
        for j in range(-(-9 * channels // LANES)):
            out[start + j * half : start + (j + 1) * half, :] = widen(
                ref[:, j * LANES : min((j + 1) * LANES, 9 * channels)]
            )
    out[starts[2] : starts[2] + channels, :] = widen(up[...])
    rows = [vector[...].astype(F32).reshape(1, -1) for vector in held[4:]]
    rows = [widen(row) for row in rows] + [jnp.zeros((16 - len(rows), LANES), F32)]
    turned = widen(pillar[...].astype(F32))
    rows += [turned, jnp.zeros((16 - turned.shape[0], LANES), F32)]
    out[starts[3] :, :] = jnp.concatenate(rows, axis=0).astype(BF16)


def unpack_kernel(
    both, w_pillar, cols, l_first, l_second, b_first, b_second, w_up, w_up_t,
    h_second, h_first_back, h_second_back, sems, *, inputs
):
    half = w_pillar.shape[0] // 2
    channels = 2 * half
    starts = layout(half, channels)
    tiles = -(-9 * channels // LANES)

    def wide(start):
        return jnp.concatenate(
            [
                jnp.concatenate(
                    [both[s, start + j * half : start + (j + 1) * half, :] for j in range(tiles)], axis=1
                )
                for s in range(2)
            ],
            axis=0,
        ).astype(F32)

    up = jnp.concatenate(
        [both[s, starts[2] : starts[2] + channels, 0:channels] for s in range(2)], axis=0
    )
    w_up[...] = up
    w_up_t[...] = jnp.transpose(up.astype(F32)).astype(BF16)
    turned = jnp.concatenate(
        [both[s, starts[4] : starts[4] + 16, 0:half].astype(F32) for s in range(2)], axis=1
    )
    w_pillar[...] = jnp.transpose(widen(turned))[0:channels, 0:inputs].astype(BF16)
    vectors = [both[s, starts[3] : starts[3] + 16, :].astype(F32) for s in range(2)]
    rows = []
    for index in range(8):
        size = half if index < 6 else channels
        row = jnp.concatenate([vectors[s][index : index + 1, 0:size] for s in range(2)], axis=1)
        rows.append(jnp.concatenate([row] * (LANES // (2 * size)), axis=1))
    cols[...] = columns_of(rows)
    zero = jnp.zeros((channels, 3 * channels), F32)
    copies = []
    for weight, ahead, back in (
        (wide(starts[0]), l_first, h_first_back), (wide(starts[1]), h_second, h_second_back)
    ):
        weight = weight[:, : 9 * channels]
        turned = jnp.transpose(weight)
        flipped = jnp.concatenate(
            [turned[tap * channels : (tap + 1) * channels] for tap in range(8, -1, -1)], axis=1
        )
        for ref, taps in ((ahead, weight), (back, flipped)):
            ref[0:channels, :] = jnp.concatenate([taps, zero], axis=1).astype(BF16)
            ref[channels : 2 * channels, :] = jnp.concatenate([zero, taps], axis=1).astype(BF16)
    copies.append(move(h_second, l_second, sems, 0))
    copies.append(move(h_first_back, b_first, sems, 1))
    copies.append(move(h_second_back, b_second, sems, 2))
    for copy in copies:
        copy.wait()


def slot_line(wide, depth, inputs):
    return jnp.concatenate([wide[pl.ds(n, inputs, stride=depth), :] for n in range(depth)], axis=1)


def slot_mask(count, depth):
    return jnp.concatenate([jnp.where(count > n, 1.0, 0.0) for n in range(depth)], axis=1)


def ranks(tile):
    pillars = tile.shape[1]
    across = jnp.broadcast_to(tile, (pillars, pillars))
    down = jnp.transpose(across)
    row = lax.broadcasted_iota(jnp.int32, (pillars, pillars), 0)
    col = lax.broadcasted_iota(jnp.int32, (pillars, pillars), 1)
    return jnp.sum(jnp.where((across == down) & (row < col), 1.0, 0.0), axis=0, keepdims=True)


def moments_kernel(*refs, capacity):
    number = 16
    sources, out, packed, lines_out = refs[:number], *refs[number : number + 3]
    held, wide, sems = refs[number + 3 : 2 * number + 3], refs[-2], refs[-1]
    copies = [move(sources[i], held[i], sems, i) for i in range(number)]
    tiles, cells, counts, points = held[:4]
    micros, _, inputs, depth, pillars = points.shape
    peers, scenes = out.shape[:2]
    copies[0].wait()
    copies[1].wait()
    lines, slot_rows = [], []
    for micro in range(micros):
        tile = tiles[micro].astype(F32)
        cell = (cells[micro] + 1).astype(F32)
        high = jnp.floor(cell * (1.0 / 16.0))
        low = cell - high * 16.0
        rank = ranks(tile)
        slot_rows.append(tile * capacity + rank)
        spot = lax.broadcasted_iota(jnp.int32, (capacity, pillars), 0).astype(F32)
        placed = jnp.where(spot == rank, 1.0, 0.0).astype(BF16)
        peer = lax.broadcasted_iota(jnp.int32, (peers, pillars), 0).astype(F32)
        for group in range(3):
            named = tile == peer + (group - 1.0)
            lines.append(
                16.0 * dot_lanes(jnp.where(named, high, 0.0).astype(BF16), placed)
                + dot_lanes(jnp.where(named, low, 0.0).astype(BF16), placed)
            )
    used = 3 * micros * capacity
    line = jnp.concatenate(lines + [jnp.zeros((peers, LANES - used), F32)], axis=1).reshape(peers, 1, LANES)
    for scene in range(scenes):
        out[:, scene, micros : micros + 1, :] = line
    copies[2].wait()
    copies[3].wait()
    parts, mean_rows, totals = [], [], []
    for micro in range(micros):
        wide[...] = points[micro, 0].astype(F32).reshape(inputs * depth, pillars)
        rows = slot_line(wide, depth, inputs)
        notes = jnp.concatenate([slot_rows[micro], counts[micro].astype(F32)], axis=0)
        notes = jnp.concatenate([notes, jnp.zeros((2, rows.shape[1] - pillars), F32)], axis=1)
        lines_out[micro] = jnp.concatenate(
            [rows, notes, jnp.zeros((14 - inputs, rows.shape[1]), F32)], axis=0
        ).astype(BF16)
        mask = slot_mask(counts[micro], depth)
        total = jnp.sum(mask, axis=1, keepdims=True)
        mean = jnp.sum(rows * mask, axis=1, keepdims=True) / total
        centred = jnp.concatenate(
            [(rows - mean) * mask, jnp.zeros((16 - inputs, rows.shape[1]), F32)], axis=0
        )
        high = centred.astype(BF16)
        parts += [high, (centred - high.astype(F32)).astype(BF16)]
        lane = lax.broadcasted_iota(jnp.int32, (inputs, inputs), 1)
        diagonal = lax.broadcasted_iota(jnp.int32, (inputs, inputs), 0) == lane
        mean_rows.append(jnp.sum(jnp.where(diagonal, mean, 0.0), axis=0, keepdims=True))
        totals.append(total)
    parts = jnp.concatenate(parts, axis=0)
    every = dot_lanes(parts, parts)
    for micro in range(micros):
        at = 32 * micro
        square = every[at : at + 32, at : at + 32]
        products = (
            square[0:inputs, 0:inputs] + square[16 : 16 + inputs, 0:inputs]
            + square[0:inputs, 16 : 16 + inputs] + square[16 : 16 + inputs, 16 : 16 + inputs]
        )
        row = jnp.concatenate(
            [products[k : k + 1] for k in range(inputs)]
            + [mean_rows[micro], totals[micro], jnp.zeros((1, LANES - inputs * inputs - inputs - 1), F32)],
            axis=1,
        )
        for scene in range(scenes):
            out[:, scene, micro : micro + 1, :] = jnp.broadcast_to(row[None], (peers, 1, LANES))
    for copy in copies[4:]:
        copy.wait()
    pack(held[4:], packed)


def cells_kernel(found, columns, rows, *, capacity):
    scene = lax.axis_index("scene")
    slots = columns.shape[0]
    peers = found.shape[0]
    values = found[:, 2, :]
    slot = lax.broadcasted_iota(jnp.int32, (slots, peers), 0)
    peer = lax.broadcasted_iota(jnp.int32, (slots, peers), 1)
    lane = lax.broadcasted_iota(jnp.int32, (slots, LANES), 1)
    row = lax.broadcasted_iota(jnp.int32, (slots, LANES), 0)
    result = jnp.zeros((slots, LANES), F32)
    chosen = jnp.where(peer == 2 * (slot // capacity) + scene, 1.0, 0.0)
    spread = dot(chosen, values, lax.Precision.HIGHEST)
    for micro in range(2):
        for group in range(3):
            mine = jnp.where(lane == (3 * micro + group) * capacity + row % capacity, spread, 0.0)
            column = jnp.sum(mine, axis=1, keepdims=True)
            result = jnp.where(lane == 2 * group + micro, column, result)
    columns[...] = result
    rows[...] = jnp.transpose(result)[0:8]


def pillar_notes(rows, micro, inputs, pillars):
    notes = rows[micro, :, 0:pillars].astype(F32)
    return notes[inputs : inputs + 1], notes[inputs + 1 : inputs + 2]


def pillar_kernel(
    found, rows_in, w_pillar, cols, send, pooled, lifted, acts, point_rows, sems, *, capacity
):
    fetched = move(rows_in, point_rows, sems, 0)
    micros = point_rows.shape[0]
    channels, inputs = w_pillar.shape
    pillars = pooled.shape[2]
    depth = point_rows.shape[2] // pillars
    weight = w_pillar[...]
    wide_weight = weight.astype(F32)
    rows_out = send.shape[0]
    square = inputs * inputs
    stacked, slot_rows = [], []
    bounds = []
    for micro in range(micros):
        moments = found[:, micro, :]
        sizes = moments[:, square + inputs : square + inputs + 1]
        means = moments[:, square : square + inputs]
        count = jnp.sum(sizes, axis=0, keepdims=True)
        mean = jnp.sum(means * sizes, axis=0, keepdims=True) / count
        away = means - mean
        products = lax.dot_general(
            away * sizes, away, (((0,), (0,)), ((), ())),
            preferred_element_type=F32, precision=lax.Precision.HIGHEST,
        )
        summed = jnp.sum(moments, axis=0, keepdims=True)
        products = products + jnp.concatenate(
            [summed[:, k * inputs : (k + 1) * inputs] for k in range(inputs)], axis=0
        )
        cov = products / count
        spun = wide_weight[:, 0:1] * cov[0:1]
        for k in range(1, inputs):
            spun = spun + wide_weight[:, k : k + 1] * cov[k : k + 1]
        spread = jnp.sum(spun * wide_weight, axis=1, keepdims=True)
        centre = jnp.sum(wide_weight * mean, axis=1, keepdims=True)
        rstd = lax.rsqrt(spread + norm_eps)
        inverse = jnp.broadcast_to(1.0 / count, (channels, 1))
        pooled[micros + micro] = jnp.concatenate(
            [
                centre, rstd, inverse, jnp.zeros((channels, 13), F32),
                spun, jnp.zeros((channels, 16 - inputs), F32),
                jnp.broadcast_to(mean, (channels, inputs)), jnp.zeros((channels, LANES - 32 - inputs), F32),
            ],
            axis=1,
        )
        bounds.append((centre, rstd * cols[0:channels, 0:1]))
    shift = cols[0:channels, 1:2]
    fetched.wait()
    for micro in range(micros):
        lifted[...] = dot(weight, point_rows[micro, 0:inputs])
        centre, scale = bounds[micro]
        slot, limit = pillar_notes(point_rows, micro, inputs, pillars)
        slot_rows.append(slot)
        top = jnp.full((channels, pillars), -jnp.inf, F32)
        for n in range(depth):
            piece = slice(n * pillars, (n + 1) * pillars)
            normed = (lifted[:, piece] - centre) * scale + shift
            act = normed * sigmoid(normed)
            acts[:, piece] = act
            top = jnp.maximum(top, jnp.where(limit > n, act, -jnp.inf))
        total = jnp.zeros((channels, pillars), F32)
        for n in range(depth):
            piece = slice(n * pillars, (n + 1) * pillars)
            total = total + jnp.where(limit > n, jnp.exp(acts[:, piece] - top), 0.0)
        result = top + jnp.log(total)
        pooled[micro] = result
        parts = [jnp.zeros((channels, pillars), F32)] * micros
        parts[micro] = result.astype(BF16).astype(F32)
        stacked.append(jnp.transpose(jnp.concatenate(parts, axis=0)))
    values = jnp.concatenate(stacked, axis=0).astype(BF16)
    for group in range(3):
        place = lax.broadcasted_iota(jnp.int32, (rows_out, pillars), 0) + (group - 1) * capacity
        chosen = jnp.concatenate(
            [jnp.where(place.astype(F32) == row, 1.0, 0.0) for row in slot_rows], axis=1
        ).astype(BF16)
        send[:, group * LANES : (group + 1) * LANES] = dot(chosen, values).astype(BF16)


def own_stats(ref, first_row, rows, send):
    micros, _, channels, width = ref.shape
    sums, squares = [], []
    for micro in range(micros):
        total = fold(ref[micro, first_row])
        for row in range(first_row + 1, first_row + rows):
            total = total + fold(ref[micro, row])
        sums.append(total * (1.0 / (rows * width)))
    means = [jnp.sum(total, axis=1, keepdims=True) for total in sums]
    for micro in range(micros):
        spread = jnp.zeros(sums[micro].shape, F32)
        for row in range(first_row, first_row + rows):
            away = ref[micro, row] - means[micro]
            spread = spread + fold(away * away)
        squares.append(spread)
    if channels == LANES:
        send_all(send, [row_of(part) for part in sums + squares])
    else:
        send_all(send, [row_of(*sums), row_of(*squares)])


def conv_pair(source, weight, micro, at, channels):
    window = source[micro, at : at + 4].reshape(12 * channels, source.shape[3])
    return dot(weight[...], window)


def conv_rows(source, weight, out, shape):
    micros, high, channels, width = shape
    for micro in range(micros):
        for at in range(0, high, 2):
            both = conv_pair(source, weight, micro, at, channels)
            out[micro, at] = both[:channels].astype(out.dtype)
            out[micro, at + 1] = both[channels:].astype(out.dtype)


def canvas_kernel(found, columns, where_rows, l_first, out, kept, send, canvas, *, rows):
    scenes, high, channels, width = out.shape
    masks = edges(channels, width)
    slots = found.shape[0]
    lane = lax.broadcasted_iota(jnp.int32, (slots, width), 1).astype(F32)
    for group in range(3):
        values = jnp.transpose(found[:, group * LANES : (group + 1) * LANES].astype(F32))
        first, count = ((rows - 2, 2), (0, rows), (0, 2))[group]
        for scene in range(scenes):
            at = 2 * group + scene
            column = columns[:, at : at + 1] - 1.0
            column = column - jnp.floor(column * (1.0 / width)) * width
            row = jnp.floor((where_rows[at : at + 1] - 1.0) * (1.0 / width))
            mine = values[scene * channels : (scene + 1) * channels]
            placed = jnp.concatenate(
                [jnp.where(row == r * 1.0, mine, 0.0) for r in range(first, first + count)], axis=0
            ).astype(BF16)
            chosen = jnp.where(lane == column, 1.0, 0.0).astype(BF16)
            grid = dot(placed, chosen).astype(BF16)
            start = (0, 2, rows + 2)[group]
            for r in range(count):
                row = grid[r * channels : (r + 1) * channels]
                canvas[scene, start + r] = spread(row, masks)
                kept[scene, start + r] = row
    conv_rows(canvas, l_first, out, out.shape)
    own_stats(out, 1, rows, send)


def second_kernel(found, cols, first_out, l_second_in, out, kept, slopes, stats, send, acts, l_second, sems,
                  *, rows, tiles):
    weight_copy = move(l_second_in, l_second, sems, 0)
    micros, high, channels, width = first_out.shape
    tile = lax.axis_index("tile")
    turned = stat_columns(found, float(rows * width))
    stats[...] = turned
    masks = edges(channels, width)
    for micro in range(micros):
        part = slice(micro * channels, (micro + 1) * channels)
        centre = turned[part, 0:1]
        scale = turned[part, 1:2] * cols[0:channels, 2:3]
        shift = cols[0:channels, 3:4]

        for row in range(high):
            normed = (first_out[micro, row] - centre) * scale + shift
            gate = sigmoid(normed)
            act = normed * gate
            slopes[micro, row] = gate + act * (1.0 - gate)
            if row == 0 or row == high - 1:
                act = act * inside(tile, row - 1, (tiles, rows))
            act = act.astype(BF16)
            acts[micro, row] = spread(act, masks)
            kept[micro, row] = act
    weight_copy.wait()
    conv_rows(acts, l_second, out, out.shape)
    own_stats(out, 0, rows, send)


def up_kernel(found, cols, second_out, w_up, acts, upper, slopes, plain, crossed, stats, send, *, rows):
    micros, _, channels, width = second_out.shape
    peers = send.shape[0]
    each = crossed.shape[0] // peers
    turned = stat_columns(found, float(rows * width))
    stats[...] = turned
    gain, shift = cols[0:channels, 4:5], cols[0:channels, 5:6]
    lines = []
    for micro in range(micros):
        part = slice(micro * channels, (micro + 1) * channels)
        centre, rstd = turned[part, 0:1], turned[part, 1:2]
        slope_sum = jnp.zeros((channels, LANES), F32)
        unit_sum = jnp.zeros((channels, LANES), F32)
        for row in range(rows):
            unit = (second_out[micro, row] - centre) * rstd
            normed = unit * gain + shift
            gate = sigmoid(normed)
            act = normed * gate
            slope = gate + act * (1.0 - gate)
            sloped = slope * unit
            slope_sum = slope_sum + fold(slope)
            unit_sum = unit_sum + fold(sloped)
            slopes[micro, row] = jnp.concatenate([slope, sloped], axis=0)
            act = act.astype(BF16)
            acts[micro, row] = act
            upper[micro, row] = dot(w_up[...], act)
        lines.append(row_of(slope_sum, unit_sum).astype(BF16).astype(F32))
        crossed[micro * channels : (micro + 1) * channels] = dot_lanes(
            jnp.concatenate([acts[micro, row] for row in range(rows)], axis=1),
            jnp.concatenate([slopes[micro, row].astype(BF16) for row in range(rows)], axis=1),
        )
    plain[...] = jnp.concatenate(lines, axis=0)
    used = micros * channels
    if crossed.shape[0] > used:
        crossed[used:] = jnp.zeros((crossed.shape[0] - used, LANES), F32)
    if 2 * micros + each < send.shape[1]:
        send[...] = jnp.zeros(send.shape, F32)
    for peer in range(peers):
        send[peer, 2 * micros : 2 * micros + each] = crossed[peer * each : (peer + 1) * each]
    own_stats(upper, 0, rows, send)


def exact_rows(rows):
    high = rows.astype(BF16).astype(F32)
    return [high, rows - high]


def top_kernel(found, cols, upper, cot, slopes, plain, w_up_t, features, grads, mixed, stats, send, *, rows, each):
    micros, _, wide, width = upper.shape
    channels = w_up_t.shape[0]
    lines = []
    for micro in range(micros):
        lines += list(pooled_stats(found[:, micro, :], found[:, micros + micro, :], float(rows * width)))
    turned = columns_of(lines)
    stats[...] = turned
    gain, shift = cols[:, 6:7], cols[:, 7:8]
    gain_rows, shift_rows, mixed_rows = [], [], []
    for micro in range(micros):
        centre, rstd = turned[:, 2 * micro : 2 * micro + 1], turned[:, 2 * micro + 1 : 2 * micro + 2]
        factor = gain * rstd
        gain_sum = jnp.zeros((wide, LANES), F32)
        shift_sum = jnp.zeros((wide, LANES), F32)
        mixed_sum = jnp.zeros((2 * channels, LANES), F32)
        for row in range(rows):
            unit = (upper[micro, row] - centre) * rstd
            normed = unit * gain + shift
            gate = sigmoid(normed)
            act = normed * gate
            grad = cot[micro, row].astype(F32) * (gate + act * (1.0 - gate))
            features[micro, row] = act.astype(BF16)
            grads[micro, row] = grad
            gain_sum = gain_sum + fold(grad * unit)
            shift_sum = shift_sum + fold(grad)
            below = dot(w_up_t[...], (grad * factor).astype(BF16))
            mixed_sum = mixed_sum + fold(
                slopes[micro, row] * jnp.concatenate([below, below], axis=0)
            )
        gain_rows.append(row_of(gain_sum))
        shift_rows.append(row_of(shift_sum))
        mixed_rows.append(row_of(mixed_sum).astype(BF16).astype(F32))
    mixed[...] = jnp.concatenate(mixed_rows, axis=0)
    rows_out = jnp.concatenate(gain_rows + shift_rows, axis=0)
    crossed = jnp.sum(found[:, 2 * micros : 2 * micros + each, :], axis=0)
    rest = send.shape[1] - 6 * micros - each
    block = exact_rows(rows_out) + mixed_rows + [plain[...], crossed]
    if rest > 0:
        block.append(jnp.zeros((rest, LANES), F32))
    block = jnp.concatenate(block, axis=0)
    send[...] = jnp.broadcast_to(block.astype(BF16)[None], send.shape)


def low_rows(turned, value_of, values, stats, gain, low, high, first, rows, tiles):
    micros, _, channels, width = values.shape
    tile = lax.axis_index("tile")
    masks = edges(channels, width)
    for micro in range(micros):
        part = slice(micro * channels, (micro + 1) * channels)
        centre, rstd = stats[part, 0:1], stats[part, 1:2]
        factor = gain * rstd
        slope_part, shift_part = rstd * turned[part, 0:1], turned[part, 1:2]
        for index in range(high):
            grad, value = value_of(micro, index)
            grad = factor * (grad - shift_part - (value - centre) * slope_part)
            if index + first < 0 or index + first >= rows:
                grad = grad * inside(tile, index + first, (tiles, rows))
            low[micro, index] = spread(grad.astype(BF16), masks)


def first_units(first_out, stats, micro, channels):
    part = slice(micro * channels, (micro + 1) * channels)
    centre, rstd = stats[part, 0:1], stats[part, 1:2]
    return lambda row: (first_out[micro, row] - centre) * rstd


def second_sums(total, weight, factors, stats, micro, micros, count):
    channels = weight.shape[1]
    factor, centre = factors[micro], stats[:, 2 * micro : 2 * micro + 1]
    columns = jnp.transpose(jnp.concatenate([total, jnp.zeros((8 - total.shape[0], LANES), F32)], axis=0))
    beta = factor * stats[:, 2 * micro + 1 : 2 * micro + 2] * columns[:, micro : micro + 1] * (1.0 / count)
    alpha = factor * columns[:, micros + micro : micros + micro + 1] * (1.0 / count)
    square = lax.dot_general(
        weight * beta, weight, (((0,), (0,)), ((), ())),
        preferred_element_type=F32, precision=lax.Precision.HIGHEST,
    )
    square = jnp.concatenate([square, square], axis=1)
    line = jnp.sum(weight * (alpha - beta * centre), axis=0, keepdims=True)
    line = jnp.concatenate([line, line], axis=1)

    def give(mixed, plain, crossed):
        mine = crossed[micro * channels : (micro + 1) * channels]
        return mixed - plain * line - jnp.sum(square * mine, axis=0, keepdims=True)

    return give


def middle_back_kernel(
    found, cols, grads, upper, top_stats, second_out, second_stats, slopes, w_up, w_up_t,
    own_mixed, own_plain, own_crossed, second_act, acts, first_out, first_stats, first_slopes, b_second_in,
    out, top_grad, weight_grad, top_gain_grad, top_shift_grad, expected, send,
    low, top_low, extras, second_dz, b_second, sems, *, rows, tiles, each
):
    weight_copy = move(b_second_in, b_second, sems, 0)
    scene = lax.axis_index("scene")
    micros, _, wide, width = grads.shape
    channels = second_out.shape[2]
    peers = found.shape[0]
    count = float(peers * rows * width)
    kept = 2 * micros
    total = jnp.sum(found[...].astype(F32), axis=0)
    mixed, plain = total[2 * kept : 2 * kept + micros], total[2 * kept + micros : 3 * kept]
    total = total[0:kept] + total[kept : 2 * kept]
    crossed = jnp.concatenate(
        [
            found[peer].astype(F32)[3 * kept : 3 * kept + each]
            for peer in range(-(-micros * channels // each))
        ],
        axis=0,
    )
    own_half(total[0:1] + total[1:2], scene, top_gain_grad)
    own_half(total[2:3] + total[3:4], scene, top_shift_grad)
    factors = [cols[:, 6:7] * top_stats[:, 2 * micro + 1 : 2 * micro + 2] for micro in range(micros)]
    wide_weight = w_up[...].astype(F32)
    turned = columns_of([total[index : index + 1] for index in range(2 * micros)]) * (1.0 / count)
    gain = cols[0:channels, 4:5]
    masks = edges(channels, width)
    second_rows = []
    for micro in range(micros):
        top_centre = top_stats[:, 2 * micro : 2 * micro + 1]
        top_slope = top_stats[:, 2 * micro + 1 : 2 * micro + 2] * turned[:, micro : micro + 1]
        top_shift = turned[:, micros + micro : micros + micro + 1]
        part = slice(micro * channels, (micro + 1) * channels)
        centre, rstd = second_stats[part, 0:1], second_stats[part, 1:2]
        gain_sum = jnp.zeros((channels, LANES), F32)
        shift_sum = jnp.zeros((channels, LANES), F32)
        for row in range(rows):
            grad = factors[micro] * (
                grads[micro, row] - top_shift - (upper[micro, row] - top_centre) * top_slope
            )
            grad = grad.astype(BF16)
            top_low[micro, row] = grad
            unit = (second_out[micro, row] - centre) * rstd
            grad = dot(w_up_t[...], grad) * slopes[micro, row, 0:channels]
            second_dz[micro, row] = grad
            shift_sum = shift_sum + fold(grad)
            gain_sum = gain_sum + fold(grad * unit)
        second_rows.append((shift_sum, gain_sum))
    parts = []
    for micro in range(micros):
        give = second_sums(total, wide_weight, factors, top_stats, micro, micros, count)
        whole = give(mixed[micro : micro + 1], plain[micro : micro + 1], crossed)
        extra = row_of(*second_rows[micro]) - give(
            own_mixed[micro : micro + 1], own_plain[micro : micro + 1], own_crossed[...]
        )
        expected[micro : micro + 1] = whole
        extras[micro : micro + 1] = extra
        parts.append(whole * (1.0 / count) + extra * (1.0 / (rows * width)))
    parts = columns_of(parts)
    for micro in range(micros):
        part = slice(micro * channels, (micro + 1) * channels)
        centre, rstd = second_stats[part, 0:1], second_stats[part, 1:2]
        factor = gain * rstd
        shift_part = parts[0:channels, micro : micro + 1]
        slope_part = parts[channels : 2 * channels, micro : micro + 1] * rstd
        for row in range(rows):
            grad = factor * (
                second_dz[micro, row] - shift_part - (second_out[micro, row] - centre) * slope_part
            )
            low[micro, row] = spread(grad.astype(BF16), masks)
    weight_copy.wait()
    first_back(
        low, top_low, second_act, acts, first_out, first_stats, first_slopes, b_second, extras,
        out, top_grad, weight_grad, send, rows, tiles,
    )


def first_back(
    low, top_low, second_act, acts, first_out, first_stats, slopes, b_second, extras,
    out, top_grad, weight_grad, send, rows, tiles
):
    tile = lax.axis_index("tile")
    micros, _, channels, width = first_out.shape
    half = 6 * channels
    gain_sums, shift_sums = [], []
    for micro in range(micros):
        units = first_units(first_out, first_stats, micro, channels)
        gain_sum = jnp.zeros((channels, LANES), F32)
        shift_sum = jnp.zeros((channels, LANES), F32)
        for at in range(0, rows + 2, 2):
            if at == 0:
                parts = dot(b_second[:, half:], low[micro, 0:2].reshape(half, width))
            elif at == rows:
                parts = dot(b_second[:, :half], low[micro, rows - 2 : rows].reshape(half, width))
            else:
                parts = conv_pair(low, b_second, micro, at - 2, channels)
            for j in range(2):
                grad = parts[channels * j : channels * (j + 1)] * slopes[micro, at + j]
                if at + j == 0 or at + j == rows + 1:
                    grad = grad * inside(tile, at + j - 1, (tiles, rows))
                out[micro, at + j] = grad
                gain_sum = gain_sum + fold(grad * units(at + j))
                shift_sum = shift_sum + fold(grad)
        gain_sums.append(gain_sum)
        shift_sums.append(shift_sum)
        product = dot_lanes(
            jnp.concatenate([second_act[micro, row] for row in range(rows)], axis=1),
            jnp.concatenate([top_low[micro, row] for row in range(rows)], axis=1),
        )
        top_grad[...] = product if micro == 0 else top_grad[...] + product
    conv_grad(low, 0, acts, 0, weight_grad, rows)
    send_all(send, [row_of(*gain_sums), row_of(*shift_sums)] + [extras[m : m + 1] for m in range(micros)])


def conv_grad(low, low_first, values, value_first, total, rows):
    micros, _, channels, width = values.shape
    for micro in range(micros):
        grads = jnp.concatenate([low[micro, row + low_first] for row in range(rows)], axis=1)
        windows = jnp.concatenate(
            [
                values[micro, row + value_first : row + value_first + 3].reshape(3 * channels, width)
                for row in range(rows)
            ],
            axis=1,
        )
        product = dot_lanes(grads, windows)
        total[...] = product if micro == 0 else total[...] + product


def half_rows(total, half, scene):
    channels = 2 * half
    start = scene * half
    mine = jnp.concatenate(
        [total[b * channels + start : b * channels + start + half, :] for b in range(2, -1, -1)], axis=0
    )
    wing = mine[:, LANES:]
    cut = wing.shape[0] // 2
    return [mine[:, :LANES], jnp.concatenate([wing[:cut], wing[cut:]], axis=1)]


def pick_kernel(
    found, cols, grads, first_out, first_stats, b_first_in, columns, where_rows,
    canvas, second_grad, top_grad, expected,
    send, gain_grad, shift_grad, second_gain_grad, second_shift_grad, low, grid, b_first, first_grad, whole, sems,
    *, rows, tiles, each
):
    weight_copy = move(b_first_in, b_first, sems, 0)
    scene = lax.axis_index("scene")
    micros, high, channels, width = grads.shape
    sums = sum_rows(found, 2 + micros)
    second = sum(sums[2:]) + jnp.sum(expected[...], axis=0, keepdims=True)
    own_half(second[:, :channels], scene, second_shift_grad)
    own_half(second[:, channels:], scene, second_gain_grad)
    sums = sums[:2]
    own_half(sums[0][:, :channels] + sums[0][:, channels:], scene, gain_grad)
    own_half(sums[1][:, :channels] + sums[1][:, channels:], scene, shift_grad)
    turned = columns_of(sums) * (1.0 / (found.shape[0] * rows * width))
    masks = edges(channels, width)
    for micro in range(micros):
        part = slice(micro * channels, (micro + 1) * channels)
        centre, rstd = first_stats[part, 0:1], first_stats[part, 1:2]
        factor = cols[0:channels, 2:3] * rstd
        slope_part, shift_part = rstd * turned[part, 0:1], turned[part, 1:2]
        for row in range(high):
            grad = grads[micro, row]
            if 1 <= row <= rows:
                grad = grad - shift_part - (first_out[micro, row] - centre) * slope_part
            low[micro, row] = spread((factor * grad).astype(BF16), masks)
    weight_copy.wait()
    half = 6 * channels
    for micro in range(micros):
        for at in range(0, rows + 4, 2):
            if at == 0:
                parts = dot(b_first[:, half:], low[micro, 0:2].reshape(half, width))
            elif at == rows + 2:
                parts = dot(b_first[:, :half], low[micro, rows : rows + 2].reshape(half, width))
            else:
                parts = conv_pair(low, b_first, micro, at - 2, channels)
            grid[micro, at] = parts[:channels].astype(BF16)
            grid[micro, at + 1] = parts[channels:].astype(BF16)
    conv_grad(low, 0, canvas, 0, first_grad, high)
    half = channels // 2
    top = jnp.transpose(top_grad[...])
    for s in range(2):
        parts = half_rows(first_grad, half, s) + half_rows(second_grad, half, s)
        mine = top[s * channels : (s + 1) * channels, :]
        parts.append(jnp.concatenate([mine[:half], mine[half:]], axis=1))
        parts = jnp.concatenate(parts, axis=0)
        whole[s, 0 : parts.shape[0]] = parts
        if whole.shape[1] > parts.shape[0]:
            whole[s, parts.shape[0] :] = jnp.zeros((whole.shape[1] - parts.shape[0], LANES), F32)
    slots = columns.shape[0]
    lane = lax.broadcasted_iota(jnp.int32, (slots, width), 1).astype(F32)
    groups = []
    for group in range(3):
        start, first, count = ((0, rows - 2, 2), (2, 0, rows), (rows + 2, 0, 2))[group]
        picked = []
        for micro in range(micros):
            at = 2 * group + micro
            column = columns[:, at : at + 1] - 1.0
            column = column - jnp.floor(column * (1.0 / width)) * width
            place = jnp.floor((where_rows[at : at + 1] - 1.0) * (1.0 / width))
            chosen = jnp.where(lane == column, 1.0, 0.0).astype(BF16)
            here = dot_lanes(grid[micro, start : start + count].reshape(count * channels, width), chosen)
            total = jnp.zeros((channels, slots), F32)
            for r in range(count):
                total = total + jnp.where(
                    place == (first + r) * 1.0, here[r * channels : (r + 1) * channels], 0.0
                )
            picked.append(total)
        groups.append(jnp.transpose(jnp.concatenate(picked, axis=0)))
    capacity = slots // tiles
    block = send.shape[1]

    def filled(parts):
        missing = block - sum(part.shape[0] for part in parts)
        if missing > 0:
            parts = parts + [jnp.zeros((missing, LANES), F32)]
        return jnp.concatenate(parts, axis=0).astype(BF16)

    for spot in range(tiles):
        mine = slice(spot * capacity, (spot + 1) * capacity)
        send[2 * spot + scene] = filled([picked[mine] for picked in groups])
        send[2 * spot + 1 - scene] = filled([whole[s, spot * each : (spot + 1) * each] for s in range(2)])


def pillar_back_kernel(found, rows_in, w_pillar, cols, pooled, send, grads, lifted, rows, sems,
                       *, capacity, each):
    fetched = move(rows_in, rows, sems, 0)
    micros = rows.shape[0]
    _, channels, pillars = pooled.shape
    stats = pooled.at[micros : 2 * micros]
    inputs = w_pillar.shape[1]
    depth = rows.shape[2] // pillars
    scene = lax.axis_index("scene")
    peers = found.shape[0]
    slot_count = peers // 2 * capacity
    blocks = [found[2 * t + scene].astype(F32) for t in range(peers // 2)]
    before, own, after = [
        jnp.concatenate([block[group * capacity : (group + 1) * capacity] for block in blocks], axis=0)
        for group in range(3)
    ]
    gap = jnp.zeros((capacity, LANES), F32)
    returned = (
        own
        + jnp.concatenate([before[capacity:], gap], axis=0)
        + jnp.concatenate([gap, after[: slot_count - capacity]], axis=0)
    )
    turned = jnp.transpose(returned)
    place = lax.broadcasted_iota(jnp.int32, (slot_count, pillars), 0).astype(F32)
    gain, shift = cols[0:channels, 0:1], cols[0:channels, 1:2]
    gain_sums, shift_sums = [], []
    outer = jnp.zeros((16, channels), F32)
    fetched.wait()
    for micro in range(micros):
        lifted[...] = dot(w_pillar[...], rows[micro, 0:inputs])
        slot, limit = pillar_notes(rows, micro, inputs, pillars)
        chosen = jnp.where(place == slot, 1.0, 0.0).astype(BF16)
        back = dot(turned[micro * channels : (micro + 1) * channels].astype(BF16), chosen)
        centre, rstd = stats[micro, :, 0:1], stats[micro, :, 1:2]
        pool = pooled[micro]
        gain_sum = jnp.zeros((channels, pillars), F32)
        shift_sum = jnp.zeros((channels, pillars), F32)
        for n in range(depth):
            piece = slice(n * pillars, (n + 1) * pillars)
            unit = (lifted[:, piece] - centre) * rstd
            normed = unit * gain + shift
            gate = sigmoid(normed)
            act = normed * gate
            slope = gate + act * (1.0 - gate)
            grad = jnp.where(limit > n, back * jnp.exp(act - pool) * slope, 0.0)
            grads[micro, :, piece] = grad
            gain_sum = gain_sum + grad * unit
            shift_sum = shift_sum + grad
        gain_sums.append(gain_sum)
        shift_sums.append(shift_sum)
        scale = jnp.transpose(jnp.broadcast_to(rstd * gain, (channels, LANES)))[0:1]
        outer = outer + dot_lanes(rows[micro], grads[micro].astype(BF16)) * scale
    exact = jnp.concatenate([row_of(*gain_sums), row_of(*shift_sums)], axis=0)
    lines = [jnp.concatenate([outer[k : k + 1], outer[k + 1 : k + 2]], axis=1) for k in range(0, 10, 2)]
    weights = found[1 - scene].astype(F32)
    for t in range(1, peers // 2):
        weights = weights + found[2 * t + 1 - scene].astype(F32)
    rest = send.shape[2] - 9 - each
    for s in range(2):
        block = exact_rows(exact) + lines + [weights[s * each : (s + 1) * each]]
        if rest > 0:
            block.append(jnp.zeros((rest, LANES), F32))
        block = jnp.concatenate(block, axis=0).astype(BF16)
        send[:, s] = jnp.broadcast_to(block[None], (send.shape[0],) + block.shape)


def points_kernel(
    found, rows_in, grads, w_pillar, cols, pooled,
    points_grad, pillar_grad, gain_grad, shift_grad, first_grad, second_grad, up_grad, rows, lifted, sems,
    *, each
):
    fetched = move(rows_in, rows, sems, 0)
    scene = lax.axis_index("scene")
    micros, channels, _ = grads.shape
    stats = pooled.at[micros : 2 * micros]
    _, _, inputs, depth, pillars = points_grad.shape
    half = channels // 2
    total = jnp.sum(found[...].astype(F32), axis=0)
    total = jnp.concatenate([total[0:2] + total[2:4], total[4:9]], axis=0)
    own_half(total[0:1, :channels] + total[0:1, channels:], scene, gain_grad)
    own_half(total[1:2, :channels] + total[1:2, channels:], scene, shift_grad)
    turned = jnp.transpose(jnp.concatenate([total, jnp.zeros((1, LANES), F32)], axis=0))
    weight_grad = jnp.concatenate(
        [turned[(k % 2) * channels : (k % 2 + 1) * channels, 2 + k // 2 : 3 + k // 2] for k in range(inputs)],
        axis=1,
    )
    weight = jnp.transpose(w_pillar[...].astype(F32)).astype(BF16)
    fetched.wait()
    for micro in range(micros):
        lifted[...] = dot(w_pillar[...], rows[micro, 0:inputs])
        part = slice(micro * channels, (micro + 1) * channels)
        centre, rstd, inverse = stats[micro, :, 0:1], stats[micro, :, 1:2], stats[micro, :, 2:3]
        factor = cols[0:channels, 0:1] * rstd
        gain_part, shift_part = turned[part, 0:1], turned[part, 1:2]
        spun, mean = stats[micro, :, 16 : 16 + inputs], stats[micro, :, 32 : 32 + inputs]
        weight_grad = weight_grad - factor * (shift_part * mean + gain_part * rstd * spun)
        gain_part, shift_part = gain_part * inverse * rstd, shift_part * inverse
        _, limit = pillar_notes(rows, micro, inputs, pillars)
        for n in range(depth):
            piece = slice(n * pillars, (n + 1) * pillars)
            low = factor * (grads[micro, :, piece] - shift_part - (lifted[:, piece] - centre) * gain_part)
            low = jnp.where(limit > n, low, 0.0).astype(BF16)
            points_grad[micro, 0, :, n, :] = dot(weight, low)
    weight_grad = jnp.concatenate([weight_grad, jnp.zeros((channels, LANES - inputs), F32)], axis=1)
    weight_grad = jnp.transpose(weight_grad)[0:inputs]
    pillar_grad[...] = jnp.where(scene == 0, weight_grad[:, :half], weight_grad[:, half:])
    whole = jnp.concatenate(
        [
            (found[2 * t].astype(F32) + found[2 * t + 1].astype(F32))[9 : 9 + each]
            for t in range(found.shape[0] // 2)
        ],
        axis=0,
    )
    for index, out in enumerate((first_grad, second_grad)):
        base = index * 9 * half * channels // LANES
        lead = 3 * half
        mine = whole[base : base + lead]
        wing = whole[base + lead : base + lead + lead // 2]
        wing = jnp.concatenate([wing[:, :channels], wing[:, channels:]], axis=0)
        both = jnp.concatenate([mine, wing], axis=1)
        for a in range(3):
            for b in range(3):
                at = (3 * a + b) * channels
                out[:, at : at + channels] = both[b * half : (b + 1) * half, a * channels : (a + 1) * channels]
    base = 2 * 9 * half * channels // LANES
    top = whole[base : base + half]
    up_grad[...] = jnp.concatenate([top[:, :channels], top[:, channels:]], axis=0)


def swap(blocks, axes):
    return lax.all_to_all(blocks, axes, split_axis=0, concat_axis=0)


def shards(
    points, point_counts, pillar_tile, pillar_cell,
    pillar_weight, pillar_gain, pillar_shift,
    first_weight, first_gain, first_shift,
    second_weight, second_gain, second_shift,
    up_weight, up_gain, up_shift, cotangent,
):
    micros, _, inputs, depth, pillars = points.shape
    channels = up_weight.shape[1]
    upper = cotangent.shape[2]
    rows, width = cotangent.shape[3:]
    tiles = lax.axis_size("tile")
    scenes = lax.axis_size("scene")
    peers = tiles * scenes
    capacity = 2 * pillars // tiles
    slot_count = tiles * capacity
    half = channels // 2

    def vmem(shape, dtype):
        return pltpu.VMEM(shape, dtype)

    def grid(high, dtype=F32, lead=channels):
        return ((micros, high, lead, width), dtype)

    sums = ((peers, 2, LANES), F32)
    sources = (
        pillar_tile, pillar_cell, point_counts, points,
        first_weight, second_weight, up_weight, pillar_weight.T,
        pillar_gain, pillar_shift, first_gain, first_shift, second_gain, second_shift, up_gain, up_shift,
    )
    moments, packed, point_rows = run(
        functools.partial(moments_kernel, capacity=capacity),
        [
            ((tiles, scenes, 4, LANES), F32), ((layout(half, channels)[-1] + 16, LANES), BF16),
            ((micros, 16, depth * pillars), BF16),
        ],
        *sources,
        hbm=range(len(sources)), copies=len(sources), limit=WIDE_LIMIT,
        scratch=[vmem(source.shape, source.dtype) for source in sources]
        + [vmem((inputs * depth, pillars), F32)],
    )
    moments = swap(moments.reshape(peers, 4, LANES), BOTH)
    both = lax.all_gather(packed, "scene")
    taps = ((2 * channels, 12 * channels), BF16)
    w_pillar, cols, l_first, l_second, b_first, b_second, w_up, w_up_t = run(
        functools.partial(unpack_kernel, inputs=inputs),
        [
            ((channels, inputs), BF16), ((LANES, 8), F32), taps, taps + (1,), taps + (1,), taps + (1,),
            ((upper, channels), BF16), ((channels, upper), BF16),
        ],
        both,
        scratch=[vmem(*taps), vmem(*taps), vmem(*taps)], copies=3,
    )
    cot = cotangent[:, 0].transpose(0, 2, 1, 3)

    send, pooled = run(
        functools.partial(pillar_kernel, capacity=capacity),
        [((slot_count, 3 * LANES), BF16), ((2 * micros, channels, pillars), F32)],
        moments, point_rows, w_pillar, cols,
        hbm=(1,), copies=1,
        scratch=[
            vmem((channels, depth * pillars), F32), vmem((channels, depth * pillars), F32),
            vmem((micros, 16, depth * pillars), BF16),
        ],
    )
    arrived = swap(send.reshape(tiles, capacity, 3 * LANES), "tile").reshape(slot_count, 3 * LANES)
    cell_columns, cell_rows = run(
        functools.partial(cells_kernel, capacity=capacity),
        [((slot_count, LANES), F32), ((8, slot_count), F32)],
        moments,
        cost=pl.CostEstimate(flops=10**7, bytes_accessed=10**6, transcendentals=0),
    )
    arrived, cot = lax.optimization_barrier((arrived, cot))

    first_out, canvas, send = run(
        functools.partial(canvas_kernel, rows=rows),
        [grid(rows + 2), grid(rows + 4, BF16), sums],
        arrived, cell_columns, cell_rows, l_first,
        scratch=[vmem(*grid(rows + 4, BF16, 3 * channels))],
    )
    second_out, first_act, first_slopes, first_stats, send = run(
        functools.partial(second_kernel, rows=rows, tiles=tiles),
        [grid(rows), grid(rows + 2, BF16), grid(rows + 2), ((LANES, 8), F32), sums],
        swap(send, BOTH), cols, first_out, l_second,
        hbm=(3,), scratch=[vmem(*grid(rows + 2, BF16, 3 * channels)), vmem(*taps)], copies=1,
    )
    part = -(-micros * channels // peers)
    second_act, up_out, slopes, plain, crossed, second_stats, send = run(
        functools.partial(up_kernel, rows=rows),
        [
            grid(rows, BF16), grid(rows, F32, upper), grid(rows, F32, 2 * channels), ((micros, LANES), F32),
            ((peers * part, LANES), F32), ((LANES, 8), F32), ((peers, -(-(2 * micros + part) // 8) * 8, LANES), F32),
        ],
        swap(send, BOTH), cols, second_out, w_up,
    )
    features, grads, mixed, top_stats, send = run(
        functools.partial(top_kernel, rows=rows, each=part),
        [
            grid(rows, BF16, upper), grid(rows, F32, upper), ((micros, LANES), F32), ((LANES, 8), F32),
            ((peers, -(-(6 * micros + part) // 8) * 8, LANES), BF16),
        ],
        swap(send, BOTH), cols, up_out, cot, slopes, plain, w_up_t,
    )
    features = with_layout_constraint(features.transpose(0, 2, 1, 3)[:, None], Layout((0, 1, 2, 3, 4)))
    features, send = lax.optimization_barrier((features, send))
    vector, top_vector, matrix = ((half,), F32), ((upper // 2,), F32), ((half, 9 * channels), F32)
    cross = ((3 * channels, 3 * channels), F32)
    first_dz, top_grad, second_cross, up_gain_grad, up_shift_grad, expected, send = run(
        functools.partial(middle_back_kernel, rows=rows, tiles=tiles, each=part),
        [
            grid(rows + 2), ((channels, upper), F32), cross, top_vector, top_vector, ((micros, LANES), F32),
            ((peers, 2 + micros, LANES), F32),
        ],
        swap(send, BOTH), cols, grads, up_out, top_stats, second_out, second_stats, slopes, w_up, w_up_t,
        mixed, plain, crossed, second_act, first_act, first_out, first_stats, first_slopes, b_second,
        hbm=(18,),
        scratch=[
            vmem(*grid(rows, BF16, 3 * channels)), vmem(*grid(rows, BF16, upper)), vmem((micros, LANES), F32),
            vmem(*grid(rows)), vmem(*taps),
        ],
        copies=1,
    )
    length = (2 * 9 * half * channels + upper * half) // LANES
    each = -(-length // tiles)
    block = -(-max(3 * capacity, 2 * each) // 8) * 8
    send, first_gain_grad, first_shift_grad, second_gain_grad, second_shift_grad = run(
        functools.partial(pick_kernel, rows=rows, tiles=tiles, each=each),
        [((peers, block, LANES), BF16), vector, vector, vector, vector],
        swap(send, BOTH), cols, first_dz, first_out, first_stats, b_first, cell_columns, cell_rows,
        canvas, second_cross, top_grad, expected,
        hbm=(5,),
        scratch=[
            vmem(*grid(rows + 2, BF16, 3 * channels)), vmem(*grid(rows + 4, BF16)), vmem(*taps), vmem(*cross),
            vmem((scenes, tiles * each, LANES), F32),
        ],
        copies=1,
    )
    block = -(-(9 + each) // 8) * 8
    send, pillar_dz = run(
        functools.partial(pillar_back_kernel, capacity=capacity, each=each),
        [((tiles, scenes, block, LANES), BF16), ((micros, channels, depth * pillars), F32)],
        swap(send, BOTH), point_rows, w_pillar, cols, pooled,
        hbm=(1,),
        scratch=[vmem((channels, depth * pillars), F32), vmem((micros, 16, depth * pillars), BF16)],
        copies=1,
    )
    points_grad, pillar_grad, pillar_gain_grad, pillar_shift_grad, first_grad, second_grad, up_grad = run(
        functools.partial(points_kernel, each=each),
        [
            ((micros, 1, inputs, depth, pillars), F32), ((inputs, half), F32), vector, vector,
            matrix, matrix, ((upper // 2, channels), F32),
        ],
        swap(send.reshape(peers, block, LANES), BOTH), point_rows, pillar_dz, w_pillar, cols, pooled,
        hbm=(1,),
        scratch=[vmem((micros, 16, depth * pillars), BF16), vmem((channels, depth * pillars), F32)],
        copies=1,
    )
    return (
        features, points_grad,
        pillar_grad.T, pillar_gain_grad, pillar_shift_grad,
        first_grad, first_gain_grad, first_shift_grad,
        second_grad, second_gain_grad, second_shift_grad,
        up_grad, up_gain_grad, up_shift_grad,
    )


def solution(mesh):
    matrix, vector = P("scene", None), P("scene")
    grid = P(None, "scene", None, "tile", None)
    cloud = P(None, "scene", None, None, "tile")
    pillar = P(None, "scene", "tile")
    weights = (matrix, vector, vector) * 4
    return jax.shard_map(
        shards,
        mesh=mesh,
        in_specs=(cloud, pillar, pillar, pillar) + weights + (grid,),
        out_specs=(grid, cloud) + weights,
        check_vma=False,
    )
```

```python
import functools

import jax
import jax.numpy as jnp
from jax import lax
from jax.experimental import pallas as pl
from jax.experimental.pallas import tpu as pltpu
from jax.sharding import PartitionSpec as P

norm_eps = 0.001
BOTH = ("tile", "scene")
F32 = jnp.float32
BF16 = jnp.bfloat16
VMEM_LIMIT = 24 * 1024 * 1024
WIDE_LIMIT = 60 * 1024 * 1024
LANES = 128


def run(kernel, outs, *args, hbm=(), scratch=(), copies=0, cost=None, limit=VMEM_LIMIT):
    specs = [
        pl.BlockSpec(memory_space=pltpu.HBM if index in hbm else pltpu.VMEM) for index in range(len(args))
    ]
    scratch = list(scratch)
    if copies:
        scratch.append(pltpu.SemaphoreType.DMA((copies,)))
    return pl.pallas_call(
        kernel,
        out_shape=[jax.ShapeDtypeStruct(out[0], out[1]) for out in outs],
        in_specs=specs,
        out_specs=[
            pl.BlockSpec(memory_space=pltpu.HBM if len(out) > 2 else pltpu.VMEM) for out in outs
        ],
        scratch_shapes=scratch,
        compiler_params=pltpu.CompilerParams(vmem_limit_bytes=limit),
        cost_estimate=cost,
    )(*args)


def move(source, target, sems, index):
    copy = pltpu.make_async_copy(source, target, sems.at[index])
    copy.start()
    return copy


def dot(left, right, precision=None):
    return jnp.dot(left, right, preferred_element_type=F32, precision=precision)


def dot_lanes(left, right, precision=None):
    return lax.dot_general(
        left, right, (((1,), (1,)), ((), ())), preferred_element_type=F32, precision=precision
    )


def sigmoid(values):
    return 0.5 + 0.5 * jnp.tanh(0.5 * values)


def fold(values):
    total = values[:, :LANES]
    for start in range(LANES, values.shape[1], LANES):
        total = total + values[:, start : start + LANES]
    return total


def row_of(left, right=None):
    both = left if right is None else jnp.concatenate([left, right], axis=0)
    return jnp.sum(jnp.transpose(both), axis=0, keepdims=True)


def columns_of(rows):
    rows = rows + [jnp.zeros((8 - len(rows), LANES), F32)] if len(rows) < 8 else rows
    return jnp.transpose(jnp.concatenate(rows, axis=0))


def inside(tile, row, height):
    tiles, rows = height
    place = tile * rows + row
    return jnp.where((place >= 0) & (place < tiles * rows), 1.0, 0.0).astype(F32)


def send_all(ref, rows):
    for index, row in enumerate(rows):
        ref[:, index : index + 1, :] = jnp.broadcast_to(row[None], (ref.shape[0], 1, LANES))


def pooled_stats(means, squares, count):
    peers = means.shape[0]
    mean = jnp.sum(means, axis=0, keepdims=True) * (1.0 / peers)
    away = means - mean
    spread = jnp.sum(squares + count * away * away, axis=0, keepdims=True) * (1.0 / (peers * count))
    return mean, lax.rsqrt(spread + norm_eps)


def stat_columns(found, count):
    return columns_of(list(pooled_stats(found[:, 0, :], found[:, 1, :], count)))


def sum_rows(found, lines):
    return [jnp.sum(found[:, index, :], axis=0, keepdims=True) for index in range(lines)]


def own_half(row, scene, out):
    size = out.shape[0]
    out[...] = jnp.where(scene == 0, row[:, 0:size], row[:, size : 2 * size]).reshape(size)


def edges(channels, width):
    lane = lax.broadcasted_iota(jnp.int32, (channels, width), 1)
    return lane > 0, lane < width - 1


def spread(row, masks):
    zero = jnp.zeros_like(row)
    left = jnp.where(masks[0], pltpu.roll(row, 1, 1), zero)
    right = jnp.where(masks[1], pltpu.roll(row, row.shape[1] - 1, 1), zero)
    return jnp.concatenate([left, row, right], axis=0)


def layout(half, channels):
    first = 0
    second = first + half * -(-9 * channels // LANES)
    up = second + half * -(-9 * channels // LANES)
    vectors = up + channels
    return first, second, up, vectors, vectors + 16


def widen(value):
    missing = LANES - value.shape[1]
    if missing == 0:
        return value
    return jnp.concatenate([value, jnp.zeros((value.shape[0], missing), value.dtype)], axis=1)


def pack(held, out):
    first, second, up, pillar = held[:4]
    half, channels = first.shape[0], up.shape[1]
    starts = layout(half, channels)
    for ref, start in ((first, starts[0]), (second, starts[1])):
        for j in range(-(-9 * channels // LANES)):
            out[start + j * half : start + (j + 1) * half, :] = widen(
                ref[:, j * LANES : min((j + 1) * LANES, 9 * channels)]
            )
    out[starts[2] : starts[2] + channels, :] = widen(up[...])
    rows = [vector[...].astype(F32).reshape(1, -1) for vector in held[4:]]
    rows = [widen(row) for row in rows] + [jnp.zeros((16 - len(rows), LANES), F32)]
    turned = widen(pillar[...].astype(F32))
    rows += [turned, jnp.zeros((16 - turned.shape[0], LANES), F32)]
    out[starts[3] :, :] = jnp.concatenate(rows, axis=0).astype(BF16)


def unpack_kernel(
    both, w_pillar, cols, l_first, l_second, b_first, b_second, w_up, w_up_t,
    h_second, h_first_back, h_second_back, sems, *, inputs
):
    half = w_pillar.shape[0] // 2
    channels = 2 * half
    starts = layout(half, channels)
    tiles = -(-9 * channels // LANES)

    def wide(start):
        return jnp.concatenate(
            [
                jnp.concatenate(
                    [both[s, start + j * half : start + (j + 1) * half, :] for j in range(tiles)], axis=1
                )
                for s in range(2)
            ],
            axis=0,
        ).astype(F32)

    up = jnp.concatenate(
        [both[s, starts[2] : starts[2] + channels, 0:channels] for s in range(2)], axis=0
    )
    w_up[...] = up
    w_up_t[...] = jnp.transpose(up.astype(F32)).astype(BF16)
    turned = jnp.concatenate(
        [both[s, starts[4] : starts[4] + 16, 0:half].astype(F32) for s in range(2)], axis=1
    )
    w_pillar[...] = jnp.transpose(widen(turned))[0:channels, 0:inputs].astype(BF16)
    vectors = [both[s, starts[3] : starts[3] + 16, :].astype(F32) for s in range(2)]
    rows = []
    for index in range(8):
        size = half if index < 6 else channels
        row = jnp.concatenate([vectors[s][index : index + 1, 0:size] for s in range(2)], axis=1)
        rows.append(jnp.concatenate([row] * (LANES // (2 * size)), axis=1))
    cols[...] = columns_of(rows)
    zero = jnp.zeros((channels, 3 * channels), F32)
    copies = []
    for weight, ahead, back in (
        (wide(starts[0]), l_first, h_first_back), (wide(starts[1]), h_second, h_second_back)
    ):
        weight = weight[:, : 9 * channels]
        turned = jnp.transpose(weight)
        flipped = jnp.concatenate(
            [turned[tap * channels : (tap + 1) * channels] for tap in range(8, -1, -1)], axis=1
        )
        for ref, taps in ((ahead, weight), (back, flipped)):
            ref[0:channels, :] = jnp.concatenate([taps, zero], axis=1).astype(BF16)
            ref[channels : 2 * channels, :] = jnp.concatenate([zero, taps], axis=1).astype(BF16)
    copies.append(move(h_second, l_second, sems, 0))
    copies.append(move(h_first_back, b_first, sems, 1))
    copies.append(move(h_second_back, b_second, sems, 2))
    for copy in copies:
        copy.wait()


def slot_line(wide, depth, inputs):
    return jnp.concatenate([wide[pl.ds(n, inputs, stride=depth), :] for n in range(depth)], axis=1)


def slot_mask(count, depth):
    return jnp.concatenate([jnp.where(count > n, 1.0, 0.0) for n in range(depth)], axis=1)


def ranks(tile):
    pillars = tile.shape[1]
    across = jnp.broadcast_to(tile, (pillars, pillars))
    down = jnp.transpose(across)
    row = lax.broadcasted_iota(jnp.int32, (pillars, pillars), 0)
    col = lax.broadcasted_iota(jnp.int32, (pillars, pillars), 1)
    return jnp.sum(jnp.where((across == down) & (row < col), 1.0, 0.0), axis=0, keepdims=True)


def moments_kernel(*refs, capacity):
    number = 16
    sources, out, packed, lines_out = refs[:number], *refs[number : number + 3]
    held, wide, sems = refs[number + 3 : 2 * number + 3], refs[-2], refs[-1]
    copies = [move(sources[i], held[i], sems, i) for i in range(number)]
    tiles, cells, counts, points = held[:4]
    micros, _, inputs, depth, pillars = points.shape
    peers, scenes = out.shape[:2]
    copies[0].wait()
    copies[1].wait()
    lines, slot_rows = [], []
    for micro in range(micros):
        tile = tiles[micro].astype(F32)
        cell = (cells[micro] + 1).astype(F32)
        high = jnp.floor(cell * (1.0 / 16.0))
        low = cell - high * 16.0
        rank = ranks(tile)
        slot_rows.append(tile * capacity + rank)
        spot = lax.broadcasted_iota(jnp.int32, (capacity, pillars), 0).astype(F32)
        placed = jnp.where(spot == rank, 1.0, 0.0).astype(BF16)
        peer = lax.broadcasted_iota(jnp.int32, (peers, pillars), 0).astype(F32)
        for group in range(3):
            named = tile == peer + (group - 1.0)
            lines.append(
                16.0 * dot_lanes(jnp.where(named, high, 0.0).astype(BF16), placed)
                + dot_lanes(jnp.where(named, low, 0.0).astype(BF16), placed)
            )
    used = 3 * micros * capacity
    line = jnp.concatenate(lines + [jnp.zeros((peers, LANES - used), F32)], axis=1).reshape(peers, 1, LANES)
    for scene in range(scenes):
        out[:, scene, micros : micros + 1, :] = line
    copies[2].wait()
    copies[3].wait()
    parts, mean_rows, totals = [], [], []
    for micro in range(micros):
        wide[...] = points[micro, 0].astype(F32).reshape(inputs * depth, pillars)
        rows = slot_line(wide, depth, inputs)
        notes = jnp.concatenate([slot_rows[micro], counts[micro].astype(F32)], axis=0)
        notes = jnp.concatenate([notes, jnp.zeros((2, rows.shape[1] - pillars), F32)], axis=1)
        lines_out[micro] = jnp.concatenate(
            [rows, notes, jnp.zeros((14 - inputs, rows.shape[1]), F32)], axis=0
        ).astype(BF16)
        mask = slot_mask(counts[micro], depth)
        total = jnp.sum(mask, axis=1, keepdims=True)
        mean = jnp.sum(rows * mask, axis=1, keepdims=True) / total
        centred = jnp.concatenate(
            [(rows - mean) * mask, jnp.zeros((16 - inputs, rows.shape[1]), F32)], axis=0
        )
        high = centred.astype(BF16)
        parts += [high, (centred - high.astype(F32)).astype(BF16)]
        lane = lax.broadcasted_iota(jnp.int32, (inputs, inputs), 1)
        diagonal = lax.broadcasted_iota(jnp.int32, (inputs, inputs), 0) == lane
        mean_rows.append(jnp.sum(jnp.where(diagonal, mean, 0.0), axis=0, keepdims=True))
        totals.append(total)
    parts = jnp.concatenate(parts, axis=0)
    every = dot_lanes(parts, parts)
    for micro in range(micros):
        at = 32 * micro
        square = every[at : at + 32, at : at + 32]
        products = (
            square[0:inputs, 0:inputs] + square[16 : 16 + inputs, 0:inputs]
            + square[0:inputs, 16 : 16 + inputs] + square[16 : 16 + inputs, 16 : 16 + inputs]
        )
        row = jnp.concatenate(
            [products[k : k + 1] for k in range(inputs)]
            + [mean_rows[micro], totals[micro], jnp.zeros((1, LANES - inputs * inputs - inputs - 1), F32)],
            axis=1,
        )
        for scene in range(scenes):
            out[:, scene, micro : micro + 1, :] = jnp.broadcast_to(row[None], (peers, 1, LANES))
    for copy in copies[4:]:
        copy.wait()
    pack(held[4:], packed)


def cells_kernel(found, columns, rows, *, capacity):
    scene = lax.axis_index("scene")
    slots = columns.shape[0]
    peers = found.shape[0]
    values = found[:, 2, :]
    slot = lax.broadcasted_iota(jnp.int32, (slots, peers), 0)
    peer = lax.broadcasted_iota(jnp.int32, (slots, peers), 1)
    lane = lax.broadcasted_iota(jnp.int32, (slots, LANES), 1)
    row = lax.broadcasted_iota(jnp.int32, (slots, LANES), 0)
    result = jnp.zeros((slots, LANES), F32)
    chosen = jnp.where(peer == 2 * (slot // capacity) + scene, 1.0, 0.0)
    spread = dot(chosen, values, lax.Precision.HIGHEST)
    for micro in range(2):
        for group in range(3):
            mine = jnp.where(lane == (3 * micro + group) * capacity + row % capacity, spread, 0.0)
            column = jnp.sum(mine, axis=1, keepdims=True)
            result = jnp.where(lane == 2 * group + micro, column, result)
    columns[...] = result
    rows[...] = jnp.transpose(result)[0:8]


def pillar_notes(rows, micro, inputs, pillars):
    notes = rows[micro, :, 0:pillars].astype(F32)
    return notes[inputs : inputs + 1], notes[inputs + 1 : inputs + 2]


def pillar_kernel(
    found, point_rows, w_pillar, cols, send, pooled, lifted, acts, *, capacity
):
    micros = point_rows.shape[0]
    channels, inputs = w_pillar.shape
    pillars = pooled.shape[2]
    depth = point_rows.shape[2] // pillars
    weight = w_pillar[...]
    wide_weight = weight.astype(F32)
    rows_out = send.shape[0]
    square = inputs * inputs
    stacked, slot_rows = [], []
    for micro in range(micros):
        lifted[...] = dot(weight, point_rows[micro, 0:inputs])
        moments = found[:, micro, :]
        sizes = moments[:, square + inputs : square + inputs + 1]
        means = moments[:, square : square + inputs]
        count = jnp.sum(sizes, axis=0, keepdims=True)
        mean = jnp.sum(means * sizes, axis=0, keepdims=True) / count
        away = means - mean
        products = lax.dot_general(
            away * sizes, away, (((0,), (0,)), ((), ())),
            preferred_element_type=F32, precision=lax.Precision.HIGHEST,
        )
        summed = jnp.sum(moments, axis=0, keepdims=True)
        products = products + jnp.concatenate(
            [summed[:, k * inputs : (k + 1) * inputs] for k in range(inputs)], axis=0
        )
        cov = products / count
        spun = wide_weight[:, 0:1] * cov[0:1]
        for k in range(1, inputs):
            spun = spun + wide_weight[:, k : k + 1] * cov[k : k + 1]
        spread = jnp.sum(spun * wide_weight, axis=1, keepdims=True)
        centre = jnp.sum(wide_weight * mean, axis=1, keepdims=True)
        rstd = lax.rsqrt(spread + norm_eps)
        inverse = jnp.broadcast_to(1.0 / count, (channels, 1))
        pooled[micros + micro] = jnp.concatenate(
            [
                centre, rstd, inverse, jnp.zeros((channels, 13), F32),
                spun, jnp.zeros((channels, 16 - inputs), F32),
                jnp.broadcast_to(mean, (channels, inputs)), jnp.zeros((channels, LANES - 32 - inputs), F32),
            ],
            axis=1,
        )
        scale = rstd * cols[0:channels, 0:1]
        shift = cols[0:channels, 1:2]
        slot, limit = pillar_notes(point_rows, micro, inputs, pillars)
        slot_rows.append(slot)
        top = jnp.full((channels, pillars), -jnp.inf, F32)
        for n in range(depth):
            piece = slice(n * pillars, (n + 1) * pillars)
            normed = (lifted[:, piece] - centre) * scale + shift
            act = normed * sigmoid(normed)
            acts[:, piece] = act
            top = jnp.maximum(top, jnp.where(limit > n, act, -jnp.inf))
        total = jnp.zeros((channels, pillars), F32)
        for n in range(depth):
            piece = slice(n * pillars, (n + 1) * pillars)
            total = total + jnp.where(limit > n, jnp.exp(acts[:, piece] - top), 0.0)
        result = top + jnp.log(total)
        pooled[micro] = result
        parts = [jnp.zeros((channels, pillars), F32)] * micros
        parts[micro] = result.astype(BF16).astype(F32)
        stacked.append(jnp.transpose(jnp.concatenate(parts, axis=0)))
    values = jnp.concatenate(stacked, axis=0).astype(BF16)
    for group in range(3):
        place = lax.broadcasted_iota(jnp.int32, (rows_out, pillars), 0) + (group - 1) * capacity
        chosen = jnp.concatenate(
            [jnp.where(place.astype(F32) == row, 1.0, 0.0) for row in slot_rows], axis=1
        ).astype(BF16)
        send[:, group * LANES : (group + 1) * LANES] = dot(chosen, values).astype(BF16)


def own_stats(ref, first_row, rows, send):
    micros, _, channels, width = ref.shape
    sums, squares = [], []
    for micro in range(micros):
        total = fold(ref[micro, first_row])
        for row in range(first_row + 1, first_row + rows):
            total = total + fold(ref[micro, row])
        sums.append(total * (1.0 / (rows * width)))
    means = [jnp.sum(total, axis=1, keepdims=True) for total in sums]
    for micro in range(micros):
        spread = jnp.zeros(sums[micro].shape, F32)
        for row in range(first_row, first_row + rows):
            away = ref[micro, row] - means[micro]
            spread = spread + fold(away * away)
        squares.append(spread)
    if channels == LANES:
        send_all(send, [row_of(part) for part in sums + squares])
    else:
        send_all(send, [row_of(*sums), row_of(*squares)])


def conv_pair(source, weight, micro, at, channels):
    window = source[micro, at : at + 4].reshape(12 * channels, source.shape[3])
    return dot(weight[...], window)


def conv_rows(source, weight, out, shape):
    micros, high, channels, width = shape
    for micro in range(micros):
        for at in range(0, high, 2):
            both = conv_pair(source, weight, micro, at, channels)
            out[micro, at] = both[:channels].astype(out.dtype)
            out[micro, at + 1] = both[channels:].astype(out.dtype)


def canvas_kernel(found, columns, where_rows, l_first, out, kept, choices, send, canvas, *, rows):
    scenes, high, channels, width = out.shape
    masks = edges(channels, width)
    slots = found.shape[0]
    lane = lax.broadcasted_iota(jnp.int32, (slots, width), 1).astype(F32)
    for group in range(3):
        values = jnp.transpose(found[:, group * LANES : (group + 1) * LANES].astype(F32))
        first, count = ((rows - 2, 2), (0, rows), (0, 2))[group]
        for scene in range(scenes):
            at = 2 * group + scene
            column = columns[:, at : at + 1] - 1.0
            column = column - jnp.floor(column * (1.0 / width)) * width
            row = jnp.floor((where_rows[at : at + 1] - 1.0) * (1.0 / width))
            mine = values[scene * channels : (scene + 1) * channels]
            placed = jnp.concatenate(
                [jnp.where(row == r * 1.0, mine, 0.0) for r in range(first, first + count)], axis=0
            ).astype(BF16)
            chosen = jnp.where(lane == column, 1.0, 0.0).astype(BF16)
            choices[at] = chosen
            grid = dot(placed, chosen).astype(BF16)
            start = (0, 2, rows + 2)[group]
            for r in range(count):
                row = grid[r * channels : (r + 1) * channels]
                canvas[scene, start + r] = spread(row, masks)
                kept[scene, start + r] = row
    conv_rows(canvas, l_first, out, out.shape)
    own_stats(out, 1, rows, send)


def second_kernel(found, cols, first_out, l_second_in, out, kept, slopes, stats, send, acts, l_second, sems,
                  *, rows, tiles):
    weight_copy = move(l_second_in, l_second, sems, 0)
    micros, high, channels, width = first_out.shape
    tile = lax.axis_index("tile")
    turned = stat_columns(found, float(rows * width))
    stats[...] = turned
    masks = edges(channels, width)
    for micro in range(micros):
        part = slice(micro * channels, (micro + 1) * channels)
        centre = turned[part, 0:1]
        scale = turned[part, 1:2] * cols[0:channels, 2:3]
        shift = cols[0:channels, 3:4]

        for row in range(high):
            normed = (first_out[micro, row] - centre) * scale + shift
            gate = sigmoid(normed)
            act = normed * gate
            slopes[micro, row] = gate + act * (1.0 - gate)
            if row == 0 or row == high - 1:
                act = act * inside(tile, row - 1, (tiles, rows))
            act = act.astype(BF16)
            acts[micro, row] = spread(act, masks)
            kept[micro, row] = act
    weight_copy.wait()
    conv_rows(acts, l_second, out, out.shape)
    own_stats(out, 0, rows, send)


def up_kernel(found, cols, second_out, w_up, acts, upper, slopes, plain, crossed, stats, send, *, rows):
    micros, _, channels, width = second_out.shape
    peers = send.shape[0]
    each = crossed.shape[0] // peers
    turned = stat_columns(found, float(rows * width))
    stats[...] = turned
    gain, shift = cols[0:channels, 4:5], cols[0:channels, 5:6]
    lines = []
    for micro in range(micros):
        part = slice(micro * channels, (micro + 1) * channels)
        centre, rstd = turned[part, 0:1], turned[part, 1:2]
        slope_sum = jnp.zeros((channels, LANES), F32)
        unit_sum = jnp.zeros((channels, LANES), F32)
        for row in range(rows):
            unit = (second_out[micro, row] - centre) * rstd
            normed = unit * gain + shift
            gate = sigmoid(normed)
            act = normed * gate
            slope = gate + act * (1.0 - gate)
            sloped = slope * unit
            slope_sum = slope_sum + fold(slope)
            unit_sum = unit_sum + fold(sloped)
            slopes[micro, row] = jnp.concatenate([slope, sloped], axis=0)
            act = act.astype(BF16)
            acts[micro, row] = act
            upper[micro, row] = dot(w_up[...], act)
        lines.append(row_of(slope_sum, unit_sum).astype(BF16).astype(F32))
        crossed[micro * channels : (micro + 1) * channels] = dot_lanes(
            jnp.concatenate([acts[micro, row] for row in range(rows)], axis=1),
            jnp.concatenate([slopes[micro, row].astype(BF16) for row in range(rows)], axis=1),
        )
    plain[...] = jnp.concatenate(lines, axis=0)
    used = micros * channels
    if crossed.shape[0] > used:
        crossed[used:] = jnp.zeros((crossed.shape[0] - used, LANES), F32)
    if 2 * micros + each < send.shape[1]:
        send[...] = jnp.zeros(send.shape, F32)
    for peer in range(peers):
        send[peer, 2 * micros : 2 * micros + each] = crossed[peer * each : (peer + 1) * each]
    own_stats(upper, 0, rows, send)


def exact_rows(rows):
    high = rows.astype(BF16).astype(F32)
    return [high, rows - high]


def top_kernel(
    found, cols, upper, cot, slopes, plain, w_up_t, features, grads, mixed, stats, send, ordered, *, rows, each
):
    micros, _, wide, width = upper.shape
    channels = w_up_t.shape[0]
    lines = []
    for micro in range(micros):
        lines += list(pooled_stats(found[:, micro, :], found[:, micros + micro, :], float(rows * width)))
    turned = columns_of(lines)
    stats[...] = turned
    gain, shift = cols[:, 6:7], cols[:, 7:8]
    gain_rows, shift_rows, mixed_rows = [], [], []
    for micro in range(micros):
        centre, rstd = turned[:, 2 * micro : 2 * micro + 1], turned[:, 2 * micro + 1 : 2 * micro + 2]
        factor = gain * rstd
        gain_sum = jnp.zeros((wide, LANES), F32)
        shift_sum = jnp.zeros((wide, LANES), F32)
        mixed_sum = jnp.zeros((2 * channels, LANES), F32)
        for row in range(rows):
            unit = (upper[micro, row] - centre) * rstd
            normed = unit * gain + shift
            gate = sigmoid(normed)
            act = normed * gate
            grad = cot[micro, row].astype(F32) * (gate + act * (1.0 - gate))
            for j in range(width // LANES):
                ordered[micro, j, pl.ds(row, wide, stride=rows), :] = act[:, j * LANES : (j + 1) * LANES]
            grads[micro, row] = grad
            gain_sum = gain_sum + fold(grad * unit)
            shift_sum = shift_sum + fold(grad)
            below = dot(w_up_t[...], (grad * factor).astype(BF16))
            mixed_sum = mixed_sum + fold(
                slopes[micro, row] * jnp.concatenate([below, below], axis=0)
            )
        gain_rows.append(row_of(gain_sum))
        shift_rows.append(row_of(shift_sum))
        mixed_rows.append(row_of(mixed_sum).astype(BF16).astype(F32))
        line = jnp.concatenate([ordered[micro, j].astype(BF16) for j in range(width // LANES)], axis=1)
        features[micro, 0] = line.reshape(wide, rows, width)
    mixed[...] = jnp.concatenate(mixed_rows, axis=0)
    rows_out = jnp.concatenate(gain_rows + shift_rows, axis=0)
    crossed = jnp.sum(found[:, 2 * micros : 2 * micros + each, :], axis=0)
    rest = send.shape[1] - 6 * micros - each
    block = exact_rows(rows_out) + mixed_rows + [plain[...], crossed]
    if rest > 0:
        block.append(jnp.zeros((rest, LANES), F32))
    block = jnp.concatenate(block, axis=0)
    send[...] = jnp.broadcast_to(block.astype(BF16)[None], send.shape)


def low_rows(turned, value_of, values, stats, gain, low, high, first, rows, tiles):
    micros, _, channels, width = values.shape
    tile = lax.axis_index("tile")
    masks = edges(channels, width)
    for micro in range(micros):
        part = slice(micro * channels, (micro + 1) * channels)
        centre, rstd = stats[part, 0:1], stats[part, 1:2]
        factor = gain * rstd
        slope_part, shift_part = rstd * turned[part, 0:1], turned[part, 1:2]
        for index in range(high):
            grad, value = value_of(micro, index)
            grad = factor * (grad - shift_part - (value - centre) * slope_part)
            if index + first < 0 or index + first >= rows:
                grad = grad * inside(tile, index + first, (tiles, rows))
            low[micro, index] = spread(grad.astype(BF16), masks)


def first_units(first_out, stats, micro, channels):
    part = slice(micro * channels, (micro + 1) * channels)
    centre, rstd = stats[part, 0:1], stats[part, 1:2]
    return lambda row: (first_out[micro, row] - centre) * rstd


def second_sums(total, weight, factors, stats, micro, micros, count):
    channels = weight.shape[1]
    factor, centre = factors[micro], stats[:, 2 * micro : 2 * micro + 1]
    columns = jnp.transpose(jnp.concatenate([total, jnp.zeros((8 - total.shape[0], LANES), F32)], axis=0))
    beta = factor * stats[:, 2 * micro + 1 : 2 * micro + 2] * columns[:, micro : micro + 1] * (1.0 / count)
    alpha = factor * columns[:, micros + micro : micros + micro + 1] * (1.0 / count)
    square = lax.dot_general(
        weight * beta, weight, (((0,), (0,)), ((), ())),
        preferred_element_type=F32, precision=lax.Precision.HIGHEST,
    )
    square = jnp.concatenate([square, square], axis=1)
    line = jnp.sum(weight * (alpha - beta * centre), axis=0, keepdims=True)
    line = jnp.concatenate([line, line], axis=1)

    def give(mixed, plain, crossed):
        mine = crossed[micro * channels : (micro + 1) * channels]
        return mixed - plain * line - jnp.sum(square * mine, axis=0, keepdims=True)

    return give


def middle_back_kernel(
    found, cols, grads, upper, top_stats, second_out, second_stats, slopes, w_up, w_up_t,
    own_mixed, own_plain, own_crossed, second_act, acts, first_out, first_stats, first_slopes, b_second_in,
    out, top_grad, weight_grad, top_gain_grad, top_shift_grad, expected, send,
    low, top_low, extras, second_dz, b_second, sems, *, rows, tiles, each
):
    weight_copy = move(b_second_in, b_second, sems, 0)
    scene = lax.axis_index("scene")
    micros, _, wide, width = grads.shape
    channels = second_out.shape[2]
    peers = found.shape[0]
    count = float(peers * rows * width)
    kept = 2 * micros
    total = jnp.sum(found[...].astype(F32), axis=0)
    mixed, plain = total[2 * kept : 2 * kept + micros], total[2 * kept + micros : 3 * kept]
    total = total[0:kept] + total[kept : 2 * kept]
    crossed = jnp.concatenate(
        [
            found[peer].astype(F32)[3 * kept : 3 * kept + each]
            for peer in range(-(-micros * channels // each))
        ],
        axis=0,
    )
    own_half(total[0:1] + total[1:2], scene, top_gain_grad)
    own_half(total[2:3] + total[3:4], scene, top_shift_grad)
    factors = [cols[:, 6:7] * top_stats[:, 2 * micro + 1 : 2 * micro + 2] for micro in range(micros)]
    wide_weight = w_up[...].astype(F32)
    turned = columns_of([total[index : index + 1] for index in range(2 * micros)]) * (1.0 / count)
    gain = cols[0:channels, 4:5]
    masks = edges(channels, width)
    second_rows = []
    for micro in range(micros):
        top_centre = top_stats[:, 2 * micro : 2 * micro + 1]
        top_slope = top_stats[:, 2 * micro + 1 : 2 * micro + 2] * turned[:, micro : micro + 1]
        top_shift = turned[:, micros + micro : micros + micro + 1]
        part = slice(micro * channels, (micro + 1) * channels)
        centre, rstd = second_stats[part, 0:1], second_stats[part, 1:2]
        gain_sum = jnp.zeros((channels, LANES), F32)
        shift_sum = jnp.zeros((channels, LANES), F32)
        for row in range(rows):
            grad = factors[micro] * (
                grads[micro, row] - top_shift - (upper[micro, row] - top_centre) * top_slope
            )
            grad = grad.astype(BF16)
            top_low[micro, row] = grad
            unit = (second_out[micro, row] - centre) * rstd
            grad = dot(w_up_t[...], grad) * slopes[micro, row, 0:channels]
            second_dz[micro, row] = grad
            shift_sum = shift_sum + fold(grad)
            gain_sum = gain_sum + fold(grad * unit)
        second_rows.append((shift_sum, gain_sum))
    parts = []
    for micro in range(micros):
        give = second_sums(total, wide_weight, factors, top_stats, micro, micros, count)
        whole = give(mixed[micro : micro + 1], plain[micro : micro + 1], crossed)
        extra = row_of(*second_rows[micro]) - give(
            own_mixed[micro : micro + 1], own_plain[micro : micro + 1], own_crossed[...]
        )
        expected[micro : micro + 1] = whole
        extras[micro : micro + 1] = extra
        parts.append(whole * (1.0 / count) + extra * (1.0 / (rows * width)))
    parts = columns_of(parts)
    for micro in range(micros):
        part = slice(micro * channels, (micro + 1) * channels)
        centre, rstd = second_stats[part, 0:1], second_stats[part, 1:2]
        factor = gain * rstd
        shift_part = parts[0:channels, micro : micro + 1]
        slope_part = parts[channels : 2 * channels, micro : micro + 1] * rstd
        for row in range(rows):
            grad = factor * (
                second_dz[micro, row] - shift_part - (second_out[micro, row] - centre) * slope_part
            )
            low[micro, row] = spread(grad.astype(BF16), masks)
    weight_copy.wait()
    first_back(
        low, top_low, second_act, acts, first_out, first_stats, first_slopes, b_second, extras,
        out, top_grad, weight_grad, send, rows, tiles,
    )


def first_back(
    low, top_low, second_act, acts, first_out, first_stats, slopes, b_second, extras,
    out, top_grad, weight_grad, send, rows, tiles
):
    tile = lax.axis_index("tile")
    micros, _, channels, width = first_out.shape
    half = 6 * channels
    gain_sums, shift_sums = [], []
    for micro in range(micros):
        units = first_units(first_out, first_stats, micro, channels)
        gain_sum = jnp.zeros((channels, LANES), F32)
        shift_sum = jnp.zeros((channels, LANES), F32)
        for at in range(0, rows + 2, 2):
            if at == 0:
                parts = dot(b_second[:, half:], low[micro, 0:2].reshape(half, width))
            elif at == rows:
                parts = dot(b_second[:, :half], low[micro, rows - 2 : rows].reshape(half, width))
            else:
                parts = conv_pair(low, b_second, micro, at - 2, channels)
            for j in range(2):
                grad = parts[channels * j : channels * (j + 1)] * slopes[micro, at + j]
                if at + j == 0 or at + j == rows + 1:
                    grad = grad * inside(tile, at + j - 1, (tiles, rows))
                out[micro, at + j] = grad
                gain_sum = gain_sum + fold(grad * units(at + j))
                shift_sum = shift_sum + fold(grad)
        gain_sums.append(gain_sum)
        shift_sums.append(shift_sum)
        product = dot_lanes(
            jnp.concatenate([top_low[micro, row] for row in range(rows)], axis=1),
            jnp.concatenate([second_act[micro, row] for row in range(rows)], axis=1),
        )
        top_grad[...] = product if micro == 0 else top_grad[...] + product
    conv_grad(low, 0, acts, 0, weight_grad, rows)
    send_all(send, [row_of(*gain_sums), row_of(*shift_sums)] + [extras[m : m + 1] for m in range(micros)])


def conv_grad(low, low_first, values, value_first, total, rows):
    micros, _, channels, width = values.shape
    for micro in range(micros):
        grads = jnp.concatenate([low[micro, row + low_first] for row in range(rows)], axis=1)
        windows = jnp.concatenate(
            [
                values[micro, row + value_first : row + value_first + 3].reshape(3 * channels, width)
                for row in range(rows)
            ],
            axis=1,
        )
        product = dot_lanes(grads, windows)
        total[...] = product if micro == 0 else total[...] + product


def half_rows(total, half, scene):
    channels = 2 * half
    start = scene * half
    mine = jnp.concatenate(
        [total[b * channels + start : b * channels + start + half, :] for b in range(2, -1, -1)], axis=0
    )
    wing = mine[:, LANES:]
    cut = wing.shape[0] // 2
    return [mine[:, :LANES], jnp.concatenate([wing[:cut], wing[cut:]], axis=1)]


def pick_kernel(
    found, cols, grads, first_out, first_stats, b_first_in, choices, where_rows,
    canvas, second_grad, top_grad, expected,
    send, gain_grad, shift_grad, second_gain_grad, second_shift_grad, low, grid, b_first, first_grad, whole, sems,
    *, rows, tiles, each
):
    weight_copy = move(b_first_in, b_first, sems, 0)
    scene = lax.axis_index("scene")
    micros, high, channels, width = grads.shape
    sums = sum_rows(found, 2 + micros)
    second = sum(sums[2:]) + jnp.sum(expected[...], axis=0, keepdims=True)
    own_half(second[:, :channels], scene, second_shift_grad)
    own_half(second[:, channels:], scene, second_gain_grad)
    sums = sums[:2]
    own_half(sums[0][:, :channels] + sums[0][:, channels:], scene, gain_grad)
    own_half(sums[1][:, :channels] + sums[1][:, channels:], scene, shift_grad)
    turned = columns_of(sums) * (1.0 / (found.shape[0] * rows * width))
    masks = edges(channels, width)
    for micro in range(micros):
        part = slice(micro * channels, (micro + 1) * channels)
        centre, rstd = first_stats[part, 0:1], first_stats[part, 1:2]
        factor = cols[0:channels, 2:3] * rstd
        slope_part, shift_part = rstd * turned[part, 0:1], turned[part, 1:2]
        for row in range(high):
            grad = grads[micro, row]
            if 1 <= row <= rows:
                grad = grad - shift_part - (first_out[micro, row] - centre) * slope_part
            low[micro, row] = spread((factor * grad).astype(BF16), masks)
    weight_copy.wait()
    half = 6 * channels
    for micro in range(micros):
        for at in range(0, rows + 4, 2):
            if at == 0:
                parts = dot(b_first[:, half:], low[micro, 0:2].reshape(half, width))
            elif at == rows + 2:
                parts = dot(b_first[:, :half], low[micro, rows : rows + 2].reshape(half, width))
            else:
                parts = conv_pair(low, b_first, micro, at - 2, channels)
            grid[micro, at] = parts[:channels].astype(BF16)
            grid[micro, at + 1] = parts[channels:].astype(BF16)
    conv_grad(low, 0, canvas, 0, first_grad, high)
    half = channels // 2
    for s in range(2):
        parts = half_rows(first_grad, half, s) + half_rows(second_grad, half, s)
        mine = top_grad[s * channels : (s + 1) * channels, :]
        parts.append(jnp.concatenate([mine[:half], mine[half:]], axis=1))
        parts = jnp.concatenate(parts, axis=0)
        whole[s, 0 : parts.shape[0]] = parts
        if whole.shape[1] > parts.shape[0]:
            whole[s, parts.shape[0] :] = jnp.zeros((whole.shape[1] - parts.shape[0], LANES), F32)
    slots = choices.shape[1]
    groups = []
    for group in range(3):
        start, first, count = ((0, rows - 2, 2), (2, 0, rows), (rows + 2, 0, 2))[group]
        picked = []
        for micro in range(micros):
            at = 2 * group + micro
            place = jnp.floor((where_rows[at : at + 1] - 1.0) * (1.0 / width))
            here = dot_lanes(grid[micro, start : start + count].reshape(count * channels, width), choices[at])
            total = jnp.zeros((channels, slots), F32)
            for r in range(count):
                total = total + jnp.where(
                    place == (first + r) * 1.0, here[r * channels : (r + 1) * channels], 0.0
                )
            picked.append(total)
        groups.append(jnp.transpose(jnp.concatenate(picked, axis=0)))
    capacity = slots // tiles
    block = send.shape[1]

    def filled(parts):
        missing = block - sum(part.shape[0] for part in parts)
        if missing > 0:
            parts = parts + [jnp.zeros((missing, LANES), F32)]
        return jnp.concatenate(parts, axis=0).astype(BF16)

    for spot in range(tiles):
        mine = slice(spot * capacity, (spot + 1) * capacity)
        send[2 * spot + scene] = filled([picked[mine] for picked in groups])
        send[2 * spot + 1 - scene] = filled([whole[s, spot * each : (spot + 1) * each] for s in range(2)])


def pillar_back_kernel(found, rows_in, w_pillar, cols, pooled, send, grads, lifted, rows, sems,
                       *, capacity, each):
    fetched = move(rows_in, rows, sems, 0)
    micros = rows.shape[0]
    _, channels, pillars = pooled.shape
    stats = pooled.at[micros : 2 * micros]
    inputs = w_pillar.shape[1]
    depth = rows.shape[2] // pillars
    scene = lax.axis_index("scene")
    peers = found.shape[0]
    slot_count = peers // 2 * capacity
    blocks = [found[2 * t + scene].astype(F32) for t in range(peers // 2)]
    before, own, after = [
        jnp.concatenate([block[group * capacity : (group + 1) * capacity] for block in blocks], axis=0)
        for group in range(3)
    ]
    gap = jnp.zeros((capacity, LANES), F32)
    returned = (
        own
        + jnp.concatenate([before[capacity:], gap], axis=0)
        + jnp.concatenate([gap, after[: slot_count - capacity]], axis=0)
    )
    turned = jnp.transpose(returned)
    place = lax.broadcasted_iota(jnp.int32, (slot_count, pillars), 0).astype(F32)
    gain, shift = cols[0:channels, 0:1], cols[0:channels, 1:2]
    gain_sums, shift_sums = [], []
    outer = jnp.zeros((16, channels), F32)
    fetched.wait()
    for micro in range(micros):
        lifted[...] = dot(w_pillar[...], rows[micro, 0:inputs])
        slot, limit = pillar_notes(rows, micro, inputs, pillars)
        chosen = jnp.where(place == slot, 1.0, 0.0).astype(BF16)
        back = dot(turned[micro * channels : (micro + 1) * channels].astype(BF16), chosen)
        centre, rstd = stats[micro, :, 0:1], stats[micro, :, 1:2]
        pool = pooled[micro]
        gain_sum = jnp.zeros((channels, pillars), F32)
        shift_sum = jnp.zeros((channels, pillars), F32)
        for n in range(depth):
            piece = slice(n * pillars, (n + 1) * pillars)
            unit = (lifted[:, piece] - centre) * rstd
            normed = unit * gain + shift
            gate = sigmoid(normed)
            act = normed * gate
            slope = gate + act * (1.0 - gate)
            grad = jnp.where(limit > n, back * jnp.exp(act - pool) * slope, 0.0)
            grads[micro, :, piece] = grad
            gain_sum = gain_sum + grad * unit
            shift_sum = shift_sum + grad
        gain_sums.append(gain_sum)
        shift_sums.append(shift_sum)
        scale = jnp.transpose(jnp.broadcast_to(rstd * gain, (channels, LANES)))[0:1]
        outer = outer + dot_lanes(rows[micro], grads[micro].astype(BF16)) * scale
    exact = jnp.concatenate([row_of(*gain_sums), row_of(*shift_sums)], axis=0)
    lines = [jnp.concatenate([outer[k : k + 1], outer[k + 1 : k + 2]], axis=1) for k in range(0, 10, 2)]
    weights = found[1 - scene].astype(F32)
    for t in range(1, peers // 2):
        weights = weights + found[2 * t + 1 - scene].astype(F32)
    rest = send.shape[2] - 9 - each
    for s in range(2):
        block = exact_rows(exact) + lines + [weights[s * each : (s + 1) * each]]
        if rest > 0:
            block.append(jnp.zeros((rest, LANES), F32))
        block = jnp.concatenate(block, axis=0).astype(BF16)
        send[:, s] = jnp.broadcast_to(block[None], (send.shape[0],) + block.shape)


def points_kernel(
    found, rows_in, grads, w_pillar, cols, pooled,
    points_grad, pillar_grad, gain_grad, shift_grad, first_grad, second_grad, up_grad, rows, lifted, sems,
    *, each
):
    fetched = move(rows_in, rows, sems, 0)
    scene = lax.axis_index("scene")
    micros, channels, _ = grads.shape
    stats = pooled.at[micros : 2 * micros]
    _, _, inputs, depth, pillars = points_grad.shape
    half = channels // 2
    total = jnp.sum(found[...].astype(F32), axis=0)
    total = jnp.concatenate([total[0:2] + total[2:4], total[4:9]], axis=0)
    own_half(total[0:1, :channels] + total[0:1, channels:], scene, gain_grad)
    own_half(total[1:2, :channels] + total[1:2, channels:], scene, shift_grad)
    turned = jnp.transpose(jnp.concatenate([total, jnp.zeros((1, LANES), F32)], axis=0))
    weight_grad = jnp.concatenate(
        [turned[(k % 2) * channels : (k % 2 + 1) * channels, 2 + k // 2 : 3 + k // 2] for k in range(inputs)],
        axis=1,
    )
    weight = jnp.transpose(w_pillar[...].astype(F32)).astype(BF16)
    fetched.wait()
    for micro in range(micros):
        lifted[...] = dot(w_pillar[...], rows[micro, 0:inputs])
        part = slice(micro * channels, (micro + 1) * channels)
        centre, rstd, inverse = stats[micro, :, 0:1], stats[micro, :, 1:2], stats[micro, :, 2:3]
        factor = cols[0:channels, 0:1] * rstd
        gain_part, shift_part = turned[part, 0:1], turned[part, 1:2]
        spun, mean = stats[micro, :, 16 : 16 + inputs], stats[micro, :, 32 : 32 + inputs]
        weight_grad = weight_grad - factor * (shift_part * mean + gain_part * rstd * spun)
        gain_part, shift_part = gain_part * inverse * rstd, shift_part * inverse
        _, limit = pillar_notes(rows, micro, inputs, pillars)
        for n in range(depth):
            piece = slice(n * pillars, (n + 1) * pillars)
            low = factor * (grads[micro, :, piece] - shift_part - (lifted[:, piece] - centre) * gain_part)
            low = jnp.where(limit > n, low, 0.0).astype(BF16)
            points_grad[micro, 0, :, n, :] = dot(weight, low)
    weight_grad = jnp.concatenate([weight_grad, jnp.zeros((channels, LANES - inputs), F32)], axis=1)
    weight_grad = jnp.transpose(weight_grad)[0:inputs]
    pillar_grad[...] = jnp.where(scene == 0, weight_grad[:, :half], weight_grad[:, half:])
    whole = jnp.concatenate(
        [
            (found[2 * t].astype(F32) + found[2 * t + 1].astype(F32))[9 : 9 + each]
            for t in range(found.shape[0] // 2)
        ],
        axis=0,
    )
    for index, out in enumerate((first_grad, second_grad)):
        base = index * 9 * half * channels // LANES
        lead = 3 * half
        mine = whole[base : base + lead]
        wing = whole[base + lead : base + lead + lead // 2]
        wing = jnp.concatenate([wing[:, :channels], wing[:, channels:]], axis=0)
        both = jnp.concatenate([mine, wing], axis=1)
        for a in range(3):
            for b in range(3):
                at = (3 * a + b) * channels
                out[:, at : at + channels] = both[b * half : (b + 1) * half, a * channels : (a + 1) * channels]
    base = 2 * 9 * half * channels // LANES
    top = whole[base : base + half]
    up_grad[...] = jnp.concatenate([top[:, :channels], top[:, channels:]], axis=0)


def swap(blocks, axes):
    return lax.all_to_all(blocks, axes, split_axis=0, concat_axis=0)


def shards(
    points, point_counts, pillar_tile, pillar_cell,
    pillar_weight, pillar_gain, pillar_shift,
    first_weight, first_gain, first_shift,
    second_weight, second_gain, second_shift,
    up_weight, up_gain, up_shift, cotangent,
):
    micros, _, inputs, depth, pillars = points.shape
    channels = up_weight.shape[1]
    upper = cotangent.shape[2]
    rows, width = cotangent.shape[3:]
    tiles = lax.axis_size("tile")
    scenes = lax.axis_size("scene")
    peers = tiles * scenes
    capacity = 2 * pillars // tiles
    slot_count = tiles * capacity
    half = channels // 2

    def vmem(shape, dtype):
        return pltpu.VMEM(shape, dtype)

    def grid(high, dtype=F32, lead=channels):
        return ((micros, high, lead, width), dtype)

    sums = ((peers, 2, LANES), F32)
    sources = (
        pillar_tile, pillar_cell, point_counts, points,
        first_weight, second_weight, up_weight, pillar_weight.T,
        pillar_gain, pillar_shift, first_gain, first_shift, second_gain, second_shift, up_gain, up_shift,
    )
    moments, packed, point_rows = run(
        functools.partial(moments_kernel, capacity=capacity),
        [
            ((tiles, scenes, 4, LANES), F32), ((layout(half, channels)[-1] + 16, LANES), BF16),
            ((micros, 16, depth * pillars), BF16),
        ],
        *sources,
        hbm=range(len(sources)), copies=len(sources), limit=WIDE_LIMIT,
        scratch=[vmem(source.shape, source.dtype) for source in sources]
        + [vmem((inputs * depth, pillars), F32)],
    )
    moments = swap(moments.reshape(peers, 4, LANES), BOTH)
    both = lax.all_gather(packed, "scene")
    taps = ((2 * channels, 12 * channels), BF16)
    w_pillar, cols, l_first, l_second, b_first, b_second, w_up, w_up_t = run(
        functools.partial(unpack_kernel, inputs=inputs),
        [
            ((channels, inputs), BF16), ((LANES, 8), F32), taps, taps + (1,), taps + (1,), taps + (1,),
            ((upper, channels), BF16), ((channels, upper), BF16),
        ],
        both,
        scratch=[vmem(*taps), vmem(*taps), vmem(*taps)], copies=3,
    )
    cot = cotangent[:, 0].transpose(0, 2, 1, 3)

    send, pooled = run(
        functools.partial(pillar_kernel, capacity=capacity),
        [((slot_count, 3 * LANES), BF16), ((2 * micros, channels, pillars), F32)],
        moments, point_rows, w_pillar, cols,
        scratch=[vmem((channels, depth * pillars), F32), vmem((channels, depth * pillars), F32)],
    )
    arrived = swap(send.reshape(tiles, capacity, 3 * LANES), "tile").reshape(slot_count, 3 * LANES)
    cell_columns, cell_rows = run(
        functools.partial(cells_kernel, capacity=capacity),
        [((slot_count, LANES), F32), ((8, slot_count), F32)],
        moments,
        cost=pl.CostEstimate(flops=10**7, bytes_accessed=10**6, transcendentals=0),
    )
    arrived, cot = lax.optimization_barrier((arrived, cot))

    first_out, canvas, choices, send = run(
        functools.partial(canvas_kernel, rows=rows),
        [grid(rows + 2), grid(rows + 4, BF16), ((3 * micros, slot_count, width), BF16), sums],
        arrived, cell_columns, cell_rows, l_first,
        scratch=[vmem(*grid(rows + 4, BF16, 3 * channels))],
    )
    second_out, first_act, first_slopes, first_stats, send = run(
        functools.partial(second_kernel, rows=rows, tiles=tiles),
        [grid(rows), grid(rows + 2, BF16), grid(rows + 2), ((LANES, 8), F32), sums],
        swap(send, BOTH), cols, first_out, l_second,
        hbm=(3,), scratch=[vmem(*grid(rows + 2, BF16, 3 * channels)), vmem(*taps)], copies=1,
    )
    part = -(-micros * channels // peers)
    second_act, up_out, slopes, plain, crossed, second_stats, send = run(
        functools.partial(up_kernel, rows=rows),
        [
            grid(rows, BF16), grid(rows, F32, upper), grid(rows, F32, 2 * channels), ((micros, LANES), F32),
            ((peers * part, LANES), F32), ((LANES, 8), F32), ((peers, -(-(2 * micros + part) // 8) * 8, LANES), F32),
        ],
        swap(send, BOTH), cols, second_out, w_up,
    )
    features, grads, mixed, top_stats, send = run(
        functools.partial(top_kernel, rows=rows, each=part),
        [
            ((micros, 1, upper, rows, width), BF16), grid(rows, F32, upper), ((micros, LANES), F32),
            ((LANES, 8), F32),
            ((peers, -(-(6 * micros + part) // 8) * 8, LANES), BF16),
        ],
        swap(send, BOTH), cols, up_out, cot, slopes, plain, w_up_t,
        scratch=[vmem((micros, width // LANES, upper * rows, LANES), F32)],
    )
    vector, top_vector, matrix = ((half,), F32), ((upper // 2,), F32), ((half, 9 * channels), F32)
    cross = ((3 * channels, 3 * channels), F32)
    first_dz, top_grad, second_cross, up_gain_grad, up_shift_grad, expected, send = run(
        functools.partial(middle_back_kernel, rows=rows, tiles=tiles, each=part),
        [
            grid(rows + 2), ((upper, channels), F32), cross, top_vector, top_vector, ((micros, LANES), F32),
            ((peers, 2 + micros, LANES), F32),
        ],
        swap(send, BOTH), cols, grads, up_out, top_stats, second_out, second_stats, slopes, w_up, w_up_t,
        mixed, plain, crossed, second_act, first_act, first_out, first_stats, first_slopes, b_second,
        hbm=(18,),
        scratch=[
            vmem(*grid(rows, BF16, 3 * channels)), vmem(*grid(rows, BF16, upper)), vmem((micros, LANES), F32),
            vmem(*grid(rows)), vmem(*taps),
        ],
        copies=1,
    )
    length = (2 * 9 * half * channels + upper * half) // LANES
    each = -(-length // tiles)
    block = -(-max(3 * capacity, 2 * each) // 8) * 8
    send, first_gain_grad, first_shift_grad, second_gain_grad, second_shift_grad = run(
        functools.partial(pick_kernel, rows=rows, tiles=tiles, each=each),
        [((peers, block, LANES), BF16), vector, vector, vector, vector],
        swap(send, BOTH), cols, first_dz, first_out, first_stats, b_first, choices, cell_rows,
        canvas, second_cross, top_grad, expected,
        hbm=(5,),
        scratch=[
            vmem(*grid(rows + 2, BF16, 3 * channels)), vmem(*grid(rows + 4, BF16)), vmem(*taps), vmem(*cross),
            vmem((scenes, tiles * each, LANES), F32),
        ],
        copies=1,
    )
    block = -(-(9 + each) // 8) * 8
    send, pillar_dz = run(
        functools.partial(pillar_back_kernel, capacity=capacity, each=each),
        [((tiles, scenes, block, LANES), BF16), ((micros, channels, depth * pillars), F32)],
        swap(send, BOTH), point_rows, w_pillar, cols, pooled,
        hbm=(1,),
        scratch=[vmem((channels, depth * pillars), F32), vmem((micros, 16, depth * pillars), BF16)],
        copies=1,
    )
    points_grad, pillar_grad, pillar_gain_grad, pillar_shift_grad, first_grad, second_grad, up_grad = run(
        functools.partial(points_kernel, each=each),
        [
            ((micros, 1, inputs, depth, pillars), F32), ((inputs, half), F32), vector, vector,
            matrix, matrix, ((upper // 2, channels), F32),
        ],
        swap(send.reshape(peers, block, LANES), BOTH), point_rows, pillar_dz, w_pillar, cols, pooled,
        hbm=(1,),
        scratch=[vmem((micros, 16, depth * pillars), BF16), vmem((channels, depth * pillars), F32)],
        copies=1,
    )
    return (
        features, points_grad,
        pillar_grad.T, pillar_gain_grad, pillar_shift_grad,
        first_grad, first_gain_grad, first_shift_grad,
        second_grad, second_gain_grad, second_shift_grad,
        up_grad, up_gain_grad, up_shift_grad,
    )


def solution(mesh):
    matrix, vector = P("scene", None), P("scene")
    grid = P(None, "scene", None, "tile", None)
    cloud = P(None, "scene", None, None, "tile")
    pillar = P(None, "scene", "tile")
    weights = (matrix, vector, vector) * 4
    return jax.shard_map(
        shards,
        mesh=mesh,
        in_specs=(cloud, pillar, pillar, pillar) + weights + (grid,),
        out_specs=(grid, cloud) + weights,
        check_vma=False,
    )
```

```python
import functools

import jax
import jax.numpy as jnp
from jax import lax
from jax.experimental import pallas as pl
from jax.experimental.pallas import tpu as pltpu
from jax.sharding import PartitionSpec as P

norm_eps = 0.001
BOTH = ("tile", "scene")
F32 = jnp.float32
BF16 = jnp.bfloat16
VMEM_LIMIT = 24 * 1024 * 1024
WIDE_LIMIT = 60 * 1024 * 1024
LANES = 128


def run(kernel, outs, *args, hbm=(), scratch=(), copies=0, cost=None, limit=VMEM_LIMIT):
    specs = [
        pl.BlockSpec(memory_space=pltpu.HBM if index in hbm else pltpu.VMEM) for index in range(len(args))
    ]
    scratch = list(scratch)
    if copies:
        scratch.append(pltpu.SemaphoreType.DMA((copies,)))
    return pl.pallas_call(
        kernel,
        out_shape=[jax.ShapeDtypeStruct(out[0], out[1]) for out in outs],
        in_specs=specs,
        out_specs=[
            pl.BlockSpec(memory_space=pltpu.HBM if len(out) > 2 else pltpu.VMEM) for out in outs
        ],
        scratch_shapes=scratch,
        compiler_params=pltpu.CompilerParams(vmem_limit_bytes=limit),
        cost_estimate=cost,
    )(*args)


def move(source, target, sems, index):
    copy = pltpu.make_async_copy(source, target, sems.at[index])
    copy.start()
    return copy


def dot(left, right, precision=None):
    return jnp.dot(left, right, preferred_element_type=F32, precision=precision)


def dot_lanes(left, right, precision=None):
    return lax.dot_general(
        left, right, (((1,), (1,)), ((), ())), preferred_element_type=F32, precision=precision
    )


def sigmoid(values):
    return 0.5 + 0.5 * jnp.tanh(0.5 * values)


def fold(values):
    total = values[:, :LANES]
    for start in range(LANES, values.shape[1], LANES):
        total = total + values[:, start : start + LANES]
    return total


def row_of(left, right=None):
    both = left if right is None else jnp.concatenate([left, right], axis=0)
    return jnp.sum(jnp.transpose(both), axis=0, keepdims=True)


def columns_of(rows):
    rows = rows + [jnp.zeros((8 - len(rows), LANES), F32)] if len(rows) < 8 else rows
    return jnp.transpose(jnp.concatenate(rows, axis=0))


def inside(tile, row, height):
    tiles, rows = height
    place = tile * rows + row
    return jnp.where((place >= 0) & (place < tiles * rows), 1.0, 0.0).astype(F32)


def send_all(ref, rows):
    for index, row in enumerate(rows):
        ref[:, index : index + 1, :] = jnp.broadcast_to(row[None], (ref.shape[0], 1, LANES))


def pooled_stats(means, squares, count):
    peers = means.shape[0]
    mean = jnp.sum(means, axis=0, keepdims=True) * (1.0 / peers)
    away = means - mean
    spread = jnp.sum(squares + count * away * away, axis=0, keepdims=True) * (1.0 / (peers * count))
    return mean, lax.rsqrt(spread + norm_eps)


def stat_columns(found, count):
    return columns_of(list(pooled_stats(found[:, 0, :], found[:, 1, :], count)))


def sum_rows(found, lines):
    return [jnp.sum(found[:, index, :], axis=0, keepdims=True) for index in range(lines)]


def own_half(row, scene, out):
    size = out.shape[0]
    out[...] = jnp.where(scene == 0, row[:, 0:size], row[:, size : 2 * size]).reshape(size)


def edges(channels, width):
    lane = lax.broadcasted_iota(jnp.int32, (channels, width), 1)
    return lane > 0, lane < width - 1


def spread(row, masks):
    zero = jnp.zeros_like(row)
    left = jnp.where(masks[0], pltpu.roll(row, 1, 1), zero)
    right = jnp.where(masks[1], pltpu.roll(row, row.shape[1] - 1, 1), zero)
    return jnp.concatenate([left, row, right], axis=0)


def layout(half, channels):
    first = 0
    second = first + half * -(-9 * channels // LANES)
    up = second + half * -(-9 * channels // LANES)
    vectors = up + channels
    return first, second, up, vectors, vectors + 16


def widen(value):
    missing = LANES - value.shape[1]
    if missing == 0:
        return value
    return jnp.concatenate([value, jnp.zeros((value.shape[0], missing), value.dtype)], axis=1)


def pack(held, out):
    first, second, up, pillar = held[:4]
    half, channels = first.shape[0], up.shape[1]
    starts = layout(half, channels)
    for ref, start in ((first, starts[0]), (second, starts[1])):
        for j in range(-(-9 * channels // LANES)):
            out[start + j * half : start + (j + 1) * half, :] = widen(
                ref[:, j * LANES : min((j + 1) * LANES, 9 * channels)]
            )
    out[starts[2] : starts[2] + channels, :] = widen(up[...])
    rows = [vector[...].astype(F32).reshape(1, -1) for vector in held[4:]]
    rows = [widen(row) for row in rows] + [jnp.zeros((16 - len(rows), LANES), F32)]
    turned = widen(pillar[...].astype(F32))
    rows += [turned, jnp.zeros((16 - turned.shape[0], LANES), F32)]
    out[starts[3] :, :] = jnp.concatenate(rows, axis=0).astype(BF16)


def unpack_kernel(
    both, w_pillar, cols, l_first, l_second, b_first, b_second, w_up, w_up_t, *, inputs
):
    half = w_pillar.shape[0] // 2
    channels = 2 * half
    starts = layout(half, channels)
    tiles = -(-9 * channels // LANES)

    def wide(start):
        return jnp.concatenate(
            [
                jnp.concatenate(
                    [both[s, start + j * half : start + (j + 1) * half, :] for j in range(tiles)], axis=1
                )
                for s in range(2)
            ],
            axis=0,
        ).astype(F32)

    up = jnp.concatenate(
        [both[s, starts[2] : starts[2] + channels, 0:channels] for s in range(2)], axis=0
    )
    w_up[...] = up
    w_up_t[...] = jnp.transpose(up.astype(F32)).astype(BF16)
    turned = jnp.concatenate(
        [both[s, starts[4] : starts[4] + 16, 0:half].astype(F32) for s in range(2)], axis=1
    )
    w_pillar[...] = jnp.transpose(widen(turned))[0:channels, 0:inputs].astype(BF16)
    vectors = [both[s, starts[3] : starts[3] + 16, :].astype(F32) for s in range(2)]
    rows = []
    for index in range(8):
        size = half if index < 6 else channels
        row = jnp.concatenate([vectors[s][index : index + 1, 0:size] for s in range(2)], axis=1)
        rows.append(jnp.concatenate([row] * (LANES // (2 * size)), axis=1))
    cols[...] = columns_of(rows)
    for weight, ahead, back in ((wide(starts[0]), l_first, b_first), (wide(starts[1]), l_second, b_second)):
        turned = jnp.transpose(weight)
        ahead[...] = weight[:, : 9 * channels].astype(BF16)
        back[...] = jnp.concatenate(
            [turned[tap * channels : (tap + 1) * channels] for tap in range(8, -1, -1)], axis=1
        ).astype(BF16)


def slot_line(wide, depth, inputs):
    return jnp.concatenate([wide[pl.ds(n, inputs, stride=depth), :] for n in range(depth)], axis=1)


def slot_mask(count, depth):
    return jnp.concatenate([jnp.where(count > n, 1.0, 0.0) for n in range(depth)], axis=1)


def ranks(tile):
    pillars = tile.shape[1]
    across = jnp.broadcast_to(tile, (pillars, pillars))
    down = jnp.transpose(across)
    row = lax.broadcasted_iota(jnp.int32, (pillars, pillars), 0)
    col = lax.broadcasted_iota(jnp.int32, (pillars, pillars), 1)
    return jnp.sum(jnp.where((across == down) & (row < col), 1.0, 0.0), axis=0, keepdims=True)


def moments_kernel(*refs, capacity):
    number = 16
    sources, out, packed, lines_out = refs[:number], *refs[number : number + 3]
    held, wide, sems = refs[number + 3 : 2 * number + 3], refs[-2], refs[-1]
    copies = [move(sources[i], held[i], sems, i) for i in range(number)]
    tiles, cells, counts, points = held[:4]
    micros, _, inputs, depth, pillars = points.shape
    peers, scenes = out.shape[:2]
    copies[0].wait()
    copies[1].wait()
    lines, slot_rows = [], []
    for micro in range(micros):
        tile = tiles[micro].astype(F32)
        cell = (cells[micro] + 1).astype(F32)
        high = jnp.floor(cell * (1.0 / 16.0))
        low = cell - high * 16.0
        rank = ranks(tile)
        slot_rows.append(tile * capacity + rank)
        spot = lax.broadcasted_iota(jnp.int32, (capacity, pillars), 0).astype(F32)
        placed = jnp.where(spot == rank, 1.0, 0.0).astype(BF16)
        peer = lax.broadcasted_iota(jnp.int32, (peers, pillars), 0).astype(F32)
        for group in range(3):
            named = tile == peer + (group - 1.0)
            lines.append(
                16.0 * dot_lanes(jnp.where(named, high, 0.0).astype(BF16), placed)
                + dot_lanes(jnp.where(named, low, 0.0).astype(BF16), placed)
            )
    used = 3 * micros * capacity
    line = jnp.concatenate(lines + [jnp.zeros((peers, LANES - used), F32)], axis=1).reshape(peers, 1, LANES)
    for scene in range(scenes):
        out[:, scene, micros : micros + 1, :] = line
    copies[2].wait()
    copies[3].wait()
    parts, mean_rows, totals = [], [], []
    for micro in range(micros):
        wide[...] = points[micro, 0].astype(F32).reshape(inputs * depth, pillars)
        rows = slot_line(wide, depth, inputs)
        notes = jnp.concatenate([slot_rows[micro], counts[micro].astype(F32)], axis=0)
        notes = jnp.concatenate([notes, jnp.zeros((2, rows.shape[1] - pillars), F32)], axis=1)
        lines_out[micro] = jnp.concatenate(
            [rows, notes, jnp.zeros((14 - inputs, rows.shape[1]), F32)], axis=0
        ).astype(BF16)
        mask = slot_mask(counts[micro], depth)
        total = jnp.sum(mask, axis=1, keepdims=True)
        mean = jnp.sum(rows * mask, axis=1, keepdims=True) / total
        centred = jnp.concatenate(
            [(rows - mean) * mask, jnp.zeros((16 - inputs, rows.shape[1]), F32)], axis=0
        )
        high = centred.astype(BF16)
        parts += [high, (centred - high.astype(F32)).astype(BF16)]
        lane = lax.broadcasted_iota(jnp.int32, (inputs, inputs), 1)
        diagonal = lax.broadcasted_iota(jnp.int32, (inputs, inputs), 0) == lane
        mean_rows.append(jnp.sum(jnp.where(diagonal, mean, 0.0), axis=0, keepdims=True))
        totals.append(total)
    parts = jnp.concatenate(parts, axis=0)
    every = dot_lanes(parts, parts)
    for micro in range(micros):
        at = 32 * micro
        square = every[at : at + 32, at : at + 32]
        products = (
            square[0:inputs, 0:inputs] + square[16 : 16 + inputs, 0:inputs]
            + square[0:inputs, 16 : 16 + inputs] + square[16 : 16 + inputs, 16 : 16 + inputs]
        )
        row = jnp.concatenate(
            [products[k : k + 1] for k in range(inputs)]
            + [mean_rows[micro], totals[micro], jnp.zeros((1, LANES - inputs * inputs - inputs - 1), F32)],
            axis=1,
        )
        for scene in range(scenes):
            out[:, scene, micro : micro + 1, :] = jnp.broadcast_to(row[None], (peers, 1, LANES))
    for copy in copies[4:]:
        copy.wait()
    pack(held[4:], packed)


def cells_kernel(found, rows, *, capacity):
    scene = lax.axis_index("scene")
    slots = rows.shape[1]
    peers = found.shape[0]
    values = found[:, 2, :]
    slot = lax.broadcasted_iota(jnp.int32, (slots, peers), 0)
    peer = lax.broadcasted_iota(jnp.int32, (slots, peers), 1)
    lane = lax.broadcasted_iota(jnp.int32, (slots, LANES), 1)
    row = lax.broadcasted_iota(jnp.int32, (slots, LANES), 0)
    result = jnp.zeros((slots, LANES), F32)
    chosen = jnp.where(peer == 2 * (slot // capacity) + scene, 1.0, 0.0)
    spread = dot(chosen, values, lax.Precision.HIGHEST)
    for micro in range(2):
        for group in range(3):
            mine = jnp.where(lane == (3 * micro + group) * capacity + row % capacity, spread, 0.0)
            column = jnp.sum(mine, axis=1, keepdims=True)
            result = jnp.where(lane == 2 * group + micro, column, result)
    rows[...] = jnp.transpose(result)[0:8]


def pillar_notes(rows, micro, inputs, pillars):
    notes = rows[micro, :, 0:pillars].astype(F32)
    return notes[inputs : inputs + 1], notes[inputs + 1 : inputs + 2]


def pillar_kernel(
    found, point_rows, w_pillar, cols, send, pooled, lifted, acts, *, capacity
):
    micros = point_rows.shape[0]
    channels, inputs = w_pillar.shape
    pillars = pooled.shape[2]
    depth = point_rows.shape[2] // pillars
    weight = w_pillar[...]
    wide_weight = weight.astype(F32)
    rows_out = send.shape[0]
    square = inputs * inputs
    stacked, slot_rows = [], []
    for micro in range(micros):
        lifted[...] = dot(weight, point_rows[micro, 0:inputs])
        moments = found[:, micro, :]
        sizes = moments[:, square + inputs : square + inputs + 1]
        means = moments[:, square : square + inputs]
        count = jnp.sum(sizes, axis=0, keepdims=True)
        mean = jnp.sum(means * sizes, axis=0, keepdims=True) / count
        away = means - mean
        products = lax.dot_general(
            away * sizes, away, (((0,), (0,)), ((), ())),
            preferred_element_type=F32, precision=lax.Precision.HIGHEST,
        )
        summed = jnp.sum(moments, axis=0, keepdims=True)
        products = products + jnp.concatenate(
            [summed[:, k * inputs : (k + 1) * inputs] for k in range(inputs)], axis=0
        )
        cov = products / count
        spun = wide_weight[:, 0:1] * cov[0:1]
        for k in range(1, inputs):
            spun = spun + wide_weight[:, k : k + 1] * cov[k : k + 1]
        spread = jnp.sum(spun * wide_weight, axis=1, keepdims=True)
        centre = jnp.sum(wide_weight * mean, axis=1, keepdims=True)
        rstd = lax.rsqrt(spread + norm_eps)
        inverse = jnp.broadcast_to(1.0 / count, (channels, 1))
        pooled[micros + micro] = jnp.concatenate(
            [
                centre, rstd, inverse, jnp.zeros((channels, 13), F32),
                spun, jnp.zeros((channels, 16 - inputs), F32),
                jnp.broadcast_to(mean, (channels, inputs)), jnp.zeros((channels, LANES - 32 - inputs), F32),
            ],
            axis=1,
        )
        scale = rstd * cols[0:channels, 0:1]
        shift = cols[0:channels, 1:2]
        slot, limit = pillar_notes(point_rows, micro, inputs, pillars)
        slot_rows.append(slot)
        top = jnp.full((channels, pillars), -jnp.inf, F32)
        for n in range(depth):
            piece = slice(n * pillars, (n + 1) * pillars)
            normed = (lifted[:, piece] - centre) * scale + shift
            act = normed * sigmoid(normed)
            acts[:, piece] = act
            top = jnp.maximum(top, jnp.where(limit > n, act, -jnp.inf))
        total = jnp.zeros((channels, pillars), F32)
        for n in range(depth):
            piece = slice(n * pillars, (n + 1) * pillars)
            total = total + jnp.where(limit > n, jnp.exp(acts[:, piece] - top), 0.0)
        result = top + jnp.log(total)
        pooled[micro] = result
        parts = [jnp.zeros((channels, pillars), F32)] * micros
        parts[micro] = result.astype(BF16).astype(F32)
        stacked.append(jnp.transpose(jnp.concatenate(parts, axis=0)))
    values = jnp.concatenate(stacked, axis=0).astype(BF16)
    for group in range(3):
        place = lax.broadcasted_iota(jnp.int32, (rows_out, pillars), 0) + (group - 1) * capacity
        chosen = jnp.concatenate(
            [jnp.where(place.astype(F32) == row, 1.0, 0.0) for row in slot_rows], axis=1
        ).astype(BF16)
        send[:, group * LANES : (group + 1) * LANES] = dot(chosen, values).astype(BF16)


def own_stats(ref, first_row, rows, send):
    micros, _, channels, width = ref.shape
    sums, squares = [], []
    for micro in range(micros):
        total = fold(ref[micro, first_row])
        for row in range(first_row + 1, first_row + rows):
            total = total + fold(ref[micro, row])
        sums.append(total * (1.0 / (rows * width)))
    means = [jnp.sum(total, axis=1, keepdims=True) for total in sums]
    for micro in range(micros):
        spread = jnp.zeros(sums[micro].shape, F32)
        for row in range(first_row, first_row + rows):
            away = ref[micro, row] - means[micro]
            spread = spread + fold(away * away)
        squares.append(spread)
    if channels == LANES:
        send_all(send, [row_of(part) for part in sums + squares])
    else:
        send_all(send, [row_of(*sums), row_of(*squares)])


def expand(taps, weight):
    channels, length = taps.shape
    gap = jnp.zeros((channels, length // 3), BF16)
    weight[0:channels] = jnp.concatenate([taps[...], gap], axis=1)
    weight[channels : 2 * channels] = jnp.concatenate([gap, taps[...]], axis=1)


def conv_pair(source, weight, micro, at, channels):
    window = source[micro, at : at + 4].reshape(12 * channels, source.shape[3])
    return dot(weight[...], window)


def conv_rows(source, weight, out, shape):
    micros, high, channels, width = shape
    for micro in range(micros):
        for at in range(0, high, 2):
            both = conv_pair(source, weight, micro, at, channels)
            out[micro, at] = both[:channels].astype(out.dtype)
            out[micro, at + 1] = both[channels:].astype(out.dtype)


def canvas_kernel(found, where_rows, l_first_in, out, kept, send, canvas, l_first, *, rows):
    expand(l_first_in, l_first)
    columns = jnp.transpose(where_rows[...])
    scenes, high, channels, width = out.shape
    masks = edges(channels, width)
    slots = found.shape[0]
    lane = lax.broadcasted_iota(jnp.int32, (slots, width), 1).astype(F32)
    for group in range(3):
        values = jnp.transpose(found[:, group * LANES : (group + 1) * LANES].astype(F32))
        first, count = ((rows - 2, 2), (0, rows), (0, 2))[group]
        for scene in range(scenes):
            at = 2 * group + scene
            column = columns[:, at : at + 1] - 1.0
            column = column - jnp.floor(column * (1.0 / width)) * width
            row = jnp.floor((where_rows[at : at + 1] - 1.0) * (1.0 / width))
            mine = values[scene * channels : (scene + 1) * channels]
            placed = jnp.concatenate(
                [jnp.where(row == r * 1.0, mine, 0.0) for r in range(first, first + count)], axis=0
            ).astype(BF16)
            chosen = jnp.where(lane == column, 1.0, 0.0).astype(BF16)
            grid = dot(placed, chosen).astype(BF16)
            start = (0, 2, rows + 2)[group]
            for r in range(count):
                row = grid[r * channels : (r + 1) * channels]
                canvas[scene, start + r] = spread(row, masks)
                kept[scene, start + r] = row
    conv_rows(canvas, l_first, out, out.shape)
    own_stats(out, 1, rows, send)


def second_kernel(found, cols, first_out, l_second_in, out, kept, slopes, stats, send, acts, l_second,
                  *, rows, tiles):
    expand(l_second_in, l_second)
    micros, high, channels, width = first_out.shape
    tile = lax.axis_index("tile")
    turned = stat_columns(found, float(rows * width))
    stats[...] = turned
    masks = edges(channels, width)
    for micro in range(micros):
        part = slice(micro * channels, (micro + 1) * channels)
        centre = turned[part, 0:1]
        scale = turned[part, 1:2] * cols[0:channels, 2:3]
        shift = cols[0:channels, 3:4]

        for row in range(high):
            normed = (first_out[micro, row] - centre) * scale + shift
            gate = sigmoid(normed)
            act = normed * gate
            slopes[micro, row] = gate + act * (1.0 - gate)
            if row == 0 or row == high - 1:
                act = act * inside(tile, row - 1, (tiles, rows))
            act = act.astype(BF16)
            acts[micro, row] = spread(act, masks)
            kept[micro, row] = act
    conv_rows(acts, l_second, out, out.shape)
    own_stats(out, 0, rows, send)


def up_kernel(found, cols, second_out, w_up, acts, upper, slopes, plain, crossed, stats, send, *, rows):
    micros, _, channels, width = second_out.shape
    peers = send.shape[0]
    each = crossed.shape[0] // peers
    turned = stat_columns(found, float(rows * width))
    stats[...] = turned
    gain, shift = cols[0:channels, 4:5], cols[0:channels, 5:6]
    lines = []
    for micro in range(micros):
        part = slice(micro * channels, (micro + 1) * channels)
        centre, rstd = turned[part, 0:1], turned[part, 1:2]
        slope_sum = jnp.zeros((channels, LANES), F32)
        unit_sum = jnp.zeros((channels, LANES), F32)
        for row in range(rows):
            unit = (second_out[micro, row] - centre) * rstd
            normed = unit * gain + shift
            gate = sigmoid(normed)
            act = normed * gate
            slope = gate + act * (1.0 - gate)
            sloped = slope * unit
            slope_sum = slope_sum + fold(slope)
            unit_sum = unit_sum + fold(sloped)
            slopes[micro, row] = jnp.concatenate([slope, sloped], axis=0)
            act = act.astype(BF16)
            acts[micro, row] = act
            upper[micro, row] = dot(w_up[...], act)
        lines.append(row_of(slope_sum, unit_sum).astype(BF16).astype(F32))
        crossed[micro * channels : (micro + 1) * channels] = dot_lanes(
            jnp.concatenate([acts[micro, row] for row in range(rows)], axis=1),
            jnp.concatenate([slopes[micro, row].astype(BF16) for row in range(rows)], axis=1),
        )
    plain[...] = jnp.concatenate(lines, axis=0)
    used = micros * channels
    if crossed.shape[0] > used:
        crossed[used:] = jnp.zeros((crossed.shape[0] - used, LANES), F32)
    if 2 * micros + each < send.shape[1]:
        send[...] = jnp.zeros(send.shape, F32)
    for peer in range(peers):
        send[peer, 2 * micros : 2 * micros + each] = crossed[peer * each : (peer + 1) * each]
    own_stats(upper, 0, rows, send)


def exact_rows(rows):
    high = rows.astype(BF16).astype(F32)
    return [high, rows - high]


def top_kernel(
    found, cols, upper, cot, slopes, plain, w_up_t, features, grads, mixed, stats, send, ordered, *, rows, each
):
    micros, _, wide, width = upper.shape
    channels = w_up_t.shape[0]
    lines = []
    for micro in range(micros):
        lines += list(pooled_stats(found[:, micro, :], found[:, micros + micro, :], float(rows * width)))
    turned = columns_of(lines)
    stats[...] = turned
    gain, shift = cols[:, 6:7], cols[:, 7:8]
    gain_rows, shift_rows, mixed_rows = [], [], []
    for micro in range(micros):
        centre, rstd = turned[:, 2 * micro : 2 * micro + 1], turned[:, 2 * micro + 1 : 2 * micro + 2]
        factor = gain * rstd
        gain_sum = jnp.zeros((wide, LANES), F32)
        shift_sum = jnp.zeros((wide, LANES), F32)
        mixed_sum = jnp.zeros((2 * channels, LANES), F32)
        for row in range(rows):
            unit = (upper[micro, row] - centre) * rstd
            normed = unit * gain + shift
            gate = sigmoid(normed)
            act = normed * gate
            grad = cot[micro, row].astype(F32) * (gate + act * (1.0 - gate))
            for j in range(width // LANES):
                ordered[micro, j, pl.ds(row, wide, stride=rows), :] = act[:, j * LANES : (j + 1) * LANES]
            grads[micro, row] = grad
            gain_sum = gain_sum + fold(grad * unit)
            shift_sum = shift_sum + fold(grad)
            below = dot(w_up_t[...], (grad * factor).astype(BF16))
            mixed_sum = mixed_sum + fold(
                slopes[micro, row] * jnp.concatenate([below, below], axis=0)
            )
        gain_rows.append(row_of(gain_sum))
        shift_rows.append(row_of(shift_sum))
        mixed_rows.append(row_of(mixed_sum).astype(BF16).astype(F32))
        line = jnp.concatenate([ordered[micro, j].astype(BF16) for j in range(width // LANES)], axis=1)
        features[micro, 0] = line.reshape(wide, rows, width)
    mixed[...] = jnp.concatenate(mixed_rows, axis=0)
    rows_out = jnp.concatenate(gain_rows + shift_rows, axis=0)
    crossed = jnp.sum(found[:, 2 * micros : 2 * micros + each, :], axis=0)
    rest = send.shape[1] - 6 * micros - each
    block = exact_rows(rows_out) + mixed_rows + [plain[...], crossed]
    if rest > 0:
        block.append(jnp.zeros((rest, LANES), F32))
    block = jnp.concatenate(block, axis=0)
    send[...] = jnp.broadcast_to(block.astype(BF16)[None], send.shape)


def low_rows(turned, value_of, values, stats, gain, low, high, first, rows, tiles):
    micros, _, channels, width = values.shape
    tile = lax.axis_index("tile")
    masks = edges(channels, width)
    for micro in range(micros):
        part = slice(micro * channels, (micro + 1) * channels)
        centre, rstd = stats[part, 0:1], stats[part, 1:2]
        factor = gain * rstd
        slope_part, shift_part = rstd * turned[part, 0:1], turned[part, 1:2]
        for index in range(high):
            grad, value = value_of(micro, index)
            grad = factor * (grad - shift_part - (value - centre) * slope_part)
            if index + first < 0 or index + first >= rows:
                grad = grad * inside(tile, index + first, (tiles, rows))
            low[micro, index] = spread(grad.astype(BF16), masks)


def first_units(first_out, stats, micro, channels):
    part = slice(micro * channels, (micro + 1) * channels)
    centre, rstd = stats[part, 0:1], stats[part, 1:2]
    return lambda row: (first_out[micro, row] - centre) * rstd


def second_sums(total, weight, factors, stats, micro, micros, count):
    channels = weight.shape[1]
    factor, centre = factors[micro], stats[:, 2 * micro : 2 * micro + 1]
    columns = jnp.transpose(jnp.concatenate([total, jnp.zeros((8 - total.shape[0], LANES), F32)], axis=0))
    beta = factor * stats[:, 2 * micro + 1 : 2 * micro + 2] * columns[:, micro : micro + 1] * (1.0 / count)
    alpha = factor * columns[:, micros + micro : micros + micro + 1] * (1.0 / count)
    square = lax.dot_general(
        weight * beta, weight, (((0,), (0,)), ((), ())),
        preferred_element_type=F32, precision=lax.Precision.HIGHEST,
    )
    square = jnp.concatenate([square, square], axis=1)
    line = jnp.sum(weight * (alpha - beta * centre), axis=0, keepdims=True)
    line = jnp.concatenate([line, line], axis=1)

    def give(mixed, plain, crossed):
        mine = crossed[micro * channels : (micro + 1) * channels]
        return mixed - plain * line - jnp.sum(square * mine, axis=0, keepdims=True)

    return give


def middle_back_kernel(
    found, cols, grads, upper, top_stats, second_out, second_stats, slopes, w_up, w_up_t,
    own_mixed, own_plain, own_crossed, second_act, acts, first_out, first_stats, first_slopes, b_second_in,
    out, top_grad, weight_grad, top_gain_grad, top_shift_grad, expected, send,
    low, top_low, extras, second_dz, b_second, *, rows, tiles, each
):
    expand(b_second_in, b_second)
    scene = lax.axis_index("scene")
    micros, _, wide, width = grads.shape
    channels = second_out.shape[2]
    peers = found.shape[0]
    count = float(peers * rows * width)
    kept = 2 * micros
    total = jnp.sum(found[...].astype(F32), axis=0)
    mixed, plain = total[2 * kept : 2 * kept + micros], total[2 * kept + micros : 3 * kept]
    total = total[0:kept] + total[kept : 2 * kept]
    crossed = jnp.concatenate(
        [
            found[peer].astype(F32)[3 * kept : 3 * kept + each]
            for peer in range(-(-micros * channels // each))
        ],
        axis=0,
    )
    own_half(total[0:1] + total[1:2], scene, top_gain_grad)
    own_half(total[2:3] + total[3:4], scene, top_shift_grad)
    factors = [cols[:, 6:7] * top_stats[:, 2 * micro + 1 : 2 * micro + 2] for micro in range(micros)]
    wide_weight = w_up[...].astype(F32)
    turned = columns_of([total[index : index + 1] for index in range(2 * micros)]) * (1.0 / count)
    gain = cols[0:channels, 4:5]
    masks = edges(channels, width)
    second_rows = []
    for micro in range(micros):
        top_centre = top_stats[:, 2 * micro : 2 * micro + 1]
        top_slope = top_stats[:, 2 * micro + 1 : 2 * micro + 2] * turned[:, micro : micro + 1]
        top_shift = turned[:, micros + micro : micros + micro + 1]
        part = slice(micro * channels, (micro + 1) * channels)
        centre, rstd = second_stats[part, 0:1], second_stats[part, 1:2]
        gain_sum = jnp.zeros((channels, LANES), F32)
        shift_sum = jnp.zeros((channels, LANES), F32)
        for row in range(rows):
            grad = factors[micro] * (
                grads[micro, row] - top_shift - (upper[micro, row] - top_centre) * top_slope
            )
            grad = grad.astype(BF16)
            top_low[micro, row] = grad
            unit = (second_out[micro, row] - centre) * rstd
            grad = dot(w_up_t[...], grad) * slopes[micro, row, 0:channels]
            second_dz[micro, row] = grad
            shift_sum = shift_sum + fold(grad)
            gain_sum = gain_sum + fold(grad * unit)
        second_rows.append((shift_sum, gain_sum))
    parts = []
    for micro in range(micros):
        give = second_sums(total, wide_weight, factors, top_stats, micro, micros, count)
        whole = give(mixed[micro : micro + 1], plain[micro : micro + 1], crossed)
        extra = row_of(*second_rows[micro]) - give(
            own_mixed[micro : micro + 1], own_plain[micro : micro + 1], own_crossed[...]
        )
        expected[micro : micro + 1] = whole
        extras[micro : micro + 1] = extra
        parts.append(whole * (1.0 / count) + extra * (1.0 / (rows * width)))
    parts = columns_of(parts)
    for micro in range(micros):
        part = slice(micro * channels, (micro + 1) * channels)
        centre, rstd = second_stats[part, 0:1], second_stats[part, 1:2]
        factor = gain * rstd
        shift_part = parts[0:channels, micro : micro + 1]
        slope_part = parts[channels : 2 * channels, micro : micro + 1] * rstd
        for row in range(rows):
            grad = factor * (
                second_dz[micro, row] - shift_part - (second_out[micro, row] - centre) * slope_part
            )
            low[micro, row] = spread(grad.astype(BF16), masks)
    first_back(
        low, top_low, second_act, acts, first_out, first_stats, first_slopes, b_second, extras,
        out, top_grad, weight_grad, send, rows, tiles,
    )


def first_back(
    low, top_low, second_act, acts, first_out, first_stats, slopes, b_second, extras,
    out, top_grad, weight_grad, send, rows, tiles
):
    tile = lax.axis_index("tile")
    micros, _, channels, width = first_out.shape
    half = 6 * channels
    gain_sums, shift_sums = [], []
    for micro in range(micros):
        units = first_units(first_out, first_stats, micro, channels)
        gain_sum = jnp.zeros((channels, LANES), F32)
        shift_sum = jnp.zeros((channels, LANES), F32)
        for at in range(0, rows + 2, 2):
            if at == 0:
                parts = dot(b_second[:, half:], low[micro, 0:2].reshape(half, width))
            elif at == rows:
                parts = dot(b_second[:, :half], low[micro, rows - 2 : rows].reshape(half, width))
            else:
                parts = conv_pair(low, b_second, micro, at - 2, channels)
            for j in range(2):
                grad = parts[channels * j : channels * (j + 1)] * slopes[micro, at + j]
                if at + j == 0 or at + j == rows + 1:
                    grad = grad * inside(tile, at + j - 1, (tiles, rows))
                out[micro, at + j] = grad
                gain_sum = gain_sum + fold(grad * units(at + j))
                shift_sum = shift_sum + fold(grad)
        gain_sums.append(gain_sum)
        shift_sums.append(shift_sum)
        product = dot_lanes(
            jnp.concatenate([top_low[micro, row] for row in range(rows)], axis=1),
            jnp.concatenate([second_act[micro, row] for row in range(rows)], axis=1),
        )
        top_grad[...] = product if micro == 0 else top_grad[...] + product
    conv_grad(low, 0, acts, 0, weight_grad, rows)
    send_all(send, [row_of(*gain_sums), row_of(*shift_sums)] + [extras[m : m + 1] for m in range(micros)])


def conv_grad(low, low_first, values, value_first, total, rows):
    micros, _, channels, width = values.shape
    for micro in range(micros):
        grads = jnp.concatenate([low[micro, row + low_first] for row in range(rows)], axis=1)
        windows = jnp.concatenate(
            [
                values[micro, row + value_first : row + value_first + 3].reshape(3 * channels, width)
                for row in range(rows)
            ],
            axis=1,
        )
        product = dot_lanes(grads, windows)
        total[...] = product if micro == 0 else total[...] + product


def half_rows(total, half, scene):
    channels = 2 * half
    start = scene * half
    mine = jnp.concatenate(
        [total[b * channels + start : b * channels + start + half, :] for b in range(2, -1, -1)], axis=0
    )
    wing = mine[:, LANES:]
    cut = wing.shape[0] // 2
    return [mine[:, :LANES], jnp.concatenate([wing[:cut], wing[cut:]], axis=1)]


def pick_kernel(
    found, cols, grads, first_out, first_stats, b_first_in, where_rows,
    canvas, second_grad, top_grad, expected,
    send, gain_grad, shift_grad, second_gain_grad, second_shift_grad, low, grid, b_first, first_grad, whole,
    *, rows, tiles, each
):
    expand(b_first_in, b_first)
    scene = lax.axis_index("scene")
    micros, high, channels, width = grads.shape
    sums = sum_rows(found, 2 + micros)
    second = sum(sums[2:]) + jnp.sum(expected[...], axis=0, keepdims=True)
    own_half(second[:, :channels], scene, second_shift_grad)
    own_half(second[:, channels:], scene, second_gain_grad)
    sums = sums[:2]
    own_half(sums[0][:, :channels] + sums[0][:, channels:], scene, gain_grad)
    own_half(sums[1][:, :channels] + sums[1][:, channels:], scene, shift_grad)
    turned = columns_of(sums) * (1.0 / (found.shape[0] * rows * width))
    masks = edges(channels, width)
    for micro in range(micros):
        part = slice(micro * channels, (micro + 1) * channels)
        centre, rstd = first_stats[part, 0:1], first_stats[part, 1:2]
        factor = cols[0:channels, 2:3] * rstd
        slope_part, shift_part = rstd * turned[part, 0:1], turned[part, 1:2]
        for row in range(high):
            grad = grads[micro, row]
            if 1 <= row <= rows:
                grad = grad - shift_part - (first_out[micro, row] - centre) * slope_part
            low[micro, row] = spread((factor * grad).astype(BF16), masks)
    half = 6 * channels
    for micro in range(micros):
        for at in range(0, rows + 4, 2):
            if at == 0:
                parts = dot(b_first[:, half:], low[micro, 0:2].reshape(half, width))
            elif at == rows + 2:
                parts = dot(b_first[:, :half], low[micro, rows : rows + 2].reshape(half, width))
            else:
                parts = conv_pair(low, b_first, micro, at - 2, channels)
            grid[micro, at] = parts[:channels].astype(BF16)
            grid[micro, at + 1] = parts[channels:].astype(BF16)
    conv_grad(low, 0, canvas, 0, first_grad, high)
    half = channels // 2
    for s in range(2):
        parts = half_rows(first_grad, half, s) + half_rows(second_grad, half, s)
        mine = top_grad[s * channels : (s + 1) * channels, :]
        parts.append(jnp.concatenate([mine[:half], mine[half:]], axis=1))
        parts = jnp.concatenate(parts, axis=0)
        whole[s, 0 : parts.shape[0]] = parts
        if whole.shape[1] > parts.shape[0]:
            whole[s, parts.shape[0] :] = jnp.zeros((whole.shape[1] - parts.shape[0], LANES), F32)
    columns = jnp.transpose(where_rows[...])
    slots = columns.shape[0]
    lane = lax.broadcasted_iota(jnp.int32, (slots, width), 1).astype(F32)
    groups = []
    for group in range(3):
        start, first, count = ((0, rows - 2, 2), (2, 0, rows), (rows + 2, 0, 2))[group]
        picked = []
        for micro in range(micros):
            at = 2 * group + micro
            column = columns[:, at : at + 1] - 1.0
            column = column - jnp.floor(column * (1.0 / width)) * width
            chosen = jnp.where(lane == column, 1.0, 0.0).astype(BF16)
            place = jnp.floor((where_rows[at : at + 1] - 1.0) * (1.0 / width))
            here = dot_lanes(grid[micro, start : start + count].reshape(count * channels, width), chosen)
            total = jnp.zeros((channels, slots), F32)
            for r in range(count):
                total = total + jnp.where(
                    place == (first + r) * 1.0, here[r * channels : (r + 1) * channels], 0.0
                )
            picked.append(total)
        groups.append(jnp.transpose(jnp.concatenate(picked, axis=0)))
    capacity = slots // tiles
    block = send.shape[1]

    def filled(parts):
        missing = block - sum(part.shape[0] for part in parts)
        if missing > 0:
            parts = parts + [jnp.zeros((missing, LANES), F32)]
        return jnp.concatenate(parts, axis=0).astype(BF16)

    for spot in range(tiles):
        mine = slice(spot * capacity, (spot + 1) * capacity)
        send[2 * spot + scene] = filled([picked[mine] for picked in groups])
        send[2 * spot + 1 - scene] = filled([whole[s, spot * each : (spot + 1) * each] for s in range(2)])


def pillar_weights_kernel(rows, w_pillar, cols, pooled, out, lifted):
    micros, channels, wide = out.shape
    pillars = pooled.shape[2]
    inputs = w_pillar.shape[1]
    gain, shift = cols[0:channels, 0:1], cols[0:channels, 1:2]
    for micro in range(micros):
        lifted[...] = dot(w_pillar[...], rows[micro, 0:inputs])
        _, limit = pillar_notes(rows, micro, inputs, pillars)
        centre, rstd = pooled[micros + micro, :, 0:1], pooled[micros + micro, :, 1:2]
        pool = pooled[micro]
        for n in range(wide // pillars):
            piece = slice(n * pillars, (n + 1) * pillars)
            normed = (lifted[:, piece] - centre) * rstd * gain + shift
            gate = sigmoid(normed)
            act = normed * gate
            slope = gate + act * (1.0 - gate)
            out[micro, :, piece] = jnp.where(limit > n, jnp.exp(act - pool) * slope, 0.0).astype(BF16)


def pillar_back_kernel(found, rows_in, w_pillar, cols, pooled, factors, send, grads, lifted, rows, sems,
                       *, capacity, each):
    fetched = move(rows_in, rows, sems, 0)
    micros = rows.shape[0]
    _, channels, pillars = pooled.shape
    stats = pooled.at[micros : 2 * micros]
    inputs = w_pillar.shape[1]
    depth = rows.shape[2] // pillars
    scene = lax.axis_index("scene")
    peers = found.shape[0]
    slot_count = peers // 2 * capacity
    blocks = [found[2 * t + scene].astype(F32) for t in range(peers // 2)]
    before, own, after = [
        jnp.concatenate([block[group * capacity : (group + 1) * capacity] for block in blocks], axis=0)
        for group in range(3)
    ]
    gap = jnp.zeros((capacity, LANES), F32)
    returned = (
        own
        + jnp.concatenate([before[capacity:], gap], axis=0)
        + jnp.concatenate([gap, after[: slot_count - capacity]], axis=0)
    )
    turned = jnp.transpose(returned)
    place = lax.broadcasted_iota(jnp.int32, (slot_count, pillars), 0).astype(F32)
    gain = cols[0:channels, 0:1]
    gain_sums, shift_sums = [], []
    outer = jnp.zeros((16, channels), F32)
    fetched.wait()
    for micro in range(micros):
        lifted[...] = dot(w_pillar[...], rows[micro, 0:inputs])
        slot, _ = pillar_notes(rows, micro, inputs, pillars)
        chosen = jnp.where(place == slot, 1.0, 0.0).astype(BF16)
        back = dot(turned[micro * channels : (micro + 1) * channels].astype(BF16), chosen)
        centre, rstd = stats[micro, :, 0:1], stats[micro, :, 1:2]
        gain_sum = jnp.zeros((channels, pillars), F32)
        shift_sum = jnp.zeros((channels, pillars), F32)
        for n in range(depth):
            piece = slice(n * pillars, (n + 1) * pillars)
            grad = back * factors[micro, :, piece].astype(F32)
            grads[micro, :, piece] = grad
            gain_sum = gain_sum + grad * (lifted[:, piece] - centre)
            shift_sum = shift_sum + grad
        gain_sum = gain_sum * rstd
        gain_sums.append(gain_sum)
        shift_sums.append(shift_sum)
        scale = jnp.transpose(jnp.broadcast_to(rstd * gain, (channels, LANES)))[0:1]
        outer = outer + dot_lanes(rows[micro], grads[micro].astype(BF16)) * scale
    exact = jnp.concatenate([row_of(*gain_sums), row_of(*shift_sums)], axis=0)
    lines = [jnp.concatenate([outer[k : k + 1], outer[k + 1 : k + 2]], axis=1) for k in range(0, 10, 2)]
    weights = found[1 - scene].astype(F32)
    for t in range(1, peers // 2):
        weights = weights + found[2 * t + 1 - scene].astype(F32)
    rest = send.shape[2] - 9 - each
    for s in range(2):
        block = exact_rows(exact) + lines + [weights[s * each : (s + 1) * each]]
        if rest > 0:
            block.append(jnp.zeros((rest, LANES), F32))
        block = jnp.concatenate(block, axis=0).astype(BF16)
        send[:, s] = jnp.broadcast_to(block[None], (send.shape[0],) + block.shape)


def points_kernel(
    found, rows_in, grads, w_pillar, cols, pooled,
    points_grad, pillar_grad, gain_grad, shift_grad, first_grad, second_grad, up_grad, rows, lifted, sems,
    *, each
):
    fetched = move(rows_in, rows, sems, 0)
    scene = lax.axis_index("scene")
    micros, channels, _ = grads.shape
    stats = pooled.at[micros : 2 * micros]
    _, _, inputs, depth, pillars = points_grad.shape
    half = channels // 2
    total = jnp.sum(found[...].astype(F32), axis=0)
    total = jnp.concatenate([total[0:2] + total[2:4], total[4:9]], axis=0)
    own_half(total[0:1, :channels] + total[0:1, channels:], scene, gain_grad)
    own_half(total[1:2, :channels] + total[1:2, channels:], scene, shift_grad)
    turned = jnp.transpose(jnp.concatenate([total, jnp.zeros((1, LANES), F32)], axis=0))
    weight_grad = jnp.concatenate(
        [turned[(k % 2) * channels : (k % 2 + 1) * channels, 2 + k // 2 : 3 + k // 2] for k in range(inputs)],
        axis=1,
    )
    weight = jnp.transpose(w_pillar[...].astype(F32)).astype(BF16)
    fetched.wait()
    for micro in range(micros):
        lifted[...] = dot(w_pillar[...], rows[micro, 0:inputs])
        part = slice(micro * channels, (micro + 1) * channels)
        centre, rstd, inverse = stats[micro, :, 0:1], stats[micro, :, 1:2], stats[micro, :, 2:3]
        factor = cols[0:channels, 0:1] * rstd
        gain_part, shift_part = turned[part, 0:1], turned[part, 1:2]
        spun, mean = stats[micro, :, 16 : 16 + inputs], stats[micro, :, 32 : 32 + inputs]
        weight_grad = weight_grad - factor * (shift_part * mean + gain_part * rstd * spun)
        gain_part, shift_part = gain_part * inverse * rstd, shift_part * inverse
        _, limit = pillar_notes(rows, micro, inputs, pillars)
        for n in range(depth):
            piece = slice(n * pillars, (n + 1) * pillars)
            low = factor * (grads[micro, :, piece] - shift_part - (lifted[:, piece] - centre) * gain_part)
            low = jnp.where(limit > n, low, 0.0).astype(BF16)
            points_grad[micro, 0, :, n, :] = dot(weight, low)
    weight_grad = jnp.concatenate([weight_grad, jnp.zeros((channels, LANES - inputs), F32)], axis=1)
    weight_grad = jnp.transpose(weight_grad)[0:inputs]
    pillar_grad[...] = jnp.where(scene == 0, weight_grad[:, :half], weight_grad[:, half:])
    whole = jnp.concatenate(
        [
            (found[2 * t].astype(F32) + found[2 * t + 1].astype(F32))[9 : 9 + each]
            for t in range(found.shape[0] // 2)
        ],
        axis=0,
    )
    for index, out in enumerate((first_grad, second_grad)):
        base = index * 9 * half * channels // LANES
        lead = 3 * half
        mine = whole[base : base + lead]
        wing = whole[base + lead : base + lead + lead // 2]
        wing = jnp.concatenate([wing[:, :channels], wing[:, channels:]], axis=0)
        both = jnp.concatenate([mine, wing], axis=1)
        for a in range(3):
            for b in range(3):
                at = (3 * a + b) * channels
                out[:, at : at + channels] = both[b * half : (b + 1) * half, a * channels : (a + 1) * channels]
    base = 2 * 9 * half * channels // LANES
    top = whole[base : base + half]
    up_grad[...] = jnp.concatenate([top[:, :channels], top[:, channels:]], axis=0)


def swap(blocks, axes):
    return lax.all_to_all(blocks, axes, split_axis=0, concat_axis=0)


def shards(
    points, point_counts, pillar_tile, pillar_cell,
    pillar_weight, pillar_gain, pillar_shift,
    first_weight, first_gain, first_shift,
    second_weight, second_gain, second_shift,
    up_weight, up_gain, up_shift, cotangent,
):
    micros, _, inputs, depth, pillars = points.shape
    channels = up_weight.shape[1]
    upper = cotangent.shape[2]
    rows, width = cotangent.shape[3:]
    tiles = lax.axis_size("tile")
    scenes = lax.axis_size("scene")
    peers = tiles * scenes
    capacity = 2 * pillars // tiles
    slot_count = tiles * capacity
    half = channels // 2

    def vmem(shape, dtype):
        return pltpu.VMEM(shape, dtype)

    def grid(high, dtype=F32, lead=channels):
        return ((micros, high, lead, width), dtype)

    sums = ((peers, 2, LANES), F32)
    sources = (
        pillar_tile, pillar_cell, point_counts, points,
        first_weight, second_weight, up_weight, pillar_weight.T,
        pillar_gain, pillar_shift, first_gain, first_shift, second_gain, second_shift, up_gain, up_shift,
    )
    moments, packed, point_rows = run(
        functools.partial(moments_kernel, capacity=capacity),
        [
            ((tiles, scenes, 4, LANES), F32), ((layout(half, channels)[-1] + 16, LANES), BF16),
            ((micros, 16, depth * pillars), BF16),
        ],
        *sources,
        hbm=range(len(sources)), copies=len(sources), limit=WIDE_LIMIT,
        scratch=[vmem(source.shape, source.dtype) for source in sources]
        + [vmem((inputs * depth, pillars), F32)],
    )
    moments = swap(moments.reshape(peers, 4, LANES), BOTH)
    both = lax.all_gather(packed, "scene")
    taps = ((2 * channels, 12 * channels), BF16)
    compact = ((channels, 9 * channels), BF16)
    w_pillar, cols, l_first, l_second, b_first, b_second, w_up, w_up_t = run(
        functools.partial(unpack_kernel, inputs=inputs),
        [
            ((channels, inputs), BF16), ((LANES, 8), F32), compact, compact, compact, compact,
            ((upper, channels), BF16), ((channels, upper), BF16),
        ],
        both,
    )
    cot = cotangent[:, 0].transpose(0, 2, 1, 3)

    send, pooled = run(
        functools.partial(pillar_kernel, capacity=capacity),
        [((slot_count, 3 * LANES), BF16), ((2 * micros, channels, pillars), F32)],
        moments, point_rows, w_pillar, cols,
        scratch=[vmem((channels, depth * pillars), F32), vmem((channels, depth * pillars), F32)],
    )
    arrived = swap(send.reshape(tiles, capacity, 3 * LANES), "tile").reshape(slot_count, 3 * LANES)
    (cell_rows,) = run(
        functools.partial(cells_kernel, capacity=capacity),
        [((8, slot_count), F32)],
        moments,
        cost=pl.CostEstimate(flops=10**7, bytes_accessed=10**6, transcendentals=0),
    )
    (factors,) = run(
        pillar_weights_kernel,
        [((micros, channels, depth * pillars), BF16)],
        point_rows, w_pillar, cols, pooled,
        scratch=[vmem((channels, depth * pillars), F32)],
        cost=pl.CostEstimate(flops=10**7, bytes_accessed=10**6, transcendentals=0),
    )
    arrived, cot, factors = lax.optimization_barrier((arrived, cot, factors))

    first_out, canvas, send = run(
        functools.partial(canvas_kernel, rows=rows),
        [grid(rows + 2), grid(rows + 4, BF16), sums],
        arrived, cell_rows, l_first,
        scratch=[vmem(*grid(rows + 4, BF16, 3 * channels)), vmem(*taps)],
    )
    second_out, first_act, first_slopes, first_stats, send = run(
        functools.partial(second_kernel, rows=rows, tiles=tiles),
        [grid(rows), grid(rows + 2, BF16), grid(rows + 2), ((LANES, 8), F32), sums],
        swap(send, BOTH), cols, first_out, l_second,
        scratch=[vmem(*grid(rows + 2, BF16, 3 * channels)), vmem(*taps)],
    )
    part = -(-micros * channels // peers)
    second_act, up_out, slopes, plain, crossed, second_stats, send = run(
        functools.partial(up_kernel, rows=rows),
        [
            grid(rows, BF16), grid(rows, F32, upper), grid(rows, F32, 2 * channels), ((micros, LANES), F32),
            ((peers * part, LANES), F32), ((LANES, 8), F32), ((peers, -(-(2 * micros + part) // 8) * 8, LANES), F32),
        ],
        swap(send, BOTH), cols, second_out, w_up,
    )
    features, grads, mixed, top_stats, send = run(
        functools.partial(top_kernel, rows=rows, each=part),
        [
            ((micros, 1, upper, rows, width), BF16), grid(rows, F32, upper), ((micros, LANES), F32),
            ((LANES, 8), F32),
            ((peers, -(-(6 * micros + part) // 8) * 8, LANES), BF16),
        ],
        swap(send, BOTH), cols, up_out, cot, slopes, plain, w_up_t,
        scratch=[vmem((micros, width // LANES, upper * rows, LANES), F32)],
    )
    vector, top_vector, matrix = ((half,), F32), ((upper // 2,), F32), ((half, 9 * channels), F32)
    cross = ((3 * channels, 3 * channels), F32)
    first_dz, top_grad, second_cross, up_gain_grad, up_shift_grad, expected, send = run(
        functools.partial(middle_back_kernel, rows=rows, tiles=tiles, each=part),
        [
            grid(rows + 2), ((upper, channels), F32), cross, top_vector, top_vector, ((micros, LANES), F32),
            ((peers, 2 + micros, LANES), F32),
        ],
        swap(send, BOTH), cols, grads, up_out, top_stats, second_out, second_stats, slopes, w_up, w_up_t,
        mixed, plain, crossed, second_act, first_act, first_out, first_stats, first_slopes, b_second,
        scratch=[
            vmem(*grid(rows, BF16, 3 * channels)), vmem(*grid(rows, BF16, upper)), vmem((micros, LANES), F32),
            vmem(*grid(rows)), vmem(*taps),
        ],
    )
    length = (2 * 9 * half * channels + upper * half) // LANES
    each = -(-length // tiles)
    block = -(-max(3 * capacity, 2 * each) // 8) * 8
    send, first_gain_grad, first_shift_grad, second_gain_grad, second_shift_grad = run(
        functools.partial(pick_kernel, rows=rows, tiles=tiles, each=each),
        [((peers, block, LANES), BF16), vector, vector, vector, vector],
        swap(send, BOTH), cols, first_dz, first_out, first_stats, b_first, cell_rows,
        canvas, second_cross, top_grad, expected,
        scratch=[
            vmem(*grid(rows + 2, BF16, 3 * channels)), vmem(*grid(rows + 4, BF16)), vmem(*taps), vmem(*cross),
            vmem((scenes, tiles * each, LANES), F32),
        ],
    )
    block = -(-(9 + each) // 8) * 8
    send, pillar_dz = run(
        functools.partial(pillar_back_kernel, capacity=capacity, each=each),
        [((tiles, scenes, block, LANES), BF16), ((micros, channels, depth * pillars), F32)],
        swap(send, BOTH), point_rows, w_pillar, cols, pooled, factors,
        hbm=(1,),
        scratch=[vmem((channels, depth * pillars), F32), vmem((micros, 16, depth * pillars), BF16)],
        copies=1,
    )
    points_grad, pillar_grad, pillar_gain_grad, pillar_shift_grad, first_grad, second_grad, up_grad = run(
        functools.partial(points_kernel, each=each),
        [
            ((micros, 1, inputs, depth, pillars), F32), ((inputs, half), F32), vector, vector,
            matrix, matrix, ((upper // 2, channels), F32),
        ],
        swap(send.reshape(peers, block, LANES), BOTH), point_rows, pillar_dz, w_pillar, cols, pooled,
        hbm=(1,),
        scratch=[vmem((micros, 16, depth * pillars), BF16), vmem((channels, depth * pillars), F32)],
        copies=1,
    )
    return (
        features, points_grad,
        pillar_grad.T, pillar_gain_grad, pillar_shift_grad,
        first_grad, first_gain_grad, first_shift_grad,
        second_grad, second_gain_grad, second_shift_grad,
        up_grad, up_gain_grad, up_shift_grad,
    )


def solution(mesh):
    matrix, vector = P("scene", None), P("scene")
    grid = P(None, "scene", None, "tile", None)
    cloud = P(None, "scene", None, None, "tile")
    pillar = P(None, "scene", "tile")
    weights = (matrix, vector, vector) * 4
    return jax.shard_map(
        shards,
        mesh=mesh,
        in_specs=(cloud, pillar, pillar, pillar) + weights + (grid,),
        out_specs=(grid, cloud) + weights,
        check_vma=False,
    )
```

```python
import functools

import jax
import jax.numpy as jnp
from jax import lax
from jax.experimental import pallas as pl
from jax.experimental.pallas import tpu as pltpu
from jax.sharding import PartitionSpec as P

norm_eps = 0.001
BOTH = ("tile", "scene")
F32 = jnp.float32
BF16 = jnp.bfloat16
VMEM_LIMIT = 24 * 1024 * 1024
WIDE_LIMIT = 60 * 1024 * 1024
LANES = 128


def run(kernel, outs, *args, hbm=(), scratch=(), copies=0, cost=None, limit=VMEM_LIMIT):
    specs = [
        pl.BlockSpec(memory_space=pltpu.HBM if index in hbm else pltpu.VMEM) for index in range(len(args))
    ]
    scratch = list(scratch)
    if copies:
        scratch.append(pltpu.SemaphoreType.DMA((copies,)))
    return pl.pallas_call(
        kernel,
        out_shape=[jax.ShapeDtypeStruct(out[0], out[1]) for out in outs],
        in_specs=specs,
        out_specs=[
            pl.BlockSpec(memory_space=pltpu.HBM if len(out) > 2 else pltpu.VMEM) for out in outs
        ],
        scratch_shapes=scratch,
        compiler_params=pltpu.CompilerParams(vmem_limit_bytes=limit),
        cost_estimate=cost,
    )(*args)


def move(source, target, sems, index):
    copy = pltpu.make_async_copy(source, target, sems.at[index])
    copy.start()
    return copy


def dot(left, right, precision=None):
    return jnp.dot(left, right, preferred_element_type=F32, precision=precision)


def dot_lanes(left, right, precision=None):
    return lax.dot_general(
        left, right, (((1,), (1,)), ((), ())), preferred_element_type=F32, precision=precision
    )


def sigmoid(values):
    return 0.5 + 0.5 * jnp.tanh(0.5 * values)


def fold(values):
    total = values[:, :LANES]
    for start in range(LANES, values.shape[1], LANES):
        total = total + values[:, start : start + LANES]
    return total


def row_of(left, right=None):
    both = left if right is None else jnp.concatenate([left, right], axis=0)
    return jnp.sum(jnp.transpose(both), axis=0, keepdims=True)


def columns_of(rows):
    rows = rows + [jnp.zeros((8 - len(rows), LANES), F32)] if len(rows) < 8 else rows
    return jnp.transpose(jnp.concatenate(rows, axis=0))


def inside(tile, row, height):
    tiles, rows = height
    place = tile * rows + row
    return jnp.where((place >= 0) & (place < tiles * rows), 1.0, 0.0).astype(F32)


def send_all(ref, rows):
    for index, row in enumerate(rows):
        ref[:, index : index + 1, :] = jnp.broadcast_to(row[None], (ref.shape[0], 1, LANES))


def pooled_stats(means, squares, count):
    peers = means.shape[0]
    mean = jnp.sum(means, axis=0, keepdims=True) * (1.0 / peers)
    away = means - mean
    spread = jnp.sum(squares + count * away * away, axis=0, keepdims=True) * (1.0 / (peers * count))
    return mean, lax.rsqrt(spread + norm_eps)


def stat_columns(found, count):
    return columns_of(list(pooled_stats(found[:, 0, :], found[:, 1, :], count)))


def sum_rows(found, lines):
    return [jnp.sum(found[:, index, :], axis=0, keepdims=True) for index in range(lines)]


def own_half(row, scene, out):
    size = out.shape[0]
    out[...] = jnp.where(scene == 0, row[:, 0:size], row[:, size : 2 * size]).reshape(size)


def edges(channels, width):
    lane = lax.broadcasted_iota(jnp.int32, (channels, width), 1)
    return lane > 0, lane < width - 1


def spread(row, masks):
    zero = jnp.zeros_like(row)
    left = jnp.where(masks[0], pltpu.roll(row, 1, 1), zero)
    right = jnp.where(masks[1], pltpu.roll(row, row.shape[1] - 1, 1), zero)
    return jnp.concatenate([left, row, right], axis=0)


def layout(half, channels):
    first = 0
    second = first + half * -(-9 * channels // LANES)
    up = second + half * -(-9 * channels // LANES)
    vectors = up + channels
    return first, second, up, vectors, vectors + 16


def widen(value):
    missing = LANES - value.shape[1]
    if missing == 0:
        return value
    return jnp.concatenate([value, jnp.zeros((value.shape[0], missing), value.dtype)], axis=1)


def pack(held, out):
    first, second, up, pillar = held[:4]
    half, channels = first.shape[0], up.shape[1]
    starts = layout(half, channels)
    for ref, start in ((first, starts[0]), (second, starts[1])):
        for j in range(-(-9 * channels // LANES)):
            out[start + j * half : start + (j + 1) * half, :] = widen(
                ref[:, j * LANES : min((j + 1) * LANES, 9 * channels)]
            )
    out[starts[2] : starts[2] + channels, :] = widen(up[...])
    rows = [vector[...].astype(F32).reshape(1, -1) for vector in held[4:]]
    rows = [widen(row) for row in rows] + [jnp.zeros((16 - len(rows), LANES), F32)]
    turned = widen(pillar[...].astype(F32))
    rows += [turned, jnp.zeros((16 - turned.shape[0], LANES), F32)]
    out[starts[3] :, :] = jnp.concatenate(rows, axis=0).astype(BF16)


def unpack_kernel(
    both, w_pillar, cols, l_first, l_second, b_first, b_second, w_up, w_up_t, *, inputs
):
    half = w_pillar.shape[0] // 2
    channels = 2 * half
    starts = layout(half, channels)
    tiles = -(-9 * channels // LANES)

    def wide(start):
        return jnp.concatenate(
            [
                jnp.concatenate(
                    [both[s, start + j * half : start + (j + 1) * half, :] for j in range(tiles)], axis=1
                )
                for s in range(2)
            ],
            axis=0,
        ).astype(F32)

    up = jnp.concatenate(
        [both[s, starts[2] : starts[2] + channels, 0:channels] for s in range(2)], axis=0
    )
    w_up[...] = up
    w_up_t[...] = jnp.transpose(up.astype(F32)).astype(BF16)
    turned = jnp.concatenate(
        [both[s, starts[4] : starts[4] + 16, 0:half].astype(F32) for s in range(2)], axis=1
    )
    w_pillar[...] = jnp.transpose(widen(turned))[0:channels, 0:inputs].astype(BF16)
    vectors = [both[s, starts[3] : starts[3] + 16, :].astype(F32) for s in range(2)]
    rows = []
    for index in range(8):
        size = half if index < 6 else channels
        row = jnp.concatenate([vectors[s][index : index + 1, 0:size] for s in range(2)], axis=1)
        rows.append(jnp.concatenate([row] * (LANES // (2 * size)), axis=1))
    cols[...] = columns_of(rows)
    for weight, ahead, back in ((wide(starts[0]), l_first, b_first), (wide(starts[1]), l_second, b_second)):
        turned = jnp.transpose(weight)
        ahead[...] = weight[:, : 9 * channels].astype(BF16)
        back[...] = jnp.concatenate(
            [turned[tap * channels : (tap + 1) * channels] for tap in range(8, -1, -1)], axis=1
        ).astype(BF16)


def slot_line(wide, depth, inputs):
    return jnp.concatenate([wide[pl.ds(n, inputs, stride=depth), :] for n in range(depth)], axis=1)


def slot_mask(count, depth):
    return jnp.concatenate([jnp.where(count > n, 1.0, 0.0) for n in range(depth)], axis=1)


def ranks(tile):
    pillars = tile.shape[1]
    across = jnp.broadcast_to(tile, (pillars, pillars))
    down = jnp.transpose(across)
    row = lax.broadcasted_iota(jnp.int32, (pillars, pillars), 0)
    col = lax.broadcasted_iota(jnp.int32, (pillars, pillars), 1)
    return jnp.sum(jnp.where((across == down) & (row < col), 1.0, 0.0), axis=0, keepdims=True)


def moments_kernel(*refs, capacity):
    number = 4
    sources, out = refs[:number], refs[number]
    held, wide, sems = refs[number + 1 : 2 * number + 1], refs[-2], refs[-1]
    copies = [move(sources[i], held[i], sems, i) for i in range(number)]
    tiles, cells, counts, points = held
    micros, _, inputs, depth, pillars = points.shape
    peers, scenes = out.shape[:2]
    copies[0].wait()
    copies[1].wait()
    lines = []
    for micro in range(micros):
        tile = tiles[micro].astype(F32)
        cell = (cells[micro] + 1).astype(F32)
        high = jnp.floor(cell * (1.0 / 16.0))
        low = cell - high * 16.0
        rank = ranks(tile)
        spot = lax.broadcasted_iota(jnp.int32, (capacity, pillars), 0).astype(F32)
        placed = jnp.where(spot == rank, 1.0, 0.0).astype(BF16)
        peer = lax.broadcasted_iota(jnp.int32, (peers, pillars), 0).astype(F32)
        for group in range(3):
            named = tile == peer + (group - 1.0)
            lines.append(
                16.0 * dot_lanes(jnp.where(named, high, 0.0).astype(BF16), placed)
                + dot_lanes(jnp.where(named, low, 0.0).astype(BF16), placed)
            )
    used = 3 * micros * capacity
    line = jnp.concatenate(lines + [jnp.zeros((peers, LANES - used), F32)], axis=1).reshape(peers, 1, LANES)
    for scene in range(scenes):
        out[:, scene, micros : micros + 1, :] = line
    copies[2].wait()
    copies[3].wait()
    parts, mean_rows, totals = [], [], []
    for micro in range(micros):
        wide[...] = points[micro, 0].astype(F32).reshape(inputs * depth, pillars)
        rows = slot_line(wide, depth, inputs)
        mask = slot_mask(counts[micro], depth)
        total = jnp.sum(mask, axis=1, keepdims=True)
        mean = jnp.sum(rows * mask, axis=1, keepdims=True) / total
        centred = jnp.concatenate(
            [(rows - mean) * mask, jnp.zeros((16 - inputs, rows.shape[1]), F32)], axis=0
        )
        high = centred.astype(BF16)
        parts += [high, (centred - high.astype(F32)).astype(BF16)]
        lane = lax.broadcasted_iota(jnp.int32, (inputs, inputs), 1)
        diagonal = lax.broadcasted_iota(jnp.int32, (inputs, inputs), 0) == lane
        mean_rows.append(jnp.sum(jnp.where(diagonal, mean, 0.0), axis=0, keepdims=True))
        totals.append(total)
    parts = jnp.concatenate(parts, axis=0)
    every = dot_lanes(parts, parts)
    for micro in range(micros):
        at = 32 * micro
        square = every[at : at + 32, at : at + 32]
        products = (
            square[0:inputs, 0:inputs] + square[16 : 16 + inputs, 0:inputs]
            + square[0:inputs, 16 : 16 + inputs] + square[16 : 16 + inputs, 16 : 16 + inputs]
        )
        row = jnp.concatenate(
            [products[k : k + 1] for k in range(inputs)]
            + [mean_rows[micro], totals[micro], jnp.zeros((1, LANES - inputs * inputs - inputs - 1), F32)],
            axis=1,
        )
        for scene in range(scenes):
            out[:, scene, micro : micro + 1, :] = jnp.broadcast_to(row[None], (peers, 1, LANES))


def pack_kernel(*refs, capacity):
    number = 15
    sources, packed, lines_out = refs[:number], refs[number], refs[number + 1]
    held, wide, sems = refs[number + 2 : 2 * number + 2], refs[-2], refs[-1]
    copies = [move(sources[i], held[i], sems, i) for i in range(number)]
    for copy in copies:
        copy.wait()
    tiles, counts, points = held[:3]
    pack(held[3:], packed)
    micros, _, inputs, depth, pillars = points.shape
    for micro in range(micros):
        tile = tiles[micro].astype(F32)
        wide[...] = points[micro, 0].astype(F32).reshape(inputs * depth, pillars)
        rows = slot_line(wide, depth, inputs)
        notes = jnp.concatenate([tile * capacity + ranks(tile), counts[micro].astype(F32)], axis=0)
        notes = jnp.concatenate([notes, jnp.zeros((2, rows.shape[1] - pillars), F32)], axis=1)
        lines_out[micro] = jnp.concatenate(
            [rows, notes, jnp.zeros((14 - inputs, rows.shape[1]), F32)], axis=0
        ).astype(BF16)


def cells_kernel(found, rows, *, capacity):
    scene = lax.axis_index("scene")
    slots = rows.shape[1]
    peers = found.shape[0]
    values = found[:, 2, :]
    slot = lax.broadcasted_iota(jnp.int32, (slots, peers), 0)
    peer = lax.broadcasted_iota(jnp.int32, (slots, peers), 1)
    lane = lax.broadcasted_iota(jnp.int32, (slots, LANES), 1)
    row = lax.broadcasted_iota(jnp.int32, (slots, LANES), 0)
    result = jnp.zeros((slots, LANES), F32)
    chosen = jnp.where(peer == 2 * (slot // capacity) + scene, 1.0, 0.0)
    spread = dot(chosen, values, lax.Precision.HIGHEST)
    for micro in range(2):
        for group in range(3):
            mine = jnp.where(lane == (3 * micro + group) * capacity + row % capacity, spread, 0.0)
            column = jnp.sum(mine, axis=1, keepdims=True)
            result = jnp.where(lane == 2 * group + micro, column, result)
    rows[...] = jnp.transpose(result)[0:8]


def pillar_notes(rows, micro, inputs, pillars):
    notes = rows[micro, :, 0:pillars].astype(F32)
    return notes[inputs : inputs + 1], notes[inputs + 1 : inputs + 2]


def pillar_kernel(
    found, point_rows, w_pillar, cols, send, pooled, lifted, acts, *, capacity
):
    micros = point_rows.shape[0]
    channels, inputs = w_pillar.shape
    pillars = pooled.shape[2]
    depth = point_rows.shape[2] // pillars
    weight = w_pillar[...]
    wide_weight = weight.astype(F32)
    rows_out = send.shape[0]
    square = inputs * inputs
    stacked, slot_rows = [], []
    for micro in range(micros):
        lifted[...] = dot(weight, point_rows[micro, 0:inputs])
        moments = found[:, micro, :]
        sizes = moments[:, square + inputs : square + inputs + 1]
        means = moments[:, square : square + inputs]
        count = jnp.sum(sizes, axis=0, keepdims=True)
        mean = jnp.sum(means * sizes, axis=0, keepdims=True) / count
        away = means - mean
        products = lax.dot_general(
            away * sizes, away, (((0,), (0,)), ((), ())),
            preferred_element_type=F32, precision=lax.Precision.HIGHEST,
        )
        summed = jnp.sum(moments, axis=0, keepdims=True)
        products = products + jnp.concatenate(
            [summed[:, k * inputs : (k + 1) * inputs] for k in range(inputs)], axis=0
        )
        cov = products / count
        spun = wide_weight[:, 0:1] * cov[0:1]
        for k in range(1, inputs):
            spun = spun + wide_weight[:, k : k + 1] * cov[k : k + 1]
        spread = jnp.sum(spun * wide_weight, axis=1, keepdims=True)
        centre = jnp.sum(wide_weight * mean, axis=1, keepdims=True)
        rstd = lax.rsqrt(spread + norm_eps)
        inverse = jnp.broadcast_to(1.0 / count, (channels, 1))
        pooled[micros + micro] = jnp.concatenate(
            [
                centre, rstd, inverse, jnp.zeros((channels, 13), F32),
                spun, jnp.zeros((channels, 16 - inputs), F32),
                jnp.broadcast_to(mean, (channels, inputs)), jnp.zeros((channels, LANES - 32 - inputs), F32),
            ],
            axis=1,
        )
        scale = rstd * cols[0:channels, 0:1]
        shift = cols[0:channels, 1:2]
        slot, limit = pillar_notes(point_rows, micro, inputs, pillars)
        slot_rows.append(slot)
        top = jnp.full((channels, pillars), -jnp.inf, F32)
        for n in range(depth):
            piece = slice(n * pillars, (n + 1) * pillars)
            normed = (lifted[:, piece] - centre) * scale + shift
            act = normed * sigmoid(normed)
            acts[:, piece] = act
            top = jnp.maximum(top, jnp.where(limit > n, act, -jnp.inf))
        total = jnp.zeros((channels, pillars), F32)
        for n in range(depth):
            piece = slice(n * pillars, (n + 1) * pillars)
            total = total + jnp.where(limit > n, jnp.exp(acts[:, piece] - top), 0.0)
        result = top + jnp.log(total)
        pooled[micro] = result
        parts = [jnp.zeros((channels, pillars), F32)] * micros
        parts[micro] = result.astype(BF16).astype(F32)
        stacked.append(jnp.transpose(jnp.concatenate(parts, axis=0)))
    values = jnp.concatenate(stacked, axis=0).astype(BF16)
    for group in range(3):
        place = lax.broadcasted_iota(jnp.int32, (rows_out, pillars), 0) + (group - 1) * capacity
        chosen = jnp.concatenate(
            [jnp.where(place.astype(F32) == row, 1.0, 0.0) for row in slot_rows], axis=1
        ).astype(BF16)
        send[:, group * LANES : (group + 1) * LANES] = dot(chosen, values).astype(BF16)


def own_stats(ref, first_row, rows, send):
    micros, _, channels, width = ref.shape
    sums, squares = [], []
    for micro in range(micros):
        total = fold(ref[micro, first_row])
        for row in range(first_row + 1, first_row + rows):
            total = total + fold(ref[micro, row])
        sums.append(total * (1.0 / (rows * width)))
    means = [jnp.sum(total, axis=1, keepdims=True) for total in sums]
    for micro in range(micros):
        spread = jnp.zeros(sums[micro].shape, F32)
        for row in range(first_row, first_row + rows):
            away = ref[micro, row] - means[micro]
            spread = spread + fold(away * away)
        squares.append(spread)
    if channels == LANES:
        send_all(send, [row_of(part) for part in sums + squares])
    else:
        send_all(send, [row_of(*sums), row_of(*squares)])


def expand(taps, weight):
    channels, length = taps.shape
    gap = jnp.zeros((channels, length // 3), BF16)
    weight[0:channels] = jnp.concatenate([taps[...], gap], axis=1)
    weight[channels : 2 * channels] = jnp.concatenate([gap, taps[...]], axis=1)


def conv_pair(source, weight, micro, at, channels):
    window = source[micro, at : at + 4].reshape(12 * channels, source.shape[3])
    return dot(weight[...], window)


def conv_rows(source, weight, out, shape):
    micros, high, channels, width = shape
    for micro in range(micros):
        for at in range(0, high, 2):
            both = conv_pair(source, weight, micro, at, channels)
            out[micro, at] = both[:channels].astype(out.dtype)
            out[micro, at + 1] = both[channels:].astype(out.dtype)


def canvas_kernel(found, where_rows, l_first_in, out, kept, send, canvas, l_first, *, rows):
    expand(l_first_in, l_first)
    columns = jnp.transpose(where_rows[...])
    scenes, high, channels, width = out.shape
    masks = edges(channels, width)
    slots = found.shape[0]
    lane = lax.broadcasted_iota(jnp.int32, (slots, width), 1).astype(F32)
    for group in range(3):
        values = jnp.transpose(found[:, group * LANES : (group + 1) * LANES].astype(F32))
        first, count = ((rows - 2, 2), (0, rows), (0, 2))[group]
        for scene in range(scenes):
            at = 2 * group + scene
            column = columns[:, at : at + 1] - 1.0
            column = column - jnp.floor(column * (1.0 / width)) * width
            row = jnp.floor((where_rows[at : at + 1] - 1.0) * (1.0 / width))
            mine = values[scene * channels : (scene + 1) * channels]
            placed = jnp.concatenate(
                [jnp.where(row == r * 1.0, mine, 0.0) for r in range(first, first + count)], axis=0
            ).astype(BF16)
            chosen = jnp.where(lane == column, 1.0, 0.0).astype(BF16)
            grid = dot(placed, chosen).astype(BF16)
            start = (0, 2, rows + 2)[group]
            for r in range(count):
                row = grid[r * channels : (r + 1) * channels]
                canvas[scene, start + r] = spread(row, masks)
                kept[scene, start + r] = row
    conv_rows(canvas, l_first, out, out.shape)
    own_stats(out, 1, rows, send)


def second_kernel(found, cols, first_out, l_second_in, out, kept, slopes, stats, send, acts, l_second,
                  *, rows, tiles):
    expand(l_second_in, l_second)
    micros, high, channels, width = first_out.shape
    tile = lax.axis_index("tile")
    turned = stat_columns(found, float(rows * width))
    stats[...] = turned
    masks = edges(channels, width)
    for micro in range(micros):
        part = slice(micro * channels, (micro + 1) * channels)
        centre = turned[part, 0:1]
        scale = turned[part, 1:2] * cols[0:channels, 2:3]
        shift = cols[0:channels, 3:4]

        for row in range(high):
            normed = (first_out[micro, row] - centre) * scale + shift
            gate = sigmoid(normed)
            act = normed * gate
            slopes[micro, row] = gate + act * (1.0 - gate)
            if row == 0 or row == high - 1:
                act = act * inside(tile, row - 1, (tiles, rows))
            act = act.astype(BF16)
            acts[micro, row] = spread(act, masks)
            kept[micro, row] = act
    conv_rows(acts, l_second, out, out.shape)
    own_stats(out, 0, rows, send)


def up_kernel(found, cols, second_out, w_up, acts, upper, slopes, plain, crossed, stats, send, *, rows):
    micros, _, channels, width = second_out.shape
    peers = send.shape[0]
    each = crossed.shape[0] // peers
    turned = stat_columns(found, float(rows * width))
    stats[...] = turned
    gain, shift = cols[0:channels, 4:5], cols[0:channels, 5:6]
    lines = []
    for micro in range(micros):
        part = slice(micro * channels, (micro + 1) * channels)
        centre, rstd = turned[part, 0:1], turned[part, 1:2]
        slope_sum = jnp.zeros((channels, LANES), F32)
        unit_sum = jnp.zeros((channels, LANES), F32)
        for row in range(rows):
            unit = (second_out[micro, row] - centre) * rstd
            normed = unit * gain + shift
            gate = sigmoid(normed)
            act = normed * gate
            slope = gate + act * (1.0 - gate)
            sloped = slope * unit
            slope_sum = slope_sum + fold(slope)
            unit_sum = unit_sum + fold(sloped)
            slopes[micro, row] = jnp.concatenate([slope, sloped], axis=0)
            act = act.astype(BF16)
            acts[micro, row] = act
            upper[micro, row] = dot(w_up[...], act)
        lines.append(row_of(slope_sum, unit_sum).astype(BF16).astype(F32))
        crossed[micro * channels : (micro + 1) * channels] = dot_lanes(
            jnp.concatenate([acts[micro, row] for row in range(rows)], axis=1),
            jnp.concatenate([slopes[micro, row].astype(BF16) for row in range(rows)], axis=1),
        )
    plain[...] = jnp.concatenate(lines, axis=0)
    used = micros * channels
    if crossed.shape[0] > used:
        crossed[used:] = jnp.zeros((crossed.shape[0] - used, LANES), F32)
    if 2 * micros + each < send.shape[1]:
        send[...] = jnp.zeros(send.shape, F32)
    for peer in range(peers):
        send[peer, 2 * micros : 2 * micros + each] = crossed[peer * each : (peer + 1) * each]
    own_stats(upper, 0, rows, send)


def exact_rows(rows):
    high = rows.astype(BF16).astype(F32)
    return [high, rows - high]


def top_kernel(
    found, cols, upper, cot, slopes, plain, w_up_t, features, grads, mixed, stats, send, ordered, *, rows, each
):
    micros, _, wide, width = upper.shape
    channels = w_up_t.shape[0]
    lines = []
    for micro in range(micros):
        lines += list(pooled_stats(found[:, micro, :], found[:, micros + micro, :], float(rows * width)))
    turned = columns_of(lines)
    stats[...] = turned
    gain, shift = cols[:, 6:7], cols[:, 7:8]
    gain_rows, shift_rows, mixed_rows = [], [], []
    for micro in range(micros):
        centre, rstd = turned[:, 2 * micro : 2 * micro + 1], turned[:, 2 * micro + 1 : 2 * micro + 2]
        factor = gain * rstd
        gain_sum = jnp.zeros((wide, LANES), F32)
        shift_sum = jnp.zeros((wide, LANES), F32)
        mixed_sum = jnp.zeros((2 * channels, LANES), F32)
        for row in range(rows):
            unit = (upper[micro, row] - centre) * rstd
            normed = unit * gain + shift
            gate = sigmoid(normed)
            act = normed * gate
            grad = cot[micro, row].astype(F32) * (gate + act * (1.0 - gate))
            for j in range(width // LANES):
                ordered[micro, j, pl.ds(row, wide, stride=rows), :] = act[:, j * LANES : (j + 1) * LANES]
            grads[micro, row] = grad
            gain_sum = gain_sum + fold(grad * unit)
            shift_sum = shift_sum + fold(grad)
            below = dot(w_up_t[...], (grad * factor).astype(BF16))
            mixed_sum = mixed_sum + fold(
                slopes[micro, row] * jnp.concatenate([below, below], axis=0)
            )
        gain_rows.append(row_of(gain_sum))
        shift_rows.append(row_of(shift_sum))
        mixed_rows.append(row_of(mixed_sum).astype(BF16).astype(F32))
        line = jnp.concatenate([ordered[micro, j].astype(BF16) for j in range(width // LANES)], axis=1)
        features[micro, 0] = line.reshape(wide, rows, width)
    mixed[...] = jnp.concatenate(mixed_rows, axis=0)
    rows_out = jnp.concatenate(gain_rows + shift_rows, axis=0)
    crossed = jnp.sum(found[:, 2 * micros : 2 * micros + each, :], axis=0)
    rest = send.shape[1] - 6 * micros - each
    block = exact_rows(rows_out) + mixed_rows + [plain[...], crossed]
    if rest > 0:
        block.append(jnp.zeros((rest, LANES), F32))
    block = jnp.concatenate(block, axis=0)
    send[...] = jnp.broadcast_to(block.astype(BF16)[None], send.shape)


def low_rows(turned, value_of, values, stats, gain, low, high, first, rows, tiles):
    micros, _, channels, width = values.shape
    tile = lax.axis_index("tile")
    masks = edges(channels, width)
    for micro in range(micros):
        part = slice(micro * channels, (micro + 1) * channels)
        centre, rstd = stats[part, 0:1], stats[part, 1:2]
        factor = gain * rstd
        slope_part, shift_part = rstd * turned[part, 0:1], turned[part, 1:2]
        for index in range(high):
            grad, value = value_of(micro, index)
            grad = factor * (grad - shift_part - (value - centre) * slope_part)
            if index + first < 0 or index + first >= rows:
                grad = grad * inside(tile, index + first, (tiles, rows))
            low[micro, index] = spread(grad.astype(BF16), masks)


def first_units(first_out, stats, micro, channels):
    part = slice(micro * channels, (micro + 1) * channels)
    centre, rstd = stats[part, 0:1], stats[part, 1:2]
    return lambda row: (first_out[micro, row] - centre) * rstd


def second_sums(total, weight, factors, stats, micro, micros, count):
    channels = weight.shape[1]
    factor, centre = factors[micro], stats[:, 2 * micro : 2 * micro + 1]
    columns = jnp.transpose(jnp.concatenate([total, jnp.zeros((8 - total.shape[0], LANES), F32)], axis=0))
    beta = factor * stats[:, 2 * micro + 1 : 2 * micro + 2] * columns[:, micro : micro + 1] * (1.0 / count)
    alpha = factor * columns[:, micros + micro : micros + micro + 1] * (1.0 / count)
    square = lax.dot_general(
        weight * beta, weight, (((0,), (0,)), ((), ())),
        preferred_element_type=F32, precision=lax.Precision.HIGHEST,
    )
    square = jnp.concatenate([square, square], axis=1)
    line = jnp.sum(weight * (alpha - beta * centre), axis=0, keepdims=True)
    line = jnp.concatenate([line, line], axis=1)

    def give(mixed, plain, crossed):
        mine = crossed[micro * channels : (micro + 1) * channels]
        return mixed - plain * line - jnp.sum(square * mine, axis=0, keepdims=True)

    return give


def middle_back_kernel(
    found, cols, grads, upper, top_stats, second_out, second_stats, slopes, w_up, w_up_t,
    own_mixed, own_plain, own_crossed, second_act, acts, first_out, first_stats, first_slopes, b_second_in,
    out, top_grad, weight_grad, top_gain_grad, top_shift_grad, expected, send,
    low, top_low, extras, second_dz, b_second, *, rows, tiles, each
):
    expand(b_second_in, b_second)
    scene = lax.axis_index("scene")
    micros, _, wide, width = grads.shape
    channels = second_out.shape[2]
    peers = found.shape[0]
    count = float(peers * rows * width)
    kept = 2 * micros
    total = jnp.sum(found[...].astype(F32), axis=0)
    mixed, plain = total[2 * kept : 2 * kept + micros], total[2 * kept + micros : 3 * kept]
    total = total[0:kept] + total[kept : 2 * kept]
    crossed = jnp.concatenate(
        [
            found[peer].astype(F32)[3 * kept : 3 * kept + each]
            for peer in range(-(-micros * channels // each))
        ],
        axis=0,
    )
    own_half(total[0:1] + total[1:2], scene, top_gain_grad)
    own_half(total[2:3] + total[3:4], scene, top_shift_grad)
    factors = [cols[:, 6:7] * top_stats[:, 2 * micro + 1 : 2 * micro + 2] for micro in range(micros)]
    wide_weight = w_up[...].astype(F32)
    turned = columns_of([total[index : index + 1] for index in range(2 * micros)]) * (1.0 / count)
    gain = cols[0:channels, 4:5]
    masks = edges(channels, width)
    second_rows = []
    for micro in range(micros):
        top_centre = top_stats[:, 2 * micro : 2 * micro + 1]
        top_slope = top_stats[:, 2 * micro + 1 : 2 * micro + 2] * turned[:, micro : micro + 1]
        top_shift = turned[:, micros + micro : micros + micro + 1]
        part = slice(micro * channels, (micro + 1) * channels)
        centre, rstd = second_stats[part, 0:1], second_stats[part, 1:2]
        gain_sum = jnp.zeros((channels, LANES), F32)
        shift_sum = jnp.zeros((channels, LANES), F32)
        for row in range(rows):
            grad = factors[micro] * (
                grads[micro, row] - top_shift - (upper[micro, row] - top_centre) * top_slope
            )
            grad = grad.astype(BF16)
            top_low[micro, row] = grad
            unit = (second_out[micro, row] - centre) * rstd
            grad = dot(w_up_t[...], grad) * slopes[micro, row, 0:channels]
            second_dz[micro, row] = grad
            shift_sum = shift_sum + fold(grad)
            gain_sum = gain_sum + fold(grad * unit)
        second_rows.append((shift_sum, gain_sum))
    parts = []
    for micro in range(micros):
        give = second_sums(total, wide_weight, factors, top_stats, micro, micros, count)
        whole = give(mixed[micro : micro + 1], plain[micro : micro + 1], crossed)
        extra = row_of(*second_rows[micro]) - give(
            own_mixed[micro : micro + 1], own_plain[micro : micro + 1], own_crossed[...]
        )
        expected[micro : micro + 1] = whole
        extras[micro : micro + 1] = extra
        parts.append(whole * (1.0 / count) + extra * (1.0 / (rows * width)))
    parts = columns_of(parts)
    for micro in range(micros):
        part = slice(micro * channels, (micro + 1) * channels)
        centre, rstd = second_stats[part, 0:1], second_stats[part, 1:2]
        factor = gain * rstd
        shift_part = parts[0:channels, micro : micro + 1]
        slope_part = parts[channels : 2 * channels, micro : micro + 1] * rstd
        for row in range(rows):
            grad = factor * (
                second_dz[micro, row] - shift_part - (second_out[micro, row] - centre) * slope_part
            )
            low[micro, row] = spread(grad.astype(BF16), masks)
    first_back(
        low, top_low, second_act, acts, first_out, first_stats, first_slopes, b_second, extras,
        out, top_grad, weight_grad, send, rows, tiles,
    )


def first_back(
    low, top_low, second_act, acts, first_out, first_stats, slopes, b_second, extras,
    out, top_grad, weight_grad, send, rows, tiles
):
    tile = lax.axis_index("tile")
    micros, _, channels, width = first_out.shape
    half = 6 * channels
    gain_sums, shift_sums = [], []
    for micro in range(micros):
        units = first_units(first_out, first_stats, micro, channels)
        gain_sum = jnp.zeros((channels, LANES), F32)
        shift_sum = jnp.zeros((channels, LANES), F32)
        for at in range(0, rows + 2, 2):
            if at == 0:
                parts = dot(b_second[:, half:], low[micro, 0:2].reshape(half, width))
            elif at == rows:
                parts = dot(b_second[:, :half], low[micro, rows - 2 : rows].reshape(half, width))
            else:
                parts = conv_pair(low, b_second, micro, at - 2, channels)
            for j in range(2):
                grad = parts[channels * j : channels * (j + 1)] * slopes[micro, at + j]
                if at + j == 0 or at + j == rows + 1:
                    grad = grad * inside(tile, at + j - 1, (tiles, rows))
                out[micro, at + j] = grad
                gain_sum = gain_sum + fold(grad * units(at + j))
                shift_sum = shift_sum + fold(grad)
        gain_sums.append(gain_sum)
        shift_sums.append(shift_sum)
        product = dot_lanes(
            jnp.concatenate([top_low[micro, row] for row in range(rows)], axis=1),
            jnp.concatenate([second_act[micro, row] for row in range(rows)], axis=1),
        )
        top_grad[...] = product if micro == 0 else top_grad[...] + product
    conv_grad(low, 0, acts, 0, weight_grad, rows)
    send_all(send, [row_of(*gain_sums), row_of(*shift_sums)] + [extras[m : m + 1] for m in range(micros)])


def conv_grad(low, low_first, values, value_first, total, rows):
    micros, _, channels, width = values.shape
    for micro in range(micros):
        grads = jnp.concatenate([low[micro, row + low_first] for row in range(rows)], axis=1)
        windows = jnp.concatenate(
            [
                values[micro, row + value_first : row + value_first + 3].reshape(3 * channels, width)
                for row in range(rows)
            ],
            axis=1,
        )
        product = dot_lanes(grads, windows)
        total[...] = product if micro == 0 else total[...] + product


def half_rows(total, half, scene):
    channels = 2 * half
    start = scene * half
    mine = jnp.concatenate(
        [total[b * channels + start : b * channels + start + half, :] for b in range(2, -1, -1)], axis=0
    )
    wing = mine[:, LANES:]
    cut = wing.shape[0] // 2
    return [mine[:, :LANES], jnp.concatenate([wing[:cut], wing[cut:]], axis=1)]


def pick_kernel(
    found, cols, grads, first_out, first_stats, b_first_in, where_rows,
    canvas, second_grad, top_grad, expected,
    send, gain_grad, shift_grad, second_gain_grad, second_shift_grad, low, grid, b_first, first_grad, whole,
    *, rows, tiles, each
):
    expand(b_first_in, b_first)
    scene = lax.axis_index("scene")
    micros, high, channels, width = grads.shape
    sums = sum_rows(found, 2 + micros)
    second = sum(sums[2:]) + jnp.sum(expected[...], axis=0, keepdims=True)
    own_half(second[:, :channels], scene, second_shift_grad)
    own_half(second[:, channels:], scene, second_gain_grad)
    sums = sums[:2]
    own_half(sums[0][:, :channels] + sums[0][:, channels:], scene, gain_grad)
    own_half(sums[1][:, :channels] + sums[1][:, channels:], scene, shift_grad)
    turned = columns_of(sums) * (1.0 / (found.shape[0] * rows * width))
    masks = edges(channels, width)
    for micro in range(micros):
        part = slice(micro * channels, (micro + 1) * channels)
        centre, rstd = first_stats[part, 0:1], first_stats[part, 1:2]
        factor = cols[0:channels, 2:3] * rstd
        slope_part, shift_part = rstd * turned[part, 0:1], turned[part, 1:2]
        for row in range(high):
            grad = grads[micro, row]
            if 1 <= row <= rows:
                grad = grad - shift_part - (first_out[micro, row] - centre) * slope_part
            low[micro, row] = spread((factor * grad).astype(BF16), masks)
    half = 6 * channels
    for micro in range(micros):
        for at in range(0, rows + 4, 2):
            if at == 0:
                parts = dot(b_first[:, half:], low[micro, 0:2].reshape(half, width))
            elif at == rows + 2:
                parts = dot(b_first[:, :half], low[micro, rows : rows + 2].reshape(half, width))
            else:
                parts = conv_pair(low, b_first, micro, at - 2, channels)
            grid[micro, at] = parts[:channels].astype(BF16)
            grid[micro, at + 1] = parts[channels:].astype(BF16)
    conv_grad(low, 0, canvas, 0, first_grad, high)
    half = channels // 2
    for s in range(2):
        parts = half_rows(first_grad, half, s) + half_rows(second_grad, half, s)
        mine = top_grad[s * channels : (s + 1) * channels, :]
        parts.append(jnp.concatenate([mine[:half], mine[half:]], axis=1))
        parts = jnp.concatenate(parts, axis=0)
        whole[s, 0 : parts.shape[0]] = parts
        if whole.shape[1] > parts.shape[0]:
            whole[s, parts.shape[0] :] = jnp.zeros((whole.shape[1] - parts.shape[0], LANES), F32)
    columns = jnp.transpose(where_rows[...])
    slots = columns.shape[0]
    lane = lax.broadcasted_iota(jnp.int32, (slots, width), 1).astype(F32)
    groups = []
    for group in range(3):
        start, first, count = ((0, rows - 2, 2), (2, 0, rows), (rows + 2, 0, 2))[group]
        picked = []
        for micro in range(micros):
            at = 2 * group + micro
            column = columns[:, at : at + 1] - 1.0
            column = column - jnp.floor(column * (1.0 / width)) * width
            chosen = jnp.where(lane == column, 1.0, 0.0).astype(BF16)
            place = jnp.floor((where_rows[at : at + 1] - 1.0) * (1.0 / width))
            here = dot_lanes(grid[micro, start : start + count].reshape(count * channels, width), chosen)
            total = jnp.zeros((channels, slots), F32)
            for r in range(count):
                total = total + jnp.where(
                    place == (first + r) * 1.0, here[r * channels : (r + 1) * channels], 0.0
                )
            picked.append(total)
        groups.append(jnp.transpose(jnp.concatenate(picked, axis=0)))
    capacity = slots // tiles
    block = send.shape[1]

    def filled(parts):
        missing = block - sum(part.shape[0] for part in parts)
        if missing > 0:
            parts = parts + [jnp.zeros((missing, LANES), F32)]
        return jnp.concatenate(parts, axis=0).astype(BF16)

    for spot in range(tiles):
        mine = slice(spot * capacity, (spot + 1) * capacity)
        send[2 * spot + scene] = filled([picked[mine] for picked in groups])
        send[2 * spot + 1 - scene] = filled([whole[s, spot * each : (spot + 1) * each] for s in range(2)])


def pillar_weights_kernel(rows, w_pillar, cols, pooled, out, lifted):
    micros, channels, wide = out.shape
    pillars = pooled.shape[2]
    inputs = w_pillar.shape[1]
    gain, shift = cols[0:channels, 0:1], cols[0:channels, 1:2]
    for micro in range(micros):
        lifted[...] = dot(w_pillar[...], rows[micro, 0:inputs])
        _, limit = pillar_notes(rows, micro, inputs, pillars)
        centre, rstd = pooled[micros + micro, :, 0:1], pooled[micros + micro, :, 1:2]
        pool = pooled[micro]
        for n in range(wide // pillars):
            piece = slice(n * pillars, (n + 1) * pillars)
            normed = (lifted[:, piece] - centre) * rstd * gain + shift
            gate = sigmoid(normed)
            act = normed * gate
            slope = gate + act * (1.0 - gate)
            out[micro, :, piece] = jnp.where(limit > n, jnp.exp(act - pool) * slope, 0.0).astype(BF16)


def pillar_back_kernel(found, rows, w_pillar, cols, pooled, factors, send, grads, lifted, *, capacity, each):
    micros = rows.shape[0]
    _, channels, pillars = pooled.shape
    stats = pooled.at[micros : 2 * micros]
    inputs = w_pillar.shape[1]
    depth = rows.shape[2] // pillars
    scene = lax.axis_index("scene")
    peers = found.shape[0]
    slot_count = peers // 2 * capacity
    blocks = [found[2 * t + scene].astype(F32) for t in range(peers // 2)]
    before, own, after = [
        jnp.concatenate([block[group * capacity : (group + 1) * capacity] for block in blocks], axis=0)
        for group in range(3)
    ]
    gap = jnp.zeros((capacity, LANES), F32)
    returned = (
        own
        + jnp.concatenate([before[capacity:], gap], axis=0)
        + jnp.concatenate([gap, after[: slot_count - capacity]], axis=0)
    )
    turned = jnp.transpose(returned)
    place = lax.broadcasted_iota(jnp.int32, (slot_count, pillars), 0).astype(F32)
    gain = cols[0:channels, 0:1]
    gain_sums, shift_sums = [], []
    outer = jnp.zeros((16, channels), F32)
    for micro in range(micros):
        lifted[...] = dot(w_pillar[...], rows[micro, 0:inputs])
        slot, _ = pillar_notes(rows, micro, inputs, pillars)
        chosen = jnp.where(place == slot, 1.0, 0.0).astype(BF16)
        back = dot(turned[micro * channels : (micro + 1) * channels].astype(BF16), chosen)
        centre, rstd = stats[micro, :, 0:1], stats[micro, :, 1:2]
        gain_sum = jnp.zeros((channels, pillars), F32)
        shift_sum = jnp.zeros((channels, pillars), F32)
        for n in range(depth):
            piece = slice(n * pillars, (n + 1) * pillars)
            grad = back * factors[micro, :, piece].astype(F32)
            grads[micro, :, piece] = grad
            gain_sum = gain_sum + grad * (lifted[:, piece] - centre)
            shift_sum = shift_sum + grad
        gain_sum = gain_sum * rstd
        gain_sums.append(gain_sum)
        shift_sums.append(shift_sum)
        scale = jnp.transpose(jnp.broadcast_to(rstd * gain, (channels, LANES)))[0:1]
        outer = outer + dot_lanes(rows[micro], grads[micro].astype(BF16)) * scale
    exact = jnp.concatenate([row_of(*gain_sums), row_of(*shift_sums)], axis=0)
    lines = [jnp.concatenate([outer[k : k + 1], outer[k + 1 : k + 2]], axis=1) for k in range(0, 10, 2)]
    weights = found[1 - scene].astype(F32)
    for t in range(1, peers // 2):
        weights = weights + found[2 * t + 1 - scene].astype(F32)
    rest = send.shape[2] - 9 - each
    for s in range(2):
        block = exact_rows(exact) + lines + [weights[s * each : (s + 1) * each]]
        if rest > 0:
            block.append(jnp.zeros((rest, LANES), F32))
        block = jnp.concatenate(block, axis=0).astype(BF16)
        send[:, s] = jnp.broadcast_to(block[None], (send.shape[0],) + block.shape)


def points_kernel(
    found, rows, grads, w_pillar, cols, pooled,
    points_grad, pillar_grad, gain_grad, shift_grad, first_grad, second_grad, up_grad, lifted, *, each
):
    scene = lax.axis_index("scene")
    micros, channels, _ = grads.shape
    stats = pooled.at[micros : 2 * micros]
    _, _, inputs, depth, pillars = points_grad.shape
    half = channels // 2
    total = jnp.sum(found[...].astype(F32), axis=0)
    total = jnp.concatenate([total[0:2] + total[2:4], total[4:9]], axis=0)
    own_half(total[0:1, :channels] + total[0:1, channels:], scene, gain_grad)
    own_half(total[1:2, :channels] + total[1:2, channels:], scene, shift_grad)
    turned = jnp.transpose(jnp.concatenate([total, jnp.zeros((1, LANES), F32)], axis=0))
    weight_grad = jnp.concatenate(
        [turned[(k % 2) * channels : (k % 2 + 1) * channels, 2 + k // 2 : 3 + k // 2] for k in range(inputs)],
        axis=1,
    )
    weight = jnp.transpose(w_pillar[...].astype(F32)).astype(BF16)
    for micro in range(micros):
        lifted[...] = dot(w_pillar[...], rows[micro, 0:inputs])
        part = slice(micro * channels, (micro + 1) * channels)
        centre, rstd, inverse = stats[micro, :, 0:1], stats[micro, :, 1:2], stats[micro, :, 2:3]
        factor = cols[0:channels, 0:1] * rstd
        gain_part, shift_part = turned[part, 0:1], turned[part, 1:2]
        spun, mean = stats[micro, :, 16 : 16 + inputs], stats[micro, :, 32 : 32 + inputs]
        weight_grad = weight_grad - factor * (shift_part * mean + gain_part * rstd * spun)
        gain_part, shift_part = gain_part * inverse * rstd, shift_part * inverse
        _, limit = pillar_notes(rows, micro, inputs, pillars)
        for n in range(depth):
            piece = slice(n * pillars, (n + 1) * pillars)
            low = factor * (grads[micro, :, piece] - shift_part - (lifted[:, piece] - centre) * gain_part)
            low = jnp.where(limit > n, low, 0.0).astype(BF16)
            points_grad[micro, 0, :, n, :] = dot(weight, low)
    weight_grad = jnp.concatenate([weight_grad, jnp.zeros((channels, LANES - inputs), F32)], axis=1)
    weight_grad = jnp.transpose(weight_grad)[0:inputs]
    pillar_grad[...] = jnp.where(scene == 0, weight_grad[:, :half], weight_grad[:, half:])
    whole = jnp.concatenate(
        [
            (found[2 * t].astype(F32) + found[2 * t + 1].astype(F32))[9 : 9 + each]
            for t in range(found.shape[0] // 2)
        ],
        axis=0,
    )
    for index, out in enumerate((first_grad, second_grad)):
        base = index * 9 * half * channels // LANES
        lead = 3 * half
        mine = whole[base : base + lead]
        wing = whole[base + lead : base + lead + lead // 2]
        wing = jnp.concatenate([wing[:, :channels], wing[:, channels:]], axis=0)
        both = jnp.concatenate([mine, wing], axis=1)
        for a in range(3):
            for b in range(3):
                at = (3 * a + b) * channels
                out[:, at : at + channels] = both[b * half : (b + 1) * half, a * channels : (a + 1) * channels]
    base = 2 * 9 * half * channels // LANES
    top = whole[base : base + half]
    up_grad[...] = jnp.concatenate([top[:, :channels], top[:, channels:]], axis=0)


def swap(blocks, axes):
    return lax.all_to_all(blocks, axes, split_axis=0, concat_axis=0)


def shards(
    points, point_counts, pillar_tile, pillar_cell,
    pillar_weight, pillar_gain, pillar_shift,
    first_weight, first_gain, first_shift,
    second_weight, second_gain, second_shift,
    up_weight, up_gain, up_shift, cotangent,
):
    micros, _, inputs, depth, pillars = points.shape
    channels = up_weight.shape[1]
    upper = cotangent.shape[2]
    rows, width = cotangent.shape[3:]
    tiles = lax.axis_size("tile")
    scenes = lax.axis_size("scene")
    peers = tiles * scenes
    capacity = 2 * pillars // tiles
    slot_count = tiles * capacity
    half = channels // 2

    def vmem(shape, dtype):
        return pltpu.VMEM(shape, dtype)

    def grid(high, dtype=F32, lead=channels):
        return ((micros, high, lead, width), dtype)

    sums = ((peers, 2, LANES), F32)
    sources = (pillar_tile, pillar_cell, point_counts, points)
    wide = vmem((inputs * depth, pillars), F32)
    (moments,) = run(
        functools.partial(moments_kernel, capacity=capacity),
        [((tiles, scenes, 4, LANES), F32)],
        *sources,
        hbm=range(len(sources)), copies=len(sources), limit=WIDE_LIMIT,
        scratch=[vmem(source.shape, source.dtype) for source in sources] + [wide],
    )
    sources = (
        pillar_tile, point_counts, points,
        first_weight, second_weight, up_weight, pillar_weight.T,
        pillar_gain, pillar_shift, first_gain, first_shift, second_gain, second_shift, up_gain, up_shift,
    )
    packed, point_rows = run(
        functools.partial(pack_kernel, capacity=capacity),
        [((layout(half, channels)[-1] + 16, LANES), BF16), ((micros, 16, depth * pillars), BF16)],
        *sources,
        hbm=range(len(sources)), copies=len(sources), limit=WIDE_LIMIT,
        scratch=[vmem(source.shape, source.dtype) for source in sources] + [wide],
        cost=pl.CostEstimate(flops=10**7, bytes_accessed=10**6, transcendentals=0),
    )
    moments = swap(moments.reshape(peers, 4, LANES), BOTH)
    both = lax.all_gather(packed, "scene")
    taps = ((2 * channels, 12 * channels), BF16)
    compact = ((channels, 9 * channels), BF16)
    w_pillar, cols, l_first, l_second, b_first, b_second, w_up, w_up_t = run(
        functools.partial(unpack_kernel, inputs=inputs),
        [
            ((channels, inputs), BF16), ((LANES, 8), F32), compact, compact, compact, compact,
            ((upper, channels), BF16), ((channels, upper), BF16),
        ],
        both,
    )
    cot = cotangent[:, 0].transpose(0, 2, 1, 3)

    send, pooled = run(
        functools.partial(pillar_kernel, capacity=capacity),
        [((slot_count, 3 * LANES), BF16), ((2 * micros, channels, pillars), F32)],
        moments, point_rows, w_pillar, cols,
        scratch=[vmem((channels, depth * pillars), F32), vmem((channels, depth * pillars), F32)],
    )
    arrived = swap(send.reshape(tiles, capacity, 3 * LANES), "tile").reshape(slot_count, 3 * LANES)
    (cell_rows,) = run(
        functools.partial(cells_kernel, capacity=capacity),
        [((8, slot_count), F32)],
        moments,
        cost=pl.CostEstimate(flops=10**7, bytes_accessed=10**6, transcendentals=0),
    )
    (factors,) = run(
        pillar_weights_kernel,
        [((micros, channels, depth * pillars), BF16)],
        point_rows, w_pillar, cols, pooled,
        scratch=[vmem((channels, depth * pillars), F32)],
        cost=pl.CostEstimate(flops=10**7, bytes_accessed=10**6, transcendentals=0),
    )
    arrived, cot, factors = lax.optimization_barrier((arrived, cot, factors))

    first_out, canvas, send = run(
        functools.partial(canvas_kernel, rows=rows),
        [grid(rows + 2), grid(rows + 4, BF16), sums],
        arrived, cell_rows, l_first,
        scratch=[vmem(*grid(rows + 4, BF16, 3 * channels)), vmem(*taps)],
    )
    second_out, first_act, first_slopes, first_stats, send = run(
        functools.partial(second_kernel, rows=rows, tiles=tiles),
        [grid(rows), grid(rows + 2, BF16), grid(rows + 2), ((LANES, 8), F32), sums],
        swap(send, BOTH), cols, first_out, l_second,
        scratch=[vmem(*grid(rows + 2, BF16, 3 * channels)), vmem(*taps)],
    )
    part = -(-micros * channels // peers)
    second_act, up_out, slopes, plain, crossed, second_stats, send = run(
        functools.partial(up_kernel, rows=rows),
        [
            grid(rows, BF16), grid(rows, F32, upper), grid(rows, F32, 2 * channels), ((micros, LANES), F32),
            ((peers * part, LANES), F32), ((LANES, 8), F32), ((peers, -(-(2 * micros + part) // 8) * 8, LANES), F32),
        ],
        swap(send, BOTH), cols, second_out, w_up,
    )
    features, grads, mixed, top_stats, send = run(
        functools.partial(top_kernel, rows=rows, each=part),
        [
            ((micros, 1, upper, rows, width), BF16), grid(rows, F32, upper), ((micros, LANES), F32),
            ((LANES, 8), F32),
            ((peers, -(-(6 * micros + part) // 8) * 8, LANES), BF16),
        ],
        swap(send, BOTH), cols, up_out, cot, slopes, plain, w_up_t,
        scratch=[vmem((micros, width // LANES, upper * rows, LANES), F32)],
    )
    vector, top_vector, matrix = ((half,), F32), ((upper // 2,), F32), ((half, 9 * channels), F32)
    cross = ((3 * channels, 3 * channels), F32)
    first_dz, top_grad, second_cross, up_gain_grad, up_shift_grad, expected, send = run(
        functools.partial(middle_back_kernel, rows=rows, tiles=tiles, each=part),
        [
            grid(rows + 2), ((upper, channels), F32), cross, top_vector, top_vector, ((micros, LANES), F32),
            ((peers, 2 + micros, LANES), F32),
        ],
        swap(send, BOTH), cols, grads, up_out, top_stats, second_out, second_stats, slopes, w_up, w_up_t,
        mixed, plain, crossed, second_act, first_act, first_out, first_stats, first_slopes, b_second,
        scratch=[
            vmem(*grid(rows, BF16, 3 * channels)), vmem(*grid(rows, BF16, upper)), vmem((micros, LANES), F32),
            vmem(*grid(rows)), vmem(*taps),
        ],
    )
    length = (2 * 9 * half * channels + upper * half) // LANES
    each = -(-length // tiles)
    block = -(-max(3 * capacity, 2 * each) // 8) * 8
    send, first_gain_grad, first_shift_grad, second_gain_grad, second_shift_grad = run(
        functools.partial(pick_kernel, rows=rows, tiles=tiles, each=each),
        [((peers, block, LANES), BF16), vector, vector, vector, vector],
        swap(send, BOTH), cols, first_dz, first_out, first_stats, b_first, cell_rows,
        canvas, second_cross, top_grad, expected,
        scratch=[
            vmem(*grid(rows + 2, BF16, 3 * channels)), vmem(*grid(rows + 4, BF16)), vmem(*taps), vmem(*cross),
            vmem((scenes, tiles * each, LANES), F32),
        ],
    )
    block = -(-(9 + each) // 8) * 8
    send, pillar_dz = run(
        functools.partial(pillar_back_kernel, capacity=capacity, each=each),
        [((tiles, scenes, block, LANES), BF16), ((micros, channels, depth * pillars), F32)],
        swap(send, BOTH), point_rows, w_pillar, cols, pooled, factors,
        scratch=[vmem((channels, depth * pillars), F32)],
    )
    points_grad, pillar_grad, pillar_gain_grad, pillar_shift_grad, first_grad, second_grad, up_grad = run(
        functools.partial(points_kernel, each=each),
        [
            ((micros, 1, inputs, depth, pillars), F32), ((inputs, half), F32), vector, vector,
            matrix, matrix, ((upper // 2, channels), F32),
        ],
        swap(send.reshape(peers, block, LANES), BOTH), point_rows, pillar_dz, w_pillar, cols, pooled,
        scratch=[vmem((channels, depth * pillars), F32)],
    )
    return (
        features, points_grad,
        pillar_grad.T, pillar_gain_grad, pillar_shift_grad,
        first_grad, first_gain_grad, first_shift_grad,
        second_grad, second_gain_grad, second_shift_grad,
        up_grad, up_gain_grad, up_shift_grad,
    )


def solution(mesh):
    matrix, vector = P("scene", None), P("scene")
    grid = P(None, "scene", None, "tile", None)
    cloud = P(None, "scene", None, None, "tile")
    pillar = P(None, "scene", "tile")
    weights = (matrix, vector, vector) * 4
    return jax.shard_map(
        shards,
        mesh=mesh,
        in_specs=(cloud, pillar, pillar, pillar) + weights + (grid,),
        out_specs=(grid, cloud) + weights,
        check_vma=False,
    )
```

```python
import functools

import jax
import jax.numpy as jnp
from jax import lax
from jax.experimental import pallas as pl
from jax.experimental.pallas import tpu as pltpu
from jax.sharding import PartitionSpec as P

norm_eps = 0.001
BOTH = ("tile", "scene")
F32 = jnp.float32
BF16 = jnp.bfloat16
VMEM_LIMIT = 24 * 1024 * 1024
WIDE_LIMIT = 60 * 1024 * 1024
LANES = 128


def run(kernel, outs, *args, hbm=(), scratch=(), copies=0, cost=None, limit=VMEM_LIMIT):
    specs = [
        pl.BlockSpec(memory_space=pltpu.HBM if index in hbm else pltpu.VMEM) for index in range(len(args))
    ]
    scratch = list(scratch)
    if copies:
        scratch.append(pltpu.SemaphoreType.DMA((copies,)))
    return pl.pallas_call(
        kernel,
        out_shape=[jax.ShapeDtypeStruct(out[0], out[1]) for out in outs],
        in_specs=specs,
        out_specs=[
            pl.BlockSpec(memory_space=pltpu.HBM if len(out) > 2 else pltpu.VMEM) for out in outs
        ],
        scratch_shapes=scratch,
        compiler_params=pltpu.CompilerParams(vmem_limit_bytes=limit),
        cost_estimate=cost,
    )(*args)


def move(source, target, sems, index):
    copy = pltpu.make_async_copy(source, target, sems.at[index])
    copy.start()
    return copy


def dot(left, right, precision=None):
    return jnp.dot(left, right, preferred_element_type=F32, precision=precision)


def dot_lanes(left, right, precision=None):
    return lax.dot_general(
        left, right, (((1,), (1,)), ((), ())), preferred_element_type=F32, precision=precision
    )


def sigmoid(values):
    return 0.5 + 0.5 * jnp.tanh(0.5 * values)


def fold(values):
    total = values[:, :LANES]
    for start in range(LANES, values.shape[1], LANES):
        total = total + values[:, start : start + LANES]
    return total


def row_of(left, right=None):
    both = left if right is None else jnp.concatenate([left, right], axis=0)
    return jnp.sum(jnp.transpose(both), axis=0, keepdims=True)


def columns_of(rows):
    rows = rows + [jnp.zeros((8 - len(rows), LANES), F32)] if len(rows) < 8 else rows
    return jnp.transpose(jnp.concatenate(rows, axis=0))


def inside(tile, row, height):
    tiles, rows = height
    place = tile * rows + row
    return jnp.where((place >= 0) & (place < tiles * rows), 1.0, 0.0).astype(F32)


def send_all(ref, rows):
    for index, row in enumerate(rows):
        ref[:, index : index + 1, :] = jnp.broadcast_to(row[None], (ref.shape[0], 1, LANES))


def pooled_stats(means, squares, count):
    peers = means.shape[0]
    mean = jnp.sum(means, axis=0, keepdims=True) * (1.0 / peers)
    away = means - mean
    spread = jnp.sum(squares + count * away * away, axis=0, keepdims=True) * (1.0 / (peers * count))
    return mean, lax.rsqrt(spread + norm_eps)


def stat_columns(found, count):
    return columns_of(list(pooled_stats(found[:, 0, :], found[:, 1, :], count)))


def sum_rows(found, lines):
    return [jnp.sum(found[:, index, :], axis=0, keepdims=True) for index in range(lines)]


def own_half(row, scene, out):
    size = out.shape[0]
    out[...] = jnp.where(scene == 0, row[:, 0:size], row[:, size : 2 * size]).reshape(size)


def edges(channels, width):
    lane = lax.broadcasted_iota(jnp.int32, (channels, width), 1)
    return lane > 0, lane < width - 1


def spread(row, masks):
    zero = jnp.zeros_like(row)
    left = jnp.where(masks[0], pltpu.roll(row, 1, 1), zero)
    right = jnp.where(masks[1], pltpu.roll(row, row.shape[1] - 1, 1), zero)
    return jnp.concatenate([left, row, right], axis=0)


def layout(half, channels):
    first = 0
    second = first + half * -(-9 * channels // LANES)
    up = second + half * -(-9 * channels // LANES)
    vectors = up + channels
    return first, second, up, vectors, vectors + 16


def widen(value):
    missing = LANES - value.shape[1]
    if missing == 0:
        return value
    return jnp.concatenate([value, jnp.zeros((value.shape[0], missing), value.dtype)], axis=1)


def pack(held, out):
    first, second, up, pillar = held[:4]
    half, channels = first.shape[0], up.shape[1]
    starts = layout(half, channels)
    for ref, start in ((first, starts[0]), (second, starts[1])):
        for j in range(-(-9 * channels // LANES)):
            out[start + j * half : start + (j + 1) * half, :] = widen(
                ref[:, j * LANES : min((j + 1) * LANES, 9 * channels)]
            )
    out[starts[2] : starts[2] + channels, :] = widen(up[...])
    rows = [vector[...].astype(F32).reshape(1, -1) for vector in held[4:]]
    rows = [widen(row) for row in rows] + [jnp.zeros((16 - len(rows), LANES), F32)]
    turned = widen(pillar[...].astype(F32))
    rows += [turned, jnp.zeros((16 - turned.shape[0], LANES), F32)]
    out[starts[3] :, :] = jnp.concatenate(rows, axis=0).astype(BF16)


def unpack_kernel(
    both, w_pillar, cols, l_first, l_second, b_first, b_second, w_up, w_up_t, *, inputs
):
    half = w_pillar.shape[0] // 2
    channels = 2 * half
    starts = layout(half, channels)
    tiles = -(-9 * channels // LANES)

    def wide(start):
        return jnp.concatenate(
            [
                jnp.concatenate(
                    [both[s, start + j * half : start + (j + 1) * half, :] for j in range(tiles)], axis=1
                )
                for s in range(2)
            ],
            axis=0,
        ).astype(F32)

    up = jnp.concatenate(
        [both[s, starts[2] : starts[2] + channels, 0:channels] for s in range(2)], axis=0
    )
    w_up[...] = up
    w_up_t[...] = jnp.transpose(up.astype(F32)).astype(BF16)
    turned = jnp.concatenate(
        [both[s, starts[4] : starts[4] + 16, 0:half].astype(F32) for s in range(2)], axis=1
    )
    w_pillar[...] = jnp.transpose(widen(turned))[0:channels, 0:inputs].astype(BF16)
    vectors = [both[s, starts[3] : starts[3] + 16, :].astype(F32) for s in range(2)]
    rows = []
    for index in range(8):
        size = half if index < 6 else channels
        row = jnp.concatenate([vectors[s][index : index + 1, 0:size] for s in range(2)], axis=1)
        rows.append(jnp.concatenate([row] * (LANES // (2 * size)), axis=1))
    cols[...] = columns_of(rows)
    for weight, ahead, back in ((wide(starts[0]), l_first, b_first), (wide(starts[1]), l_second, b_second)):
        turned = jnp.transpose(weight)
        ahead[...] = weight[:, : 9 * channels].astype(BF16)
        back[...] = jnp.concatenate(
            [turned[tap * channels : (tap + 1) * channels] for tap in range(8, -1, -1)], axis=1
        ).astype(BF16)


def slot_line(wide, depth, inputs):
    return jnp.concatenate([wide[pl.ds(n, inputs, stride=depth), :] for n in range(depth)], axis=1)


def slot_mask(count, depth):
    return jnp.concatenate([jnp.where(count > n, 1.0, 0.0) for n in range(depth)], axis=1)


def ranks(tile):
    pillars = tile.shape[1]
    across = jnp.broadcast_to(tile, (pillars, pillars))
    down = jnp.transpose(across)
    row = lax.broadcasted_iota(jnp.int32, (pillars, pillars), 0)
    col = lax.broadcasted_iota(jnp.int32, (pillars, pillars), 1)
    return jnp.sum(jnp.where((across == down) & (row < col), 1.0, 0.0), axis=0, keepdims=True)


def moments_kernel(*refs, capacity):
    number = 4
    sources, out = refs[:number], refs[number]
    held, wide, sems = refs[number + 1 : 2 * number + 1], refs[-2], refs[-1]
    copies = [move(sources[i], held[i], sems, i) for i in range(number)]
    tiles, cells, counts, points = held
    micros, _, inputs, depth, pillars = points.shape
    peers, scenes = out.shape[:2]
    copies[0].wait()
    copies[1].wait()
    lines = []
    for micro in range(micros):
        tile = tiles[micro].astype(F32)
        cell = (cells[micro] + 1).astype(F32)
        high = jnp.floor(cell * (1.0 / 16.0))
        low = cell - high * 16.0
        rank = ranks(tile)
        spot = lax.broadcasted_iota(jnp.int32, (capacity, pillars), 0).astype(F32)
        placed = jnp.where(spot == rank, 1.0, 0.0).astype(BF16)
        peer = lax.broadcasted_iota(jnp.int32, (peers, pillars), 0).astype(F32)
        for group in range(3):
            named = tile == peer + (group - 1.0)
            lines.append(
                16.0 * dot_lanes(jnp.where(named, high, 0.0).astype(BF16), placed)
                + dot_lanes(jnp.where(named, low, 0.0).astype(BF16), placed)
            )
    used = 3 * micros * capacity
    line = jnp.concatenate(lines + [jnp.zeros((peers, LANES - used), F32)], axis=1).reshape(peers, 1, LANES)
    for scene in range(scenes):
        out[:, scene, micros : micros + 1, :] = line
    copies[2].wait()
    copies[3].wait()
    parts, mean_rows, totals = [], [], []
    for micro in range(micros):
        wide[...] = points[micro, 0].astype(F32).reshape(inputs * depth, pillars)
        rows = slot_line(wide, depth, inputs)
        mask = slot_mask(counts[micro], depth)
        total = jnp.sum(mask, axis=1, keepdims=True)
        mean = jnp.sum(rows * mask, axis=1, keepdims=True) / total
        centred = jnp.concatenate(
            [(rows - mean) * mask, jnp.zeros((16 - inputs, rows.shape[1]), F32)], axis=0
        )
        high = centred.astype(BF16)
        parts += [high, (centred - high.astype(F32)).astype(BF16)]
        lane = lax.broadcasted_iota(jnp.int32, (inputs, inputs), 1)
        diagonal = lax.broadcasted_iota(jnp.int32, (inputs, inputs), 0) == lane
        mean_rows.append(jnp.sum(jnp.where(diagonal, mean, 0.0), axis=0, keepdims=True))
        totals.append(total)
    parts = jnp.concatenate(parts, axis=0)
    every = dot_lanes(parts, parts)
    for micro in range(micros):
        at = 32 * micro
        square = every[at : at + 32, at : at + 32]
        products = (
            square[0:inputs, 0:inputs] + square[16 : 16 + inputs, 0:inputs]
            + square[0:inputs, 16 : 16 + inputs] + square[16 : 16 + inputs, 16 : 16 + inputs]
        )
        row = jnp.concatenate(
            [products[k : k + 1] for k in range(inputs)]
            + [mean_rows[micro], totals[micro], jnp.zeros((1, LANES - inputs * inputs - inputs - 1), F32)],
            axis=1,
        )
        for scene in range(scenes):
            out[:, scene, micro : micro + 1, :] = jnp.broadcast_to(row[None], (peers, 1, LANES))


def pack_kernel(*refs, capacity):
    number = 15
    sources, packed, lines_out = refs[:number], refs[number], refs[number + 1]
    held, wide, sems = refs[number + 2 : 2 * number + 2], refs[-2], refs[-1]
    copies = [move(sources[i], held[i], sems, i) for i in range(number)]
    for copy in copies:
        copy.wait()
    tiles, counts, points = held[:3]
    pack(held[3:], packed)
    micros, _, inputs, depth, pillars = points.shape
    for micro in range(micros):
        tile = tiles[micro].astype(F32)
        wide[...] = points[micro, 0].astype(F32).reshape(inputs * depth, pillars)
        rows = slot_line(wide, depth, inputs)
        notes = jnp.concatenate([tile * capacity + ranks(tile), counts[micro].astype(F32)], axis=0)
        notes = jnp.concatenate([notes, jnp.zeros((2, rows.shape[1] - pillars), F32)], axis=1)
        lines_out[micro] = jnp.concatenate(
            [rows, notes, jnp.zeros((14 - inputs, rows.shape[1]), F32)], axis=0
        ).astype(BF16)


def cells_kernel(found, rows, *, capacity):
    scene = lax.axis_index("scene")
    slots = rows.shape[1]
    peers = found.shape[0]
    values = found[:, 2, :]
    slot = lax.broadcasted_iota(jnp.int32, (slots, peers), 0)
    peer = lax.broadcasted_iota(jnp.int32, (slots, peers), 1)
    lane = lax.broadcasted_iota(jnp.int32, (slots, LANES), 1)
    row = lax.broadcasted_iota(jnp.int32, (slots, LANES), 0)
    result = jnp.zeros((slots, LANES), F32)
    chosen = jnp.where(peer == 2 * (slot // capacity) + scene, 1.0, 0.0)
    spread = dot(chosen, values, lax.Precision.HIGHEST)
    for micro in range(2):
        for group in range(3):
            mine = jnp.where(lane == (3 * micro + group) * capacity + row % capacity, spread, 0.0)
            column = jnp.sum(mine, axis=1, keepdims=True)
            result = jnp.where(lane == 2 * group + micro, column, result)
    rows[...] = jnp.transpose(result)[0:8]


def pillar_notes(rows, micro, inputs, pillars):
    notes = rows[micro, :, 0:pillars].astype(F32)
    return notes[inputs : inputs + 1], notes[inputs + 1 : inputs + 2]


def pillar_kernel(
    found, point_rows, w_pillar, cols, send, pooled, lifted, acts, choices, *, capacity
):
    micros = point_rows.shape[0]
    channels, inputs = w_pillar.shape
    pillars = pooled.shape[2]
    depth = point_rows.shape[2] // pillars
    weight = w_pillar[...]
    wide_weight = weight.astype(F32)
    rows_out = send.shape[0]
    square = inputs * inputs
    stacked = []
    notes = [pillar_notes(point_rows, micro, inputs, pillars) for micro in range(micros)]
    for micro in range(micros):
        lifted[micro] = dot(weight, point_rows[micro, 0:inputs])
    for group in range(3):
        place = lax.broadcasted_iota(jnp.int32, (rows_out, pillars), 0) + (group - 1) * capacity
        choices[group] = jnp.concatenate(
            [jnp.where(place.astype(F32) == slot, 1.0, 0.0) for slot, _ in notes], axis=1
        ).astype(BF16)
    for micro in range(micros):
        moments = found[:, micro, :]
        sizes = moments[:, square + inputs : square + inputs + 1]
        means = moments[:, square : square + inputs]
        count = jnp.sum(sizes, axis=0, keepdims=True)
        mean = jnp.sum(means * sizes, axis=0, keepdims=True) / count
        away = means - mean
        products = lax.dot_general(
            away * sizes, away, (((0,), (0,)), ((), ())),
            preferred_element_type=F32, precision=lax.Precision.HIGHEST,
        )
        summed = jnp.sum(moments, axis=0, keepdims=True)
        products = products + jnp.concatenate(
            [summed[:, k * inputs : (k + 1) * inputs] for k in range(inputs)], axis=0
        )
        cov = products / count
        spun = wide_weight[:, 0:1] * cov[0:1]
        for k in range(1, inputs):
            spun = spun + wide_weight[:, k : k + 1] * cov[k : k + 1]
        spread = jnp.sum(spun * wide_weight, axis=1, keepdims=True)
        centre = jnp.sum(wide_weight * mean, axis=1, keepdims=True)
        rstd = lax.rsqrt(spread + norm_eps)
        inverse = jnp.broadcast_to(1.0 / count, (channels, 1))
        pooled[micros + micro] = jnp.concatenate(
            [
                centre, rstd, inverse, jnp.zeros((channels, 13), F32),
                spun, jnp.zeros((channels, 16 - inputs), F32),
                jnp.broadcast_to(mean, (channels, inputs)), jnp.zeros((channels, LANES - 32 - inputs), F32),
            ],
            axis=1,
        )
        scale = rstd * cols[0:channels, 0:1]
        shift = cols[0:channels, 1:2]
        limit = notes[micro][1]
        top = jnp.full((channels, pillars), -jnp.inf, F32)
        for n in range(depth):
            piece = slice(n * pillars, (n + 1) * pillars)
            normed = (lifted[micro, :, piece] - centre) * scale + shift
            act = normed * sigmoid(normed)
            acts[:, piece] = act
            top = jnp.maximum(top, jnp.where(limit > n, act, -jnp.inf))
        total = jnp.zeros((channels, pillars), F32)
        for n in range(depth):
            piece = slice(n * pillars, (n + 1) * pillars)
            total = total + jnp.where(limit > n, jnp.exp(acts[:, piece] - top), 0.0)
        result = top + jnp.log(total)
        pooled[micro] = result
        parts = [jnp.zeros((channels, pillars), F32)] * micros
        parts[micro] = result.astype(BF16).astype(F32)
        stacked.append(jnp.transpose(jnp.concatenate(parts, axis=0)))
    values = jnp.concatenate(stacked, axis=0).astype(BF16)
    for group in range(3):
        send[:, group * LANES : (group + 1) * LANES] = dot(choices[group], values).astype(BF16)


def own_stats(ref, first_row, rows, send):
    micros, _, channels, width = ref.shape
    sums, squares = [], []
    for micro in range(micros):
        total = fold(ref[micro, first_row])
        for row in range(first_row + 1, first_row + rows):
            total = total + fold(ref[micro, row])
        sums.append(total * (1.0 / (rows * width)))
    means = [jnp.sum(total, axis=1, keepdims=True) for total in sums]
    for micro in range(micros):
        spread = jnp.zeros(sums[micro].shape, F32)
        for row in range(first_row, first_row + rows):
            away = ref[micro, row] - means[micro]
            spread = spread + fold(away * away)
        squares.append(spread)
    if channels == LANES:
        send_all(send, [row_of(part) for part in sums + squares])
    else:
        send_all(send, [row_of(*sums), row_of(*squares)])


def expand(taps, weight):
    channels, length = taps.shape
    gap = jnp.zeros((channels, length // 3), BF16)
    weight[0:channels] = jnp.concatenate([taps[...], gap], axis=1)
    weight[channels : 2 * channels] = jnp.concatenate([gap, taps[...]], axis=1)


def conv_pair(source, weight, micro, at, channels):
    window = source[micro, at : at + 4].reshape(12 * channels, source.shape[3])
    return dot(weight[...], window)


def conv_rows(source, weight, out, shape):
    micros, high, channels, width = shape
    for micro in range(micros):
        for at in range(0, high, 2):
            both = conv_pair(source, weight, micro, at, channels)
            out[micro, at] = both[:channels].astype(out.dtype)
            out[micro, at + 1] = both[channels:].astype(out.dtype)


def canvas_kernel(found, where_rows, l_first_in, out, kept, send, canvas, l_first, *, rows):
    expand(l_first_in, l_first)
    columns = jnp.transpose(where_rows[...])
    scenes, high, channels, width = out.shape
    masks = edges(channels, width)
    slots = found.shape[0]
    lane = lax.broadcasted_iota(jnp.int32, (slots, width), 1).astype(F32)
    for group in range(3):
        values = jnp.transpose(found[:, group * LANES : (group + 1) * LANES].astype(F32))
        first, count = ((rows - 2, 2), (0, rows), (0, 2))[group]
        for scene in range(scenes):
            at = 2 * group + scene
            column = columns[:, at : at + 1] - 1.0
            column = column - jnp.floor(column * (1.0 / width)) * width
            row = jnp.floor((where_rows[at : at + 1] - 1.0) * (1.0 / width))
            mine = values[scene * channels : (scene + 1) * channels]
            placed = jnp.concatenate(
                [jnp.where(row == r * 1.0, mine, 0.0) for r in range(first, first + count)], axis=0
            ).astype(BF16)
            chosen = jnp.where(lane == column, 1.0, 0.0).astype(BF16)
            grid = dot(placed, chosen).astype(BF16)
            start = (0, 2, rows + 2)[group]
            for r in range(count):
                row = grid[r * channels : (r + 1) * channels]
                canvas[scene, start + r] = spread(row, masks)
                kept[scene, start + r] = row
    conv_rows(canvas, l_first, out, out.shape)
    own_stats(out, 1, rows, send)


def second_kernel(found, cols, first_out, l_second_in, out, kept, slopes, stats, send, acts, l_second,
                  *, rows, tiles):
    expand(l_second_in, l_second)
    micros, high, channels, width = first_out.shape
    tile = lax.axis_index("tile")
    turned = stat_columns(found, float(rows * width))
    stats[...] = turned
    masks = edges(channels, width)
    for micro in range(micros):
        part = slice(micro * channels, (micro + 1) * channels)
        centre = turned[part, 0:1]
        scale = turned[part, 1:2] * cols[0:channels, 2:3]
        shift = cols[0:channels, 3:4]

        for row in range(high):
            normed = (first_out[micro, row] - centre) * scale + shift
            gate = sigmoid(normed)
            act = normed * gate
            slopes[micro, row] = gate + act * (1.0 - gate)
            if row == 0 or row == high - 1:
                act = act * inside(tile, row - 1, (tiles, rows))
            act = act.astype(BF16)
            acts[micro, row] = spread(act, masks)
            kept[micro, row] = act
    conv_rows(acts, l_second, out, out.shape)
    own_stats(out, 0, rows, send)


def up_kernel(found, cols, second_out, w_up, acts, upper, slopes, plain, crossed, stats, send, *, rows):
    micros, _, channels, width = second_out.shape
    peers = send.shape[0]
    each = crossed.shape[0] // peers
    turned = stat_columns(found, float(rows * width))
    stats[...] = turned
    gain, shift = cols[0:channels, 4:5], cols[0:channels, 5:6]
    lines = []
    for micro in range(micros):
        part = slice(micro * channels, (micro + 1) * channels)
        centre, rstd = turned[part, 0:1], turned[part, 1:2]
        slope_sum = jnp.zeros((channels, LANES), F32)
        unit_sum = jnp.zeros((channels, LANES), F32)
        for row in range(rows):
            unit = (second_out[micro, row] - centre) * rstd
            normed = unit * gain + shift
            gate = sigmoid(normed)
            act = normed * gate
            slope = gate + act * (1.0 - gate)
            sloped = slope * unit
            slope_sum = slope_sum + fold(slope)
            unit_sum = unit_sum + fold(sloped)
            slopes[micro, row] = jnp.concatenate([slope, sloped], axis=0)
            act = act.astype(BF16)
            acts[micro, row] = act
            upper[micro, row] = dot(w_up[...], act)
        lines.append(row_of(slope_sum, unit_sum).astype(BF16).astype(F32))
        crossed[micro * channels : (micro + 1) * channels] = dot_lanes(
            jnp.concatenate([acts[micro, row] for row in range(rows)], axis=1),
            jnp.concatenate([slopes[micro, row].astype(BF16) for row in range(rows)], axis=1),
        )
    plain[...] = jnp.concatenate(lines, axis=0)
    used = micros * channels
    if crossed.shape[0] > used:
        crossed[used:] = jnp.zeros((crossed.shape[0] - used, LANES), F32)
    if 2 * micros + each < send.shape[1]:
        send[...] = jnp.zeros(send.shape, F32)
    for peer in range(peers):
        send[peer, 2 * micros : 2 * micros + each] = crossed[peer * each : (peer + 1) * each]
    own_stats(upper, 0, rows, send)


def exact_rows(rows):
    high = rows.astype(BF16).astype(F32)
    return [high, rows - high]


def top_kernel(
    found, cols, upper, cot, slopes, plain, w_up_t, features, grads, mixed, stats, send, ordered, *, rows, each
):
    micros, _, wide, width = upper.shape
    channels = w_up_t.shape[0]
    lines = []
    for micro in range(micros):
        lines += list(pooled_stats(found[:, micro, :], found[:, micros + micro, :], float(rows * width)))
    turned = columns_of(lines)
    stats[...] = turned
    gain, shift = cols[:, 6:7], cols[:, 7:8]
    gain_rows, shift_rows, mixed_rows = [], [], []
    for micro in range(micros):
        centre, rstd = turned[:, 2 * micro : 2 * micro + 1], turned[:, 2 * micro + 1 : 2 * micro + 2]
        factor = gain * rstd
        gain_sum = jnp.zeros((wide, LANES), F32)
        shift_sum = jnp.zeros((wide, LANES), F32)
        mixed_sum = jnp.zeros((2 * channels, LANES), F32)
        for row in range(rows):
            unit = (upper[micro, row] - centre) * rstd
            normed = unit * gain + shift
            gate = sigmoid(normed)
            act = normed * gate
            grad = cot[micro, row].astype(F32) * (gate + act * (1.0 - gate))
            for j in range(width // LANES):
                ordered[micro, j, pl.ds(row, wide, stride=rows), :] = act[:, j * LANES : (j + 1) * LANES]
            grads[micro, row] = grad
            gain_sum = gain_sum + fold(grad * unit)
            shift_sum = shift_sum + fold(grad)
            below = dot(w_up_t[...], (grad * factor).astype(BF16))
            mixed_sum = mixed_sum + fold(
                slopes[micro, row] * jnp.concatenate([below, below], axis=0)
            )
        gain_rows.append(row_of(gain_sum))
        shift_rows.append(row_of(shift_sum))
        mixed_rows.append(row_of(mixed_sum).astype(BF16).astype(F32))
        line = jnp.concatenate([ordered[micro, j].astype(BF16) for j in range(width // LANES)], axis=1)
        features[micro, 0] = line.reshape(wide, rows, width)
    mixed[...] = jnp.concatenate(mixed_rows, axis=0)
    rows_out = jnp.concatenate(gain_rows + shift_rows, axis=0)
    crossed = jnp.sum(found[:, 2 * micros : 2 * micros + each, :], axis=0)
    rest = send.shape[1] - 6 * micros - each
    block = exact_rows(rows_out) + mixed_rows + [plain[...], crossed]
    if rest > 0:
        block.append(jnp.zeros((rest, LANES), F32))
    block = jnp.concatenate(block, axis=0)
    send[...] = jnp.broadcast_to(block.astype(BF16)[None], send.shape)


def low_rows(turned, value_of, values, stats, gain, low, high, first, rows, tiles):
    micros, _, channels, width = values.shape
    tile = lax.axis_index("tile")
    masks = edges(channels, width)
    for micro in range(micros):
        part = slice(micro * channels, (micro + 1) * channels)
        centre, rstd = stats[part, 0:1], stats[part, 1:2]
        factor = gain * rstd
        slope_part, shift_part = rstd * turned[part, 0:1], turned[part, 1:2]
        for index in range(high):
            grad, value = value_of(micro, index)
            grad = factor * (grad - shift_part - (value - centre) * slope_part)
            if index + first < 0 or index + first >= rows:
                grad = grad * inside(tile, index + first, (tiles, rows))
            low[micro, index] = spread(grad.astype(BF16), masks)


def first_units(first_out, stats, micro, channels):
    part = slice(micro * channels, (micro + 1) * channels)
    centre, rstd = stats[part, 0:1], stats[part, 1:2]
    return lambda row: (first_out[micro, row] - centre) * rstd


def second_sums(total, weight, factors, stats, micro, micros, count):
    channels = weight.shape[1]
    factor, centre = factors[micro], stats[:, 2 * micro : 2 * micro + 1]
    columns = jnp.transpose(jnp.concatenate([total, jnp.zeros((8 - total.shape[0], LANES), F32)], axis=0))
    beta = factor * stats[:, 2 * micro + 1 : 2 * micro + 2] * columns[:, micro : micro + 1] * (1.0 / count)
    alpha = factor * columns[:, micros + micro : micros + micro + 1] * (1.0 / count)
    square = lax.dot_general(
        weight * beta, weight, (((0,), (0,)), ((), ())),
        preferred_element_type=F32, precision=lax.Precision.HIGHEST,
    )
    square = jnp.concatenate([square, square], axis=1)
    line = jnp.sum(weight * (alpha - beta * centre), axis=0, keepdims=True)
    line = jnp.concatenate([line, line], axis=1)

    def give(mixed, plain, crossed):
        mine = crossed[micro * channels : (micro + 1) * channels]
        return mixed - plain * line - jnp.sum(square * mine, axis=0, keepdims=True)

    return give


def middle_back_kernel(
    found, cols, grads, upper, top_stats, second_out, second_stats, slopes, w_up, w_up_t,
    own_mixed, own_plain, own_crossed, second_act, acts, first_out, first_stats, first_slopes, b_second_in,
    out, top_grad, weight_grad, top_gain_grad, top_shift_grad, expected, send,
    low, top_low, extras, second_dz, b_second, *, rows, tiles, each
):
    expand(b_second_in, b_second)
    scene = lax.axis_index("scene")
    micros, _, wide, width = grads.shape
    channels = second_out.shape[2]
    peers = found.shape[0]
    count = float(peers * rows * width)
    kept = 2 * micros
    total = jnp.sum(found[...].astype(F32), axis=0)
    mixed, plain = total[2 * kept : 2 * kept + micros], total[2 * kept + micros : 3 * kept]
    total = total[0:kept] + total[kept : 2 * kept]
    crossed = jnp.concatenate(
        [
            found[peer].astype(F32)[3 * kept : 3 * kept + each]
            for peer in range(-(-micros * channels // each))
        ],
        axis=0,
    )
    own_half(total[0:1] + total[1:2], scene, top_gain_grad)
    own_half(total[2:3] + total[3:4], scene, top_shift_grad)
    factors = [cols[:, 6:7] * top_stats[:, 2 * micro + 1 : 2 * micro + 2] for micro in range(micros)]
    wide_weight = w_up[...].astype(F32)
    turned = columns_of([total[index : index + 1] for index in range(2 * micros)]) * (1.0 / count)
    gain = cols[0:channels, 4:5]
    masks = edges(channels, width)
    second_rows = []
    for micro in range(micros):
        top_centre = top_stats[:, 2 * micro : 2 * micro + 1]
        top_slope = top_stats[:, 2 * micro + 1 : 2 * micro + 2] * turned[:, micro : micro + 1]
        top_shift = turned[:, micros + micro : micros + micro + 1]
        part = slice(micro * channels, (micro + 1) * channels)
        centre, rstd = second_stats[part, 0:1], second_stats[part, 1:2]
        gain_sum = jnp.zeros((channels, LANES), F32)
        shift_sum = jnp.zeros((channels, LANES), F32)
        for row in range(rows):
            grad = factors[micro] * (
                grads[micro, row] - top_shift - (upper[micro, row] - top_centre) * top_slope
            )
            grad = grad.astype(BF16)
            top_low[micro, row] = grad
            unit = (second_out[micro, row] - centre) * rstd
            grad = dot(w_up_t[...], grad) * slopes[micro, row, 0:channels]
            second_dz[micro, row] = grad
            shift_sum = shift_sum + fold(grad)
            gain_sum = gain_sum + fold(grad * unit)
        second_rows.append((shift_sum, gain_sum))
    parts = []
    for micro in range(micros):
        give = second_sums(total, wide_weight, factors, top_stats, micro, micros, count)
        whole = give(mixed[micro : micro + 1], plain[micro : micro + 1], crossed)
        extra = row_of(*second_rows[micro]) - give(
            own_mixed[micro : micro + 1], own_plain[micro : micro + 1], own_crossed[...]
        )
        expected[micro : micro + 1] = whole
        extras[micro : micro + 1] = extra
        parts.append(whole * (1.0 / count) + extra * (1.0 / (rows * width)))
    parts = columns_of(parts)
    for micro in range(micros):
        part = slice(micro * channels, (micro + 1) * channels)
        centre, rstd = second_stats[part, 0:1], second_stats[part, 1:2]
        factor = gain * rstd
        shift_part = parts[0:channels, micro : micro + 1]
        slope_part = parts[channels : 2 * channels, micro : micro + 1] * rstd
        for row in range(rows):
            grad = factor * (
                second_dz[micro, row] - shift_part - (second_out[micro, row] - centre) * slope_part
            )
            low[micro, row] = spread(grad.astype(BF16), masks)
    first_back(
        low, top_low, second_act, acts, first_out, first_stats, first_slopes, b_second, extras,
        out, top_grad, weight_grad, send, rows, tiles,
    )


def first_back(
    low, top_low, second_act, acts, first_out, first_stats, slopes, b_second, extras,
    out, top_grad, weight_grad, send, rows, tiles
):
    tile = lax.axis_index("tile")
    micros, _, channels, width = first_out.shape
    half = 6 * channels
    gain_sums, shift_sums = [], []
    for micro in range(micros):
        units = first_units(first_out, first_stats, micro, channels)
        gain_sum = jnp.zeros((channels, LANES), F32)
        shift_sum = jnp.zeros((channels, LANES), F32)
        for at in range(0, rows + 2, 2):
            if at == 0:
                parts = dot(b_second[:, half:], low[micro, 0:2].reshape(half, width))
            elif at == rows:
                parts = dot(b_second[:, :half], low[micro, rows - 2 : rows].reshape(half, width))
            else:
                parts = conv_pair(low, b_second, micro, at - 2, channels)
            for j in range(2):
                grad = parts[channels * j : channels * (j + 1)] * slopes[micro, at + j]
                if at + j == 0 or at + j == rows + 1:
                    grad = grad * inside(tile, at + j - 1, (tiles, rows))
                out[micro, at + j] = grad
                gain_sum = gain_sum + fold(grad * units(at + j))
                shift_sum = shift_sum + fold(grad)
        gain_sums.append(gain_sum)
        shift_sums.append(shift_sum)
        product = dot_lanes(
            jnp.concatenate([top_low[micro, row] for row in range(rows)], axis=1),
            jnp.concatenate([second_act[micro, row] for row in range(rows)], axis=1),
        )
        top_grad[...] = product if micro == 0 else top_grad[...] + product
    conv_grad(low, 0, acts, 0, weight_grad, rows)
    send_all(send, [row_of(*gain_sums), row_of(*shift_sums)] + [extras[m : m + 1] for m in range(micros)])


def conv_grad(low, low_first, values, value_first, total, rows):
    micros, _, channels, width = values.shape
    for micro in range(micros):
        grads = jnp.concatenate([low[micro, row + low_first] for row in range(rows)], axis=1)
        windows = jnp.concatenate(
            [
                values[micro, row + value_first : row + value_first + 3].reshape(3 * channels, width)
                for row in range(rows)
            ],
            axis=1,
        )
        product = dot_lanes(grads, windows)
        total[...] = product if micro == 0 else total[...] + product


def half_rows(total, half, scene):
    channels = 2 * half
    start = scene * half
    mine = jnp.concatenate(
        [total[b * channels + start : b * channels + start + half, :] for b in range(2, -1, -1)], axis=0
    )
    wing = mine[:, LANES:]
    cut = wing.shape[0] // 2
    return [mine[:, :LANES], jnp.concatenate([wing[:cut], wing[cut:]], axis=1)]


def pick_kernel(
    found, cols, grads, first_out, first_stats, b_first_in, where_rows,
    canvas, second_grad, top_grad, expected,
    send, gain_grad, shift_grad, second_gain_grad, second_shift_grad, low, grid, b_first, first_grad, whole,
    choices,
    *, rows, tiles, each
):
    expand(b_first_in, b_first)
    columns = jnp.transpose(where_rows[...])
    slots, width = columns.shape[0], grads.shape[3]
    lane = lax.broadcasted_iota(jnp.int32, (slots, width), 1).astype(F32)
    for at in range(choices.shape[0]):
        column = columns[:, at : at + 1] - 1.0
        column = column - jnp.floor(column * (1.0 / width)) * width
        choices[at] = jnp.where(lane == column, 1.0, 0.0).astype(BF16)
    scene = lax.axis_index("scene")
    micros, high, channels, width = grads.shape
    sums = sum_rows(found, 2 + micros)
    second = sum(sums[2:]) + jnp.sum(expected[...], axis=0, keepdims=True)
    own_half(second[:, :channels], scene, second_shift_grad)
    own_half(second[:, channels:], scene, second_gain_grad)
    sums = sums[:2]
    own_half(sums[0][:, :channels] + sums[0][:, channels:], scene, gain_grad)
    own_half(sums[1][:, :channels] + sums[1][:, channels:], scene, shift_grad)
    turned = columns_of(sums) * (1.0 / (found.shape[0] * rows * width))
    masks = edges(channels, width)
    for micro in range(micros):
        part = slice(micro * channels, (micro + 1) * channels)
        centre, rstd = first_stats[part, 0:1], first_stats[part, 1:2]
        factor = cols[0:channels, 2:3] * rstd
        slope_part, shift_part = rstd * turned[part, 0:1], turned[part, 1:2]
        for row in range(high):
            grad = grads[micro, row]
            if 1 <= row <= rows:
                grad = grad - shift_part - (first_out[micro, row] - centre) * slope_part
            low[micro, row] = spread((factor * grad).astype(BF16), masks)
    half = 6 * channels
    for micro in range(micros):
        for at in range(0, rows + 4, 2):
            if at == 0:
                parts = dot(b_first[:, half:], low[micro, 0:2].reshape(half, width))
            elif at == rows + 2:
                parts = dot(b_first[:, :half], low[micro, rows : rows + 2].reshape(half, width))
            else:
                parts = conv_pair(low, b_first, micro, at - 2, channels)
            grid[micro, at] = parts[:channels].astype(BF16)
            grid[micro, at + 1] = parts[channels:].astype(BF16)
    conv_grad(low, 0, canvas, 0, first_grad, high)
    half = channels // 2
    for s in range(2):
        parts = half_rows(first_grad, half, s) + half_rows(second_grad, half, s)
        mine = top_grad[s * channels : (s + 1) * channels, :]
        parts.append(jnp.concatenate([mine[:half], mine[half:]], axis=1))
        parts = jnp.concatenate(parts, axis=0)
        whole[s, 0 : parts.shape[0]] = parts
        if whole.shape[1] > parts.shape[0]:
            whole[s, parts.shape[0] :] = jnp.zeros((whole.shape[1] - parts.shape[0], LANES), F32)
    groups = []
    for group in range(3):
        start, first, count = ((0, rows - 2, 2), (2, 0, rows), (rows + 2, 0, 2))[group]
        picked = []
        for micro in range(micros):
            at = 2 * group + micro
            place = jnp.floor((where_rows[at : at + 1] - 1.0) * (1.0 / width))
            here = dot_lanes(grid[micro, start : start + count].reshape(count * channels, width), choices[at])
            total = jnp.zeros((channels, slots), F32)
            for r in range(count):
                total = total + jnp.where(
                    place == (first + r) * 1.0, here[r * channels : (r + 1) * channels], 0.0
                )
            picked.append(total)
        groups.append(jnp.transpose(jnp.concatenate(picked, axis=0)))
    capacity = slots // tiles
    block = send.shape[1]

    def filled(parts):
        missing = block - sum(part.shape[0] for part in parts)
        if missing > 0:
            parts = parts + [jnp.zeros((missing, LANES), F32)]
        return jnp.concatenate(parts, axis=0).astype(BF16)

    for spot in range(tiles):
        mine = slice(spot * capacity, (spot + 1) * capacity)
        send[2 * spot + scene] = filled([picked[mine] for picked in groups])
        send[2 * spot + 1 - scene] = filled([whole[s, spot * each : (spot + 1) * each] for s in range(2)])


def pillar_weights_kernel(rows, w_pillar, cols, pooled, out, lifted):
    micros, channels, wide = out.shape
    pillars = pooled.shape[2]
    inputs = w_pillar.shape[1]
    gain, shift = cols[0:channels, 0:1], cols[0:channels, 1:2]
    for micro in range(micros):
        lifted[...] = dot(w_pillar[...], rows[micro, 0:inputs])
        _, limit = pillar_notes(rows, micro, inputs, pillars)
        centre, rstd = pooled[micros + micro, :, 0:1], pooled[micros + micro, :, 1:2]
        pool = pooled[micro]
        for n in range(wide // pillars):
            piece = slice(n * pillars, (n + 1) * pillars)
            normed = (lifted[:, piece] - centre) * rstd * gain + shift
            gate = sigmoid(normed)
            act = normed * gate
            slope = gate + act * (1.0 - gate)
            out[micro, :, piece] = jnp.where(limit > n, jnp.exp(act - pool) * slope, 0.0).astype(BF16)


def pillar_back_kernel(found, rows, w_pillar, cols, pooled, factors, send, grads, lifted, choices, *, capacity, each):
    micros = rows.shape[0]
    _, channels, pillars = pooled.shape
    stats = pooled.at[micros : 2 * micros]
    inputs = w_pillar.shape[1]
    depth = rows.shape[2] // pillars
    scene = lax.axis_index("scene")
    peers = found.shape[0]
    slot_count = peers // 2 * capacity
    place = lax.broadcasted_iota(jnp.int32, (slot_count, pillars), 0).astype(F32)
    for micro in range(micros):
        lifted[micro] = dot(w_pillar[...], rows[micro, 0:inputs])
        slot, _ = pillar_notes(rows, micro, inputs, pillars)
        choices[micro] = jnp.where(place == slot, 1.0, 0.0).astype(BF16)
    blocks = [found[2 * t + scene].astype(F32) for t in range(peers // 2)]
    before, own, after = [
        jnp.concatenate([block[group * capacity : (group + 1) * capacity] for block in blocks], axis=0)
        for group in range(3)
    ]
    gap = jnp.zeros((capacity, LANES), F32)
    returned = (
        own
        + jnp.concatenate([before[capacity:], gap], axis=0)
        + jnp.concatenate([gap, after[: slot_count - capacity]], axis=0)
    )
    turned = jnp.transpose(returned)
    gain = cols[0:channels, 0:1]
    gain_sums, shift_sums = [], []
    outer = jnp.zeros((16, channels), F32)
    for micro in range(micros):
        back = dot(turned[micro * channels : (micro + 1) * channels].astype(BF16), choices[micro])
        centre, rstd = stats[micro, :, 0:1], stats[micro, :, 1:2]
        gain_sum = jnp.zeros((channels, pillars), F32)
        shift_sum = jnp.zeros((channels, pillars), F32)
        for n in range(depth):
            piece = slice(n * pillars, (n + 1) * pillars)
            grad = back * factors[micro, :, piece].astype(F32)
            grads[micro, :, piece] = grad
            gain_sum = gain_sum + grad * (lifted[micro, :, piece] - centre)
            shift_sum = shift_sum + grad
        gain_sum = gain_sum * rstd
        gain_sums.append(gain_sum)
        shift_sums.append(shift_sum)
        scale = jnp.transpose(jnp.broadcast_to(rstd * gain, (channels, LANES)))[0:1]
        outer = outer + dot_lanes(rows[micro], grads[micro].astype(BF16)) * scale
    exact = jnp.concatenate([row_of(*gain_sums), row_of(*shift_sums)], axis=0)
    lines = [jnp.concatenate([outer[k : k + 1], outer[k + 1 : k + 2]], axis=1) for k in range(0, 10, 2)]
    weights = found[1 - scene].astype(F32)
    for t in range(1, peers // 2):
        weights = weights + found[2 * t + 1 - scene].astype(F32)
    rest = send.shape[2] - 9 - each
    for s in range(2):
        block = exact_rows(exact) + lines + [weights[s * each : (s + 1) * each]]
        if rest > 0:
            block.append(jnp.zeros((rest, LANES), F32))
        block = jnp.concatenate(block, axis=0).astype(BF16)
        send[:, s] = jnp.broadcast_to(block[None], (send.shape[0],) + block.shape)


def points_kernel(
    found, rows, grads, w_pillar, cols, pooled,
    points_grad, pillar_grad, gain_grad, shift_grad, first_grad, second_grad, up_grad, lifted, *, each
):
    scene = lax.axis_index("scene")
    micros, channels, _ = grads.shape
    stats = pooled.at[micros : 2 * micros]
    _, _, inputs, depth, pillars = points_grad.shape
    half = channels // 2
    for micro in range(micros):
        lifted[micro] = dot(w_pillar[...], rows[micro, 0:inputs])
    total = jnp.sum(found[...].astype(F32), axis=0)
    total = jnp.concatenate([total[0:2] + total[2:4], total[4:9]], axis=0)
    own_half(total[0:1, :channels] + total[0:1, channels:], scene, gain_grad)
    own_half(total[1:2, :channels] + total[1:2, channels:], scene, shift_grad)
    turned = jnp.transpose(jnp.concatenate([total, jnp.zeros((1, LANES), F32)], axis=0))
    weight_grad = jnp.concatenate(
        [turned[(k % 2) * channels : (k % 2 + 1) * channels, 2 + k // 2 : 3 + k // 2] for k in range(inputs)],
        axis=1,
    )
    weight = jnp.transpose(w_pillar[...].astype(F32)).astype(BF16)
    for micro in range(micros):
        part = slice(micro * channels, (micro + 1) * channels)
        centre, rstd, inverse = stats[micro, :, 0:1], stats[micro, :, 1:2], stats[micro, :, 2:3]
        factor = cols[0:channels, 0:1] * rstd
        gain_part, shift_part = turned[part, 0:1], turned[part, 1:2]
        spun, mean = stats[micro, :, 16 : 16 + inputs], stats[micro, :, 32 : 32 + inputs]
        weight_grad = weight_grad - factor * (shift_part * mean + gain_part * rstd * spun)
        gain_part, shift_part = gain_part * inverse * rstd, shift_part * inverse
        _, limit = pillar_notes(rows, micro, inputs, pillars)
        for n in range(depth):
            piece = slice(n * pillars, (n + 1) * pillars)
            low = factor * (grads[micro, :, piece] - shift_part - (lifted[micro, :, piece] - centre) * gain_part)
            low = jnp.where(limit > n, low, 0.0).astype(BF16)
            points_grad[micro, 0, :, n, :] = dot(weight, low)
    weight_grad = jnp.concatenate([weight_grad, jnp.zeros((channels, LANES - inputs), F32)], axis=1)
    weight_grad = jnp.transpose(weight_grad)[0:inputs]
    pillar_grad[...] = jnp.where(scene == 0, weight_grad[:, :half], weight_grad[:, half:])
    whole = jnp.concatenate(
        [
            (found[2 * t].astype(F32) + found[2 * t + 1].astype(F32))[9 : 9 + each]
            for t in range(found.shape[0] // 2)
        ],
        axis=0,
    )
    for index, out in enumerate((first_grad, second_grad)):
        base = index * 9 * half * channels // LANES
        lead = 3 * half
        mine = whole[base : base + lead]
        wing = whole[base + lead : base + lead + lead // 2]
        wing = jnp.concatenate([wing[:, :channels], wing[:, channels:]], axis=0)
        both = jnp.concatenate([mine, wing], axis=1)
        for a in range(3):
            for b in range(3):
                at = (3 * a + b) * channels
                out[:, at : at + channels] = both[b * half : (b + 1) * half, a * channels : (a + 1) * channels]
    base = 2 * 9 * half * channels // LANES
    top = whole[base : base + half]
    up_grad[...] = jnp.concatenate([top[:, :channels], top[:, channels:]], axis=0)


def swap(blocks, axes):
    return lax.all_to_all(blocks, axes, split_axis=0, concat_axis=0)


def shards(
    points, point_counts, pillar_tile, pillar_cell,
    pillar_weight, pillar_gain, pillar_shift,
    first_weight, first_gain, first_shift,
    second_weight, second_gain, second_shift,
    up_weight, up_gain, up_shift, cotangent,
):
    micros, _, inputs, depth, pillars = points.shape
    channels = up_weight.shape[1]
    upper = cotangent.shape[2]
    rows, width = cotangent.shape[3:]
    tiles = lax.axis_size("tile")
    scenes = lax.axis_size("scene")
    peers = tiles * scenes
    capacity = 2 * pillars // tiles
    slot_count = tiles * capacity
    half = channels // 2

    def vmem(shape, dtype):
        return pltpu.VMEM(shape, dtype)

    def grid(high, dtype=F32, lead=channels):
        return ((micros, high, lead, width), dtype)

    sums = ((peers, 2, LANES), F32)
    sources = (pillar_tile, pillar_cell, point_counts, points)
    wide = vmem((inputs * depth, pillars), F32)
    (moments,) = run(
        functools.partial(moments_kernel, capacity=capacity),
        [((tiles, scenes, 4, LANES), F32)],
        *sources,
        hbm=range(len(sources)), copies=len(sources), limit=WIDE_LIMIT,
        scratch=[vmem(source.shape, source.dtype) for source in sources] + [wide],
    )
    sources = (
        pillar_tile, point_counts, points,
        first_weight, second_weight, up_weight, pillar_weight.T,
        pillar_gain, pillar_shift, first_gain, first_shift, second_gain, second_shift, up_gain, up_shift,
    )
    packed, point_rows = run(
        functools.partial(pack_kernel, capacity=capacity),
        [((layout(half, channels)[-1] + 16, LANES), BF16), ((micros, 16, depth * pillars), BF16)],
        *sources,
        hbm=range(len(sources)), copies=len(sources), limit=WIDE_LIMIT,
        scratch=[vmem(source.shape, source.dtype) for source in sources] + [wide],
        cost=pl.CostEstimate(flops=10**7, bytes_accessed=10**6, transcendentals=0),
    )
    moments = swap(moments.reshape(peers, 4, LANES), BOTH)
    both = lax.all_gather(packed, "scene")
    taps = ((2 * channels, 12 * channels), BF16)
    compact = ((channels, 9 * channels), BF16)
    w_pillar, cols, l_first, l_second, b_first, b_second, w_up, w_up_t = run(
        functools.partial(unpack_kernel, inputs=inputs),
        [
            ((channels, inputs), BF16), ((LANES, 8), F32), compact, compact, compact, compact,
            ((upper, channels), BF16), ((channels, upper), BF16),
        ],
        both,
    )
    cot = cotangent[:, 0].transpose(0, 2, 1, 3)

    send, pooled = run(
        functools.partial(pillar_kernel, capacity=capacity),
        [((slot_count, 3 * LANES), BF16), ((2 * micros, channels, pillars), F32)],
        moments, point_rows, w_pillar, cols,
        scratch=[
            vmem((micros, channels, depth * pillars), F32), vmem((channels, depth * pillars), F32),
            vmem((3, slot_count, micros * pillars), BF16),
        ],
    )
    arrived = swap(send.reshape(tiles, capacity, 3 * LANES), "tile").reshape(slot_count, 3 * LANES)
    (cell_rows,) = run(
        functools.partial(cells_kernel, capacity=capacity),
        [((8, slot_count), F32)],
        moments,
        cost=pl.CostEstimate(flops=10**7, bytes_accessed=10**6, transcendentals=0),
    )
    (factors,) = run(
        pillar_weights_kernel,
        [((micros, channels, depth * pillars), BF16)],
        point_rows, w_pillar, cols, pooled,
        scratch=[vmem((channels, depth * pillars), F32)],
        cost=pl.CostEstimate(flops=10**7, bytes_accessed=10**6, transcendentals=0),
    )
    arrived, cot, factors = lax.optimization_barrier((arrived, cot, factors))

    first_out, canvas, send = run(
        functools.partial(canvas_kernel, rows=rows),
        [grid(rows + 2), grid(rows + 4, BF16), sums],
        arrived, cell_rows, l_first,
        scratch=[vmem(*grid(rows + 4, BF16, 3 * channels)), vmem(*taps)],
    )
    second_out, first_act, first_slopes, first_stats, send = run(
        functools.partial(second_kernel, rows=rows, tiles=tiles),
        [grid(rows), grid(rows + 2, BF16), grid(rows + 2), ((LANES, 8), F32), sums],
        swap(send, BOTH), cols, first_out, l_second,
        scratch=[vmem(*grid(rows + 2, BF16, 3 * channels)), vmem(*taps)],
    )
    part = -(-micros * channels // peers)
    second_act, up_out, slopes, plain, crossed, second_stats, send = run(
        functools.partial(up_kernel, rows=rows),
        [
            grid(rows, BF16), grid(rows, F32, upper), grid(rows, F32, 2 * channels), ((micros, LANES), F32),
            ((peers * part, LANES), F32), ((LANES, 8), F32), ((peers, -(-(2 * micros + part) // 8) * 8, LANES), F32),
        ],
        swap(send, BOTH), cols, second_out, w_up,
    )
    features, grads, mixed, top_stats, send = run(
        functools.partial(top_kernel, rows=rows, each=part),
        [
            ((micros, 1, upper, rows, width), BF16), grid(rows, F32, upper), ((micros, LANES), F32),
            ((LANES, 8), F32),
            ((peers, -(-(6 * micros + part) // 8) * 8, LANES), BF16),
        ],
        swap(send, BOTH), cols, up_out, cot, slopes, plain, w_up_t,
        scratch=[vmem((micros, width // LANES, upper * rows, LANES), F32)],
    )
    vector, top_vector, matrix = ((half,), F32), ((upper // 2,), F32), ((half, 9 * channels), F32)
    cross = ((3 * channels, 3 * channels), F32)
    first_dz, top_grad, second_cross, up_gain_grad, up_shift_grad, expected, send = run(
        functools.partial(middle_back_kernel, rows=rows, tiles=tiles, each=part),
        [
            grid(rows + 2), ((upper, channels), F32), cross, top_vector, top_vector, ((micros, LANES), F32),
            ((peers, 2 + micros, LANES), F32),
        ],
        swap(send, BOTH), cols, grads, up_out, top_stats, second_out, second_stats, slopes, w_up, w_up_t,
        mixed, plain, crossed, second_act, first_act, first_out, first_stats, first_slopes, b_second,
        scratch=[
            vmem(*grid(rows, BF16, 3 * channels)), vmem(*grid(rows, BF16, upper)), vmem((micros, LANES), F32),
            vmem(*grid(rows)), vmem(*taps),
        ],
    )
    length = (2 * 9 * half * channels + upper * half) // LANES
    each = -(-length // tiles)
    block = -(-max(3 * capacity, 2 * each) // 8) * 8
    send, first_gain_grad, first_shift_grad, second_gain_grad, second_shift_grad = run(
        functools.partial(pick_kernel, rows=rows, tiles=tiles, each=each),
        [((peers, block, LANES), BF16), vector, vector, vector, vector],
        swap(send, BOTH), cols, first_dz, first_out, first_stats, b_first, cell_rows,
        canvas, second_cross, top_grad, expected,
        scratch=[
            vmem(*grid(rows + 2, BF16, 3 * channels)), vmem(*grid(rows + 4, BF16)), vmem(*taps), vmem(*cross),
            vmem((scenes, tiles * each, LANES), F32), vmem((3 * micros, slot_count, width), BF16),
        ],
    )
    block = -(-(9 + each) // 8) * 8
    send, pillar_dz = run(
        functools.partial(pillar_back_kernel, capacity=capacity, each=each),
        [((tiles, scenes, block, LANES), BF16), ((micros, channels, depth * pillars), F32)],
        swap(send, BOTH), point_rows, w_pillar, cols, pooled, factors,
        scratch=[
            vmem((micros, channels, depth * pillars), F32), vmem((micros, slot_count, pillars), BF16),
        ],
    )
    points_grad, pillar_grad, pillar_gain_grad, pillar_shift_grad, first_grad, second_grad, up_grad = run(
        functools.partial(points_kernel, each=each),
        [
            ((micros, 1, inputs, depth, pillars), F32), ((inputs, half), F32), vector, vector,
            matrix, matrix, ((upper // 2, channels), F32),
        ],
        swap(send.reshape(peers, block, LANES), BOTH), point_rows, pillar_dz, w_pillar, cols, pooled,
        scratch=[vmem((micros, channels, depth * pillars), F32)],
    )
    return (
        features, points_grad,
        pillar_grad.T, pillar_gain_grad, pillar_shift_grad,
        first_grad, first_gain_grad, first_shift_grad,
        second_grad, second_gain_grad, second_shift_grad,
        up_grad, up_gain_grad, up_shift_grad,
    )


def solution(mesh):
    matrix, vector = P("scene", None), P("scene")
    grid = P(None, "scene", None, "tile", None)
    cloud = P(None, "scene", None, None, "tile")
    pillar = P(None, "scene", "tile")
    weights = (matrix, vector, vector) * 4
    return jax.shard_map(
        shards,
        mesh=mesh,
        in_specs=(cloud, pillar, pillar, pillar) + weights + (grid,),
        out_specs=(grid, cloud) + weights,
        check_vma=False,
    )
```
